32 devices in a mesh: ctx: 8 (over y, x, core), tp: 4 (over z).
Axes of the slice: x: 2, y: 2, z: 4, core: 2. Of those that a mesh axis runs over, the one named last changes fastest.
Arguments:
- tokens_in: bfloat16 [4096, 2560], P('ctx'), may hold values from -1.5 to 1.5
- w_qa: bfloat16 [2560, 768], replicated, may hold values from -0.125 to 0.125
- w_kva: bfloat16 [2560, 288], replicated, may hold values from -0.125 to 0.125
- w_qb: bfloat16 [768, 3840], P(None, 'tp'), may hold values from -0.4375 to 0.4375
- w_kvb: bfloat16 [256, 5120], P(None, 'tp'), may hold values from -0.375 to 0.375
- w_out: bfloat16 [2560, 2560], P(None, 'tp'), may hold values from -1 to 1
- w_gate: bfloat16 [2560, 6400], P(None, 'tp'), may hold values from -0.125 to 0.125
- w_up: bfloat16 [2560, 6400], P(None, 'tp'), may hold values from -0.125 to 0.125
- w_down: bfloat16 [2560, 6400], P(None, 'tp'), may hold values from -0.15625 to 0.15625
- gain_in: float32 [2560], replicated, may hold values from 0.5 to 1.5
- gain_q: float32 [768], replicated, may hold values from 0.5 to 1.5
- gain_kv: float32 [256], replicated, may hold values from 0.5 to 1.5
- gain_mid: float32 [2560], replicated, may hold values from 0.5 to 1.5
- cotangent: bfloat16 [4096, 2560], P('ctx'), may hold values from -6 to 6
- block_map: int32 [8, 2], replicated, may hold values from 0 to 15, as said below
- doc_lengths: int32 [4], replicated, may hold values from 1 to 3072, as said below
Outputs:
- out: bfloat16 [4096, 2560], P('ctx')
- grad_in: float32 [4096, 2560], P('ctx')
- grad_w_qa: float32 [2560, 768], P('ctx')
- grad_w_kva: float32 [2560, 288], P('ctx')
- grad_w_qb: float32 [768, 3840], P('ctx', 'tp')
- grad_w_kvb: float32 [256, 5120], P('ctx', 'tp')
- grad_w_out: float32 [2560, 2560], P('ctx', 'tp')
- grad_w_gate: float32 [2560, 6400], P('ctx', 'tp')
- grad_w_up: float32 [2560, 6400], P('ctx', 'tp')
- grad_w_down: float32 [2560, 6400], P('ctx', 'tp')
- grad_gain_in: float32 [2560], P('ctx')
- grad_gain_q: float32 [768], P('ctx')
- grad_gain_kv: float32 [256], P('ctx')
- grad_gain_mid: float32 [2560], P('ctx')
The draws below stay inside these ranges and needn't reach their ends.
Inputs may be any that keep to these rules, and one draw needn't show every extreme that they name: `block_map`: row c lists the two blocks of 256 context places whose tokens ctx index c holds, first the one in column 0, then the one in column 1. Column 0 holds each block of the first half of the context once, column 1 each block of the second half once. `doc_lengths`: the lengths sum to 4096. The first or the last sequence has 3072 tokens.
All inputs are finite; a program needn't handle non-finite values.
Results may differ from the reference program's by a relative error of at most 0.025.
Values may be sent and summed in bfloat16 or wider, within the bound.
A program may use at most 320 MiB of HBM per device.

```python
import math
import jax
import jax.numpy as jnp
from jax import lax

D = 2560
QR = 768
KVR = 256
HEADS = 40
NOPE = 64
ROPE = 32
VDIM = 64
FF = 6400
TOK_DEV = 512
SEQS = 4
TOKENS = 4096
N_CTX = 8


def draw_block_map(key, part):
    key = jax.random.fold_in(key, 5)
    first_key, second_key = jax.random.split(key)
    low_blocks = jax.random.permutation(first_key, N_CTX)
    high_blocks = N_CTX + jax.random.permutation(second_key, N_CTX)
    return jnp.stack([low_blocks, high_blocks], axis=1).astype(jnp.int32)


def draw_doc_lengths(key, part):
    key = jax.random.fold_in(key, 9)
    cut_key, side_key = jax.random.split(key)
    longest = 3 * TOKENS // 4
    remain = TOKENS - longest
    cut_points = jnp.sort(jax.random.permutation(cut_key, remain - 1)[:SEQS - 2] + 1).astype(jnp.int32)
    bounds = jnp.concatenate([jnp.zeros((1,), jnp.int32), cut_points, jnp.full((1,), remain, jnp.int32)])
    pieces = bounds[1:] - bounds[:-1]
    where_long = jax.random.randint(side_key, (), 0, 2) * (SEQS - 1)
    slot_order = jnp.arange(SEQS, dtype=jnp.int32)
    others = jnp.clip(slot_order - (slot_order > where_long).astype(jnp.int32), 0, SEQS - 2)
    picked = others[:, None] == jnp.arange(SEQS - 1, dtype=jnp.int32)[None, :]
    chosen = jnp.sum(jnp.where(picked, pieces[None, :], 0), axis=1)
    return jnp.where(slot_order == where_long, longest, chosen).astype(jnp.int32)


def steps_of(stream_key, dims, cuts, smallest, largest):
    loudness, own = 1.0, jax.random.fold_in(stream_key, 6)
    for axis_at, blocks in cuts:
        heights = jnp.exp(jax.random.uniform(jax.random.fold_in(own, axis_at), (blocks,), jnp.float32, smallest / len(cuts), largest / len(cuts)))
        loudness = loudness * jnp.repeat(heights, dims[axis_at] // blocks).reshape([-1 if axis == axis_at else 1 for axis in range(len(dims))])
    return loudness


def noise(own_key, extent, width, bound, shards=(), kind=jnp.bfloat16):
    gain = steps_of(own_key, extent, shards, -0.22, 0.18) if shards else 1.0
    drawn = jax.random.normal(own_key, extent, jnp.float32) * width * gain
    return jnp.minimum(jnp.maximum(drawn, -bound), bound).astype(kind)


def setup_inputs(seed: int = 0) -> dict:
    keys = jax.random.split(jax.random.key(seed), 17)
    tokens_in = noise(keys[0], (TOKENS, D), 0.25, 1.5, ((0, 8),))
    w_qa = noise(keys[1], (D, QR), D ** -0.5, 0.125)
    w_kva = noise(keys[2], (D, KVR + ROPE), D ** -0.5, 0.125)
    w_qb = noise(keys[3], (QR, HEADS * (NOPE + ROPE)), (QR // 4) ** -0.5, 0.4375, ((1, 4),))
    w_kvb = noise(keys[4], (KVR, HEADS * (NOPE + VDIM)), KVR ** -0.5, 0.375, ((1, 4),))
    w_out = noise(keys[5], (D, HEADS * VDIM), (HEADS * VDIM // 64) ** -0.5, 1.0, ((1, 4),))
    w_gate = noise(keys[6], (D, FF), D ** -0.5, 0.125, ((1, 4),))
    w_up = noise(keys[7], (D, FF), D ** -0.5, 0.125, ((1, 4),))
    w_down = noise(keys[8], (D, FF), (FF // 4) ** -0.5, 0.15625, ((1, 4),))
    gain_in = jnp.clip(1.0 + 0.1 * jax.random.normal(keys[9], (D,), jnp.float32), 0.5, 1.5)
    gain_q = jnp.clip(1.0 + 0.1 * jax.random.normal(keys[10], (QR,), jnp.float32), 0.5, 1.5)
    gain_kv = jnp.clip(1.0 + 0.1 * jax.random.normal(keys[11], (KVR,), jnp.float32), 0.5, 1.5)
    gain_mid = jnp.clip(1.0 + 0.1 * jax.random.normal(keys[12], (D,), jnp.float32), 0.5, 1.5)
    cotangent = noise(keys[13], (TOKENS, D), 1.0, 6.0, ((0, 8),))
    block_map = draw_block_map(jax.random.fold_in(keys[16], 71), 0)
    doc_lengths = draw_doc_lengths(jax.random.fold_in(keys[16], 71), 0)
    return dict(tokens_in=tokens_in, w_qa=w_qa, w_kva=w_kva, w_qb=w_qb, w_kvb=w_kvb, w_out=w_out, w_gate=w_gate, w_up=w_up, w_down=w_down, gain_in=gain_in, gain_q=gain_q, gain_kv=gain_kv, gain_mid=gain_mid, cotangent=cotangent, block_map=block_map, doc_lengths=doc_lengths)


EPSILON = 1e-05
ROPE_BASE = 10000.0
MASKED = -1e+30
RESIDUAL_SCALE = 1.4 / math.sqrt(62.0)
HIGH = lax.Precision.HIGHEST

@jax.custom_vjp
def low(v):
    return lax.optimization_barrier(v.astype(jnp.bfloat16)).astype(jnp.float32)

@jax.custom_vjp
def low_back(v):
    return v

def low_keep(v):
    return (low(v), None)

def low_pass(kept, grad):
    return (grad,)

def back_keep(v):
    return (v, None)

def back_low(kept, grad):
    return (low(grad),)
low.defvjp(low_keep, low_pass)
low_back.defvjp(back_keep, back_low)

def token_places(block_map, doc_lengths, per_device, devices):
    all_rows = per_device * devices
    half_block = per_device // 2
    token_rows = jnp.arange(all_rows, dtype=jnp.int32)
    device_of = token_rows // per_device
    within = token_rows % per_device
    wanted = device_of * 2 + within // half_block
    select = wanted[:, None] == jnp.arange(2 * devices, dtype=jnp.int32)[None, :]
    blocks = lax.optimization_barrier(jnp.sum(jnp.where(select, block_map.reshape(-1)[None, :], 0), axis=1)).astype(jnp.int32)
    places = (blocks * half_block + within % half_block).astype(jnp.int32)
    ends = jnp.cumsum(doc_lengths).astype(jnp.int32)
    segment = lax.optimization_barrier(jnp.sum((places[:, None] >= ends[None, :]).astype(jnp.int32), axis=1)).astype(jnp.int32)
    starts = (ends - doc_lengths).astype(jnp.int32)
    picked = segment[:, None] == jnp.arange(doc_lengths.shape[0], dtype=jnp.int32)[None, :]
    begins = lax.optimization_barrier(jnp.sum(jnp.where(picked, starts[None, :], 0), axis=1)).astype(jnp.int32)
    return (places, segment, (places - begins).astype(jnp.int32))

def tables(inside):
    half_width = ROPE // 2
    frequency = ROPE_BASE ** (-2.0 * jnp.arange(half_width, dtype=jnp.float32) / ROPE)
    angles = inside.astype(jnp.float32)[:, None] * frequency[None, :]
    cosine_table = jnp.concatenate([jnp.cos(angles), jnp.cos(angles)], axis=1)
    sine_table = jnp.concatenate([jnp.sin(angles), jnp.sin(angles)], axis=1)
    return (cosine_table, sine_table)

def rotate(values, cosine_table, sine_table):
    half_width = values.shape[-1] // 2
    turned = jnp.concatenate([-values[..., half_width:], values[..., :half_width]], axis=-1)
    return values * cosine_table + turned * sine_table

def rms_norm(values, gain_vec):
    return values * lax.rsqrt(lax.optimization_barrier(jnp.mean(values * values, axis=-1, keepdims=True)) + EPSILON) * gain_vec

def matmul(left_op, right_op):
    return jnp.dot(left_op, right_op, precision=HIGH, preferred_element_type=jnp.float32)

def matmul_cols(left_op, right_op):
    return lax.dot_general(left_op, right_op, (((1,), (1,)), ((), ())), precision=HIGH, preferred_element_type=jnp.float32)

def reference(tokens_in, w_qa, w_kva, w_qb, w_kvb, w_out, w_gate, w_up, w_down, gain_in, gain_q, gain_kv, gain_mid, cotangent, block_map, doc_lengths):
    all_rows = tokens_in.shape[0]
    places, segment, inside = token_places(block_map, doc_lengths, TOK_DEV, N_CTX)
    cosine_table, sine_table = tables(inside)
    score_scale = (NOPE + ROPE) ** (-0.5)
    span = math.gcd(all_rows, 256)
    block_count = all_rows // span

    def forward(tokens, wq_down, wkv_down, wq_up, wkv_up, wo_proj, wg_proj, wu_proj, wd_proj, gain_first, gain_query, gain_latent, gain_second):
        normed_in = low(rms_norm(tokens, gain_first))
        q_latent = low(rms_norm(low_back(matmul(normed_in, wq_down)), gain_query))
        query_pre = low_back(matmul(q_latent, wq_up)).reshape(all_rows, HEADS, NOPE + ROPE)
        queries = low(jnp.concatenate([query_pre[..., :NOPE], rotate(query_pre[..., NOPE:], cosine_table[:, None, :], sine_table[:, None, :])], axis=-1))
        kv_input = low_back(matmul(normed_in, wkv_down))
        latent = low(rms_norm(kv_input[:, :KVR], gain_latent))
        key_rope = low(rotate(kv_input[:, KVR:], cosine_table, sine_table))
        expanded = low(matmul(latent, wkv_up)).reshape(all_rows, HEADS, NOPE + VDIM)
        key_part = expanded[..., :NOPE]
        value_part = expanded[..., NOPE:]

        def attend(block_in):
            query_block, place_block, segment_block = block_in
            raw_scores = jnp.einsum('qhd,khd->hqk', query_block[..., :NOPE], key_part, precision=HIGH)
            raw_scores = raw_scores + jnp.einsum('qhd,kd->hqk', query_block[..., NOPE:], key_rope, precision=HIGH)
            scores = low_back(raw_scores * score_scale)
            allowed = (segment[None, :] == segment_block[:, None]) & (places[None, :] <= place_block[:, None])
            scores = jnp.where(allowed[None], scores, MASKED)
            row_top = lax.optimization_barrier(jnp.max(scores, axis=-1, keepdims=True))
            log_total = row_top + jnp.log(lax.optimization_barrier(jnp.sum(jnp.where(allowed[None], jnp.exp(scores - row_top), 0.0), axis=-1, keepdims=True)))
            weights = low(jnp.where(allowed[None], jnp.exp(scores - log_total), 0.0))
            return jnp.einsum('hqk,khd->qhd', weights, value_part, precision=HIGH)
        blocks_in = (queries.reshape(block_count, span, HEADS, NOPE + ROPE), places.reshape(block_count, span), segment.reshape(block_count, span))
        mixed = lax.map(jax.checkpoint(attend), blocks_in).reshape(all_rows, HEADS * VDIM)
        heads_out = low(low_back(mixed))
        attention = low_back(matmul_cols(heads_out, wo_proj))
        middle = tokens + RESIDUAL_SCALE * attention
        normed_mid = low(rms_norm(middle, gain_second))
        gate_val = low_back(matmul(normed_mid, wg_proj))
        up_val = low_back(matmul(normed_mid, wu_proj))
        activation = low(jax.nn.silu(gate_val) * up_val)
        feed_out = low_back(matmul_cols(activation, wd_proj))
        return middle + RESIDUAL_SCALE * feed_out
    params = tuple((array_in.astype(jnp.float32) for array_in in (tokens_in, w_qa, w_kva, w_qb, w_kvb, w_out, w_gate, w_up, w_down, gain_in, gain_q, gain_kv, gain_mid)))
    result, pullback = jax.vjp(forward, *params)
    grads = pullback(cotangent.astype(jnp.float32))
    return (result.astype(jnp.bfloat16), grads[0], grads[1], grads[2], grads[3], grads[4], grads[5], grads[6], grads[7], grads[8], grads[9], grads[10], grads[11], grads[12])
```

```python
import functools
import math

import jax
import jax.numpy as jnp
from jax import lax
from jax.experimental import pallas as pl
from jax.experimental.pallas import tpu as pltpu
from jax.sharding import PartitionSpec as P

KVR = 256
NOPE = 64
ROPE = 32
VDIM = 64
HEAD = NOPE + VDIM
WIDE = 2 * HEAD
MASKED = -1e30
SCORE_SCALE = (NOPE + ROPE) ** (-0.5)
EXP2_SCALE = SCORE_SCALE * math.log2(math.e)
FOLD_AT = 96
VMEM_LIMIT = 56 * 1024 * 1024

EPSILON = 1e-05
ROPE_BASE = 10000.0
RESIDUAL_SCALE = 1.4 / math.sqrt(62.0)


def dot_nn(left_op, right_op):
    return jnp.dot(left_op, right_op, preferred_element_type=jnp.float32)


def dot_nt(left_op, right_op):
    return lax.dot_general(
        left_op, right_op, (((1,), (1,)), ((), ())), preferred_element_type=jnp.float32
    )


def begin_of(place, starts):
    begin = jnp.zeros_like(place)
    for start in starts:
        begin = jnp.where(start <= place, start, begin)
    return begin


def pair_kind(key_block, query_block, starts, block_rows):
    key_first = key_block * block_rows
    query_first = query_block * block_rows
    early = begin_of(query_first, starts)
    late = begin_of(query_first + block_rows - 1, starts)
    needed = (key_block <= query_block) & (key_first + block_rows - 1 >= early)
    whole = (key_block < query_block) & (late <= key_first)
    return needed, whole


def mask_bias(key_block, query_block, starts, block_rows, keys_first):
    key_dim = 0 if keys_first else 1
    shape = (block_rows, block_rows)
    key_place = key_block * block_rows + lax.broadcasted_iota(jnp.int32, shape, key_dim)
    query_place = query_block * block_rows + lax.broadcasted_iota(jnp.int32, shape, 1 - key_dim)
    begin = jnp.zeros(shape, jnp.int32)
    for start in starts:
        begin = jnp.where(start <= query_place, start, begin)
    allowed = (key_place <= query_place) & (key_place >= begin)
    return jnp.where(allowed, 0.0, MASKED)


def shared_key_tile(rope_rows, block_rows):
    place = lax.broadcasted_iota(jnp.int32, (ROPE, HEAD), 0)
    lane = lax.broadcasted_iota(jnp.int32, (ROPE, HEAD), 1)
    eye = jnp.where(place == lane, 1.0, 0.0).astype(jnp.bfloat16)
    tile = dot_nn(rope_rows, eye)
    lanes = lax.broadcasted_iota(jnp.int32, (block_rows, HEAD), 1)
    ones = (lanes >= FOLD_AT) & (lanes < FOLD_AT + 3)
    return jnp.where(ones, 1.0, tile).astype(jnp.bfloat16)


def head_groups(heads):
    return [(h, min(h + 2, heads)) for h in range(0, heads, 2)]


def forward_kernel(
    blocks, heads, seqs, meta, cq, wqb, lat, wkvb, cos, sin, qx, o_out, ob_out, u_out,
    wkvt, xs, xr, vt, top, total, acc, bias,
):
    rows_all = cq.shape[0]
    block_rows = bias.shape[0]
    q_blocks = rows_all // block_rows
    starts = [meta[blocks + s] for s in range(seqs)]
    own = [meta[blocks + seqs + j] for j in range(q_blocks)]
    for first, last in head_groups(heads):
        wkvt[first * HEAD : last * HEAD, :] = (
            wkvb[:, first * HEAD : last * HEAD].astype(jnp.float32).T.astype(jnp.bfloat16)
        )
    lane = lax.broadcasted_iota(jnp.int32, (block_rows, HEAD), 1)
    for j in range(q_blocks):
        here = pl.ds(j * block_rows, block_rows)
        cos_j, sin_j = cos[here, :], sin[here, :]
        for first, last in head_groups(heads):
            pre = dot_nn(cq[here, :], wqb[:, first * HEAD : last * HEAD])
            for h in range(first, last):
                own_part = pre[:, (h - first) * HEAD : (h - first + 1) * HEAD]
                turned = pltpu.roll(own_part, NOPE, 1)
                left = pltpu.roll(turned, HEAD - ROPE // 2, 1)
                right = pltpu.roll(turned, ROPE // 2, 1)
                swapped = jnp.where(lane < ROPE // 2, -left, right)
                rope = turned * cos_j + swapped * sin_j
                qx[j, h, :, :HEAD] = jnp.where(lane < NOPE, own_part, 0.0).astype(jnp.bfloat16)
                qx[j, h, :, HEAD:] = rope.astype(jnp.bfloat16)
    top[...] = jnp.full(top.shape, MASKED, jnp.float32)
    total[...] = jnp.zeros(total.shape, jnp.float32)
    acc[...] = jnp.zeros(acc.shape, jnp.float32)

    def pair(j, masked):
        def one(h):
            keys = jnp.concatenate([xs[h], xr[...]], axis=1)
            scores = dot_nt(keys, qx[j, h])
            if masked:
                scores = scores + bias[...]
            old = top[j, h]
            new = jnp.maximum(old, jnp.max(scores, axis=0, keepdims=True))
            fade = jnp.exp2((old - new) * EXP2_SCALE)
            terms = jnp.exp2((scores - new) * EXP2_SCALE)
            top[j, h] = new
            total[j, h] = fade * total[j, h] + jnp.sum(terms, axis=0, keepdims=True)
            acc[j, h] = fade * acc[j, h] + dot_nn(vt[h], terms.astype(jnp.bfloat16))

        for h in range(heads):
            one(h)

    def step(r, carry):
        key_block = meta[r]
        kinds = [pair_kind(key_block, own[j], starts, block_rows) for j in range(q_blocks)]
        wanted = functools.reduce(jnp.logical_or, [k[0] for k in kinds])

        @pl.when(wanted)
        def _():
            here = pl.ds(pl.multiple_of(r * block_rows, block_rows), block_rows)
            latent = lat[here, :KVR]
            xr[...] = shared_key_tile(lat[here, KVR : KVR + ROPE], block_rows)
            for first, last in head_groups(heads):
                keys = dot_nn(latent, wkvb[:, first * HEAD : last * HEAD]).astype(jnp.bfloat16)
                values = dot_nt(wkvt[first * HEAD : last * HEAD, :], latent).astype(jnp.bfloat16)
                for h in range(first, last):
                    at = (h - first) * HEAD
                    xs[h] = keys[:, at : at + HEAD]
                    vt[h] = values[at + NOPE : at + HEAD, :]

        for j in range(q_blocks):
            needed, whole = kinds[j]

            @pl.when(needed & whole)
            def _():
                pair(j, False)

            @pl.when(needed & jnp.logical_not(whole))
            def _():
                bias[...] = mask_bias(key_block, own[j], starts, block_rows, True)
                pair(j, True)

        return carry

    lax.fori_loop(0, blocks, step, 0)
    for j in range(q_blocks):
        here = pl.ds(j * block_rows, block_rows)
        for first, last in head_groups(heads):
            parts = []
            for h in range(first, last):
                parts.append(acc[j, h] * (1.0 / total[j, h]))
                u_out[j, h : h + 1, :] = top[j, h] + jnp.log2(total[j, h]) * (1.0 / EXP2_SCALE)
            if len(parts) == 1:
                parts.append(jnp.zeros_like(parts[0]))
            both = jnp.concatenate(parts, axis=0).T
            width = (last - first) * VDIM
            o_out[here, first * VDIM : first * VDIM + width] = both[:, :width]
            ob_out[here, first * VDIM : first * VDIM + width] = both[:, :width].astype(jnp.bfloat16)


def attention_forward(meta, cq, wqb, lat, wkvb, cos, sin, block_rows, seqs):
    heads = wkvb.shape[1] // HEAD
    blocks = lat.shape[0] // block_rows
    rows = cq.shape[0]
    q_blocks = rows // block_rows
    vmem = pl.BlockSpec(memory_space=pltpu.VMEM)
    pairs = q_blocks * blocks * heads // 2
    return pl.pallas_call(
        functools.partial(forward_kernel, blocks, heads, seqs),
        out_shape=(
            jax.ShapeDtypeStruct((q_blocks, heads, block_rows, WIDE), jnp.bfloat16),
            jax.ShapeDtypeStruct((rows, heads * VDIM), jnp.float32),
            jax.ShapeDtypeStruct((rows, heads * VDIM), jnp.bfloat16),
            jax.ShapeDtypeStruct((q_blocks, 16 * -(-heads // 16), block_rows), jnp.float32),
        ),
        in_specs=[pl.BlockSpec(memory_space=pltpu.SMEM)] + [vmem] * 6,
        out_specs=(vmem,) * 4,
        scratch_shapes=[
            pltpu.VMEM((heads * HEAD, KVR), jnp.bfloat16),
            pltpu.VMEM((heads, block_rows, HEAD), jnp.bfloat16),
            pltpu.VMEM((block_rows, HEAD), jnp.bfloat16),
            pltpu.VMEM((heads, VDIM, block_rows), jnp.bfloat16),
            pltpu.VMEM((q_blocks, heads, 1, block_rows), jnp.float32),
            pltpu.VMEM((q_blocks, heads, 1, block_rows), jnp.float32),
            pltpu.VMEM((q_blocks, heads, VDIM, block_rows), jnp.float32),
            pltpu.VMEM((block_rows, block_rows), jnp.float32),
        ],
        compiler_params=pltpu.CompilerParams(vmem_limit_bytes=VMEM_LIMIT),
        cost_estimate=pl.CostEstimate(
            flops=pairs * 4 * block_rows * block_rows * WIDE,
            bytes_accessed=16 * 1024 * 1024,
            transcendentals=pairs * block_rows * block_rows,
        ),
        name="attention_forward",
    )(meta, cq, wqb, lat, wkvb, cos, sin)


def three_terms(column):
    first = column.astype(jnp.bfloat16).astype(jnp.float32)
    rest = column - first
    second = rest.astype(jnp.bfloat16).astype(jnp.float32)
    return first, second, rest - second


def fold_in(tile, column, lane):
    for k, term in enumerate(three_terms(column)):
        tile = jnp.where(lane == FOLD_AT + k, term, tile)
    return tile


def backward_kernel(
    blocks, heads, seqs, meta, qx, u_in, o_in, dob, lat, wkvb, cos, sin, dq_out, dlat, gkvb,
    xs, xr, qo, qt, dt, dq, dkv, dkpe, gsum, bias,
):
    block_rows = bias.shape[0]
    q_blocks = qx.shape[0]
    starts = [meta[blocks + s] for s in range(seqs)]
    own = [meta[blocks + seqs + j] for j in range(q_blocks)]
    lane = lax.broadcasted_iota(jnp.int32, (block_rows, HEAD), 1)
    for j in range(q_blocks):
        here = pl.ds(j * block_rows, block_rows)
        logs = u_in[j].T
        for first, last in head_groups(heads):
            d_pair = dob[here, first * VDIM : first * VDIM + HEAD].astype(jnp.float32)
            weighted = d_pair * o_in[here, first * VDIM : first * VDIM + HEAD]
            turned = pltpu.roll(d_pair, VDIM, 1)
            for h in range(first, last):
                mine = lane < VDIM if h == first else lane >= VDIM
                delta = jnp.sum(jnp.where(mine, weighted, 0.0), axis=1, keepdims=True)
                d_head = jnp.where(lane >= VDIM, turned if h == first else d_pair, 0.0)
                q_first = qx[j, h, :, :HEAD].astype(jnp.float32)
                q_second = qx[j, h, :, HEAD:].astype(jnp.float32)
                qo[j, h, :block_rows, :HEAD] = qx[j, h, :, :HEAD]
                qo[j, h, :block_rows, HEAD:] = fold_in(q_second, -logs[:, h : h + 1], lane).astype(
                    jnp.bfloat16
                )
                qo[j, h, block_rows:, :HEAD] = d_head.astype(jnp.bfloat16)
                qo[j, h, block_rows:, HEAD:] = fold_in(
                    jnp.zeros((block_rows, HEAD), jnp.float32), -delta, lane
                ).astype(jnp.bfloat16)
                qt[j, h, :NOPE, :] = q_first.T[:NOPE, :].astype(jnp.bfloat16)
                qt[j, h, NOPE:, :] = q_second.T[:ROPE, :].astype(jnp.bfloat16)
                dt[j, h] = d_head.T[VDIM:, :].astype(jnp.bfloat16)
    dq[...] = jnp.zeros(dq.shape, jnp.float32)
    gsum[...] = jnp.zeros(gsum.shape, jnp.float32)

    def pair(j, masked):
        def one(h):
            keys = jnp.concatenate([xs[h], xr[...]], axis=1)
            both = dot_nt(qo[j, h], keys)
            scores = both[:block_rows] * EXP2_SCALE
            if masked:
                scores = scores + bias[...]
            probs = jnp.exp2(scores)
            d_scores = (probs * both[block_rows:]).astype(jnp.bfloat16)
            dq[j, h] += dot_nn(d_scores, keys)
            d_keys = dot_nn(qt[j, h], d_scores)
            dkv[h, :NOPE, :] += d_keys[:NOPE]
            dkpe[...] += d_keys[NOPE:]
            dkv[h, NOPE:, :] += dot_nn(dt[j, h], probs.astype(jnp.bfloat16))

        for h in range(heads):
            one(h)

    def step(r, carry):
        key_block = meta[r]
        kinds = [pair_kind(key_block, own[j], starts, block_rows) for j in range(q_blocks)]
        wanted = functools.reduce(jnp.logical_or, [k[0] for k in kinds])
        here = pl.ds(pl.multiple_of(r * block_rows, block_rows), block_rows)

        @pl.when(wanted)
        def _():
            latent = lat[here, :KVR]
            xr[...] = shared_key_tile(lat[here, KVR : KVR + ROPE], block_rows)
            for first, last in head_groups(heads):
                keys = dot_nn(latent, wkvb[:, first * HEAD : last * HEAD]).astype(jnp.bfloat16)
                for h in range(first, last):
                    xs[h] = keys[:, (h - first) * HEAD : (h - first + 1) * HEAD]
            dkv[...] = jnp.zeros(dkv.shape, jnp.float32)
            dkpe[...] = jnp.zeros(dkpe.shape, jnp.float32)

        for j in range(q_blocks):
            needed, whole = kinds[j]

            @pl.when(needed & whole)
            def _():
                pair(j, False)

            @pl.when(needed & jnp.logical_not(whole))
            def _():
                bias[...] = mask_bias(key_block, own[j], starts, block_rows, False)
                pair(j, True)

        @pl.when(wanted)
        def _():
            latent = lat[here, :KVR]
            d_latent = jnp.zeros((KVR, block_rows), jnp.float32)
            for h in range(heads):
                d_head = jnp.concatenate(
                    [dkv[h, :NOPE, :] * SCORE_SCALE, dkv[h, NOPE:, :]], axis=0
                ).astype(jnp.bfloat16)
                d_latent += dot_nn(wkvb[:, h * HEAD : (h + 1) * HEAD], d_head)
                gsum[h * HEAD : (h + 1) * HEAD, :] += dot_nn(d_head, latent)
            dlat[here, :KVR] = d_latent.T.astype(jnp.bfloat16)
            rope = jnp.concatenate(
                [dkpe[...] * SCORE_SCALE, jnp.zeros((HEAD - ROPE, block_rows), jnp.float32)], axis=0
            )
            dlat[here, KVR:] = rope.T[:, :ROPE].astype(jnp.bfloat16)

        @pl.when(jnp.logical_not(wanted))
        def _():
            dlat[here, :] = jnp.zeros((block_rows, KVR + ROPE), jnp.bfloat16)

        return carry

    lax.fori_loop(0, blocks, step, 0)
    for h in range(heads):
        gkvb[:, h * HEAD : (h + 1) * HEAD] = gsum[h * HEAD : (h + 1) * HEAD, :].T.astype(
            jnp.bfloat16
        )
    for j in range(q_blocks):
        here = pl.ds(j * block_rows, block_rows)
        cos_j, sin_j = cos[here, :], sin[here, :]
        for h in range(heads):
            nope = jnp.where(lane < NOPE, dq[j, h, :, :HEAD], 0.0)
            rope = dq[j, h, :, HEAD:]
            shifted = rope * sin_j
            left = pltpu.roll(shifted, HEAD - ROPE // 2, 1)
            right = pltpu.roll(shifted, ROPE // 2, 1)
            swapped = jnp.where(lane < ROPE // 2, left, jnp.where(lane < ROPE, -right, 0.0))
            back = pltpu.roll(rope * cos_j + swapped, NOPE, 1)
            dq_out[here, h * HEAD : (h + 1) * HEAD] = ((nope + back) * SCORE_SCALE).astype(
                jnp.bfloat16
            )


def attention_backward(meta, qx, u_in, o_in, dob, lat, wkvb, cos, sin, block_rows, seqs):
    heads = wkvb.shape[1] // HEAD
    blocks = lat.shape[0] // block_rows
    q_blocks = qx.shape[0]
    rows = q_blocks * block_rows
    odd = -(heads * VDIM) % HEAD
    if odd:
        o_in = jnp.pad(o_in, ((0, 0), (0, odd)))
        dob = jnp.pad(dob, ((0, 0), (0, odd)))
    vmem = pl.BlockSpec(memory_space=pltpu.VMEM)
    pairs = q_blocks * blocks * heads // 2
    return pl.pallas_call(
        functools.partial(backward_kernel, blocks, heads, seqs),
        out_shape=(
            jax.ShapeDtypeStruct((rows, heads * HEAD), jnp.bfloat16),
            jax.ShapeDtypeStruct((lat.shape[0], KVR + ROPE), jnp.bfloat16),
            jax.ShapeDtypeStruct((KVR, heads * HEAD), jnp.bfloat16),
        ),
        in_specs=[pl.BlockSpec(memory_space=pltpu.SMEM)] + [vmem] * 8,
        out_specs=(vmem,) * 3,
        scratch_shapes=[
            pltpu.VMEM((heads, block_rows, HEAD), jnp.bfloat16),
            pltpu.VMEM((block_rows, HEAD), jnp.bfloat16),
            pltpu.VMEM((q_blocks, heads, 2 * block_rows, WIDE), jnp.bfloat16),
            pltpu.VMEM((q_blocks, heads, NOPE + ROPE, block_rows), jnp.bfloat16),
            pltpu.VMEM((q_blocks, heads, VDIM, block_rows), jnp.bfloat16),
            pltpu.VMEM((q_blocks, heads, block_rows, WIDE), jnp.float32),
            pltpu.VMEM((heads, HEAD, block_rows), jnp.float32),
            pltpu.VMEM((ROPE, block_rows), jnp.float32),
            pltpu.VMEM((heads * HEAD, KVR), jnp.float32),
            pltpu.VMEM((block_rows, block_rows), jnp.float32),
        ],
        compiler_params=pltpu.CompilerParams(vmem_limit_bytes=VMEM_LIMIT),
        cost_estimate=pl.CostEstimate(
            flops=pairs * 8 * block_rows * block_rows * WIDE,
            bytes_accessed=24 * 1024 * 1024,
            transcendentals=pairs * block_rows * block_rows,
        ),
        name="attention_backward",
    )(meta, qx, u_in, o_in, dob, lat, wkvb, cos, sin)


def dot_plain(left_op, right_op):
    return jnp.dot(left_op, right_op, preferred_element_type=jnp.float32)


def dot_rows(left_op, right_op):
    return lax.dot_general(
        left_op, right_op, (((0,), (0,)), ((), ())), preferred_element_type=jnp.float32
    )


def dot_cols(left_op, right_op):
    return lax.dot_general(
        left_op, right_op, (((1,), (1,)), ((), ())), preferred_element_type=jnp.float32
    )


def rms_scale(values):
    return lax.rsqrt(jnp.mean(values * values, axis=-1, keepdims=True) + EPSILON)


def rms_back(incoming, values, inv_rms, gain_vec):
    weighted = incoming * gain_vec
    d_values = inv_rms * weighted - values * inv_rms**3 * jnp.mean(
        weighted * values, axis=-1, keepdims=True
    )
    return (d_values, jnp.sum(incoming * values * inv_rms, axis=0))


def token_places(block_map, doc_lengths, per_device, devices):
    all_rows = per_device * devices
    half_block = per_device // 2
    token_rows = jnp.arange(all_rows, dtype=jnp.int32)
    device_of = token_rows // per_device
    within = token_rows % per_device
    wanted = device_of * 2 + within // half_block
    select = wanted[:, None] == jnp.arange(2 * devices, dtype=jnp.int32)[None, :]
    blocks = jnp.sum(jnp.where(select, block_map.reshape(-1)[None, :], 0), axis=1)
    places = blocks * half_block + within % half_block
    ends = jnp.cumsum(doc_lengths)
    segment = jnp.sum((places[:, None] >= ends[None, :]).astype(jnp.int32), axis=1)
    starts = ends - doc_lengths
    picked = segment[:, None] == jnp.arange(doc_lengths.shape[0], dtype=jnp.int32)[None, :]
    begins = jnp.sum(jnp.where(picked, starts[None, :], 0), axis=1)
    return (places, segment, places - begins)


def tables(inside):
    half_width = ROPE // 2
    frequency = ROPE_BASE ** (-2.0 * jnp.arange(half_width, dtype=jnp.float32) / ROPE)
    angles = inside.astype(jnp.float32)[:, None] * frequency[None, :]
    cosine_table = jnp.concatenate([jnp.cos(angles), jnp.cos(angles)], axis=1)
    sine_table = jnp.concatenate([jnp.sin(angles), jnp.sin(angles)], axis=1)
    return (cosine_table, sine_table)


def rotate(values, cosine_table, sine_table):
    half_width = values.shape[-1] // 2
    turned = jnp.concatenate([-values[..., half_width:], values[..., :half_width]], axis=-1)
    return values * cosine_table + turned * sine_table


def rotate_back(incoming, cosine_table, sine_table):
    half_width = incoming.shape[-1] // 2
    shifted = incoming * sine_table
    turned = jnp.concatenate([shifted[..., half_width:], -shifted[..., :half_width]], axis=-1)
    return incoming * cosine_table + turned


def wide_tables(inside):
    cosine_table, sine_table = tables(inside)
    rest = ((0, 0), (0, HEAD - ROPE))
    return cosine_table, sine_table, jnp.pad(cosine_table, rest), jnp.pad(sine_table, rest)


def sum_over_ctx(grad):
    return lax.psum_scatter(
        grad.astype(jnp.bfloat16), "ctx", scatter_dimension=0, tiled=True
    ).astype(jnp.float32)


def on_device(
    tokens_in,
    w_qa,
    w_kva,
    w_qb,
    w_kvb,
    w_out,
    w_gate,
    w_up,
    w_down,
    gain_in,
    gain_q,
    gain_kv,
    gain_mid,
    cotangent,
    block_map,
    doc_lengths,
):
    local_rows = tokens_in.shape[0]
    half_rows = local_rows // 2
    devices = lax.axis_size("ctx")
    ctx_index = lax.axis_index("ctx")
    seqs = doc_lengths.shape[0]
    own_blocks = lax.dynamic_slice_in_dim(block_map, ctx_index, 1, 0)[0]
    ends = jnp.cumsum(doc_lengths)
    starts = ends - doc_lengths
    meta = jnp.concatenate([block_map.reshape(-1), starts, own_blocks])
    within = jnp.arange(half_rows, dtype=jnp.int32)
    query_place = (own_blocks[:, None] * half_rows + within[None, :]).reshape(-1)
    began = jnp.max(
        jnp.where(starts[None, :] <= query_place[:, None], starts[None, :], 0), axis=1
    )
    cosine_table, sine_table, cosine_wide, sine_wide = wide_tables(query_place - began)
    head_count = w_qb.shape[1] // (NOPE + ROPE)
    w_qb_wide = jnp.pad(
        w_qb.reshape(-1, head_count, NOPE + ROPE), ((0, 0), (0, 0), (0, HEAD - NOPE - ROPE))
    ).reshape(-1, head_count * HEAD)
    tokens_f = tokens_in.astype(jnp.float32)
    scale_in = rms_scale(tokens_f)
    normed_in = (tokens_f * scale_in * gain_in).astype(jnp.bfloat16)
    kv_input = dot_plain(normed_in, w_kva)
    latent_raw = kv_input[:, :KVR]
    scale_kv = rms_scale(latent_raw)
    latent = (latent_raw * scale_kv * gain_kv).astype(jnp.bfloat16)
    key_rope = rotate(kv_input[:, KVR:], cosine_table, sine_table).astype(jnp.bfloat16)
    latents = lax.all_gather(
        jnp.concatenate([latent, key_rope], axis=1), "ctx", axis=0, tiled=True
    )
    q_latent_pre = dot_plain(normed_in, w_qa)
    scale_q = rms_scale(q_latent_pre)
    q_latent = (q_latent_pre * scale_q * gain_q).astype(jnp.bfloat16)
    queries, attn_f, heads_out, log_totals = attention_forward(
        meta, q_latent, w_qb_wide, latents, w_kvb, cosine_wide, sine_wide, half_rows, seqs
    )
    attention = lax.psum(dot_cols(heads_out, w_out).astype(jnp.bfloat16), "tp").astype(jnp.float32)
    middle = tokens_f + RESIDUAL_SCALE * attention
    scale_mid = rms_scale(middle)
    normed_mid = (middle * scale_mid * gain_mid).astype(jnp.bfloat16)
    gate_val = dot_plain(normed_mid, w_gate)
    up_val = dot_plain(normed_mid, w_up)
    sig_gate = jax.nn.sigmoid(gate_val)
    silu_gate = gate_val * sig_gate
    activation = (silu_gate * up_val).astype(jnp.bfloat16)
    feed_out = lax.psum(dot_cols(activation, w_down).astype(jnp.bfloat16), "tp").astype(jnp.float32)
    out = (middle + RESIDUAL_SCALE * feed_out).astype(jnp.bfloat16)
    cotangent_f = cotangent.astype(jnp.float32)
    d_feed = (RESIDUAL_SCALE * cotangent_f).astype(jnp.bfloat16)
    gw_down = dot_rows(d_feed, activation)
    d_activation = dot_plain(d_feed, w_down)
    d_gate = (d_activation * up_val * sig_gate * (1.0 + gate_val * (1.0 - sig_gate))).astype(
        jnp.bfloat16
    )
    d_up = (d_activation * silu_gate).astype(jnp.bfloat16)
    gw_gate = dot_rows(normed_mid, d_gate)
    gw_up = dot_rows(normed_mid, d_up)
    d_normed_mid = lax.psum(
        (dot_cols(d_gate, w_gate) + dot_cols(d_up, w_up)).astype(jnp.bfloat16), "tp"
    ).astype(jnp.float32)
    d_middle_norm, d_gain_mid = rms_back(d_normed_mid, middle, scale_mid, gain_mid)
    d_middle = cotangent_f + d_middle_norm
    d_attention = (RESIDUAL_SCALE * d_middle).astype(jnp.bfloat16)
    gw_out = dot_rows(d_attention, heads_out)
    d_heads = dot_plain(d_attention, w_out).astype(jnp.bfloat16)
    d_query_pre, d_latents, gw_kvb = attention_backward(
        meta, queries, log_totals, attn_f, d_heads, latents, w_kvb, cosine_wide, sine_wide,
        half_rows, seqs,
    )
    d_latent_part = lax.psum_scatter(d_latents, "ctx", scatter_dimension=0, tiled=True)
    gw_qb = dot_rows(q_latent, d_query_pre)
    d_q_latent = dot_cols(d_query_pre, w_qb_wide).astype(jnp.bfloat16)
    summed_tp = lax.psum(jnp.concatenate([d_q_latent, d_latent_part], axis=1), "tp").astype(
        jnp.float32
    )
    q_rank = w_qa.shape[1]
    d_q_latent = summed_tp[:, :q_rank]
    d_latent = summed_tp[:, q_rank : q_rank + KVR]
    d_rope_sum = summed_tp[:, q_rank + KVR :]
    d_q_pre, d_gain_q = rms_back(d_q_latent, q_latent_pre, scale_q, gain_q)
    d_q_low = d_q_pre.astype(jnp.bfloat16)
    d_latent_raw, d_gain_kv = rms_back(d_latent, latent_raw, scale_kv, gain_kv)
    d_kv_input = jnp.concatenate(
        [d_latent_raw, rotate_back(d_rope_sum, cosine_table, sine_table)], axis=-1
    ).astype(jnp.bfloat16)
    gw_qa = dot_rows(normed_in, d_q_low)
    gw_kva = dot_rows(normed_in, d_kv_input)
    d_normed_in = dot_cols(d_q_low, w_qa) + dot_cols(d_kv_input, w_kva)
    d_tokens_norm, d_gain_in = rms_back(d_normed_in, tokens_f, scale_in, gain_in)
    grad_in = d_middle + d_tokens_norm
    gw_qb_own = sum_over_ctx(gw_qb)
    gw_qb_own = gw_qb_own.reshape(-1, head_count, HEAD)[..., : NOPE + ROPE].reshape(
        -1, head_count * (NOPE + ROPE)
    )
    return (
        out,
        grad_in,
        sum_over_ctx(gw_qa),
        sum_over_ctx(gw_kva),
        gw_qb_own,
        sum_over_ctx(gw_kvb),
        sum_over_ctx(gw_out),
        sum_over_ctx(gw_gate),
        sum_over_ctx(gw_up),
        sum_over_ctx(gw_down),
        sum_over_ctx(d_gain_in),
        sum_over_ctx(d_gain_q),
        sum_over_ctx(d_gain_kv),
        sum_over_ctx(d_gain_mid),
    )


def solution(mesh):
    return jax.shard_map(
        on_device,
        mesh=mesh,
        in_specs=(
            P("ctx", None),
            P(),
            P(),
            P(None, "tp"),
            P(None, "tp"),
            P(None, "tp"),
            P(None, "tp"),
            P(None, "tp"),
            P(None, "tp"),
            P(),
            P(),
            P(),
            P(),
            P("ctx", None),
            P(),
            P(),
        ),
        out_specs=(
            P("ctx", None),
            P("ctx", None),
            P("ctx", None),
            P("ctx", None),
            P("ctx", "tp"),
            P("ctx", "tp"),
            P("ctx", "tp"),
            P("ctx", "tp"),
            P("ctx", "tp"),
            P("ctx", "tp"),
            P("ctx"),
            P("ctx"),
            P("ctx"),
            P("ctx"),
        ),
        check_vma=False,
    )
```

```python
import functools
import math

import jax
import jax.numpy as jnp
from jax import lax
from jax.experimental import pallas as pl
from jax.experimental.pallas import tpu as pltpu
from jax.sharding import PartitionSpec as P

KVR = 256
NOPE = 64
ROPE = 32
VDIM = 64
HEAD = NOPE + VDIM
WIDE = 2 * HEAD
MASKED = -1e30
SCORE_SCALE = (NOPE + ROPE) ** (-0.5)
EXP2_SCALE = SCORE_SCALE * math.log2(math.e)
FOLD_AT = 96
VMEM_LIMIT = 56 * 1024 * 1024

EPSILON = 1e-05
ROPE_BASE = 10000.0
RESIDUAL_SCALE = 1.4 / math.sqrt(62.0)


def dot_nn(left_op, right_op):
    return jnp.dot(left_op, right_op, preferred_element_type=jnp.float32)


def dot_nt(left_op, right_op):
    return lax.dot_general(
        left_op, right_op, (((1,), (1,)), ((), ())), preferred_element_type=jnp.float32
    )


def begin_of(place, starts):
    begin = jnp.zeros_like(place)
    for start in starts:
        begin = jnp.where(start <= place, start, begin)
    return begin


def pair_kind(key_block, query_block, starts, block_rows):
    key_first = key_block * block_rows
    query_first = query_block * block_rows
    early = begin_of(query_first, starts)
    late = begin_of(query_first + block_rows - 1, starts)
    needed = (key_block <= query_block) & (key_first + block_rows - 1 >= early)
    whole = (key_block < query_block) & (late <= key_first)
    return needed, whole


def mask_bias(key_block, query_block, starts, block_rows, keys_first):
    key_dim = 0 if keys_first else 1
    shape = (block_rows, block_rows)
    key_place = key_block * block_rows + lax.broadcasted_iota(jnp.int32, shape, key_dim)
    query_place = query_block * block_rows + lax.broadcasted_iota(jnp.int32, shape, 1 - key_dim)
    begin = jnp.zeros(shape, jnp.int32)
    for start in starts:
        begin = jnp.where(start <= query_place, start, begin)
    allowed = (key_place <= query_place) & (key_place >= begin)
    return jnp.where(allowed, 0.0, MASKED)


def shared_key_tile(rope_rows, block_rows):
    place = lax.broadcasted_iota(jnp.int32, (ROPE, HEAD), 0)
    lane = lax.broadcasted_iota(jnp.int32, (ROPE, HEAD), 1)
    eye = jnp.where(place == lane, 1.0, 0.0).astype(jnp.bfloat16)
    tile = dot_nn(rope_rows, eye)
    lanes = lax.broadcasted_iota(jnp.int32, (block_rows, HEAD), 1)
    ones = (lanes >= FOLD_AT) & (lanes < FOLD_AT + 3)
    return jnp.where(ones, 1.0, tile).astype(jnp.bfloat16)


def head_window(h):
    at = h * (NOPE + ROPE)
    return at // HEAD * HEAD, at % HEAD


def window_columns(heads):
    return head_window(heads - 1)[0] + WIDE


def head_groups(heads):
    return [(h, min(h + 2, heads)) for h in range(0, heads, 2)]


def forward_kernel(
    blocks, heads, seqs, meta, cq, wqb, lat, wkvb, cos, sin, qx, o_out, ob_out, u_out,
    wkvt, xs, xr, vt, top, total, acc, bias, pre,
):
    rows_all = cq.shape[0]
    block_rows = bias.shape[0]
    q_blocks = rows_all // block_rows
    starts = [meta[blocks + s] for s in range(seqs)]
    own = [meta[blocks + seqs + j] for j in range(q_blocks)]
    for first, last in head_groups(heads):
        wkvt[first * HEAD : last * HEAD, :] = (
            wkvb[:, first * HEAD : last * HEAD].astype(jnp.float32).T.astype(jnp.bfloat16)
        )
    lane = lax.broadcasted_iota(jnp.int32, (block_rows, HEAD), 1)
    for j in range(q_blocks):
        here = pl.ds(j * block_rows, block_rows)
        cos_j, sin_j = cos[here, :], sin[here, :]
        width = heads * (NOPE + ROPE)
        for at in range(0, width, WIDE):
            end = min(at + WIDE, width)
            pre[:, at:end] = dot_nn(cq[here, :], wqb[:, at:end])
        for h in range(heads):
            at, shift = head_window(h)
            own_part = pltpu.roll(pre[:, at : at + WIDE], (WIDE - shift) % WIDE, 1)[:, :HEAD]
            turned = pltpu.roll(own_part, NOPE, 1)
            left = pltpu.roll(turned, HEAD - ROPE // 2, 1)
            right = pltpu.roll(turned, ROPE // 2, 1)
            swapped = jnp.where(lane < ROPE // 2, -left, right)
            rope = jnp.where(lane < ROPE, turned * cos_j + swapped * sin_j, 0.0)
            qx[j, h, :, :HEAD] = jnp.where(lane < NOPE, own_part, 0.0).astype(jnp.bfloat16)
            qx[j, h, :, HEAD:] = rope.astype(jnp.bfloat16)
    top[...] = jnp.full(top.shape, MASKED, jnp.float32)
    total[...] = jnp.zeros(total.shape, jnp.float32)
    acc[...] = jnp.zeros(acc.shape, jnp.float32)

    def pair(j, masked):
        def one(h):
            keys = jnp.concatenate([xs[h], xr[...]], axis=1)
            scores = dot_nt(keys, qx[j, h])
            if masked:
                scores = scores + bias[...]
            old = top[j, h]
            new = jnp.maximum(old, jnp.max(scores, axis=0, keepdims=True))
            fade = jnp.exp2((old - new) * EXP2_SCALE)
            terms = jnp.exp2((scores - new) * EXP2_SCALE)
            top[j, h] = new
            total[j, h] = fade * total[j, h] + jnp.sum(terms, axis=0, keepdims=True)
            acc[j, h] = fade * acc[j, h] + dot_nn(vt[h], terms.astype(jnp.bfloat16))

        for h in range(heads):
            one(h)

    def step(r, carry):
        key_block = meta[r]
        kinds = [pair_kind(key_block, own[j], starts, block_rows) for j in range(q_blocks)]
        wanted = functools.reduce(jnp.logical_or, [k[0] for k in kinds])

        @pl.when(wanted)
        def _():
            here = pl.ds(pl.multiple_of(r * block_rows, block_rows), block_rows)
            latent = lat[here, :KVR]
            xr[...] = shared_key_tile(lat[here, KVR : KVR + ROPE], block_rows)
            for first, last in head_groups(heads):
                keys = dot_nn(latent, wkvb[:, first * HEAD : last * HEAD]).astype(jnp.bfloat16)
                values = dot_nt(wkvt[first * HEAD : last * HEAD, :], latent).astype(jnp.bfloat16)
                for h in range(first, last):
                    at = (h - first) * HEAD
                    xs[h] = keys[:, at : at + HEAD]
                    vt[h] = values[at + NOPE : at + HEAD, :]

        for j in range(q_blocks):
            needed, whole = kinds[j]

            @pl.when(needed & whole)
            def _():
                pair(j, False)

            @pl.when(needed & jnp.logical_not(whole))
            def _():
                bias[...] = mask_bias(key_block, own[j], starts, block_rows, True)
                pair(j, True)

        return carry

    lax.fori_loop(0, blocks, step, 0)
    for j in range(q_blocks):
        here = pl.ds(j * block_rows, block_rows)
        for first, last in head_groups(heads):
            parts = []
            for h in range(first, last):
                parts.append(acc[j, h] * (1.0 / total[j, h]))
                u_out[j, h : h + 1, :] = top[j, h] + jnp.log2(total[j, h]) * (1.0 / EXP2_SCALE)
            if len(parts) == 1:
                parts.append(jnp.zeros_like(parts[0]))
            both = jnp.concatenate(parts, axis=0).T
            width = (last - first) * VDIM
            o_out[here, first * VDIM : first * VDIM + width] = both[:, :width]
            ob_out[here, first * VDIM : first * VDIM + width] = both[:, :width].astype(jnp.bfloat16)


def attention_forward(meta, cq, wqb, lat, wkvb, cos, sin, block_rows, seqs):
    heads = wkvb.shape[1] // HEAD
    blocks = lat.shape[0] // block_rows
    rows = cq.shape[0]
    q_blocks = rows // block_rows
    vmem = pl.BlockSpec(memory_space=pltpu.VMEM)
    pairs = q_blocks * blocks * heads // 2
    return pl.pallas_call(
        functools.partial(forward_kernel, blocks, heads, seqs),
        out_shape=(
            jax.ShapeDtypeStruct((q_blocks, heads, block_rows, WIDE), jnp.bfloat16),
            jax.ShapeDtypeStruct((rows, heads * VDIM), jnp.float32),
            jax.ShapeDtypeStruct((rows, heads * VDIM), jnp.bfloat16),
            jax.ShapeDtypeStruct((q_blocks, 16 * -(-heads // 16), block_rows), jnp.float32),
        ),
        in_specs=[pl.BlockSpec(memory_space=pltpu.SMEM)] + [vmem] * 6,
        out_specs=(vmem,) * 4,
        scratch_shapes=[
            pltpu.VMEM((heads * HEAD, KVR), jnp.bfloat16),
            pltpu.VMEM((heads, block_rows, HEAD), jnp.bfloat16),
            pltpu.VMEM((block_rows, HEAD), jnp.bfloat16),
            pltpu.VMEM((heads, VDIM, block_rows), jnp.bfloat16),
            pltpu.VMEM((q_blocks, heads, 1, block_rows), jnp.float32),
            pltpu.VMEM((q_blocks, heads, 1, block_rows), jnp.float32),
            pltpu.VMEM((q_blocks, heads, VDIM, block_rows), jnp.float32),
            pltpu.VMEM((block_rows, block_rows), jnp.float32),
            pltpu.VMEM((block_rows, window_columns(heads)), jnp.float32),
        ],
        compiler_params=pltpu.CompilerParams(vmem_limit_bytes=VMEM_LIMIT),
        cost_estimate=pl.CostEstimate(
            flops=pairs * 4 * block_rows * block_rows * WIDE,
            bytes_accessed=16 * 1024 * 1024,
            transcendentals=pairs * block_rows * block_rows,
        ),
        name="attention_forward",
    )(meta, cq, wqb, lat, wkvb, cos, sin)


def three_terms(column):
    first = column.astype(jnp.bfloat16).astype(jnp.float32)
    rest = column - first
    second = rest.astype(jnp.bfloat16).astype(jnp.float32)
    return first, second, rest - second


def fold_in(tile, column, lane):
    for k, term in enumerate(three_terms(column)):
        tile = jnp.where(lane == FOLD_AT + k, term, tile)
    return tile


def backward_kernel(
    blocks, heads, seqs, meta, qx, u_in, o_in, dob, lat, wkvb, cos, sin, dq_out, dlat, gkvb,
    xs, xr, qo, qt, dt, dq, dkv, dkpe, gsum, bias, flat,
):
    block_rows = bias.shape[0]
    q_blocks = qx.shape[0]
    starts = [meta[blocks + s] for s in range(seqs)]
    own = [meta[blocks + seqs + j] for j in range(q_blocks)]
    lane = lax.broadcasted_iota(jnp.int32, (block_rows, HEAD), 1)
    for j in range(q_blocks):
        here = pl.ds(j * block_rows, block_rows)
        logs = u_in[j].T
        for first, last in head_groups(heads):
            d_pair = dob[here, first * VDIM : first * VDIM + HEAD].astype(jnp.float32)
            weighted = d_pair * o_in[here, first * VDIM : first * VDIM + HEAD]
            turned = pltpu.roll(d_pair, VDIM, 1)
            for h in range(first, last):
                mine = lane < VDIM if h == first else lane >= VDIM
                delta = jnp.sum(jnp.where(mine, weighted, 0.0), axis=1, keepdims=True)
                d_head = jnp.where(lane >= VDIM, turned if h == first else d_pair, 0.0)
                q_first = qx[j, h, :, :HEAD].astype(jnp.float32)
                q_second = qx[j, h, :, HEAD:].astype(jnp.float32)
                qo[j, h, :block_rows, :HEAD] = qx[j, h, :, :HEAD]
                qo[j, h, :block_rows, HEAD:] = fold_in(q_second, -logs[:, h : h + 1], lane).astype(
                    jnp.bfloat16
                )
                qo[j, h, block_rows:, :HEAD] = d_head.astype(jnp.bfloat16)
                qo[j, h, block_rows:, HEAD:] = fold_in(
                    jnp.zeros((block_rows, HEAD), jnp.float32), -delta, lane
                ).astype(jnp.bfloat16)
                qt[j, h, :NOPE, :] = q_first.T[:NOPE, :].astype(jnp.bfloat16)
                qt[j, h, NOPE:, :] = q_second.T[:ROPE, :].astype(jnp.bfloat16)
                dt[j, h] = d_head.T[VDIM:, :].astype(jnp.bfloat16)
    dq[...] = jnp.zeros(dq.shape, jnp.float32)
    gsum[...] = jnp.zeros(gsum.shape, jnp.float32)

    def pair(j, masked):
        def one(h):
            keys = jnp.concatenate([xs[h], xr[...]], axis=1)
            both = dot_nt(qo[j, h], keys)
            scores = both[:block_rows] * EXP2_SCALE
            if masked:
                scores = scores + bias[...]
            probs = jnp.exp2(scores)
            d_scores = (probs * both[block_rows:]).astype(jnp.bfloat16)
            dq[j, h] += dot_nn(d_scores, keys)
            d_keys = dot_nn(qt[j, h], d_scores)
            dkv[h, :NOPE, :] += d_keys[:NOPE]
            dkpe[...] += d_keys[NOPE:]
            dkv[h, NOPE:, :] += dot_nn(dt[j, h], probs.astype(jnp.bfloat16))

        for h in range(heads):
            one(h)

    def step(r, carry):
        key_block = meta[r]
        kinds = [pair_kind(key_block, own[j], starts, block_rows) for j in range(q_blocks)]
        wanted = functools.reduce(jnp.logical_or, [k[0] for k in kinds])
        here = pl.ds(pl.multiple_of(r * block_rows, block_rows), block_rows)

        @pl.when(wanted)
        def _():
            latent = lat[here, :KVR]
            xr[...] = shared_key_tile(lat[here, KVR : KVR + ROPE], block_rows)
            for first, last in head_groups(heads):
                keys = dot_nn(latent, wkvb[:, first * HEAD : last * HEAD]).astype(jnp.bfloat16)
                for h in range(first, last):
                    xs[h] = keys[:, (h - first) * HEAD : (h - first + 1) * HEAD]
            dkv[...] = jnp.zeros(dkv.shape, jnp.float32)
            dkpe[...] = jnp.zeros(dkpe.shape, jnp.float32)

        for j in range(q_blocks):
            needed, whole = kinds[j]

            @pl.when(needed & whole)
            def _():
                pair(j, False)

            @pl.when(needed & jnp.logical_not(whole))
            def _():
                bias[...] = mask_bias(key_block, own[j], starts, block_rows, False)
                pair(j, True)

        @pl.when(wanted)
        def _():
            latent = lat[here, :KVR]
            d_latent = jnp.zeros((KVR, block_rows), jnp.float32)
            for h in range(heads):
                d_head = jnp.concatenate(
                    [dkv[h, :NOPE, :] * SCORE_SCALE, dkv[h, NOPE:, :]], axis=0
                ).astype(jnp.bfloat16)
                d_latent += dot_nn(wkvb[:, h * HEAD : (h + 1) * HEAD], d_head)
                gsum[h * HEAD : (h + 1) * HEAD, :] += dot_nn(d_head, latent)
            dlat[here, :KVR] = d_latent.T.astype(jnp.bfloat16)
            rope = jnp.concatenate(
                [dkpe[...] * SCORE_SCALE, jnp.zeros((HEAD - ROPE, block_rows), jnp.float32)], axis=0
            )
            dlat[here, KVR:] = rope.T[:, :ROPE].astype(jnp.bfloat16)

        @pl.when(jnp.logical_not(wanted))
        def _():
            dlat[here, :] = jnp.zeros((block_rows, KVR + ROPE), jnp.bfloat16)

        return carry

    lax.fori_loop(0, blocks, step, 0)
    for h in range(heads):
        gkvb[:, h * HEAD : (h + 1) * HEAD] = gsum[h * HEAD : (h + 1) * HEAD, :].T.astype(
            jnp.bfloat16
        )
    for j in range(q_blocks):
        here = pl.ds(j * block_rows, block_rows)
        cos_j, sin_j = cos[here, :], sin[here, :]
        flat[...] = jnp.zeros(flat.shape, jnp.float32)
        for h in range(heads):
            nope = jnp.where(lane < NOPE, dq[j, h, :, :HEAD], 0.0)
            rope = dq[j, h, :, HEAD:]
            shifted = rope * sin_j
            left = pltpu.roll(shifted, HEAD - ROPE // 2, 1)
            right = pltpu.roll(shifted, ROPE // 2, 1)
            swapped = jnp.where(lane < ROPE // 2, left, jnp.where(lane < ROPE, -right, 0.0))
            back = pltpu.roll(jnp.where(lane < ROPE, rope * cos_j + swapped, 0.0), NOPE, 1)
            whole = jnp.concatenate([(nope + back) * SCORE_SCALE, jnp.zeros_like(nope)], axis=1)
            at, shift = head_window(h)
            flat[:, at : at + WIDE] += pltpu.roll(whole, shift, 1)
        dq_out[here, :] = flat[:, : heads * (NOPE + ROPE)].astype(jnp.bfloat16)


def attention_backward(meta, qx, u_in, o_in, dob, lat, wkvb, cos, sin, block_rows, seqs):
    heads = wkvb.shape[1] // HEAD
    blocks = lat.shape[0] // block_rows
    q_blocks = qx.shape[0]
    rows = q_blocks * block_rows
    odd = -(heads * VDIM) % HEAD
    if odd:
        o_in = jnp.pad(o_in, ((0, 0), (0, odd)))
        dob = jnp.pad(dob, ((0, 0), (0, odd)))
    vmem = pl.BlockSpec(memory_space=pltpu.VMEM)
    pairs = q_blocks * blocks * heads // 2
    return pl.pallas_call(
        functools.partial(backward_kernel, blocks, heads, seqs),
        out_shape=(
            jax.ShapeDtypeStruct((rows, heads * (NOPE + ROPE)), jnp.bfloat16),
            jax.ShapeDtypeStruct((lat.shape[0], KVR + ROPE), jnp.bfloat16),
            jax.ShapeDtypeStruct((KVR, heads * HEAD), jnp.bfloat16),
        ),
        in_specs=[pl.BlockSpec(memory_space=pltpu.SMEM)] + [vmem] * 8,
        out_specs=(vmem,) * 3,
        scratch_shapes=[
            pltpu.VMEM((heads, block_rows, HEAD), jnp.bfloat16),
            pltpu.VMEM((block_rows, HEAD), jnp.bfloat16),
            pltpu.VMEM((q_blocks, heads, 2 * block_rows, WIDE), jnp.bfloat16),
            pltpu.VMEM((q_blocks, heads, NOPE + ROPE, block_rows), jnp.bfloat16),
            pltpu.VMEM((q_blocks, heads, VDIM, block_rows), jnp.bfloat16),
            pltpu.VMEM((q_blocks, heads, block_rows, WIDE), jnp.float32),
            pltpu.VMEM((heads, HEAD, block_rows), jnp.float32),
            pltpu.VMEM((ROPE, block_rows), jnp.float32),
            pltpu.VMEM((heads * HEAD, KVR), jnp.float32),
            pltpu.VMEM((block_rows, block_rows), jnp.float32),
            pltpu.VMEM((block_rows, window_columns(heads)), jnp.float32),
        ],
        compiler_params=pltpu.CompilerParams(vmem_limit_bytes=VMEM_LIMIT),
        cost_estimate=pl.CostEstimate(
            flops=pairs * 8 * block_rows * block_rows * WIDE,
            bytes_accessed=24 * 1024 * 1024,
            transcendentals=pairs * block_rows * block_rows,
        ),
        name="attention_backward",
    )(meta, qx, u_in, o_in, dob, lat, wkvb, cos, sin)


MESH = pl.DeviceIdType.MESH


class Scatter:
    def __init__(self, n, given=None, left=None, right=None):
        self.operands = [given] if given is not None else [left, right]
        self.is_given = given is not None
        self.rows = self.operands[0].shape[0] // n
        self.columns = self.operands[-1].shape[1]
        self.depth = 0 if self.is_given else right.shape[0]
        self.parts = 2 if self.rows % 32 == 0 else 1


def scatter_blocks(bits_left):
    chips = []
    for value in range(1 << len(bits_left)):
        chip = 0
        for at, bit in enumerate(bits_left):
            chip = chip + (((value >> at) & 1) << (bit - 1))
        chips.append(chip)
    return chips


def scatter_kernel(n, items, *refs):
    count = n.bit_length() - 1
    me = lax.axis_index("ctx")
    refs = list(refs)
    take = lambda k: [refs.pop(0) for _ in range(k)]
    inputs = [take(len(item.operands)) for item in items]
    outputs = take(len(items))
    held, sent, landed, core_sems, step_sems = [], [], [], [], []
    for item in items:
        held.append(refs.pop(0))
        sent.append(None if item.is_given else refs.pop(0))
        landed.append(take(count - 1))
        core_sems.append(take(2))
        step_sems.append([take(2) for _ in range(count - 1)])
    barrier = pltpu.get_barrier_semaphore()
    for bit in range(count):
        pl.semaphore_signal(barrier, inc=1, device_id={"ctx": me ^ (1 << bit)}, device_id_type=MESH)
    pl.semaphore_wait(barrier, count)
    core = me & 1
    chips = n // 2
    orders = (tuple(range(1, count)), tuple(range(count - 1, 0, -1)))

    def columns_of(item):
        return [(c, min(c + 512, item.columns)) for c in range(0, item.columns, 512)]

    def product(k, dest, first, last):
        item = items[k]
        left, right = inputs[k]
        at = pl.ds(pl.multiple_of(dest * item.rows, 16), item.rows)
        return dot_nn(left[at, :], right[:, first:last])

    def core_copy(k, chip):
        item = items[k]
        if item.is_given:
            at = pl.ds(pl.multiple_of((2 * chip + 1 - core) * item.rows, 16), item.rows)
            source = inputs[k][0].at[at, :]
        else:
            source = sent[k].at[chip]
        return pltpu.make_async_remote_copy(
            src_ref=source,
            dst_ref=held[k].at[chip],
            send_sem=core_sems[k][0].at[chip],
            recv_sem=core_sems[k][1].at[chip],
            device_id={"ctx": me ^ 1},
            device_id_type=MESH,
        )

    def step_copies(k, step):
        item = items[k]
        half = item.rows // item.parts
        copies = []
        for part, order in enumerate(orders[: item.parts]):
            bit = order[step]
            left = sorted(order[step + 1 :])
            fixed = [b for b in order[:step]]
            at = pl.ds(part * half, half)
            for slot, free in enumerate(scatter_blocks(left)):
                keep = free + ((me >> bit) & 1) * (1 << (bit - 1))
                send = free + (1 - ((me >> bit) & 1)) * (1 << (bit - 1))
                for b in fixed:
                    own = ((me >> b) & 1) * (1 << (b - 1))
                    keep, send = keep + own, send + own
                copies.append(
                    (
                        pltpu.make_async_remote_copy(
                            src_ref=held[k].at[send, at, :],
                            dst_ref=landed[k][step].at[slot, at, :],
                            send_sem=step_sems[k][step][0].at[part, slot],
                            recv_sem=step_sems[k][step][1].at[part, slot],
                            device_id={"ctx": me ^ (1 << bit)},
                            device_id_type=MESH,
                        ),
                        keep,
                        slot,
                        at,
                    )
                )
        return copies

    def start_core(k):
        item = items[k]

        def body(chip, carry):
            if not item.is_given:
                for first, last in columns_of(item):
                    sent[k][chip, :, first:last] = product(
                        k, 2 * chip + 1 - core, first, last
                    ).astype(jnp.bfloat16)
            core_copy(k, chip).start()
            return carry

        lax.fori_loop(0, chips, body, 0)

    def finish_core(k):
        item = items[k]

        def body(chip, carry):
            core_copy(k, chip).wait_recv()
            at = pl.ds(pl.multiple_of((2 * chip + core) * item.rows, 16), item.rows)
            for first, last in columns_of(item):
                if item.is_given:
                    own = inputs[k][0][at, first:last].astype(jnp.float32)
                else:
                    own = product(k, 2 * chip + core, first, last)
                total = own + held[k][chip, :, first:last].astype(jnp.float32)
                held[k][chip, :, first:last] = total.astype(jnp.bfloat16)
            return carry

        lax.fori_loop(0, chips, body, 0)

    def start_step(k, step):
        for copy, _, _, _ in step_copies(k, step):
            copy.start()

    def finish_step(k, step):
        item = items[k]
        for copy, keep, slot, at in step_copies(k, step):
            copy.wait_recv()
            for first, last in columns_of(item):
                total = held[k][keep, at, first:last].astype(jnp.float32) + landed[k][step][
                    slot, at, first:last
                ].astype(jnp.float32)
                if step == count - 2:
                    outputs[k][at, first:last] = total
                else:
                    held[k][keep, at, first:last] = total.astype(jnp.bfloat16)

    every = range(len(items))
    start_core(0)
    for k in every:
        if k + 1 < len(items):
            start_core(k + 1)
        finish_core(k)
        start_step(k, 0)
    for step in range(count - 1):
        for k in every:
            finish_step(k, step)
            if step + 1 < count - 1:
                start_step(k, step + 1)
    for k in every:

        def drain(chip, carry, k=k):
            core_copy(k, chip).wait_send()
            return carry

        lax.fori_loop(0, chips, drain, 0)
        for step in range(count - 1):
            for copy, _, _, _ in step_copies(k, step):
                copy.wait_send()


def scatter_over_ctx(n, items, collective_id):
    vmem = pl.BlockSpec(memory_space=pltpu.VMEM)
    count = n.bit_length() - 1
    scratch = []
    flops = 0
    for item in items:
        scratch.append(pltpu.VMEM((n // 2, item.rows, item.columns), jnp.bfloat16))
        if not item.is_given:
            scratch.append(pltpu.VMEM((n // 2, item.rows, item.columns), jnp.bfloat16))
        scratch += [
            pltpu.VMEM((n >> (step + 2), item.rows, item.columns), jnp.bfloat16)
            for step in range(count - 1)
        ]
        scratch += [pltpu.SemaphoreType.DMA((n // 2,))] * 2
        for step in range(count - 1):
            scratch += [pltpu.SemaphoreType.DMA((2, n >> (step + 2)))] * 2
        flops += 2 * n * item.rows * item.columns * item.depth
    operands = [array for item in items for array in item.operands]
    return pl.pallas_call(
        functools.partial(scatter_kernel, n, items),
        out_shape=tuple(
            jax.ShapeDtypeStruct((item.rows, item.columns), jnp.float32) for item in items
        ),
        in_specs=[vmem] * len(operands),
        out_specs=(vmem,) * len(items),
        scratch_shapes=scratch,
        compiler_params=pltpu.CompilerParams(
            vmem_limit_bytes=VMEM_LIMIT, collective_id=collective_id, has_side_effects=True
        ),
        cost_estimate=pl.CostEstimate(
            flops=flops, bytes_accessed=64 * 1024 * 1024, transcendentals=0
        ),
        name=f"scatter_over_ctx_{collective_id}",
    )(*operands)


def gather_kernel(n, own, out, local_sem, step_sends, step_lands, core_sends, core_lands):
    count = n.bit_length() - 1
    me = lax.axis_index("ctx")
    rows = own.shape[0]
    half = rows // 2
    barrier = pltpu.get_barrier_semaphore()
    for bit in range(count):
        pl.semaphore_signal(barrier, inc=1, device_id={"ctx": me ^ (1 << bit)}, device_id_type=MESH)
    pl.semaphore_wait(barrier, count)
    orders = (tuple(range(1, count)), tuple(range(count - 1, 0, -1)))
    local = pltpu.make_async_copy(own, out.at[me], local_sem)
    local.start()

    def chip_copy(part, step, slot, block, first):
        at = pl.ds(part * half, half)
        return pltpu.make_async_remote_copy(
            src_ref=own.at[at, :] if first else out.at[block, at, :],
            dst_ref=out.at[block, at, :],
            send_sem=step_sends.at[part, step, slot],
            recv_sem=step_lands.at[part, step, slot],
            device_id={"ctx": me ^ (1 << orders[part][step])},
            device_id_type=MESH,
        )

    def core_copy(block, slot, first):
        return pltpu.make_async_remote_copy(
            src_ref=own if first else out.at[block],
            dst_ref=out.at[block],
            send_sem=core_sends.at[slot],
            recv_sem=core_lands.at[slot],
            device_id={"ctx": me ^ 1},
            device_id_type=MESH,
        )

    started = []
    core_copy(me, 0, True).start()
    for step in range(count - 1):
        for part, order in enumerate(orders):
            for slot in range(1 << step):
                flips = 0
                for at in range(step):
                    flips |= ((slot >> at) & 1) << order[at]
                copy = chip_copy(part, step, slot, me ^ flips, slot == 0)
                copy.start()
                started.append(copy)
        for part, order in enumerate(orders):
            for slot in range(1 << step):
                chip_copy(part, step, slot, me, slot == 0).wait_recv()
    for chip in range(1, n // 2):
        core_copy(me ^ (2 * chip), chip, False).start()
    for chip in range(n // 2):
        core_copy(me, chip, chip == 0).wait_recv()
    for copy in started:
        copy.wait_send()
    for chip in range(n // 2):
        core_copy(me, chip, chip == 0).wait_send()
    local.wait()


def gather_over_ctx(n, own, collective_id):
    count = n.bit_length() - 1
    vmem = pl.BlockSpec(memory_space=pltpu.VMEM)
    slots = max(n // 4, 1)
    gathered = pl.pallas_call(
        functools.partial(gather_kernel, n),
        out_shape=jax.ShapeDtypeStruct((n,) + own.shape, own.dtype),
        in_specs=[vmem],
        out_specs=vmem,
        scratch_shapes=[
            pltpu.SemaphoreType.DMA,
            pltpu.SemaphoreType.DMA((2, count - 1, slots)),
            pltpu.SemaphoreType.DMA((2, count - 1, slots)),
            pltpu.SemaphoreType.DMA((n // 2,)),
            pltpu.SemaphoreType.DMA((n // 2,)),
        ],
        compiler_params=pltpu.CompilerParams(
            vmem_limit_bytes=VMEM_LIMIT, collective_id=collective_id, has_side_effects=True
        ),
        cost_estimate=pl.CostEstimate(
            flops=0, bytes_accessed=16 * 1024 * 1024, transcendentals=0
        ),
        name=f"gather_over_ctx_{collective_id}",
    )(own)
    return gathered.reshape((-1,) + own.shape[1:])


def dot_plain(left_op, right_op):
    return jnp.dot(left_op, right_op, preferred_element_type=jnp.float32)


def dot_rows(left_op, right_op):
    return lax.dot_general(
        left_op, right_op, (((0,), (0,)), ((), ())), preferred_element_type=jnp.float32
    )


def dot_cols(left_op, right_op):
    return lax.dot_general(
        left_op, right_op, (((1,), (1,)), ((), ())), preferred_element_type=jnp.float32
    )


def rms_scale(values):
    return lax.rsqrt(jnp.mean(values * values, axis=-1, keepdims=True) + EPSILON)


def rms_back(incoming, values, inv_rms, gain_vec):
    weighted = incoming * gain_vec
    d_values = inv_rms * weighted - values * inv_rms**3 * jnp.mean(
        weighted * values, axis=-1, keepdims=True
    )
    return (d_values, jnp.sum(incoming * values * inv_rms, axis=0))


def token_places(block_map, doc_lengths, per_device, devices):
    all_rows = per_device * devices
    half_block = per_device // 2
    token_rows = jnp.arange(all_rows, dtype=jnp.int32)
    device_of = token_rows // per_device
    within = token_rows % per_device
    wanted = device_of * 2 + within // half_block
    select = wanted[:, None] == jnp.arange(2 * devices, dtype=jnp.int32)[None, :]
    blocks = jnp.sum(jnp.where(select, block_map.reshape(-1)[None, :], 0), axis=1)
    places = blocks * half_block + within % half_block
    ends = jnp.cumsum(doc_lengths)
    segment = jnp.sum((places[:, None] >= ends[None, :]).astype(jnp.int32), axis=1)
    starts = ends - doc_lengths
    picked = segment[:, None] == jnp.arange(doc_lengths.shape[0], dtype=jnp.int32)[None, :]
    begins = jnp.sum(jnp.where(picked, starts[None, :], 0), axis=1)
    return (places, segment, places - begins)


def tables(inside):
    half_width = ROPE // 2
    frequency = ROPE_BASE ** (-2.0 * jnp.arange(half_width, dtype=jnp.float32) / ROPE)
    angles = inside.astype(jnp.float32)[:, None] * frequency[None, :]
    cosine_table = jnp.concatenate([jnp.cos(angles), jnp.cos(angles)], axis=1)
    sine_table = jnp.concatenate([jnp.sin(angles), jnp.sin(angles)], axis=1)
    return (cosine_table, sine_table)


def rotate(values, cosine_table, sine_table):
    half_width = values.shape[-1] // 2
    turned = jnp.concatenate([-values[..., half_width:], values[..., :half_width]], axis=-1)
    return values * cosine_table + turned * sine_table


def rotate_back(incoming, cosine_table, sine_table):
    half_width = incoming.shape[-1] // 2
    shifted = incoming * sine_table
    turned = jnp.concatenate([shifted[..., half_width:], -shifted[..., :half_width]], axis=-1)
    return incoming * cosine_table + turned


def wide_tables(inside):
    half_width = ROPE // 2
    lane = jnp.arange(HEAD, dtype=jnp.int32)
    frequency = ROPE_BASE ** (-2.0 * (lane % half_width).astype(jnp.float32) / ROPE)
    angles = inside.astype(jnp.float32)[:, None] * frequency[None, :]
    used = lane[None, :] < ROPE
    return jnp.where(used, jnp.cos(angles), 0.0), jnp.where(used, jnp.sin(angles), 0.0)


def on_device(
    tokens_in,
    w_qa,
    w_kva,
    w_qb,
    w_kvb,
    w_out,
    w_gate,
    w_up,
    w_down,
    gain_in,
    gain_q,
    gain_kv,
    gain_mid,
    cotangent,
    block_map,
    doc_lengths,
):
    local_rows = tokens_in.shape[0]
    half_rows = local_rows // 2
    devices = lax.axis_size("ctx")
    ctx_index = lax.axis_index("ctx")
    seqs = doc_lengths.shape[0]
    own_blocks = lax.dynamic_slice_in_dim(block_map, ctx_index, 1, 0)[0]
    ends = jnp.cumsum(doc_lengths)
    starts = ends - doc_lengths
    meta = jnp.concatenate([block_map.reshape(-1), starts, own_blocks])
    within = jnp.arange(half_rows, dtype=jnp.int32)
    query_place = (own_blocks[:, None] * half_rows + within[None, :]).reshape(-1)
    began = jnp.max(
        jnp.where(starts[None, :] <= query_place[:, None], starts[None, :], 0), axis=1
    )
    cosine_wide, sine_wide = wide_tables(query_place - began)
    cosine_table, sine_table = cosine_wide[:, :ROPE], sine_wide[:, :ROPE]
    head_count = w_qb.shape[1] // (NOPE + ROPE)
    tokens_f = tokens_in.astype(jnp.float32)
    scale_in = rms_scale(tokens_f)
    normed_in = (tokens_f * scale_in * gain_in).astype(jnp.bfloat16)
    kv_input = dot_plain(normed_in, w_kva)
    latent_raw = kv_input[:, :KVR]
    scale_kv = rms_scale(latent_raw)
    latent = (latent_raw * scale_kv * gain_kv).astype(jnp.bfloat16)
    key_rope = rotate(kv_input[:, KVR:], cosine_table, sine_table).astype(jnp.bfloat16)
    latents = gather_over_ctx(devices, jnp.concatenate([latent, key_rope], axis=1), 0)
    q_latent_pre = dot_plain(normed_in, w_qa)
    scale_q = rms_scale(q_latent_pre)
    q_latent = (q_latent_pre * scale_q * gain_q).astype(jnp.bfloat16)
    queries, attn_f, heads_out, log_totals = attention_forward(
        meta, q_latent, w_qb, latents, w_kvb, cosine_wide, sine_wide, half_rows, seqs
    )
    attention = lax.psum(dot_cols(heads_out, w_out).astype(jnp.bfloat16), "tp").astype(jnp.float32)
    middle = tokens_f + RESIDUAL_SCALE * attention
    scale_mid = rms_scale(middle)
    normed_mid = (middle * scale_mid * gain_mid).astype(jnp.bfloat16)
    gate_val = dot_plain(normed_mid, w_gate)
    up_val = dot_plain(normed_mid, w_up)
    sig_gate = jax.nn.sigmoid(gate_val)
    silu_gate = gate_val * sig_gate
    activation = (silu_gate * up_val).astype(jnp.bfloat16)
    cotangent_f = cotangent.astype(jnp.float32)
    d_feed = (RESIDUAL_SCALE * cotangent_f).astype(jnp.bfloat16)
    d_activation = dot_plain(d_feed, w_down)
    d_gate = (d_activation * up_val * sig_gate * (1.0 + gate_val * (1.0 - sig_gate))).astype(
        jnp.bfloat16
    )
    d_up = (d_activation * silu_gate).astype(jnp.bfloat16)
    d_normed_mid = lax.psum(
        (dot_cols(d_gate, w_gate) + dot_cols(d_up, w_up)).astype(jnp.bfloat16), "tp"
    ).astype(jnp.float32)
    gw_gate, gw_up, gw_down = scatter_over_ctx(
        devices,
        [
            Scatter(devices, left=normed_mid.T, right=d_gate),
            Scatter(devices, left=normed_mid.T, right=d_up),
            Scatter(devices, left=d_feed.T, right=activation),
        ],
        1,
    )
    activation_later, d_normed_mid = lax.optimization_barrier((activation, d_normed_mid))
    feed_own = lax.psum_scatter(
        dot_cols(activation_later, w_down).astype(jnp.bfloat16),
        "tp",
        scatter_dimension=0,
        tiled=True,
    ).astype(jnp.float32)
    own_rows = feed_own.shape[0]
    middle_own = lax.dynamic_slice_in_dim(middle, lax.axis_index("tp") * own_rows, own_rows, 0)
    out = lax.all_gather(
        (middle_own + RESIDUAL_SCALE * feed_own).astype(jnp.bfloat16), "tp", axis=0, tiled=True
    )
    d_middle_norm, d_gain_mid = rms_back(d_normed_mid, middle, scale_mid, gain_mid)
    d_middle = cotangent_f + d_middle_norm
    d_attention = (RESIDUAL_SCALE * d_middle).astype(jnp.bfloat16)
    d_heads = dot_plain(d_attention, w_out).astype(jnp.bfloat16)
    d_query_pre, d_latents, gw_kvb = attention_backward(
        meta, queries, log_totals, attn_f, d_heads, latents, w_kvb, cosine_wide, sine_wide,
        half_rows, seqs,
    )
    (d_latent_part,) = scatter_over_ctx(devices, [Scatter(devices, given=d_latents)], 2)
    d_q_latent = dot_cols(d_query_pre, w_qb).astype(jnp.bfloat16)
    summed_tp = lax.psum(
        jnp.concatenate([d_q_latent, d_latent_part.astype(jnp.bfloat16)], axis=1), "tp"
    ).astype(jnp.float32)
    gw_out, gw_qb, gw_kvb = scatter_over_ctx(
        devices,
        [
            Scatter(devices, left=d_attention.T, right=heads_out),
            Scatter(devices, left=q_latent.T, right=d_query_pre),
            Scatter(devices, given=gw_kvb),
        ],
        3,
    )
    q_rank = w_qa.shape[1]
    d_q_latent = summed_tp[:, :q_rank]
    d_latent = summed_tp[:, q_rank : q_rank + KVR]
    d_rope_sum = summed_tp[:, q_rank + KVR :]
    d_q_pre, d_gain_q = rms_back(d_q_latent, q_latent_pre, scale_q, gain_q)
    d_q_low = d_q_pre.astype(jnp.bfloat16)
    d_latent_raw, d_gain_kv = rms_back(d_latent, latent_raw, scale_kv, gain_kv)
    d_kv_input = jnp.concatenate(
        [d_latent_raw, rotate_back(d_rope_sum, cosine_table, sine_table)], axis=-1
    ).astype(jnp.bfloat16)
    d_normed_in = dot_cols(d_q_low, w_qa) + dot_cols(d_kv_input, w_kva)
    d_tokens_norm, d_gain_in = rms_back(d_normed_in, tokens_f, scale_in, gain_in)
    grad_in = d_middle + d_tokens_norm
    gains = jnp.concatenate(
        [g.reshape(devices, -1) for g in (d_gain_in, d_gain_mid, d_gain_q, d_gain_kv)], axis=1
    )
    lines = -(-gains.shape[1] // (32 * HEAD)) * 32
    gains = jnp.pad(gains, ((0, 0), (0, lines * HEAD - gains.shape[1])))
    gw_qa, gw_kva, gains = scatter_over_ctx(
        devices,
        [
            Scatter(devices, left=normed_in.T, right=d_q_low),
            Scatter(devices, left=normed_in.T, right=d_kv_input),
            Scatter(devices, given=gains.astype(jnp.bfloat16).reshape(devices * lines, HEAD)),
        ],
        4,
    )
    gains = gains.reshape(-1)
    ends = [0]
    for whole in (d_gain_in, d_gain_mid, d_gain_q, d_gain_kv):
        ends.append(ends[-1] + whole.shape[0] // devices)
    own_gains = [gains[first:last] for first, last in zip(ends, ends[1:])]
    return (
        out,
        grad_in,
        gw_qa,
        gw_kva,
        gw_qb,
        gw_kvb,
        gw_out,
        gw_gate,
        gw_up,
        gw_down,
        own_gains[0],
        own_gains[2],
        own_gains[3],
        own_gains[1],
    )


def solution(mesh):
    return jax.shard_map(
        on_device,
        mesh=mesh,
        in_specs=(
            P("ctx", None),
            P(),
            P(),
            P(None, "tp"),
            P(None, "tp"),
            P(None, "tp"),
            P(None, "tp"),
            P(None, "tp"),
            P(None, "tp"),
            P(),
            P(),
            P(),
            P(),
            P("ctx", None),
            P(),
            P(),
        ),
        out_specs=(
            P("ctx", None),
            P("ctx", None),
            P("ctx", None),
            P("ctx", None),
            P("ctx", "tp"),
            P("ctx", "tp"),
            P("ctx", "tp"),
            P("ctx", "tp"),
            P("ctx", "tp"),
            P("ctx", "tp"),
            P("ctx"),
            P("ctx"),
            P("ctx"),
            P("ctx"),
        ),
        check_vma=False,
    )
```

```python
import functools
import math

import jax
import jax.numpy as jnp
from jax import lax
from jax.experimental import pallas as pl
from jax.experimental.pallas import tpu as pltpu
from jax.sharding import PartitionSpec as P

KVR = 256
NOPE = 64
ROPE = 32
VDIM = 64
HEAD = NOPE + VDIM
WIDE = 2 * HEAD
MASKED = -1e30
SCORE_SCALE = (NOPE + ROPE) ** (-0.5)
EXP2_SCALE = SCORE_SCALE * math.log2(math.e)
FOLD_AT = 96
VMEM_LIMIT = 56 * 1024 * 1024

EPSILON = 1e-05
ROPE_BASE = 10000.0
RESIDUAL_SCALE = 1.4 / math.sqrt(62.0)


def dot_nn(left_op, right_op):
    return jnp.dot(left_op, right_op, preferred_element_type=jnp.float32)


def dot_nt(left_op, right_op):
    return lax.dot_general(
        left_op, right_op, (((1,), (1,)), ((), ())), preferred_element_type=jnp.float32
    )


def begin_of(place, starts):
    begin = jnp.zeros_like(place)
    for start in starts:
        begin = jnp.where(start <= place, start, begin)
    return begin


def pair_kind(key_block, query_block, starts, block_rows):
    key_first = key_block * block_rows
    query_first = query_block * block_rows
    early = begin_of(query_first, starts)
    late = begin_of(query_first + block_rows - 1, starts)
    needed = (key_block <= query_block) & (key_first + block_rows - 1 >= early)
    whole = (key_block < query_block) & (late <= key_first)
    return needed, whole


def mask_bias(key_block, query_block, starts, block_rows, keys_first):
    key_dim = 0 if keys_first else 1
    shape = (block_rows, block_rows)
    key_place = key_block * block_rows + lax.broadcasted_iota(jnp.int32, shape, key_dim)
    query_place = query_block * block_rows + lax.broadcasted_iota(jnp.int32, shape, 1 - key_dim)
    begin = jnp.zeros(shape, jnp.int32)
    for start in starts:
        begin = jnp.where(start <= query_place, start, begin)
    allowed = (key_place <= query_place) & (key_place >= begin)
    return jnp.where(allowed, 0.0, MASKED)


def shared_key_tile(rope_rows, block_rows):
    place = lax.broadcasted_iota(jnp.int32, (ROPE, HEAD), 0)
    lane = lax.broadcasted_iota(jnp.int32, (ROPE, HEAD), 1)
    eye = jnp.where(place == lane, 1.0, 0.0).astype(jnp.bfloat16)
    tile = dot_nn(rope_rows, eye)
    lanes = lax.broadcasted_iota(jnp.int32, (block_rows, HEAD), 1)
    ones = (lanes >= FOLD_AT) & (lanes < FOLD_AT + 3)
    return jnp.where(ones, 1.0, tile).astype(jnp.bfloat16)


def head_window(h):
    at = h * (NOPE + ROPE)
    return at // HEAD * HEAD, at % HEAD


def window_columns(heads):
    return head_window(heads - 1)[0] + WIDE


def head_groups(heads):
    return [(h, min(h + 2, heads)) for h in range(0, heads, 2)]


def forward_kernel(
    blocks, heads, seqs, meta, cq, wqb, lat, wkvb, cos, sin, qx, o_out, ob_out, u_out,
    wkvt, xs, xr, vt, top, total, acc, bias, pre,
):
    rows_all = cq.shape[0]
    block_rows = bias.shape[0]
    q_blocks = rows_all // block_rows
    starts = [meta[blocks + s] for s in range(seqs)]
    own = [meta[blocks + seqs + j] for j in range(q_blocks)]
    for first, last in head_groups(heads):
        wkvt[first * HEAD : last * HEAD, :] = (
            wkvb[:, first * HEAD : last * HEAD].astype(jnp.float32).T.astype(jnp.bfloat16)
        )
    lane = lax.broadcasted_iota(jnp.int32, (block_rows, HEAD), 1)
    for j in range(q_blocks):
        here = pl.ds(j * block_rows, block_rows)
        cos_j, sin_j = cos[here, :], sin[here, :]
        width = heads * (NOPE + ROPE)
        for at in range(0, width, WIDE):
            end = min(at + WIDE, width)
            pre[:, at:end] = dot_nn(cq[here, :], wqb[:, at:end])
        for h in range(heads):
            at, shift = head_window(h)
            own_part = pltpu.roll(pre[:, at : at + WIDE], (WIDE - shift) % WIDE, 1)[:, :HEAD]
            turned = pltpu.roll(own_part, NOPE, 1)
            left = pltpu.roll(turned, HEAD - ROPE // 2, 1)
            right = pltpu.roll(turned, ROPE // 2, 1)
            swapped = jnp.where(lane < ROPE // 2, -left, right)
            rope = jnp.where(lane < ROPE, turned * cos_j + swapped * sin_j, 0.0)
            qx[j, h, :, :HEAD] = jnp.where(lane < NOPE, own_part, 0.0).astype(jnp.bfloat16)
            qx[j, h, :, HEAD:] = rope.astype(jnp.bfloat16)
    top[...] = jnp.full(top.shape, MASKED, jnp.float32)
    total[...] = jnp.zeros(total.shape, jnp.float32)
    acc[...] = jnp.zeros(acc.shape, jnp.float32)

    def pair(j, masked):
        def one(h):
            keys = jnp.concatenate([xs[h], xr[...]], axis=1)
            scores = dot_nt(keys, qx[j, h])
            if masked:
                scores = scores + bias[...]
            old = top[j, h]
            new = jnp.maximum(old, jnp.max(scores, axis=0, keepdims=True))
            fade = jnp.exp2((old - new) * EXP2_SCALE)
            terms = jnp.exp2((scores - new) * EXP2_SCALE)
            top[j, h] = new
            total[j, h] = fade * total[j, h] + jnp.sum(terms, axis=0, keepdims=True)
            acc[j, h] = fade * acc[j, h] + dot_nn(vt[h], terms.astype(jnp.bfloat16))

        for h in range(heads):
            one(h)

    def step(r, carry):
        key_block = meta[r]
        kinds = [pair_kind(key_block, own[j], starts, block_rows) for j in range(q_blocks)]
        wanted = functools.reduce(jnp.logical_or, [k[0] for k in kinds])

        @pl.when(wanted)
        def _():
            here = pl.ds(pl.multiple_of(r * block_rows, block_rows), block_rows)
            latent = lat[here, :KVR]
            xr[...] = shared_key_tile(lat[here, KVR : KVR + ROPE], block_rows)
            for first, last in head_groups(heads):
                keys = dot_nn(latent, wkvb[:, first * HEAD : last * HEAD]).astype(jnp.bfloat16)
                values = dot_nt(wkvt[first * HEAD : last * HEAD, :], latent).astype(jnp.bfloat16)
                for h in range(first, last):
                    at = (h - first) * HEAD
                    xs[h] = keys[:, at : at + HEAD]
                    vt[h] = values[at + NOPE : at + HEAD, :]

        for j in range(q_blocks):
            needed, whole = kinds[j]

            @pl.when(needed & whole)
            def _():
                pair(j, False)

            @pl.when(needed & jnp.logical_not(whole))
            def _():
                bias[...] = mask_bias(key_block, own[j], starts, block_rows, True)
                pair(j, True)

        return carry

    lax.fori_loop(0, blocks, step, 0)
    for j in range(q_blocks):
        here = pl.ds(j * block_rows, block_rows)
        for first, last in head_groups(heads):
            parts = []
            for h in range(first, last):
                parts.append(acc[j, h] * (1.0 / total[j, h]))
                u_out[j, h : h + 1, :] = top[j, h] + jnp.log2(total[j, h]) * (1.0 / EXP2_SCALE)
            if len(parts) == 1:
                parts.append(jnp.zeros_like(parts[0]))
            both = jnp.concatenate(parts, axis=0).T
            width = (last - first) * VDIM
            o_out[here, first * VDIM : first * VDIM + width] = both[:, :width]
            ob_out[here, first * VDIM : first * VDIM + width] = both[:, :width].astype(jnp.bfloat16)


def attention_forward(meta, cq, wqb, lat, wkvb, cos, sin, block_rows, seqs):
    heads = wkvb.shape[1] // HEAD
    blocks = lat.shape[0] // block_rows
    rows = cq.shape[0]
    q_blocks = rows // block_rows
    vmem = pl.BlockSpec(memory_space=pltpu.VMEM)
    pairs = q_blocks * blocks * heads // 2
    return pl.pallas_call(
        functools.partial(forward_kernel, blocks, heads, seqs),
        out_shape=(
            jax.ShapeDtypeStruct((q_blocks, heads, block_rows, WIDE), jnp.bfloat16),
            jax.ShapeDtypeStruct((rows, heads * VDIM), jnp.float32),
            jax.ShapeDtypeStruct((rows, heads * VDIM), jnp.bfloat16),
            jax.ShapeDtypeStruct((q_blocks, 16 * -(-heads // 16), block_rows), jnp.float32),
        ),
        in_specs=[pl.BlockSpec(memory_space=pltpu.SMEM)] + [vmem] * 6,
        out_specs=(vmem,) * 4,
        scratch_shapes=[
            pltpu.VMEM((heads * HEAD, KVR), jnp.bfloat16),
            pltpu.VMEM((heads, block_rows, HEAD), jnp.bfloat16),
            pltpu.VMEM((block_rows, HEAD), jnp.bfloat16),
            pltpu.VMEM((heads, VDIM, block_rows), jnp.bfloat16),
            pltpu.VMEM((q_blocks, heads, 1, block_rows), jnp.float32),
            pltpu.VMEM((q_blocks, heads, 1, block_rows), jnp.float32),
            pltpu.VMEM((q_blocks, heads, VDIM, block_rows), jnp.float32),
            pltpu.VMEM((block_rows, block_rows), jnp.float32),
            pltpu.VMEM((block_rows, window_columns(heads)), jnp.float32),
        ],
        compiler_params=pltpu.CompilerParams(vmem_limit_bytes=VMEM_LIMIT),
        cost_estimate=pl.CostEstimate(
            flops=pairs * 4 * block_rows * block_rows * WIDE,
            bytes_accessed=16 * 1024 * 1024,
            transcendentals=pairs * block_rows * block_rows,
        ),
        name="attention_forward",
    )(meta, cq, wqb, lat, wkvb, cos, sin)


def three_terms(column):
    first = column.astype(jnp.bfloat16).astype(jnp.float32)
    rest = column - first
    second = rest.astype(jnp.bfloat16).astype(jnp.float32)
    return first, second, rest - second


def fold_in(tile, column, lane):
    for k, term in enumerate(three_terms(column)):
        tile = jnp.where(lane == FOLD_AT + k, term, tile)
    return tile


def backward_kernel(
    blocks, heads, seqs, meta, qx, u_in, o_in, dob, lat, wkvb, cos, sin, dq_out, dlat, gkvb,
    xs, xr, qo, qt, dt, dq, dkv, dkpe, gsum, bias, flat,
):
    block_rows = bias.shape[0]
    q_blocks = qx.shape[0]
    starts = [meta[blocks + s] for s in range(seqs)]
    own = [meta[blocks + seqs + j] for j in range(q_blocks)]
    lane = lax.broadcasted_iota(jnp.int32, (block_rows, HEAD), 1)
    for j in range(q_blocks):
        here = pl.ds(j * block_rows, block_rows)
        logs = u_in[j].T
        for first, last in head_groups(heads):
            d_pair = dob[here, first * VDIM : first * VDIM + HEAD].astype(jnp.float32)
            weighted = d_pair * o_in[here, first * VDIM : first * VDIM + HEAD]
            turned = pltpu.roll(d_pair, VDIM, 1)
            for h in range(first, last):
                mine = lane < VDIM if h == first else lane >= VDIM
                delta = jnp.sum(jnp.where(mine, weighted, 0.0), axis=1, keepdims=True)
                d_head = jnp.where(lane >= VDIM, turned if h == first else d_pair, 0.0)
                q_first = qx[j, h, :, :HEAD].astype(jnp.float32)
                q_second = qx[j, h, :, HEAD:].astype(jnp.float32)
                qo[j, h, :block_rows, :HEAD] = qx[j, h, :, :HEAD]
                qo[j, h, :block_rows, HEAD:] = fold_in(q_second, -logs[:, h : h + 1], lane).astype(
                    jnp.bfloat16
                )
                qo[j, h, block_rows:, :HEAD] = d_head.astype(jnp.bfloat16)
                qo[j, h, block_rows:, HEAD:] = fold_in(
                    jnp.zeros((block_rows, HEAD), jnp.float32), -delta, lane
                ).astype(jnp.bfloat16)
                qt[j, h, :NOPE, :] = q_first.T[:NOPE, :].astype(jnp.bfloat16)
                qt[j, h, NOPE:, :] = q_second.T[:ROPE, :].astype(jnp.bfloat16)
                dt[j, h] = d_head.T[VDIM:, :].astype(jnp.bfloat16)
    dq[...] = jnp.zeros(dq.shape, jnp.float32)
    gsum[...] = jnp.zeros(gsum.shape, jnp.float32)

    def pair(j, masked):
        def one(h):
            keys = jnp.concatenate([xs[h], xr[...]], axis=1)
            both = dot_nt(qo[j, h], keys)
            scores = both[:block_rows] * EXP2_SCALE
            if masked:
                scores = scores + bias[...]
            probs = jnp.exp2(scores)
            d_scores = (probs * both[block_rows:]).astype(jnp.bfloat16)
            dq[j, h] += dot_nn(d_scores, keys)
            d_keys = dot_nn(qt[j, h], d_scores)
            dkv[h, :NOPE, :] += d_keys[:NOPE]
            dkpe[...] += d_keys[NOPE:]
            dkv[h, NOPE:, :] += dot_nn(dt[j, h], probs.astype(jnp.bfloat16))

        for h in range(heads):
            one(h)

    def step(r, carry):
        key_block = meta[r]
        kinds = [pair_kind(key_block, own[j], starts, block_rows) for j in range(q_blocks)]
        wanted = functools.reduce(jnp.logical_or, [k[0] for k in kinds])
        here = pl.ds(pl.multiple_of(r * block_rows, block_rows), block_rows)

        @pl.when(wanted)
        def _():
            latent = lat[here, :KVR]
            xr[...] = shared_key_tile(lat[here, KVR : KVR + ROPE], block_rows)
            for first, last in head_groups(heads):
                keys = dot_nn(latent, wkvb[:, first * HEAD : last * HEAD]).astype(jnp.bfloat16)
                for h in range(first, last):
                    xs[h] = keys[:, (h - first) * HEAD : (h - first + 1) * HEAD]
            dkv[...] = jnp.zeros(dkv.shape, jnp.float32)
            dkpe[...] = jnp.zeros(dkpe.shape, jnp.float32)

        for j in range(q_blocks):
            needed, whole = kinds[j]

            @pl.when(needed & whole)
            def _():
                pair(j, False)

            @pl.when(needed & jnp.logical_not(whole))
            def _():
                bias[...] = mask_bias(key_block, own[j], starts, block_rows, False)
                pair(j, True)

        @pl.when(wanted)
        def _():
            latent = lat[here, :KVR]
            d_latent = jnp.zeros((KVR, block_rows), jnp.float32)
            for h in range(heads):
                d_head = jnp.concatenate(
                    [dkv[h, :NOPE, :] * SCORE_SCALE, dkv[h, NOPE:, :]], axis=0
                ).astype(jnp.bfloat16)
                d_latent += dot_nn(wkvb[:, h * HEAD : (h + 1) * HEAD], d_head)
                gsum[h * HEAD : (h + 1) * HEAD, :] += dot_nn(d_head, latent)
            dlat[here, :KVR] = d_latent.T.astype(jnp.bfloat16)
            rope = jnp.concatenate(
                [dkpe[...] * SCORE_SCALE, jnp.zeros((HEAD - ROPE, block_rows), jnp.float32)], axis=0
            )
            dlat[here, KVR:] = rope.T[:, :ROPE].astype(jnp.bfloat16)

        @pl.when(jnp.logical_not(wanted))
        def _():
            dlat[here, :] = jnp.zeros((block_rows, KVR + ROPE), jnp.bfloat16)

        return carry

    lax.fori_loop(0, blocks, step, 0)
    for h in range(heads):
        gkvb[:, h * HEAD : (h + 1) * HEAD] = gsum[h * HEAD : (h + 1) * HEAD, :].T.astype(
            jnp.bfloat16
        )
    for j in range(q_blocks):
        here = pl.ds(j * block_rows, block_rows)
        cos_j, sin_j = cos[here, :], sin[here, :]
        flat[...] = jnp.zeros(flat.shape, jnp.float32)
        for h in range(heads):
            nope = jnp.where(lane < NOPE, dq[j, h, :, :HEAD], 0.0)
            rope = dq[j, h, :, HEAD:]
            shifted = rope * sin_j
            left = pltpu.roll(shifted, HEAD - ROPE // 2, 1)
            right = pltpu.roll(shifted, ROPE // 2, 1)
            swapped = jnp.where(lane < ROPE // 2, left, jnp.where(lane < ROPE, -right, 0.0))
            back = pltpu.roll(jnp.where(lane < ROPE, rope * cos_j + swapped, 0.0), NOPE, 1)
            whole = jnp.concatenate([(nope + back) * SCORE_SCALE, jnp.zeros_like(nope)], axis=1)
            at, shift = head_window(h)
            flat[:, at : at + WIDE] += pltpu.roll(whole, shift, 1)
        dq_out[here, :] = flat[:, : heads * (NOPE + ROPE)].astype(jnp.bfloat16)


def attention_backward(meta, qx, u_in, o_in, dob, lat, wkvb, cos, sin, block_rows, seqs):
    heads = wkvb.shape[1] // HEAD
    blocks = lat.shape[0] // block_rows
    q_blocks = qx.shape[0]
    rows = q_blocks * block_rows
    odd = -(heads * VDIM) % HEAD
    if odd:
        o_in = jnp.pad(o_in, ((0, 0), (0, odd)))
        dob = jnp.pad(dob, ((0, 0), (0, odd)))
    vmem = pl.BlockSpec(memory_space=pltpu.VMEM)
    pairs = q_blocks * blocks * heads // 2
    return pl.pallas_call(
        functools.partial(backward_kernel, blocks, heads, seqs),
        out_shape=(
            jax.ShapeDtypeStruct((rows, heads * (NOPE + ROPE)), jnp.bfloat16),
            jax.ShapeDtypeStruct((lat.shape[0], KVR + ROPE), jnp.bfloat16),
            jax.ShapeDtypeStruct((KVR, heads * HEAD), jnp.bfloat16),
        ),
        in_specs=[pl.BlockSpec(memory_space=pltpu.SMEM)] + [vmem] * 8,
        out_specs=(vmem,) * 3,
        scratch_shapes=[
            pltpu.VMEM((heads, block_rows, HEAD), jnp.bfloat16),
            pltpu.VMEM((block_rows, HEAD), jnp.bfloat16),
            pltpu.VMEM((q_blocks, heads, 2 * block_rows, WIDE), jnp.bfloat16),
            pltpu.VMEM((q_blocks, heads, NOPE + ROPE, block_rows), jnp.bfloat16),
            pltpu.VMEM((q_blocks, heads, VDIM, block_rows), jnp.bfloat16),
            pltpu.VMEM((q_blocks, heads, block_rows, WIDE), jnp.float32),
            pltpu.VMEM((heads, HEAD, block_rows), jnp.float32),
            pltpu.VMEM((ROPE, block_rows), jnp.float32),
            pltpu.VMEM((heads * HEAD, KVR), jnp.float32),
            pltpu.VMEM((block_rows, block_rows), jnp.float32),
            pltpu.VMEM((block_rows, window_columns(heads)), jnp.float32),
        ],
        compiler_params=pltpu.CompilerParams(vmem_limit_bytes=VMEM_LIMIT),
        cost_estimate=pl.CostEstimate(
            flops=pairs * 8 * block_rows * block_rows * WIDE,
            bytes_accessed=24 * 1024 * 1024,
            transcendentals=pairs * block_rows * block_rows,
        ),
        name="attention_backward",
    )(meta, qx, u_in, o_in, dob, lat, wkvb, cos, sin)


MESH = pl.DeviceIdType.MESH


class Scatter:
    def __init__(self, n, given=None, left=None, right=None):
        self.operands = [given] if given is not None else [left, right]
        self.is_given = given is not None
        self.rows = self.operands[0].shape[0] // n
        self.columns = self.operands[-1].shape[1]
        self.depth = 0 if self.is_given else right.shape[0]
        self.parts = 2 if self.rows % 32 == 0 else 1


def scatter_blocks(bits_left):
    chips = []
    for value in range(1 << len(bits_left)):
        chip = 0
        for at, bit in enumerate(bits_left):
            chip = chip + (((value >> at) & 1) << (bit - 1))
        chips.append(chip)
    return chips


def scatter_kernel(n, items, *refs):
    count = n.bit_length() - 1
    me = lax.axis_index("ctx")
    refs = list(refs)
    take = lambda k: [refs.pop(0) for _ in range(k)]
    inputs = [take(len(item.operands)) for item in items]
    outputs = take(len(items))
    held, sent, landed, core_sems, step_sems = [], [], [], [], []
    for item in items:
        held.append(refs.pop(0))
        sent.append(None if item.is_given else refs.pop(0))
        landed.append(take(count - 1))
        core_sems.append(take(2))
        step_sems.append([take(2) for _ in range(count - 1)])
    barrier = pltpu.get_barrier_semaphore()
    for bit in range(count):
        pl.semaphore_signal(barrier, inc=1, device_id={"ctx": me ^ (1 << bit)}, device_id_type=MESH)
    pl.semaphore_wait(barrier, count)
    core = me & 1
    chips = n // 2
    orders = (tuple(range(1, count)), tuple(range(count - 1, 0, -1)))

    def columns_of(item):
        return [(c, min(c + 512, item.columns)) for c in range(0, item.columns, 512)]

    def product(k, dest, first, last):
        item = items[k]
        left, right = inputs[k]
        at = pl.ds(pl.multiple_of(dest * item.rows, 16), item.rows)
        return dot_nn(left[at, :], right[:, first:last])

    def core_copy(k, chip):
        item = items[k]
        if item.is_given:
            at = pl.ds(pl.multiple_of((2 * chip + 1 - core) * item.rows, 16), item.rows)
            source = inputs[k][0].at[at, :]
        else:
            source = sent[k].at[chip]
        return pltpu.make_async_remote_copy(
            src_ref=source,
            dst_ref=held[k].at[chip],
            send_sem=core_sems[k][0].at[chip],
            recv_sem=core_sems[k][1].at[chip],
            device_id={"ctx": me ^ 1},
            device_id_type=MESH,
        )

    def step_copies(k, step):
        item = items[k]
        half = item.rows // item.parts
        copies = []
        for part, order in enumerate(orders[: item.parts]):
            bit = order[step]
            left = sorted(order[step + 1 :])
            fixed = [b for b in order[:step]]
            at = pl.ds(part * half, half)
            for slot, free in enumerate(scatter_blocks(left)):
                keep = free + ((me >> bit) & 1) * (1 << (bit - 1))
                send = free + (1 - ((me >> bit) & 1)) * (1 << (bit - 1))
                for b in fixed:
                    own = ((me >> b) & 1) * (1 << (b - 1))
                    keep, send = keep + own, send + own
                copies.append(
                    (
                        pltpu.make_async_remote_copy(
                            src_ref=held[k].at[send, at, :],
                            dst_ref=landed[k][step].at[slot, at, :],
                            send_sem=step_sems[k][step][0].at[part, slot],
                            recv_sem=step_sems[k][step][1].at[part, slot],
                            device_id={"ctx": me ^ (1 << bit)},
                            device_id_type=MESH,
                        ),
                        keep,
                        slot,
                        at,
                    )
                )
        return copies

    def start_core(k):
        item = items[k]

        def body(chip, carry):
            if not item.is_given:
                for first, last in columns_of(item):
                    sent[k][chip, :, first:last] = product(
                        k, 2 * chip + 1 - core, first, last
                    ).astype(jnp.bfloat16)
            core_copy(k, chip).start()
            return carry

        lax.fori_loop(0, chips, body, 0)

    def finish_core(k):
        item = items[k]

        def body(chip, carry):
            core_copy(k, chip).wait_recv()
            at = pl.ds(pl.multiple_of((2 * chip + core) * item.rows, 16), item.rows)
            for first, last in columns_of(item):
                if item.is_given:
                    own = inputs[k][0][at, first:last].astype(jnp.float32)
                else:
                    own = product(k, 2 * chip + core, first, last)
                total = own + held[k][chip, :, first:last].astype(jnp.float32)
                held[k][chip, :, first:last] = total.astype(jnp.bfloat16)
            return carry

        lax.fori_loop(0, chips, body, 0)

    def start_step(k, step):
        for copy, _, _, _ in step_copies(k, step):
            copy.start()

    def finish_step(k, step):
        item = items[k]
        for copy, keep, slot, at in step_copies(k, step):
            copy.wait_recv()
            for first, last in columns_of(item):
                total = held[k][keep, at, first:last].astype(jnp.float32) + landed[k][step][
                    slot, at, first:last
                ].astype(jnp.float32)
                if step == count - 2:
                    outputs[k][at, first:last] = total
                else:
                    held[k][keep, at, first:last] = total.astype(jnp.bfloat16)

    every = range(len(items))
    start_core(0)
    for k in every:
        if k + 1 < len(items):
            start_core(k + 1)
        finish_core(k)
        start_step(k, 0)
    for step in range(count - 1):
        for k in every:
            finish_step(k, step)
            if step + 1 < count - 1:
                start_step(k, step + 1)
    for k in every:

        def drain(chip, carry, k=k):
            core_copy(k, chip).wait_send()
            return carry

        lax.fori_loop(0, chips, drain, 0)
        for step in range(count - 1):
            for copy, _, _, _ in step_copies(k, step):
                copy.wait_send()


def scatter_over_ctx(n, items, collective_id):
    vmem = pl.BlockSpec(memory_space=pltpu.VMEM)
    count = n.bit_length() - 1
    scratch = []
    flops = 0
    for item in items:
        scratch.append(pltpu.VMEM((n // 2, item.rows, item.columns), jnp.bfloat16))
        if not item.is_given:
            scratch.append(pltpu.VMEM((n // 2, item.rows, item.columns), jnp.bfloat16))
        scratch += [
            pltpu.VMEM((n >> (step + 2), item.rows, item.columns), jnp.bfloat16)
            for step in range(count - 1)
        ]
        scratch += [pltpu.SemaphoreType.DMA((n // 2,))] * 2
        for step in range(count - 1):
            scratch += [pltpu.SemaphoreType.DMA((2, n >> (step + 2)))] * 2
        flops += 2 * n * item.rows * item.columns * item.depth
    operands = [array for item in items for array in item.operands]
    return pl.pallas_call(
        functools.partial(scatter_kernel, n, items),
        out_shape=tuple(
            jax.ShapeDtypeStruct((item.rows, item.columns), jnp.float32) for item in items
        ),
        in_specs=[vmem] * len(operands),
        out_specs=(vmem,) * len(items),
        scratch_shapes=scratch,
        compiler_params=pltpu.CompilerParams(
            vmem_limit_bytes=VMEM_LIMIT, collective_id=collective_id, has_side_effects=True
        ),
        cost_estimate=pl.CostEstimate(
            flops=flops, bytes_accessed=64 * 1024 * 1024, transcendentals=0
        ),
        name=f"scatter_over_ctx_{collective_id}",
    )(*operands)


def gather_kernel(n, own, out, local_sem, step_sends, step_lands, core_sends, core_lands):
    count = n.bit_length() - 1
    me = lax.axis_index("ctx")
    rows = own.shape[0]
    half = rows // 2
    barrier = pltpu.get_barrier_semaphore()
    for bit in range(count):
        pl.semaphore_signal(barrier, inc=1, device_id={"ctx": me ^ (1 << bit)}, device_id_type=MESH)
    pl.semaphore_wait(barrier, count)
    orders = (tuple(range(1, count)), tuple(range(count - 1, 0, -1)))
    local = pltpu.make_async_copy(own, out.at[me], local_sem)
    local.start()

    def chip_copy(part, step, slot, block, first):
        at = pl.ds(part * half, half)
        return pltpu.make_async_remote_copy(
            src_ref=own.at[at, :] if first else out.at[block, at, :],
            dst_ref=out.at[block, at, :],
            send_sem=step_sends.at[part, step, slot],
            recv_sem=step_lands.at[part, step, slot],
            device_id={"ctx": me ^ (1 << orders[part][step])},
            device_id_type=MESH,
        )

    def core_copy(block, slot, first):
        return pltpu.make_async_remote_copy(
            src_ref=own if first else out.at[block],
            dst_ref=out.at[block],
            send_sem=core_sends.at[slot],
            recv_sem=core_lands.at[slot],
            device_id={"ctx": me ^ 1},
            device_id_type=MESH,
        )

    started = []
    core_copy(me, 0, True).start()
    for step in range(count - 1):
        for part, order in enumerate(orders):
            for slot in range(1 << step):
                flips = 0
                for at in range(step):
                    flips |= ((slot >> at) & 1) << order[at]
                copy = chip_copy(part, step, slot, me ^ flips, slot == 0)
                copy.start()
                started.append(copy)
        for part, order in enumerate(orders):
            for slot in range(1 << step):
                chip_copy(part, step, slot, me, slot == 0).wait_recv()
    for chip in range(1, n // 2):
        core_copy(me ^ (2 * chip), chip, False).start()
    for chip in range(n // 2):
        core_copy(me, chip, chip == 0).wait_recv()
    for copy in started:
        copy.wait_send()
    for chip in range(n // 2):
        core_copy(me, chip, chip == 0).wait_send()
    local.wait()


def gather_over_ctx(n, own, collective_id):
    count = n.bit_length() - 1
    vmem = pl.BlockSpec(memory_space=pltpu.VMEM)
    slots = max(n // 4, 1)
    gathered = pl.pallas_call(
        functools.partial(gather_kernel, n),
        out_shape=jax.ShapeDtypeStruct((n,) + own.shape, own.dtype),
        in_specs=[vmem],
        out_specs=vmem,
        scratch_shapes=[
            pltpu.SemaphoreType.DMA,
            pltpu.SemaphoreType.DMA((2, count - 1, slots)),
            pltpu.SemaphoreType.DMA((2, count - 1, slots)),
            pltpu.SemaphoreType.DMA((n // 2,)),
            pltpu.SemaphoreType.DMA((n // 2,)),
        ],
        compiler_params=pltpu.CompilerParams(
            vmem_limit_bytes=VMEM_LIMIT, collective_id=collective_id, has_side_effects=True
        ),
        cost_estimate=pl.CostEstimate(
            flops=0, bytes_accessed=16 * 1024 * 1024, transcendentals=0
        ),
        name=f"gather_over_ctx_{collective_id}",
    )(own)
    return gathered.reshape((-1,) + own.shape[1:])


def dot_plain(left_op, right_op):
    return jnp.dot(left_op, right_op, preferred_element_type=jnp.float32)


def dot_rows(left_op, right_op):
    return lax.dot_general(
        left_op, right_op, (((0,), (0,)), ((), ())), preferred_element_type=jnp.float32
    )


def dot_cols(left_op, right_op):
    return lax.dot_general(
        left_op, right_op, (((1,), (1,)), ((), ())), preferred_element_type=jnp.float32
    )


def rms_scale(values):
    return lax.rsqrt(jnp.mean(values * values, axis=-1, keepdims=True) + EPSILON)


def rms_back(incoming, values, inv_rms, gain_vec):
    weighted = incoming * gain_vec
    d_values = inv_rms * weighted - values * inv_rms**3 * jnp.mean(
        weighted * values, axis=-1, keepdims=True
    )
    return (d_values, jnp.sum(incoming * values * inv_rms, axis=0))


def token_places(block_map, doc_lengths, per_device, devices):
    all_rows = per_device * devices
    half_block = per_device // 2
    token_rows = jnp.arange(all_rows, dtype=jnp.int32)
    device_of = token_rows // per_device
    within = token_rows % per_device
    wanted = device_of * 2 + within // half_block
    select = wanted[:, None] == jnp.arange(2 * devices, dtype=jnp.int32)[None, :]
    blocks = jnp.sum(jnp.where(select, block_map.reshape(-1)[None, :], 0), axis=1)
    places = blocks * half_block + within % half_block
    ends = jnp.cumsum(doc_lengths)
    segment = jnp.sum((places[:, None] >= ends[None, :]).astype(jnp.int32), axis=1)
    starts = ends - doc_lengths
    picked = segment[:, None] == jnp.arange(doc_lengths.shape[0], dtype=jnp.int32)[None, :]
    begins = jnp.sum(jnp.where(picked, starts[None, :], 0), axis=1)
    return (places, segment, places - begins)


def tables(inside):
    half_width = ROPE // 2
    frequency = ROPE_BASE ** (-2.0 * jnp.arange(half_width, dtype=jnp.float32) / ROPE)
    angles = inside.astype(jnp.float32)[:, None] * frequency[None, :]
    cosine_table = jnp.concatenate([jnp.cos(angles), jnp.cos(angles)], axis=1)
    sine_table = jnp.concatenate([jnp.sin(angles), jnp.sin(angles)], axis=1)
    return (cosine_table, sine_table)


def rotate(values, cosine_table, sine_table):
    half_width = values.shape[-1] // 2
    turned = jnp.concatenate([-values[..., half_width:], values[..., :half_width]], axis=-1)
    return values * cosine_table + turned * sine_table


def rotate_back(incoming, cosine_table, sine_table):
    half_width = incoming.shape[-1] // 2
    shifted = incoming * sine_table
    turned = jnp.concatenate([shifted[..., half_width:], -shifted[..., :half_width]], axis=-1)
    return incoming * cosine_table + turned


def wide_tables(inside):
    half_width = ROPE // 2
    lane = jnp.arange(HEAD, dtype=jnp.int32)
    frequency = ROPE_BASE ** (-2.0 * (lane % half_width).astype(jnp.float32) / ROPE)
    angles = inside.astype(jnp.float32)[:, None] * frequency[None, :]
    used = lane[None, :] < ROPE
    return jnp.where(used, jnp.cos(angles), 0.0), jnp.where(used, jnp.sin(angles), 0.0)


def on_device(
    tokens_in,
    w_qa,
    w_kva,
    w_qb,
    w_kvb,
    w_out,
    w_gate,
    w_up,
    w_down,
    gain_in,
    gain_q,
    gain_kv,
    gain_mid,
    cotangent,
    block_map,
    doc_lengths,
):
    local_rows = tokens_in.shape[0]
    half_rows = local_rows // 2
    devices = lax.axis_size("ctx")
    ctx_index = lax.axis_index("ctx")
    seqs = doc_lengths.shape[0]
    own_blocks = lax.dynamic_slice_in_dim(block_map, ctx_index, 1, 0)[0]
    ends = jnp.cumsum(doc_lengths)
    starts = ends - doc_lengths
    meta = jnp.concatenate([block_map.reshape(-1), starts, own_blocks])
    within = jnp.arange(half_rows, dtype=jnp.int32)
    query_place = (own_blocks[:, None] * half_rows + within[None, :]).reshape(-1)
    began = jnp.max(
        jnp.where(starts[None, :] <= query_place[:, None], starts[None, :], 0), axis=1
    )
    cosine_wide, sine_wide = wide_tables(query_place - began)
    cosine_table, sine_table = cosine_wide[:, :ROPE], sine_wide[:, :ROPE]
    head_count = w_qb.shape[1] // (NOPE + ROPE)
    tokens_f = tokens_in.astype(jnp.float32)
    scale_in = rms_scale(tokens_f)
    normed_in = (tokens_f * scale_in * gain_in).astype(jnp.bfloat16)
    kv_input = dot_plain(normed_in, w_kva)
    latent_raw = kv_input[:, :KVR]
    scale_kv = rms_scale(latent_raw)
    latent = (latent_raw * scale_kv * gain_kv).astype(jnp.bfloat16)
    key_rope = rotate(kv_input[:, KVR:], cosine_table, sine_table).astype(jnp.bfloat16)
    latents = gather_over_ctx(devices, jnp.concatenate([latent, key_rope], axis=1), 0)
    q_latent_pre = dot_plain(normed_in, w_qa)
    scale_q = rms_scale(q_latent_pre)
    q_latent = (q_latent_pre * scale_q * gain_q).astype(jnp.bfloat16)
    queries, attn_f, heads_out, log_totals = attention_forward(
        meta, q_latent, w_qb, latents, w_kvb, cosine_wide, sine_wide, half_rows, seqs
    )
    attention = lax.psum(dot_cols(heads_out, w_out).astype(jnp.bfloat16), "tp").astype(jnp.float32)
    middle = tokens_f + RESIDUAL_SCALE * attention
    scale_mid = rms_scale(middle)
    normed_mid = (middle * scale_mid * gain_mid).astype(jnp.bfloat16)
    gate_val = dot_plain(normed_mid, w_gate)
    up_val = dot_plain(normed_mid, w_up)
    sig_gate = jax.nn.sigmoid(gate_val)
    silu_gate = gate_val * sig_gate
    activation = (silu_gate * up_val).astype(jnp.bfloat16)
    cotangent_f = cotangent.astype(jnp.float32)
    d_feed = (RESIDUAL_SCALE * cotangent_f).astype(jnp.bfloat16)
    d_activation = dot_plain(d_feed, w_down)
    d_gate = (d_activation * up_val * sig_gate * (1.0 + gate_val * (1.0 - sig_gate))).astype(
        jnp.bfloat16
    )
    d_up = (d_activation * silu_gate).astype(jnp.bfloat16)
    d_normed_mid = lax.psum(
        (dot_cols(d_gate, w_gate) + dot_cols(d_up, w_up)).astype(jnp.bfloat16), "tp"
    ).astype(jnp.float32)
    gw_gate, gw_up, gw_down = scatter_over_ctx(
        devices,
        [
            Scatter(devices, left=normed_mid.T, right=d_gate),
            Scatter(devices, left=normed_mid.T, right=d_up),
            Scatter(devices, left=d_feed.T, right=activation),
        ],
        1,
    )
    feed_part = dot_cols(activation, w_down).astype(jnp.bfloat16)
    d_normed_mid, feed_part, gw_gate, gw_up, gw_down = lax.optimization_barrier(
        (d_normed_mid, feed_part, gw_gate, gw_up, gw_down)
    )
    feed_own = lax.psum_scatter(feed_part, "tp", scatter_dimension=0, tiled=True)
    own_rows = feed_own.shape[0]
    middle_own = lax.dynamic_slice_in_dim(middle, lax.axis_index("tp") * own_rows, own_rows, 0)
    out_own = (middle_own + RESIDUAL_SCALE * feed_own.astype(jnp.float32)).astype(jnp.bfloat16)
    d_middle_norm, d_gain_mid = rms_back(d_normed_mid, middle, scale_mid, gain_mid)
    d_middle = cotangent_f + d_middle_norm
    d_attention = (RESIDUAL_SCALE * d_middle).astype(jnp.bfloat16)
    d_heads = dot_plain(d_attention, w_out).astype(jnp.bfloat16)
    d_query_pre, d_latents, gw_kvb = attention_backward(
        meta, queries, log_totals, attn_f, d_heads, latents, w_kvb, cosine_wide, sine_wide,
        half_rows, seqs,
    )
    (d_latent_part,) = scatter_over_ctx(devices, [Scatter(devices, given=d_latents)], 2)
    d_q_latent = dot_cols(d_query_pre, w_qb).astype(jnp.bfloat16)
    before_tp = jnp.concatenate([d_q_latent, d_latent_part.astype(jnp.bfloat16)], axis=1)
    before_tp, out_own = lax.optimization_barrier((before_tp, out_own))
    summed_tp = lax.psum(before_tp, "tp")
    gw_out, gw_qb, gw_kvb = scatter_over_ctx(
        devices,
        [
            Scatter(devices, left=d_attention.T, right=heads_out),
            Scatter(devices, left=q_latent.T, right=d_query_pre),
            Scatter(devices, given=gw_kvb),
        ],
        3,
    )
    summed_tp, out_own, gw_out, gw_qb, gw_kvb = lax.optimization_barrier(
        (summed_tp, out_own, gw_out, gw_qb, gw_kvb)
    )
    out = lax.all_gather(out_own, "tp", axis=0, tiled=True)
    summed_tp = summed_tp.astype(jnp.float32)
    q_rank = w_qa.shape[1]
    d_q_latent = summed_tp[:, :q_rank]
    d_latent = summed_tp[:, q_rank : q_rank + KVR]
    d_rope_sum = summed_tp[:, q_rank + KVR :]
    d_q_pre, d_gain_q = rms_back(d_q_latent, q_latent_pre, scale_q, gain_q)
    d_q_low = d_q_pre.astype(jnp.bfloat16)
    d_latent_raw, d_gain_kv = rms_back(d_latent, latent_raw, scale_kv, gain_kv)
    d_kv_input = jnp.concatenate(
        [d_latent_raw, rotate_back(d_rope_sum, cosine_table, sine_table)], axis=-1
    ).astype(jnp.bfloat16)
    d_normed_in = dot_cols(d_q_low, w_qa) + dot_cols(d_kv_input, w_kva)
    d_tokens_norm, d_gain_in = rms_back(d_normed_in, tokens_f, scale_in, gain_in)
    grad_in = d_middle + d_tokens_norm
    gains = jnp.concatenate(
        [g.reshape(devices, -1) for g in (d_gain_in, d_gain_mid, d_gain_q, d_gain_kv)], axis=1
    )
    lines = -(-gains.shape[1] // (32 * HEAD)) * 32
    gains = jnp.pad(gains, ((0, 0), (0, lines * HEAD - gains.shape[1])))
    gw_qa, gw_kva, gains = scatter_over_ctx(
        devices,
        [
            Scatter(devices, left=normed_in.T, right=d_q_low),
            Scatter(devices, left=normed_in.T, right=d_kv_input),
            Scatter(devices, given=gains.astype(jnp.bfloat16).reshape(devices * lines, HEAD)),
        ],
        4,
    )
    gains = gains.reshape(-1)
    ends = [0]
    for whole in (d_gain_in, d_gain_mid, d_gain_q, d_gain_kv):
        ends.append(ends[-1] + whole.shape[0] // devices)
    own_gains = [gains[first:last] for first, last in zip(ends, ends[1:])]
    return (
        out,
        grad_in,
        gw_qa,
        gw_kva,
        gw_qb,
        gw_kvb,
        gw_out,
        gw_gate,
        gw_up,
        gw_down,
        own_gains[0],
        own_gains[2],
        own_gains[3],
        own_gains[1],
    )


def solution(mesh):
    return jax.shard_map(
        on_device,
        mesh=mesh,
        in_specs=(
            P("ctx", None),
            P(),
            P(),
            P(None, "tp"),
            P(None, "tp"),
            P(None, "tp"),
            P(None, "tp"),
            P(None, "tp"),
            P(None, "tp"),
            P(),
            P(),
            P(),
            P(),
            P("ctx", None),
            P(),
            P(),
        ),
        out_specs=(
            P("ctx", None),
            P("ctx", None),
            P("ctx", None),
            P("ctx", None),
            P("ctx", "tp"),
            P("ctx", "tp"),
            P("ctx", "tp"),
            P("ctx", "tp"),
            P("ctx", "tp"),
            P("ctx", "tp"),
            P("ctx"),
            P("ctx"),
            P("ctx"),
            P("ctx"),
        ),
        check_vma=False,
    )
```

```python
import functools
import math

import jax
import jax.numpy as jnp
from jax import lax
from jax.experimental import pallas as pl
from jax.experimental.pallas import tpu as pltpu
from jax.sharding import PartitionSpec as P

KVR = 256
NOPE = 64
ROPE = 32
VDIM = 64
HEAD = NOPE + VDIM
WIDE = 2 * HEAD
MASKED = -1e30
SCORE_SCALE = (NOPE + ROPE) ** (-0.5)
EXP2_SCALE = SCORE_SCALE * math.log2(math.e)
FOLD_AT = 96
VMEM_LIMIT = 56 * 1024 * 1024

EPSILON = 1e-05
ROPE_BASE = 10000.0
RESIDUAL_SCALE = 1.4 / math.sqrt(62.0)


def dot_nn(left_op, right_op):
    return jnp.dot(left_op, right_op, preferred_element_type=jnp.float32)


def dot_nt(left_op, right_op):
    return lax.dot_general(
        left_op, right_op, (((1,), (1,)), ((), ())), preferred_element_type=jnp.float32
    )


def begin_of(place, starts):
    begin = jnp.zeros_like(place)
    for start in starts:
        begin = jnp.where(start <= place, start, begin)
    return begin


def pair_kind(key_block, query_block, starts, block_rows):
    key_first = key_block * block_rows
    query_first = query_block * block_rows
    early = begin_of(query_first, starts)
    late = begin_of(query_first + block_rows - 1, starts)
    needed = (key_block <= query_block) & (key_first + block_rows - 1 >= early)
    whole = (key_block < query_block) & (late <= key_first)
    return needed, whole


def mask_bias(key_block, query_block, starts, block_rows, keys_first):
    key_dim = 0 if keys_first else 1
    shape = (block_rows, block_rows)
    key_place = key_block * block_rows + lax.broadcasted_iota(jnp.int32, shape, key_dim)
    query_place = query_block * block_rows + lax.broadcasted_iota(jnp.int32, shape, 1 - key_dim)
    begin = jnp.zeros(shape, jnp.int32)
    for start in starts:
        begin = jnp.where(start <= query_place, start, begin)
    allowed = (key_place <= query_place) & (key_place >= begin)
    return jnp.where(allowed, 0.0, MASKED)


def shared_key_tile(rope_rows, block_rows):
    place = lax.broadcasted_iota(jnp.int32, (ROPE, HEAD), 0)
    lane = lax.broadcasted_iota(jnp.int32, (ROPE, HEAD), 1)
    eye = jnp.where(place == lane, 1.0, 0.0).astype(jnp.bfloat16)
    tile = dot_nn(rope_rows, eye)
    lanes = lax.broadcasted_iota(jnp.int32, (block_rows, HEAD), 1)
    ones = (lanes >= FOLD_AT) & (lanes < FOLD_AT + 3)
    return jnp.where(ones, 1.0, tile).astype(jnp.bfloat16)


def head_window(h):
    at = h * (NOPE + ROPE)
    return at // HEAD * HEAD, at % HEAD


def window_columns(heads):
    return head_window(heads - 1)[0] + WIDE


def head_groups(heads):
    return [(h, min(h + 2, heads)) for h in range(0, heads, 2)]


def forward_kernel(
    blocks, heads, seqs, meta, cq, wqb, lat, wkvb, cos, sin, qx, o_out, ob_out, u_out,
    wkvt, xs, xr, vt, top, total, acc, bias, pre,
):
    rows_all = cq.shape[0]
    block_rows = bias.shape[0]
    q_blocks = rows_all // block_rows
    starts = [meta[blocks + s] for s in range(seqs)]
    own = [meta[blocks + seqs + j] for j in range(q_blocks)]
    for first, last in head_groups(heads):
        wkvt[first * HEAD : last * HEAD, :] = (
            wkvb[:, first * HEAD : last * HEAD].astype(jnp.float32).T.astype(jnp.bfloat16)
        )
    lane = lax.broadcasted_iota(jnp.int32, (block_rows, HEAD), 1)
    for j in range(q_blocks):
        here = pl.ds(j * block_rows, block_rows)
        cos_j, sin_j = cos[here, :], sin[here, :]
        width = heads * (NOPE + ROPE)
        for at in range(0, width, WIDE):
            end = min(at + WIDE, width)
            pre[:, at:end] = dot_nt(cq[here, :], wqb[at:end, :])
        for h in range(heads):
            at, shift = head_window(h)
            own_part = pltpu.roll(pre[:, at : at + WIDE], (WIDE - shift) % WIDE, 1)[:, :HEAD]
            turned = pltpu.roll(own_part, NOPE, 1)
            left = pltpu.roll(turned, HEAD - ROPE // 2, 1)
            right = pltpu.roll(turned, ROPE // 2, 1)
            swapped = jnp.where(lane < ROPE // 2, -left, right)
            rope = jnp.where(lane < ROPE, turned * cos_j + swapped * sin_j, 0.0)
            qx[j, h, :, :HEAD] = jnp.where(lane < NOPE, own_part, 0.0).astype(jnp.bfloat16)
            qx[j, h, :, HEAD:] = rope.astype(jnp.bfloat16)
    top[...] = jnp.full(top.shape, MASKED, jnp.float32)
    total[...] = jnp.zeros(total.shape, jnp.float32)
    acc[...] = jnp.zeros(acc.shape, jnp.float32)

    def pair(j, masked):
        def one(h):
            keys = jnp.concatenate([xs[h], xr[...]], axis=1)
            scores = dot_nt(keys, qx[j, h])
            if masked:
                scores = scores + bias[...]
            old = top[j, h]
            new = jnp.maximum(old, jnp.max(scores, axis=0, keepdims=True))
            fade = jnp.exp2((old - new) * EXP2_SCALE)
            terms = jnp.exp2((scores - new) * EXP2_SCALE)
            top[j, h] = new
            total[j, h] = fade * total[j, h] + jnp.sum(terms, axis=0, keepdims=True)
            acc[j, h] = fade * acc[j, h] + dot_nn(vt[h], terms.astype(jnp.bfloat16))

        for h in range(heads):
            one(h)

    def step(r, carry):
        key_block = meta[r]
        kinds = [pair_kind(key_block, own[j], starts, block_rows) for j in range(q_blocks)]
        wanted = functools.reduce(jnp.logical_or, [k[0] for k in kinds])

        @pl.when(wanted)
        def _():
            here = pl.ds(pl.multiple_of(r * block_rows, block_rows), block_rows)
            latent = lat[here, :KVR]
            xr[...] = shared_key_tile(lat[here, KVR : KVR + ROPE], block_rows)
            for first, last in head_groups(heads):
                keys = dot_nn(latent, wkvb[:, first * HEAD : last * HEAD]).astype(jnp.bfloat16)
                values = dot_nt(wkvt[first * HEAD : last * HEAD, :], latent).astype(jnp.bfloat16)
                for h in range(first, last):
                    at = (h - first) * HEAD
                    xs[h] = keys[:, at : at + HEAD]
                    vt[h] = values[at + NOPE : at + HEAD, :]

        for j in range(q_blocks):
            needed, whole = kinds[j]

            @pl.when(needed & whole)
            def _():
                pair(j, False)

            @pl.when(needed & jnp.logical_not(whole))
            def _():
                bias[...] = mask_bias(key_block, own[j], starts, block_rows, True)
                pair(j, True)

        return carry

    lax.fori_loop(0, blocks, step, 0)
    for j in range(q_blocks):
        here = pl.ds(j * block_rows, block_rows)
        for first, last in head_groups(heads):
            parts = []
            for h in range(first, last):
                parts.append(acc[j, h] * (1.0 / total[j, h]))
                u_out[j, h : h + 1, :] = top[j, h] + jnp.log2(total[j, h]) * (1.0 / EXP2_SCALE)
            if len(parts) == 1:
                parts.append(jnp.zeros_like(parts[0]))
            both = jnp.concatenate(parts, axis=0).T
            width = (last - first) * VDIM
            o_out[here, first * VDIM : first * VDIM + width] = both[:, :width]
            ob_out[here, first * VDIM : first * VDIM + width] = both[:, :width].astype(jnp.bfloat16)


def attention_forward(meta, cq, wqb, lat, wkvb, cos, sin, block_rows, seqs):
    heads = wkvb.shape[1] // HEAD
    blocks = lat.shape[0] // block_rows
    rows = cq.shape[0]
    q_blocks = rows // block_rows
    vmem = pl.BlockSpec(memory_space=pltpu.VMEM)
    pairs = q_blocks * blocks * heads // 2
    return pl.pallas_call(
        functools.partial(forward_kernel, blocks, heads, seqs),
        out_shape=(
            jax.ShapeDtypeStruct((q_blocks, heads, block_rows, WIDE), jnp.bfloat16),
            jax.ShapeDtypeStruct((rows, heads * VDIM), jnp.float32),
            jax.ShapeDtypeStruct((rows, heads * VDIM), jnp.bfloat16),
            jax.ShapeDtypeStruct((q_blocks, 16 * -(-heads // 16), block_rows), jnp.float32),
        ),
        in_specs=[pl.BlockSpec(memory_space=pltpu.SMEM)] + [vmem] * 6,
        out_specs=(vmem,) * 4,
        scratch_shapes=[
            pltpu.VMEM((heads * HEAD, KVR), jnp.bfloat16),
            pltpu.VMEM((heads, block_rows, HEAD), jnp.bfloat16),
            pltpu.VMEM((block_rows, HEAD), jnp.bfloat16),
            pltpu.VMEM((heads, VDIM, block_rows), jnp.bfloat16),
            pltpu.VMEM((q_blocks, heads, 1, block_rows), jnp.float32),
            pltpu.VMEM((q_blocks, heads, 1, block_rows), jnp.float32),
            pltpu.VMEM((q_blocks, heads, VDIM, block_rows), jnp.float32),
            pltpu.VMEM((block_rows, block_rows), jnp.float32),
            pltpu.VMEM((block_rows, window_columns(heads)), jnp.float32),
        ],
        compiler_params=pltpu.CompilerParams(vmem_limit_bytes=VMEM_LIMIT),
        cost_estimate=pl.CostEstimate(
            flops=pairs * 4 * block_rows * block_rows * WIDE,
            bytes_accessed=16 * 1024 * 1024,
            transcendentals=pairs * block_rows * block_rows,
        ),
        name="attention_forward",
    )(meta, cq, wqb, lat, wkvb, cos, sin)


def three_terms(column):
    first = column.astype(jnp.bfloat16).astype(jnp.float32)
    rest = column - first
    second = rest.astype(jnp.bfloat16).astype(jnp.float32)
    return first, second, rest - second


def fold_in(tile, column, lane):
    for k, term in enumerate(three_terms(column)):
        tile = jnp.where(lane == FOLD_AT + k, term, tile)
    return tile


def backward_kernel(
    blocks, heads, seqs, meta, qx, u_in, o_in, dob, lat, wkvb, cos, sin, dq_out, dlat, gkvb,
    xs, xr, qo, qt, dt, dq, dkv, dkpe, gsum, bias, flat,
):
    block_rows = bias.shape[0]
    q_blocks = qx.shape[0]
    starts = [meta[blocks + s] for s in range(seqs)]
    own = [meta[blocks + seqs + j] for j in range(q_blocks)]
    lane = lax.broadcasted_iota(jnp.int32, (block_rows, HEAD), 1)
    for j in range(q_blocks):
        here = pl.ds(j * block_rows, block_rows)
        logs = u_in[j].T
        for first, last in head_groups(heads):
            d_pair = dob[here, first * VDIM : first * VDIM + HEAD].astype(jnp.float32)
            weighted = d_pair * o_in[here, first * VDIM : first * VDIM + HEAD]
            turned = pltpu.roll(d_pair, VDIM, 1)
            for h in range(first, last):
                mine = lane < VDIM if h == first else lane >= VDIM
                delta = jnp.sum(jnp.where(mine, weighted, 0.0), axis=1, keepdims=True)
                d_head = jnp.where(lane >= VDIM, turned if h == first else d_pair, 0.0)
                q_first = qx[j, h, :, :HEAD].astype(jnp.float32)
                q_second = qx[j, h, :, HEAD:].astype(jnp.float32)
                qo[j, h, :block_rows, :HEAD] = qx[j, h, :, :HEAD]
                qo[j, h, :block_rows, HEAD:] = fold_in(q_second, -logs[:, h : h + 1], lane).astype(
                    jnp.bfloat16
                )
                qo[j, h, block_rows:, :HEAD] = d_head.astype(jnp.bfloat16)
                qo[j, h, block_rows:, HEAD:] = fold_in(
                    jnp.zeros((block_rows, HEAD), jnp.float32), -delta, lane
                ).astype(jnp.bfloat16)
                qt[j, h, :NOPE, :] = q_first.T[:NOPE, :].astype(jnp.bfloat16)
                qt[j, h, NOPE:, :] = q_second.T[:ROPE, :].astype(jnp.bfloat16)
                dt[j, h] = d_head.T[VDIM:, :].astype(jnp.bfloat16)
    dq[...] = jnp.zeros(dq.shape, jnp.float32)
    gsum[...] = jnp.zeros(gsum.shape, jnp.float32)

    def pair(j, masked):
        def one(h):
            keys = jnp.concatenate([xs[h], xr[...]], axis=1)
            both = dot_nt(qo[j, h], keys)
            scores = both[:block_rows] * EXP2_SCALE
            if masked:
                scores = scores + bias[...]
            probs = jnp.exp2(scores)
            d_scores = (probs * both[block_rows:]).astype(jnp.bfloat16)
            dq[j, h] += dot_nn(d_scores, keys)
            d_keys = dot_nn(qt[j, h], d_scores)
            dkv[h, :NOPE, :] += d_keys[:NOPE]
            dkpe[...] += d_keys[NOPE:]
            dkv[h, NOPE:, :] += dot_nn(dt[j, h], probs.astype(jnp.bfloat16))

        for h in range(heads):
            one(h)

    def step(r, carry):
        key_block = meta[r]
        kinds = [pair_kind(key_block, own[j], starts, block_rows) for j in range(q_blocks)]
        wanted = functools.reduce(jnp.logical_or, [k[0] for k in kinds])
        here = pl.ds(pl.multiple_of(r * block_rows, block_rows), block_rows)

        @pl.when(wanted)
        def _():
            latent = lat[here, :KVR]
            xr[...] = shared_key_tile(lat[here, KVR : KVR + ROPE], block_rows)
            for first, last in head_groups(heads):
                keys = dot_nn(latent, wkvb[:, first * HEAD : last * HEAD]).astype(jnp.bfloat16)
                for h in range(first, last):
                    xs[h] = keys[:, (h - first) * HEAD : (h - first + 1) * HEAD]
            dkv[...] = jnp.zeros(dkv.shape, jnp.float32)
            dkpe[...] = jnp.zeros(dkpe.shape, jnp.float32)

        for j in range(q_blocks):
            needed, whole = kinds[j]

            @pl.when(needed & whole)
            def _():
                pair(j, False)

            @pl.when(needed & jnp.logical_not(whole))
            def _():
                bias[...] = mask_bias(key_block, own[j], starts, block_rows, False)
                pair(j, True)

        @pl.when(wanted)
        def _():
            latent = lat[here, :KVR]
            d_latent = jnp.zeros((KVR, block_rows), jnp.float32)
            for h in range(heads):
                d_head = jnp.concatenate(
                    [dkv[h, :NOPE, :] * SCORE_SCALE, dkv[h, NOPE:, :]], axis=0
                ).astype(jnp.bfloat16)
                d_latent += dot_nn(wkvb[:, h * HEAD : (h + 1) * HEAD], d_head)
                gsum[h * HEAD : (h + 1) * HEAD, :] += dot_nn(d_head, latent)
            dlat[here, :KVR] = d_latent.T.astype(jnp.bfloat16)
            rope = jnp.concatenate(
                [dkpe[...] * SCORE_SCALE, jnp.zeros((HEAD - ROPE, block_rows), jnp.float32)], axis=0
            )
            dlat[here, KVR:] = rope.T[:, :ROPE].astype(jnp.bfloat16)

        @pl.when(jnp.logical_not(wanted))
        def _():
            dlat[here, :] = jnp.zeros((block_rows, KVR + ROPE), jnp.bfloat16)

        return carry

    lax.fori_loop(0, blocks, step, 0)
    for h in range(heads):
        gkvb[:, h * HEAD : (h + 1) * HEAD] = gsum[h * HEAD : (h + 1) * HEAD, :].T.astype(
            jnp.bfloat16
        )
    for j in range(q_blocks):
        here = pl.ds(j * block_rows, block_rows)
        cos_j, sin_j = cos[here, :], sin[here, :]
        flat[...] = jnp.zeros(flat.shape, jnp.float32)
        for h in range(heads):
            nope = jnp.where(lane < NOPE, dq[j, h, :, :HEAD], 0.0)
            rope = dq[j, h, :, HEAD:]
            shifted = rope * sin_j
            left = pltpu.roll(shifted, HEAD - ROPE // 2, 1)
            right = pltpu.roll(shifted, ROPE // 2, 1)
            swapped = jnp.where(lane < ROPE // 2, left, jnp.where(lane < ROPE, -right, 0.0))
            back = pltpu.roll(jnp.where(lane < ROPE, rope * cos_j + swapped, 0.0), NOPE, 1)
            whole = jnp.concatenate([(nope + back) * SCORE_SCALE, jnp.zeros_like(nope)], axis=1)
            at, shift = head_window(h)
            flat[:, at : at + WIDE] += pltpu.roll(whole, shift, 1)
        dq_out[here, :] = flat[:, : heads * (NOPE + ROPE)].astype(jnp.bfloat16)


def attention_backward(meta, qx, u_in, o_in, dob, lat, wkvb, cos, sin, block_rows, seqs):
    heads = wkvb.shape[1] // HEAD
    blocks = lat.shape[0] // block_rows
    q_blocks = qx.shape[0]
    rows = q_blocks * block_rows
    odd = -(heads * VDIM) % HEAD
    if odd:
        o_in = jnp.pad(o_in, ((0, 0), (0, odd)))
        dob = jnp.pad(dob, ((0, 0), (0, odd)))
    vmem = pl.BlockSpec(memory_space=pltpu.VMEM)
    pairs = q_blocks * blocks * heads // 2
    return pl.pallas_call(
        functools.partial(backward_kernel, blocks, heads, seqs),
        out_shape=(
            jax.ShapeDtypeStruct((rows, heads * (NOPE + ROPE)), jnp.bfloat16),
            jax.ShapeDtypeStruct((lat.shape[0], KVR + ROPE), jnp.bfloat16),
            jax.ShapeDtypeStruct((KVR, heads * HEAD), jnp.bfloat16),
        ),
        in_specs=[pl.BlockSpec(memory_space=pltpu.SMEM)] + [vmem] * 8,
        out_specs=(vmem,) * 3,
        scratch_shapes=[
            pltpu.VMEM((heads, block_rows, HEAD), jnp.bfloat16),
            pltpu.VMEM((block_rows, HEAD), jnp.bfloat16),
            pltpu.VMEM((q_blocks, heads, 2 * block_rows, WIDE), jnp.bfloat16),
            pltpu.VMEM((q_blocks, heads, NOPE + ROPE, block_rows), jnp.bfloat16),
            pltpu.VMEM((q_blocks, heads, VDIM, block_rows), jnp.bfloat16),
            pltpu.VMEM((q_blocks, heads, block_rows, WIDE), jnp.float32),
            pltpu.VMEM((heads, HEAD, block_rows), jnp.float32),
            pltpu.VMEM((ROPE, block_rows), jnp.float32),
            pltpu.VMEM((heads * HEAD, KVR), jnp.float32),
            pltpu.VMEM((block_rows, block_rows), jnp.float32),
            pltpu.VMEM((block_rows, window_columns(heads)), jnp.float32),
        ],
        compiler_params=pltpu.CompilerParams(vmem_limit_bytes=VMEM_LIMIT),
        cost_estimate=pl.CostEstimate(
            flops=pairs * 8 * block_rows * block_rows * WIDE,
            bytes_accessed=24 * 1024 * 1024,
            transcendentals=pairs * block_rows * block_rows,
        ),
        name="attention_backward",
    )(meta, qx, u_in, o_in, dob, lat, wkvb, cos, sin)


MESH = pl.DeviceIdType.MESH


class Scatter:
    def __init__(self, n, given=None, left=None, right=None):
        self.operands = [given] if given is not None else [left, right]
        self.is_given = given is not None
        self.rows = self.operands[0].shape[0] // n
        self.columns = self.operands[-1].shape[1]
        self.depth = 0 if self.is_given else right.shape[0]
        self.parts = 2 if self.rows % 32 == 0 else 1


def scatter_blocks(bits_left):
    chips = []
    for value in range(1 << len(bits_left)):
        chip = 0
        for at, bit in enumerate(bits_left):
            chip = chip + (((value >> at) & 1) << (bit - 1))
        chips.append(chip)
    return chips


def scatter_kernel(n, items, *refs):
    count = n.bit_length() - 1
    me = lax.axis_index("ctx")
    refs = list(refs)
    take = lambda k: [refs.pop(0) for _ in range(k)]
    inputs = [take(len(item.operands)) for item in items]
    outputs = take(len(items))
    held, sent, landed, core_sems, step_sems = [], [], [], [], []
    for item in items:
        held.append(refs.pop(0))
        sent.append(None if item.is_given else refs.pop(0))
        landed.append(take(count - 1))
        core_sems.append(take(2))
        step_sems.append([take(2) for _ in range(count - 1)])
    barrier = pltpu.get_barrier_semaphore()
    for bit in range(count):
        pl.semaphore_signal(barrier, inc=1, device_id={"ctx": me ^ (1 << bit)}, device_id_type=MESH)
    pl.semaphore_wait(barrier, count)
    core = me & 1
    chips = n // 2
    orders = (tuple(range(1, count)), tuple(range(count - 1, 0, -1)))

    def columns_of(item):
        return [(c, min(c + 512, item.columns)) for c in range(0, item.columns, 512)]

    def product(k, dest, first, last):
        item = items[k]
        left, right = inputs[k]
        at = pl.ds(pl.multiple_of(dest * item.rows, 16), item.rows)
        return dot_nn(left[at, :], right[:, first:last])

    def core_copy(k, chip):
        item = items[k]
        if item.is_given:
            at = pl.ds(pl.multiple_of((2 * chip + 1 - core) * item.rows, 16), item.rows)
            source = inputs[k][0].at[at, :]
        else:
            source = sent[k].at[chip]
        return pltpu.make_async_remote_copy(
            src_ref=source,
            dst_ref=held[k].at[chip],
            send_sem=core_sems[k][0].at[chip],
            recv_sem=core_sems[k][1].at[chip],
            device_id={"ctx": me ^ 1},
            device_id_type=MESH,
        )

    def step_copies(k, step):
        item = items[k]
        half = item.rows // item.parts
        copies = []
        for part, order in enumerate(orders[: item.parts]):
            bit = order[step]
            left = sorted(order[step + 1 :])
            fixed = [b for b in order[:step]]
            at = pl.ds(part * half, half)
            for slot, free in enumerate(scatter_blocks(left)):
                keep = free + ((me >> bit) & 1) * (1 << (bit - 1))
                send = free + (1 - ((me >> bit) & 1)) * (1 << (bit - 1))
                for b in fixed:
                    own = ((me >> b) & 1) * (1 << (b - 1))
                    keep, send = keep + own, send + own
                copies.append(
                    (
                        pltpu.make_async_remote_copy(
                            src_ref=held[k].at[send, at, :],
                            dst_ref=landed[k][step].at[slot, at, :],
                            send_sem=step_sems[k][step][0].at[part, slot],
                            recv_sem=step_sems[k][step][1].at[part, slot],
                            device_id={"ctx": me ^ (1 << bit)},
                            device_id_type=MESH,
                        ),
                        keep,
                        slot,
                        at,
                    )
                )
        return copies

    def start_core(k):
        item = items[k]

        def body(chip, carry):
            if not item.is_given:
                for first, last in columns_of(item):
                    sent[k][chip, :, first:last] = product(
                        k, 2 * chip + 1 - core, first, last
                    ).astype(jnp.bfloat16)
            core_copy(k, chip).start()
            return carry

        lax.fori_loop(0, chips, body, 0)

    def finish_core(k):
        item = items[k]

        def body(chip, carry):
            core_copy(k, chip).wait_recv()
            at = pl.ds(pl.multiple_of((2 * chip + core) * item.rows, 16), item.rows)
            for first, last in columns_of(item):
                if item.is_given:
                    own = inputs[k][0][at, first:last].astype(jnp.float32)
                else:
                    own = product(k, 2 * chip + core, first, last)
                total = own + held[k][chip, :, first:last].astype(jnp.float32)
                held[k][chip, :, first:last] = total.astype(jnp.bfloat16)
            return carry

        lax.fori_loop(0, chips, body, 0)

    def start_step(k, step):
        for copy, _, _, _ in step_copies(k, step):
            copy.start()

    def finish_step(k, step):
        item = items[k]
        for copy, keep, slot, at in step_copies(k, step):
            copy.wait_recv()
            for first, last in columns_of(item):
                total = held[k][keep, at, first:last].astype(jnp.float32) + landed[k][step][
                    slot, at, first:last
                ].astype(jnp.float32)
                if step == count - 2:
                    outputs[k][at, first:last] = total
                else:
                    held[k][keep, at, first:last] = total.astype(jnp.bfloat16)

    every = range(len(items))
    start_core(0)
    for k in every:
        if k + 1 < len(items):
            start_core(k + 1)
        finish_core(k)
        start_step(k, 0)
    for step in range(count - 1):
        for k in every:
            finish_step(k, step)
            if step + 1 < count - 1:
                start_step(k, step + 1)
    for k in every:

        def drain(chip, carry, k=k):
            core_copy(k, chip).wait_send()
            return carry

        lax.fori_loop(0, chips, drain, 0)
        for step in range(count - 1):
            for copy, _, _, _ in step_copies(k, step):
                copy.wait_send()


def scatter_over_ctx(n, items, collective_id):
    vmem = pl.BlockSpec(memory_space=pltpu.VMEM)
    count = n.bit_length() - 1
    scratch = []
    flops = 0
    for item in items:
        scratch.append(pltpu.VMEM((n // 2, item.rows, item.columns), jnp.bfloat16))
        if not item.is_given:
            scratch.append(pltpu.VMEM((n // 2, item.rows, item.columns), jnp.bfloat16))
        scratch += [
            pltpu.VMEM((n >> (step + 2), item.rows, item.columns), jnp.bfloat16)
            for step in range(count - 1)
        ]
        scratch += [pltpu.SemaphoreType.DMA((n // 2,))] * 2
        for step in range(count - 1):
            scratch += [pltpu.SemaphoreType.DMA((2, n >> (step + 2)))] * 2
        flops += 2 * n * item.rows * item.columns * item.depth
    operands = [array for item in items for array in item.operands]
    return pl.pallas_call(
        functools.partial(scatter_kernel, n, items),
        out_shape=tuple(
            jax.ShapeDtypeStruct((item.rows, item.columns), jnp.float32) for item in items
        ),
        in_specs=[vmem] * len(operands),
        out_specs=(vmem,) * len(items),
        scratch_shapes=scratch,
        compiler_params=pltpu.CompilerParams(
            vmem_limit_bytes=VMEM_LIMIT, collective_id=collective_id, has_side_effects=True
        ),
        cost_estimate=pl.CostEstimate(
            flops=flops, bytes_accessed=64 * 1024 * 1024, transcendentals=0
        ),
        name=f"scatter_over_ctx_{collective_id}",
    )(*operands)


def gather_kernel(n, own, out, local_sem, step_sends, step_lands, core_sends, core_lands):
    count = n.bit_length() - 1
    me = lax.axis_index("ctx")
    rows = own.shape[0]
    half = rows // 2
    barrier = pltpu.get_barrier_semaphore()
    for bit in range(count):
        pl.semaphore_signal(barrier, inc=1, device_id={"ctx": me ^ (1 << bit)}, device_id_type=MESH)
    pl.semaphore_wait(barrier, count)
    orders = (tuple(range(1, count)), tuple(range(count - 1, 0, -1)))
    local = pltpu.make_async_copy(own, out.at[me], local_sem)
    local.start()

    def chip_copy(part, step, slot, block, first):
        at = pl.ds(part * half, half)
        return pltpu.make_async_remote_copy(
            src_ref=own.at[at, :] if first else out.at[block, at, :],
            dst_ref=out.at[block, at, :],
            send_sem=step_sends.at[part, step, slot],
            recv_sem=step_lands.at[part, step, slot],
            device_id={"ctx": me ^ (1 << orders[part][step])},
            device_id_type=MESH,
        )

    def core_copy(block, slot, first):
        return pltpu.make_async_remote_copy(
            src_ref=own if first else out.at[block],
            dst_ref=out.at[block],
            send_sem=core_sends.at[slot],
            recv_sem=core_lands.at[slot],
            device_id={"ctx": me ^ 1},
            device_id_type=MESH,
        )

    started = []
    core_copy(me, 0, True).start()
    for step in range(count - 1):
        for part, order in enumerate(orders):
            for slot in range(1 << step):
                flips = 0
                for at in range(step):
                    flips |= ((slot >> at) & 1) << order[at]
                copy = chip_copy(part, step, slot, me ^ flips, slot == 0)
                copy.start()
                started.append(copy)
        for part, order in enumerate(orders):
            for slot in range(1 << step):
                chip_copy(part, step, slot, me, slot == 0).wait_recv()
    for chip in range(1, n // 2):
        core_copy(me ^ (2 * chip), chip, False).start()
    for chip in range(n // 2):
        core_copy(me, chip, chip == 0).wait_recv()
    for copy in started:
        copy.wait_send()
    for chip in range(n // 2):
        core_copy(me, chip, chip == 0).wait_send()
    local.wait()


def gather_over_ctx(n, own, collective_id):
    count = n.bit_length() - 1
    vmem = pl.BlockSpec(memory_space=pltpu.VMEM)
    slots = max(n // 4, 1)
    gathered = pl.pallas_call(
        functools.partial(gather_kernel, n),
        out_shape=jax.ShapeDtypeStruct((n,) + own.shape, own.dtype),
        in_specs=[vmem],
        out_specs=vmem,
        scratch_shapes=[
            pltpu.SemaphoreType.DMA,
            pltpu.SemaphoreType.DMA((2, count - 1, slots)),
            pltpu.SemaphoreType.DMA((2, count - 1, slots)),
            pltpu.SemaphoreType.DMA((n // 2,)),
            pltpu.SemaphoreType.DMA((n // 2,)),
        ],
        compiler_params=pltpu.CompilerParams(
            vmem_limit_bytes=VMEM_LIMIT, collective_id=collective_id, has_side_effects=True
        ),
        cost_estimate=pl.CostEstimate(
            flops=0, bytes_accessed=16 * 1024 * 1024, transcendentals=0
        ),
        name=f"gather_over_ctx_{collective_id}",
    )(own)
    return gathered.reshape((-1,) + own.shape[1:])


CHUNK = 32
BLOCK = 4 * CHUNK
MIDDLE_VMEM = 62 * 1024 * 1024


def middle_kernel(
    n, ob, tokens, cot, gain, w_out, w_gate, w_up, w_down,
    tt, d_out, f_out, act_out, dg_out, du_out,
    own, up, wo, wg, wu, wd, h2, dfs, d_acc, f_acc,
    w_sems, up_send, up_land, down_send, back_send, down_land,
):
    me = lax.axis_index("tp")
    root = (n - 1) // 2
    width = tokens.shape[1]
    hidden = wg.shape[0]
    chunks = own.shape[0]
    blocks = chunks // 4
    root_lag = n - 1 - root
    land_lag = 2 * root_lag
    block_lag = -(-(4 + land_lag) // 4)
    tiles = [(c, min(c + 512, width)) for c in range(0, width, 512)]
    quarter = hidden // 4 // 128 * 128
    cuts = [0, quarter, 2 * quarter, 3 * quarter, hidden]
    loads = [
        pltpu.make_async_copy(w_out, wo, w_sems.at[0]),
        pltpu.make_async_copy(w_gate, wg, w_sems.at[1]),
        pltpu.make_async_copy(w_up, wu, w_sems.at[2]),
        pltpu.make_async_copy(w_down, wd, w_sems.at[3]),
    ]
    for load in loads:
        load.start()
    barrier = pltpu.get_barrier_semaphore()
    has_left, has_right = me > 0, me < n - 1
    for there, other in ((has_left, me - 1), (has_right, me + 1)):

        @pl.when(there)
        def _(other=other):
            pl.semaphore_signal(barrier, inc=1, device_id={"tp": other}, device_id_type=MESH)

    @pl.when(has_left & has_right)
    def _():
        pl.semaphore_wait(barrier, 2)

    @pl.when(jnp.logical_not(has_left & has_right))
    def _():
        pl.semaphore_wait(barrier, 1)

    def copy_to(source, target, send, land, c, other):
        return pltpu.make_async_remote_copy(
            src_ref=source.at[c],
            dst_ref=target.at[c],
            send_sem=send.at[c],
            recv_sem=land.at[c],
            device_id={"tp": other},
            device_id_type=MESH,
        )

    def rise_left(c):
        return copy_to(own, up, up_send, up_land, c, me + 1)

    def rise_right(c):
        return copy_to(own, up, up_send, up_land, c, me - 1)

    def rise_last(c):
        return copy_to(own, tt, up_send, down_land, c, me - 1)

    def fall_right(c):
        return copy_to(tt, tt, down_send, down_land, c, me + 1)

    def fall_left(c):
        return copy_to(tt, tt, back_send, down_land, c, me - 1)

    rises = [(me < root, rise_left)] if root else []
    rises.append((me == root + 1, rise_last))
    if n - 1 > root + 1:
        rises.append((me > root + 1, rise_right))

    def rise(c):
        for who, copy in rises:

            @pl.when(who)
            def _(copy=copy):
                copy(c).start()

    def inside(c):
        return (c >= 0) & (c < chunks)

    def added(refs, c):
        total = refs[0][c].astype(jnp.float32)
        for ref in refs[1:]:
            total = total + ref[c].astype(jnp.float32)
        return total.astype(jnp.bfloat16)

    def duties(t):
        leaf = (me == 0) | (me == n - 1) if root else me == n - 1
        @pl.when(leaf & (t < chunks))
        def _():
            rise(t)

        if n > 3:
            c = t - jnp.where(me < root, me, n - 1 - me)

            @pl.when((me != root) & has_left & has_right & inside(c))
            def _():
                rise_right(c).wait_recv()
                own[c] = added([own, up], c)
                rise(c)

        c_root = t - root_lag

        @pl.when((me == root) & inside(c_root))
        def _():
            if root:
                rise_left(c_root).wait_recv()
            fall_right(c_root).wait_recv()
            tt[c_root] = added([own, up, tt] if root else [own, tt], c_root)
            fall_right(c_root).start()
            if root:
                fall_left(c_root).start()

        c_fall = t - root_lag - jnp.where(me < root, root - me, me - root)

        @pl.when((me != root) & inside(c_fall))
        def _():
            fall_right(c_fall).wait_recv()

            @pl.when((me > root) & has_right)
            def _():
                fall_right(c_fall).start()

            @pl.when((me < root) & has_left)
            def _():
                fall_left(c_fall).start()

        c_norm = t - land_lag

        @pl.when(inside(c_norm))
        def _():
            rows = pl.ds(pl.multiple_of(c_norm * CHUNK, CHUNK), CHUNK)
            middle = tokens[rows, :].astype(jnp.float32) + RESIDUAL_SCALE * tt[c_norm].astype(
                jnp.float32
            )
            scale = lax.rsqrt(jnp.mean(middle * middle, axis=-1, keepdims=True) + EPSILON)
            slot = lax.rem(lax.div(c_norm, 4), 2)
            h2[slot, pl.ds(pl.multiple_of(lax.rem(c_norm, 4) * CHUNK, CHUNK), CHUNK), :] = (
                middle * scale * gain[...]
            ).astype(jnp.bfloat16)

    def project(b):
        rows = pl.ds(pl.multiple_of(b * BLOCK, BLOCK), BLOCK)
        for first, last in tiles:
            part = dot_nt(ob[rows, :], wo[first:last, :]).astype(jnp.bfloat16)
            for k in range(4):
                own[4 * b + k, :, first:last] = part[k * CHUNK : (k + 1) * CHUNK, :]

    def feed(b, i):
        rows = pl.ds(pl.multiple_of(b * BLOCK, BLOCK), BLOCK)
        slot = lax.rem(b, 2)
        first, last = cuts[i], cuts[i + 1]
        if i == 0:
            dfs[...] = (RESIDUAL_SCALE * cot[rows, :].astype(jnp.float32)).astype(jnp.bfloat16)
        gate = dot_nt(h2[slot], wg[first:last, :])
        upper = dot_nt(h2[slot], wu[first:last, :])
        d_act = dot_nt(dfs[...], wd[first:last, :])
        sig = jax.nn.sigmoid(gate)
        silu = gate * sig
        act = (silu * upper).astype(jnp.bfloat16)
        dg = (d_act * upper * sig * (1.0 + gate * (1.0 - sig))).astype(jnp.bfloat16)
        du = (d_act * silu).astype(jnp.bfloat16)
        act_out[rows, first:last] = act
        dg_out[rows, first:last] = dg
        du_out[rows, first:last] = du
        for lo, hi in tiles:
            d_part = dot_nn(dg, wg[first:last, lo:hi]) + dot_nn(du, wu[first:last, lo:hi])
            f_part = dot_nn(act, wd[first:last, lo:hi])
            if i:
                d_part = d_part + d_acc[:, lo:hi]
                f_part = f_part + f_acc[:, lo:hi]
            if i < 3:
                d_acc[:, lo:hi] = d_part
                f_acc[:, lo:hi] = f_part
            else:
                d_out[rows, lo:hi] = d_part.astype(jnp.bfloat16)
                f_out[rows, lo:hi] = f_part.astype(jnp.bfloat16)

    loads[0].wait()

    def outer(o, carry):
        @pl.when(o < blocks)
        def _():
            project(o)

        @pl.when(o == block_lag)
        def _():
            for load in loads[1:]:
                load.wait()

        for i in range(4):
            duties(4 * o + i)

            @pl.when(o >= block_lag)
            def _(i=i):
                feed(o - block_lag, i)

        return carry

    lax.fori_loop(0, blocks + block_lag, outer, 0)

    def drain(c, carry):
        @pl.when(me != root)
        def _():
            rise_right(c).wait_send()

        @pl.when((me >= root) & has_right)
        def _():
            fall_right(c).wait_send()

        @pl.when((me <= root) & has_left)
        def _():
            fall_left(c).wait_send()

        return carry

    lax.fori_loop(0, chunks, drain, 0)


def middle_layer(n, ob, tokens, cot, gain, w_out, w_gate, w_up, w_down, collective_id):
    rows, width = tokens.shape
    hidden = w_gate.shape[0]
    chunks = rows // CHUNK
    vmem = pl.BlockSpec(memory_space=pltpu.VMEM)
    anywhere = pl.BlockSpec(memory_space=pl.ANY)
    half = jnp.bfloat16
    dma = pltpu.SemaphoreType.DMA
    attn, d_part, f_part, act, dg, du = pl.pallas_call(
        functools.partial(middle_kernel, n),
        out_shape=(
            jax.ShapeDtypeStruct((chunks, CHUNK, width), half),
            jax.ShapeDtypeStruct((rows, width), half),
            jax.ShapeDtypeStruct((rows, width), half),
            jax.ShapeDtypeStruct((rows, hidden), half),
            jax.ShapeDtypeStruct((rows, hidden), half),
            jax.ShapeDtypeStruct((rows, hidden), half),
        ),
        in_specs=[vmem] * 4 + [anywhere] * 4,
        out_specs=(vmem,) * 6,
        scratch_shapes=[
            pltpu.VMEM((chunks, CHUNK, width), half),
            pltpu.VMEM((chunks, CHUNK, width), half),
            pltpu.VMEM(w_out.shape, half),
            pltpu.VMEM(w_gate.shape, half),
            pltpu.VMEM(w_up.shape, half),
            pltpu.VMEM(w_down.shape, half),
            pltpu.VMEM((2, BLOCK, width), half),
            pltpu.VMEM((BLOCK, width), half),
            pltpu.VMEM((BLOCK, width), jnp.float32),
            pltpu.VMEM((BLOCK, width), jnp.float32),
            dma((4,)),
            dma((chunks,)),
            dma((chunks,)),
            dma((chunks,)),
            dma((chunks,)),
            dma((chunks,)),
        ],
        compiler_params=pltpu.CompilerParams(
            vmem_limit_bytes=MIDDLE_VMEM, collective_id=collective_id, has_side_effects=True
        ),
        cost_estimate=pl.CostEstimate(
            flops=2 * rows * width * (6 * hidden + ob.shape[1]),
            bytes_accessed=64 * 1024 * 1024,
            transcendentals=rows * hidden,
        ),
        name=f"middle_layer_{collective_id}",
    )(ob, tokens, cot, gain.reshape(1, -1), w_out, w_gate, w_up, w_down)
    return attn.reshape(rows, width), d_part, f_part, act, dg, du


def dot_plain(left_op, right_op):
    return jnp.dot(left_op, right_op, preferred_element_type=jnp.float32)


def dot_rows(left_op, right_op):
    return lax.dot_general(
        left_op, right_op, (((0,), (0,)), ((), ())), preferred_element_type=jnp.float32
    )


def dot_cols(left_op, right_op):
    return lax.dot_general(
        left_op, right_op, (((1,), (1,)), ((), ())), preferred_element_type=jnp.float32
    )


def rms_scale(values):
    return lax.rsqrt(jnp.mean(values * values, axis=-1, keepdims=True) + EPSILON)


def rms_back(incoming, values, inv_rms, gain_vec):
    weighted = incoming * gain_vec
    d_values = inv_rms * weighted - values * inv_rms**3 * jnp.mean(
        weighted * values, axis=-1, keepdims=True
    )
    return (d_values, jnp.sum(incoming * values * inv_rms, axis=0))


def token_places(block_map, doc_lengths, per_device, devices):
    all_rows = per_device * devices
    half_block = per_device // 2
    token_rows = jnp.arange(all_rows, dtype=jnp.int32)
    device_of = token_rows // per_device
    within = token_rows % per_device
    wanted = device_of * 2 + within // half_block
    select = wanted[:, None] == jnp.arange(2 * devices, dtype=jnp.int32)[None, :]
    blocks = jnp.sum(jnp.where(select, block_map.reshape(-1)[None, :], 0), axis=1)
    places = blocks * half_block + within % half_block
    ends = jnp.cumsum(doc_lengths)
    segment = jnp.sum((places[:, None] >= ends[None, :]).astype(jnp.int32), axis=1)
    starts = ends - doc_lengths
    picked = segment[:, None] == jnp.arange(doc_lengths.shape[0], dtype=jnp.int32)[None, :]
    begins = jnp.sum(jnp.where(picked, starts[None, :], 0), axis=1)
    return (places, segment, places - begins)


def tables(inside):
    half_width = ROPE // 2
    frequency = ROPE_BASE ** (-2.0 * jnp.arange(half_width, dtype=jnp.float32) / ROPE)
    angles = inside.astype(jnp.float32)[:, None] * frequency[None, :]
    cosine_table = jnp.concatenate([jnp.cos(angles), jnp.cos(angles)], axis=1)
    sine_table = jnp.concatenate([jnp.sin(angles), jnp.sin(angles)], axis=1)
    return (cosine_table, sine_table)


def rotate(values, cosine_table, sine_table):
    half_width = values.shape[-1] // 2
    turned = jnp.concatenate([-values[..., half_width:], values[..., :half_width]], axis=-1)
    return values * cosine_table + turned * sine_table


def rotate_back(incoming, cosine_table, sine_table):
    half_width = incoming.shape[-1] // 2
    shifted = incoming * sine_table
    turned = jnp.concatenate([shifted[..., half_width:], -shifted[..., :half_width]], axis=-1)
    return incoming * cosine_table + turned


def wide_tables(inside):
    half_width = ROPE // 2
    lane = jnp.arange(HEAD, dtype=jnp.int32)
    frequency = ROPE_BASE ** (-2.0 * (lane % half_width).astype(jnp.float32) / ROPE)
    angles = inside.astype(jnp.float32)[:, None] * frequency[None, :]
    used = lane[None, :] < ROPE
    return jnp.where(used, jnp.cos(angles), 0.0), jnp.where(used, jnp.sin(angles), 0.0)


def on_device(
    tokens_in,
    w_qa,
    w_kva,
    w_qb,
    w_kvb,
    w_out,
    w_gate,
    w_up,
    w_down,
    gain_in,
    gain_q,
    gain_kv,
    gain_mid,
    cotangent,
    block_map,
    doc_lengths,
):
    local_rows = tokens_in.shape[0]
    half_rows = local_rows // 2
    devices = lax.axis_size("ctx")
    ctx_index = lax.axis_index("ctx")
    seqs = doc_lengths.shape[0]
    own_blocks = lax.dynamic_slice_in_dim(block_map, ctx_index, 1, 0)[0]
    ends = jnp.cumsum(doc_lengths)
    starts = ends - doc_lengths
    meta = jnp.concatenate([block_map.reshape(-1), starts, own_blocks])
    within = jnp.arange(half_rows, dtype=jnp.int32)
    query_place = (own_blocks[:, None] * half_rows + within[None, :]).reshape(-1)
    began = jnp.max(
        jnp.where(starts[None, :] <= query_place[:, None], starts[None, :], 0), axis=1
    )
    cosine_wide, sine_wide = wide_tables(query_place - began)
    cosine_table, sine_table = cosine_wide[:, :ROPE], sine_wide[:, :ROPE]
    head_count = w_qb.shape[1] // (NOPE + ROPE)
    tokens_f = tokens_in.astype(jnp.float32)
    scale_in = rms_scale(tokens_f)
    normed_in = (tokens_f * scale_in * gain_in).astype(jnp.bfloat16)
    kv_input = dot_plain(normed_in, w_kva)
    latent_raw = kv_input[:, :KVR]
    scale_kv = rms_scale(latent_raw)
    latent = (latent_raw * scale_kv * gain_kv).astype(jnp.bfloat16)
    key_rope = rotate(kv_input[:, KVR:], cosine_table, sine_table).astype(jnp.bfloat16)
    latents = gather_over_ctx(devices, jnp.concatenate([latent, key_rope], axis=1), 0)
    q_latent_pre = dot_plain(normed_in, w_qa)
    scale_q = rms_scale(q_latent_pre)
    q_latent = (q_latent_pre * scale_q * gain_q).astype(jnp.bfloat16)
    queries, attn_f, heads_out, log_totals = attention_forward(
        meta, q_latent, w_qb.T, latents, w_kvb, cosine_wide, sine_wide, half_rows, seqs
    )
    attention, d_part, feed_part, activation, d_gate, d_up = middle_layer(
        lax.axis_size("tp"), heads_out, tokens_in, cotangent, gain_mid, w_out, w_gate.T, w_up.T,
        w_down.T, 5,
    )
    middle = tokens_f + RESIDUAL_SCALE * attention.astype(jnp.float32)
    scale_mid = rms_scale(middle)
    normed_mid = (middle * scale_mid * gain_mid).astype(jnp.bfloat16)
    cotangent_f = cotangent.astype(jnp.float32)
    d_feed = (RESIDUAL_SCALE * cotangent_f).astype(jnp.bfloat16)
    d_normed_mid = lax.psum(d_part, "tp")
    gw_gate, gw_up, gw_down = scatter_over_ctx(
        devices,
        [
            Scatter(devices, left=normed_mid.T, right=d_gate),
            Scatter(devices, left=normed_mid.T, right=d_up),
            Scatter(devices, left=d_feed.T, right=activation),
        ],
        1,
    )
    d_normed_mid, feed_part, gw_gate, gw_up, gw_down = lax.optimization_barrier(
        (d_normed_mid, feed_part, gw_gate, gw_up, gw_down)
    )
    d_normed_mid = d_normed_mid.astype(jnp.float32)
    feed_own = lax.psum_scatter(feed_part, "tp", scatter_dimension=0, tiled=True)
    own_rows = feed_own.shape[0]
    middle_own = lax.dynamic_slice_in_dim(middle, lax.axis_index("tp") * own_rows, own_rows, 0)
    out_own = (middle_own + RESIDUAL_SCALE * feed_own.astype(jnp.float32)).astype(jnp.bfloat16)
    d_middle_norm, d_gain_mid = rms_back(d_normed_mid, middle, scale_mid, gain_mid)
    d_middle = cotangent_f + d_middle_norm
    d_attention = (RESIDUAL_SCALE * d_middle).astype(jnp.bfloat16)
    d_heads = dot_plain(d_attention, w_out).astype(jnp.bfloat16)
    d_query_pre, d_latents, gw_kvb = attention_backward(
        meta, queries, log_totals, attn_f, d_heads, latents, w_kvb, cosine_wide, sine_wide,
        half_rows, seqs,
    )
    (d_latent_part,) = scatter_over_ctx(devices, [Scatter(devices, given=d_latents)], 2)
    d_q_latent = dot_cols(d_query_pre, w_qb).astype(jnp.bfloat16)
    before_tp = jnp.concatenate([d_q_latent, d_latent_part.astype(jnp.bfloat16)], axis=1)
    before_tp, out_own = lax.optimization_barrier((before_tp, out_own))
    summed_tp = lax.psum(before_tp, "tp")
    gw_out, gw_qb, gw_kvb = scatter_over_ctx(
        devices,
        [
            Scatter(devices, left=d_attention.T, right=heads_out),
            Scatter(devices, left=q_latent.T, right=d_query_pre),
            Scatter(devices, given=gw_kvb),
        ],
        3,
    )
    summed_tp, out_own, gw_out, gw_qb, gw_kvb = lax.optimization_barrier(
        (summed_tp, out_own, gw_out, gw_qb, gw_kvb)
    )
    out = lax.all_gather(out_own, "tp", axis=0, tiled=True)
    summed_tp = summed_tp.astype(jnp.float32)
    q_rank = w_qa.shape[1]
    d_q_latent = summed_tp[:, :q_rank]
    d_latent = summed_tp[:, q_rank : q_rank + KVR]
    d_rope_sum = summed_tp[:, q_rank + KVR :]
    d_q_pre, d_gain_q = rms_back(d_q_latent, q_latent_pre, scale_q, gain_q)
    d_q_low = d_q_pre.astype(jnp.bfloat16)
    d_latent_raw, d_gain_kv = rms_back(d_latent, latent_raw, scale_kv, gain_kv)
    d_kv_input = jnp.concatenate(
        [d_latent_raw, rotate_back(d_rope_sum, cosine_table, sine_table)], axis=-1
    ).astype(jnp.bfloat16)
    d_normed_in = dot_cols(d_q_low, w_qa) + dot_cols(d_kv_input, w_kva)
    d_tokens_norm, d_gain_in = rms_back(d_normed_in, tokens_f, scale_in, gain_in)
    grad_in = d_middle + d_tokens_norm
    gains = jnp.concatenate(
        [g.reshape(devices, -1) for g in (d_gain_in, d_gain_mid, d_gain_q, d_gain_kv)], axis=1
    )
    lines = -(-gains.shape[1] // (32 * HEAD)) * 32
    gains = jnp.pad(gains, ((0, 0), (0, lines * HEAD - gains.shape[1])))
    gw_qa, gw_kva, gains = scatter_over_ctx(
        devices,
        [
            Scatter(devices, left=normed_in.T, right=d_q_low),
            Scatter(devices, left=normed_in.T, right=d_kv_input),
            Scatter(devices, given=gains.astype(jnp.bfloat16).reshape(devices * lines, HEAD)),
        ],
        4,
    )
    gains = gains.reshape(-1)
    ends = [0]
    for whole in (d_gain_in, d_gain_mid, d_gain_q, d_gain_kv):
        ends.append(ends[-1] + whole.shape[0] // devices)
    own_gains = [gains[first:last] for first, last in zip(ends, ends[1:])]
    return (
        out,
        grad_in,
        gw_qa,
        gw_kva,
        gw_qb,
        gw_kvb,
        gw_out,
        gw_gate,
        gw_up,
        gw_down,
        own_gains[0],
        own_gains[2],
        own_gains[3],
        own_gains[1],
    )


def solution(mesh):
    return jax.shard_map(
        on_device,
        mesh=mesh,
        in_specs=(
            P("ctx", None),
            P(),
            P(),
            P(None, "tp"),
            P(None, "tp"),
            P(None, "tp"),
            P(None, "tp"),
            P(None, "tp"),
            P(None, "tp"),
            P(),
            P(),
            P(),
            P(),
            P("ctx", None),
            P(),
            P(),
        ),
        out_specs=(
            P("ctx", None),
            P("ctx", None),
            P("ctx", None),
            P("ctx", None),
            P("ctx", "tp"),
            P("ctx", "tp"),
            P("ctx", "tp"),
            P("ctx", "tp"),
            P("ctx", "tp"),
            P("ctx", "tp"),
            P("ctx"),
            P("ctx"),
            P("ctx"),
            P("ctx"),
        ),
        check_vma=False,
    )
```

```python
import functools
import math

import jax
import jax.numpy as jnp
from jax import lax
from jax.experimental import pallas as pl
from jax.experimental.pallas import tpu as pltpu
from jax.sharding import PartitionSpec as P

KVR = 256
NOPE = 64
ROPE = 32
VDIM = 64
HEAD = NOPE + VDIM
WIDE = 2 * HEAD
MASKED = -1e30
SCORE_SCALE = (NOPE + ROPE) ** (-0.5)
EXP2_SCALE = SCORE_SCALE * math.log2(math.e)
FOLD_AT = 96
VMEM_LIMIT = 56 * 1024 * 1024

EPSILON = 1e-05
ROPE_BASE = 10000.0
RESIDUAL_SCALE = 1.4 / math.sqrt(62.0)


def dot_nn(left_op, right_op):
    return jnp.dot(left_op, right_op, preferred_element_type=jnp.float32)


def dot_nt(left_op, right_op):
    return lax.dot_general(
        left_op, right_op, (((1,), (1,)), ((), ())), preferred_element_type=jnp.float32
    )


def begin_of(place, starts):
    begin = jnp.zeros_like(place)
    for start in starts:
        begin = jnp.where(start <= place, start, begin)
    return begin


def pair_kind(key_block, query_block, starts, block_rows):
    key_first = key_block * block_rows
    query_first = query_block * block_rows
    early = begin_of(query_first, starts)
    late = begin_of(query_first + block_rows - 1, starts)
    needed = (key_block <= query_block) & (key_first + block_rows - 1 >= early)
    whole = (key_block < query_block) & (late <= key_first)
    return needed, whole


def mask_bias(key_block, query_block, starts, block_rows, keys_first):
    key_dim = 0 if keys_first else 1
    shape = (block_rows, block_rows)
    key_place = key_block * block_rows + lax.broadcasted_iota(jnp.int32, shape, key_dim)
    query_place = query_block * block_rows + lax.broadcasted_iota(jnp.int32, shape, 1 - key_dim)
    begin = jnp.zeros(shape, jnp.int32)
    for start in starts:
        begin = jnp.where(start <= query_place, start, begin)
    allowed = (key_place <= query_place) & (key_place >= begin)
    return jnp.where(allowed, 0.0, MASKED)


def shared_key_tile(rope_rows, block_rows):
    place = lax.broadcasted_iota(jnp.int32, (ROPE, HEAD), 0)
    lane = lax.broadcasted_iota(jnp.int32, (ROPE, HEAD), 1)
    eye = jnp.where(place == lane, 1.0, 0.0).astype(jnp.bfloat16)
    tile = dot_nn(rope_rows, eye)
    lanes = lax.broadcasted_iota(jnp.int32, (block_rows, HEAD), 1)
    ones = (lanes >= FOLD_AT) & (lanes < FOLD_AT + 3)
    return jnp.where(ones, 1.0, tile).astype(jnp.bfloat16)


def head_window(h):
    at = h * (NOPE + ROPE)
    return at // HEAD * HEAD, at % HEAD


def window_columns(heads):
    return head_window(heads - 1)[0] + WIDE


def head_groups(heads):
    return [(h, min(h + 2, heads)) for h in range(0, heads, 2)]


def forward_kernel(
    blocks, heads, seqs, meta, cq, wqb, lat, wkvb, cos, sin, qx, o_out, ob_out, u_out,
    wkvt, xs, xr, vt, top, total, acc, bias, pre,
):
    rows_all = cq.shape[0]
    block_rows = bias.shape[0]
    q_blocks = rows_all // block_rows
    starts = [meta[blocks + s] for s in range(seqs)]
    own = [meta[blocks + seqs + j] for j in range(q_blocks)]
    for first, last in head_groups(heads):
        wkvt[first * HEAD : last * HEAD, :] = (
            wkvb[:, first * HEAD : last * HEAD].astype(jnp.float32).T.astype(jnp.bfloat16)
        )
    lane = lax.broadcasted_iota(jnp.int32, (block_rows, HEAD), 1)
    for j in range(q_blocks):
        here = pl.ds(j * block_rows, block_rows)
        cos_j, sin_j = cos[here, :], sin[here, :]
        width = heads * (NOPE + ROPE)
        for at in range(0, width, WIDE):
            end = min(at + WIDE, width)
            pre[:, at:end] = dot_nt(cq[here, :], wqb[at:end, :])
        for h in range(heads):
            at, shift = head_window(h)
            own_part = pltpu.roll(pre[:, at : at + WIDE], (WIDE - shift) % WIDE, 1)[:, :HEAD]
            turned = pltpu.roll(own_part, NOPE, 1)
            left = pltpu.roll(turned, HEAD - ROPE // 2, 1)
            right = pltpu.roll(turned, ROPE // 2, 1)
            swapped = jnp.where(lane < ROPE // 2, -left, right)
            rope = jnp.where(lane < ROPE, turned * cos_j + swapped * sin_j, 0.0)
            qx[j, h, :, :HEAD] = jnp.where(lane < NOPE, own_part, 0.0).astype(jnp.bfloat16)
            qx[j, h, :, HEAD:] = rope.astype(jnp.bfloat16)
    top[...] = jnp.full(top.shape, MASKED, jnp.float32)
    total[...] = jnp.zeros(total.shape, jnp.float32)
    acc[...] = jnp.zeros(acc.shape, jnp.float32)

    def pair(j, masked):
        def one(h):
            keys = jnp.concatenate([xs[h], xr[...]], axis=1)
            scores = dot_nt(keys, qx[j, h])
            if masked:
                scores = scores + bias[...]
            old = top[j, h]
            new = jnp.maximum(old, jnp.max(scores, axis=0, keepdims=True))
            fade = jnp.exp2((old - new) * EXP2_SCALE)
            terms = jnp.exp2((scores - new) * EXP2_SCALE)
            top[j, h] = new
            total[j, h] = fade * total[j, h] + jnp.sum(terms, axis=0, keepdims=True)
            acc[j, h] = fade * acc[j, h] + dot_nn(vt[h], terms.astype(jnp.bfloat16))

        for h in range(heads):
            one(h)

    def step(r, carry):
        key_block = meta[r]
        kinds = [pair_kind(key_block, own[j], starts, block_rows) for j in range(q_blocks)]
        wanted = functools.reduce(jnp.logical_or, [k[0] for k in kinds])

        @pl.when(wanted)
        def _():
            here = pl.ds(pl.multiple_of(r * block_rows, block_rows), block_rows)
            latent = lat[here, :KVR]
            xr[...] = shared_key_tile(lat[here, KVR : KVR + ROPE], block_rows)
            for first, last in head_groups(heads):
                keys = dot_nn(latent, wkvb[:, first * HEAD : last * HEAD]).astype(jnp.bfloat16)
                values = dot_nt(wkvt[first * HEAD : last * HEAD, :], latent).astype(jnp.bfloat16)
                for h in range(first, last):
                    at = (h - first) * HEAD
                    xs[h] = keys[:, at : at + HEAD]
                    vt[h] = values[at + NOPE : at + HEAD, :]

        for j in range(q_blocks):
            needed, whole = kinds[j]

            @pl.when(needed & whole)
            def _():
                pair(j, False)

            @pl.when(needed & jnp.logical_not(whole))
            def _():
                bias[...] = mask_bias(key_block, own[j], starts, block_rows, True)
                pair(j, True)

        return carry

    lax.fori_loop(0, blocks, step, 0)
    for j in range(q_blocks):
        here = pl.ds(j * block_rows, block_rows)
        for first, last in head_groups(heads):
            parts = []
            for h in range(first, last):
                parts.append(acc[j, h] * (1.0 / total[j, h]))
                u_out[j, h : h + 1, :] = top[j, h] + jnp.log2(total[j, h]) * (1.0 / EXP2_SCALE)
            if len(parts) == 1:
                parts.append(jnp.zeros_like(parts[0]))
            both = jnp.concatenate(parts, axis=0).T
            width = (last - first) * VDIM
            o_out[here, first * VDIM : first * VDIM + width] = both[:, :width]
            ob_out[here, first * VDIM : first * VDIM + width] = both[:, :width].astype(jnp.bfloat16)


def attention_forward(meta, cq, wqb, lat, wkvb, cos, sin, block_rows, seqs):
    heads = wkvb.shape[1] // HEAD
    blocks = lat.shape[0] // block_rows
    rows = cq.shape[0]
    q_blocks = rows // block_rows
    vmem = pl.BlockSpec(memory_space=pltpu.VMEM)
    pairs = q_blocks * blocks * heads // 2
    return pl.pallas_call(
        functools.partial(forward_kernel, blocks, heads, seqs),
        out_shape=(
            jax.ShapeDtypeStruct((q_blocks, heads, block_rows, WIDE), jnp.bfloat16),
            jax.ShapeDtypeStruct((rows, heads * VDIM), jnp.float32),
            jax.ShapeDtypeStruct((rows, heads * VDIM), jnp.bfloat16),
            jax.ShapeDtypeStruct((q_blocks, 16 * -(-heads // 16), block_rows), jnp.float32),
        ),
        in_specs=[pl.BlockSpec(memory_space=pltpu.SMEM)] + [vmem] * 6,
        out_specs=(vmem,) * 4,
        scratch_shapes=[
            pltpu.VMEM((heads * HEAD, KVR), jnp.bfloat16),
            pltpu.VMEM((heads, block_rows, HEAD), jnp.bfloat16),
            pltpu.VMEM((block_rows, HEAD), jnp.bfloat16),
            pltpu.VMEM((heads, VDIM, block_rows), jnp.bfloat16),
            pltpu.VMEM((q_blocks, heads, 1, block_rows), jnp.float32),
            pltpu.VMEM((q_blocks, heads, 1, block_rows), jnp.float32),
            pltpu.VMEM((q_blocks, heads, VDIM, block_rows), jnp.float32),
            pltpu.VMEM((block_rows, block_rows), jnp.float32),
            pltpu.VMEM((block_rows, window_columns(heads)), jnp.float32),
        ],
        compiler_params=pltpu.CompilerParams(vmem_limit_bytes=VMEM_LIMIT),
        cost_estimate=pl.CostEstimate(
            flops=pairs * 4 * block_rows * block_rows * WIDE,
            bytes_accessed=16 * 1024 * 1024,
            transcendentals=pairs * block_rows * block_rows,
        ),
        name="attention_forward",
    )(meta, cq, wqb, lat, wkvb, cos, sin)


def three_terms(column):
    first = column.astype(jnp.bfloat16).astype(jnp.float32)
    rest = column - first
    second = rest.astype(jnp.bfloat16).astype(jnp.float32)
    return first, second, rest - second


def fold_in(tile, column, lane):
    for k, term in enumerate(three_terms(column)):
        tile = jnp.where(lane == FOLD_AT + k, term, tile)
    return tile


def backward_kernel(
    blocks, heads, seqs, meta, qx, u_in, o_in, dob, lat, wkvb, cos, sin, dq_out, dlat, gkvb,
    xs, xr, qo, qt, dt, dq, dkv, dkpe, gsum, bias, flat,
):
    block_rows = bias.shape[0]
    q_blocks = qx.shape[0]
    starts = [meta[blocks + s] for s in range(seqs)]
    own = [meta[blocks + seqs + j] for j in range(q_blocks)]
    lane = lax.broadcasted_iota(jnp.int32, (block_rows, HEAD), 1)
    for j in range(q_blocks):
        here = pl.ds(j * block_rows, block_rows)
        logs = u_in[j].T
        for first, last in head_groups(heads):
            d_pair = dob[here, first * VDIM : first * VDIM + HEAD].astype(jnp.float32)
            weighted = d_pair * o_in[here, first * VDIM : first * VDIM + HEAD]
            turned = pltpu.roll(d_pair, VDIM, 1)
            for h in range(first, last):
                mine = lane < VDIM if h == first else lane >= VDIM
                delta = jnp.sum(jnp.where(mine, weighted, 0.0), axis=1, keepdims=True)
                d_head = jnp.where(lane >= VDIM, turned if h == first else d_pair, 0.0)
                q_first = qx[j, h, :, :HEAD].astype(jnp.float32)
                q_second = qx[j, h, :, HEAD:].astype(jnp.float32)
                qo[j, h, :block_rows, :HEAD] = qx[j, h, :, :HEAD]
                qo[j, h, :block_rows, HEAD:] = fold_in(q_second, -logs[:, h : h + 1], lane).astype(
                    jnp.bfloat16
                )
                qo[j, h, block_rows:, :HEAD] = d_head.astype(jnp.bfloat16)
                qo[j, h, block_rows:, HEAD:] = fold_in(
                    jnp.zeros((block_rows, HEAD), jnp.float32), -delta, lane
                ).astype(jnp.bfloat16)
                qt[j, h, :NOPE, :] = q_first.T[:NOPE, :].astype(jnp.bfloat16)
                qt[j, h, NOPE:, :] = q_second.T[:ROPE, :].astype(jnp.bfloat16)
                dt[j, h] = d_head.T[VDIM:, :].astype(jnp.bfloat16)
    dq[...] = jnp.zeros(dq.shape, jnp.float32)
    gsum[...] = jnp.zeros(gsum.shape, jnp.float32)

    def pair(j, masked):
        def one(h):
            keys = jnp.concatenate([xs[h], xr[...]], axis=1)
            both = dot_nt(qo[j, h], keys)
            scores = both[:block_rows] * EXP2_SCALE
            if masked:
                scores = scores + bias[...]
            probs = jnp.exp2(scores)
            d_scores = (probs * both[block_rows:]).astype(jnp.bfloat16)
            dq[j, h] += dot_nn(d_scores, keys)
            d_keys = dot_nn(qt[j, h], d_scores)
            dkv[h, :NOPE, :] += d_keys[:NOPE]
            dkpe[...] += d_keys[NOPE:]
            dkv[h, NOPE:, :] += dot_nn(dt[j, h], probs.astype(jnp.bfloat16))

        for h in range(heads):
            one(h)

    def step(r, carry):
        key_block = meta[r]
        kinds = [pair_kind(key_block, own[j], starts, block_rows) for j in range(q_blocks)]
        wanted = functools.reduce(jnp.logical_or, [k[0] for k in kinds])
        here = pl.ds(pl.multiple_of(r * block_rows, block_rows), block_rows)

        @pl.when(wanted)
        def _():
            latent = lat[here, :KVR]
            xr[...] = shared_key_tile(lat[here, KVR : KVR + ROPE], block_rows)
            for first, last in head_groups(heads):
                keys = dot_nn(latent, wkvb[:, first * HEAD : last * HEAD]).astype(jnp.bfloat16)
                for h in range(first, last):
                    xs[h] = keys[:, (h - first) * HEAD : (h - first + 1) * HEAD]
            dkv[...] = jnp.zeros(dkv.shape, jnp.float32)
            dkpe[...] = jnp.zeros(dkpe.shape, jnp.float32)

        for j in range(q_blocks):
            needed, whole = kinds[j]

            @pl.when(needed & whole)
            def _():
                pair(j, False)

            @pl.when(needed & jnp.logical_not(whole))
            def _():
                bias[...] = mask_bias(key_block, own[j], starts, block_rows, False)
                pair(j, True)

        @pl.when(wanted)
        def _():
            latent = lat[here, :KVR]
            d_latent = jnp.zeros((KVR, block_rows), jnp.float32)
            for h in range(heads):
                d_head = jnp.concatenate(
                    [dkv[h, :NOPE, :] * SCORE_SCALE, dkv[h, NOPE:, :]], axis=0
                ).astype(jnp.bfloat16)
                d_latent += dot_nn(wkvb[:, h * HEAD : (h + 1) * HEAD], d_head)
                gsum[h * HEAD : (h + 1) * HEAD, :] += dot_nn(d_head, latent)
            dlat[here, :KVR] = d_latent.T.astype(jnp.bfloat16)
            rope = jnp.concatenate(
                [dkpe[...] * SCORE_SCALE, jnp.zeros((HEAD - ROPE, block_rows), jnp.float32)], axis=0
            )
            dlat[here, KVR:] = rope.T[:, :ROPE].astype(jnp.bfloat16)

        @pl.when(jnp.logical_not(wanted))
        def _():
            dlat[here, :] = jnp.zeros((block_rows, KVR + ROPE), jnp.bfloat16)

        return carry

    lax.fori_loop(0, blocks, step, 0)
    for h in range(heads):
        gkvb[:, h * HEAD : (h + 1) * HEAD] = gsum[h * HEAD : (h + 1) * HEAD, :].T.astype(
            jnp.bfloat16
        )
    for j in range(q_blocks):
        here = pl.ds(j * block_rows, block_rows)
        cos_j, sin_j = cos[here, :], sin[here, :]
        flat[...] = jnp.zeros(flat.shape, jnp.float32)
        for h in range(heads):
            nope = jnp.where(lane < NOPE, dq[j, h, :, :HEAD], 0.0)
            rope = dq[j, h, :, HEAD:]
            shifted = rope * sin_j
            left = pltpu.roll(shifted, HEAD - ROPE // 2, 1)
            right = pltpu.roll(shifted, ROPE // 2, 1)
            swapped = jnp.where(lane < ROPE // 2, left, jnp.where(lane < ROPE, -right, 0.0))
            back = pltpu.roll(jnp.where(lane < ROPE, rope * cos_j + swapped, 0.0), NOPE, 1)
            whole = jnp.concatenate([(nope + back) * SCORE_SCALE, jnp.zeros_like(nope)], axis=1)
            at, shift = head_window(h)
            flat[:, at : at + WIDE] += pltpu.roll(whole, shift, 1)
        dq_out[here, :] = flat[:, : heads * (NOPE + ROPE)].astype(jnp.bfloat16)


def attention_backward(meta, qx, u_in, o_in, dob, lat, wkvb, cos, sin, block_rows, seqs):
    heads = wkvb.shape[1] // HEAD
    blocks = lat.shape[0] // block_rows
    q_blocks = qx.shape[0]
    rows = q_blocks * block_rows
    odd = -(heads * VDIM) % HEAD
    if odd:
        o_in = jnp.pad(o_in, ((0, 0), (0, odd)))
        dob = jnp.pad(dob, ((0, 0), (0, odd)))
    vmem = pl.BlockSpec(memory_space=pltpu.VMEM)
    pairs = q_blocks * blocks * heads // 2
    return pl.pallas_call(
        functools.partial(backward_kernel, blocks, heads, seqs),
        out_shape=(
            jax.ShapeDtypeStruct((rows, heads * (NOPE + ROPE)), jnp.bfloat16),
            jax.ShapeDtypeStruct((lat.shape[0], KVR + ROPE), jnp.bfloat16),
            jax.ShapeDtypeStruct((KVR, heads * HEAD), jnp.bfloat16),
        ),
        in_specs=[pl.BlockSpec(memory_space=pltpu.SMEM)] + [vmem] * 8,
        out_specs=(vmem,) * 3,
        scratch_shapes=[
            pltpu.VMEM((heads, block_rows, HEAD), jnp.bfloat16),
            pltpu.VMEM((block_rows, HEAD), jnp.bfloat16),
            pltpu.VMEM((q_blocks, heads, 2 * block_rows, WIDE), jnp.bfloat16),
            pltpu.VMEM((q_blocks, heads, NOPE + ROPE, block_rows), jnp.bfloat16),
            pltpu.VMEM((q_blocks, heads, VDIM, block_rows), jnp.bfloat16),
            pltpu.VMEM((q_blocks, heads, block_rows, WIDE), jnp.float32),
            pltpu.VMEM((heads, HEAD, block_rows), jnp.float32),
            pltpu.VMEM((ROPE, block_rows), jnp.float32),
            pltpu.VMEM((heads * HEAD, KVR), jnp.float32),
            pltpu.VMEM((block_rows, block_rows), jnp.float32),
            pltpu.VMEM((block_rows, window_columns(heads)), jnp.float32),
        ],
        compiler_params=pltpu.CompilerParams(vmem_limit_bytes=VMEM_LIMIT),
        cost_estimate=pl.CostEstimate(
            flops=pairs * 8 * block_rows * block_rows * WIDE,
            bytes_accessed=24 * 1024 * 1024,
            transcendentals=pairs * block_rows * block_rows,
        ),
        name="attention_backward",
    )(meta, qx, u_in, o_in, dob, lat, wkvb, cos, sin)


MESH = pl.DeviceIdType.MESH


class Scatter:
    def __init__(self, n, given=None, left=None, right=None):
        self.operands = [given] if given is not None else [left, right]
        self.is_given = given is not None
        self.rows = self.operands[0].shape[0 if self.is_given else 1] // n
        self.columns = self.operands[-1].shape[1]
        self.depth = 0 if self.is_given else right.shape[0]
        self.parts = 2 if self.rows % 32 == 0 else 1


def scatter_blocks(bits_left):
    chips = []
    for value in range(1 << len(bits_left)):
        chip = 0
        for at, bit in enumerate(bits_left):
            chip = chip + (((value >> at) & 1) << (bit - 1))
        chips.append(chip)
    return chips


def scatter_operands(items):
    given = [item.operands[0] for item in items if item.is_given]
    lefts = []
    for item in items:
        if not item.is_given and not any(item.operands[0] is left for left in lefts):
            lefts.append(item.operands[0])
    return given, lefts, [item.operands[1] for item in items if not item.is_given]


def scatter_kernel(n, items, *refs):
    count = n.bit_length() - 1
    me = lax.axis_index("ctx")
    refs = list(refs)
    take = lambda k: [refs.pop(0) for _ in range(k)]
    given, lefts, rights = scatter_operands(items)
    inputs = dict(zip(map(id, given + lefts + rights), take(len(given + lefts + rights))))
    outputs = take(len(items))
    held, sent, landed, core_sems, step_sems = [], [], [], [], []
    for item in items:
        held.append(refs.pop(0))
        sent.append(None if item.is_given else refs.pop(0))
        landed.append(take(count - 1))
        core_sems.append(take(2))
        step_sems.append([take(2) for _ in range(count - 1)])
    turned = dict(zip(map(id, lefts), take(len(lefts))))
    barrier = pltpu.get_barrier_semaphore()
    for bit in range(count):
        pl.semaphore_signal(barrier, inc=1, device_id={"ctx": me ^ (1 << bit)}, device_id_type=MESH)
    pl.semaphore_wait(barrier, count)
    core = me & 1
    chips = n // 2
    orders = (tuple(range(1, count)), tuple(range(count - 1, 0, -1)))

    def columns_of(item):
        return [(c, min(c + 512, item.columns)) for c in range(0, item.columns, 512)]

    def product(k, dest, first, last):
        item = items[k]
        left, right = turned[id(item.operands[0])], inputs[id(item.operands[1])]
        at = pl.ds(pl.multiple_of(dest * item.rows, 16), item.rows)
        return dot_nn(left[at, :], right[:, first:last])

    def core_copy(k, chip):
        item = items[k]
        if item.is_given:
            at = pl.ds(pl.multiple_of((2 * chip + 1 - core) * item.rows, 16), item.rows)
            source = inputs[id(item.operands[0])].at[at, :]
        else:
            source = sent[k].at[chip]
        return pltpu.make_async_remote_copy(
            src_ref=source,
            dst_ref=held[k].at[chip],
            send_sem=core_sems[k][0].at[chip],
            recv_sem=core_sems[k][1].at[chip],
            device_id={"ctx": me ^ 1},
            device_id_type=MESH,
        )

    def step_copies(k, step):
        item = items[k]
        half = item.rows // item.parts
        copies = []
        for part, order in enumerate(orders[: item.parts]):
            bit = order[step]
            left = sorted(order[step + 1 :])
            fixed = [b for b in order[:step]]
            at = pl.ds(part * half, half)
            for slot, free in enumerate(scatter_blocks(left)):
                keep = free + ((me >> bit) & 1) * (1 << (bit - 1))
                send = free + (1 - ((me >> bit) & 1)) * (1 << (bit - 1))
                for b in fixed:
                    own = ((me >> b) & 1) * (1 << (b - 1))
                    keep, send = keep + own, send + own
                copies.append(
                    (
                        pltpu.make_async_remote_copy(
                            src_ref=held[k].at[send, at, :],
                            dst_ref=landed[k][step].at[slot, at, :],
                            send_sem=step_sems[k][step][0].at[part, slot],
                            recv_sem=step_sems[k][step][1].at[part, slot],
                            device_id={"ctx": me ^ (1 << bit)},
                            device_id_type=MESH,
                        ),
                        keep,
                        slot,
                        at,
                    )
                )
        return copies

    def start_core(k):
        item = items[k]

        def body(chip, carry):
            if not item.is_given:
                for first, last in columns_of(item):
                    sent[k][chip, :, first:last] = product(
                        k, 2 * chip + 1 - core, first, last
                    ).astype(jnp.bfloat16)
            core_copy(k, chip).start()
            return carry

        lax.fori_loop(0, chips, body, 0)

    def finish_core(k):
        item = items[k]

        def body(chip, carry):
            core_copy(k, chip).wait_recv()
            at = pl.ds(pl.multiple_of((2 * chip + core) * item.rows, 16), item.rows)
            for first, last in columns_of(item):
                if item.is_given:
                    own = inputs[id(item.operands[0])][at, first:last].astype(jnp.float32)
                else:
                    own = product(k, 2 * chip + core, first, last)
                total = own + held[k][chip, :, first:last].astype(jnp.float32)
                held[k][chip, :, first:last] = total.astype(jnp.bfloat16)
            return carry

        lax.fori_loop(0, chips, body, 0)

    def start_step(k, step):
        for copy, _, _, _ in step_copies(k, step):
            copy.start()

    def finish_step(k, step):
        item = items[k]
        for copy, keep, slot, at in step_copies(k, step):
            copy.wait_recv()
            for first, last in columns_of(item):
                total = held[k][keep, at, first:last].astype(jnp.float32) + landed[k][step][
                    slot, at, first:last
                ].astype(jnp.float32)
                if step == count - 2:
                    outputs[k][at, first:last] = total
                else:
                    held[k][keep, at, first:last] = total.astype(jnp.bfloat16)

    def turn(k):
        key = None if items[k].is_given else id(items[k].operands[0])
        if key in turned and key not in done:
            done.add(key)
            source, target = inputs[key], turned[key]

            def body(c, carry):
                at = pl.ds(pl.multiple_of(c * 128, 128), 128)
                target[at, :] = source[:, at].astype(jnp.float32).T.astype(jnp.bfloat16)
                return carry

            lax.fori_loop(0, source.shape[1] // 128, body, 0)

    done = set()
    every = range(len(items))
    turn(0)
    start_core(0)
    for k in every:
        if k + 1 < len(items):
            turn(k + 1)
            start_core(k + 1)
        finish_core(k)
        start_step(k, 0)
    for step in range(count - 1):
        for k in every:
            finish_step(k, step)
            if step + 1 < count - 1:
                start_step(k, step + 1)
    for k in every:

        def drain(chip, carry, k=k):
            core_copy(k, chip).wait_send()
            return carry

        lax.fori_loop(0, chips, drain, 0)
        for step in range(count - 1):
            for copy, _, _, _ in step_copies(k, step):
                copy.wait_send()


def scatter_over_ctx(n, items, collective_id):
    vmem = pl.BlockSpec(memory_space=pltpu.VMEM)
    count = n.bit_length() - 1
    scratch = []
    flops = 0
    for item in items:
        scratch.append(pltpu.VMEM((n // 2, item.rows, item.columns), jnp.bfloat16))
        if not item.is_given:
            scratch.append(pltpu.VMEM((n // 2, item.rows, item.columns), jnp.bfloat16))
        scratch += [
            pltpu.VMEM((n >> (step + 2), item.rows, item.columns), jnp.bfloat16)
            for step in range(count - 1)
        ]
        scratch += [pltpu.SemaphoreType.DMA((n // 2,))] * 2
        for step in range(count - 1):
            scratch += [pltpu.SemaphoreType.DMA((2, n >> (step + 2)))] * 2
        flops += 2 * n * item.rows * item.columns * item.depth
    given, lefts, rights = scatter_operands(items)
    operands = given + lefts + rights
    scratch += [pltpu.VMEM(left.shape[::-1], jnp.bfloat16) for left in lefts]
    return pl.pallas_call(
        functools.partial(scatter_kernel, n, items),
        out_shape=tuple(
            jax.ShapeDtypeStruct((item.rows, item.columns), jnp.float32) for item in items
        ),
        in_specs=[vmem] * len(operands),
        out_specs=(vmem,) * len(items),
        scratch_shapes=scratch,
        compiler_params=pltpu.CompilerParams(
            vmem_limit_bytes=MIDDLE_VMEM, collective_id=collective_id, has_side_effects=True
        ),
        cost_estimate=pl.CostEstimate(
            flops=flops, bytes_accessed=64 * 1024 * 1024, transcendentals=0
        ),
        name=f"scatter_over_ctx_{collective_id}",
    )(*operands)


CHUNK = 32
BLOCK = 4 * CHUNK
MIDDLE_VMEM = 62 * 1024 * 1024


def middle_kernel(
    n, ob, tokens, cot, gain, w_out, w_gate, w_up, w_down,
    tt, d_out, f_out, act_out, dg_out, du_out, h_out, df_out,
    own, up, wo, wg, wu, wd, d_acc, f_acc,
    w_sems, up_send, up_land, down_send, back_send, down_land,
):
    me = lax.axis_index("tp")
    root = (n - 1) // 2
    width = tokens.shape[1]
    hidden = wg.shape[0]
    chunks = own.shape[0]
    blocks = chunks // 4
    root_lag = n - 1 - root
    land_lag = 2 * root_lag
    block_lag = -(-(4 + land_lag) // 4)
    tiles = [(c, min(c + 512, width)) for c in range(0, width, 512)]
    quarter = hidden // 4 // 128 * 128
    cuts = [0, quarter, 2 * quarter, 3 * quarter, hidden]
    loads = [
        pltpu.make_async_copy(w_out, wo, w_sems.at[0]),
        pltpu.make_async_copy(w_gate, wg, w_sems.at[1]),
        pltpu.make_async_copy(w_up, wu, w_sems.at[2]),
        pltpu.make_async_copy(w_down, wd, w_sems.at[3]),
    ]
    for load in loads:
        load.start()
    barrier = pltpu.get_barrier_semaphore()
    has_left, has_right = me > 0, me < n - 1
    for there, other in ((has_left, me - 1), (has_right, me + 1)):

        @pl.when(there)
        def _(other=other):
            pl.semaphore_signal(barrier, inc=1, device_id={"tp": other}, device_id_type=MESH)

    @pl.when(has_left & has_right)
    def _():
        pl.semaphore_wait(barrier, 2)

    @pl.when(jnp.logical_not(has_left & has_right))
    def _():
        pl.semaphore_wait(barrier, 1)

    def copy_to(source, target, send, land, c, other):
        return pltpu.make_async_remote_copy(
            src_ref=source.at[c],
            dst_ref=target.at[c],
            send_sem=send.at[c],
            recv_sem=land.at[c],
            device_id={"tp": other},
            device_id_type=MESH,
        )

    def rise_left(c):
        return copy_to(own, up, up_send, up_land, c, me + 1)

    def rise_right(c):
        return copy_to(own, up, up_send, up_land, c, me - 1)

    def rise_last(c):
        return copy_to(own, tt, up_send, down_land, c, me - 1)

    def fall_right(c):
        return copy_to(tt, tt, down_send, down_land, c, me + 1)

    def fall_left(c):
        return copy_to(tt, tt, back_send, down_land, c, me - 1)

    rises = [(me < root, rise_left)] if root else []
    rises.append((me == root + 1, rise_last))
    if n - 1 > root + 1:
        rises.append((me > root + 1, rise_right))

    def rise(c):
        for who, copy in rises:

            @pl.when(who)
            def _(copy=copy):
                copy(c).start()

    def inside(c):
        return (c >= 0) & (c < chunks)

    def added(refs, c):
        total = refs[0][c].astype(jnp.float32)
        for ref in refs[1:]:
            total = total + ref[c].astype(jnp.float32)
        return total.astype(jnp.bfloat16)

    def duties(t):
        leaf = (me == 0) | (me == n - 1) if root else me == n - 1
        @pl.when(leaf & (t < chunks))
        def _():
            rise(t)

        if n > 3:
            c = t - jnp.where(me < root, me, n - 1 - me)

            @pl.when((me != root) & has_left & has_right & inside(c))
            def _():
                rise_right(c).wait_recv()
                own[c] = added([own, up], c)
                rise(c)

        c_root = t - root_lag

        @pl.when((me == root) & inside(c_root))
        def _():
            if root:
                rise_left(c_root).wait_recv()
            fall_right(c_root).wait_recv()
            tt[c_root] = added([own, up, tt] if root else [own, tt], c_root)
            fall_right(c_root).start()
            if root:
                fall_left(c_root).start()

        c_fall = t - root_lag - jnp.where(me < root, root - me, me - root)

        @pl.when((me != root) & inside(c_fall))
        def _():
            fall_right(c_fall).wait_recv()

            @pl.when((me > root) & has_right)
            def _():
                fall_right(c_fall).start()

            @pl.when((me < root) & has_left)
            def _():
                fall_left(c_fall).start()

        c_norm = t - land_lag

        @pl.when(inside(c_norm))
        def _():
            rows = pl.ds(pl.multiple_of(c_norm * CHUNK, CHUNK), CHUNK)
            middle = tokens[rows, :].astype(jnp.float32) + RESIDUAL_SCALE * tt[c_norm].astype(
                jnp.float32
            )
            scale = lax.rsqrt(jnp.mean(middle * middle, axis=-1, keepdims=True) + EPSILON)
            h_out[rows, :] = (middle * scale * gain[...]).astype(jnp.bfloat16)

    def project(b):
        rows = pl.ds(pl.multiple_of(b * BLOCK, BLOCK), BLOCK)
        for first, last in tiles:
            part = dot_nt(ob[rows, :], wo[first:last, :]).astype(jnp.bfloat16)
            for k in range(4):
                own[4 * b + k, :, first:last] = part[k * CHUNK : (k + 1) * CHUNK, :]

    def feed(b, i):
        rows = pl.ds(pl.multiple_of(b * BLOCK, BLOCK), BLOCK)
        first, last = cuts[i], cuts[i + 1]
        if i == 0:
            df_out[rows, :] = (RESIDUAL_SCALE * cot[rows, :].astype(jnp.float32)).astype(jnp.bfloat16)
        gate = dot_nt(h_out[rows, :], wg[first:last, :])
        upper = dot_nt(h_out[rows, :], wu[first:last, :])
        d_act = dot_nt(df_out[rows, :], wd[first:last, :])
        sig = jax.nn.sigmoid(gate)
        silu = gate * sig
        act = (silu * upper).astype(jnp.bfloat16)
        dg = (d_act * upper * sig * (1.0 + gate * (1.0 - sig))).astype(jnp.bfloat16)
        du = (d_act * silu).astype(jnp.bfloat16)
        act_out[rows, first:last] = act
        dg_out[rows, first:last] = dg
        du_out[rows, first:last] = du
        for lo, hi in tiles:
            d_part = dot_nn(dg, wg[first:last, lo:hi]) + dot_nn(du, wu[first:last, lo:hi])
            f_part = dot_nn(act, wd[first:last, lo:hi])
            if i:
                d_part = d_part + d_acc[:, lo:hi]
                f_part = f_part + f_acc[:, lo:hi]
            if i < 3:
                d_acc[:, lo:hi] = d_part
                f_acc[:, lo:hi] = f_part
            else:
                d_out[rows, lo:hi] = d_part.astype(jnp.bfloat16)
                f_out[rows, lo:hi] = f_part.astype(jnp.bfloat16)

    loads[0].wait()

    def outer(o, carry):
        @pl.when(o < blocks)
        def _():
            project(o)

        @pl.when(o == block_lag)
        def _():
            for load in loads[1:]:
                load.wait()

        for i in range(4):
            duties(4 * o + i)

            @pl.when(o >= block_lag)
            def _(i=i):
                feed(o - block_lag, i)

        return carry

    lax.fori_loop(0, blocks + block_lag, outer, 0)

    def drain(c, carry):
        @pl.when(me != root)
        def _():
            rise_right(c).wait_send()

        @pl.when((me >= root) & has_right)
        def _():
            fall_right(c).wait_send()

        @pl.when((me <= root) & has_left)
        def _():
            fall_left(c).wait_send()

        return carry

    lax.fori_loop(0, chunks, drain, 0)


def middle_layer(n, ob, tokens, cot, gain, w_out, w_gate, w_up, w_down, collective_id):
    rows, width = tokens.shape
    hidden = w_gate.shape[0]
    chunks = rows // CHUNK
    vmem = pl.BlockSpec(memory_space=pltpu.VMEM)
    anywhere = pl.BlockSpec(memory_space=pl.ANY)
    half = jnp.bfloat16
    dma = pltpu.SemaphoreType.DMA
    attn, *rest = pl.pallas_call(
        functools.partial(middle_kernel, n),
        out_shape=(
            jax.ShapeDtypeStruct((chunks, CHUNK, width), half),
            jax.ShapeDtypeStruct((rows, width), half),
            jax.ShapeDtypeStruct((rows, width), half),
            jax.ShapeDtypeStruct((rows, hidden), half),
            jax.ShapeDtypeStruct((rows, hidden), half),
            jax.ShapeDtypeStruct((rows, hidden), half),
            jax.ShapeDtypeStruct((rows, width), half),
            jax.ShapeDtypeStruct((rows, width), half),
        ),
        in_specs=[vmem] * 4 + [anywhere] * 4,
        out_specs=(vmem,) * 8,
        scratch_shapes=[
            pltpu.VMEM((chunks, CHUNK, width), half),
            pltpu.VMEM((chunks, CHUNK, width), half),
            pltpu.VMEM(w_out.shape, half),
            pltpu.VMEM(w_gate.shape, half),
            pltpu.VMEM(w_up.shape, half),
            pltpu.VMEM(w_down.shape, half),
            pltpu.VMEM((BLOCK, width), jnp.float32),
            pltpu.VMEM((BLOCK, width), jnp.float32),
            dma((4,)),
            dma((chunks,)),
            dma((chunks,)),
            dma((chunks,)),
            dma((chunks,)),
            dma((chunks,)),
        ],
        compiler_params=pltpu.CompilerParams(
            vmem_limit_bytes=MIDDLE_VMEM, collective_id=collective_id, has_side_effects=True
        ),
        cost_estimate=pl.CostEstimate(
            flops=2 * rows * width * (6 * hidden + ob.shape[1]),
            bytes_accessed=64 * 1024 * 1024,
            transcendentals=rows * hidden,
        ),
        name=f"middle_layer_{collective_id}",
    )(ob, tokens, cot, gain.reshape(1, -1), w_out, w_gate, w_up, w_down)
    return attn.reshape(rows, width), *rest


def norm_scale(values):
    return lax.rsqrt(jnp.mean(values * values, axis=-1, keepdims=True) + EPSILON)


def norm_back(incoming, values, inv_rms, gain_vec):
    weighted = incoming * gain_vec
    mean = jnp.mean(weighted * values, axis=-1, keepdims=True)
    d_values = inv_rms * weighted - values * (inv_rms * inv_rms * inv_rms) * mean
    return d_values, jnp.sum(incoming * values * inv_rms, axis=0, keepdims=True)


def rope_tile(tile, cos, sin, lane):
    left = pltpu.roll(tile, HEAD - ROPE // 2, 1)
    right = pltpu.roll(tile, ROPE // 2, 1)
    swapped = jnp.where(lane < ROPE // 2, -left, right)
    return jnp.where(lane < ROPE, tile * cos + swapped * sin, 0.0)


def rope_tile_back(tile, cos, sin, lane):
    shifted = tile * sin
    left = pltpu.roll(shifted, HEAD - ROPE // 2, 1)
    right = pltpu.roll(shifted, ROPE // 2, 1)
    swapped = jnp.where(lane < ROPE // 2, left, -right)
    return jnp.where(lane < ROPE, tile * cos + swapped, 0.0)


def second_norm_kernel(
    d_sum, attn, tokens, cot, gain, w_out, d_middle, d_attn, d_heads, d_gain
):
    middle = tokens[...].astype(jnp.float32) + RESIDUAL_SCALE * attn[...].astype(jnp.float32)
    d_norm, gain_terms = norm_back(
        d_sum[...].astype(jnp.float32), middle, norm_scale(middle), gain[...]
    )
    total = cot[...].astype(jnp.float32) + d_norm
    d_middle[...] = total
    scaled = (RESIDUAL_SCALE * total).astype(jnp.bfloat16)
    d_attn[...] = scaled
    d_heads[...] = dot_nn(scaled, w_out[...]).astype(jnp.bfloat16)

    @pl.when(pl.program_id(0) == 0)
    def _():
        d_gain[...] = jnp.zeros(d_gain.shape, jnp.float32)

    d_gain[...] += gain_terms


def second_norm_back(d_sum, attn, tokens, cot, gain, w_out):
    rows, width = tokens.shape
    block = rows // 4
    head_width = w_out.shape[1]
    whole = lambda shape: pl.BlockSpec(shape, lambda i: (0, 0))
    tile = lambda columns: pl.BlockSpec((block, columns), lambda i: (i, 0))
    return pl.pallas_call(
        second_norm_kernel,
        grid=(rows // block,),
        out_shape=(
            jax.ShapeDtypeStruct((rows, width), jnp.float32),
            jax.ShapeDtypeStruct((rows, width), jnp.bfloat16),
            jax.ShapeDtypeStruct((rows, head_width), jnp.bfloat16),
            jax.ShapeDtypeStruct((1, width), jnp.float32),
        ),
        in_specs=[tile(width)] * 4 + [whole((1, width)), whole((width, head_width))],
        out_specs=(tile(width), tile(width), tile(head_width), whole((1, width))),
        compiler_params=pltpu.CompilerParams(vmem_limit_bytes=VMEM_LIMIT),
        cost_estimate=pl.CostEstimate(
            flops=2 * rows * width * head_width,
            bytes_accessed=24 * 1024 * 1024,
            transcendentals=rows,
        ),
        name="second_norm_back",
    )(d_sum, attn, tokens, cot, gain.reshape(1, -1), w_out)


def first_norm_kernel(
    d_tp, q_pre, lat_raw, tokens, d_middle, gain_in, gain_q, gain_kv, w_qa, w_kva, cos, sin,
    normed, d_q, d_kv, grad_in, g_in, g_q, g_kv,
):
    rank = q_pre.shape[1]
    block = tokens.shape[0]
    lane = lax.broadcasted_iota(jnp.int32, (block, HEAD), 1)

    @pl.when(pl.program_id(0) == 0)
    def _():
        for ref in (g_in, g_q, g_kv):
            ref[...] = jnp.zeros(ref.shape, jnp.float32)

    pre = q_pre[...]
    d_pre, terms = norm_back(d_tp[:, :rank].astype(jnp.float32), pre, norm_scale(pre), gain_q[...])
    g_q[...] += terms
    d_low = d_pre.astype(jnp.bfloat16)
    d_q[...] = d_low
    raw = lat_raw[...]
    d_raw, terms = norm_back(
        d_tp[:, rank : rank + KVR].astype(jnp.float32), raw, norm_scale(raw), gain_kv[...]
    )
    g_kv[...] += terms
    rope = rope_tile_back(
        d_tp[:, rank + KVR : rank + KVR + HEAD].astype(jnp.float32), cos[...], sin[...], lane
    )
    d_raw = d_raw.astype(jnp.bfloat16)
    d_rope = rope[:, :ROPE].astype(jnp.bfloat16)
    d_kv[:, :KVR] = d_raw
    d_kv[:, KVR:] = d_rope
    d_normed = dot_nt(d_low, w_qa[...])
    d_normed = d_normed + dot_nn(d_raw, w_kva[:KVR, :]) + dot_nn(d_rope, w_kva[KVR:, :])
    values = tokens[...].astype(jnp.float32)
    scale = norm_scale(values)
    normed[...] = (values * scale * gain_in[...]).astype(jnp.bfloat16)
    d_values, terms = norm_back(d_normed, values, scale, gain_in[...])
    g_in[...] += terms
    grad_in[...] = d_middle[...] + d_values


def first_norm_back(
    d_tp, q_pre, lat_raw, tokens, d_middle, gain_in, gain_q, gain_kv, w_qa, w_kva, cos, sin
):
    rows, width = tokens.shape
    block = rows // 4
    rank = q_pre.shape[1]
    whole = lambda array: pl.BlockSpec(array.shape, lambda i: (0, 0))
    tile = lambda columns: pl.BlockSpec((block, columns), lambda i: (i, 0))
    gains = [g.reshape(1, -1) for g in (gain_in, gain_q, gain_kv)]
    wide = jax.ShapeDtypeStruct
    return pl.pallas_call(
        first_norm_kernel,
        grid=(rows // block,),
        out_shape=(
            wide((rows, width), jnp.bfloat16),
            wide((rows, rank), jnp.bfloat16),
            wide((rows, KVR + ROPE), jnp.bfloat16),
            wide((rows, width), jnp.float32),
            wide((1, width), jnp.float32),
            wide((1, rank), jnp.float32),
            wide((1, KVR), jnp.float32),
        ),
        in_specs=[tile(d_tp.shape[1]), tile(rank), tile(KVR), tile(width), tile(width)]
        + [whole(g) for g in gains]
        + [whole(w_qa), whole(w_kva), tile(HEAD), tile(HEAD)],
        out_specs=(
            tile(width),
            tile(rank),
            tile(KVR + ROPE),
            tile(width),
            *[whole(g) for g in gains],
        ),
        compiler_params=pltpu.CompilerParams(vmem_limit_bytes=VMEM_LIMIT),
        cost_estimate=pl.CostEstimate(
            flops=2 * rows * width * (rank + KVR + ROPE),
            bytes_accessed=32 * 1024 * 1024,
            transcendentals=rows,
        ),
        name="first_norm_back",
    )(d_tp, q_pre, lat_raw, tokens, d_middle, *gains, w_qa, w_kva, cos, sin)


def head_kernel(
    n, tokens, gain_in, gain_q, gain_kv, w_qa, w_kva, cos, sin, out, q_latent, q_pre, lat_raw,
    own, normed, w_rope, local_sem, step_sends, step_lands, core_sends, core_lands,
):
    count = n.bit_length() - 1
    me = lax.axis_index("ctx")
    rows = own.shape[0]
    half = rows // 2
    block = rows // 4
    barrier = pltpu.get_barrier_semaphore()
    for bit in range(count):
        pl.semaphore_signal(barrier, inc=1, device_id={"ctx": me ^ (1 << bit)}, device_id_type=MESH)
    orders = (tuple(range(1, count)), tuple(range(count - 1, 0, -1)))
    lane = lax.broadcasted_iota(jnp.int32, (block, HEAD), 1)
    w_rope[...] = jnp.zeros(w_rope.shape, jnp.bfloat16)
    w_rope[:ROPE, :] = w_kva[KVR : KVR + ROPE, :]

    def latents(k, carry):
        at = pl.ds(pl.multiple_of(k * block, block), block)
        values = tokens[at, :].astype(jnp.float32)
        normed[at, :] = (values * norm_scale(values) * gain_in[...]).astype(jnp.bfloat16)
        raw = dot_nt(normed[at, :], w_kva[:KVR, :])
        lat_raw[at, :] = raw
        own[at, :KVR] = (raw * norm_scale(raw) * gain_kv[...]).astype(jnp.bfloat16)
        rope = rope_tile(dot_nt(normed[at, :], w_rope[...]), cos[at, :], sin[at, :], lane)
        own[at, KVR:] = rope[:, :ROPE].astype(jnp.bfloat16)
        return carry

    lax.fori_loop(0, 4, latents, 0)
    pl.semaphore_wait(barrier, count)
    local = pltpu.make_async_copy(own, out.at[me], local_sem)
    local.start()

    def chip_copy(part, step, slot, block, first):
        at = pl.ds(part * half, half)
        return pltpu.make_async_remote_copy(
            src_ref=own.at[at, :] if first else out.at[block, at, :],
            dst_ref=out.at[block, at, :],
            send_sem=step_sends.at[part, step, slot],
            recv_sem=step_lands.at[part, step, slot],
            device_id={"ctx": me ^ (1 << orders[part][step])},
            device_id_type=MESH,
        )

    def core_copy(block, slot, first):
        return pltpu.make_async_remote_copy(
            src_ref=own if first else out.at[block],
            dst_ref=out.at[block],
            send_sem=core_sends.at[slot],
            recv_sem=core_lands.at[slot],
            device_id={"ctx": me ^ 1},
            device_id_type=MESH,
        )

    def query(k, carry):
        at = pl.ds(pl.multiple_of(k * block, block), block)
        pre = dot_nn(normed[at, :], w_qa[...])
        q_pre[at, :] = pre
        q_latent[at, :] = (pre * norm_scale(pre) * gain_q[...]).astype(jnp.bfloat16)
        return carry

    started = []
    for step in range(count - 1):
        for part, order in enumerate(orders):
            for slot in range(1 << step):
                flips = 0
                for at in range(step):
                    flips |= ((slot >> at) & 1) << order[at]
                copy = chip_copy(part, step, slot, me ^ flips, slot == 0)
                copy.start()
                started.append(copy)
        if step == 0:
            core_copy(me, 0, True).start()
        lax.fori_loop(2 * step, min(2 * step + 2, 4) if step < count - 2 else 4, query, 0)
        for part, order in enumerate(orders):
            for slot in range(1 << step):
                chip_copy(part, step, slot, me, slot == 0).wait_recv()
    for chip in range(1, n // 2):
        core_copy(me ^ (2 * chip), chip, False).start()
    for chip in range(n // 2):
        core_copy(me, chip, chip == 0).wait_recv()
    for copy in started:
        copy.wait_send()
    for chip in range(n // 2):
        core_copy(me, chip, chip == 0).wait_send()
    local.wait()


def head_layer(n, tokens, gain_in, gain_q, gain_kv, w_qa, w_kva, cos, sin, collective_id):
    rows, width = tokens.shape
    rank = w_qa.shape[1]
    count = n.bit_length() - 1
    vmem = pl.BlockSpec(memory_space=pltpu.VMEM)
    slots = max(n // 4, 1)
    dma = pltpu.SemaphoreType.DMA
    gathered, q_latent, q_pre, lat_raw = pl.pallas_call(
        functools.partial(head_kernel, n),
        out_shape=(
            jax.ShapeDtypeStruct((n, rows, KVR + ROPE), jnp.bfloat16),
            jax.ShapeDtypeStruct((rows, rank), jnp.bfloat16),
            jax.ShapeDtypeStruct((rows, rank), jnp.float32),
            jax.ShapeDtypeStruct((rows, KVR), jnp.float32),
        ),
        in_specs=[vmem] * 8,
        out_specs=(vmem,) * 4,
        scratch_shapes=[
            pltpu.VMEM((rows, KVR + ROPE), jnp.bfloat16),
            pltpu.VMEM((rows, width), jnp.bfloat16),
            pltpu.VMEM((HEAD, width), jnp.bfloat16),
            dma,
            dma((2, count - 1, slots)),
            dma((2, count - 1, slots)),
            dma((n // 2,)),
            dma((n // 2,)),
        ],
        compiler_params=pltpu.CompilerParams(
            vmem_limit_bytes=VMEM_LIMIT, collective_id=collective_id, has_side_effects=True
        ),
        cost_estimate=pl.CostEstimate(
            flops=2 * rows * width * (rank + KVR + ROPE),
            bytes_accessed=24 * 1024 * 1024,
            transcendentals=rows,
        ),
        name=f"head_layer_{collective_id}",
    )(
        tokens,
        gain_in.reshape(1, -1),
        gain_q.reshape(1, -1),
        gain_kv.reshape(1, -1),
        w_qa,
        w_kva,
        cos,
        sin,
    )
    return gathered.reshape(n * rows, -1), q_latent, q_pre, lat_raw


def wide_tables(inside):
    half_width = ROPE // 2
    lane = jnp.arange(HEAD, dtype=jnp.int32)
    frequency = ROPE_BASE ** (-2.0 * (lane % half_width).astype(jnp.float32) / ROPE)
    angles = inside.astype(jnp.float32)[:, None] * frequency[None, :]
    used = lane[None, :] < ROPE
    return jnp.where(used, jnp.cos(angles), 0.0), jnp.where(used, jnp.sin(angles), 0.0)


def on_device(
    tokens_in,
    w_qa,
    w_kva,
    w_qb,
    w_kvb,
    w_out,
    w_gate,
    w_up,
    w_down,
    gain_in,
    gain_q,
    gain_kv,
    gain_mid,
    cotangent,
    block_map,
    doc_lengths,
):
    local_rows = tokens_in.shape[0]
    half_rows = local_rows // 2
    devices = lax.axis_size("ctx")
    ctx_index = lax.axis_index("ctx")
    seqs = doc_lengths.shape[0]
    own_blocks = lax.dynamic_slice_in_dim(block_map, ctx_index, 1, 0)[0]
    ends = jnp.cumsum(doc_lengths)
    starts = ends - doc_lengths
    meta = jnp.concatenate([block_map.reshape(-1), starts, own_blocks])
    within = jnp.arange(half_rows, dtype=jnp.int32)
    query_place = (own_blocks[:, None] * half_rows + within[None, :]).reshape(-1)
    began = jnp.max(
        jnp.where(starts[None, :] <= query_place[:, None], starts[None, :], 0), axis=1
    )
    cosine, sine = wide_tables(query_place - began)
    latents, q_latent, q_latent_pre, latent_raw = head_layer(
        devices, tokens_in, gain_in, gain_q, gain_kv, w_qa, w_kva.T, cosine, sine, 0
    )
    queries, attn_f, heads_out, log_totals = attention_forward(
        meta, q_latent, w_qb.T, latents, w_kvb, cosine, sine, half_rows, seqs
    )
    attention, d_part, feed_part, activation, d_gate, d_up, normed_mid, d_feed = middle_layer(
        lax.axis_size("tp"), heads_out, tokens_in, cotangent, gain_mid, w_out, w_gate.T, w_up.T,
        w_down.T, 5,
    )
    d_normed_mid = lax.psum(d_part, "tp")
    gw_gate, gw_up, gw_down = scatter_over_ctx(
        devices,
        [
            Scatter(devices, left=normed_mid, right=d_gate),
            Scatter(devices, left=normed_mid, right=d_up),
            Scatter(devices, left=d_feed, right=activation),
        ],
        1,
    )
    d_normed_mid, feed_part, gw_gate, gw_up, gw_down = lax.optimization_barrier(
        (d_normed_mid, feed_part, gw_gate, gw_up, gw_down)
    )
    feed_own = lax.psum_scatter(feed_part, "tp", scatter_dimension=0, tiled=True)
    own_rows = feed_own.shape[0]
    own_at = lax.axis_index("tp") * own_rows
    tokens_own = lax.dynamic_slice_in_dim(tokens_in, own_at, own_rows, 0).astype(jnp.float32)
    attention_own = lax.dynamic_slice_in_dim(attention, own_at, own_rows, 0).astype(jnp.float32)
    middle_own = tokens_own + RESIDUAL_SCALE * attention_own
    out_own = (middle_own + RESIDUAL_SCALE * feed_own.astype(jnp.float32)).astype(jnp.bfloat16)
    d_middle, d_attention, d_heads, d_gain_mid = second_norm_back(
        d_normed_mid, attention, tokens_in, cotangent, gain_mid, w_out
    )
    d_query_pre, d_latents, gw_kvb = attention_backward(
        meta, queries, log_totals, attn_f, d_heads, latents, w_kvb, cosine, sine, half_rows, seqs
    )
    (d_latent_part,) = scatter_over_ctx(devices, [Scatter(devices, given=d_latents)], 2)
    d_q_latent = dot_nt(d_query_pre, w_qb).astype(jnp.bfloat16)
    before_tp = jnp.concatenate([d_q_latent, d_latent_part.astype(jnp.bfloat16)], axis=1)
    before_tp, out_own = lax.optimization_barrier((before_tp, out_own))
    summed_tp = lax.psum(before_tp, "tp")
    gw_out, gw_qb, gw_kvb = scatter_over_ctx(
        devices,
        [
            Scatter(devices, left=d_attention, right=heads_out),
            Scatter(devices, left=q_latent, right=d_query_pre),
            Scatter(devices, given=gw_kvb),
        ],
        3,
    )
    summed_tp, out_own, gw_out, gw_qb, gw_kvb = lax.optimization_barrier(
        (summed_tp, out_own, gw_out, gw_qb, gw_kvb)
    )
    out = lax.all_gather(out_own, "tp", axis=0, tiled=True)
    lanes = jnp.pad(summed_tp, ((0, 0), (0, -summed_tp.shape[1] % HEAD)))
    normed_in, d_q_low, d_kv_input, grad_in, d_gain_in, d_gain_q, d_gain_kv = first_norm_back(
        lanes, q_latent_pre, latent_raw, tokens_in, d_middle, gain_in, gain_q, gain_kv, w_qa,
        w_kva.T, cosine, sine,
    )
    gain_grads = (d_gain_in, d_gain_mid, d_gain_q, d_gain_kv)
    gains = jnp.concatenate([g.reshape(devices, -1) for g in gain_grads], axis=1)
    lines = -(-gains.shape[1] // (32 * HEAD)) * 32
    gains = jnp.pad(gains, ((0, 0), (0, lines * HEAD - gains.shape[1])))
    gw_qa, gw_kva, gains = scatter_over_ctx(
        devices,
        [
            Scatter(devices, left=normed_in, right=d_q_low),
            Scatter(devices, left=normed_in, right=d_kv_input),
            Scatter(devices, given=gains.astype(jnp.bfloat16).reshape(devices * lines, HEAD)),
        ],
        4,
    )
    gains = gains.reshape(-1)
    ends = [0]
    for whole in gain_grads:
        ends.append(ends[-1] + whole.size // devices)
    own_gains = [gains[first:last] for first, last in zip(ends, ends[1:])]
    return (
        out,
        grad_in,
        gw_qa,
        gw_kva,
        gw_qb,
        gw_kvb,
        gw_out,
        gw_gate,
        gw_up,
        gw_down,
        own_gains[0],
        own_gains[2],
        own_gains[3],
        own_gains[1],
    )


def solution(mesh):
    return jax.shard_map(
        on_device,
        mesh=mesh,
        in_specs=(
            P("ctx", None),
            P(),
            P(),
            P(None, "tp"),
            P(None, "tp"),
            P(None, "tp"),
            P(None, "tp"),
            P(None, "tp"),
            P(None, "tp"),
            P(),
            P(),
            P(),
            P(),
            P("ctx", None),
            P(),
            P(),
        ),
        out_specs=(
            P("ctx", None),
            P("ctx", None),
            P("ctx", None),
            P("ctx", None),
            P("ctx", "tp"),
            P("ctx", "tp"),
            P("ctx", "tp"),
            P("ctx", "tp"),
            P("ctx", "tp"),
            P("ctx", "tp"),
            P("ctx"),
            P("ctx"),
            P("ctx"),
            P("ctx"),
        ),
        check_vma=False,
    )
```

```python
import functools
import math

import jax
import jax.numpy as jnp
from jax import lax
from jax.experimental import pallas as pl
from jax.experimental.pallas import tpu as pltpu
from jax.sharding import PartitionSpec as P

KVR = 256
NOPE = 64
ROPE = 32
VDIM = 64
HEAD = NOPE + VDIM
WIDE = 2 * HEAD
MASKED = -1e30
SCORE_SCALE = (NOPE + ROPE) ** (-0.5)
EXP2_SCALE = SCORE_SCALE * math.log2(math.e)
FOLD_AT = 96
SUM_ROWS = 16
VMEM_LIMIT = 56 * 1024 * 1024

EPSILON = 1e-05
ROPE_BASE = 10000.0
RESIDUAL_SCALE = 1.4 / math.sqrt(62.0)


def dot_nn(left_op, right_op):
    return jnp.dot(left_op, right_op, preferred_element_type=jnp.float32)


def dot_nt(left_op, right_op):
    return lax.dot_general(
        left_op, right_op, (((1,), (1,)), ((), ())), preferred_element_type=jnp.float32
    )


def begin_of(place, starts):
    begin = jnp.zeros_like(place)
    for start in starts:
        begin = jnp.where(start <= place, start, begin)
    return begin


def pair_kind(key_block, query_block, starts, block_rows):
    key_first = key_block * block_rows
    query_first = query_block * block_rows
    early = begin_of(query_first, starts)
    late = begin_of(query_first + block_rows - 1, starts)
    needed = (key_block <= query_block) & (key_first + block_rows - 1 >= early)
    whole = (key_block < query_block) & (late <= key_first)
    return needed, whole


def mask_bias(key_block, query_block, starts, block_rows, keys_first):
    key_dim = 0 if keys_first else 1
    shape = (block_rows, block_rows)
    key_place = key_block * block_rows + lax.broadcasted_iota(jnp.int32, shape, key_dim)
    query_place = query_block * block_rows + lax.broadcasted_iota(jnp.int32, shape, 1 - key_dim)
    begin = jnp.zeros(shape, jnp.int32)
    for start in starts:
        begin = jnp.where(start <= query_place, start, begin)
    allowed = (key_place <= query_place) & (key_place >= begin)
    return jnp.where(allowed, 0.0, MASKED)


def shared_key_tile(rope_rows, block_rows):
    place = lax.broadcasted_iota(jnp.int32, (ROPE, HEAD), 0)
    lane = lax.broadcasted_iota(jnp.int32, (ROPE, HEAD), 1)
    eye = jnp.where(place == lane, 1.0, 0.0).astype(jnp.bfloat16)
    tile = dot_nn(rope_rows, eye)
    lanes = lax.broadcasted_iota(jnp.int32, (block_rows, HEAD), 1)
    ones = (lanes >= FOLD_AT) & (lanes < FOLD_AT + 3)
    return jnp.where(ones, 1.0, tile).astype(jnp.bfloat16)


def head_window(h):
    at = h * (NOPE + ROPE)
    return at // HEAD * HEAD, at % HEAD


def window_columns(heads):
    return head_window(heads - 1)[0] + WIDE


def head_groups(heads):
    return [(h, min(h + 2, heads)) for h in range(0, heads, 2)]


def forward_kernel(
    blocks, heads, seqs, meta, cq, wqb, lat, wkvb, cos, sin, qx, o_out, ob_out, u_out,
    wkvt, xs, xr, vt, top, acc, bias, pre, s_ref, p_ref,
):
    rows_all = cq.shape[0]
    block_rows = bias.shape[0]
    q_blocks = rows_all // block_rows
    starts = [meta[blocks + s] for s in range(seqs)]
    own = [meta[blocks + seqs + j] for j in range(q_blocks)]
    for first, last in head_groups(heads):
        wkvt[first * HEAD : last * HEAD, :] = (
            wkvb[:, first * HEAD : last * HEAD].astype(jnp.float32).T.astype(jnp.bfloat16)
        )
    lane = lax.broadcasted_iota(jnp.int32, (block_rows, HEAD), 1)
    for j in range(q_blocks):
        here = pl.ds(j * block_rows, block_rows)
        cos_j, sin_j = cos[here, :], sin[here, :]
        width = heads * (NOPE + ROPE)
        for at in range(0, width, WIDE):
            end = min(at + WIDE, width)
            pre[:, at:end] = dot_nt(cq[here, :], wqb[at:end, :])
        for h in range(heads):
            at, shift = head_window(h)
            own_part = pltpu.roll(pre[:, at : at + WIDE], (WIDE - shift) % WIDE, 1)[:, :HEAD]
            turned = pltpu.roll(own_part, NOPE, 1)
            left = pltpu.roll(turned, HEAD - ROPE // 2, 1)
            right = pltpu.roll(turned, ROPE // 2, 1)
            swapped = jnp.where(lane < ROPE // 2, -left, right)
            rope = jnp.where(lane < ROPE, turned * cos_j + swapped * sin_j, 0.0)
            qx[j, h, :, :HEAD] = jnp.where(lane < NOPE, own_part, 0.0).astype(jnp.bfloat16)
            qx[j, h, :, HEAD:] = rope.astype(jnp.bfloat16)
    top[...] = jnp.full(top.shape, MASKED, jnp.float32)
    vt[:, VDIM:, :] = jnp.ones((heads, SUM_ROWS, block_rows), jnp.bfloat16)
    acc[...] = jnp.zeros(acc.shape, jnp.float32)

    def pair(j, masked):
        def one(h):
            keys = jnp.concatenate([xs[h], xr[...]], axis=1)
            s_ref[h % 3] = dot_nt(keys, qx[j, h])

        def weigh(h):
            old = top[j, h]
            new = old
            for k in range(0, block_rows, 128):
                part = s_ref[h % 3, k : k + 128, :]
                if masked:
                    part = part + bias[k : k + 128, :]
                    s_ref[h % 3, k : k + 128, :] = part
                new = jnp.maximum(new, jnp.max(part, axis=0, keepdims=True))
            fade = jnp.exp2((old - new) * EXP2_SCALE)
            top[j, h] = new
            for k in range(0, block_rows, 128):
                terms = jnp.exp2((s_ref[h % 3, k : k + 128, :] - new) * EXP2_SCALE)
                p_ref[h % 3, k : k + 128, :] = terms.astype(jnp.bfloat16)
            return fade

        def add(h, fade):
            acc[j, h] = fade * acc[j, h] + dot_nn(vt[h], p_ref[h % 3])

        one(0)
        if heads > 1:
            one(1)
        fades = {}
        for h in range(heads):
            if h + 2 < heads:
                one(h + 2)
            fades[h] = weigh(h)
            if h > 1:
                add(h - 2, fades[h - 2])
        for h in range(max(heads - 2, 0), heads):
            add(h, fades[h])

    def step(r, carry):
        key_block = meta[r]
        kinds = [pair_kind(key_block, own[j], starts, block_rows) for j in range(q_blocks)]
        wanted = functools.reduce(jnp.logical_or, [k[0] for k in kinds])

        @pl.when(wanted)
        def _():
            here = pl.ds(pl.multiple_of(r * block_rows, block_rows), block_rows)
            latent = lat[here, :KVR]
            xr[...] = shared_key_tile(lat[here, KVR : KVR + ROPE], block_rows)
            for first, last in head_groups(heads):
                keys = dot_nn(latent, wkvb[:, first * HEAD : last * HEAD]).astype(jnp.bfloat16)
                values = dot_nt(wkvt[first * HEAD : last * HEAD, :], latent).astype(jnp.bfloat16)
                for h in range(first, last):
                    at = (h - first) * HEAD
                    xs[h] = keys[:, at : at + HEAD]
                    vt[h, :VDIM, :] = values[at + NOPE : at + HEAD, :]

        for j in range(q_blocks):
            needed, whole = kinds[j]

            @pl.when(needed & whole)
            def _():
                pair(j, False)

            @pl.when(needed & jnp.logical_not(whole))
            def _():
                bias[...] = mask_bias(key_block, own[j], starts, block_rows, True)
                pair(j, True)

        return carry

    lax.fori_loop(0, blocks, step, 0)
    for j in range(q_blocks):
        here = pl.ds(j * block_rows, block_rows)
        for first, last in head_groups(heads):
            parts = []
            for h in range(first, last):
                total = acc[j, h, VDIM : VDIM + 1, :]
                parts.append(acc[j, h, :VDIM, :] * (1.0 / total))
                u_out[j, h : h + 1, :] = top[j, h] + jnp.log2(total) * (1.0 / EXP2_SCALE)
            if len(parts) == 1:
                parts.append(jnp.zeros_like(parts[0]))
            both = jnp.concatenate(parts, axis=0).T
            width = (last - first) * VDIM
            o_out[here, first * VDIM : first * VDIM + width] = both[:, :width]
            ob_out[here, first * VDIM : first * VDIM + width] = both[:, :width].astype(jnp.bfloat16)


def attention_forward(meta, cq, wqb, lat, wkvb, cos, sin, block_rows, seqs):
    heads = wkvb.shape[1] // HEAD
    blocks = lat.shape[0] // block_rows
    rows = cq.shape[0]
    q_blocks = rows // block_rows
    vmem = pl.BlockSpec(memory_space=pltpu.VMEM)
    pairs = q_blocks * blocks * heads // 2
    return pl.pallas_call(
        functools.partial(forward_kernel, blocks, heads, seqs),
        out_shape=(
            jax.ShapeDtypeStruct((q_blocks, heads, block_rows, WIDE), jnp.bfloat16),
            jax.ShapeDtypeStruct((rows, heads * VDIM), jnp.float32),
            jax.ShapeDtypeStruct((rows, heads * VDIM), jnp.bfloat16),
            jax.ShapeDtypeStruct((q_blocks, 16 * -(-heads // 16), block_rows), jnp.float32),
        ),
        in_specs=[pl.BlockSpec(memory_space=pltpu.SMEM)] + [vmem] * 6,
        out_specs=(vmem,) * 4,
        scratch_shapes=[
            pltpu.VMEM((heads * HEAD, KVR), jnp.bfloat16),
            pltpu.VMEM((heads, block_rows, HEAD), jnp.bfloat16),
            pltpu.VMEM((block_rows, HEAD), jnp.bfloat16),
            pltpu.VMEM((heads, VDIM + SUM_ROWS, block_rows), jnp.bfloat16),
            pltpu.VMEM((q_blocks, heads, 1, block_rows), jnp.float32),
            pltpu.VMEM((q_blocks, heads, VDIM + SUM_ROWS, block_rows), jnp.float32),
            pltpu.VMEM((block_rows, block_rows), jnp.float32),
            pltpu.VMEM((block_rows, window_columns(heads)), jnp.float32),
            pltpu.VMEM((3, block_rows, block_rows), jnp.float32),
            pltpu.VMEM((3, block_rows, block_rows), jnp.bfloat16),
        ],
        compiler_params=pltpu.CompilerParams(vmem_limit_bytes=VMEM_LIMIT),
        cost_estimate=pl.CostEstimate(
            flops=pairs * 4 * block_rows * block_rows * WIDE,
            bytes_accessed=16 * 1024 * 1024,
            transcendentals=pairs * block_rows * block_rows,
        ),
        name="attention_forward",
    )(meta, cq, wqb, lat, wkvb, cos, sin)


def three_terms(column):
    first = column.astype(jnp.bfloat16).astype(jnp.float32)
    rest = column - first
    second = rest.astype(jnp.bfloat16).astype(jnp.float32)
    return first, second, rest - second


def fold_in(tile, column, lane):
    for k, term in enumerate(three_terms(column)):
        tile = jnp.where(lane == FOLD_AT + k, term, tile)
    return tile


def backward_kernel(
    blocks, heads, seqs, meta, qx, u_in, o_in, dob, lat, wkvb, cos, sin, dq_out, dlat, gkvb,
    xs, xr, qo, qt, dt, dq, dkv, dkpe, gsum, bias, flat, s_ref, p_ref, d_ref,
):
    block_rows = bias.shape[0]
    q_blocks = qx.shape[0]
    starts = [meta[blocks + s] for s in range(seqs)]
    own = [meta[blocks + seqs + j] for j in range(q_blocks)]
    lane = lax.broadcasted_iota(jnp.int32, (block_rows, HEAD), 1)
    for j in range(q_blocks):
        here = pl.ds(j * block_rows, block_rows)
        logs = u_in[j].T
        for first, last in head_groups(heads):
            d_pair = dob[here, first * VDIM : first * VDIM + HEAD].astype(jnp.float32)
            weighted = d_pair * o_in[here, first * VDIM : first * VDIM + HEAD]
            turned = pltpu.roll(d_pair, VDIM, 1)
            for h in range(first, last):
                mine = lane < VDIM if h == first else lane >= VDIM
                delta = jnp.sum(jnp.where(mine, weighted, 0.0), axis=1, keepdims=True)
                d_head = jnp.where(lane >= VDIM, turned if h == first else d_pair, 0.0)
                q_first = qx[j, h, :, :HEAD].astype(jnp.float32)
                q_second = qx[j, h, :, HEAD:].astype(jnp.float32)
                qo[j, h, :block_rows, :HEAD] = qx[j, h, :, :HEAD]
                qo[j, h, :block_rows, HEAD:] = fold_in(q_second, -logs[:, h : h + 1], lane).astype(
                    jnp.bfloat16
                )
                qo[j, h, block_rows:, :HEAD] = d_head.astype(jnp.bfloat16)
                qo[j, h, block_rows:, HEAD:] = fold_in(
                    jnp.zeros((block_rows, HEAD), jnp.float32), -delta, lane
                ).astype(jnp.bfloat16)
                qt[j, h, :NOPE, :] = q_first.T[:NOPE, :].astype(jnp.bfloat16)
                qt[j, h, NOPE:, :] = q_second.T[:ROPE, :].astype(jnp.bfloat16)
                dt[j, h] = d_head.T[VDIM:, :].astype(jnp.bfloat16)
    dq[...] = jnp.zeros(dq.shape, jnp.float32)
    gsum[...] = jnp.zeros(gsum.shape, jnp.float32)

    def pair(j, masked):
        def raw(h):
            keys = jnp.concatenate([xs[h], xr[...]], axis=1)
            s_ref[h % 2] = dot_nt(qo[j, h], keys)

        def weigh(h):
            for k in range(0, block_rows, 128):
                scores = s_ref[h % 2, k : k + 128, :] * EXP2_SCALE
                if masked:
                    scores = scores + bias[k : k + 128, :]
                probs = jnp.exp2(scores)
                p_ref[h % 2, k : k + 128, :] = probs.astype(jnp.bfloat16)
                d_ref[h % 2, k : k + 128, :] = (
                    probs * s_ref[h % 2, block_rows + k : block_rows + k + 128, :]
                ).astype(jnp.bfloat16)

        def add(h):
            keys = jnp.concatenate([xs[h], xr[...]], axis=1)
            d_scores = d_ref[h % 2]
            dq[j, h] += dot_nn(d_scores, keys)
            d_keys = dot_nn(qt[j, h], d_scores)
            dkv[h, :NOPE, :] += d_keys[:NOPE]
            dkpe[...] += d_keys[NOPE:]
            dkv[h, NOPE:, :] += dot_nn(dt[j, h], p_ref[h % 2])

        raw(0)
        for h in range(heads):
            if h + 1 < heads:
                raw(h + 1)
            weigh(h)
            if h:
                add(h - 1)
        add(heads - 1)

    def step(r, carry):
        key_block = meta[r]
        kinds = [pair_kind(key_block, own[j], starts, block_rows) for j in range(q_blocks)]
        wanted = functools.reduce(jnp.logical_or, [k[0] for k in kinds])
        here = pl.ds(pl.multiple_of(r * block_rows, block_rows), block_rows)

        @pl.when(wanted)
        def _():
            latent = lat[here, :KVR]
            xr[...] = shared_key_tile(lat[here, KVR : KVR + ROPE], block_rows)
            for first, last in head_groups(heads):
                keys = dot_nn(latent, wkvb[:, first * HEAD : last * HEAD]).astype(jnp.bfloat16)
                for h in range(first, last):
                    xs[h] = keys[:, (h - first) * HEAD : (h - first + 1) * HEAD]
            dkv[...] = jnp.zeros(dkv.shape, jnp.float32)
            dkpe[...] = jnp.zeros(dkpe.shape, jnp.float32)

        for j in range(q_blocks):
            needed, whole = kinds[j]

            @pl.when(needed & whole)
            def _():
                pair(j, False)

            @pl.when(needed & jnp.logical_not(whole))
            def _():
                bias[...] = mask_bias(key_block, own[j], starts, block_rows, False)
                pair(j, True)

        @pl.when(wanted)
        def _():
            latent = lat[here, :KVR]
            d_latent = jnp.zeros((KVR, block_rows), jnp.float32)
            for h in range(heads):
                d_head = jnp.concatenate(
                    [dkv[h, :NOPE, :] * SCORE_SCALE, dkv[h, NOPE:, :]], axis=0
                ).astype(jnp.bfloat16)
                d_latent += dot_nn(wkvb[:, h * HEAD : (h + 1) * HEAD], d_head)
                gsum[h * HEAD : (h + 1) * HEAD, :] += dot_nn(d_head, latent)
            dlat[here, :KVR] = d_latent.T.astype(jnp.bfloat16)
            rope = jnp.concatenate(
                [dkpe[...] * SCORE_SCALE, jnp.zeros((HEAD - ROPE, block_rows), jnp.float32)], axis=0
            )
            dlat[here, KVR:] = rope.T[:, :ROPE].astype(jnp.bfloat16)

        @pl.when(jnp.logical_not(wanted))
        def _():
            dlat[here, :] = jnp.zeros((block_rows, KVR + ROPE), jnp.bfloat16)

        return carry

    lax.fori_loop(0, blocks, step, 0)
    for h in range(heads):
        gkvb[:, h * HEAD : (h + 1) * HEAD] = gsum[h * HEAD : (h + 1) * HEAD, :].T.astype(
            jnp.bfloat16
        )
    for j in range(q_blocks):
        here = pl.ds(j * block_rows, block_rows)
        cos_j, sin_j = cos[here, :], sin[here, :]
        flat[...] = jnp.zeros(flat.shape, jnp.float32)
        for h in range(heads):
            nope = jnp.where(lane < NOPE, dq[j, h, :, :HEAD], 0.0)
            rope = dq[j, h, :, HEAD:]
            shifted = rope * sin_j
            left = pltpu.roll(shifted, HEAD - ROPE // 2, 1)
            right = pltpu.roll(shifted, ROPE // 2, 1)
            swapped = jnp.where(lane < ROPE // 2, left, jnp.where(lane < ROPE, -right, 0.0))
            back = pltpu.roll(jnp.where(lane < ROPE, rope * cos_j + swapped, 0.0), NOPE, 1)
            whole = jnp.concatenate([(nope + back) * SCORE_SCALE, jnp.zeros_like(nope)], axis=1)
            at, shift = head_window(h)
            flat[:, at : at + WIDE] += pltpu.roll(whole, shift, 1)
        dq_out[here, :] = flat[:, : heads * (NOPE + ROPE)].astype(jnp.bfloat16)


def attention_backward(meta, qx, u_in, o_in, dob, lat, wkvb, cos, sin, block_rows, seqs):
    heads = wkvb.shape[1] // HEAD
    blocks = lat.shape[0] // block_rows
    q_blocks = qx.shape[0]
    rows = q_blocks * block_rows
    odd = -(heads * VDIM) % HEAD
    if odd:
        o_in = jnp.pad(o_in, ((0, 0), (0, odd)))
        dob = jnp.pad(dob, ((0, 0), (0, odd)))
    vmem = pl.BlockSpec(memory_space=pltpu.VMEM)
    pairs = q_blocks * blocks * heads // 2
    return pl.pallas_call(
        functools.partial(backward_kernel, blocks, heads, seqs),
        out_shape=(
            jax.ShapeDtypeStruct((rows, heads * (NOPE + ROPE)), jnp.bfloat16),
            jax.ShapeDtypeStruct((lat.shape[0], KVR + ROPE), jnp.bfloat16),
            jax.ShapeDtypeStruct((KVR, heads * HEAD), jnp.bfloat16),
        ),
        in_specs=[pl.BlockSpec(memory_space=pltpu.SMEM)] + [vmem] * 8,
        out_specs=(vmem,) * 3,
        scratch_shapes=[
            pltpu.VMEM((heads, block_rows, HEAD), jnp.bfloat16),
            pltpu.VMEM((block_rows, HEAD), jnp.bfloat16),
            pltpu.VMEM((q_blocks, heads, 2 * block_rows, WIDE), jnp.bfloat16),
            pltpu.VMEM((q_blocks, heads, NOPE + ROPE, block_rows), jnp.bfloat16),
            pltpu.VMEM((q_blocks, heads, VDIM, block_rows), jnp.bfloat16),
            pltpu.VMEM((q_blocks, heads, block_rows, WIDE), jnp.float32),
            pltpu.VMEM((heads, HEAD, block_rows), jnp.float32),
            pltpu.VMEM((ROPE, block_rows), jnp.float32),
            pltpu.VMEM((heads * HEAD, KVR), jnp.float32),
            pltpu.VMEM((block_rows, block_rows), jnp.float32),
            pltpu.VMEM((block_rows, window_columns(heads)), jnp.float32),
            pltpu.VMEM((2, 2 * block_rows, block_rows), jnp.float32),
            pltpu.VMEM((2, block_rows, block_rows), jnp.bfloat16),
            pltpu.VMEM((2, block_rows, block_rows), jnp.bfloat16),
        ],
        compiler_params=pltpu.CompilerParams(vmem_limit_bytes=VMEM_LIMIT),
        cost_estimate=pl.CostEstimate(
            flops=pairs * 8 * block_rows * block_rows * WIDE,
            bytes_accessed=24 * 1024 * 1024,
            transcendentals=pairs * block_rows * block_rows,
        ),
        name="attention_backward",
    )(meta, qx, u_in, o_in, dob, lat, wkvb, cos, sin)


class LineSum:
    def __init__(self, n, own, landing, total, sems, lag):
        self.n, self.own, self.landing, self.total, self.lag = n, own, landing, total, lag
        self.up_send, self.up_land, self.down_send, self.back_send, self.down_land = sems
        self.me = lax.axis_index("tp")
        self.root = (n - 1) // 2
        self.chunks = own.shape[0]
        self.has_left, self.has_right = self.me > 0, self.me < n - 1
        self.root_lag = (n - 1 - self.root) * lag
        self.land_lag = 2 * self.root_lag
        self.ticks = self.chunks + self.land_lag

    def greet(self, barrier):
        me = self.me
        for there, other in ((self.has_left, me - 1), (self.has_right, me + 1)):

            @pl.when(there)
            def _(other=other):
                pl.semaphore_signal(barrier, inc=1, device_id={"tp": other}, device_id_type=MESH)

    def wait_greetings(self, barrier, others):
        both = self.has_left & self.has_right

        @pl.when(both)
        def _():
            pl.semaphore_wait(barrier, 2 + others)

        @pl.when(jnp.logical_not(both))
        def _():
            pl.semaphore_wait(barrier, 1 + others)

    def copy_to(self, source, target, send, land, c, other):
        return pltpu.make_async_remote_copy(
            src_ref=source.at[c],
            dst_ref=target.at[c],
            send_sem=send.at[c],
            recv_sem=land.at[c],
            device_id={"tp": other},
            device_id_type=MESH,
        )

    def rise_left(self, c):
        return self.copy_to(self.own, self.landing, self.up_send, self.up_land, c, self.me + 1)

    def rise_right(self, c):
        return self.copy_to(self.own, self.landing, self.up_send, self.up_land, c, self.me - 1)

    def rise_last(self, c):
        return self.copy_to(self.own, self.total, self.up_send, self.down_land, c, self.me - 1)

    def fall_right(self, c):
        return self.copy_to(self.total, self.total, self.down_send, self.down_land, c, self.me + 1)

    def fall_left(self, c):
        return self.copy_to(self.total, self.total, self.back_send, self.down_land, c, self.me - 1)

    def rise(self, c):
        me, root = self.me, self.root
        rises = [(me == root + 1, self.rise_last)]
        if root:
            rises.append((me < root, self.rise_left))
        if self.n - 1 > root + 1:
            rises.append((me > root + 1, self.rise_right))
        for who, copy in rises:

            @pl.when(who)
            def _(copy=copy):
                copy(c).start()

    def inside(self, c):
        return (c >= 0) & (c < self.chunks)

    def added(self, refs, c):
        sums = refs[0][c].astype(jnp.float32)
        for ref in refs[1:]:
            sums = sums + ref[c].astype(jnp.float32)
        return sums.astype(self.total.dtype)

    def leaf(self, c):
        is_leaf = self.me == self.n - 1
        if self.root:
            is_leaf = is_leaf | (self.me == 0)

        @pl.when(is_leaf & self.inside(c))
        def _():
            self.rise(c)

    def duty(self, t):
        me, root = self.me, self.root
        if self.n > 3:
            c = t - self.lag * jnp.where(me < root, me, self.n - 1 - me)

            @pl.when((me != root) & self.has_left & self.has_right & self.inside(c))
            def _():
                self.rise_right(c).wait_recv()
                self.own[c] = self.added([self.own, self.landing], c)
                self.rise(c)

        c_root = t - self.root_lag

        @pl.when((me == root) & self.inside(c_root))
        def _():
            if root:
                self.rise_left(c_root).wait_recv()
            self.fall_right(c_root).wait_recv()
            terms = [self.own, self.landing, self.total] if root else [self.own, self.total]
            self.total[c_root] = self.added(terms, c_root)
            self.fall_right(c_root).start()
            if root:
                self.fall_left(c_root).start()

        c_fall = t - self.root_lag - self.lag * jnp.where(me < root, root - me, me - root)

        @pl.when((me != root) & self.inside(c_fall))
        def _():
            self.fall_right(c_fall).wait_recv()

            @pl.when((me > root) & self.has_right)
            def _():
                self.fall_right(c_fall).start()

            @pl.when((me < root) & self.has_left)
            def _():
                self.fall_left(c_fall).start()

    def landed(self, t):
        return t - self.land_lag

    def drain(self):
        me = self.me

        def body(c, carry):
            @pl.when(me != self.root)
            def _():
                self.rise_right(c).wait_send()

            @pl.when((me >= self.root) & self.has_right)
            def _():
                self.fall_right(c).wait_send()

            @pl.when((me <= self.root) & self.has_left)
            def _():
                self.fall_left(c).wait_send()

            return carry

        lax.fori_loop(0, self.chunks, body, 0)


def line_sems(chunks):
    return [pltpu.SemaphoreType.DMA((chunks,))] * 5


MESH = pl.DeviceIdType.MESH


class Scatter:
    def __init__(self, n, given=None, left=None, right=None):
        self.operands = [given] if given is not None else [left, right]
        self.is_given = given is not None
        self.rows = self.operands[0].shape[0 if self.is_given else 1] // n
        self.columns = self.operands[-1].shape[1]
        self.depth = 0 if self.is_given else right.shape[0]
        self.parts = 2 if self.rows % 32 == 0 else 1


def scatter_blocks(bits_left):
    chips = []
    for value in range(1 << len(bits_left)):
        chip = 0
        for at, bit in enumerate(bits_left):
            chip = chip + (((value >> at) & 1) << (bit - 1))
        chips.append(chip)
    return chips


def scatter_operands(items):
    given = [item.operands[0] for item in items if item.is_given]
    lefts = []
    for item in items:
        if not item.is_given and not any(item.operands[0] is left for left in lefts):
            lefts.append(item.operands[0])
    return given, lefts, [item.operands[1] for item in items if not item.is_given]


def scatter_kernel(n, items, line_n, *refs):
    count = n.bit_length() - 1
    me = lax.axis_index("ctx")
    refs = list(refs)
    take = lambda k: [refs.pop(0) for _ in range(k)]
    given, lefts, rights = scatter_operands(items)
    inputs = dict(zip(map(id, given + lefts + rights), take(len(given + lefts + rights))))
    line_in = take(1) if line_n else None
    outputs = take(len(items))
    line_out = take(1)[0] if line_n else None
    held, sent, landed, core_sems, step_sems = [], [], [], [], []
    for item in items:
        held.append(refs.pop(0))
        sent.append(None if item.is_given else refs.pop(0))
        landed.append(take(count - 1))
        core_sems.append(take(2))
        step_sems.append([take(2) for _ in range(count - 1)])
    turned = dict(zip(map(id, lefts), take(len(lefts))))
    line = None
    if line_n:
        own, landing = take(2)
        line = LineSum(line_n, own, landing, line_out, take(5), LAG)
    barrier = pltpu.get_barrier_semaphore()
    for bit in range(count):
        pl.semaphore_signal(barrier, inc=1, device_id={"ctx": me ^ (1 << bit)}, device_id_type=MESH)
    if line_n:
        line.greet(barrier)
        own[...] = line_in[0][...]
        line.wait_greetings(barrier, count)

        def leaf(c, carry):
            line.leaf(c)
            return carry

        lax.fori_loop(0, line.chunks, leaf, 0)
    else:
        pl.semaphore_wait(barrier, count)
    core = me & 1
    chips = n // 2
    orders = (tuple(range(1, count)), tuple(range(count - 1, 0, -1)))

    def columns_of(item):
        return [(c, min(c + 512, item.columns)) for c in range(0, item.columns, 512)]

    def product(k, dest, first, last):
        item = items[k]
        left, right = turned[id(item.operands[0])], inputs[id(item.operands[1])]
        at = pl.ds(pl.multiple_of(dest * item.rows, 16), item.rows)
        return dot_nn(left[at, :], right[:, first:last])

    def core_copy(k, chip):
        item = items[k]
        if item.is_given:
            at = pl.ds(pl.multiple_of((2 * chip + 1 - core) * item.rows, 16), item.rows)
            source = inputs[id(item.operands[0])].at[at, :]
        else:
            source = sent[k].at[chip]
        return pltpu.make_async_remote_copy(
            src_ref=source,
            dst_ref=held[k].at[chip],
            send_sem=core_sems[k][0].at[chip],
            recv_sem=core_sems[k][1].at[chip],
            device_id={"ctx": me ^ 1},
            device_id_type=MESH,
        )

    def step_copies(k, step):
        item = items[k]
        half = item.rows // item.parts
        copies = []
        for part, order in enumerate(orders[: item.parts]):
            bit = order[step]
            left = sorted(order[step + 1 :])
            fixed = [b for b in order[:step]]
            at = pl.ds(part * half, half)
            for slot, free in enumerate(scatter_blocks(left)):
                keep = free + ((me >> bit) & 1) * (1 << (bit - 1))
                send = free + (1 - ((me >> bit) & 1)) * (1 << (bit - 1))
                for b in fixed:
                    own = ((me >> b) & 1) * (1 << (b - 1))
                    keep, send = keep + own, send + own
                copies.append(
                    (
                        pltpu.make_async_remote_copy(
                            src_ref=held[k].at[send, at, :],
                            dst_ref=landed[k][step].at[slot, at, :],
                            send_sem=step_sems[k][step][0].at[part, slot],
                            recv_sem=step_sems[k][step][1].at[part, slot],
                            device_id={"ctx": me ^ (1 << bit)},
                            device_id_type=MESH,
                        ),
                        keep,
                        slot,
                        at,
                    )
                )
        return copies

    def pump(first, last):
        def body(t, carry):
            line.duty(t)
            return carry

        if line_n:
            lax.fori_loop(first, min(last, line.ticks), body, 0)

    def start_core(k):
        item = items[k]

        def body(chip, carry):
            if line_n and k:
                line.duty(ticks * k - ticks + chip)
            if not item.is_given:
                for first, last in columns_of(item):
                    sent[k][chip, :, first:last] = product(
                        k, 2 * chip + 1 - core, first, last
                    ).astype(jnp.bfloat16)
            core_copy(k, chip).start()
            return carry

        lax.fori_loop(0, chips, body, 0)

    def finish_core(k):
        item = items[k]

        def body(chip, carry):
            if line_n:
                line.duty(ticks * (len(items) - 1 + k) + chip)
            core_copy(k, chip).wait_recv()
            at = pl.ds(pl.multiple_of((2 * chip + core) * item.rows, 16), item.rows)
            for first, last in columns_of(item):
                if item.is_given:
                    own = inputs[id(item.operands[0])][at, first:last].astype(jnp.float32)
                else:
                    own = product(k, 2 * chip + core, first, last)
                total = own + held[k][chip, :, first:last].astype(jnp.float32)
                held[k][chip, :, first:last] = total.astype(jnp.bfloat16)
            return carry

        lax.fori_loop(0, chips, body, 0)

    def start_step(k, step):
        for copy, _, _, _ in step_copies(k, step):
            copy.start()

    def finish_step(k, step):
        item = items[k]
        for copy, keep, slot, at in step_copies(k, step):
            copy.wait_recv()
            for first, last in columns_of(item):
                total = held[k][keep, at, first:last].astype(jnp.float32) + landed[k][step][
                    slot, at, first:last
                ].astype(jnp.float32)
                if step == count - 2:
                    outputs[k][at, first:last] = total
                else:
                    held[k][keep, at, first:last] = total.astype(jnp.bfloat16)

    def turn(k):
        key = None if items[k].is_given else id(items[k].operands[0])
        if key in turned and key not in done:
            done.add(key)
            source, target = inputs[key], turned[key]

            def body(c, carry):
                at = pl.ds(pl.multiple_of(c * 128, 128), 128)
                target[at, :] = source[:, at].astype(jnp.float32).T.astype(jnp.bfloat16)
                return carry

            lax.fori_loop(0, source.shape[1] // 128, body, 0)

    done = set()
    every = range(len(items))
    ticks = chips
    pumped = ticks * (2 * len(items) - 1)
    waits = (count - 1) * len(items)
    portion = -(-(line.ticks - pumped) // waits) if line_n else 0
    turn(0)
    start_core(0)
    for k in every:
        if k + 1 < len(items):
            turn(k + 1)
            start_core(k + 1)
        finish_core(k)
        start_step(k, 0)
    for step in range(count - 1):
        for k in every:
            pump(pumped, pumped + portion)
            pumped += portion
            finish_step(k, step)
            if step + 1 < count - 1:
                start_step(k, step + 1)
    for k in every:

        def drain(chip, carry, k=k):
            core_copy(k, chip).wait_send()
            return carry

        lax.fori_loop(0, chips, drain, 0)
        for step in range(count - 1):
            for copy, _, _, _ in step_copies(k, step):
                copy.wait_send()
    if line_n:
        line.drain()


def scatter_over_ctx(n, items, collective_id, line_n=0, line_rows=None):
    vmem = pl.BlockSpec(memory_space=pltpu.VMEM)
    count = n.bit_length() - 1
    scratch = []
    flops = 0
    for item in items:
        scratch.append(pltpu.VMEM((n // 2, item.rows, item.columns), jnp.bfloat16))
        if not item.is_given:
            scratch.append(pltpu.VMEM((n // 2, item.rows, item.columns), jnp.bfloat16))
        scratch += [
            pltpu.VMEM((n >> (step + 2), item.rows, item.columns), jnp.bfloat16)
            for step in range(count - 1)
        ]
        scratch += [pltpu.SemaphoreType.DMA((n // 2,))] * 2
        for step in range(count - 1):
            scratch += [pltpu.SemaphoreType.DMA((2, n >> (step + 2)))] * 2
        flops += 2 * n * item.rows * item.columns * item.depth
    given, lefts, rights = scatter_operands(items)
    operands = given + lefts + rights
    scratch += [pltpu.VMEM(left.shape[::-1], jnp.bfloat16) for left in lefts]
    outs = [jax.ShapeDtypeStruct((item.rows, item.columns), jnp.float32) for item in items]
    if line_n:
        rows, width = line_rows.shape
        chunked = (rows // CHUNK, CHUNK, width)
        operands.append(line_rows.reshape(chunked))
        outs.append(jax.ShapeDtypeStruct(chunked, line_rows.dtype))
        scratch += [pltpu.VMEM(chunked, line_rows.dtype)] * 2 + line_sems(rows // CHUNK)
    results = pl.pallas_call(
        functools.partial(scatter_kernel, n, items, line_n),
        out_shape=tuple(outs),
        in_specs=[vmem] * len(operands),
        out_specs=(vmem,) * len(outs),
        scratch_shapes=scratch,
        compiler_params=pltpu.CompilerParams(
            vmem_limit_bytes=MIDDLE_VMEM, collective_id=collective_id, has_side_effects=True
        ),
        cost_estimate=pl.CostEstimate(
            flops=flops, bytes_accessed=64 * 1024 * 1024, transcendentals=0
        ),
        name=f"scatter_over_ctx_{collective_id}",
    )(*operands)
    if line_n:
        return *results[:-1], results[-1].reshape(line_rows.shape)
    return results


CHUNK = 16
BLOCK = 8 * CHUNK
LAG = 2
MIDDLE_VMEM = 63 * 1024 * 1024


def middle_kernel(
    n, lag, ob, tokens_in, cot_in, gain, w_out, w_gate, w_up, w_down,
    tt_to, d_to, f_to, act_to, dg_to, du_to, h_to, df_to,
    tt, d_out, f_out, act_out, dg_out, du_out, h_out, df_out,
    tokens, cot, own, up, wo, wg, wu, wd, d_acc, f_acc, w_sems, out_sems, *sems,
):
    line = LineSum(n, own, up, tt, sems, lag)
    width = tokens.shape[1]
    hidden = wg.shape[0]
    chunks, chunk = own.shape[:2]
    per_block = BLOCK // chunk
    blocks = chunks // per_block
    block_lag = -(-(per_block + line.land_lag) // per_block)
    tiles = [(c, min(c + 512, width)) for c in range(0, width, 512)]
    quarter = hidden // 4 // 128 * 128
    cuts = [0, quarter, 2 * quarter, 3 * quarter, hidden]
    loads = [
        pltpu.make_async_copy(source, target, w_sems.at[k])
        for k, (source, target) in enumerate(
            (
                (w_out, wo),
                (tokens_in, tokens),
                (cot_in, cot),
                (w_gate, wg),
                (w_up, wu),
                (w_down, wd),
            )
        )
    ]
    kept = ((d_out, d_to), (f_out, f_to), (act_out, act_to), (dg_out, dg_to), (du_out, du_to))
    kept += ((h_out, h_to), (df_out, df_to))

    def keep(b):
        rows = pl.ds(pl.multiple_of(b * BLOCK, BLOCK), BLOCK)
        copies = [
            pltpu.make_async_copy(source.at[rows, :], target.at[rows, :], out_sems.at[k, b])
            for k, (source, target) in enumerate(kept)
        ]
        some = pl.ds(b * per_block, per_block)
        return copies + [
            pltpu.make_async_copy(tt.at[some], tt_to.at[some], out_sems.at[len(kept), b])
        ]

    for load in loads:
        load.start()
    barrier = pltpu.get_barrier_semaphore()
    line.greet(barrier)
    line.wait_greetings(barrier, 0)

    def project(b, carry):
        rows = pl.ds(pl.multiple_of(b * BLOCK, BLOCK), BLOCK)
        for first, last in tiles:
            part = dot_nt(ob[rows, :], wo[first:last, :]).astype(jnp.bfloat16)
            for k in range(per_block):
                own[per_block * b + k, :, first:last] = part[k * chunk : (k + 1) * chunk, :]
        for k in range(per_block):
            line.leaf(per_block * b + k)
        return carry

    def normalize(b, part):
        for k in range(part * per_block // 2, (part + 1) * per_block // 2, 2):
            rows = pl.ds(pl.multiple_of(b * BLOCK + k * chunk, 2 * chunk), 2 * chunk)
            sums = jnp.concatenate([tt[b * per_block + k], tt[b * per_block + k + 1]], axis=0)
            middle = tokens[rows, :].astype(jnp.float32) + RESIDUAL_SCALE * sums.astype(jnp.float32)
            h_out[rows, :] = (middle * norm_scale(middle) * gain[...]).astype(jnp.bfloat16)

    def feed(b, i):
        rows = pl.ds(pl.multiple_of(b * BLOCK, BLOCK), BLOCK)
        first, last = cuts[i], cuts[i + 1]
        if i == 0:
            normalize(b, 0)
            normalize(b, 1)
            df_out[rows, :] = (RESIDUAL_SCALE * cot[rows, :].astype(jnp.float32)).astype(
                jnp.bfloat16
            )
        gate = dot_nt(h_out[rows, :], wg[first:last, :])
        upper = dot_nt(h_out[rows, :], wu[first:last, :])
        d_act = dot_nt(df_out[rows, :], wd[first:last, :])
        sig = jax.nn.sigmoid(gate)
        silu = gate * sig
        act_out[rows, first:last] = (silu * upper).astype(jnp.bfloat16)
        dg_out[rows, first:last] = (d_act * upper * sig * (1.0 + gate * (1.0 - sig))).astype(
            jnp.bfloat16
        )
        du_out[rows, first:last] = (d_act * silu).astype(jnp.bfloat16)

    def feed_back(b, i):
        rows = pl.ds(pl.multiple_of(b * BLOCK, BLOCK), BLOCK)
        first, last = cuts[i], cuts[i + 1]
        act, dg, du = (ref[rows, first:last] for ref in (act_out, dg_out, du_out))
        for lo, hi in tiles:
            d_part = dot_nn(dg, wg[first:last, lo:hi]) + dot_nn(du, wu[first:last, lo:hi])
            f_part = dot_nn(act, wd[first:last, lo:hi])
            if i:
                d_part = d_part + d_acc[:, lo:hi]
                f_part = f_part + f_acc[:, lo:hi]
            if i < 3:
                d_acc[:, lo:hi] = d_part
                f_acc[:, lo:hi] = f_part
            else:
                d_out[rows, lo:hi] = d_part.astype(jnp.bfloat16)
                f_out[rows, lo:hi] = f_part.astype(jnp.bfloat16)

    loads[0].wait()
    lax.fori_loop(0, blocks, project, 0)

    def outer(o, carry):
        b = o - block_lag

        @pl.when(b == 0)
        def _():
            for load in loads[1:]:
                load.wait()

        share = per_block // 8
        for i in range(4):
            for step, work in enumerate((feed, feed_back)):

                @pl.when(o * per_block < line.ticks)
                def _(at=(2 * i + step) * share):
                    for k in range(share):
                        line.duty(o * per_block + at + k)

                @pl.when(b >= 0)
                def _(i=i, work=work):
                    work(b, i)

        @pl.when(b >= 0)
        def _():
            for copy in keep(b):
                copy.start()

        return carry

    lax.fori_loop(0, blocks + block_lag, outer, 0)
    line.drain()

    def finish(b, carry):
        for copy in keep(b):
            copy.wait()
        return carry

    lax.fori_loop(0, blocks, finish, 0)


def middle_layer(n, ob, tokens, cot, gain, w_out, w_gate, w_up, w_down, collective_id):
    rows, width = tokens.shape
    hidden = w_gate.shape[0]
    chunks = rows // CHUNK
    vmem = pl.BlockSpec(memory_space=pltpu.VMEM)
    anywhere = pl.BlockSpec(memory_space=pl.ANY)
    half = jnp.bfloat16
    dma = pltpu.SemaphoreType.DMA
    attn, *rest = pl.pallas_call(
        functools.partial(middle_kernel, n, LAG),
        out_shape=(
            jax.ShapeDtypeStruct((chunks, CHUNK, width), half),
            jax.ShapeDtypeStruct((rows, width), half),
            jax.ShapeDtypeStruct((rows, width), half),
            jax.ShapeDtypeStruct((rows, hidden), half),
            jax.ShapeDtypeStruct((rows, hidden), half),
            jax.ShapeDtypeStruct((rows, hidden), half),
            jax.ShapeDtypeStruct((rows, width), half),
            jax.ShapeDtypeStruct((rows, width), half),
        ),
        in_specs=[vmem, anywhere, anywhere, vmem] + [anywhere] * 4,
        out_specs=(anywhere,) * 8,
        scratch_shapes=[
            pltpu.VMEM((chunks, CHUNK, width), half),
            pltpu.VMEM((rows, width), half),
            pltpu.VMEM((rows, width), half),
            pltpu.VMEM((rows, hidden), half),
            pltpu.VMEM((rows, hidden), half),
            pltpu.VMEM((rows, hidden), half),
            pltpu.VMEM((rows, width), half),
            pltpu.VMEM((rows, width), half),
            pltpu.VMEM((rows, width), half),
            pltpu.VMEM((rows, width), half),
            pltpu.VMEM((chunks, CHUNK, width), half),
            pltpu.VMEM((chunks, CHUNK, width), half),
            pltpu.VMEM(w_out.shape, half),
            pltpu.VMEM(w_gate.shape, half),
            pltpu.VMEM(w_up.shape, half),
            pltpu.VMEM(w_down.shape, half),
            pltpu.VMEM((BLOCK, width), jnp.float32),
            pltpu.VMEM((BLOCK, width), jnp.float32),
            dma((6,)),
            dma((8, rows // BLOCK)),
            *line_sems(chunks),
        ],
        compiler_params=pltpu.CompilerParams(
            vmem_limit_bytes=MIDDLE_VMEM, collective_id=collective_id, has_side_effects=True
        ),
        cost_estimate=pl.CostEstimate(
            flops=2 * rows * width * (6 * hidden + ob.shape[1]),
            bytes_accessed=64 * 1024 * 1024,
            transcendentals=rows * hidden,
        ),
        name=f"middle_layer_{collective_id}",
    )(ob, tokens, cot, gain.reshape(1, -1), w_out, w_gate, w_up, w_down)
    return attn.reshape(rows, width), *rest


def norm_scale(values):
    return lax.rsqrt(jnp.mean(values * values, axis=-1, keepdims=True) + EPSILON)


def norm_back(incoming, values, inv_rms, gain_vec):
    weighted = incoming * gain_vec
    mean = jnp.mean(weighted * values, axis=-1, keepdims=True)
    d_values = inv_rms * weighted - values * (inv_rms * inv_rms * inv_rms) * mean
    return d_values, jnp.sum(incoming * values * inv_rms, axis=0, keepdims=True)


def rope_tile(tile, cos, sin, lane):
    left = pltpu.roll(tile, HEAD - ROPE // 2, 1)
    right = pltpu.roll(tile, ROPE // 2, 1)
    swapped = jnp.where(lane < ROPE // 2, -left, right)
    return jnp.where(lane < ROPE, tile * cos + swapped * sin, 0.0)


def rope_tile_back(tile, cos, sin, lane):
    shifted = tile * sin
    left = pltpu.roll(shifted, HEAD - ROPE // 2, 1)
    right = pltpu.roll(shifted, ROPE // 2, 1)
    swapped = jnp.where(lane < ROPE // 2, left, -right)
    return jnp.where(lane < ROPE, tile * cos + swapped, 0.0)


def second_norm_kernel(
    d_sum, attn, tokens, cot, gain, w_out, d_middle, d_attn, d_heads, d_gain
):
    middle = tokens[...].astype(jnp.float32) + RESIDUAL_SCALE * attn[...].astype(jnp.float32)
    d_norm, gain_terms = norm_back(
        d_sum[...].astype(jnp.float32), middle, norm_scale(middle), gain[...]
    )
    total = cot[...].astype(jnp.float32) + d_norm
    d_middle[...] = total
    scaled = (RESIDUAL_SCALE * total).astype(jnp.bfloat16)
    d_attn[...] = scaled
    d_heads[...] = dot_nn(scaled, w_out[...]).astype(jnp.bfloat16)

    @pl.when(pl.program_id(0) == 0)
    def _():
        d_gain[...] = jnp.zeros(d_gain.shape, jnp.float32)

    d_gain[...] += gain_terms


def second_norm_back(d_sum, attn, tokens, cot, gain, w_out):
    rows, width = tokens.shape
    block = rows // 4
    head_width = w_out.shape[1]
    whole = lambda shape: pl.BlockSpec(shape, lambda i: (0, 0))
    tile = lambda columns: pl.BlockSpec((block, columns), lambda i: (i, 0))
    return pl.pallas_call(
        second_norm_kernel,
        grid=(rows // block,),
        out_shape=(
            jax.ShapeDtypeStruct((rows, width), jnp.float32),
            jax.ShapeDtypeStruct((rows, width), jnp.bfloat16),
            jax.ShapeDtypeStruct((rows, head_width), jnp.bfloat16),
            jax.ShapeDtypeStruct((1, width), jnp.float32),
        ),
        in_specs=[tile(width)] * 4 + [whole((1, width)), whole((width, head_width))],
        out_specs=(tile(width), tile(width), tile(head_width), whole((1, width))),
        compiler_params=pltpu.CompilerParams(vmem_limit_bytes=VMEM_LIMIT),
        cost_estimate=pl.CostEstimate(
            flops=2 * rows * width * head_width,
            bytes_accessed=24 * 1024 * 1024,
            transcendentals=rows,
        ),
        name="second_norm_back",
    )(d_sum, attn, tokens, cot, gain.reshape(1, -1), w_out)


def first_norm_kernel(
    d_tp, q_pre, lat_raw, tokens, d_middle, gain_in, gain_q, gain_kv, w_qa, w_kva, cos, sin,
    normed, d_q, d_kv, grad_in, g_in, g_q, g_kv,
):
    rank = q_pre.shape[1]
    block = tokens.shape[0]
    lane = lax.broadcasted_iota(jnp.int32, (block, HEAD), 1)

    @pl.when(pl.program_id(0) == 0)
    def _():
        for ref in (g_in, g_q, g_kv):
            ref[...] = jnp.zeros(ref.shape, jnp.float32)

    pre = q_pre[...]
    d_pre, terms = norm_back(d_tp[:, :rank].astype(jnp.float32), pre, norm_scale(pre), gain_q[...])
    g_q[...] += terms
    d_low = d_pre.astype(jnp.bfloat16)
    d_q[...] = d_low
    raw = lat_raw[...]
    d_raw, terms = norm_back(
        d_tp[:, rank : rank + KVR].astype(jnp.float32), raw, norm_scale(raw), gain_kv[...]
    )
    g_kv[...] += terms
    rope = rope_tile_back(
        d_tp[:, rank + KVR : rank + KVR + HEAD].astype(jnp.float32), cos[...], sin[...], lane
    )
    d_raw = d_raw.astype(jnp.bfloat16)
    d_rope = rope[:, :ROPE].astype(jnp.bfloat16)
    d_kv[:, :KVR] = d_raw
    d_kv[:, KVR:] = d_rope
    d_normed = dot_nt(d_low, w_qa[...])
    d_normed = d_normed + dot_nn(d_raw, w_kva[:KVR, :]) + dot_nn(d_rope, w_kva[KVR:, :])
    values = tokens[...].astype(jnp.float32)
    scale = norm_scale(values)
    normed[...] = (values * scale * gain_in[...]).astype(jnp.bfloat16)
    d_values, terms = norm_back(d_normed, values, scale, gain_in[...])
    g_in[...] += terms
    grad_in[...] = d_middle[...] + d_values


def first_norm_back(
    d_tp, q_pre, lat_raw, tokens, d_middle, gain_in, gain_q, gain_kv, w_qa, w_kva, cos, sin
):
    rows, width = tokens.shape
    block = rows // 4
    rank = q_pre.shape[1]
    whole = lambda array: pl.BlockSpec(array.shape, lambda i: (0, 0))
    tile = lambda columns: pl.BlockSpec((block, columns), lambda i: (i, 0))
    gains = [g.reshape(1, -1) for g in (gain_in, gain_q, gain_kv)]
    wide = jax.ShapeDtypeStruct
    return pl.pallas_call(
        first_norm_kernel,
        grid=(rows // block,),
        out_shape=(
            wide((rows, width), jnp.bfloat16),
            wide((rows, rank), jnp.bfloat16),
            wide((rows, KVR + ROPE), jnp.bfloat16),
            wide((rows, width), jnp.float32),
            wide((1, width), jnp.float32),
            wide((1, rank), jnp.float32),
            wide((1, KVR), jnp.float32),
        ),
        in_specs=[tile(d_tp.shape[1]), tile(rank), tile(KVR), tile(width), tile(width)]
        + [whole(g) for g in gains]
        + [whole(w_qa), whole(w_kva), tile(HEAD), tile(HEAD)],
        out_specs=(
            tile(width),
            tile(rank),
            tile(KVR + ROPE),
            tile(width),
            *[whole(g) for g in gains],
        ),
        compiler_params=pltpu.CompilerParams(vmem_limit_bytes=VMEM_LIMIT),
        cost_estimate=pl.CostEstimate(
            flops=2 * rows * width * (rank + KVR + ROPE),
            bytes_accessed=32 * 1024 * 1024,
            transcendentals=rows,
        ),
        name="first_norm_back",
    )(d_tp, q_pre, lat_raw, tokens, d_middle, *gains, w_qa, w_kva, cos, sin)


def head_kernel(
    n, tokens, gain_in, gain_q, gain_kv, w_qa, w_kva, cos, sin, out, q_latent, q_pre, lat_raw,
    own, normed, w_rope, local_sem, step_sends, step_lands, core_sends, core_lands,
):
    count = n.bit_length() - 1
    me = lax.axis_index("ctx")
    rows = own.shape[0]
    half = rows // 2
    block = rows // 4
    barrier = pltpu.get_barrier_semaphore()
    for bit in range(count):
        pl.semaphore_signal(barrier, inc=1, device_id={"ctx": me ^ (1 << bit)}, device_id_type=MESH)
    orders = (tuple(range(1, count)), tuple(range(count - 1, 0, -1)))
    lane = lax.broadcasted_iota(jnp.int32, (block, HEAD), 1)
    w_rope[...] = jnp.zeros(w_rope.shape, jnp.bfloat16)
    w_rope[:ROPE, :] = w_kva[KVR : KVR + ROPE, :]

    def latents(k, carry):
        at = pl.ds(pl.multiple_of(k * block, block), block)
        values = tokens[at, :].astype(jnp.float32)
        normed[at, :] = (values * norm_scale(values) * gain_in[...]).astype(jnp.bfloat16)
        raw = dot_nt(normed[at, :], w_kva[:KVR, :])
        lat_raw[at, :] = raw
        own[at, :KVR] = (raw * norm_scale(raw) * gain_kv[...]).astype(jnp.bfloat16)
        rope = rope_tile(dot_nt(normed[at, :], w_rope[...]), cos[at, :], sin[at, :], lane)
        own[at, KVR:] = rope[:, :ROPE].astype(jnp.bfloat16)
        return carry

    lax.fori_loop(0, 4, latents, 0)
    pl.semaphore_wait(barrier, count)
    local = pltpu.make_async_copy(own, out.at[me], local_sem)
    local.start()

    def chip_copy(part, step, slot, block, first):
        at = pl.ds(part * half, half)
        return pltpu.make_async_remote_copy(
            src_ref=own.at[at, :] if first else out.at[block, at, :],
            dst_ref=out.at[block, at, :],
            send_sem=step_sends.at[part, step, slot],
            recv_sem=step_lands.at[part, step, slot],
            device_id={"ctx": me ^ (1 << orders[part][step])},
            device_id_type=MESH,
        )

    def core_copy(block, slot, first):
        return pltpu.make_async_remote_copy(
            src_ref=own if first else out.at[block],
            dst_ref=out.at[block],
            send_sem=core_sends.at[slot],
            recv_sem=core_lands.at[slot],
            device_id={"ctx": me ^ 1},
            device_id_type=MESH,
        )

    def query(k, carry):
        at = pl.ds(pl.multiple_of(k * block, block), block)
        pre = dot_nn(normed[at, :], w_qa[...])
        q_pre[at, :] = pre
        q_latent[at, :] = (pre * norm_scale(pre) * gain_q[...]).astype(jnp.bfloat16)
        return carry

    started = []
    for step in range(count - 1):
        for part, order in enumerate(orders):
            for slot in range(1 << step):
                flips = 0
                for at in range(step):
                    flips |= ((slot >> at) & 1) << order[at]
                copy = chip_copy(part, step, slot, me ^ flips, slot == 0)
                copy.start()
                started.append(copy)
        if step == 0:
            core_copy(me, 0, True).start()
        lax.fori_loop(2 * step, min(2 * step + 2, 4) if step < count - 2 else 4, query, 0)
        for part, order in enumerate(orders):
            for slot in range(1 << step):
                chip_copy(part, step, slot, me, slot == 0).wait_recv()
    for chip in range(1, n // 2):
        core_copy(me ^ (2 * chip), chip, False).start()
    for chip in range(n // 2):
        core_copy(me, chip, chip == 0).wait_recv()
    for copy in started:
        copy.wait_send()
    for chip in range(n // 2):
        core_copy(me, chip, chip == 0).wait_send()
    local.wait()


def head_layer(n, tokens, gain_in, gain_q, gain_kv, w_qa, w_kva, cos, sin, collective_id):
    rows, width = tokens.shape
    rank = w_qa.shape[1]
    count = n.bit_length() - 1
    vmem = pl.BlockSpec(memory_space=pltpu.VMEM)
    slots = max(n // 4, 1)
    dma = pltpu.SemaphoreType.DMA
    gathered, q_latent, q_pre, lat_raw = pl.pallas_call(
        functools.partial(head_kernel, n),
        out_shape=(
            jax.ShapeDtypeStruct((n, rows, KVR + ROPE), jnp.bfloat16),
            jax.ShapeDtypeStruct((rows, rank), jnp.bfloat16),
            jax.ShapeDtypeStruct((rows, rank), jnp.float32),
            jax.ShapeDtypeStruct((rows, KVR), jnp.float32),
        ),
        in_specs=[vmem] * 8,
        out_specs=(vmem,) * 4,
        scratch_shapes=[
            pltpu.VMEM((rows, KVR + ROPE), jnp.bfloat16),
            pltpu.VMEM((rows, width), jnp.bfloat16),
            pltpu.VMEM((HEAD, width), jnp.bfloat16),
            dma,
            dma((2, count - 1, slots)),
            dma((2, count - 1, slots)),
            dma((n // 2,)),
            dma((n // 2,)),
        ],
        compiler_params=pltpu.CompilerParams(
            vmem_limit_bytes=VMEM_LIMIT, collective_id=collective_id, has_side_effects=True
        ),
        cost_estimate=pl.CostEstimate(
            flops=2 * rows * width * (rank + KVR + ROPE),
            bytes_accessed=24 * 1024 * 1024,
            transcendentals=rows,
        ),
        name=f"head_layer_{collective_id}",
    )(
        tokens,
        gain_in.reshape(1, -1),
        gain_q.reshape(1, -1),
        gain_kv.reshape(1, -1),
        w_qa,
        w_kva,
        cos,
        sin,
    )
    return gathered.reshape(n * rows, -1), q_latent, q_pre, lat_raw


def wide_tables(inside):
    half_width = ROPE // 2
    lane = jnp.arange(HEAD, dtype=jnp.int32)
    frequency = ROPE_BASE ** (-2.0 * (lane % half_width).astype(jnp.float32) / ROPE)
    angles = inside.astype(jnp.float32)[:, None] * frequency[None, :]
    used = lane[None, :] < ROPE
    return jnp.where(used, jnp.cos(angles), 0.0), jnp.where(used, jnp.sin(angles), 0.0)


def on_device(
    tokens_in,
    w_qa,
    w_kva,
    w_qb,
    w_kvb,
    w_out,
    w_gate,
    w_up,
    w_down,
    gain_in,
    gain_q,
    gain_kv,
    gain_mid,
    cotangent,
    block_map,
    doc_lengths,
):
    local_rows = tokens_in.shape[0]
    half_rows = local_rows // 2
    devices = lax.axis_size("ctx")
    ctx_index = lax.axis_index("ctx")
    seqs = doc_lengths.shape[0]
    own_blocks = lax.dynamic_slice_in_dim(block_map, ctx_index, 1, 0)[0]
    ends = jnp.cumsum(doc_lengths)
    starts = ends - doc_lengths
    meta = jnp.concatenate([block_map.reshape(-1), starts, own_blocks])
    within = jnp.arange(half_rows, dtype=jnp.int32)
    query_place = (own_blocks[:, None] * half_rows + within[None, :]).reshape(-1)
    began = jnp.max(
        jnp.where(starts[None, :] <= query_place[:, None], starts[None, :], 0), axis=1
    )
    cosine, sine = wide_tables(query_place - began)
    latents, q_latent, q_latent_pre, latent_raw = head_layer(
        devices, tokens_in, gain_in, gain_q, gain_kv, w_qa, w_kva.T, cosine, sine, 0
    )
    queries, attn_f, heads_out, log_totals = attention_forward(
        meta, q_latent, w_qb.T, latents, w_kvb, cosine, sine, half_rows, seqs
    )
    attention, d_part, feed_part, activation, d_gate, d_up, normed_mid, d_feed = middle_layer(
        lax.axis_size("tp"), heads_out, tokens_in, cotangent, gain_mid, w_out, w_gate.T, w_up.T,
        w_down.T, 5,
    )
    gw_gate, gw_up, d_normed_mid = scatter_over_ctx(
        devices,
        [
            Scatter(devices, left=normed_mid, right=d_gate),
            Scatter(devices, left=normed_mid, right=d_up),
        ],
        1,
        lax.axis_size("tp"),
        d_part,
    )
    d_normed_mid, feed_part = lax.optimization_barrier((d_normed_mid, feed_part))
    feed_own = lax.psum_scatter(feed_part, "tp", scatter_dimension=0, tiled=True)
    own_rows = feed_own.shape[0]
    own_at = lax.axis_index("tp") * own_rows
    tokens_own = lax.dynamic_slice_in_dim(tokens_in, own_at, own_rows, 0).astype(jnp.float32)
    attention_own = lax.dynamic_slice_in_dim(attention, own_at, own_rows, 0).astype(jnp.float32)
    middle_own = tokens_own + RESIDUAL_SCALE * attention_own
    out_own = (middle_own + RESIDUAL_SCALE * feed_own.astype(jnp.float32)).astype(jnp.bfloat16)
    d_middle, d_attention, d_heads, d_gain_mid = second_norm_back(
        d_normed_mid, attention, tokens_in, cotangent, gain_mid, w_out
    )
    d_query_pre, d_latents, gw_kvb = attention_backward(
        meta, queries, log_totals, attn_f, d_heads, latents, w_kvb, cosine, sine, half_rows, seqs
    )
    (d_latent_part,) = scatter_over_ctx(devices, [Scatter(devices, given=d_latents)], 2)
    d_q_latent = dot_nt(d_query_pre, w_qb).astype(jnp.bfloat16)
    before_tp = jnp.concatenate([d_q_latent, d_latent_part.astype(jnp.bfloat16)], axis=1)
    before_tp, out_own = lax.optimization_barrier((before_tp, out_own))
    summed_tp = lax.psum(before_tp, "tp")
    gw_down, gw_out, gw_qb, gw_kvb = scatter_over_ctx(
        devices,
        [
            Scatter(devices, left=d_feed, right=activation),
            Scatter(devices, left=d_attention, right=heads_out),
            Scatter(devices, left=q_latent, right=d_query_pre),
            Scatter(devices, given=gw_kvb),
        ],
        3,
    )
    summed_tp, out_own, gw_down, gw_out, gw_qb, gw_kvb = lax.optimization_barrier(
        (summed_tp, out_own, gw_down, gw_out, gw_qb, gw_kvb)
    )
    out = lax.all_gather(out_own, "tp", axis=0, tiled=True)
    lanes = jnp.pad(summed_tp, ((0, 0), (0, -summed_tp.shape[1] % HEAD)))
    normed_in, d_q_low, d_kv_input, grad_in, d_gain_in, d_gain_q, d_gain_kv = first_norm_back(
        lanes, q_latent_pre, latent_raw, tokens_in, d_middle, gain_in, gain_q, gain_kv, w_qa,
        w_kva.T, cosine, sine,
    )
    gain_grads = (d_gain_in, d_gain_mid, d_gain_q, d_gain_kv)
    gains = jnp.concatenate([g.reshape(devices, -1) for g in gain_grads], axis=1)
    lines = -(-gains.shape[1] // (32 * HEAD)) * 32
    gains = jnp.pad(gains, ((0, 0), (0, lines * HEAD - gains.shape[1])))
    gw_qa, gw_kva, gains = scatter_over_ctx(
        devices,
        [
            Scatter(devices, left=normed_in, right=d_q_low),
            Scatter(devices, left=normed_in, right=d_kv_input),
            Scatter(devices, given=gains.astype(jnp.bfloat16).reshape(devices * lines, HEAD)),
        ],
        4,
    )
    gains = gains.reshape(-1)
    ends = [0]
    for whole in gain_grads:
        ends.append(ends[-1] + whole.size // devices)
    own_gains = [gains[first:last] for first, last in zip(ends, ends[1:])]
    return (
        out,
        grad_in,
        gw_qa,
        gw_kva,
        gw_qb,
        gw_kvb,
        gw_out,
        gw_gate,
        gw_up,
        gw_down,
        own_gains[0],
        own_gains[2],
        own_gains[3],
        own_gains[1],
    )


def solution(mesh):
    return jax.shard_map(
        on_device,
        mesh=mesh,
        in_specs=(
            P("ctx", None),
            P(),
            P(),
            P(None, "tp"),
            P(None, "tp"),
            P(None, "tp"),
            P(None, "tp"),
            P(None, "tp"),
            P(None, "tp"),
            P(),
            P(),
            P(),
            P(),
            P("ctx", None),
            P(),
            P(),
        ),
        out_specs=(
            P("ctx", None),
            P("ctx", None),
            P("ctx", None),
            P("ctx", None),
            P("ctx", "tp"),
            P("ctx", "tp"),
            P("ctx", "tp"),
            P("ctx", "tp"),
            P("ctx", "tp"),
            P("ctx", "tp"),
            P("ctx"),
            P("ctx"),
            P("ctx"),
            P("ctx"),
        ),
        check_vma=False,
    )
```

```python
import functools
import math

import jax
import jax.numpy as jnp
from jax import lax
from jax.experimental import pallas as pl
from jax.experimental.pallas import tpu as pltpu
from jax.sharding import PartitionSpec as P

KVR = 256
NOPE = 64
ROPE = 32
VDIM = 64
HEAD = NOPE + VDIM
WIDE = 2 * HEAD
MASKED = -1e30
SCORE_SCALE = (NOPE + ROPE) ** (-0.5)
EXP2_SCALE = SCORE_SCALE * math.log2(math.e)
FOLD_AT = 96
SUM_ROWS = 16
VMEM_LIMIT = 56 * 1024 * 1024

EPSILON = 1e-05
ROPE_BASE = 10000.0
RESIDUAL_SCALE = 1.4 / math.sqrt(62.0)


def dot_nn(left_op, right_op):
    return jnp.dot(left_op, right_op, preferred_element_type=jnp.float32)


def dot_nt(left_op, right_op):
    return lax.dot_general(
        left_op, right_op, (((1,), (1,)), ((), ())), preferred_element_type=jnp.float32
    )


def begin_of(place, starts):
    begin = jnp.zeros_like(place)
    for start in starts:
        begin = jnp.where(start <= place, start, begin)
    return begin


def pair_kind(key_block, query_block, starts, block_rows):
    key_first = key_block * block_rows
    query_first = query_block * block_rows
    early = begin_of(query_first, starts)
    late = begin_of(query_first + block_rows - 1, starts)
    needed = (key_block <= query_block) & (key_first + block_rows - 1 >= early)
    whole = (key_block < query_block) & (late <= key_first)
    return needed, whole


def mask_bias(key_block, query_block, starts, block_rows, keys_first):
    key_dim = 0 if keys_first else 1
    shape = (block_rows, block_rows)
    key_place = key_block * block_rows + lax.broadcasted_iota(jnp.int32, shape, key_dim)
    query_place = query_block * block_rows + lax.broadcasted_iota(jnp.int32, shape, 1 - key_dim)
    begin = jnp.zeros(shape, jnp.int32)
    for start in starts:
        begin = jnp.where(start <= query_place, start, begin)
    allowed = (key_place <= query_place) & (key_place >= begin)
    return jnp.where(allowed, 0.0, MASKED)


def shared_key_tile(rope_rows, block_rows):
    place = lax.broadcasted_iota(jnp.int32, (ROPE, HEAD), 0)
    lane = lax.broadcasted_iota(jnp.int32, (ROPE, HEAD), 1)
    eye = jnp.where(place == lane, 1.0, 0.0).astype(jnp.bfloat16)
    tile = dot_nn(rope_rows, eye)
    lanes = lax.broadcasted_iota(jnp.int32, (block_rows, HEAD), 1)
    ones = (lanes >= FOLD_AT) & (lanes < FOLD_AT + 3)
    return jnp.where(ones, 1.0, tile).astype(jnp.bfloat16)


def head_window(h):
    at = h * (NOPE + ROPE)
    return at // HEAD * HEAD, at % HEAD


def window_columns(heads):
    return head_window(heads - 1)[0] + WIDE


def head_groups(heads):
    return [(h, min(h + 2, heads)) for h in range(0, heads, 2)]


def forward_kernel(
    blocks, heads, seqs, meta, cq, wqb, lat, wkvb, cos, sin, qx, o_out, ob_out, u_out,
    wkvt, xs, xr, vt, top, acc, bias, pre, s_ref, p_ref,
):
    rows_all = cq.shape[0]
    block_rows = bias.shape[0]
    q_blocks = rows_all // block_rows
    starts = [meta[blocks + s] for s in range(seqs)]
    own = [meta[blocks + seqs + j] for j in range(q_blocks)]
    for first, last in head_groups(heads):
        wkvt[first * HEAD : last * HEAD, :] = (
            wkvb[:, first * HEAD : last * HEAD].astype(jnp.float32).T.astype(jnp.bfloat16)
        )
    lane = lax.broadcasted_iota(jnp.int32, (block_rows, HEAD), 1)
    for j in range(q_blocks):
        here = pl.ds(j * block_rows, block_rows)
        cos_j, sin_j = cos[here, :], sin[here, :]
        width = heads * (NOPE + ROPE)
        for at in range(0, width, WIDE):
            end = min(at + WIDE, width)
            pre[:, at:end] = dot_nt(cq[here, :], wqb[at:end, :])
        for h in range(heads):
            at, shift = head_window(h)
            own_part = pltpu.roll(pre[:, at : at + WIDE], (WIDE - shift) % WIDE, 1)[:, :HEAD]
            turned = pltpu.roll(own_part, NOPE, 1)
            left = pltpu.roll(turned, HEAD - ROPE // 2, 1)
            right = pltpu.roll(turned, ROPE // 2, 1)
            swapped = jnp.where(lane < ROPE // 2, -left, right)
            rope = jnp.where(lane < ROPE, turned * cos_j + swapped * sin_j, 0.0)
            qx[j, h, :, :HEAD] = jnp.where(lane < NOPE, own_part, 0.0).astype(jnp.bfloat16)
            qx[j, h, :, HEAD:] = rope.astype(jnp.bfloat16)
    top[...] = jnp.full(top.shape, MASKED, jnp.float32)
    vt[:, VDIM:, :] = jnp.ones((heads, SUM_ROWS, block_rows), jnp.bfloat16)
    acc[...] = jnp.zeros(acc.shape, jnp.float32)

    def pair(j, masked):
        def one(h):
            keys = jnp.concatenate([xs[h], xr[...]], axis=1)
            s_ref[h % 3] = dot_nt(keys, qx[j, h])

        def weigh(h):
            old = top[j, h]
            new = old
            for k in range(0, block_rows, 128):
                part = s_ref[h % 3, k : k + 128, :]
                if masked:
                    part = part + bias[k : k + 128, :]
                    s_ref[h % 3, k : k + 128, :] = part
                new = jnp.maximum(new, jnp.max(part, axis=0, keepdims=True))
            fade = jnp.exp2((old - new) * EXP2_SCALE)
            top[j, h] = new
            for k in range(0, block_rows, 128):
                terms = jnp.exp2((s_ref[h % 3, k : k + 128, :] - new) * EXP2_SCALE)
                p_ref[h % 3, k : k + 128, :] = terms.astype(jnp.bfloat16)
            return fade

        def add(h, fade):
            acc[j, h] = fade * acc[j, h] + dot_nn(vt[h], p_ref[h % 3])

        one(0)
        if heads > 1:
            one(1)
        fades = {}
        for h in range(heads):
            if h + 2 < heads:
                one(h + 2)
            fades[h] = weigh(h)
            if h > 1:
                add(h - 2, fades[h - 2])
        for h in range(max(heads - 2, 0), heads):
            add(h, fades[h])

    def step(r, carry):
        key_block = meta[r]
        kinds = [pair_kind(key_block, own[j], starts, block_rows) for j in range(q_blocks)]
        wanted = functools.reduce(jnp.logical_or, [k[0] for k in kinds])

        @pl.when(wanted)
        def _():
            here = pl.ds(pl.multiple_of(r * block_rows, block_rows), block_rows)
            latent = lat[here, :KVR]
            xr[...] = shared_key_tile(lat[here, KVR : KVR + ROPE], block_rows)
            for first, last in head_groups(heads):
                keys = dot_nn(latent, wkvb[:, first * HEAD : last * HEAD]).astype(jnp.bfloat16)
                values = dot_nt(wkvt[first * HEAD : last * HEAD, :], latent).astype(jnp.bfloat16)
                for h in range(first, last):
                    at = (h - first) * HEAD
                    xs[h] = keys[:, at : at + HEAD]
                    vt[h, :VDIM, :] = values[at + NOPE : at + HEAD, :]

        for j in range(q_blocks):
            needed, whole = kinds[j]

            @pl.when(needed & whole)
            def _():
                pair(j, False)

            @pl.when(needed & jnp.logical_not(whole))
            def _():
                bias[...] = mask_bias(key_block, own[j], starts, block_rows, True)
                pair(j, True)

        return carry

    lax.fori_loop(0, blocks, step, 0)
    for j in range(q_blocks):
        here = pl.ds(j * block_rows, block_rows)
        for first, last in head_groups(heads):
            parts = []
            for h in range(first, last):
                total = acc[j, h, VDIM : VDIM + 1, :]
                parts.append(acc[j, h, :VDIM, :] * (1.0 / total))
                u_out[j, h : h + 1, :] = top[j, h] + jnp.log2(total) * (1.0 / EXP2_SCALE)
            if len(parts) == 1:
                parts.append(jnp.zeros_like(parts[0]))
            both = jnp.concatenate(parts, axis=0).T
            width = (last - first) * VDIM
            o_out[here, first * VDIM : first * VDIM + width] = both[:, :width]
            ob_out[here, first * VDIM : first * VDIM + width] = both[:, :width].astype(jnp.bfloat16)


def attention_forward(meta, cq, wqb, lat, wkvb, cos, sin, block_rows, seqs):
    heads = wkvb.shape[1] // HEAD
    blocks = lat.shape[0] // block_rows
    rows = cq.shape[0]
    q_blocks = rows // block_rows
    vmem = pl.BlockSpec(memory_space=pltpu.VMEM)
    pairs = q_blocks * blocks * heads // 2
    return pl.pallas_call(
        functools.partial(forward_kernel, blocks, heads, seqs),
        out_shape=(
            jax.ShapeDtypeStruct((q_blocks, heads, block_rows, WIDE), jnp.bfloat16),
            jax.ShapeDtypeStruct((rows, heads * VDIM), jnp.float32),
            jax.ShapeDtypeStruct((rows, heads * VDIM), jnp.bfloat16),
            jax.ShapeDtypeStruct((q_blocks, 16 * -(-heads // 16), block_rows), jnp.float32),
        ),
        in_specs=[pl.BlockSpec(memory_space=pltpu.SMEM)] + [vmem] * 6,
        out_specs=(vmem,) * 4,
        scratch_shapes=[
            pltpu.VMEM((heads * HEAD, KVR), jnp.bfloat16),
            pltpu.VMEM((heads, block_rows, HEAD), jnp.bfloat16),
            pltpu.VMEM((block_rows, HEAD), jnp.bfloat16),
            pltpu.VMEM((heads, VDIM + SUM_ROWS, block_rows), jnp.bfloat16),
            pltpu.VMEM((q_blocks, heads, 1, block_rows), jnp.float32),
            pltpu.VMEM((q_blocks, heads, VDIM + SUM_ROWS, block_rows), jnp.float32),
            pltpu.VMEM((block_rows, block_rows), jnp.float32),
            pltpu.VMEM((block_rows, window_columns(heads)), jnp.float32),
            pltpu.VMEM((3, block_rows, block_rows), jnp.float32),
            pltpu.VMEM((3, block_rows, block_rows), jnp.bfloat16),
        ],
        compiler_params=pltpu.CompilerParams(vmem_limit_bytes=VMEM_LIMIT),
        cost_estimate=pl.CostEstimate(
            flops=pairs * 4 * block_rows * block_rows * WIDE,
            bytes_accessed=16 * 1024 * 1024,
            transcendentals=pairs * block_rows * block_rows,
        ),
        name="attention_forward",
    )(meta, cq, wqb, lat, wkvb, cos, sin)


def three_terms(column):
    first = column.astype(jnp.bfloat16).astype(jnp.float32)
    rest = column - first
    second = rest.astype(jnp.bfloat16).astype(jnp.float32)
    return first, second, rest - second


def fold_in(tile, column, lane):
    for k, term in enumerate(three_terms(column)):
        tile = jnp.where(lane == FOLD_AT + k, term, tile)
    return tile


def backward_kernel(
    blocks, heads, seqs, meta, qx, u_in, o_in, dob, lat, wkvb, cos, sin, dq_out, dlat, gkvb,
    xs, xr, qo, qt, dt, dq, dkv, dkpe, gsum, bias, flat, s_ref, p_ref, d_ref,
):
    block_rows = bias.shape[0]
    q_blocks = qx.shape[0]
    starts = [meta[blocks + s] for s in range(seqs)]
    own = [meta[blocks + seqs + j] for j in range(q_blocks)]
    lane = lax.broadcasted_iota(jnp.int32, (block_rows, HEAD), 1)
    for j in range(q_blocks):
        here = pl.ds(j * block_rows, block_rows)
        logs = u_in[j].T
        for first, last in head_groups(heads):
            d_pair = dob[here, first * VDIM : first * VDIM + HEAD].astype(jnp.float32)
            weighted = d_pair * o_in[here, first * VDIM : first * VDIM + HEAD]
            turned = pltpu.roll(d_pair, VDIM, 1)
            for h in range(first, last):
                mine = lane < VDIM if h == first else lane >= VDIM
                delta = jnp.sum(jnp.where(mine, weighted, 0.0), axis=1, keepdims=True)
                d_head = jnp.where(lane >= VDIM, turned if h == first else d_pair, 0.0)
                q_first = qx[j, h, :, :HEAD].astype(jnp.float32)
                q_second = qx[j, h, :, HEAD:].astype(jnp.float32)
                qo[j, h, :block_rows, :HEAD] = qx[j, h, :, :HEAD]
                qo[j, h, :block_rows, HEAD:] = fold_in(q_second, -logs[:, h : h + 1], lane).astype(
                    jnp.bfloat16
                )
                qo[j, h, block_rows:, :HEAD] = d_head.astype(jnp.bfloat16)
                qo[j, h, block_rows:, HEAD:] = fold_in(
                    jnp.zeros((block_rows, HEAD), jnp.float32), -delta, lane
                ).astype(jnp.bfloat16)
                qt[j, h, :NOPE, :] = q_first.T[:NOPE, :].astype(jnp.bfloat16)
                qt[j, h, NOPE:, :] = q_second.T[:ROPE, :].astype(jnp.bfloat16)
                dt[j, h] = d_head.T[VDIM:, :].astype(jnp.bfloat16)
    dq[...] = jnp.zeros(dq.shape, jnp.float32)
    gsum[...] = jnp.zeros(gsum.shape, jnp.float32)

    def pair(j, masked):
        def raw(h):
            keys = jnp.concatenate([xs[h], xr[...]], axis=1)
            s_ref[h % 2] = dot_nt(qo[j, h], keys)

        def weigh(h):
            for k in range(0, block_rows, 128):
                scores = s_ref[h % 2, k : k + 128, :] * EXP2_SCALE
                if masked:
                    scores = scores + bias[k : k + 128, :]
                probs = jnp.exp2(scores)
                p_ref[h % 2, k : k + 128, :] = probs.astype(jnp.bfloat16)
                d_ref[h % 2, k : k + 128, :] = (
                    probs * s_ref[h % 2, block_rows + k : block_rows + k + 128, :]
                ).astype(jnp.bfloat16)

        def add(h):
            keys = jnp.concatenate([xs[h], xr[...]], axis=1)
            d_scores = d_ref[h % 2]
            dq[j, h] += dot_nn(d_scores, keys)
            d_keys = dot_nn(qt[j, h], d_scores)
            dkv[h, :NOPE, :] += d_keys[:NOPE]
            dkpe[...] += d_keys[NOPE:]
            dkv[h, NOPE:, :] += dot_nn(dt[j, h], p_ref[h % 2])

        raw(0)
        for h in range(heads):
            if h + 1 < heads:
                raw(h + 1)
            weigh(h)
            if h:
                add(h - 1)
        add(heads - 1)

    def step(r, carry):
        key_block = meta[r]
        kinds = [pair_kind(key_block, own[j], starts, block_rows) for j in range(q_blocks)]
        wanted = functools.reduce(jnp.logical_or, [k[0] for k in kinds])
        here = pl.ds(pl.multiple_of(r * block_rows, block_rows), block_rows)

        @pl.when(wanted)
        def _():
            latent = lat[here, :KVR]
            xr[...] = shared_key_tile(lat[here, KVR : KVR + ROPE], block_rows)
            for first, last in head_groups(heads):
                keys = dot_nn(latent, wkvb[:, first * HEAD : last * HEAD]).astype(jnp.bfloat16)
                for h in range(first, last):
                    xs[h] = keys[:, (h - first) * HEAD : (h - first + 1) * HEAD]
            dkv[...] = jnp.zeros(dkv.shape, jnp.float32)
            dkpe[...] = jnp.zeros(dkpe.shape, jnp.float32)

        for j in range(q_blocks):
            needed, whole = kinds[j]

            @pl.when(needed & whole)
            def _():
                pair(j, False)

            @pl.when(needed & jnp.logical_not(whole))
            def _():
                bias[...] = mask_bias(key_block, own[j], starts, block_rows, False)
                pair(j, True)

        @pl.when(wanted)
        def _():
            latent = lat[here, :KVR]
            d_latent = jnp.zeros((KVR, block_rows), jnp.float32)
            for h in range(heads):
                d_head = jnp.concatenate(
                    [dkv[h, :NOPE, :] * SCORE_SCALE, dkv[h, NOPE:, :]], axis=0
                ).astype(jnp.bfloat16)
                d_latent += dot_nn(wkvb[:, h * HEAD : (h + 1) * HEAD], d_head)
                gsum[h * HEAD : (h + 1) * HEAD, :] += dot_nn(d_head, latent)
            dlat[here, :KVR] = d_latent.T.astype(jnp.bfloat16)
            rope = jnp.concatenate(
                [dkpe[...] * SCORE_SCALE, jnp.zeros((HEAD - ROPE, block_rows), jnp.float32)], axis=0
            )
            dlat[here, KVR:] = rope.T[:, :ROPE].astype(jnp.bfloat16)

        @pl.when(jnp.logical_not(wanted))
        def _():
            dlat[here, :] = jnp.zeros((block_rows, KVR + ROPE), jnp.bfloat16)

        return carry

    lax.fori_loop(0, blocks, step, 0)
    for h in range(heads):
        gkvb[:, h * HEAD : (h + 1) * HEAD] = gsum[h * HEAD : (h + 1) * HEAD, :].T.astype(
            jnp.bfloat16
        )
    for j in range(q_blocks):
        here = pl.ds(j * block_rows, block_rows)
        cos_j, sin_j = cos[here, :], sin[here, :]
        flat[...] = jnp.zeros(flat.shape, jnp.float32)
        for h in range(heads):
            nope = jnp.where(lane < NOPE, dq[j, h, :, :HEAD], 0.0)
            rope = dq[j, h, :, HEAD:]
            shifted = rope * sin_j
            left = pltpu.roll(shifted, HEAD - ROPE // 2, 1)
            right = pltpu.roll(shifted, ROPE // 2, 1)
            swapped = jnp.where(lane < ROPE // 2, left, jnp.where(lane < ROPE, -right, 0.0))
            back = pltpu.roll(jnp.where(lane < ROPE, rope * cos_j + swapped, 0.0), NOPE, 1)
            whole = jnp.concatenate([(nope + back) * SCORE_SCALE, jnp.zeros_like(nope)], axis=1)
            at, shift = head_window(h)
            flat[:, at : at + WIDE] += pltpu.roll(whole, shift, 1)
        dq_out[here, :] = flat[:, : heads * (NOPE + ROPE)].astype(jnp.bfloat16)


def attention_backward(meta, qx, u_in, o_in, dob, lat, wkvb, cos, sin, block_rows, seqs):
    heads = wkvb.shape[1] // HEAD
    blocks = lat.shape[0] // block_rows
    q_blocks = qx.shape[0]
    rows = q_blocks * block_rows
    odd = -(heads * VDIM) % HEAD
    if odd:
        o_in = jnp.pad(o_in, ((0, 0), (0, odd)))
        dob = jnp.pad(dob, ((0, 0), (0, odd)))
    vmem = pl.BlockSpec(memory_space=pltpu.VMEM)
    pairs = q_blocks * blocks * heads // 2
    return pl.pallas_call(
        functools.partial(backward_kernel, blocks, heads, seqs),
        out_shape=(
            jax.ShapeDtypeStruct((rows, heads * (NOPE + ROPE)), jnp.bfloat16),
            jax.ShapeDtypeStruct((lat.shape[0], KVR + ROPE), jnp.bfloat16),
            jax.ShapeDtypeStruct((KVR, heads * HEAD), jnp.bfloat16),
        ),
        in_specs=[pl.BlockSpec(memory_space=pltpu.SMEM)] + [vmem] * 8,
        out_specs=(vmem,) * 3,
        scratch_shapes=[
            pltpu.VMEM((heads, block_rows, HEAD), jnp.bfloat16),
            pltpu.VMEM((block_rows, HEAD), jnp.bfloat16),
            pltpu.VMEM((q_blocks, heads, 2 * block_rows, WIDE), jnp.bfloat16),
            pltpu.VMEM((q_blocks, heads, NOPE + ROPE, block_rows), jnp.bfloat16),
            pltpu.VMEM((q_blocks, heads, VDIM, block_rows), jnp.bfloat16),
            pltpu.VMEM((q_blocks, heads, block_rows, WIDE), jnp.float32),
            pltpu.VMEM((heads, HEAD, block_rows), jnp.float32),
            pltpu.VMEM((ROPE, block_rows), jnp.float32),
            pltpu.VMEM((heads * HEAD, KVR), jnp.float32),
            pltpu.VMEM((block_rows, block_rows), jnp.float32),
            pltpu.VMEM((block_rows, window_columns(heads)), jnp.float32),
            pltpu.VMEM((2, 2 * block_rows, block_rows), jnp.float32),
            pltpu.VMEM((2, block_rows, block_rows), jnp.bfloat16),
            pltpu.VMEM((2, block_rows, block_rows), jnp.bfloat16),
        ],
        compiler_params=pltpu.CompilerParams(vmem_limit_bytes=VMEM_LIMIT),
        cost_estimate=pl.CostEstimate(
            flops=pairs * 8 * block_rows * block_rows * WIDE,
            bytes_accessed=24 * 1024 * 1024,
            transcendentals=pairs * block_rows * block_rows,
        ),
        name="attention_backward",
    )(meta, qx, u_in, o_in, dob, lat, wkvb, cos, sin)


MESH = pl.DeviceIdType.MESH


class LineSum:
    def __init__(self, n, own, landing, total, sems, lag):
        self.n, self.own, self.landing, self.total, self.lag = n, own, landing, total, lag
        self.up_send, self.up_land, self.down_send, self.back_send, self.down_land = sems
        self.me = lax.axis_index("tp")
        self.root = (n - 1) // 2
        self.chunks = own.shape[0]
        self.has_left, self.has_right = self.me > 0, self.me < n - 1
        self.root_lag = (n - 1 - self.root) * lag
        self.land_lag = 2 * self.root_lag
        self.ticks = self.chunks + self.land_lag

    def greet(self, barrier):
        me = self.me
        for there, other in ((self.has_left, me - 1), (self.has_right, me + 1)):

            @pl.when(there)
            def _(other=other):
                pl.semaphore_signal(barrier, inc=1, device_id={"tp": other}, device_id_type=MESH)

    def wait_greetings(self, barrier, others):
        both = self.has_left & self.has_right

        @pl.when(both)
        def _():
            pl.semaphore_wait(barrier, 2 + others)

        @pl.when(jnp.logical_not(both))
        def _():
            pl.semaphore_wait(barrier, 1 + others)

    def copy_to(self, source, target, send, land, c, other):
        return pltpu.make_async_remote_copy(
            src_ref=source.at[c],
            dst_ref=target.at[c],
            send_sem=send.at[c],
            recv_sem=land.at[c],
            device_id={"tp": other},
            device_id_type=MESH,
        )

    def rise_left(self, c):
        return self.copy_to(self.own, self.landing, self.up_send, self.up_land, c, self.me + 1)

    def rise_right(self, c):
        return self.copy_to(self.own, self.landing, self.up_send, self.up_land, c, self.me - 1)

    def rise_last(self, c):
        return self.copy_to(self.own, self.total, self.up_send, self.down_land, c, self.me - 1)

    def fall_right(self, c):
        return self.copy_to(self.total, self.total, self.down_send, self.down_land, c, self.me + 1)

    def fall_left(self, c):
        return self.copy_to(self.total, self.total, self.back_send, self.down_land, c, self.me - 1)

    def rise(self, c):
        me, root = self.me, self.root
        rises = [(me == root + 1, self.rise_last)]
        if root:
            rises.append((me < root, self.rise_left))
        if self.n - 1 > root + 1:
            rises.append((me > root + 1, self.rise_right))
        for who, copy in rises:

            @pl.when(who)
            def _(copy=copy):
                copy(c).start()

    def inside(self, c):
        return (c >= 0) & (c < self.chunks)

    def added(self, refs, c):
        sums = refs[0][c].astype(jnp.float32)
        for ref in refs[1:]:
            sums = sums + ref[c].astype(jnp.float32)
        return sums.astype(self.total.dtype)

    def leaf(self, c):
        is_leaf = self.me == self.n - 1
        if self.root:
            is_leaf = is_leaf | (self.me == 0)

        @pl.when(is_leaf & self.inside(c))
        def _():
            self.rise(c)

    def leaves(self):
        def body(c, carry):
            self.leaf(c)
            return carry

        lax.fori_loop(0, self.chunks, body, 0)

    def pump(self, first, last):
        def body(t, carry):
            self.duty(t)
            return carry

        lax.fori_loop(first, last, body, 0)

    def duty(self, t):
        me, root = self.me, self.root
        if self.n > 3:
            c = t - self.lag * jnp.where(me < root, me, self.n - 1 - me)

            @pl.when((me != root) & self.has_left & self.has_right & self.inside(c))
            def _():
                self.rise_right(c).wait_recv()
                self.own[c] = self.added([self.own, self.landing], c)
                self.rise(c)

        c_root = t - self.root_lag

        @pl.when((me == root) & self.inside(c_root))
        def _():
            if root:
                self.rise_left(c_root).wait_recv()
            self.fall_right(c_root).wait_recv()
            terms = [self.own, self.landing, self.total] if root else [self.own, self.total]
            self.total[c_root] = self.added(terms, c_root)
            self.fall_right(c_root).start()
            if root:
                self.fall_left(c_root).start()

        c_fall = t - self.root_lag - self.lag * jnp.where(me < root, root - me, me - root)

        @pl.when((me != root) & self.inside(c_fall))
        def _():
            self.fall_right(c_fall).wait_recv()

            @pl.when((me > root) & self.has_right)
            def _():
                self.fall_right(c_fall).start()

            @pl.when((me < root) & self.has_left)
            def _():
                self.fall_left(c_fall).start()

    def landed(self, t):
        return t - self.land_lag

    def drain(self):
        me = self.me

        def body(c, carry):
            @pl.when(me != self.root)
            def _():
                self.rise_right(c).wait_send()

            @pl.when((me >= self.root) & self.has_right)
            def _():
                self.fall_right(c).wait_send()

            @pl.when((me <= self.root) & self.has_left)
            def _():
                self.fall_left(c).wait_send()

            return carry

        lax.fori_loop(0, self.chunks, body, 0)


def line_sems(chunks):
    return [pltpu.SemaphoreType.DMA((chunks,))] * 5


def scatter_blocks(bits_left):
    chips = []
    for value in range(1 << len(bits_left)):
        chip = 0
        for at, bit in enumerate(bits_left):
            chip = chip + (((value >> at) & 1) << (bit - 1))
        chips.append(chip)
    return chips


class Scatter:
    def __init__(self, n, rows, columns, is_given):
        self.n, self.rows, self.columns, self.is_given = n, rows, columns, is_given
        self.count = n.bit_length() - 1
        self.parts = 2 if rows % 32 == 0 else 1

    def scratch(self):
        n, count = self.n, self.count
        half = jnp.bfloat16
        dma = pltpu.SemaphoreType.DMA
        shapes = [pltpu.VMEM((n // 2, self.rows, self.columns), half)]
        if not self.is_given:
            shapes.append(pltpu.VMEM((n // 2, self.rows, self.columns), half))
        for step in range(count - 1):
            shapes.append(pltpu.VMEM((n >> (step + 2), self.rows, self.columns), half))
        shapes += [dma((n // 2,))] * 2
        for step in range(count - 1):
            shapes += [dma((2, n >> (step + 2)))] * 2
        return shapes

    def bind(self, take, source, emit):
        self.held = take(1)[0]
        self.sent = None if self.is_given else take(1)[0]
        self.landed = take(self.count - 1)
        self.core_sems = take(2)
        self.step_sems = [take(2) for _ in range(self.count - 1)]
        self.source, self.emit = source, emit
        self.me = lax.axis_index("ctx")
        self.core = self.me & 1
        self.chips = self.n // 2
        self.orders = (tuple(range(1, self.count)), tuple(range(self.count - 1, 0, -1)))
        self.tiles = [(c, min(c + 512, self.columns)) for c in range(0, self.columns, 512)]
        return self

    def own(self, dest, first, last):
        at = pl.ds(pl.multiple_of(dest * self.rows, 16), self.rows)
        if self.is_given:
            return self.source[at, first:last].astype(jnp.float32)
        return dot_nn(self.source[0][at, :], self.source[1][:, first:last])

    def core_copy(self, chip):
        if self.is_given:
            at = pl.ds(pl.multiple_of((2 * chip + 1 - self.core) * self.rows, 16), self.rows)
            source = self.source.at[at, :]
        else:
            source = self.sent.at[chip]
        return pltpu.make_async_remote_copy(
            src_ref=source,
            dst_ref=self.held.at[chip],
            send_sem=self.core_sems[0].at[chip],
            recv_sem=self.core_sems[1].at[chip],
            device_id={"ctx": self.me ^ 1},
            device_id_type=MESH,
        )

    def step_copies(self, step):
        half = self.rows // self.parts
        me = self.me
        copies = []
        for part, order in enumerate(self.orders[: self.parts]):
            bit = order[step]
            at = pl.ds(part * half, half)
            for slot, free in enumerate(scatter_blocks(sorted(order[step + 1 :]))):
                keep = free + ((me >> bit) & 1) * (1 << (bit - 1))
                send = free + (1 - ((me >> bit) & 1)) * (1 << (bit - 1))
                for b in order[:step]:
                    own = ((me >> b) & 1) * (1 << (b - 1))
                    keep, send = keep + own, send + own
                copy = pltpu.make_async_remote_copy(
                    src_ref=self.held.at[send, at, :],
                    dst_ref=self.landed[step].at[slot, at, :],
                    send_sem=self.step_sems[step][0].at[part, slot],
                    recv_sem=self.step_sems[step][1].at[part, slot],
                    device_id={"ctx": me ^ (1 << bit)},
                    device_id_type=MESH,
                )
                copies.append((copy, keep, slot, at))
        return copies

    def start_core(self, also=None):
        def body(chip, carry):
            if also is not None:
                also(chip)
            if not self.is_given:
                for first, last in self.tiles:
                    self.sent[chip, :, first:last] = self.own(
                        2 * chip + 1 - self.core, first, last
                    ).astype(jnp.bfloat16)
            self.core_copy(chip).start()
            return carry

        lax.fori_loop(0, self.chips, body, 0)

    def finish_core(self, also=None):
        def body(chip, carry):
            if also is not None:
                also(chip)
            self.core_copy(chip).wait_recv()
            for first, last in self.tiles:
                total = self.own(2 * chip + self.core, first, last)
                total = total + self.held[chip, :, first:last].astype(jnp.float32)
                self.held[chip, :, first:last] = total.astype(jnp.bfloat16)
            return carry

        lax.fori_loop(0, self.chips, body, 0)

    def start_step(self, step):
        for copy, _, _, _ in self.step_copies(step):
            copy.start()

    def finish_step(self, step):
        for copy, keep, slot, at in self.step_copies(step):
            copy.wait_recv()
            for first, last in self.tiles:
                total = self.held[keep, at, first:last].astype(jnp.float32)
                total = total + self.landed[step][slot, at, first:last].astype(jnp.float32)
                if step == self.count - 2:
                    self.emit(at, first, last, total)
                else:
                    self.held[keep, at, first:last] = total.astype(jnp.bfloat16)
        if step + 1 < self.count - 1:
            self.start_step(step + 1)

    def drain(self):
        def body(chip, carry):
            self.core_copy(chip).wait_send()
            return carry

        lax.fori_loop(0, self.chips, body, 0)
        for step in range(self.count - 1):
            for copy, _, _, _ in self.step_copies(step):
                copy.wait_send()


def taker(refs):
    refs = list(refs)

    def take(k):
        taken = refs[:k]
        del refs[:k]
        return taken

    return take


def store_in(ref):
    def emit(at, first, last, total):
        ref[at, first:last] = total.astype(ref.dtype)

    return emit


def turn(source, target):
    def body(c, carry):
        at = pl.ds(pl.multiple_of(c * 128, 128), 128)
        target[at, :] = source[:, at].astype(jnp.float32).T.astype(jnp.bfloat16)
        return carry

    lax.fori_loop(0, source.shape[1] // 128, body, 0)


def greet_ctx(n, barrier):
    me = lax.axis_index("ctx")
    count = n.bit_length() - 1
    for bit in range(count):
        pl.semaphore_signal(barrier, inc=1, device_id={"ctx": me ^ (1 << bit)}, device_id_type=MESH)
    return count


def spread(waits, ticks):
    portion = -(-ticks // waits)
    return [(min(k * portion, ticks), min((k + 1) * portion, ticks)) for k in range(waits)]


def gate_up_kernel(n, tp, plans, normed, d_gate, d_up, terms, gate_out, up_out, sums, *refs):
    take = taker(refs)
    own, landing, normed_t = take(3)
    line = LineSum(tp, own, landing, sums, take(5), LAG)
    gate = plans[0].bind(take, (normed_t, d_gate), store_in(gate_out))
    up = plans[1].bind(take, (normed_t, d_up), store_in(up_out))
    barrier = pltpu.get_barrier_semaphore()
    others = greet_ctx(n, barrier)
    line.greet(barrier)
    own[...] = terms[...]
    line.wait_greetings(barrier, others)
    line.leaves()
    turn(normed, normed_t)
    chips = n // 2
    gate.start_core()
    up.start_core(line.duty)
    gate.finish_core(lambda chip: line.duty(chips + chip))
    gate.start_step(0)
    up.finish_core(lambda chip: line.duty(2 * chips + chip))
    up.start_step(0)
    steps = [(item, step) for step in range(gate.count - 1) for item in (gate, up)]
    done = 3 * chips
    for (item, step), (first, last) in zip(steps, spread(len(steps), line.ticks - done)):
        line.pump(done + first, done + last)
        item.finish_step(step)
    for item in (gate, up, line):
        item.drain()


def gate_up_grads(n, tp, normed, d_gate, d_up, terms, collective_id):
    rows, width = normed.shape
    hidden = d_gate.shape[1]
    vmem = pl.BlockSpec(memory_space=pltpu.VMEM)
    half = jnp.bfloat16
    plans = [Scatter(n, width // n, hidden, False) for _ in range(2)]
    chunked = (rows // CHUNK, CHUNK, width)
    gate, up, sums = pl.pallas_call(
        functools.partial(gate_up_kernel, n, tp, plans),
        out_shape=(
            jax.ShapeDtypeStruct((width // n, hidden), half),
            jax.ShapeDtypeStruct((width // n, hidden), half),
            jax.ShapeDtypeStruct(chunked, half),
        ),
        in_specs=[vmem] * 4,
        out_specs=(vmem,) * 3,
        scratch_shapes=[
            pltpu.VMEM(chunked, half),
            pltpu.VMEM(chunked, half),
            pltpu.VMEM((width, rows), half),
            *line_sems(rows // CHUNK),
            *plans[0].scratch(),
            *plans[1].scratch(),
        ],
        compiler_params=pltpu.CompilerParams(
            vmem_limit_bytes=MIDDLE_VMEM, collective_id=collective_id, has_side_effects=True
        ),
        cost_estimate=pl.CostEstimate(
            flops=4 * rows * width * hidden, bytes_accessed=16 * 1024 * 1024, transcendentals=0
        ),
        name=f"gate_up_grads_{collective_id}",
    )(normed, d_gate, d_up, terms.reshape(chunked))
    return gate, up, sums.reshape(rows, width)


TAIL_CHUNK = 64


def up_tail_kernel(
    n, tp, plans, d_lat, d_query, w_qb, g_kvb, d_attn, ob, q_latent, d_feed, act,
    sum_q, sum_lat, down_out, out_out, qb_out, kvb_out, *refs,
):
    take = taker(refs)
    own_q, land_q, own_lat, land_lat, d_attn_t, q_latent_t, d_feed_t = take(7)
    line_q = LineSum(tp, own_q, land_q, sum_q, take(5), LAG)
    line_lat = LineSum(tp, own_lat, land_lat, sum_lat, take(5), LAG)
    chunk = own_q.shape[1]

    def store_lat(at, first, last, total):
        for k in range(at.size // chunk):
            own_lat[at.start // chunk + k, :, first:last] = total[
                k * chunk : (k + 1) * chunk
            ].astype(jnp.bfloat16)

    lat, down, out, qb, kvb = plans
    lat.bind(take, d_lat, store_lat)
    down.bind(take, (d_feed_t, act), store_in(down_out))
    out.bind(take, (d_attn_t, ob), store_in(out_out))
    qb.bind(take, (q_latent_t, d_query), store_in(qb_out))
    kvb.bind(take, g_kvb, store_in(kvb_out))
    barrier = pltpu.get_barrier_semaphore()
    others = greet_ctx(n, barrier)
    line_q.greet(barrier)
    line_q.wait_greetings(barrier, others)
    lat.start_core()

    def query(c, carry):
        rows = pl.ds(pl.multiple_of(c * 2 * chunk, 2 * chunk), 2 * chunk)
        part = dot_nn(d_query[rows, :], w_qb[...]).astype(jnp.bfloat16)
        for k in range(2):
            own_q[2 * c + k] = part[k * chunk : (k + 1) * chunk]
            line_q.leaf(2 * c + k)
        return carry

    lax.fori_loop(0, own_q.shape[0] // 2, query, 0)
    lat.finish_core()
    lat.start_step(0)
    turn(d_attn, d_attn_t)
    line_q.pump(0, 3)
    out.start_core()
    line_q.pump(3, 6)
    for step in range(lat.count - 1):
        lat.finish_step(step)
    out.finish_core()
    out.start_step(0)
    line_lat.leaves()
    lat_ticks = spread(6, line_lat.ticks)
    q_ticks = [(6 + a, 6 + b) for a, b in spread(3, line_q.ticks - 6)]
    turn(d_feed, d_feed_t)
    line_q.pump(*q_ticks[0])
    down.start_core()
    line_lat.pump(*lat_ticks[0])
    line_q.pump(*q_ticks[1])
    down.finish_core()
    down.start_step(0)
    line_lat.pump(*lat_ticks[1])
    line_q.pump(*q_ticks[2])
    kvb.start_core()
    turn(q_latent, q_latent_t)
    qb.start_core()
    line_lat.pump(*lat_ticks[2])
    kvb.finish_core()
    kvb.start_step(0)
    qb.finish_core()
    qb.start_step(0)
    line_lat.pump(*lat_ticks[3])
    out.finish_step(0)
    line_lat.pump(*lat_ticks[4])
    down.finish_step(0)
    line_lat.pump(*lat_ticks[5])
    kvb.finish_step(0)
    qb.finish_step(0)
    for step in range(1, lat.count - 1):
        for item in (out, down, kvb, qb):
            item.finish_step(step)
    for item in (*plans, line_q, line_lat):
        item.drain()


def up_tail(n, tp, d_lat, d_query, w_qb, g_kvb, d_attn, ob, q_latent, d_feed, act, collective_id):
    rows, width = d_attn.shape
    rank = q_latent.shape[1]
    hidden = act.shape[1]
    lat_width = d_lat.shape[1]
    vmem = pl.BlockSpec(memory_space=pltpu.VMEM)
    half = jnp.bfloat16
    plans = [
        Scatter(n, rows, lat_width, True),
        Scatter(n, width // n, hidden, False),
        Scatter(n, width // n, ob.shape[1], False),
        Scatter(n, rank // n, d_query.shape[1], False),
        Scatter(n, KVR // n, g_kvb.shape[1], True),
    ]
    q_shape = (rows // TAIL_CHUNK, TAIL_CHUNK, rank)
    lat_shape = (rows // TAIL_CHUNK, TAIL_CHUNK, lat_width)
    sum_q, sum_lat, *grads = pl.pallas_call(
        functools.partial(up_tail_kernel, n, tp, plans),
        out_shape=(
            jax.ShapeDtypeStruct(q_shape, half),
            jax.ShapeDtypeStruct(lat_shape, half),
            *[jax.ShapeDtypeStruct((plan.rows, plan.columns), half) for plan in plans[1:]],
        ),
        in_specs=[vmem] * 9,
        out_specs=(vmem,) * 6,
        scratch_shapes=[
            pltpu.VMEM(q_shape, half),
            pltpu.VMEM(q_shape, half),
            pltpu.VMEM(lat_shape, half),
            pltpu.VMEM(lat_shape, half),
            pltpu.VMEM((width, rows), half),
            pltpu.VMEM((rank, rows), half),
            pltpu.VMEM((width, rows), half),
            *line_sems(rows // TAIL_CHUNK),
            *line_sems(rows // TAIL_CHUNK),
            *[shape for plan in plans for shape in plan.scratch()],
        ],
        compiler_params=pltpu.CompilerParams(
            vmem_limit_bytes=MIDDLE_VMEM, collective_id=collective_id, has_side_effects=True
        ),
        cost_estimate=pl.CostEstimate(
            flops=2 * rows * width * (hidden + ob.shape[1]) + 4 * rows * rank * d_query.shape[1],
            bytes_accessed=32 * 1024 * 1024,
            transcendentals=0,
        ),
        name=f"up_tail_{collective_id}",
    )(d_lat, d_query, w_qb, g_kvb, d_attn, ob, q_latent, d_feed, act)
    return sum_q.reshape(rows, rank), sum_lat.reshape(rows, lat_width), *grads


def down_tail_kernel(
    n, plans, sum_q, sum_lat, q_pre, lat_raw, tokens, d_middle, gain_in, gain_q, gain_kv, g_mid,
    w_qa, w_kva, cos, sin, grad_in, qa_out, kva_out, gains_out,
    d_q, d_kv, normed_t, scales, g_in, g_q, g_kv, packed, packing, mid_slots, grad_slots, in_sems, out_sems,
    *refs,
):
    take = taker(refs)
    qa, kva, gains = plans
    qa.bind(take, (normed_t, d_q), store_in(qa_out))
    kva.bind(take, (normed_t, d_kv), store_in(kva_out))
    gains.bind(take, packed, store_in(gains_out))
    rows = tokens.shape[0]
    block = rows // 4
    lane = lax.broadcasted_iota(jnp.int32, (block, HEAD), 1)
    barrier = pltpu.get_barrier_semaphore()
    others = greet_ctx(n, barrier)

    def rows_of(k):
        return pl.ds(pl.multiple_of(k * block, block), block)

    def fetch(k, slot):
        return pltpu.make_async_copy(
            d_middle.at[rows_of(k), :], mid_slots.at[slot], in_sems.at[slot]
        )

    def deliver(k, slot):
        return pltpu.make_async_copy(
            grad_slots.at[slot], grad_in.at[rows_of(k), :], out_sems.at[slot]
        )

    fetch(0, 0).start()
    fetch(1, 1).start()
    for ref in (g_in, g_q, g_kv):
        ref[...] = jnp.zeros(ref.shape, jnp.float32)

    def norms(k, carry):
        at = rows_of(k)
        pre = q_pre[at, :]
        d_pre, terms = norm_back(
            sum_q[at, :].astype(jnp.float32), pre, norm_scale(pre), gain_q[...]
        )
        g_q[...] += terms
        d_q[at, :] = d_pre.astype(jnp.bfloat16)
        raw = lat_raw[at, :]
        d_raw, terms = norm_back(
            sum_lat[at, :KVR].astype(jnp.float32), raw, norm_scale(raw), gain_kv[...]
        )
        g_kv[...] += terms
        d_kv[at, :KVR] = d_raw.astype(jnp.bfloat16)
        rope = sum_lat[at, KVR:].astype(jnp.float32)
        rope = jnp.concatenate([rope, jnp.zeros((block, HEAD - ROPE), jnp.float32)], axis=1)
        rope = rope_tile_back(rope, cos[at, :], sin[at, :], lane)
        d_kv[at, KVR:] = rope[:, :ROPE].astype(jnp.bfloat16)
        values = tokens[at, :].astype(jnp.float32)
        scale = norm_scale(values)
        scales[at, :] = jnp.broadcast_to(scale, (block, HEAD))
        normed = values * scale * gain_in[...]
        for c in range(0, normed.shape[1], 128):
            normed_t[c : c + 128, at] = normed[:, c : c + 128].T.astype(jnp.bfloat16)
        return carry

    lax.fori_loop(0, 4, norms, 0)
    pl.semaphore_wait(barrier, others)
    qa.start_core()
    kva.start_core()
    qa.finish_core()
    qa.start_step(0)
    kva.finish_core()
    kva.start_step(0)
    for k in range(4):
        at = pl.ds(k * block, block)
        fetch(k, k % 2).wait()
        if k >= 2:
            deliver(k - 2, k % 2).wait()
        d_normed = dot_nt(d_q[at, :], w_qa[...]) + dot_nn(d_kv[at, :], w_kva[...])
        d_values, terms = norm_back(
            d_normed, tokens[at, :].astype(jnp.float32), scales[at, :1], gain_in[...]
        )
        g_in[...] += terms
        grad_slots[k % 2] = mid_slots[k % 2] + d_values
        deliver(k, k % 2).start()
        if k + 2 < 4:
            fetch(k + 2, k % 2).start()
    packing[...] = jnp.zeros(packing.shape, jnp.float32)
    lines = gains.rows
    at = 0
    for whole in (g_in, g_mid, g_q, g_kv):
        share = whole.shape[1] // n
        piece = 32 if share % 32 == 0 else 16
        for dest in range(n):
            for place in range(0, share, piece):
                row, column = divmod(at + place, HEAD)
                row += dest * lines
                first = dest * share + place
                packing[row : row + 1, column : column + piece] = whole[:, first : first + piece]
        at += share
    packed[...] = packing[...].astype(jnp.bfloat16)
    gains.start_core()
    gains.finish_core()
    gains.start_step(0)
    for step in range(qa.count - 1):
        for item in (qa, kva, gains):
            item.finish_step(step)
    deliver(2, 0).wait()
    deliver(3, 1).wait()
    for item in plans:
        item.drain()


def down_tail(
    n, sum_q, sum_lat, q_pre, lat_raw, tokens, d_middle, gain_in, gain_q, gain_kv, g_mid, w_qa,
    w_kva, cos, sin, collective_id,
):
    rows, width = tokens.shape
    rank = q_pre.shape[1]
    vmem = pl.BlockSpec(memory_space=pltpu.VMEM)
    anywhere = pl.BlockSpec(memory_space=pl.ANY)
    half, full = jnp.bfloat16, jnp.float32
    dma = pltpu.SemaphoreType.DMA
    share = (2 * width + rank + KVR) // n
    lines = -(-share // (32 * HEAD)) * 32
    plans = [
        Scatter(n, width // n, rank, False),
        Scatter(n, width // n, KVR + ROPE, False),
        Scatter(n, lines, HEAD, True),
    ]
    slots = pltpu.VMEM((2, rows // 4, width), full)
    grad_in, qa, kva, gains = pl.pallas_call(
        functools.partial(down_tail_kernel, n, plans),
        out_shape=(
            jax.ShapeDtypeStruct((rows, width), full),
            *[jax.ShapeDtypeStruct((plan.rows, plan.columns), half) for plan in plans],
        ),
        in_specs=[vmem] * 5 + [anywhere] + [vmem] * 8,
        out_specs=(anywhere, vmem, vmem, vmem),
        scratch_shapes=[
            pltpu.VMEM((rows, rank), half),
            pltpu.VMEM((rows, KVR + ROPE), half),
            pltpu.VMEM((width, rows), half),
            pltpu.VMEM((rows, HEAD), full),
            pltpu.VMEM((1, width), full),
            pltpu.VMEM((1, rank), full),
            pltpu.VMEM((1, KVR), full),
            pltpu.VMEM((n * lines, HEAD), half),
            pltpu.VMEM((n * lines, HEAD), full),
            slots,
            slots,
            dma((2,)),
            dma((2,)),
            *[shape for plan in plans for shape in plan.scratch()],
        ],
        compiler_params=pltpu.CompilerParams(
            vmem_limit_bytes=MIDDLE_VMEM, collective_id=collective_id, has_side_effects=True
        ),
        cost_estimate=pl.CostEstimate(
            flops=4 * rows * width * (rank + KVR + ROPE),
            bytes_accessed=40 * 1024 * 1024,
            transcendentals=rows,
        ),
        name=f"down_tail_{collective_id}",
    )(
        sum_q,
        sum_lat,
        q_pre,
        lat_raw,
        tokens,
        d_middle,
        gain_in.reshape(1, -1),
        gain_q.reshape(1, -1),
        gain_kv.reshape(1, -1),
        g_mid,
        w_qa,
        w_kva,
        cos,
        sin,
    )
    gains = gains.astype(full).reshape(-1)
    ends = [0]
    for size in (width, width, rank, KVR):
        ends.append(ends[-1] + size // n)
    return grad_in, qa, kva, [gains[first:last] for first, last in zip(ends, ends[1:])]


CHUNK = 16
BLOCK = 8 * CHUNK
LAG = 2
MIDDLE_VMEM = 63 * 1024 * 1024


def middle_kernel(
    n, lag, ob, tokens_in, cot_in, gain, w_out, w_gate, w_up, w_down,
    tt_to, d_to, f_to, act_to, dg_to, du_to, h_to, df_to,
    tt, d_out, f_out, act_out, dg_out, du_out, h_out, df_out,
    tokens, cot, own, up, wo, wg, wu, wd, d_acc, f_acc, w_sems, out_sems, *sems,
):
    line = LineSum(n, own, up, tt, sems, lag)
    width = tokens.shape[1]
    hidden = wg.shape[0]
    chunks, chunk = own.shape[:2]
    per_block = BLOCK // chunk
    blocks = chunks // per_block
    block_lag = -(-(per_block + line.land_lag) // per_block)
    tiles = [(c, min(c + 512, width)) for c in range(0, width, 512)]
    quarter = hidden // 4 // 128 * 128
    cuts = [0, quarter, 2 * quarter, 3 * quarter, hidden]
    loads = [
        pltpu.make_async_copy(source, target, w_sems.at[k])
        for k, (source, target) in enumerate(
            (
                (w_out, wo),
                (tokens_in, tokens),
                (cot_in, cot),
                (w_gate, wg),
                (w_up, wu),
                (w_down, wd),
            )
        )
    ]
    kept = ((d_out, d_to), (f_out, f_to), (act_out, act_to), (dg_out, dg_to), (du_out, du_to))
    kept += ((h_out, h_to), (df_out, df_to))

    def keep(b):
        rows = pl.ds(pl.multiple_of(b * BLOCK, BLOCK), BLOCK)
        copies = [
            pltpu.make_async_copy(source.at[rows, :], target.at[rows, :], out_sems.at[k, b])
            for k, (source, target) in enumerate(kept)
        ]
        some = pl.ds(b * per_block, per_block)
        return copies + [
            pltpu.make_async_copy(tt.at[some], tt_to.at[some], out_sems.at[len(kept), b])
        ]

    for load in loads:
        load.start()
    barrier = pltpu.get_barrier_semaphore()
    line.greet(barrier)
    line.wait_greetings(barrier, 0)

    def project(b, carry):
        rows = pl.ds(pl.multiple_of(b * BLOCK, BLOCK), BLOCK)
        for first, last in tiles:
            part = dot_nt(ob[rows, :], wo[first:last, :]).astype(jnp.bfloat16)
            for k in range(per_block):
                own[per_block * b + k, :, first:last] = part[k * chunk : (k + 1) * chunk, :]
        for k in range(per_block):
            line.leaf(per_block * b + k)
        return carry

    def normalize(b, part):
        for k in range(part * per_block // 2, (part + 1) * per_block // 2, 2):
            rows = pl.ds(pl.multiple_of(b * BLOCK + k * chunk, 2 * chunk), 2 * chunk)
            sums = jnp.concatenate([tt[b * per_block + k], tt[b * per_block + k + 1]], axis=0)
            middle = tokens[rows, :].astype(jnp.float32) + RESIDUAL_SCALE * sums.astype(jnp.float32)
            h_out[rows, :] = (middle * norm_scale(middle) * gain[...]).astype(jnp.bfloat16)

    def feed(b, i):
        rows = pl.ds(pl.multiple_of(b * BLOCK, BLOCK), BLOCK)
        first, last = cuts[i], cuts[i + 1]
        if i == 0:
            normalize(b, 0)
            normalize(b, 1)
            df_out[rows, :] = (RESIDUAL_SCALE * cot[rows, :].astype(jnp.float32)).astype(
                jnp.bfloat16
            )
        gate = dot_nt(h_out[rows, :], wg[first:last, :])
        upper = dot_nt(h_out[rows, :], wu[first:last, :])
        d_act = dot_nt(df_out[rows, :], wd[first:last, :])
        sig = jax.nn.sigmoid(gate)
        silu = gate * sig
        act_out[rows, first:last] = (silu * upper).astype(jnp.bfloat16)
        dg_out[rows, first:last] = (d_act * upper * sig * (1.0 + gate * (1.0 - sig))).astype(
            jnp.bfloat16
        )
        du_out[rows, first:last] = (d_act * silu).astype(jnp.bfloat16)

    def feed_back(b, i):
        rows = pl.ds(pl.multiple_of(b * BLOCK, BLOCK), BLOCK)
        first, last = cuts[i], cuts[i + 1]
        act, dg, du = (ref[rows, first:last] for ref in (act_out, dg_out, du_out))
        for lo, hi in tiles:
            d_part = dot_nn(dg, wg[first:last, lo:hi]) + dot_nn(du, wu[first:last, lo:hi])
            f_part = dot_nn(act, wd[first:last, lo:hi])
            if i:
                d_part = d_part + d_acc[:, lo:hi]
                f_part = f_part + f_acc[:, lo:hi]
            if i < 3:
                d_acc[:, lo:hi] = d_part
                f_acc[:, lo:hi] = f_part
            else:
                d_out[rows, lo:hi] = d_part.astype(jnp.bfloat16)
                f_out[rows, lo:hi] = f_part.astype(jnp.bfloat16)

    loads[0].wait()
    lax.fori_loop(0, blocks, project, 0)

    def outer(o, carry):
        b = o - block_lag

        @pl.when(b == 0)
        def _():
            for load in loads[1:]:
                load.wait()

        share = per_block // 8
        for i in range(4):
            for step, work in enumerate((feed, feed_back)):

                @pl.when(o * per_block < line.ticks)
                def _(at=(2 * i + step) * share):
                    for k in range(share):
                        line.duty(o * per_block + at + k)

                @pl.when(b >= 0)
                def _(i=i, work=work):
                    work(b, i)

        @pl.when(b >= 0)
        def _():
            for copy in keep(b):
                copy.start()

        return carry

    lax.fori_loop(0, blocks + block_lag, outer, 0)
    line.drain()

    def finish(b, carry):
        for copy in keep(b):
            copy.wait()
        return carry

    lax.fori_loop(0, blocks, finish, 0)


def middle_layer(n, ob, tokens, cot, gain, w_out, w_gate, w_up, w_down, collective_id):
    rows, width = tokens.shape
    hidden = w_gate.shape[0]
    chunks = rows // CHUNK
    vmem = pl.BlockSpec(memory_space=pltpu.VMEM)
    anywhere = pl.BlockSpec(memory_space=pl.ANY)
    half = jnp.bfloat16
    dma = pltpu.SemaphoreType.DMA
    attn, *rest = pl.pallas_call(
        functools.partial(middle_kernel, n, LAG),
        out_shape=(
            jax.ShapeDtypeStruct((chunks, CHUNK, width), half),
            jax.ShapeDtypeStruct((rows, width), half),
            jax.ShapeDtypeStruct((rows, width), half),
            jax.ShapeDtypeStruct((rows, hidden), half),
            jax.ShapeDtypeStruct((rows, hidden), half),
            jax.ShapeDtypeStruct((rows, hidden), half),
            jax.ShapeDtypeStruct((rows, width), half),
            jax.ShapeDtypeStruct((rows, width), half),
        ),
        in_specs=[vmem, anywhere, anywhere, vmem] + [anywhere] * 4,
        out_specs=(anywhere,) * 8,
        scratch_shapes=[
            pltpu.VMEM((chunks, CHUNK, width), half),
            pltpu.VMEM((rows, width), half),
            pltpu.VMEM((rows, width), half),
            pltpu.VMEM((rows, hidden), half),
            pltpu.VMEM((rows, hidden), half),
            pltpu.VMEM((rows, hidden), half),
            pltpu.VMEM((rows, width), half),
            pltpu.VMEM((rows, width), half),
            pltpu.VMEM((rows, width), half),
            pltpu.VMEM((rows, width), half),
            pltpu.VMEM((chunks, CHUNK, width), half),
            pltpu.VMEM((chunks, CHUNK, width), half),
            pltpu.VMEM(w_out.shape, half),
            pltpu.VMEM(w_gate.shape, half),
            pltpu.VMEM(w_up.shape, half),
            pltpu.VMEM(w_down.shape, half),
            pltpu.VMEM((BLOCK, width), jnp.float32),
            pltpu.VMEM((BLOCK, width), jnp.float32),
            dma((6,)),
            dma((8, rows // BLOCK)),
            *line_sems(chunks),
        ],
        compiler_params=pltpu.CompilerParams(
            vmem_limit_bytes=MIDDLE_VMEM, collective_id=collective_id, has_side_effects=True
        ),
        cost_estimate=pl.CostEstimate(
            flops=2 * rows * width * (6 * hidden + ob.shape[1]),
            bytes_accessed=64 * 1024 * 1024,
            transcendentals=rows * hidden,
        ),
        name=f"middle_layer_{collective_id}",
    )(ob, tokens, cot, gain.reshape(1, -1), w_out, w_gate, w_up, w_down)
    return attn.reshape(rows, width), *rest


def norm_scale(values):
    return lax.rsqrt(jnp.mean(values * values, axis=-1, keepdims=True) + EPSILON)


def norm_back(incoming, values, inv_rms, gain_vec):
    weighted = incoming * gain_vec
    mean = jnp.mean(weighted * values, axis=-1, keepdims=True)
    d_values = inv_rms * weighted - values * (inv_rms * inv_rms * inv_rms) * mean
    return d_values, jnp.sum(incoming * values * inv_rms, axis=0, keepdims=True)


def rope_tile(tile, cos, sin, lane):
    left = pltpu.roll(tile, HEAD - ROPE // 2, 1)
    right = pltpu.roll(tile, ROPE // 2, 1)
    swapped = jnp.where(lane < ROPE // 2, -left, right)
    return jnp.where(lane < ROPE, tile * cos + swapped * sin, 0.0)


def rope_tile_back(tile, cos, sin, lane):
    shifted = tile * sin
    left = pltpu.roll(shifted, HEAD - ROPE // 2, 1)
    right = pltpu.roll(shifted, ROPE // 2, 1)
    swapped = jnp.where(lane < ROPE // 2, left, -right)
    return jnp.where(lane < ROPE, tile * cos + swapped, 0.0)


def second_norm_kernel(
    d_sum, attn, tokens, cot, gain, w_out, d_middle, d_attn, d_heads, d_gain
):
    middle = tokens[...].astype(jnp.float32) + RESIDUAL_SCALE * attn[...].astype(jnp.float32)
    d_norm, gain_terms = norm_back(
        d_sum[...].astype(jnp.float32), middle, norm_scale(middle), gain[...]
    )
    total = cot[...].astype(jnp.float32) + d_norm
    d_middle[...] = total
    scaled = (RESIDUAL_SCALE * total).astype(jnp.bfloat16)
    d_attn[...] = scaled
    d_heads[...] = dot_nn(scaled, w_out[...]).astype(jnp.bfloat16)

    @pl.when(pl.program_id(0) == 0)
    def _():
        d_gain[...] = jnp.zeros(d_gain.shape, jnp.float32)

    d_gain[...] += gain_terms


def second_norm_back(d_sum, attn, tokens, cot, gain, w_out):
    rows, width = tokens.shape
    block = rows // 4
    head_width = w_out.shape[1]
    whole = lambda shape: pl.BlockSpec(shape, lambda i: (0, 0))
    tile = lambda columns: pl.BlockSpec((block, columns), lambda i: (i, 0))
    return pl.pallas_call(
        second_norm_kernel,
        grid=(rows // block,),
        out_shape=(
            jax.ShapeDtypeStruct((rows, width), jnp.float32),
            jax.ShapeDtypeStruct((rows, width), jnp.bfloat16),
            jax.ShapeDtypeStruct((rows, head_width), jnp.bfloat16),
            jax.ShapeDtypeStruct((1, width), jnp.float32),
        ),
        in_specs=[tile(width)] * 4 + [whole((1, width)), whole((width, head_width))],
        out_specs=(tile(width), tile(width), tile(head_width), whole((1, width))),
        compiler_params=pltpu.CompilerParams(vmem_limit_bytes=VMEM_LIMIT),
        cost_estimate=pl.CostEstimate(
            flops=2 * rows * width * head_width,
            bytes_accessed=24 * 1024 * 1024,
            transcendentals=rows,
        ),
        name="second_norm_back",
    )(d_sum, attn, tokens, cot, gain.reshape(1, -1), w_out)


def head_kernel(
    n, tokens, gain_in, gain_q, gain_kv, w_qa, w_kva, cos, sin, out, q_latent, q_pre, lat_raw,
    own, normed, w_rope, local_sem, step_sends, step_lands, core_sends, core_lands,
):
    count = n.bit_length() - 1
    me = lax.axis_index("ctx")
    rows = own.shape[0]
    half = rows // 2
    block = rows // 4
    barrier = pltpu.get_barrier_semaphore()
    for bit in range(count):
        pl.semaphore_signal(barrier, inc=1, device_id={"ctx": me ^ (1 << bit)}, device_id_type=MESH)
    orders = (tuple(range(1, count)), tuple(range(count - 1, 0, -1)))
    lane = lax.broadcasted_iota(jnp.int32, (block, HEAD), 1)
    w_rope[...] = jnp.zeros(w_rope.shape, jnp.bfloat16)
    w_rope[:ROPE, :] = w_kva[KVR : KVR + ROPE, :]

    def latents(k, carry):
        at = pl.ds(pl.multiple_of(k * block, block), block)
        values = tokens[at, :].astype(jnp.float32)
        normed[at, :] = (values * norm_scale(values) * gain_in[...]).astype(jnp.bfloat16)
        raw = dot_nt(normed[at, :], w_kva[:KVR, :])
        lat_raw[at, :] = raw
        own[at, :KVR] = (raw * norm_scale(raw) * gain_kv[...]).astype(jnp.bfloat16)
        rope = rope_tile(dot_nt(normed[at, :], w_rope[...]), cos[at, :], sin[at, :], lane)
        own[at, KVR:] = rope[:, :ROPE].astype(jnp.bfloat16)
        return carry

    lax.fori_loop(0, 4, latents, 0)
    pl.semaphore_wait(barrier, count)
    local = pltpu.make_async_copy(own, out.at[me], local_sem)
    local.start()

    def chip_copy(part, step, slot, block, first):
        at = pl.ds(part * half, half)
        return pltpu.make_async_remote_copy(
            src_ref=own.at[at, :] if first else out.at[block, at, :],
            dst_ref=out.at[block, at, :],
            send_sem=step_sends.at[part, step, slot],
            recv_sem=step_lands.at[part, step, slot],
            device_id={"ctx": me ^ (1 << orders[part][step])},
            device_id_type=MESH,
        )

    def core_copy(block, slot, first):
        return pltpu.make_async_remote_copy(
            src_ref=own if first else out.at[block],
            dst_ref=out.at[block],
            send_sem=core_sends.at[slot],
            recv_sem=core_lands.at[slot],
            device_id={"ctx": me ^ 1},
            device_id_type=MESH,
        )

    def query(k, carry):
        at = pl.ds(pl.multiple_of(k * block, block), block)
        pre = dot_nn(normed[at, :], w_qa[...])
        q_pre[at, :] = pre
        q_latent[at, :] = (pre * norm_scale(pre) * gain_q[...]).astype(jnp.bfloat16)
        return carry

    started = []
    for step in range(count - 1):
        for part, order in enumerate(orders):
            for slot in range(1 << step):
                flips = 0
                for at in range(step):
                    flips |= ((slot >> at) & 1) << order[at]
                copy = chip_copy(part, step, slot, me ^ flips, slot == 0)
                copy.start()
                started.append(copy)
        if step == 0:
            core_copy(me, 0, True).start()
        lax.fori_loop(2 * step, min(2 * step + 2, 4) if step < count - 2 else 4, query, 0)
        for part, order in enumerate(orders):
            for slot in range(1 << step):
                chip_copy(part, step, slot, me, slot == 0).wait_recv()
    for chip in range(1, n // 2):
        core_copy(me ^ (2 * chip), chip, False).start()
    for chip in range(n // 2):
        core_copy(me, chip, chip == 0).wait_recv()
    for copy in started:
        copy.wait_send()
    for chip in range(n // 2):
        core_copy(me, chip, chip == 0).wait_send()
    local.wait()


def head_layer(n, tokens, gain_in, gain_q, gain_kv, w_qa, w_kva, cos, sin, collective_id):
    rows, width = tokens.shape
    rank = w_qa.shape[1]
    count = n.bit_length() - 1
    vmem = pl.BlockSpec(memory_space=pltpu.VMEM)
    slots = max(n // 4, 1)
    dma = pltpu.SemaphoreType.DMA
    gathered, q_latent, q_pre, lat_raw = pl.pallas_call(
        functools.partial(head_kernel, n),
        out_shape=(
            jax.ShapeDtypeStruct((n, rows, KVR + ROPE), jnp.bfloat16),
            jax.ShapeDtypeStruct((rows, rank), jnp.bfloat16),
            jax.ShapeDtypeStruct((rows, rank), jnp.float32),
            jax.ShapeDtypeStruct((rows, KVR), jnp.float32),
        ),
        in_specs=[vmem] * 8,
        out_specs=(vmem,) * 4,
        scratch_shapes=[
            pltpu.VMEM((rows, KVR + ROPE), jnp.bfloat16),
            pltpu.VMEM((rows, width), jnp.bfloat16),
            pltpu.VMEM((HEAD, width), jnp.bfloat16),
            dma,
            dma((2, count - 1, slots)),
            dma((2, count - 1, slots)),
            dma((n // 2,)),
            dma((n // 2,)),
        ],
        compiler_params=pltpu.CompilerParams(
            vmem_limit_bytes=VMEM_LIMIT, collective_id=collective_id, has_side_effects=True
        ),
        cost_estimate=pl.CostEstimate(
            flops=2 * rows * width * (rank + KVR + ROPE),
            bytes_accessed=24 * 1024 * 1024,
            transcendentals=rows,
        ),
        name=f"head_layer_{collective_id}",
    )(
        tokens,
        gain_in.reshape(1, -1),
        gain_q.reshape(1, -1),
        gain_kv.reshape(1, -1),
        w_qa,
        w_kva,
        cos,
        sin,
    )
    return gathered.reshape(n * rows, -1), q_latent, q_pre, lat_raw


def wide_tables(inside):
    half_width = ROPE // 2
    lane = jnp.arange(HEAD, dtype=jnp.int32)
    frequency = ROPE_BASE ** (-2.0 * (lane % half_width).astype(jnp.float32) / ROPE)
    angles = inside.astype(jnp.float32)[:, None] * frequency[None, :]
    used = lane[None, :] < ROPE
    return jnp.where(used, jnp.cos(angles), 0.0), jnp.where(used, jnp.sin(angles), 0.0)


def on_device(
    tokens_in,
    w_qa,
    w_kva,
    w_qb,
    w_kvb,
    w_out,
    w_gate,
    w_up,
    w_down,
    gain_in,
    gain_q,
    gain_kv,
    gain_mid,
    cotangent,
    block_map,
    doc_lengths,
):
    local_rows = tokens_in.shape[0]
    half_rows = local_rows // 2
    devices = lax.axis_size("ctx")
    ctx_index = lax.axis_index("ctx")
    seqs = doc_lengths.shape[0]
    own_blocks = lax.dynamic_slice_in_dim(block_map, ctx_index, 1, 0)[0]
    ends = jnp.cumsum(doc_lengths)
    starts = ends - doc_lengths
    meta = jnp.concatenate([block_map.reshape(-1), starts, own_blocks])
    within = jnp.arange(half_rows, dtype=jnp.int32)
    query_place = (own_blocks[:, None] * half_rows + within[None, :]).reshape(-1)
    began = jnp.max(
        jnp.where(starts[None, :] <= query_place[:, None], starts[None, :], 0), axis=1
    )
    cosine, sine = wide_tables(query_place - began)
    latents, q_latent, q_latent_pre, latent_raw = head_layer(
        devices, tokens_in, gain_in, gain_q, gain_kv, w_qa, w_kva.T, cosine, sine, 0
    )
    queries, attn_f, heads_out, log_totals = attention_forward(
        meta, q_latent, w_qb.T, latents, w_kvb, cosine, sine, half_rows, seqs
    )
    attention, d_part, feed_part, activation, d_gate, d_up, normed_mid, d_feed = middle_layer(
        lax.axis_size("tp"), heads_out, tokens_in, cotangent, gain_mid, w_out, w_gate.T, w_up.T,
        w_down.T, 5,
    )
    gw_gate, gw_up, d_normed_mid = gate_up_grads(
        devices, lax.axis_size("tp"), normed_mid, d_gate, d_up, d_part, 1
    )
    d_normed_mid, feed_part = lax.optimization_barrier((d_normed_mid, feed_part))
    feed_own = lax.psum_scatter(feed_part, "tp", scatter_dimension=0, tiled=True)
    own_rows = feed_own.shape[0]
    own_at = lax.axis_index("tp") * own_rows
    tokens_own = lax.dynamic_slice_in_dim(tokens_in, own_at, own_rows, 0).astype(jnp.float32)
    attention_own = lax.dynamic_slice_in_dim(attention, own_at, own_rows, 0).astype(jnp.float32)
    middle_own = tokens_own + RESIDUAL_SCALE * attention_own
    out_own = (middle_own + RESIDUAL_SCALE * feed_own.astype(jnp.float32)).astype(jnp.bfloat16)
    d_middle, d_attention, d_heads, d_gain_mid = second_norm_back(
        d_normed_mid, attention, tokens_in, cotangent, gain_mid, w_out
    )
    d_query_pre, d_latents, gw_kvb = attention_backward(
        meta, queries, log_totals, attn_f, d_heads, latents, w_kvb, cosine, sine, half_rows, seqs
    )
    sum_q, sum_lat, gw_down, gw_out, gw_qb, gw_kvb = up_tail(
        devices, lax.axis_size("tp"), d_latents, d_query_pre, w_qb.T, gw_kvb, d_attention, heads_out,
        q_latent, d_feed, activation, 2,
    )
    sum_q, out_own = lax.optimization_barrier((sum_q, out_own))
    out = lax.all_gather(out_own, "tp", axis=0, tiled=True)
    grad_in, gw_qa, gw_kva, own_gains = down_tail(
        devices, sum_q, sum_lat, q_latent_pre, latent_raw, tokens_in, d_middle, gain_in, gain_q,
        gain_kv, d_gain_mid, w_qa, w_kva.T, cosine, sine, 3,
    )
    grads = (gw_qa, gw_kva, gw_qb, gw_kvb, gw_out, gw_gate, gw_up, gw_down)
    return (
        out,
        grad_in,
        *[grad.astype(jnp.float32) for grad in grads],
        own_gains[0],
        own_gains[2],
        own_gains[3],
        own_gains[1],
    )


def solution(mesh):
    return jax.shard_map(
        on_device,
        mesh=mesh,
        in_specs=(
            P("ctx", None),
            P(),
            P(),
            P(None, "tp"),
            P(None, "tp"),
            P(None, "tp"),
            P(None, "tp"),
            P(None, "tp"),
            P(None, "tp"),
            P(),
            P(),
            P(),
            P(),
            P("ctx", None),
            P(),
            P(),
        ),
        out_specs=(
            P("ctx", None),
            P("ctx", None),
            P("ctx", None),
            P("ctx", None),
            P("ctx", "tp"),
            P("ctx", "tp"),
            P("ctx", "tp"),
            P("ctx", "tp"),
            P("ctx", "tp"),
            P("ctx", "tp"),
            P("ctx"),
            P("ctx"),
            P("ctx"),
            P("ctx"),
        ),
        check_vma=False,
    )
```

```python
import functools
import math

import jax
import jax.numpy as jnp
import numpy as np
from jax import lax
from jax.experimental import pallas as pl
from jax.experimental.pallas import tpu as pltpu
from jax.sharding import PartitionSpec as P

KVR = 256
NOPE = 64
ROPE = 32
VDIM = 64
HEAD = NOPE + VDIM
WIDE = 2 * HEAD
MASKED = -1e30
SCORE_SCALE = (NOPE + ROPE) ** (-0.5)
EXP2_SCALE = SCORE_SCALE * math.log2(math.e)
FOLD_AT = 96
SUM_ROWS = 16
VMEM_LIMIT = 56 * 1024 * 1024

EPSILON = 1e-05
ROPE_BASE = 10000.0
RESIDUAL_SCALE = 1.4 / math.sqrt(62.0)


def dot_nn(left_op, right_op):
    return jnp.dot(left_op, right_op, preferred_element_type=jnp.float32)


def dot_nt(left_op, right_op):
    return lax.dot_general(
        left_op, right_op, (((1,), (1,)), ((), ())), preferred_element_type=jnp.float32
    )


def starts_of(lengths):
    starts = [jnp.int32(0)]
    for s in range(lengths.shape[0] - 1):
        starts.append(starts[-1] + lengths[s])
    return starts


def begin_of(place, starts):
    begin = jnp.zeros_like(place)
    for start in starts:
        begin = jnp.where(start <= place, start, begin)
    return begin


def pair_kind(key_block, query_block, starts, block_rows):
    key_first = key_block * block_rows
    query_first = query_block * block_rows
    early = begin_of(query_first, starts)
    late = begin_of(query_first + block_rows - 1, starts)
    needed = (key_block <= query_block) & (key_first + block_rows - 1 >= early)
    whole = (key_block < query_block) & (late <= key_first)
    return needed, whole


def mask_bias(key_block, query_block, starts, block_rows, keys_first):
    key_dim = 0 if keys_first else 1
    shape = (block_rows, block_rows)
    key_place = key_block * block_rows + lax.broadcasted_iota(jnp.int32, shape, key_dim)
    query_place = query_block * block_rows + lax.broadcasted_iota(jnp.int32, shape, 1 - key_dim)
    begin = jnp.zeros(shape, jnp.int32)
    for start in starts:
        begin = jnp.where(start <= query_place, start, begin)
    allowed = (key_place <= query_place) & (key_place >= begin)
    return jnp.where(allowed, 0.0, MASKED)


def shared_key_tile(rope_rows, block_rows):
    place = lax.broadcasted_iota(jnp.int32, (ROPE, HEAD), 0)
    lane = lax.broadcasted_iota(jnp.int32, (ROPE, HEAD), 1)
    eye = jnp.where(place == lane, 1.0, 0.0).astype(jnp.bfloat16)
    tile = dot_nn(rope_rows, eye)
    lanes = lax.broadcasted_iota(jnp.int32, (block_rows, HEAD), 1)
    ones = (lanes >= FOLD_AT) & (lanes < FOLD_AT + 3)
    return jnp.where(ones, 1.0, tile).astype(jnp.bfloat16)


def head_window(h):
    at = h * (NOPE + ROPE)
    return at // HEAD * HEAD, at % HEAD


def window_columns(heads):
    return head_window(heads - 1)[0] + WIDE


def head_groups(heads):
    return [(h, min(h + 2, heads)) for h in range(0, heads, 2)]


def forward_kernel(
    blocks, heads, block_map, lengths, qx, lat, wkvb, o_out, ob_out, u_out,
    wkvt, xs, xr, vt, top, acc, bias, s_ref, p_ref,
):
    block_rows = bias.shape[0]
    q_blocks = qx.shape[0]
    starts = starts_of(lengths)
    own = [block_map[j, lax.axis_index("ctx")] for j in range(q_blocks)]
    for first, last in head_groups(heads):
        wkvt[first * HEAD : last * HEAD, :] = (
            wkvb[:, first * HEAD : last * HEAD].astype(jnp.float32).T.astype(jnp.bfloat16)
        )
    top[...] = jnp.full(top.shape, MASKED, jnp.float32)
    vt[:, VDIM:, :] = jnp.ones((heads, SUM_ROWS, block_rows), jnp.bfloat16)
    acc[...] = jnp.zeros(acc.shape, jnp.float32)

    def pair(j, masked):
        def one(h):
            keys = jnp.concatenate([xs[h], xr[...]], axis=1)
            s_ref[h % 3] = dot_nt(keys, qx[j, h])

        def weigh(h):
            old = top[j, h]
            new = old
            for k in range(0, block_rows, 128):
                part = s_ref[h % 3, k : k + 128, :]
                if masked:
                    part = part + bias[k : k + 128, :]
                    s_ref[h % 3, k : k + 128, :] = part
                new = jnp.maximum(new, jnp.max(part, axis=0, keepdims=True))
            fade = jnp.exp2((old - new) * EXP2_SCALE)
            top[j, h] = new
            for k in range(0, block_rows, 128):
                terms = jnp.exp2((s_ref[h % 3, k : k + 128, :] - new) * EXP2_SCALE)
                p_ref[h % 3, k : k + 128, :] = terms.astype(jnp.bfloat16)
            return fade

        def add(h, fade):
            acc[j, h] = fade * acc[j, h] + dot_nn(vt[h], p_ref[h % 3])

        one(0)
        if heads > 1:
            one(1)
        fades = {}
        for h in range(heads):
            if h + 2 < heads:
                one(h + 2)
            fades[h] = weigh(h)
            if h > 1:
                add(h - 2, fades[h - 2])
        for h in range(max(heads - 2, 0), heads):
            add(h, fades[h])

    def step(r, carry):
        key_block = block_map[lax.rem(r, 2), lax.div(r, 2)]
        kinds = [pair_kind(key_block, own[j], starts, block_rows) for j in range(q_blocks)]
        wanted = functools.reduce(jnp.logical_or, [k[0] for k in kinds])

        @pl.when(wanted)
        def _():
            here = pl.ds(pl.multiple_of(r * block_rows, block_rows), block_rows)
            latent = lat[here, :KVR]
            xr[...] = shared_key_tile(lat[here, KVR : KVR + ROPE], block_rows)
            for first, last in head_groups(heads):
                keys = dot_nn(latent, wkvb[:, first * HEAD : last * HEAD]).astype(jnp.bfloat16)
                values = dot_nt(wkvt[first * HEAD : last * HEAD, :], latent).astype(jnp.bfloat16)
                for h in range(first, last):
                    at = (h - first) * HEAD
                    xs[h] = keys[:, at : at + HEAD]
                    vt[h, :VDIM, :] = values[at + NOPE : at + HEAD, :]

        for j in range(q_blocks):
            needed, whole = kinds[j]

            @pl.when(needed & whole)
            def _():
                pair(j, False)

            @pl.when(needed & jnp.logical_not(whole))
            def _():
                bias[...] = mask_bias(key_block, own[j], starts, block_rows, True)
                pair(j, True)

        return carry

    lax.fori_loop(0, blocks, step, 0)
    for j in range(q_blocks):
        here = pl.ds(j * block_rows, block_rows)
        for first, last in head_groups(heads):
            parts = []
            for h in range(first, last):
                total = acc[j, h, VDIM : VDIM + 1, :]
                parts.append(acc[j, h, :VDIM, :] * (1.0 / total))
                u_out[j, h : h + 1, :] = top[j, h] + jnp.log2(total) * (1.0 / EXP2_SCALE)
            if len(parts) == 1:
                parts.append(jnp.zeros_like(parts[0]))
            both = jnp.concatenate(parts, axis=0).T
            width = (last - first) * VDIM
            o_out[here, first * VDIM : first * VDIM + width] = both[:, :width]
            ob_out[here, first * VDIM : first * VDIM + width] = both[:, :width].astype(jnp.bfloat16)


def attention_forward(block_map, lengths, qx, lat, wkvb):
    q_blocks, heads, block_rows, _ = qx.shape
    blocks = lat.shape[0] // block_rows
    rows = q_blocks * block_rows
    vmem = pl.BlockSpec(memory_space=pltpu.VMEM)
    smem = pl.BlockSpec(memory_space=pltpu.SMEM)
    pairs = q_blocks * blocks * heads // 2
    return pl.pallas_call(
        functools.partial(forward_kernel, blocks, heads),
        out_shape=(
            jax.ShapeDtypeStruct((rows, heads * VDIM), jnp.float32),
            jax.ShapeDtypeStruct((rows, heads * VDIM), jnp.bfloat16),
            jax.ShapeDtypeStruct((q_blocks, 16 * -(-heads // 16), block_rows), jnp.float32),
        ),
        in_specs=[smem] * 2 + [vmem] * 3,
        out_specs=(vmem,) * 3,
        scratch_shapes=[
            pltpu.VMEM((heads * HEAD, KVR), jnp.bfloat16),
            pltpu.VMEM((heads, block_rows, HEAD), jnp.bfloat16),
            pltpu.VMEM((block_rows, HEAD), jnp.bfloat16),
            pltpu.VMEM((heads, VDIM + SUM_ROWS, block_rows), jnp.bfloat16),
            pltpu.VMEM((q_blocks, heads, 1, block_rows), jnp.float32),
            pltpu.VMEM((q_blocks, heads, VDIM + SUM_ROWS, block_rows), jnp.float32),
            pltpu.VMEM((block_rows, block_rows), jnp.float32),
            pltpu.VMEM((3, block_rows, block_rows), jnp.float32),
            pltpu.VMEM((3, block_rows, block_rows), jnp.bfloat16),
        ],
        compiler_params=pltpu.CompilerParams(vmem_limit_bytes=VMEM_LIMIT),
        cost_estimate=pl.CostEstimate(
            flops=pairs * 4 * block_rows * block_rows * WIDE,
            bytes_accessed=16 * 1024 * 1024,
            transcendentals=pairs * block_rows * block_rows,
        ),
        name="attention_forward",
    )(block_map, lengths, qx, lat, wkvb)


def three_terms(column):
    first = column.astype(jnp.bfloat16).astype(jnp.float32)
    rest = column - first
    second = rest.astype(jnp.bfloat16).astype(jnp.float32)
    return first, second, rest - second


def fold_in(tile, column, lane):
    for k, term in enumerate(three_terms(column)):
        tile = jnp.where(lane == FOLD_AT + k, term, tile)
    return tile


def backward_kernel(
    blocks, heads, block_map, lengths, qx, qt, u_in, o_in, dob, lat, wkvb, cos, sin,
    dq_out, dlat, gkvb, xs, xr, qo, dt, dq, dkv, dkpe, gsum, bias, flat, s_ref, p_ref, d_ref,
):
    block_rows = bias.shape[0]
    q_blocks = qx.shape[0]
    starts = starts_of(lengths)
    own = [block_map[j, lax.axis_index("ctx")] for j in range(q_blocks)]
    lane = lax.broadcasted_iota(jnp.int32, (block_rows, HEAD), 1)
    for j in range(q_blocks):
        here = pl.ds(j * block_rows, block_rows)
        logs = u_in[j].T
        for first, last in head_groups(heads):
            d_pair = dob[here, first * VDIM : first * VDIM + HEAD].astype(jnp.float32)
            weighted = d_pair * o_in[here, first * VDIM : first * VDIM + HEAD]
            turned = pltpu.roll(d_pair, VDIM, 1)
            for h in range(first, last):
                mine = lane < VDIM if h == first else lane >= VDIM
                delta = jnp.sum(jnp.where(mine, weighted, 0.0), axis=1, keepdims=True)
                d_head = jnp.where(lane >= VDIM, turned if h == first else d_pair, 0.0)
                q_second = qx[j, h, :, HEAD:].astype(jnp.float32)
                qo[j, h, :block_rows, :HEAD] = qx[j, h, :, :HEAD]
                qo[j, h, :block_rows, HEAD:] = fold_in(q_second, -logs[:, h : h + 1], lane).astype(
                    jnp.bfloat16
                )
                qo[j, h, block_rows:, :HEAD] = d_head.astype(jnp.bfloat16)
                qo[j, h, block_rows:, HEAD:] = fold_in(
                    jnp.zeros((block_rows, HEAD), jnp.float32), -delta, lane
                ).astype(jnp.bfloat16)
                dt[j, h] = d_head.T[VDIM:, :].astype(jnp.bfloat16)
    dq[...] = jnp.zeros(dq.shape, jnp.float32)
    gsum[...] = jnp.zeros(gsum.shape, jnp.float32)

    def pair(j, masked):
        def raw(h):
            keys = jnp.concatenate([xs[h], xr[...]], axis=1)
            s_ref[h % 2] = dot_nt(qo[j, h], keys)

        def weigh(h):
            for k in range(0, block_rows, 128):
                scores = s_ref[h % 2, k : k + 128, :] * EXP2_SCALE
                if masked:
                    scores = scores + bias[k : k + 128, :]
                probs = jnp.exp2(scores)
                p_ref[h % 2, k : k + 128, :] = probs.astype(jnp.bfloat16)
                d_ref[h % 2, k : k + 128, :] = (
                    probs * s_ref[h % 2, block_rows + k : block_rows + k + 128, :]
                ).astype(jnp.bfloat16)

        def add(h):
            keys = jnp.concatenate([xs[h], xr[...]], axis=1)
            d_scores = d_ref[h % 2]
            dq[j, h] += dot_nn(d_scores, keys)
            d_keys = dot_nn(qt[j, h], d_scores)
            dkv[h, :NOPE, :] += d_keys[:NOPE]
            dkpe[...] += d_keys[NOPE:]
            dkv[h, NOPE:, :] += dot_nn(dt[j, h], p_ref[h % 2])

        raw(0)
        for h in range(heads):
            if h + 1 < heads:
                raw(h + 1)
            weigh(h)
            if h:
                add(h - 1)
        add(heads - 1)

    def step(r, carry):
        key_block = block_map[lax.rem(r, 2), lax.div(r, 2)]
        kinds = [pair_kind(key_block, own[j], starts, block_rows) for j in range(q_blocks)]
        wanted = functools.reduce(jnp.logical_or, [k[0] for k in kinds])
        here = pl.ds(pl.multiple_of(r * block_rows, block_rows), block_rows)

        @pl.when(wanted)
        def _():
            latent = lat[here, :KVR]
            xr[...] = shared_key_tile(lat[here, KVR : KVR + ROPE], block_rows)
            for first, last in head_groups(heads):
                keys = dot_nn(latent, wkvb[:, first * HEAD : last * HEAD]).astype(jnp.bfloat16)
                for h in range(first, last):
                    xs[h] = keys[:, (h - first) * HEAD : (h - first + 1) * HEAD]
            dkv[...] = jnp.zeros(dkv.shape, jnp.float32)
            dkpe[...] = jnp.zeros(dkpe.shape, jnp.float32)

        for j in range(q_blocks):
            needed, whole = kinds[j]

            @pl.when(needed & whole)
            def _():
                pair(j, False)

            @pl.when(needed & jnp.logical_not(whole))
            def _():
                bias[...] = mask_bias(key_block, own[j], starts, block_rows, False)
                pair(j, True)

        @pl.when(wanted)
        def _():
            latent = lat[here, :KVR]
            d_latent = jnp.zeros((KVR, block_rows), jnp.float32)
            for h in range(heads):
                d_head = jnp.concatenate(
                    [dkv[h, :NOPE, :] * SCORE_SCALE, dkv[h, NOPE:, :]], axis=0
                ).astype(jnp.bfloat16)
                d_latent += dot_nn(wkvb[:, h * HEAD : (h + 1) * HEAD], d_head)
                gsum[h * HEAD : (h + 1) * HEAD, :] += dot_nn(d_head, latent)
            dlat[here, :KVR] = d_latent.T.astype(jnp.bfloat16)
            rope = jnp.concatenate(
                [dkpe[...] * SCORE_SCALE, jnp.zeros((HEAD - ROPE, block_rows), jnp.float32)], axis=0
            )
            dlat[here, KVR:] = rope.T[:, :ROPE].astype(jnp.bfloat16)

        @pl.when(jnp.logical_not(wanted))
        def _():
            dlat[here, :] = jnp.zeros((block_rows, KVR + ROPE), jnp.bfloat16)

        return carry

    lax.fori_loop(0, blocks, step, 0)
    for h in range(heads):
        gkvb[:, h * HEAD : (h + 1) * HEAD] = gsum[h * HEAD : (h + 1) * HEAD, :].T.astype(
            jnp.bfloat16
        )
    for j in range(q_blocks):
        here = pl.ds(j * block_rows, block_rows)
        cos_j, sin_j = cos[here, :], sin[here, :]
        flat[...] = jnp.zeros(flat.shape, jnp.float32)
        for h in range(heads):
            nope = jnp.where(lane < NOPE, dq[j, h, :, :HEAD], 0.0)
            rope = dq[j, h, :, HEAD:]
            shifted = rope * sin_j
            left = pltpu.roll(shifted, HEAD - ROPE // 2, 1)
            right = pltpu.roll(shifted, ROPE // 2, 1)
            swapped = jnp.where(lane < ROPE // 2, left, jnp.where(lane < ROPE, -right, 0.0))
            back = pltpu.roll(jnp.where(lane < ROPE, rope * cos_j + swapped, 0.0), NOPE, 1)
            whole = jnp.concatenate([(nope + back) * SCORE_SCALE, jnp.zeros_like(nope)], axis=1)
            at, shift = head_window(h)
            flat[:, at : at + WIDE] += pltpu.roll(whole, shift, 1)
        dq_out[here, :] = flat[:, : heads * (NOPE + ROPE)].astype(jnp.bfloat16)


def attention_backward(block_map, lengths, qx, qt, u_in, o_in, dob, lat, wkvb, cos, sin):
    q_blocks, heads, block_rows, _ = qx.shape
    blocks = lat.shape[0] // block_rows
    rows = q_blocks * block_rows
    odd = -(heads * VDIM) % HEAD
    if odd:
        o_in = jnp.pad(o_in, ((0, 0), (0, odd)))
        dob = jnp.pad(dob, ((0, 0), (0, odd)))
    vmem = pl.BlockSpec(memory_space=pltpu.VMEM)
    smem = pl.BlockSpec(memory_space=pltpu.SMEM)
    pairs = q_blocks * blocks * heads // 2
    return pl.pallas_call(
        functools.partial(backward_kernel, blocks, heads),
        out_shape=(
            jax.ShapeDtypeStruct((rows, heads * (NOPE + ROPE)), jnp.bfloat16),
            jax.ShapeDtypeStruct((lat.shape[0], KVR + ROPE), jnp.bfloat16),
            jax.ShapeDtypeStruct((KVR, heads * HEAD), jnp.bfloat16),
        ),
        in_specs=[smem] * 2 + [vmem] * 9,
        out_specs=(vmem,) * 3,
        scratch_shapes=[
            pltpu.VMEM((heads, block_rows, HEAD), jnp.bfloat16),
            pltpu.VMEM((block_rows, HEAD), jnp.bfloat16),
            pltpu.VMEM((q_blocks, heads, 2 * block_rows, WIDE), jnp.bfloat16),
            pltpu.VMEM((q_blocks, heads, VDIM, block_rows), jnp.bfloat16),
            pltpu.VMEM((q_blocks, heads, block_rows, WIDE), jnp.float32),
            pltpu.VMEM((heads, HEAD, block_rows), jnp.float32),
            pltpu.VMEM((ROPE, block_rows), jnp.float32),
            pltpu.VMEM((heads * HEAD, KVR), jnp.float32),
            pltpu.VMEM((block_rows, block_rows), jnp.float32),
            pltpu.VMEM((block_rows, window_columns(heads)), jnp.float32),
            pltpu.VMEM((2, 2 * block_rows, block_rows), jnp.float32),
            pltpu.VMEM((2, block_rows, block_rows), jnp.bfloat16),
            pltpu.VMEM((2, block_rows, block_rows), jnp.bfloat16),
        ],
        compiler_params=pltpu.CompilerParams(vmem_limit_bytes=VMEM_LIMIT),
        cost_estimate=pl.CostEstimate(
            flops=pairs * 8 * block_rows * block_rows * WIDE,
            bytes_accessed=24 * 1024 * 1024,
            transcendentals=pairs * block_rows * block_rows,
        ),
        name="attention_backward",
    )(block_map, lengths, qx, qt, u_in, o_in, dob, lat, wkvb, cos, sin)


MESH = pl.DeviceIdType.MESH


class LineSum:
    def __init__(self, n, own, landing, total, sems, lag):
        self.n, self.own, self.landing, self.total, self.lag = n, own, landing, total, lag
        self.up_send, self.up_land, self.down_send, self.back_send, self.down_land = sems
        self.me = lax.axis_index("tp")
        self.root = (n - 1) // 2
        self.chunks = own.shape[0]
        self.has_left, self.has_right = self.me > 0, self.me < n - 1
        self.root_lag = (n - 1 - self.root) * lag
        self.land_lag = 2 * self.root_lag
        self.ticks = self.chunks + self.land_lag

    def greet(self, barrier):
        me = self.me
        for there, other in ((self.has_left, me - 1), (self.has_right, me + 1)):

            @pl.when(there)
            def _(other=other):
                pl.semaphore_signal(barrier, inc=1, device_id={"tp": other}, device_id_type=MESH)

    def wait_greetings(self, barrier, others):
        both = self.has_left & self.has_right

        @pl.when(both)
        def _():
            pl.semaphore_wait(barrier, 2 + others)

        @pl.when(jnp.logical_not(both))
        def _():
            pl.semaphore_wait(barrier, 1 + others)

    def copy_to(self, source, target, send, land, c, other):
        return pltpu.make_async_remote_copy(
            src_ref=source.at[c],
            dst_ref=target.at[c],
            send_sem=send.at[c],
            recv_sem=land.at[c],
            device_id={"tp": other},
            device_id_type=MESH,
        )

    def rise_left(self, c):
        return self.copy_to(self.own, self.landing, self.up_send, self.up_land, c, self.me + 1)

    def rise_right(self, c):
        return self.copy_to(self.own, self.landing, self.up_send, self.up_land, c, self.me - 1)

    def rise_last(self, c):
        return self.copy_to(self.own, self.total, self.up_send, self.down_land, c, self.me - 1)

    def fall_right(self, c):
        return self.copy_to(self.total, self.total, self.down_send, self.down_land, c, self.me + 1)

    def fall_left(self, c):
        return self.copy_to(self.total, self.total, self.back_send, self.down_land, c, self.me - 1)

    def rise(self, c):
        me, root = self.me, self.root
        rises = [(me == root + 1, self.rise_last)]
        if root:
            rises.append((me < root, self.rise_left))
        if self.n - 1 > root + 1:
            rises.append((me > root + 1, self.rise_right))
        for who, copy in rises:

            @pl.when(who)
            def _(copy=copy):
                copy(c).start()

    def inside(self, c):
        return (c >= 0) & (c < self.chunks)

    def added(self, refs, c):
        sums = refs[0][c].astype(jnp.float32)
        for ref in refs[1:]:
            sums = sums + ref[c].astype(jnp.float32)
        return sums.astype(self.total.dtype)

    def leaf(self, c):
        is_leaf = self.me == self.n - 1
        if self.root:
            is_leaf = is_leaf | (self.me == 0)

        @pl.when(is_leaf & self.inside(c))
        def _():
            self.rise(c)

    def leaves(self):
        def body(c, carry):
            self.leaf(c)
            return carry

        lax.fori_loop(0, self.chunks, body, 0)

    def pump(self, first, last):
        def body(t, carry):
            self.duty(t)
            return carry

        lax.fori_loop(first, last, body, 0)

    def duty(self, t):
        me, root = self.me, self.root
        if self.n > 3:
            c = t - self.lag * jnp.where(me < root, me, self.n - 1 - me)

            @pl.when((me != root) & self.has_left & self.has_right & self.inside(c))
            def _():
                self.rise_right(c).wait_recv()
                self.own[c] = self.added([self.own, self.landing], c)
                self.rise(c)

        c_root = t - self.root_lag

        @pl.when((me == root) & self.inside(c_root))
        def _():
            if root:
                self.rise_left(c_root).wait_recv()
            self.fall_right(c_root).wait_recv()
            terms = [self.own, self.landing, self.total] if root else [self.own, self.total]
            self.total[c_root] = self.added(terms, c_root)
            self.fall_right(c_root).start()
            if root:
                self.fall_left(c_root).start()

        c_fall = t - self.root_lag - self.lag * jnp.where(me < root, root - me, me - root)

        @pl.when((me != root) & self.inside(c_fall))
        def _():
            self.fall_right(c_fall).wait_recv()

            @pl.when((me > root) & self.has_right)
            def _():
                self.fall_right(c_fall).start()

            @pl.when((me < root) & self.has_left)
            def _():
                self.fall_left(c_fall).start()

    def landed(self, t):
        return t - self.land_lag

    def drain(self):
        me = self.me

        def body(c, carry):
            @pl.when(me != self.root)
            def _():
                self.rise_right(c).wait_send()

            @pl.when((me >= self.root) & self.has_right)
            def _():
                self.fall_right(c).wait_send()

            @pl.when((me <= self.root) & self.has_left)
            def _():
                self.fall_left(c).wait_send()

            return carry

        lax.fori_loop(0, self.chunks, body, 0)


def line_sems(chunks):
    return [pltpu.SemaphoreType.DMA((chunks,))] * 5


def scatter_blocks(bits_left):
    chips = []
    for value in range(1 << len(bits_left)):
        chip = 0
        for at, bit in enumerate(bits_left):
            chip = chip + (((value >> at) & 1) << (bit - 1))
        chips.append(chip)
    return chips


class Scatter:
    def __init__(self, n, rows, columns, is_given):
        self.n, self.rows, self.columns, self.is_given = n, rows, columns, is_given
        self.count = n.bit_length() - 1
        self.parts = 2 if rows % 32 == 0 else 1

    def scratch(self):
        n, count = self.n, self.count
        half = jnp.bfloat16
        dma = pltpu.SemaphoreType.DMA
        shapes = [pltpu.VMEM((n // 2, self.rows, self.columns), half)]
        if not self.is_given:
            shapes.append(pltpu.VMEM((n // 2, self.rows, self.columns), half))
        for step in range(count - 1):
            shapes.append(pltpu.VMEM((n >> (step + 2), self.rows, self.columns), half))
        shapes += [dma((n // 2,))] * 2
        for step in range(count - 1):
            shapes += [dma((2, n >> (step + 2)))] * 2
        return shapes

    def bind(self, take, source, emit):
        self.held = take(1)[0]
        self.sent = None if self.is_given else take(1)[0]
        self.landed = take(self.count - 1)
        self.core_sems = take(2)
        self.step_sems = [take(2) for _ in range(self.count - 1)]
        self.source, self.emit = source, emit
        self.me = lax.axis_index("ctx")
        self.core = self.me & 1
        self.chips = self.n // 2
        self.orders = (tuple(range(1, self.count)), tuple(range(self.count - 1, 0, -1)))
        self.tiles = [(c, min(c + 512, self.columns)) for c in range(0, self.columns, 512)]
        return self

    def own(self, dest, first, last):
        at = pl.ds(pl.multiple_of(dest * self.rows, 16), self.rows)
        if self.is_given:
            return self.source[at, first:last].astype(jnp.float32)
        return dot_nn(self.source[0][at, :], self.source[1][:, first:last])

    def core_copy(self, chip):
        if self.is_given:
            at = pl.ds(pl.multiple_of((2 * chip + 1 - self.core) * self.rows, 16), self.rows)
            source = self.source.at[at, :]
        else:
            source = self.sent.at[chip]
        return pltpu.make_async_remote_copy(
            src_ref=source,
            dst_ref=self.held.at[chip],
            send_sem=self.core_sems[0].at[chip],
            recv_sem=self.core_sems[1].at[chip],
            device_id={"ctx": self.me ^ 1},
            device_id_type=MESH,
        )

    def step_copies(self, step):
        half = self.rows // self.parts
        me = self.me
        copies = []
        for part, order in enumerate(self.orders[: self.parts]):
            bit = order[step]
            at = pl.ds(part * half, half)
            for slot, free in enumerate(scatter_blocks(sorted(order[step + 1 :]))):
                keep = free + ((me >> bit) & 1) * (1 << (bit - 1))
                send = free + (1 - ((me >> bit) & 1)) * (1 << (bit - 1))
                for b in order[:step]:
                    own = ((me >> b) & 1) * (1 << (b - 1))
                    keep, send = keep + own, send + own
                copy = pltpu.make_async_remote_copy(
                    src_ref=self.held.at[send, at, :],
                    dst_ref=self.landed[step].at[slot, at, :],
                    send_sem=self.step_sems[step][0].at[part, slot],
                    recv_sem=self.step_sems[step][1].at[part, slot],
                    device_id={"ctx": me ^ (1 << bit)},
                    device_id_type=MESH,
                )
                copies.append((copy, keep, slot, at))
        return copies

    def start_core(self, also=None):
        def body(chip, carry):
            if also is not None:
                also(chip)
            if not self.is_given:
                for first, last in self.tiles:
                    self.sent[chip, :, first:last] = self.own(
                        2 * chip + 1 - self.core, first, last
                    ).astype(jnp.bfloat16)
            self.core_copy(chip).start()
            return carry

        lax.fori_loop(0, self.chips, body, 0)

    def finish_core(self, also=None):
        def body(chip, carry):
            if also is not None:
                also(chip)
            self.core_copy(chip).wait_recv()
            for first, last in self.tiles:
                total = self.own(2 * chip + self.core, first, last)
                total = total + self.held[chip, :, first:last].astype(jnp.float32)
                self.held[chip, :, first:last] = total.astype(jnp.bfloat16)
            return carry

        lax.fori_loop(0, self.chips, body, 0)

    def start_step(self, step):
        for copy, _, _, _ in self.step_copies(step):
            copy.start()

    def finish_step(self, step):
        for copy, keep, slot, at in self.step_copies(step):
            copy.wait_recv()
            for first, last in self.tiles:
                total = self.held[keep, at, first:last].astype(jnp.float32)
                total = total + self.landed[step][slot, at, first:last].astype(jnp.float32)
                if step == self.count - 2:
                    self.emit(at, first, last, total)
                else:
                    self.held[keep, at, first:last] = total.astype(jnp.bfloat16)
        if step + 1 < self.count - 1:
            self.start_step(step + 1)

    def drain(self):
        def body(chip, carry):
            self.core_copy(chip).wait_send()
            return carry

        lax.fori_loop(0, self.chips, body, 0)
        for step in range(self.count - 1):
            for copy, _, _, _ in self.step_copies(step):
                copy.wait_send()


def taker(refs):
    refs = list(refs)

    def take(k):
        taken = refs[:k]
        del refs[:k]
        return taken

    return take


def store_in(ref):
    def emit(at, first, last, total):
        ref[at, first:last] = total.astype(ref.dtype)

    return emit


def turn(source, target):
    def body(c, carry):
        at = pl.ds(pl.multiple_of(c * 128, 128), 128)
        target[at, :] = source[:, at].astype(jnp.float32).T.astype(jnp.bfloat16)
        return carry

    lax.fori_loop(0, source.shape[1] // 128, body, 0)


def greet_ctx(n, barrier):
    me = lax.axis_index("ctx")
    count = n.bit_length() - 1
    for bit in range(count):
        pl.semaphore_signal(barrier, inc=1, device_id={"ctx": me ^ (1 << bit)}, device_id_type=MESH)
    return count


def spread(waits, ticks):
    portion = -(-ticks // waits)
    return [(min(k * portion, ticks), min((k + 1) * portion, ticks)) for k in range(waits)]


def gate_up_kernel(n, tp, plans, normed, d_gate, d_up, terms, gate_out, up_out, sums, *refs):
    take = taker(refs)
    own, landing, normed_t = take(3)
    line = LineSum(tp, own, landing, sums, take(5), LAG)
    gate = plans[0].bind(take, (normed_t, d_gate), store_in(gate_out))
    up = plans[1].bind(take, (normed_t, d_up), store_in(up_out))
    barrier = pltpu.get_barrier_semaphore()
    others = greet_ctx(n, barrier)
    line.greet(barrier)
    own[...] = terms[...]
    line.wait_greetings(barrier, others)
    line.leaves()
    turn(normed, normed_t)
    chips = n // 2
    gate.start_core()
    gate.finish_core(line.duty)
    gate.start_step(0)
    up.start_core(lambda chip: line.duty(chips + chip))
    up.finish_core(lambda chip: line.duty(2 * chips + chip))
    up.start_step(0)
    steps = [(item, step) for step in range(gate.count - 1) for item in (gate, up)]
    done = 3 * chips
    for (item, step), (first, last) in zip(steps, spread(len(steps), line.ticks - done)):
        line.pump(done + first, done + last)
        item.finish_step(step)
    for item in (gate, up, line):
        item.drain()


def gate_up_grads(n, tp, normed, d_gate, d_up, terms, collective_id):
    rows, width = normed.shape
    hidden = d_gate.shape[1]
    vmem = pl.BlockSpec(memory_space=pltpu.VMEM)
    half = jnp.bfloat16
    plans = [Scatter(n, width // n, hidden, False) for _ in range(2)]
    chunked = (rows // CHUNK, CHUNK, width)
    gate, up, sums = pl.pallas_call(
        functools.partial(gate_up_kernel, n, tp, plans),
        out_shape=(
            jax.ShapeDtypeStruct((width // n, hidden), half),
            jax.ShapeDtypeStruct((width // n, hidden), half),
            jax.ShapeDtypeStruct(chunked, half),
        ),
        in_specs=[vmem] * 4,
        out_specs=(vmem,) * 3,
        scratch_shapes=[
            pltpu.VMEM(chunked, half),
            pltpu.VMEM(chunked, half),
            pltpu.VMEM((width, rows), half),
            *line_sems(rows // CHUNK),
            *plans[0].scratch(),
            *plans[1].scratch(),
        ],
        compiler_params=pltpu.CompilerParams(
            vmem_limit_bytes=MIDDLE_VMEM, collective_id=collective_id, has_side_effects=True
        ),
        cost_estimate=pl.CostEstimate(
            flops=4 * rows * width * hidden, bytes_accessed=16 * 1024 * 1024, transcendentals=0
        ),
        name=f"gate_up_grads_{collective_id}",
    )(normed, d_gate, d_up, terms.reshape(chunked))
    return gate, up, sums.reshape(rows, width)


TAIL_CHUNK = 64


def up_tail_kernel(
    n, tp, plans, d_lat, d_query, w_qb, g_kvb, d_attn, ob, q_latent, d_feed, act,
    sum_q, sum_lat, down_out, out_out, qb_out, kvb_out, *refs,
):
    take = taker(refs)
    own_q, land_q, own_lat, land_lat, d_attn_t, q_latent_t, d_feed_t = take(7)
    line_q = LineSum(tp, own_q, land_q, sum_q, take(5), LAG)
    line_lat = LineSum(tp, own_lat, land_lat, sum_lat, take(5), LAG)
    chunk = own_q.shape[1]

    def store_lat(at, first, last, total):
        for k in range(at.size // chunk):
            own_lat[at.start // chunk + k, :, first:last] = total[
                k * chunk : (k + 1) * chunk
            ].astype(jnp.bfloat16)

    lat, down, out, qb, kvb = plans
    lat.bind(take, d_lat, store_lat)
    down.bind(take, (d_feed_t, act), store_in(down_out))
    out.bind(take, (d_attn_t, ob), store_in(out_out))
    qb.bind(take, (q_latent_t, d_query), store_in(qb_out))
    kvb.bind(take, g_kvb, store_in(kvb_out))
    barrier = pltpu.get_barrier_semaphore()
    others = greet_ctx(n, barrier)
    line_q.greet(barrier)
    line_q.wait_greetings(barrier, others)
    lat.start_core()

    def query(c, carry):
        rows = pl.ds(pl.multiple_of(c * 2 * chunk, 2 * chunk), 2 * chunk)
        part = dot_nn(d_query[rows, :], w_qb[...]).astype(jnp.bfloat16)
        for k in range(2):
            own_q[2 * c + k] = part[k * chunk : (k + 1) * chunk]
            line_q.leaf(2 * c + k)
        return carry

    lax.fori_loop(0, own_q.shape[0] // 2, query, 0)
    lat.finish_core()
    lat.start_step(0)
    turn(d_feed, d_feed_t)
    down.start_core()
    lat.finish_step(0)
    down.finish_core()
    for step in range(1, lat.count - 1):
        lat.finish_step(step)
    line_lat.leaves()
    down.start_step(0)
    chips = n // 2
    turn(d_attn, d_attn_t)
    out.start_core(line_q.duty)
    out.finish_core(lambda chip: line_q.duty(chips + chip))
    out.start_step(0)
    kvb.start_core()
    turn(q_latent, q_latent_t)
    qb.start_core(lambda chip: line_q.duty(2 * chips + chip))
    kvb.finish_core()
    kvb.start_step(0)
    qb.finish_core(line_lat.duty)
    qb.start_step(0)
    steps = [(item, step) for step in range(lat.count - 1) for item in (down, out, kvb, qb)]
    q_share = spread(len(steps), line_q.ticks - 3 * chips)
    lat_share = spread(len(steps), line_lat.ticks - chips)
    for (item, step), (a, b), (c, d) in zip(steps, q_share, lat_share):
        line_q.pump(3 * chips + a, 3 * chips + b)
        line_lat.pump(chips + c, chips + d)
        item.finish_step(step)
    for item in (*plans, line_q, line_lat):
        item.drain()


def up_tail(n, tp, d_lat, d_query, w_qb, g_kvb, d_attn, ob, q_latent, d_feed, act, collective_id):
    rows, width = d_attn.shape
    rank = q_latent.shape[1]
    hidden = act.shape[1]
    lat_width = d_lat.shape[1]
    vmem = pl.BlockSpec(memory_space=pltpu.VMEM)
    half = jnp.bfloat16
    plans = [
        Scatter(n, rows, lat_width, True),
        Scatter(n, width // n, hidden, False),
        Scatter(n, width // n, ob.shape[1], False),
        Scatter(n, rank // n, d_query.shape[1], False),
        Scatter(n, KVR // n, g_kvb.shape[1], True),
    ]
    q_shape = (rows // TAIL_CHUNK, TAIL_CHUNK, rank)
    lat_shape = (rows // TAIL_CHUNK, TAIL_CHUNK, lat_width)
    sum_q, sum_lat, *grads = pl.pallas_call(
        functools.partial(up_tail_kernel, n, tp, plans),
        out_shape=(
            jax.ShapeDtypeStruct(q_shape, half),
            jax.ShapeDtypeStruct(lat_shape, half),
            *[jax.ShapeDtypeStruct((plan.rows, plan.columns), half) for plan in plans[1:]],
        ),
        in_specs=[vmem] * 9,
        out_specs=(vmem,) * 6,
        scratch_shapes=[
            pltpu.VMEM(q_shape, half),
            pltpu.VMEM(q_shape, half),
            pltpu.VMEM(lat_shape, half),
            pltpu.VMEM(lat_shape, half),
            pltpu.VMEM((width, rows), half),
            pltpu.VMEM((rank, rows), half),
            pltpu.VMEM((width, rows), half),
            *line_sems(rows // TAIL_CHUNK),
            *line_sems(rows // TAIL_CHUNK),
            *[shape for plan in plans for shape in plan.scratch()],
        ],
        compiler_params=pltpu.CompilerParams(
            vmem_limit_bytes=MIDDLE_VMEM, collective_id=collective_id, has_side_effects=True
        ),
        cost_estimate=pl.CostEstimate(
            flops=2 * rows * width * (hidden + ob.shape[1]) + 4 * rows * rank * d_query.shape[1],
            bytes_accessed=32 * 1024 * 1024,
            transcendentals=0,
        ),
        name=f"up_tail_{collective_id}",
    )(d_lat, d_query, w_qb, g_kvb, d_attn, ob, q_latent, d_feed, act)
    return sum_q.reshape(rows, rank), sum_lat.reshape(rows, lat_width), *grads


def down_tail_kernel(
    n, plans, sum_q, sum_lat, q_pre, lat_raw, tokens, d_middle, gain_row, g_mid, w_qa, w_kva, cos, sin, grad_in, qa_out, kva_out, gains_out,
    d_q, d_kv, normed_t, scales, g_in, g_q, g_kv, packed, packing, mid_slots, grad_slots, in_sems, out_sems,
    *refs,
):
    take = taker(refs)
    qa, kva, gains = plans
    qa.bind(take, (normed_t, d_q), store_in(qa_out))
    kva.bind(take, (normed_t, d_kv), store_in(kva_out))
    gains.bind(take, packed, store_in(gains_out))
    rows = tokens.shape[0]
    block = rows // 4
    gain_in, _, gain_q, gain_kv = split_gains(gain_row, tokens.shape[1], q_pre.shape[1])
    lane = lax.broadcasted_iota(jnp.int32, (block, HEAD), 1)
    barrier = pltpu.get_barrier_semaphore()
    others = greet_ctx(n, barrier)

    def rows_of(k):
        return pl.ds(pl.multiple_of(k * block, block), block)

    def fetch(k, slot):
        return pltpu.make_async_copy(
            d_middle.at[rows_of(k), :], mid_slots.at[slot], in_sems.at[slot]
        )

    def deliver(k, slot):
        return pltpu.make_async_copy(
            grad_slots.at[slot], grad_in.at[rows_of(k), :], out_sems.at[slot]
        )

    fetch(0, 0).start()
    fetch(1, 1).start()
    for ref in (g_in, g_q, g_kv):
        ref[...] = jnp.zeros(ref.shape, jnp.float32)

    def norms(k, carry):
        at = rows_of(k)
        pre = q_pre[at, :]
        d_pre, terms = norm_back(
            sum_q[at, :].astype(jnp.float32), pre, norm_scale(pre), gain_q
        )
        g_q[...] += terms
        d_q[at, :] = d_pre.astype(jnp.bfloat16)
        raw = lat_raw[at, :]
        d_raw, terms = norm_back(
            sum_lat[at, :KVR].astype(jnp.float32), raw, norm_scale(raw), gain_kv
        )
        g_kv[...] += terms
        d_kv[at, :KVR] = d_raw.astype(jnp.bfloat16)
        rope = sum_lat[at, KVR:].astype(jnp.float32)
        rope = jnp.concatenate([rope, jnp.zeros((block, HEAD - ROPE), jnp.float32)], axis=1)
        rope = rope_tile_back(rope, cos[at, :], sin[at, :], lane)
        d_kv[at, KVR:] = rope[:, :ROPE].astype(jnp.bfloat16)
        values = tokens[at, :].astype(jnp.float32)
        scale = norm_scale(values)
        scales[at, :] = jnp.broadcast_to(scale, (block, HEAD))
        normed = values * scale * gain_in
        for c in range(0, normed.shape[1], 128):
            normed_t[c : c + 128, at] = normed[:, c : c + 128].T.astype(jnp.bfloat16)
        return carry

    lax.fori_loop(0, 4, norms, 0)
    pl.semaphore_wait(barrier, others)
    qa.start_core()
    kva.start_core()
    qa.finish_core()
    qa.start_step(0)
    kva.finish_core()
    kva.start_step(0)
    for k in range(4):
        at = pl.ds(k * block, block)
        fetch(k, k % 2).wait()
        if k >= 2:
            deliver(k - 2, k % 2).wait()
        d_normed = dot_nt(d_q[at, :], w_qa[...]) + dot_nn(d_kv[at, :], w_kva[...])
        d_values, terms = norm_back(
            d_normed, tokens[at, :].astype(jnp.float32), scales[at, :1], gain_in
        )
        g_in[...] += terms
        grad_slots[k % 2] = mid_slots[k % 2] + d_values
        deliver(k, k % 2).start()
        if k + 2 < 4:
            fetch(k + 2, k % 2).start()
    packing[...] = jnp.zeros(packing.shape, jnp.float32)
    lines = gains.rows
    at = 0
    for whole in (g_in, g_mid, g_q, g_kv):
        share = whole.shape[1] // n
        piece = 32 if share % 32 == 0 else 16
        for dest in range(n):
            for place in range(0, share, piece):
                row, column = divmod(at + place, HEAD)
                row += dest * lines
                first = dest * share + place
                packing[row : row + 1, column : column + piece] = whole[:, first : first + piece]
        at += share
    packed[...] = packing[...].astype(jnp.bfloat16)
    gains.start_core()
    gains.finish_core()
    gains.start_step(0)
    for step in range(qa.count - 1):
        for item in (qa, kva, gains):
            item.finish_step(step)
    deliver(2, 0).wait()
    deliver(3, 1).wait()
    for item in plans:
        item.drain()


def down_tail(
    n, sum_q, sum_lat, q_pre, lat_raw, tokens, d_middle, gain_row, g_mid, w_qa, w_kva, cos, sin,
    collective_id,
):
    rows, width = tokens.shape
    rank = q_pre.shape[1]
    vmem = pl.BlockSpec(memory_space=pltpu.VMEM)
    anywhere = pl.BlockSpec(memory_space=pl.ANY)
    half, full = jnp.bfloat16, jnp.float32
    dma = pltpu.SemaphoreType.DMA
    share = (2 * width + rank + KVR) // n
    lines = -(-share // (32 * HEAD)) * 32
    plans = [
        Scatter(n, width // n, rank, False),
        Scatter(n, width // n, KVR + ROPE, False),
        Scatter(n, lines, HEAD, True),
    ]
    slots = pltpu.VMEM((2, rows // 4, width), full)
    grad_in, qa, kva, gains = pl.pallas_call(
        functools.partial(down_tail_kernel, n, plans),
        out_shape=(
            jax.ShapeDtypeStruct((rows, width), full),
            *[jax.ShapeDtypeStruct((plan.rows, plan.columns), half) for plan in plans],
        ),
        in_specs=[vmem] * 5 + [anywhere] + [vmem] * 6,
        out_specs=(anywhere, vmem, vmem, vmem),
        scratch_shapes=[
            pltpu.VMEM((rows, rank), half),
            pltpu.VMEM((rows, KVR + ROPE), half),
            pltpu.VMEM((width, rows), half),
            pltpu.VMEM((rows, HEAD), full),
            pltpu.VMEM((1, width), full),
            pltpu.VMEM((1, rank), full),
            pltpu.VMEM((1, KVR), full),
            pltpu.VMEM((n * lines, HEAD), half),
            pltpu.VMEM((n * lines, HEAD), full),
            slots,
            slots,
            dma((2,)),
            dma((2,)),
            *[shape for plan in plans for shape in plan.scratch()],
        ],
        compiler_params=pltpu.CompilerParams(
            vmem_limit_bytes=MIDDLE_VMEM, collective_id=collective_id, has_side_effects=True
        ),
        cost_estimate=pl.CostEstimate(
            flops=4 * rows * width * (rank + KVR + ROPE),
            bytes_accessed=40 * 1024 * 1024,
            transcendentals=rows,
        ),
        name=f"down_tail_{collective_id}",
    )(
        sum_q,
        sum_lat,
        q_pre,
        lat_raw,
        tokens,
        d_middle,
        gain_row,
        g_mid,
        w_qa,
        w_kva,
        cos,
        sin,
    )
    gains = gains.astype(full).reshape(-1)
    ends = [0]
    for size in (width, width, rank, KVR):
        ends.append(ends[-1] + size // n)
    return grad_in, qa, kva, [gains[first:last] for first, last in zip(ends, ends[1:])]


CHUNK = 16
BLOCK = 8 * CHUNK
LAG = 2
MIDDLE_VMEM = 63 * 1024 * 1024


def middle_kernel(
    n, lag, ob, tokens_in, cot_in, gain, w_out, w_gate, w_up, w_down,
    tt_to, d_to, f_to, act_to, dg_to, du_to, h_to, df_to,
    tt, d_out, f_out, act_out, dg_out, du_out, h_out, df_out,
    tokens, cot, own, up, wo, wg, wu, wd, d_acc, f_acc, w_sems, out_sems, *sems,
):
    line = LineSum(n, own, up, tt, sems, lag)
    width = tokens.shape[1]
    hidden = wg.shape[0]
    chunks, chunk = own.shape[:2]
    per_block = BLOCK // chunk
    blocks = chunks // per_block
    block_lag = -(-(per_block + line.land_lag) // per_block)
    tiles = [(c, min(c + 512, width)) for c in range(0, width, 512)]
    quarter = hidden // 4 // 128 * 128
    cuts = [0, quarter, 2 * quarter, 3 * quarter, hidden]
    loads = [
        pltpu.make_async_copy(source, target, w_sems.at[k])
        for k, (source, target) in enumerate(
            (
                (w_out, wo),
                (tokens_in, tokens),
                (cot_in, cot),
                (w_gate, wg),
                (w_up, wu),
                (w_down, wd),
            )
        )
    ]
    kept = ((d_out, d_to), (f_out, f_to), (act_out, act_to), (dg_out, dg_to), (du_out, du_to))
    kept += ((h_out, h_to), (df_out, df_to))

    def keep(b):
        rows = pl.ds(pl.multiple_of(b * BLOCK, BLOCK), BLOCK)
        copies = [
            pltpu.make_async_copy(source.at[rows, :], target.at[rows, :], out_sems.at[k, b])
            for k, (source, target) in enumerate(kept)
        ]
        some = pl.ds(b * per_block, per_block)
        return copies + [
            pltpu.make_async_copy(tt.at[some], tt_to.at[some], out_sems.at[len(kept), b])
        ]

    for load in loads:
        load.start()
    barrier = pltpu.get_barrier_semaphore()
    line.greet(barrier)
    line.wait_greetings(barrier, 0)

    def project(b, carry):
        rows = pl.ds(pl.multiple_of(b * BLOCK, BLOCK), BLOCK)
        for first, last in tiles:
            part = dot_nt(ob[rows, :], wo[first:last, :]).astype(jnp.bfloat16)
            for k in range(per_block):
                own[per_block * b + k, :, first:last] = part[k * chunk : (k + 1) * chunk, :]
        for k in range(per_block):
            line.leaf(per_block * b + k)
        return carry

    def normalize(b, part):
        for k in range(part * per_block // 2, (part + 1) * per_block // 2, 2):
            rows = pl.ds(pl.multiple_of(b * BLOCK + k * chunk, 2 * chunk), 2 * chunk)
            sums = jnp.concatenate([tt[b * per_block + k], tt[b * per_block + k + 1]], axis=0)
            middle = tokens[rows, :].astype(jnp.float32) + RESIDUAL_SCALE * sums.astype(jnp.float32)
            h_out[rows, :] = (middle * norm_scale(middle) * gain[:, width : 2 * width]).astype(jnp.bfloat16)

    def feed(b, i):
        rows = pl.ds(pl.multiple_of(b * BLOCK, BLOCK), BLOCK)
        first, last = cuts[i], cuts[i + 1]
        if i == 0:
            normalize(b, 0)
            normalize(b, 1)
            df_out[rows, :] = (RESIDUAL_SCALE * cot[rows, :].astype(jnp.float32)).astype(
                jnp.bfloat16
            )
        gate = dot_nt(h_out[rows, :], wg[first:last, :])
        upper = dot_nt(h_out[rows, :], wu[first:last, :])
        d_act = dot_nt(df_out[rows, :], wd[first:last, :])
        sig = jax.nn.sigmoid(gate)
        silu = gate * sig
        act_out[rows, first:last] = (silu * upper).astype(jnp.bfloat16)
        dg_out[rows, first:last] = (d_act * upper * sig * (1.0 + gate * (1.0 - sig))).astype(
            jnp.bfloat16
        )
        du_out[rows, first:last] = (d_act * silu).astype(jnp.bfloat16)

    def feed_back(b, i):
        rows = pl.ds(pl.multiple_of(b * BLOCK, BLOCK), BLOCK)
        first, last = cuts[i], cuts[i + 1]
        act, dg, du = (ref[rows, first:last] for ref in (act_out, dg_out, du_out))
        for lo, hi in tiles:
            d_part = dot_nn(dg, wg[first:last, lo:hi]) + dot_nn(du, wu[first:last, lo:hi])
            f_part = dot_nn(act, wd[first:last, lo:hi])
            if i:
                d_part = d_part + d_acc[:, lo:hi]
                f_part = f_part + f_acc[:, lo:hi]
            if i < 3:
                d_acc[:, lo:hi] = d_part
                f_acc[:, lo:hi] = f_part
            else:
                d_out[rows, lo:hi] = d_part.astype(jnp.bfloat16)
                f_out[rows, lo:hi] = f_part.astype(jnp.bfloat16)

    loads[0].wait()
    lax.fori_loop(0, blocks, project, 0)

    def outer(o, carry):
        b = o - block_lag

        @pl.when(b == 0)
        def _():
            for load in loads[1:]:
                load.wait()

        share = per_block // 8
        for i in range(4):
            for step, work in enumerate((feed, feed_back)):

                @pl.when(o * per_block < line.ticks)
                def _(at=(2 * i + step) * share):
                    for k in range(share):
                        line.duty(o * per_block + at + k)

                @pl.when(b >= 0)
                def _(i=i, work=work):
                    work(b, i)

        @pl.when(b >= 0)
        def _():
            for copy in keep(b):
                copy.start()

        return carry

    lax.fori_loop(0, blocks + block_lag, outer, 0)
    line.drain()

    def finish(b, carry):
        for copy in keep(b):
            copy.wait()
        return carry

    lax.fori_loop(0, blocks, finish, 0)


def middle_layer(n, ob, tokens, cot, gains, w_out, w_gate, w_up, w_down, collective_id):
    rows, width = tokens.shape
    hidden = w_gate.shape[0]
    chunks = rows // CHUNK
    vmem = pl.BlockSpec(memory_space=pltpu.VMEM)
    anywhere = pl.BlockSpec(memory_space=pl.ANY)
    half = jnp.bfloat16
    dma = pltpu.SemaphoreType.DMA
    attn, *rest = pl.pallas_call(
        functools.partial(middle_kernel, n, LAG),
        out_shape=(
            jax.ShapeDtypeStruct((chunks, CHUNK, width), half),
            jax.ShapeDtypeStruct((rows, width), half),
            jax.ShapeDtypeStruct((rows, width), half),
            jax.ShapeDtypeStruct((rows, hidden), half),
            jax.ShapeDtypeStruct((rows, hidden), half),
            jax.ShapeDtypeStruct((rows, hidden), half),
            jax.ShapeDtypeStruct((rows, width), half),
            jax.ShapeDtypeStruct((rows, width), half),
        ),
        in_specs=[vmem, anywhere, anywhere, vmem] + [anywhere] * 4,
        out_specs=(anywhere,) * 8,
        scratch_shapes=[
            pltpu.VMEM((chunks, CHUNK, width), half),
            pltpu.VMEM((rows, width), half),
            pltpu.VMEM((rows, width), half),
            pltpu.VMEM((rows, hidden), half),
            pltpu.VMEM((rows, hidden), half),
            pltpu.VMEM((rows, hidden), half),
            pltpu.VMEM((rows, width), half),
            pltpu.VMEM((rows, width), half),
            pltpu.VMEM((rows, width), half),
            pltpu.VMEM((rows, width), half),
            pltpu.VMEM((chunks, CHUNK, width), half),
            pltpu.VMEM((chunks, CHUNK, width), half),
            pltpu.VMEM(w_out.shape, half),
            pltpu.VMEM(w_gate.shape, half),
            pltpu.VMEM(w_up.shape, half),
            pltpu.VMEM(w_down.shape, half),
            pltpu.VMEM((BLOCK, width), jnp.float32),
            pltpu.VMEM((BLOCK, width), jnp.float32),
            dma((6,)),
            dma((8, rows // BLOCK)),
            *line_sems(chunks),
        ],
        compiler_params=pltpu.CompilerParams(
            vmem_limit_bytes=MIDDLE_VMEM, collective_id=collective_id, has_side_effects=True
        ),
        cost_estimate=pl.CostEstimate(
            flops=2 * rows * width * (6 * hidden + ob.shape[1]),
            bytes_accessed=64 * 1024 * 1024,
            transcendentals=rows * hidden,
        ),
        name=f"middle_layer_{collective_id}",
    )(ob, tokens, cot, gains, w_out, w_gate, w_up, w_down)
    return attn.reshape(rows, width), *rest


def norm_scale(values):
    return lax.rsqrt(jnp.mean(values * values, axis=-1, keepdims=True) + EPSILON)


def norm_back(incoming, values, inv_rms, gain_vec):
    weighted = incoming * gain_vec
    mean = jnp.mean(weighted * values, axis=-1, keepdims=True)
    d_values = inv_rms * weighted - values * (inv_rms * inv_rms * inv_rms) * mean
    return d_values, jnp.sum(incoming * values * inv_rms, axis=0, keepdims=True)


def rope_tile(tile, cos, sin, lane):
    left = pltpu.roll(tile, HEAD - ROPE // 2, 1)
    right = pltpu.roll(tile, ROPE // 2, 1)
    swapped = jnp.where(lane < ROPE // 2, -left, right)
    return jnp.where(lane < ROPE, tile * cos + swapped * sin, 0.0)


def rope_tile_back(tile, cos, sin, lane):
    shifted = tile * sin
    left = pltpu.roll(shifted, HEAD - ROPE // 2, 1)
    right = pltpu.roll(shifted, ROPE // 2, 1)
    swapped = jnp.where(lane < ROPE // 2, left, -right)
    return jnp.where(lane < ROPE, tile * cos + swapped, 0.0)


def split_gains(gains, width, rank):
    ends = (0, width, 2 * width, 2 * width + rank, 2 * width + rank + KVR)
    return [gains[:, first:last] for first, last in zip(ends, ends[1:])]


def second_norm_kernel(
    d_sum, attn, tokens, cot, gain, w_out, d_middle, d_attn, d_heads, d_gain
):
    width = tokens.shape[1]
    middle = tokens[...].astype(jnp.float32) + RESIDUAL_SCALE * attn[...].astype(jnp.float32)
    d_norm, gain_terms = norm_back(
        d_sum[...].astype(jnp.float32), middle, norm_scale(middle), gain[:, width : 2 * width]
    )
    total = cot[...].astype(jnp.float32) + d_norm
    d_middle[...] = total
    scaled = (RESIDUAL_SCALE * total).astype(jnp.bfloat16)
    d_attn[...] = scaled
    d_heads[...] = dot_nn(scaled, w_out[...]).astype(jnp.bfloat16)

    @pl.when(pl.program_id(0) == 0)
    def _():
        d_gain[...] = jnp.zeros(d_gain.shape, jnp.float32)

    d_gain[...] += gain_terms


def second_norm_back(d_sum, attn, tokens, cot, gains, w_out):
    rows, width = tokens.shape
    block = rows // 4
    head_width = w_out.shape[1]
    whole = lambda shape: pl.BlockSpec(shape, lambda i: (0, 0))
    tile = lambda columns: pl.BlockSpec((block, columns), lambda i: (i, 0))
    return pl.pallas_call(
        second_norm_kernel,
        grid=(rows // block,),
        out_shape=(
            jax.ShapeDtypeStruct((rows, width), jnp.float32),
            jax.ShapeDtypeStruct((rows, width), jnp.bfloat16),
            jax.ShapeDtypeStruct((rows, head_width), jnp.bfloat16),
            jax.ShapeDtypeStruct((1, width), jnp.float32),
        ),
        in_specs=[tile(width)] * 4 + [whole(gains.shape), whole((width, head_width))],
        out_specs=(tile(width), tile(width), tile(head_width), whole((1, width))),
        compiler_params=pltpu.CompilerParams(vmem_limit_bytes=VMEM_LIMIT),
        cost_estimate=pl.CostEstimate(
            flops=2 * rows * width * head_width,
            bytes_accessed=24 * 1024 * 1024,
            transcendentals=rows,
        ),
        name="second_norm_back",
    )(d_sum, attn, tokens, cot, gains, w_out)


def head_kernel(
    n, block_map, lengths, tokens, gains, rates, w_qa, w_kva, w_qb,
    out, q_latent, q_pre, lat_raw, cos, sin, qx, qt,
    own, normed, w_rope, flat, local_sem, step_sends, step_lands, core_sends, core_lands,
):
    gain_in, _, gain_q, gain_kv = split_gains(gains, tokens.shape[1], w_qa.shape[1])
    heads = qx.shape[1]
    count = n.bit_length() - 1
    me = lax.axis_index("ctx")
    rows = own.shape[0]
    half = rows // 2
    block = rows // 4
    barrier = pltpu.get_barrier_semaphore()
    for bit in range(count):
        pl.semaphore_signal(barrier, inc=1, device_id={"ctx": me ^ (1 << bit)}, device_id_type=MESH)
    orders = (tuple(range(1, count)), tuple(range(count - 1, 0, -1)))
    lane = lax.broadcasted_iota(jnp.int32, (block, HEAD), 1)
    w_rope[...] = jnp.zeros(w_rope.shape, jnp.bfloat16)
    w_rope[:ROPE, :] = w_kva[KVR : KVR + ROPE, :]

    starts = starts_of(lengths)
    places = lax.broadcasted_iota(jnp.int32, (half, HEAD), 0)
    lanes = lax.broadcasted_iota(jnp.int32, (half, HEAD), 1)
    for j in range(2):
        at = pl.ds(j * half, half)
        place = block_map[j, me] * half + places
        angles = (place - begin_of(place, starts)).astype(jnp.float32) * rates[...]
        cos[at, :] = jnp.where(lanes < ROPE, jnp.cos(angles), 0.0)
        sin[at, :] = jnp.where(lanes < ROPE, jnp.sin(angles), 0.0)

    def latents(k, carry):
        at = pl.ds(pl.multiple_of(k * block, block), block)
        values = tokens[at, :].astype(jnp.float32)
        normed[at, :] = (values * norm_scale(values) * gain_in).astype(jnp.bfloat16)
        raw = dot_nt(normed[at, :], w_kva[:KVR, :])
        lat_raw[at, :] = raw
        own[at, :KVR] = (raw * norm_scale(raw) * gain_kv).astype(jnp.bfloat16)
        rope = rope_tile(dot_nt(normed[at, :], w_rope[...]), cos[at, :], sin[at, :], lane)
        own[at, KVR:] = rope[:, :ROPE].astype(jnp.bfloat16)
        return carry

    lax.fori_loop(0, 4, latents, 0)
    pl.semaphore_wait(barrier, count)
    local = pltpu.make_async_copy(own, out.at[me], local_sem)
    local.start()

    def chip_copy(part, step, slot, block, first):
        at = pl.ds(part * half, half)
        return pltpu.make_async_remote_copy(
            src_ref=own.at[at, :] if first else out.at[block, at, :],
            dst_ref=out.at[block, at, :],
            send_sem=step_sends.at[part, step, slot],
            recv_sem=step_lands.at[part, step, slot],
            device_id={"ctx": me ^ (1 << orders[part][step])},
            device_id_type=MESH,
        )

    def core_copy(block, slot, first):
        return pltpu.make_async_remote_copy(
            src_ref=own if first else out.at[block],
            dst_ref=out.at[block],
            send_sem=core_sends.at[slot],
            recv_sem=core_lands.at[slot],
            device_id={"ctx": me ^ 1},
            device_id_type=MESH,
        )

    def query(k, carry):
        at = pl.ds(pl.multiple_of(k * block, block), block)
        pre = dot_nn(normed[at, :], w_qa[...])
        q_pre[at, :] = pre
        q_latent[at, :] = (pre * norm_scale(pre) * gain_q).astype(jnp.bfloat16)
        return carry

    def queries(j):
        here = pl.ds(j * half, half)
        cos_j, sin_j = cos[here, :], sin[here, :]
        width = heads * (NOPE + ROPE)
        for at in range(0, width, WIDE):
            end = min(at + WIDE, width)
            flat[:, at:end] = dot_nt(q_latent[here, :], w_qb[at:end, :])
        for h in range(heads):
            at, shift = head_window(h)
            own_part = pltpu.roll(flat[:, at : at + WIDE], (WIDE - shift) % WIDE, 1)[:, :HEAD]
            nope = jnp.where(lanes < NOPE, own_part, 0.0)
            rope = rope_tile(pltpu.roll(own_part, NOPE, 1), cos_j, sin_j, lanes)
            qx[j, h, :, :HEAD] = nope.astype(jnp.bfloat16)
            qx[j, h, :, HEAD:] = rope.astype(jnp.bfloat16)
            qt[j, h, :NOPE, :] = nope.T[:NOPE, :].astype(jnp.bfloat16)
            qt[j, h, NOPE:, :] = rope.T[:ROPE, :].astype(jnp.bfloat16)

    started = []
    for step in range(count - 1):
        for part, order in enumerate(orders):
            for slot in range(1 << step):
                flips = 0
                for at in range(step):
                    flips |= ((slot >> at) & 1) << order[at]
                copy = chip_copy(part, step, slot, me ^ flips, slot == 0)
                copy.start()
                started.append(copy)
        if step == 0:
            core_copy(me, 0, True).start()
        lax.fori_loop(min(2 * step, 4), min(2 * step + 2, 4) if step < count - 2 else 4, query, 0)
        if step == count - 2:
            queries(0)
        for part, order in enumerate(orders):
            for slot in range(1 << step):
                chip_copy(part, step, slot, me, slot == 0).wait_recv()
    for chip in range(1, n // 2):
        core_copy(me ^ (2 * chip), chip, False).start()
    queries(1)
    for chip in range(n // 2):
        core_copy(me, chip, chip == 0).wait_recv()
    for copy in started:
        copy.wait_send()
    for chip in range(n // 2):
        core_copy(me, chip, chip == 0).wait_send()
    local.wait()


def head_layer(n, block_map, lengths, tokens, gains, w_qa, w_kva, w_qb, collective_id):
    rows, width = tokens.shape
    rank = w_qa.shape[1]
    count = n.bit_length() - 1
    vmem = pl.BlockSpec(memory_space=pltpu.VMEM)
    slots = max(n // 4, 1)
    dma = pltpu.SemaphoreType.DMA
    smem = pl.BlockSpec(memory_space=pltpu.SMEM)
    heads = w_qb.shape[0] // (NOPE + ROPE)
    pairs = (2, heads)
    lane = np.arange(HEAD)
    rates = ROPE_BASE ** (-2.0 * (lane % (ROPE // 2)) / ROPE)
    gathered, *rest = pl.pallas_call(
        functools.partial(head_kernel, n),
        out_shape=(
            jax.ShapeDtypeStruct((n, rows, KVR + ROPE), jnp.bfloat16),
            jax.ShapeDtypeStruct((rows, rank), jnp.bfloat16),
            jax.ShapeDtypeStruct((rows, rank), jnp.float32),
            jax.ShapeDtypeStruct((rows, KVR), jnp.float32),
            jax.ShapeDtypeStruct((rows, HEAD), jnp.float32),
            jax.ShapeDtypeStruct((rows, HEAD), jnp.float32),
            jax.ShapeDtypeStruct((*pairs, rows // 2, WIDE), jnp.bfloat16),
            jax.ShapeDtypeStruct((*pairs, NOPE + ROPE, rows // 2), jnp.bfloat16),
        ),
        in_specs=[smem] * 2 + [vmem] * 6,
        out_specs=(vmem,) * 8,
        scratch_shapes=[
            pltpu.VMEM((rows, KVR + ROPE), jnp.bfloat16),
            pltpu.VMEM((rows, width), jnp.bfloat16),
            pltpu.VMEM((HEAD, width), jnp.bfloat16),
            pltpu.VMEM((rows // 2, window_columns(heads)), jnp.float32),
            dma,
            dma((2, count - 1, slots)),
            dma((2, count - 1, slots)),
            dma((n // 2,)),
            dma((n // 2,)),
        ],
        compiler_params=pltpu.CompilerParams(
            vmem_limit_bytes=VMEM_LIMIT, collective_id=collective_id, has_side_effects=True
        ),
        cost_estimate=pl.CostEstimate(
            flops=2 * rows * width * (rank + KVR + ROPE),
            bytes_accessed=24 * 1024 * 1024,
            transcendentals=rows,
        ),
        name=f"head_layer_{collective_id}",
    )(
        block_map,
        lengths,
        tokens,
        gains,
        jnp.asarray(rates.astype(np.float32).reshape(1, -1)),
        w_qa,
        w_kva,
        w_qb,
    )
    return gathered.reshape(n * rows, -1), *rest


def on_device(
    tokens_in,
    w_qa,
    w_kva,
    w_qb,
    w_kvb,
    w_out,
    w_gate,
    w_up,
    w_down,
    gain_in,
    gain_q,
    gain_kv,
    gain_mid,
    cotangent,
    block_map,
    doc_lengths,
):
    devices = lax.axis_size("ctx")
    block_map = block_map.T
    gains = jnp.concatenate([gain_in, gain_mid, gain_q, gain_kv]).reshape(1, -1)
    latents, q_latent, q_latent_pre, latent_raw, cosine, sine, queries, queries_t = head_layer(
        devices, block_map, doc_lengths, tokens_in, gains, w_qa, w_kva.T, w_qb.T, 0
    )
    attn_f, heads_out, log_totals = attention_forward(
        block_map, doc_lengths, queries, latents, w_kvb
    )
    attention, d_part, feed_part, activation, d_gate, d_up, normed_mid, d_feed = middle_layer(
        lax.axis_size("tp"), heads_out, tokens_in, cotangent, gains, w_out, w_gate.T, w_up.T,
        w_down.T, 5,
    )
    gw_gate, gw_up, d_normed_mid = gate_up_grads(
        devices, lax.axis_size("tp"), normed_mid, d_gate, d_up, d_part, 1
    )
    d_normed_mid, feed_part = lax.optimization_barrier((d_normed_mid, feed_part))
    feed_own = lax.psum_scatter(feed_part, "tp", scatter_dimension=0, tiled=True)
    own_rows = feed_own.shape[0]
    own_at = lax.axis_index("tp") * own_rows
    tokens_own = lax.dynamic_slice_in_dim(tokens_in, own_at, own_rows, 0).astype(jnp.float32)
    attention_own = lax.dynamic_slice_in_dim(attention, own_at, own_rows, 0).astype(jnp.float32)
    middle_own = tokens_own + RESIDUAL_SCALE * attention_own
    out_own = (middle_own + RESIDUAL_SCALE * feed_own.astype(jnp.float32)).astype(jnp.bfloat16)
    d_middle, d_attention, d_heads, d_gain_mid = second_norm_back(
        d_normed_mid, attention, tokens_in, cotangent, gains, w_out
    )
    d_query_pre, d_latents, gw_kvb = attention_backward(
        block_map, doc_lengths, queries, queries_t, log_totals, attn_f, d_heads, latents, w_kvb,
        cosine, sine,
    )
    sum_q, sum_lat, gw_down, gw_out, gw_qb, gw_kvb = up_tail(
        devices, lax.axis_size("tp"), d_latents, d_query_pre, w_qb.T, gw_kvb, d_attention, heads_out,
        q_latent, d_feed, activation, 2,
    )
    sum_q, out_own = lax.optimization_barrier((sum_q, out_own))
    out = lax.all_gather(out_own, "tp", axis=0, tiled=True)
    grad_in, gw_qa, gw_kva, own_gains = down_tail(
        devices, sum_q, sum_lat, q_latent_pre, latent_raw, tokens_in, d_middle, gains,
        d_gain_mid, w_qa, w_kva.T, cosine, sine, 3,
    )
    grads = (gw_qa, gw_kva, gw_qb, gw_kvb, gw_out, gw_gate, gw_up, gw_down)
    return (
        out,
        grad_in,
        *[grad.astype(jnp.float32) for grad in grads],
        own_gains[0],
        own_gains[2],
        own_gains[3],
        own_gains[1],
    )


def solution(mesh):
    return jax.shard_map(
        on_device,
        mesh=mesh,
        in_specs=(
            P("ctx", None),
            P(),
            P(),
            P(None, "tp"),
            P(None, "tp"),
            P(None, "tp"),
            P(None, "tp"),
            P(None, "tp"),
            P(None, "tp"),
            P(),
            P(),
            P(),
            P(),
            P("ctx", None),
            P(),
            P(),
        ),
        out_specs=(
            P("ctx", None),
            P("ctx", None),
            P("ctx", None),
            P("ctx", None),
            P("ctx", "tp"),
            P("ctx", "tp"),
            P("ctx", "tp"),
            P("ctx", "tp"),
            P("ctx", "tp"),
            P("ctx", "tp"),
            P("ctx"),
            P("ctx"),
            P("ctx"),
            P("ctx"),
        ),
        check_vma=False,
    )
```

```python
import functools
import math

import jax
import jax.numpy as jnp
import numpy as np
from jax import lax
from jax.experimental import pallas as pl
from jax.experimental.pallas import tpu as pltpu
from jax.sharding import PartitionSpec as P

KVR = 256
NOPE = 64
ROPE = 32
VDIM = 64
HEAD = NOPE + VDIM
WIDE = 2 * HEAD
MASKED = -1e30
SCORE_SCALE = (NOPE + ROPE) ** (-0.5)
EXP2_SCALE = SCORE_SCALE * math.log2(math.e)
FOLD_AT = 96
SUM_ROWS = 16
VMEM_LIMIT = 56 * 1024 * 1024

EPSILON = 1e-05
ROPE_BASE = 10000.0
RESIDUAL_SCALE = 1.4 / math.sqrt(62.0)


def dot_nn(left_op, right_op):
    return jnp.dot(left_op, right_op, preferred_element_type=jnp.float32)


def dot_nt(left_op, right_op):
    return lax.dot_general(
        left_op, right_op, (((1,), (1,)), ((), ())), preferred_element_type=jnp.float32
    )


def starts_of(lengths):
    starts = [jnp.int32(0)]
    for s in range(lengths.shape[0] - 1):
        starts.append(starts[-1] + lengths[s])
    return starts


def begin_of(place, starts):
    begin = jnp.zeros_like(place)
    for start in starts:
        begin = jnp.where(start <= place, start, begin)
    return begin


def pair_kind(key_block, query_block, starts, block_rows):
    key_first = key_block * block_rows
    query_first = query_block * block_rows
    early = begin_of(query_first, starts)
    late = begin_of(query_first + block_rows - 1, starts)
    needed = (key_block <= query_block) & (key_first + block_rows - 1 >= early)
    whole = (key_block < query_block) & (late <= key_first)
    return needed, whole


def mask_bias(key_block, query_block, starts, block_rows, keys_first):
    key_dim = 0 if keys_first else 1
    shape = (block_rows, block_rows)
    key_place = key_block * block_rows + lax.broadcasted_iota(jnp.int32, shape, key_dim)
    query_place = query_block * block_rows + lax.broadcasted_iota(jnp.int32, shape, 1 - key_dim)
    begin = jnp.zeros(shape, jnp.int32)
    for start in starts:
        begin = jnp.where(start <= query_place, start, begin)
    allowed = (key_place <= query_place) & (key_place >= begin)
    return jnp.where(allowed, 0.0, MASKED)


def shared_key_tile(rope_rows, block_rows):
    place = lax.broadcasted_iota(jnp.int32, (ROPE, HEAD), 0)
    lane = lax.broadcasted_iota(jnp.int32, (ROPE, HEAD), 1)
    eye = jnp.where(place == lane, 1.0, 0.0).astype(jnp.bfloat16)
    tile = dot_nn(rope_rows, eye)
    lanes = lax.broadcasted_iota(jnp.int32, (block_rows, HEAD), 1)
    ones = (lanes >= FOLD_AT) & (lanes < FOLD_AT + 3)
    return jnp.where(ones, 1.0, tile).astype(jnp.bfloat16)


def head_window(h):
    at = h * (NOPE + ROPE)
    return at // HEAD * HEAD, at % HEAD


def window_columns(heads):
    return head_window(heads - 1)[0] + WIDE


def head_groups(heads):
    return [(h, min(h + 2, heads)) for h in range(0, heads, 2)]


def forward_kernel(
    blocks, heads, block_map, lengths, qx, lat, wkvb, o_out, ob_out, u_out,
    wkvt, xs, xr, vt, top, acc, bias, s_ref, p_ref,
):
    block_rows = bias.shape[0]
    q_blocks = qx.shape[0]
    starts = starts_of(lengths)
    own = [block_map[j, lax.axis_index("ctx")] for j in range(q_blocks)]
    for first, last in head_groups(heads):
        wkvt[first * HEAD : last * HEAD, :] = (
            wkvb[:, first * HEAD : last * HEAD].astype(jnp.float32).T.astype(jnp.bfloat16)
        )
    top[...] = jnp.full(top.shape, MASKED, jnp.float32)
    vt[:, VDIM:, :] = jnp.ones((heads, SUM_ROWS, block_rows), jnp.bfloat16)
    acc[...] = jnp.zeros(acc.shape, jnp.float32)

    def pair(j, masked):
        def one(h):
            keys = jnp.concatenate([xs[h], xr[...]], axis=1)
            s_ref[h % 3] = dot_nt(keys, qx[j, h])

        def weigh(h):
            old = top[j, h]
            new = old
            for k in range(0, block_rows, 128):
                part = s_ref[h % 3, k : k + 128, :]
                if masked:
                    part = part + bias[k : k + 128, :]
                    s_ref[h % 3, k : k + 128, :] = part
                new = jnp.maximum(new, jnp.max(part, axis=0, keepdims=True))
            fade = jnp.exp2((old - new) * EXP2_SCALE)
            top[j, h] = new
            for k in range(0, block_rows, 128):
                terms = jnp.exp2((s_ref[h % 3, k : k + 128, :] - new) * EXP2_SCALE)
                p_ref[h % 3, k : k + 128, :] = terms.astype(jnp.bfloat16)
            return fade

        def add(h, fade):
            acc[j, h] = fade * acc[j, h] + dot_nn(vt[h], p_ref[h % 3])

        one(0)
        if heads > 1:
            one(1)
        fades = {}
        for h in range(heads):
            if h + 2 < heads:
                one(h + 2)
            fades[h] = weigh(h)
            if h > 1:
                add(h - 2, fades[h - 2])
        for h in range(max(heads - 2, 0), heads):
            add(h, fades[h])

    def step(r, carry):
        key_block = block_map[lax.rem(r, 2), lax.div(r, 2)]
        kinds = [pair_kind(key_block, own[j], starts, block_rows) for j in range(q_blocks)]
        wanted = functools.reduce(jnp.logical_or, [k[0] for k in kinds])

        @pl.when(wanted)
        def _():
            here = pl.ds(pl.multiple_of(r * block_rows, block_rows), block_rows)
            latent = lat[here, :KVR]
            xr[...] = shared_key_tile(lat[here, KVR : KVR + ROPE], block_rows)
            for first, last in head_groups(heads):
                keys = dot_nn(latent, wkvb[:, first * HEAD : last * HEAD]).astype(jnp.bfloat16)
                values = dot_nt(wkvt[first * HEAD : last * HEAD, :], latent).astype(jnp.bfloat16)
                for h in range(first, last):
                    at = (h - first) * HEAD
                    xs[h] = keys[:, at : at + HEAD]
                    vt[h, :VDIM, :] = values[at + NOPE : at + HEAD, :]

        for j in range(q_blocks):
            needed, whole = kinds[j]

            @pl.when(needed & whole)
            def _():
                pair(j, False)

            @pl.when(needed & jnp.logical_not(whole))
            def _():
                bias[...] = mask_bias(key_block, own[j], starts, block_rows, True)
                pair(j, True)

        return carry

    lax.fori_loop(0, blocks, step, 0)
    for j in range(q_blocks):
        here = pl.ds(j * block_rows, block_rows)
        for first, last in head_groups(heads):
            parts = []
            for h in range(first, last):
                total = acc[j, h, VDIM : VDIM + 1, :]
                parts.append(acc[j, h, :VDIM, :] * (1.0 / total))
                u_out[j, h : h + 1, :] = top[j, h] + jnp.log2(total) * (1.0 / EXP2_SCALE)
            if len(parts) == 1:
                parts.append(jnp.zeros_like(parts[0]))
            both = jnp.concatenate(parts, axis=0).T
            width = (last - first) * VDIM
            o_out[here, first * VDIM : first * VDIM + width] = both[:, :width]
            ob_out[here, first * VDIM : first * VDIM + width] = both[:, :width].astype(jnp.bfloat16)


def attention_forward(block_map, lengths, qx, lat, wkvb):
    q_blocks, heads, block_rows, _ = qx.shape
    blocks = lat.shape[0] // block_rows
    rows = q_blocks * block_rows
    vmem = pl.BlockSpec(memory_space=pltpu.VMEM)
    smem = pl.BlockSpec(memory_space=pltpu.SMEM)
    pairs = q_blocks * blocks * heads // 2
    return pl.pallas_call(
        functools.partial(forward_kernel, blocks, heads),
        out_shape=(
            jax.ShapeDtypeStruct((rows, heads * VDIM), jnp.float32),
            jax.ShapeDtypeStruct((rows, heads * VDIM), jnp.bfloat16),
            jax.ShapeDtypeStruct((q_blocks, 16 * -(-heads // 16), block_rows), jnp.float32),
        ),
        in_specs=[smem] * 2 + [vmem] * 3,
        out_specs=(vmem,) * 3,
        scratch_shapes=[
            pltpu.VMEM((heads * HEAD, KVR), jnp.bfloat16),
            pltpu.VMEM((heads, block_rows, HEAD), jnp.bfloat16),
            pltpu.VMEM((block_rows, HEAD), jnp.bfloat16),
            pltpu.VMEM((heads, VDIM + SUM_ROWS, block_rows), jnp.bfloat16),
            pltpu.VMEM((q_blocks, heads, 1, block_rows), jnp.float32),
            pltpu.VMEM((q_blocks, heads, VDIM + SUM_ROWS, block_rows), jnp.float32),
            pltpu.VMEM((block_rows, block_rows), jnp.float32),
            pltpu.VMEM((3, block_rows, block_rows), jnp.float32),
            pltpu.VMEM((3, block_rows, block_rows), jnp.bfloat16),
        ],
        compiler_params=pltpu.CompilerParams(vmem_limit_bytes=VMEM_LIMIT),
        cost_estimate=pl.CostEstimate(
            flops=pairs * 4 * block_rows * block_rows * WIDE,
            bytes_accessed=16 * 1024 * 1024,
            transcendentals=pairs * block_rows * block_rows,
        ),
        name="attention_forward",
    )(block_map, lengths, qx, lat, wkvb)


def three_terms(column):
    first = column.astype(jnp.bfloat16).astype(jnp.float32)
    rest = column - first
    second = rest.astype(jnp.bfloat16).astype(jnp.float32)
    return first, second, rest - second


def fold_in(tile, column, lane):
    for k, term in enumerate(three_terms(column)):
        tile = jnp.where(lane == FOLD_AT + k, term, tile)
    return tile


def backward_kernel(
    blocks, heads, block_map, lengths, qx, qt, u_in, o_in, dob, lat, wkvb, cos, sin,
    dq_out, dlat, gkvb, xs, xr, qo, dt, dq, dkv, dkpe, gsum, bias, flat, s_ref, p_ref, d_ref,
):
    block_rows = bias.shape[0]
    q_blocks = qx.shape[0]
    starts = starts_of(lengths)
    own = [block_map[j, lax.axis_index("ctx")] for j in range(q_blocks)]
    lane = lax.broadcasted_iota(jnp.int32, (block_rows, HEAD), 1)
    for j in range(q_blocks):
        here = pl.ds(j * block_rows, block_rows)
        logs = u_in[j].T
        for first, last in head_groups(heads):
            d_pair = dob[here, first * VDIM : first * VDIM + HEAD].astype(jnp.float32)
            weighted = d_pair * o_in[here, first * VDIM : first * VDIM + HEAD]
            turned = pltpu.roll(d_pair, VDIM, 1)
            for h in range(first, last):
                mine = lane < VDIM if h == first else lane >= VDIM
                delta = jnp.sum(jnp.where(mine, weighted, 0.0), axis=1, keepdims=True)
                d_head = jnp.where(lane >= VDIM, turned if h == first else d_pair, 0.0)
                q_second = qx[j, h, :, HEAD:].astype(jnp.float32)
                qo[j, h, :block_rows, :HEAD] = qx[j, h, :, :HEAD]
                qo[j, h, :block_rows, HEAD:] = fold_in(q_second, -logs[:, h : h + 1], lane).astype(
                    jnp.bfloat16
                )
                qo[j, h, block_rows:, :HEAD] = d_head.astype(jnp.bfloat16)
                qo[j, h, block_rows:, HEAD:] = fold_in(
                    jnp.zeros((block_rows, HEAD), jnp.float32), -delta, lane
                ).astype(jnp.bfloat16)
                dt[j, h] = d_head.T[VDIM:, :].astype(jnp.bfloat16)
    dq[...] = jnp.zeros(dq.shape, jnp.float32)
    gsum[...] = jnp.zeros(gsum.shape, jnp.float32)

    def pair(j, masked):
        def raw(h):
            keys = jnp.concatenate([xs[h], xr[...]], axis=1)
            s_ref[h % 2] = dot_nt(qo[j, h], keys)

        def weigh(h):
            for k in range(0, block_rows, 128):
                scores = s_ref[h % 2, k : k + 128, :] * EXP2_SCALE
                if masked:
                    scores = scores + bias[k : k + 128, :]
                probs = jnp.exp2(scores)
                p_ref[h % 2, k : k + 128, :] = probs.astype(jnp.bfloat16)
                d_ref[h % 2, k : k + 128, :] = (
                    probs * s_ref[h % 2, block_rows + k : block_rows + k + 128, :]
                ).astype(jnp.bfloat16)

        def add(h):
            keys = jnp.concatenate([xs[h], xr[...]], axis=1)
            d_scores = d_ref[h % 2]
            dq[j, h] += dot_nn(d_scores, keys)
            d_keys = dot_nn(qt[j, h], d_scores)
            dkv[h, :NOPE, :] += d_keys[:NOPE]
            dkpe[...] += d_keys[NOPE:]
            dkv[h, NOPE:, :] += dot_nn(dt[j, h], p_ref[h % 2])

        raw(0)
        for h in range(heads):
            if h + 1 < heads:
                raw(h + 1)
            weigh(h)
            if h:
                add(h - 1)
        add(heads - 1)

    def step(r, carry):
        key_block = block_map[lax.rem(r, 2), lax.div(r, 2)]
        kinds = [pair_kind(key_block, own[j], starts, block_rows) for j in range(q_blocks)]
        wanted = functools.reduce(jnp.logical_or, [k[0] for k in kinds])
        here = pl.ds(pl.multiple_of(r * block_rows, block_rows), block_rows)

        @pl.when(wanted)
        def _():
            latent = lat[here, :KVR]
            xr[...] = shared_key_tile(lat[here, KVR : KVR + ROPE], block_rows)
            for first, last in head_groups(heads):
                keys = dot_nn(latent, wkvb[:, first * HEAD : last * HEAD]).astype(jnp.bfloat16)
                for h in range(first, last):
                    xs[h] = keys[:, (h - first) * HEAD : (h - first + 1) * HEAD]
            dkv[...] = jnp.zeros(dkv.shape, jnp.float32)
            dkpe[...] = jnp.zeros(dkpe.shape, jnp.float32)

        for j in range(q_blocks):
            needed, whole = kinds[j]

            @pl.when(needed & whole)
            def _():
                pair(j, False)

            @pl.when(needed & jnp.logical_not(whole))
            def _():
                bias[...] = mask_bias(key_block, own[j], starts, block_rows, False)
                pair(j, True)

        @pl.when(wanted)
        def _():
            latent = lat[here, :KVR]
            d_latent = jnp.zeros((KVR, block_rows), jnp.float32)
            for h in range(heads):
                d_head = jnp.concatenate(
                    [dkv[h, :NOPE, :] * SCORE_SCALE, dkv[h, NOPE:, :]], axis=0
                ).astype(jnp.bfloat16)
                d_latent += dot_nn(wkvb[:, h * HEAD : (h + 1) * HEAD], d_head)
                gsum[h * HEAD : (h + 1) * HEAD, :] += dot_nn(d_head, latent)
            dlat[here, :KVR] = d_latent.T.astype(jnp.bfloat16)
            rope = jnp.concatenate(
                [dkpe[...] * SCORE_SCALE, jnp.zeros((HEAD - ROPE, block_rows), jnp.float32)], axis=0
            )
            dlat[here, KVR:] = rope.T[:, :ROPE].astype(jnp.bfloat16)

        @pl.when(jnp.logical_not(wanted))
        def _():
            dlat[here, :] = jnp.zeros((block_rows, KVR + ROPE), jnp.bfloat16)

        return carry

    lax.fori_loop(0, blocks, step, 0)
    for h in range(heads):
        gkvb[:, h * HEAD : (h + 1) * HEAD] = gsum[h * HEAD : (h + 1) * HEAD, :].T.astype(
            jnp.bfloat16
        )
    for j in range(q_blocks):
        here = pl.ds(j * block_rows, block_rows)
        cos_j, sin_j = cos[here, :], sin[here, :]
        flat[...] = jnp.zeros(flat.shape, jnp.float32)
        for h in range(heads):
            nope = jnp.where(lane < NOPE, dq[j, h, :, :HEAD], 0.0)
            rope = dq[j, h, :, HEAD:]
            shifted = rope * sin_j
            left = pltpu.roll(shifted, HEAD - ROPE // 2, 1)
            right = pltpu.roll(shifted, ROPE // 2, 1)
            swapped = jnp.where(lane < ROPE // 2, left, jnp.where(lane < ROPE, -right, 0.0))
            back = pltpu.roll(jnp.where(lane < ROPE, rope * cos_j + swapped, 0.0), NOPE, 1)
            whole = jnp.concatenate([(nope + back) * SCORE_SCALE, jnp.zeros_like(nope)], axis=1)
            at, shift = head_window(h)
            flat[:, at : at + WIDE] += pltpu.roll(whole, shift, 1)
        dq_out[here, :] = flat[:, : heads * (NOPE + ROPE)].astype(jnp.bfloat16)


def attention_backward(block_map, lengths, qx, qt, u_in, o_in, dob, lat, wkvb, cos, sin):
    q_blocks, heads, block_rows, _ = qx.shape
    blocks = lat.shape[0] // block_rows
    rows = q_blocks * block_rows
    odd = -(heads * VDIM) % HEAD
    if odd:
        o_in = jnp.pad(o_in, ((0, 0), (0, odd)))
        dob = jnp.pad(dob, ((0, 0), (0, odd)))
    vmem = pl.BlockSpec(memory_space=pltpu.VMEM)
    smem = pl.BlockSpec(memory_space=pltpu.SMEM)
    pairs = q_blocks * blocks * heads // 2
    return pl.pallas_call(
        functools.partial(backward_kernel, blocks, heads),
        out_shape=(
            jax.ShapeDtypeStruct((rows, heads * (NOPE + ROPE)), jnp.bfloat16),
            jax.ShapeDtypeStruct((lat.shape[0], KVR + ROPE), jnp.bfloat16),
            jax.ShapeDtypeStruct((KVR, heads * HEAD), jnp.bfloat16),
        ),
        in_specs=[smem] * 2 + [vmem] * 9,
        out_specs=(vmem,) * 3,
        scratch_shapes=[
            pltpu.VMEM((heads, block_rows, HEAD), jnp.bfloat16),
            pltpu.VMEM((block_rows, HEAD), jnp.bfloat16),
            pltpu.VMEM((q_blocks, heads, 2 * block_rows, WIDE), jnp.bfloat16),
            pltpu.VMEM((q_blocks, heads, VDIM, block_rows), jnp.bfloat16),
            pltpu.VMEM((q_blocks, heads, block_rows, WIDE), jnp.float32),
            pltpu.VMEM((heads, HEAD, block_rows), jnp.float32),
            pltpu.VMEM((ROPE, block_rows), jnp.float32),
            pltpu.VMEM((heads * HEAD, KVR), jnp.float32),
            pltpu.VMEM((block_rows, block_rows), jnp.float32),
            pltpu.VMEM((block_rows, window_columns(heads)), jnp.float32),
            pltpu.VMEM((2, 2 * block_rows, block_rows), jnp.float32),
            pltpu.VMEM((2, block_rows, block_rows), jnp.bfloat16),
            pltpu.VMEM((2, block_rows, block_rows), jnp.bfloat16),
        ],
        compiler_params=pltpu.CompilerParams(vmem_limit_bytes=VMEM_LIMIT),
        cost_estimate=pl.CostEstimate(
            flops=pairs * 8 * block_rows * block_rows * WIDE,
            bytes_accessed=24 * 1024 * 1024,
            transcendentals=pairs * block_rows * block_rows,
        ),
        name="attention_backward",
    )(block_map, lengths, qx, qt, u_in, o_in, dob, lat, wkvb, cos, sin)


MESH = pl.DeviceIdType.MESH


class LineSum:
    def __init__(self, n, own, landing, total, sems, lag):
        self.n, self.own, self.landing, self.total, self.lag = n, own, landing, total, lag
        self.up_send, self.up_land, self.down_send, self.back_send, self.down_land = sems
        self.me = lax.axis_index("tp")
        self.root = (n - 1) // 2
        self.chunks = own.shape[0]
        self.has_left, self.has_right = self.me > 0, self.me < n - 1
        self.root_lag = (n - 1 - self.root) * lag
        self.land_lag = 2 * self.root_lag
        self.ticks = self.chunks + self.land_lag

    def greet(self, barrier):
        me = self.me
        for there, other in ((self.has_left, me - 1), (self.has_right, me + 1)):

            @pl.when(there)
            def _(other=other):
                pl.semaphore_signal(barrier, inc=1, device_id={"tp": other}, device_id_type=MESH)

    def wait_greetings(self, barrier, others):
        both = self.has_left & self.has_right

        @pl.when(both)
        def _():
            pl.semaphore_wait(barrier, 2 + others)

        @pl.when(jnp.logical_not(both))
        def _():
            pl.semaphore_wait(barrier, 1 + others)

    def copy_to(self, source, target, send, land, c, other):
        return pltpu.make_async_remote_copy(
            src_ref=source.at[c],
            dst_ref=target.at[c],
            send_sem=send.at[c],
            recv_sem=land.at[c],
            device_id={"tp": other},
            device_id_type=MESH,
        )

    def rise_left(self, c):
        return self.copy_to(self.own, self.landing, self.up_send, self.up_land, c, self.me + 1)

    def rise_right(self, c):
        return self.copy_to(self.own, self.landing, self.up_send, self.up_land, c, self.me - 1)

    def rise_last(self, c):
        return self.copy_to(self.own, self.total, self.up_send, self.down_land, c, self.me - 1)

    def fall_right(self, c):
        return self.copy_to(self.total, self.total, self.down_send, self.down_land, c, self.me + 1)

    def fall_left(self, c):
        return self.copy_to(self.total, self.total, self.back_send, self.down_land, c, self.me - 1)

    def rise(self, c):
        me, root = self.me, self.root
        rises = [(me == root + 1, self.rise_last)]
        if root:
            rises.append((me < root, self.rise_left))
        if self.n - 1 > root + 1:
            rises.append((me > root + 1, self.rise_right))
        for who, copy in rises:

            @pl.when(who)
            def _(copy=copy):
                copy(c).start()

    def inside(self, c):
        return (c >= 0) & (c < self.chunks)

    def added(self, refs, c):
        sums = refs[0][c].astype(jnp.float32)
        for ref in refs[1:]:
            sums = sums + ref[c].astype(jnp.float32)
        return sums.astype(self.total.dtype)

    def leaf(self, c):
        is_leaf = self.me == self.n - 1
        if self.root:
            is_leaf = is_leaf | (self.me == 0)

        @pl.when(is_leaf & self.inside(c))
        def _():
            self.rise(c)

    def leaves(self):
        def body(c, carry):
            self.leaf(c)
            return carry

        lax.fori_loop(0, self.chunks, body, 0)

    def pump(self, first, last):
        def body(t, carry):
            self.duty(t)
            return carry

        lax.fori_loop(first, last, body, 0)

    def duty(self, t):
        me, root = self.me, self.root
        if self.n > 3:
            c = t - self.lag * jnp.where(me < root, me, self.n - 1 - me)

            @pl.when((me != root) & self.has_left & self.has_right & self.inside(c))
            def _():
                self.rise_right(c).wait_recv()
                self.own[c] = self.added([self.own, self.landing], c)
                self.rise(c)

        c_root = t - self.root_lag

        @pl.when((me == root) & self.inside(c_root))
        def _():
            if root:
                self.rise_left(c_root).wait_recv()
            self.fall_right(c_root).wait_recv()
            terms = [self.own, self.landing, self.total] if root else [self.own, self.total]
            self.total[c_root] = self.added(terms, c_root)
            self.fall_right(c_root).start()
            if root:
                self.fall_left(c_root).start()

        c_fall = t - self.root_lag - self.lag * jnp.where(me < root, root - me, me - root)

        @pl.when((me != root) & self.inside(c_fall))
        def _():
            self.fall_right(c_fall).wait_recv()

            @pl.when((me > root) & self.has_right)
            def _():
                self.fall_right(c_fall).start()

            @pl.when((me < root) & self.has_left)
            def _():
                self.fall_left(c_fall).start()

    def landed(self, t):
        return t - self.land_lag

    def drain(self):
        me = self.me

        def body(c, carry):
            @pl.when(me != self.root)
            def _():
                self.rise_right(c).wait_send()

            @pl.when((me >= self.root) & self.has_right)
            def _():
                self.fall_right(c).wait_send()

            @pl.when((me <= self.root) & self.has_left)
            def _():
                self.fall_left(c).wait_send()

            return carry

        lax.fori_loop(0, self.chunks, body, 0)


def line_sems(chunks):
    return [pltpu.SemaphoreType.DMA((chunks,))] * 5


def scatter_blocks(bits_left):
    chips = []
    for value in range(1 << len(bits_left)):
        chip = 0
        for at, bit in enumerate(bits_left):
            chip = chip + (((value >> at) & 1) << (bit - 1))
        chips.append(chip)
    return chips


class Scatter:
    def __init__(self, n, rows, columns, is_given):
        self.n, self.rows, self.columns, self.is_given = n, rows, columns, is_given
        self.count = n.bit_length() - 1
        self.parts = 2 if rows % 32 == 0 else 1

    def scratch(self):
        n, count = self.n, self.count
        half = jnp.bfloat16
        dma = pltpu.SemaphoreType.DMA
        shapes = [pltpu.VMEM((n // 2, self.rows, self.columns), half)]
        if not self.is_given:
            shapes.append(pltpu.VMEM((n // 2, self.rows, self.columns), half))
        for step in range(count - 1):
            shapes.append(pltpu.VMEM((n >> (step + 2), self.rows, self.columns), half))
        shapes += [dma((n // 2,))] * 2
        for step in range(count - 1):
            shapes += [dma((2, n >> (step + 2)))] * 2
        return shapes

    def bind(self, take, source, emit):
        self.held = take(1)[0]
        self.sent = None if self.is_given else take(1)[0]
        self.landed = take(self.count - 1)
        self.core_sems = take(2)
        self.step_sems = [take(2) for _ in range(self.count - 1)]
        self.source, self.emit = source, emit
        self.me = lax.axis_index("ctx")
        self.core = self.me & 1
        self.chips = self.n // 2
        self.orders = (tuple(range(1, self.count)), tuple(range(self.count - 1, 0, -1)))
        self.tiles = [(c, min(c + 512, self.columns)) for c in range(0, self.columns, 512)]
        return self

    def own(self, dest, first, last):
        at = pl.ds(pl.multiple_of(dest * self.rows, 16), self.rows)
        if self.is_given:
            return self.source[at, first:last].astype(jnp.float32)
        return dot_nn(self.source[0][at, :], self.source[1][:, first:last])

    def core_copy(self, chip):
        if self.is_given:
            at = pl.ds(pl.multiple_of((2 * chip + 1 - self.core) * self.rows, 16), self.rows)
            source = self.source.at[at, :]
        else:
            source = self.sent.at[chip]
        return pltpu.make_async_remote_copy(
            src_ref=source,
            dst_ref=self.held.at[chip],
            send_sem=self.core_sems[0].at[chip],
            recv_sem=self.core_sems[1].at[chip],
            device_id={"ctx": self.me ^ 1},
            device_id_type=MESH,
        )

    def step_copies(self, step):
        half = self.rows // self.parts
        me = self.me
        copies = []
        for part, order in enumerate(self.orders[: self.parts]):
            bit = order[step]
            at = pl.ds(part * half, half)
            for slot, free in enumerate(scatter_blocks(sorted(order[step + 1 :]))):
                keep = free + ((me >> bit) & 1) * (1 << (bit - 1))
                send = free + (1 - ((me >> bit) & 1)) * (1 << (bit - 1))
                for b in order[:step]:
                    own = ((me >> b) & 1) * (1 << (b - 1))
                    keep, send = keep + own, send + own
                copy = pltpu.make_async_remote_copy(
                    src_ref=self.held.at[send, at, :],
                    dst_ref=self.landed[step].at[slot, at, :],
                    send_sem=self.step_sems[step][0].at[part, slot],
                    recv_sem=self.step_sems[step][1].at[part, slot],
                    device_id={"ctx": me ^ (1 << bit)},
                    device_id_type=MESH,
                )
                copies.append((copy, keep, slot, at))
        return copies

    def start_core(self, also=None):
        def body(chip, carry):
            if also is not None:
                also(chip)
            if not self.is_given:
                for first, last in self.tiles:
                    self.sent[chip, :, first:last] = self.own(
                        2 * chip + 1 - self.core, first, last
                    ).astype(jnp.bfloat16)
            self.core_copy(chip).start()
            return carry

        lax.fori_loop(0, self.chips, body, 0)

    def finish_core(self, also=None):
        def body(chip, carry):
            if also is not None:
                also(chip)
            self.core_copy(chip).wait_recv()
            for first, last in self.tiles:
                total = self.own(2 * chip + self.core, first, last)
                total = total + self.held[chip, :, first:last].astype(jnp.float32)
                self.held[chip, :, first:last] = total.astype(jnp.bfloat16)
            return carry

        lax.fori_loop(0, self.chips, body, 0)

    def start_step(self, step):
        for copy, _, _, _ in self.step_copies(step):
            copy.start()

    def finish_step(self, step):
        for copy, keep, slot, at in self.step_copies(step):
            copy.wait_recv()
            for first, last in self.tiles:
                total = self.held[keep, at, first:last].astype(jnp.float32)
                total = total + self.landed[step][slot, at, first:last].astype(jnp.float32)
                if step == self.count - 2:
                    self.emit(at, first, last, total)
                else:
                    self.held[keep, at, first:last] = total.astype(jnp.bfloat16)
        if step + 1 < self.count - 1:
            self.start_step(step + 1)

    def drain(self):
        def body(chip, carry):
            self.core_copy(chip).wait_send()
            return carry

        lax.fori_loop(0, self.chips, body, 0)
        for step in range(self.count - 1):
            for copy, _, _, _ in self.step_copies(step):
                copy.wait_send()


def taker(refs):
    refs = list(refs)

    def take(k):
        taken = refs[:k]
        del refs[:k]
        return taken

    return take


def store_in(ref):
    def emit(at, first, last, total):
        ref[at, first:last] = total.astype(ref.dtype)

    return emit


def turn(source, target):
    def body(c, carry):
        at = pl.ds(pl.multiple_of(c * 128, 128), 128)
        target[at, :] = source[:, at].astype(jnp.float32).T.astype(jnp.bfloat16)
        return carry

    lax.fori_loop(0, source.shape[1] // 128, body, 0)


def greet_ctx(n, barrier):
    me = lax.axis_index("ctx")
    count = n.bit_length() - 1
    for bit in range(count):
        pl.semaphore_signal(barrier, inc=1, device_id={"ctx": me ^ (1 << bit)}, device_id_type=MESH)
    return count


def spread(waits, ticks):
    portion = -(-ticks // waits)
    return [(min(k * portion, ticks), min((k + 1) * portion, ticks)) for k in range(waits)]


def gate_up_kernel(
    n, tp, plans, normed, d_gate, d_up, terms, tokens, attn, cot, gain_row, w_out,
    gate_out, up_out, d_attn, d_heads, g_mid, *refs,
):
    take = taker(refs)
    own, landing, sums, normed_t, slots, in_sems, own_sem = take(7)
    line = LineSum(tp, own, landing, sums, take(5), LAG)
    gate = plans[0].bind(take, (normed_t, d_gate), store_in(gate_out))
    up = plans[1].bind(take, (normed_t, d_up), store_in(up_out))
    width = normed.shape[1]
    blocks = normed.shape[0] // BLOCK
    per_block = BLOCK // CHUNK
    load = pltpu.make_async_copy(terms, own, own_sem)
    load.start()
    barrier = pltpu.get_barrier_semaphore()
    others = greet_ctx(n, barrier)
    line.greet(barrier)

    def fetch(b):
        rows = pl.ds(b * BLOCK, BLOCK)
        return [
            pltpu.make_async_copy(
                source.at[rows, :], slots.at[b % 2, k], in_sems.at[b % 2, k]
            )
            for k, source in enumerate((tokens, attn, cot))
        ]

    for b in range(min(2, blocks)):
        for copy in fetch(b):
            copy.start()
    g_mid[...] = jnp.zeros(g_mid.shape, jnp.float32)

    def norm(b):
        for copy in fetch(b):
            copy.wait()
        for part in range(0, BLOCK, 2 * CHUNK):
            rows = pl.ds(b * BLOCK + part, 2 * CHUNK)
            here = pl.ds(part, 2 * CHUNK)
            c = b * per_block + part // CHUNK
            incoming = jnp.concatenate([sums[c], sums[c + 1]], axis=0).astype(jnp.float32)
            middle = slots[b % 2, 0, here, :].astype(jnp.float32)
            middle = middle + RESIDUAL_SCALE * slots[b % 2, 1, here, :].astype(jnp.float32)
            d_norm, gain_terms = norm_back(
                incoming, middle, norm_scale(middle), gain_row[:, width : 2 * width]
            )
            g_mid[...] += gain_terms
            total = slots[b % 2, 2, here, :].astype(jnp.float32) + d_norm
            d_attn[rows, :] = (RESIDUAL_SCALE * total).astype(jnp.bfloat16)
        rows = pl.ds(b * BLOCK, BLOCK)
        d_heads[rows, :] = dot_nn(d_attn[rows, :], w_out[...]).astype(jnp.bfloat16)
        if b + 2 < blocks:
            for copy in fetch(b + 2):
                copy.start()

    load.wait()
    line.wait_greetings(barrier, others)
    line.leaves()
    turn(normed, normed_t)
    chips = n // 2
    gate.start_core()
    gate.finish_core(line.duty)
    gate.start_step(0)
    up.start_core(lambda chip: line.duty(chips + chip))
    up.finish_core(lambda chip: line.duty(2 * chips + chip))
    up.start_step(0)
    steps = [(item, step) for step in range(gate.count - 1) for item in (gate, up)]
    done = 3 * chips
    next_block = 0
    for (item, step), (first, last) in zip(steps, spread(len(steps), line.ticks - done)):
        line.pump(done + first, done + last)
        while next_block < blocks and line.landed(done + last - 1) >= (next_block + 1) * per_block - 1:
            norm(next_block)
            next_block += 1
        item.finish_step(step)
    for item in (gate, up, line):
        item.drain()


def gate_up_grads(
    n, tp, normed, d_gate, d_up, terms, tokens, attn, cot, gain_row, w_out, collective_id
):
    rows, width = normed.shape
    hidden = d_gate.shape[1]
    head_width = w_out.shape[1]
    vmem = pl.BlockSpec(memory_space=pltpu.VMEM)
    anywhere = pl.BlockSpec(memory_space=pl.ANY)
    half = jnp.bfloat16
    plans = [Scatter(n, width // n, hidden, False) for _ in range(2)]
    chunked = (rows // CHUNK, CHUNK, width)
    return pl.pallas_call(
        functools.partial(gate_up_kernel, n, tp, plans),
        out_shape=(
            jax.ShapeDtypeStruct((width // n, hidden), half),
            jax.ShapeDtypeStruct((width // n, hidden), half),
            jax.ShapeDtypeStruct((rows, width), half),
            jax.ShapeDtypeStruct((rows, head_width), half),
            jax.ShapeDtypeStruct((1, width), jnp.float32),
        ),
        in_specs=[vmem] * 3 + [anywhere] * 4 + [vmem] * 2,
        out_specs=(vmem,) * 5,
        scratch_shapes=[
            pltpu.VMEM(chunked, half),
            pltpu.VMEM(chunked, half),
            pltpu.VMEM(chunked, half),
            pltpu.VMEM((width, rows), half),
            pltpu.VMEM((2, 3, BLOCK, width), half),
            pltpu.SemaphoreType.DMA((2, 3)),
            pltpu.SemaphoreType.DMA,
            *line_sems(rows // CHUNK),
            *plans[0].scratch(),
            *plans[1].scratch(),
        ],
        compiler_params=pltpu.CompilerParams(
            vmem_limit_bytes=MIDDLE_VMEM, collective_id=collective_id, has_side_effects=True
        ),
        cost_estimate=pl.CostEstimate(
            flops=2 * rows * width * (2 * hidden + head_width),
            bytes_accessed=28 * 1024 * 1024,
            transcendentals=0,
        ),
        name=f"gate_up_grads_{collective_id}",
    )(normed, d_gate, d_up, terms.reshape(chunked), tokens, attn, cot, gain_row, w_out)


class FeedSum:
    def __init__(self, tp, take, at, chunks, terms, tokens, attn, out):
        own, landing, sums, self.tokens, self.attn, sems = take(6)
        self.out = out
        some = pl.ds(at, chunks)
        pairs = ((terms, own), (tokens, self.tokens), (attn, self.attn))
        self.loads = [
            pltpu.make_async_copy(source.at[some], target, sems.at[k])
            for k, (source, target) in enumerate(pairs)
        ]
        self.line = LineSum(tp, own, landing, sums, take(5), LAG)
        self.ticks = self.line.ticks

    def load(self):
        for load in self.loads:
            load.start()

    def begin(self):
        for load in self.loads:
            load.wait()
        self.line.leaves()

    def duty(self, t):
        self.line.duty(t)
        c = self.line.landed(t)

        @pl.when(self.line.inside(c))
        def _():
            both = self.attn[c].astype(jnp.float32) + self.line.total[c].astype(jnp.float32)
            total = self.tokens[c].astype(jnp.float32) + RESIDUAL_SCALE * both
            self.out[c] = total.astype(jnp.bfloat16)

    def pump(self, first, last):
        def body(t, carry):
            self.duty(t)
            return carry

        lax.fori_loop(first, last, body, 0)


def feed_scratch(chunks, width):
    return [pltpu.VMEM((chunks, CHUNK, width), jnp.bfloat16)] * 5 + [
        pltpu.SemaphoreType.DMA((3,)),
        *line_sems(chunks),
    ]


TAIL_CHUNK = 64


def up_tail_kernel(
    n, tp, plans, feed_chunks, d_lat, d_query, w_qb, g_kvb, d_attn, ob, q_latent, d_feed, act,
    f_part, tokens, attn, sum_q, sum_lat, down_out, out_out, qb_out, kvb_out, layer_out, *refs,
):
    take = taker(refs)
    own_q, land_q, own_lat, land_lat, d_attn_t, q_latent_t, d_feed_t = take(7)
    line_q = LineSum(tp, own_q, land_q, sum_q, take(5), LAG)
    line_lat = LineSum(tp, own_lat, land_lat, sum_lat, take(5), LAG)
    feed = FeedSum(tp, take, 0, feed_chunks, f_part, tokens, attn, layer_out)
    feed.load()
    chunk = own_q.shape[1]

    def store_lat(at, first, last, total):
        for k in range(at.size // chunk):
            own_lat[at.start // chunk + k, :, first:last] = total[
                k * chunk : (k + 1) * chunk
            ].astype(jnp.bfloat16)

    lat, down, out, qb, kvb = plans
    lat.bind(take, d_lat, store_lat)
    down.bind(take, (d_feed_t, act), store_in(down_out))
    out.bind(take, (d_attn_t, ob), store_in(out_out))
    qb.bind(take, (q_latent_t, d_query), store_in(qb_out))
    kvb.bind(take, g_kvb, store_in(kvb_out))
    barrier = pltpu.get_barrier_semaphore()
    others = greet_ctx(n, barrier)
    line_q.greet(barrier)
    line_q.wait_greetings(barrier, others)
    lat.start_core()

    def query(c, carry):
        rows = pl.ds(pl.multiple_of(c * 2 * chunk, 2 * chunk), 2 * chunk)
        part = dot_nn(d_query[rows, :], w_qb[...]).astype(jnp.bfloat16)
        for k in range(2):
            own_q[2 * c + k] = part[k * chunk : (k + 1) * chunk]
            line_q.leaf(2 * c + k)
        return carry

    lax.fori_loop(0, own_q.shape[0] // 2, query, 0)
    lat.finish_core()
    lat.start_step(0)
    turn(d_feed, d_feed_t)
    down.start_core()
    lat.finish_step(0)
    down.finish_core()
    for step in range(1, lat.count - 1):
        lat.finish_step(step)
    line_lat.leaves()
    down.start_step(0)
    feed.begin()
    chips = n // 2
    turn(d_attn, d_attn_t)
    out.start_core(line_q.duty)
    out.finish_core(lambda chip: line_q.duty(chips + chip))
    out.start_step(0)
    kvb.start_core()
    turn(q_latent, q_latent_t)
    qb.start_core(lambda chip: line_q.duty(2 * chips + chip))
    kvb.finish_core()
    kvb.start_step(0)
    qb.finish_core(line_lat.duty)
    qb.start_step(0)
    steps = [(item, step) for step in range(lat.count - 1) for item in (down, out, kvb, qb)]
    q_share = spread(len(steps), line_q.ticks - 3 * chips)
    lat_share = spread(len(steps), line_lat.ticks - chips)
    feed_share = spread(len(steps), feed.ticks)
    for (item, step), (a, b), (c, d), (e, f) in zip(steps, q_share, lat_share, feed_share):
        line_q.pump(3 * chips + a, 3 * chips + b)
        line_lat.pump(chips + c, chips + d)
        feed.pump(e, f)
        item.finish_step(step)
    for item in (*plans, line_q, line_lat, feed.line):
        item.drain()


def up_tail(
    n, tp, d_lat, d_query, w_qb, g_kvb, d_attn, ob, q_latent, d_feed, act, f_part, tokens, attn,
    feed_chunks, collective_id,
):
    rows, width = d_attn.shape
    rank = q_latent.shape[1]
    hidden = act.shape[1]
    lat_width = d_lat.shape[1]
    vmem = pl.BlockSpec(memory_space=pltpu.VMEM)
    half = jnp.bfloat16
    plans = [
        Scatter(n, rows, lat_width, True),
        Scatter(n, width // n, hidden, False),
        Scatter(n, width // n, ob.shape[1], False),
        Scatter(n, rank // n, d_query.shape[1], False),
        Scatter(n, KVR // n, g_kvb.shape[1], True),
    ]
    q_shape = (rows // TAIL_CHUNK, TAIL_CHUNK, rank)
    lat_shape = (rows // TAIL_CHUNK, TAIL_CHUNK, lat_width)
    anywhere = pl.BlockSpec(memory_space=pl.ANY)
    chunked = (-1, CHUNK, width)
    sum_q, sum_lat, *grads, layer_out = pl.pallas_call(
        functools.partial(up_tail_kernel, n, tp, plans, feed_chunks),
        out_shape=(
            jax.ShapeDtypeStruct(q_shape, half),
            jax.ShapeDtypeStruct(lat_shape, half),
            *[jax.ShapeDtypeStruct((plan.rows, plan.columns), half) for plan in plans[1:]],
            jax.ShapeDtypeStruct((feed_chunks, CHUNK, width), half),
        ),
        in_specs=[vmem] * 9 + [anywhere] * 3,
        out_specs=(vmem,) * 7,
        scratch_shapes=[
            pltpu.VMEM(q_shape, half),
            pltpu.VMEM(q_shape, half),
            pltpu.VMEM(lat_shape, half),
            pltpu.VMEM(lat_shape, half),
            pltpu.VMEM((width, rows), half),
            pltpu.VMEM((rank, rows), half),
            pltpu.VMEM((width, rows), half),
            *line_sems(rows // TAIL_CHUNK),
            *line_sems(rows // TAIL_CHUNK),
            *feed_scratch(feed_chunks, width),
            *[shape for plan in plans for shape in plan.scratch()],
        ],
        compiler_params=pltpu.CompilerParams(
            vmem_limit_bytes=MIDDLE_VMEM, collective_id=collective_id, has_side_effects=True
        ),
        cost_estimate=pl.CostEstimate(
            flops=2 * rows * width * (hidden + ob.shape[1]) + 4 * rows * rank * d_query.shape[1],
            bytes_accessed=32 * 1024 * 1024,
            transcendentals=0,
        ),
        name=f"up_tail_{collective_id}",
    )(
        d_lat,
        d_query,
        w_qb,
        g_kvb,
        d_attn,
        ob,
        q_latent,
        d_feed,
        act,
        *[array.reshape(chunked) for array in (f_part, tokens, attn)],
    )
    return (
        sum_q.reshape(rows, rank),
        sum_lat.reshape(rows, lat_width),
        *grads,
        layer_out.reshape(-1, width),
    )


def down_tail_kernel(
    n, tp, plans, feed_chunks, sum_q, sum_lat, q_pre, lat_raw, tokens, d_attn, gain_row, g_mid, w_qa,
    w_kva, cos, sin, f_part, tokens_chunked, attn, grad_in, qa_out, kva_out, gains_out, layer_out,
    d_q, d_kv, normed_t, scales, g_in, g_q, g_kv, packed, packing, grad_slots, out_sems, *refs,
):
    take = taker(refs)
    qa, kva, gains = plans
    qa.bind(take, (normed_t, d_q), store_in(qa_out))
    kva.bind(take, (normed_t, d_kv), store_in(kva_out))
    gains.bind(take, packed, store_in(gains_out))
    at = f_part.shape[0] - feed_chunks
    feed = FeedSum(tp, take, at, feed_chunks, f_part, tokens_chunked, attn, layer_out)
    feed.load()
    rows = tokens.shape[0]
    block = rows // 4
    gain_in, _, gain_q, gain_kv = split_gains(gain_row, tokens.shape[1], q_pre.shape[1])
    lane = lax.broadcasted_iota(jnp.int32, (block, HEAD), 1)
    barrier = pltpu.get_barrier_semaphore()
    others = greet_ctx(n, barrier)
    feed.line.greet(barrier)

    def rows_of(k):
        return pl.ds(pl.multiple_of(k * block, block), block)

    def deliver(k, slot):
        return pltpu.make_async_copy(
            grad_slots.at[slot], grad_in.at[rows_of(k), :], out_sems.at[slot]
        )

    feed.line.wait_greetings(barrier, others)
    feed.begin()
    for ref in (g_in, g_q, g_kv):
        ref[...] = jnp.zeros(ref.shape, jnp.float32)

    def norms(k, carry):
        at = rows_of(k)
        pre = q_pre[at, :]
        d_pre, terms = norm_back(
            sum_q[at, :].astype(jnp.float32), pre, norm_scale(pre), gain_q
        )
        g_q[...] += terms
        d_q[at, :] = d_pre.astype(jnp.bfloat16)
        raw = lat_raw[at, :]
        d_raw, terms = norm_back(
            sum_lat[at, :KVR].astype(jnp.float32), raw, norm_scale(raw), gain_kv
        )
        g_kv[...] += terms
        d_kv[at, :KVR] = d_raw.astype(jnp.bfloat16)
        rope = sum_lat[at, KVR:].astype(jnp.float32)
        rope = jnp.concatenate([rope, jnp.zeros((block, HEAD - ROPE), jnp.float32)], axis=1)
        rope = rope_tile_back(rope, cos[at, :], sin[at, :], lane)
        d_kv[at, KVR:] = rope[:, :ROPE].astype(jnp.bfloat16)
        values = tokens[at, :].astype(jnp.float32)
        scale = norm_scale(values)
        scales[at, :] = jnp.broadcast_to(scale, (block, HEAD))
        normed = values * scale * gain_in
        for c in range(0, normed.shape[1], 128):
            normed_t[c : c + 128, at] = normed[:, c : c + 128].T.astype(jnp.bfloat16)
        return carry

    lax.fori_loop(0, 4, norms, 0)
    chips = n // 2
    qa.start_core()
    kva.start_core()
    qa.finish_core()
    qa.start_step(0)
    kva.finish_core(feed.duty)
    kva.start_step(0)
    shares = [(chips + a, chips + b) for a, b in spread(4 + 3, feed.ticks - chips)]
    for k in range(4):
        at = pl.ds(k * block, block)
        feed.pump(*shares[k])
        if k >= 2:
            deliver(k - 2, k % 2).wait()
        d_normed = dot_nt(d_q[at, :], w_qa[...]) + dot_nn(d_kv[at, :], w_kva[...])
        d_values, terms = norm_back(
            d_normed, tokens[at, :].astype(jnp.float32), scales[at, :1], gain_in
        )
        g_in[...] += terms
        d_middle = d_attn[at, :].astype(jnp.float32) * (1.0 / RESIDUAL_SCALE)
        grad_slots[k % 2] = d_middle + d_values
        deliver(k, k % 2).start()
    packing[...] = jnp.zeros(packing.shape, jnp.float32)
    lines = gains.rows
    at = 0
    for whole in (g_in, g_mid, g_q, g_kv):
        share = whole.shape[1] // n
        piece = 32 if share % 32 == 0 else 16
        for dest in range(n):
            for place in range(0, share, piece):
                row, column = divmod(at + place, HEAD)
                row += dest * lines
                first = dest * share + place
                packing[row : row + 1, column : column + piece] = whole[:, first : first + piece]
        at += share
    packed[...] = packing[...].astype(jnp.bfloat16)
    gains.start_core()
    feed.pump(*shares[4])
    gains.finish_core()
    gains.start_step(0)
    feed.pump(*shares[5])
    feed.pump(*shares[6])
    for step in range(qa.count - 1):
        for item in (qa, kva, gains):
            item.finish_step(step)
    deliver(2, 0).wait()
    deliver(3, 1).wait()
    for item in (*plans, feed.line):
        item.drain()


def down_tail(
    n, tp, sum_q, sum_lat, q_pre, lat_raw, tokens, d_attn, gain_row, g_mid, w_qa, w_kva, cos, sin,
    f_part, attn, feed_chunks, collective_id,
):
    rows, width = tokens.shape
    rank = q_pre.shape[1]
    vmem = pl.BlockSpec(memory_space=pltpu.VMEM)
    anywhere = pl.BlockSpec(memory_space=pl.ANY)
    half, full = jnp.bfloat16, jnp.float32
    dma = pltpu.SemaphoreType.DMA
    share = (2 * width + rank + KVR) // n
    lines = -(-share // (32 * HEAD)) * 32
    plans = [
        Scatter(n, width // n, rank, False),
        Scatter(n, width // n, KVR + ROPE, False),
        Scatter(n, lines, HEAD, True),
    ]
    slots = pltpu.VMEM((2, rows // 4, width), full)
    chunked = (-1, CHUNK, width)
    grad_in, qa, kva, gains, layer_out = pl.pallas_call(
        functools.partial(down_tail_kernel, n, tp, plans, feed_chunks),
        out_shape=(
            jax.ShapeDtypeStruct((rows, width), full),
            *[jax.ShapeDtypeStruct((plan.rows, plan.columns), half) for plan in plans],
            jax.ShapeDtypeStruct((feed_chunks, CHUNK, width), half),
        ),
        in_specs=[vmem] * 12 + [anywhere] * 3,
        out_specs=(anywhere, vmem, vmem, vmem, vmem),
        scratch_shapes=[
            pltpu.VMEM((rows, rank), half),
            pltpu.VMEM((rows, KVR + ROPE), half),
            pltpu.VMEM((width, rows), half),
            pltpu.VMEM((rows, HEAD), full),
            pltpu.VMEM((1, width), full),
            pltpu.VMEM((1, rank), full),
            pltpu.VMEM((1, KVR), full),
            pltpu.VMEM((n * lines, HEAD), half),
            pltpu.VMEM((n * lines, HEAD), full),
            slots,
            dma((2,)),
            *[shape for plan in plans for shape in plan.scratch()],
            *feed_scratch(feed_chunks, width),
        ],
        compiler_params=pltpu.CompilerParams(
            vmem_limit_bytes=MIDDLE_VMEM, collective_id=collective_id, has_side_effects=True
        ),
        cost_estimate=pl.CostEstimate(
            flops=4 * rows * width * (rank + KVR + ROPE),
            bytes_accessed=40 * 1024 * 1024,
            transcendentals=rows,
        ),
        name=f"down_tail_{collective_id}",
    )(
        sum_q,
        sum_lat,
        q_pre,
        lat_raw,
        tokens,
        d_attn,
        gain_row,
        g_mid,
        w_qa,
        w_kva,
        cos,
        sin,
        *[array.reshape(chunked) for array in (f_part, tokens, attn)],
    )
    gains = gains.astype(full).reshape(-1)
    ends = [0]
    for size in (width, width, rank, KVR):
        ends.append(ends[-1] + size // n)
    own_gains = [gains[first:last] for first, last in zip(ends, ends[1:])]
    return grad_in, qa, kva, own_gains, layer_out.reshape(-1, width)


CHUNK = 16
BLOCK = 8 * CHUNK
LAG = 2
MIDDLE_VMEM = 63 * 1024 * 1024


def middle_kernel(
    n, lag, ob, tokens_in, cot_in, gain, w_out, w_gate, w_up, w_down,
    tt_to, d_to, f_to, act_to, dg_to, du_to, h_to, df_to,
    tt, d_out, f_out, act_out, dg_out, du_out, h_out, df_out,
    tokens, cot, own, up, wo, wg, wu, wd, d_acc, f_acc, w_sems, out_sems, *sems,
):
    line = LineSum(n, own, up, tt, sems, lag)
    width = tokens.shape[1]
    hidden = wg.shape[0]
    chunks, chunk = own.shape[:2]
    per_block = BLOCK // chunk
    blocks = chunks // per_block
    block_lag = -(-(per_block + line.land_lag) // per_block)
    tiles = [(c, min(c + 512, width)) for c in range(0, width, 512)]
    quarter = hidden // 4 // 128 * 128
    cuts = [0, quarter, 2 * quarter, 3 * quarter, hidden]
    loads = [
        pltpu.make_async_copy(source, target, w_sems.at[k])
        for k, (source, target) in enumerate(
            (
                (w_out, wo),
                (tokens_in, tokens),
                (cot_in, cot),
                (w_gate, wg),
                (w_up, wu),
                (w_down, wd),
            )
        )
    ]
    kept = ((d_out, d_to), (f_out, f_to), (act_out, act_to), (dg_out, dg_to), (du_out, du_to))
    kept += ((h_out, h_to), (df_out, df_to))

    def keep(b):
        rows = pl.ds(pl.multiple_of(b * BLOCK, BLOCK), BLOCK)
        copies = [
            pltpu.make_async_copy(source.at[rows, :], target.at[rows, :], out_sems.at[k, b])
            for k, (source, target) in enumerate(kept)
        ]
        some = pl.ds(b * per_block, per_block)
        return copies + [
            pltpu.make_async_copy(tt.at[some], tt_to.at[some], out_sems.at[len(kept), b])
        ]

    for load in loads:
        load.start()
    barrier = pltpu.get_barrier_semaphore()
    line.greet(barrier)
    line.wait_greetings(barrier, 0)

    def project(b, carry):
        rows = pl.ds(pl.multiple_of(b * BLOCK, BLOCK), BLOCK)
        for first, last in tiles:
            part = dot_nt(ob[rows, :], wo[first:last, :]).astype(jnp.bfloat16)
            for k in range(per_block):
                own[per_block * b + k, :, first:last] = part[k * chunk : (k + 1) * chunk, :]
        for k in range(per_block):
            line.leaf(per_block * b + k)
        return carry

    def normalize(b, part):
        for k in range(part * per_block // 2, (part + 1) * per_block // 2, 2):
            rows = pl.ds(pl.multiple_of(b * BLOCK + k * chunk, 2 * chunk), 2 * chunk)
            sums = jnp.concatenate([tt[b * per_block + k], tt[b * per_block + k + 1]], axis=0)
            middle = tokens[rows, :].astype(jnp.float32) + RESIDUAL_SCALE * sums.astype(jnp.float32)
            h_out[rows, :] = (middle * norm_scale(middle) * gain[:, width : 2 * width]).astype(jnp.bfloat16)

    def feed(b, i):
        rows = pl.ds(pl.multiple_of(b * BLOCK, BLOCK), BLOCK)
        first, last = cuts[i], cuts[i + 1]
        if i == 0:
            normalize(b, 0)
            normalize(b, 1)
            df_out[rows, :] = (RESIDUAL_SCALE * cot[rows, :].astype(jnp.float32)).astype(
                jnp.bfloat16
            )
        gate = dot_nt(h_out[rows, :], wg[first:last, :])
        upper = dot_nt(h_out[rows, :], wu[first:last, :])
        d_act = dot_nt(df_out[rows, :], wd[first:last, :])
        sig = jax.nn.sigmoid(gate)
        silu = gate * sig
        act_out[rows, first:last] = (silu * upper).astype(jnp.bfloat16)
        dg_out[rows, first:last] = (d_act * upper * sig * (1.0 + gate * (1.0 - sig))).astype(
            jnp.bfloat16
        )
        du_out[rows, first:last] = (d_act * silu).astype(jnp.bfloat16)

    def feed_back(b, i):
        rows = pl.ds(pl.multiple_of(b * BLOCK, BLOCK), BLOCK)
        first, last = cuts[i], cuts[i + 1]
        act, dg, du = (ref[rows, first:last] for ref in (act_out, dg_out, du_out))
        for lo, hi in tiles:
            d_part = dot_nn(dg, wg[first:last, lo:hi]) + dot_nn(du, wu[first:last, lo:hi])
            f_part = dot_nn(act, wd[first:last, lo:hi])
            if i:
                d_part = d_part + d_acc[:, lo:hi]
                f_part = f_part + f_acc[:, lo:hi]
            if i < 3:
                d_acc[:, lo:hi] = d_part
                f_acc[:, lo:hi] = f_part
            else:
                d_out[rows, lo:hi] = d_part.astype(jnp.bfloat16)
                f_out[rows, lo:hi] = f_part.astype(jnp.bfloat16)

    loads[0].wait()
    lax.fori_loop(0, blocks, project, 0)

    def outer(o, carry):
        b = o - block_lag

        @pl.when(b == 0)
        def _():
            for load in loads[1:]:
                load.wait()

        share = per_block // 8
        for i in range(4):
            for step, work in enumerate((feed, feed_back)):

                @pl.when(o * per_block < line.ticks)
                def _(at=(2 * i + step) * share):
                    for k in range(share):
                        line.duty(o * per_block + at + k)

                @pl.when(b >= 0)
                def _(i=i, work=work):
                    work(b, i)

        @pl.when(b >= 0)
        def _():
            for copy in keep(b):
                copy.start()

        return carry

    lax.fori_loop(0, blocks + block_lag, outer, 0)
    line.drain()

    def finish(b, carry):
        for copy in keep(b):
            copy.wait()
        return carry

    lax.fori_loop(0, blocks, finish, 0)


def middle_layer(n, ob, tokens, cot, gains, w_out, w_gate, w_up, w_down, collective_id):
    rows, width = tokens.shape
    hidden = w_gate.shape[0]
    chunks = rows // CHUNK
    vmem = pl.BlockSpec(memory_space=pltpu.VMEM)
    anywhere = pl.BlockSpec(memory_space=pl.ANY)
    half = jnp.bfloat16
    dma = pltpu.SemaphoreType.DMA
    attn, *rest = pl.pallas_call(
        functools.partial(middle_kernel, n, LAG),
        out_shape=(
            jax.ShapeDtypeStruct((chunks, CHUNK, width), half),
            jax.ShapeDtypeStruct((rows, width), half),
            jax.ShapeDtypeStruct((rows, width), half),
            jax.ShapeDtypeStruct((rows, hidden), half),
            jax.ShapeDtypeStruct((rows, hidden), half),
            jax.ShapeDtypeStruct((rows, hidden), half),
            jax.ShapeDtypeStruct((rows, width), half),
            jax.ShapeDtypeStruct((rows, width), half),
        ),
        in_specs=[vmem, anywhere, anywhere, vmem] + [anywhere] * 4,
        out_specs=(anywhere,) * 8,
        scratch_shapes=[
            pltpu.VMEM((chunks, CHUNK, width), half),
            pltpu.VMEM((rows, width), half),
            pltpu.VMEM((rows, width), half),
            pltpu.VMEM((rows, hidden), half),
            pltpu.VMEM((rows, hidden), half),
            pltpu.VMEM((rows, hidden), half),
            pltpu.VMEM((rows, width), half),
            pltpu.VMEM((rows, width), half),
            pltpu.VMEM((rows, width), half),
            pltpu.VMEM((rows, width), half),
            pltpu.VMEM((chunks, CHUNK, width), half),
            pltpu.VMEM((chunks, CHUNK, width), half),
            pltpu.VMEM(w_out.shape, half),
            pltpu.VMEM(w_gate.shape, half),
            pltpu.VMEM(w_up.shape, half),
            pltpu.VMEM(w_down.shape, half),
            pltpu.VMEM((BLOCK, width), jnp.float32),
            pltpu.VMEM((BLOCK, width), jnp.float32),
            dma((6,)),
            dma((8, rows // BLOCK)),
            *line_sems(chunks),
        ],
        compiler_params=pltpu.CompilerParams(
            vmem_limit_bytes=MIDDLE_VMEM, collective_id=collective_id, has_side_effects=True
        ),
        cost_estimate=pl.CostEstimate(
            flops=2 * rows * width * (6 * hidden + ob.shape[1]),
            bytes_accessed=64 * 1024 * 1024,
            transcendentals=rows * hidden,
        ),
        name=f"middle_layer_{collective_id}",
    )(ob, tokens, cot, gains, w_out, w_gate, w_up, w_down)
    return attn.reshape(rows, width), *rest


def norm_scale(values):
    return lax.rsqrt(jnp.mean(values * values, axis=-1, keepdims=True) + EPSILON)


def norm_back(incoming, values, inv_rms, gain_vec):
    weighted = incoming * gain_vec
    mean = jnp.mean(weighted * values, axis=-1, keepdims=True)
    d_values = inv_rms * weighted - values * (inv_rms * inv_rms * inv_rms) * mean
    return d_values, jnp.sum(incoming * values * inv_rms, axis=0, keepdims=True)


def rope_tile(tile, cos, sin, lane):
    left = pltpu.roll(tile, HEAD - ROPE // 2, 1)
    right = pltpu.roll(tile, ROPE // 2, 1)
    swapped = jnp.where(lane < ROPE // 2, -left, right)
    return jnp.where(lane < ROPE, tile * cos + swapped * sin, 0.0)


def rope_tile_back(tile, cos, sin, lane):
    shifted = tile * sin
    left = pltpu.roll(shifted, HEAD - ROPE // 2, 1)
    right = pltpu.roll(shifted, ROPE // 2, 1)
    swapped = jnp.where(lane < ROPE // 2, left, -right)
    return jnp.where(lane < ROPE, tile * cos + swapped, 0.0)


def split_gains(gains, width, rank):
    ends = (0, width, 2 * width, 2 * width + rank, 2 * width + rank + KVR)
    return [gains[:, first:last] for first, last in zip(ends, ends[1:])]


def head_kernel(
    n, block_map, lengths, tokens, gains, rates, w_qa, w_kva, w_qb,
    out, q_latent, q_pre, lat_raw, cos, sin, qx, qt,
    own, normed, w_rope, flat, local_sem, step_sends, step_lands, core_sends, core_lands,
):
    gain_in, _, gain_q, gain_kv = split_gains(gains, tokens.shape[1], w_qa.shape[1])
    heads = qx.shape[1]
    count = n.bit_length() - 1
    me = lax.axis_index("ctx")
    rows = own.shape[0]
    half = rows // 2
    block = rows // 4
    barrier = pltpu.get_barrier_semaphore()
    for bit in range(count):
        pl.semaphore_signal(barrier, inc=1, device_id={"ctx": me ^ (1 << bit)}, device_id_type=MESH)
    orders = (tuple(range(1, count)), tuple(range(count - 1, 0, -1)))
    lane = lax.broadcasted_iota(jnp.int32, (block, HEAD), 1)
    w_rope[...] = jnp.zeros(w_rope.shape, jnp.bfloat16)
    w_rope[:ROPE, :] = w_kva[KVR : KVR + ROPE, :]

    starts = starts_of(lengths)
    places = lax.broadcasted_iota(jnp.int32, (half, HEAD), 0)
    lanes = lax.broadcasted_iota(jnp.int32, (half, HEAD), 1)
    for j in range(2):
        at = pl.ds(j * half, half)
        place = block_map[j, me] * half + places
        angles = (place - begin_of(place, starts)).astype(jnp.float32) * rates[...]
        cos[at, :] = jnp.where(lanes < ROPE, jnp.cos(angles), 0.0)
        sin[at, :] = jnp.where(lanes < ROPE, jnp.sin(angles), 0.0)

    def latents(k, carry):
        at = pl.ds(pl.multiple_of(k * block, block), block)
        values = tokens[at, :].astype(jnp.float32)
        normed[at, :] = (values * norm_scale(values) * gain_in).astype(jnp.bfloat16)
        raw = dot_nt(normed[at, :], w_kva[:KVR, :])
        lat_raw[at, :] = raw
        own[at, :KVR] = (raw * norm_scale(raw) * gain_kv).astype(jnp.bfloat16)
        rope = rope_tile(dot_nt(normed[at, :], w_rope[...]), cos[at, :], sin[at, :], lane)
        own[at, KVR:] = rope[:, :ROPE].astype(jnp.bfloat16)
        return carry

    lax.fori_loop(0, 4, latents, 0)
    pl.semaphore_wait(barrier, count)
    local = pltpu.make_async_copy(own, out.at[me], local_sem)
    local.start()

    def chip_copy(part, step, slot, block, first):
        at = pl.ds(part * half, half)
        return pltpu.make_async_remote_copy(
            src_ref=own.at[at, :] if first else out.at[block, at, :],
            dst_ref=out.at[block, at, :],
            send_sem=step_sends.at[part, step, slot],
            recv_sem=step_lands.at[part, step, slot],
            device_id={"ctx": me ^ (1 << orders[part][step])},
            device_id_type=MESH,
        )

    def core_copy(block, slot, first):
        return pltpu.make_async_remote_copy(
            src_ref=own if first else out.at[block],
            dst_ref=out.at[block],
            send_sem=core_sends.at[slot],
            recv_sem=core_lands.at[slot],
            device_id={"ctx": me ^ 1},
            device_id_type=MESH,
        )

    def query(k, carry):
        at = pl.ds(pl.multiple_of(k * block, block), block)
        pre = dot_nn(normed[at, :], w_qa[...])
        q_pre[at, :] = pre
        q_latent[at, :] = (pre * norm_scale(pre) * gain_q).astype(jnp.bfloat16)
        return carry

    def queries(j):
        here = pl.ds(j * half, half)
        cos_j, sin_j = cos[here, :], sin[here, :]
        width = heads * (NOPE + ROPE)
        for at in range(0, width, WIDE):
            end = min(at + WIDE, width)
            flat[:, at:end] = dot_nt(q_latent[here, :], w_qb[at:end, :])
        for h in range(heads):
            at, shift = head_window(h)
            own_part = pltpu.roll(flat[:, at : at + WIDE], (WIDE - shift) % WIDE, 1)[:, :HEAD]
            nope = jnp.where(lanes < NOPE, own_part, 0.0)
            rope = rope_tile(pltpu.roll(own_part, NOPE, 1), cos_j, sin_j, lanes)
            qx[j, h, :, :HEAD] = nope.astype(jnp.bfloat16)
            qx[j, h, :, HEAD:] = rope.astype(jnp.bfloat16)
            qt[j, h, :NOPE, :] = nope.T[:NOPE, :].astype(jnp.bfloat16)
            qt[j, h, NOPE:, :] = rope.T[:ROPE, :].astype(jnp.bfloat16)

    started = []
    for step in range(count - 1):
        for part, order in enumerate(orders):
            for slot in range(1 << step):
                flips = 0
                for at in range(step):
                    flips |= ((slot >> at) & 1) << order[at]
                copy = chip_copy(part, step, slot, me ^ flips, slot == 0)
                copy.start()
                started.append(copy)
        if step == 0:
            core_copy(me, 0, True).start()
        lax.fori_loop(min(2 * step, 4), min(2 * step + 2, 4) if step < count - 2 else 4, query, 0)
        if step == count - 2:
            queries(0)
        for part, order in enumerate(orders):
            for slot in range(1 << step):
                chip_copy(part, step, slot, me, slot == 0).wait_recv()
    for chip in range(1, n // 2):
        core_copy(me ^ (2 * chip), chip, False).start()
    queries(1)
    for chip in range(n // 2):
        core_copy(me, chip, chip == 0).wait_recv()
    for copy in started:
        copy.wait_send()
    for chip in range(n // 2):
        core_copy(me, chip, chip == 0).wait_send()
    local.wait()


def head_layer(n, block_map, lengths, tokens, gains, w_qa, w_kva, w_qb, collective_id):
    rows, width = tokens.shape
    rank = w_qa.shape[1]
    count = n.bit_length() - 1
    vmem = pl.BlockSpec(memory_space=pltpu.VMEM)
    slots = max(n // 4, 1)
    dma = pltpu.SemaphoreType.DMA
    smem = pl.BlockSpec(memory_space=pltpu.SMEM)
    heads = w_qb.shape[0] // (NOPE + ROPE)
    pairs = (2, heads)
    lane = np.arange(HEAD)
    rates = ROPE_BASE ** (-2.0 * (lane % (ROPE // 2)) / ROPE)
    gathered, *rest = pl.pallas_call(
        functools.partial(head_kernel, n),
        out_shape=(
            jax.ShapeDtypeStruct((n, rows, KVR + ROPE), jnp.bfloat16),
            jax.ShapeDtypeStruct((rows, rank), jnp.bfloat16),
            jax.ShapeDtypeStruct((rows, rank), jnp.float32),
            jax.ShapeDtypeStruct((rows, KVR), jnp.float32),
            jax.ShapeDtypeStruct((rows, HEAD), jnp.float32),
            jax.ShapeDtypeStruct((rows, HEAD), jnp.float32),
            jax.ShapeDtypeStruct((*pairs, rows // 2, WIDE), jnp.bfloat16),
            jax.ShapeDtypeStruct((*pairs, NOPE + ROPE, rows // 2), jnp.bfloat16),
        ),
        in_specs=[smem] * 2 + [vmem] * 6,
        out_specs=(vmem,) * 8,
        scratch_shapes=[
            pltpu.VMEM((rows, KVR + ROPE), jnp.bfloat16),
            pltpu.VMEM((rows, width), jnp.bfloat16),
            pltpu.VMEM((HEAD, width), jnp.bfloat16),
            pltpu.VMEM((rows // 2, window_columns(heads)), jnp.float32),
            dma,
            dma((2, count - 1, slots)),
            dma((2, count - 1, slots)),
            dma((n // 2,)),
            dma((n // 2,)),
        ],
        compiler_params=pltpu.CompilerParams(
            vmem_limit_bytes=VMEM_LIMIT, collective_id=collective_id, has_side_effects=True
        ),
        cost_estimate=pl.CostEstimate(
            flops=2 * rows * width * (rank + KVR + ROPE),
            bytes_accessed=24 * 1024 * 1024,
            transcendentals=rows,
        ),
        name=f"head_layer_{collective_id}",
    )(
        block_map,
        lengths,
        tokens,
        gains,
        jnp.asarray(rates.astype(np.float32).reshape(1, -1)),
        w_qa,
        w_kva,
        w_qb,
    )
    return gathered.reshape(n * rows, -1), *rest


def on_device(
    tokens_in,
    w_qa,
    w_kva,
    w_qb,
    w_kvb,
    w_out,
    w_gate,
    w_up,
    w_down,
    gain_in,
    gain_q,
    gain_kv,
    gain_mid,
    cotangent,
    block_map,
    doc_lengths,
):
    devices = lax.axis_size("ctx")
    block_map = block_map.T
    gains = jnp.concatenate([gain_in, gain_mid, gain_q, gain_kv]).reshape(1, -1)
    latents, q_latent, q_latent_pre, latent_raw, cosine, sine, queries, queries_t = head_layer(
        devices, block_map, doc_lengths, tokens_in, gains, w_qa, w_kva.T, w_qb.T, 0
    )
    attn_f, heads_out, log_totals = attention_forward(
        block_map, doc_lengths, queries, latents, w_kvb
    )
    attention, d_part, feed_part, activation, d_gate, d_up, normed_mid, d_feed = middle_layer(
        lax.axis_size("tp"), heads_out, tokens_in, cotangent, gains, w_out, w_gate.T, w_up.T,
        w_down.T, 5,
    )
    gw_gate, gw_up, d_attention, d_heads, d_gain_mid = gate_up_grads(
        devices, lax.axis_size("tp"), normed_mid, d_gate, d_up, d_part, tokens_in, attention,
        cotangent, gains, w_out, 1,
    )
    d_query_pre, d_latents, gw_kvb = attention_backward(
        block_map, doc_lengths, queries, queries_t, log_totals, attn_f, d_heads, latents, w_kvb,
        cosine, sine,
    )
    chunks = tokens_in.shape[0] // CHUNK
    sum_q, sum_lat, gw_down, gw_out, gw_qb, gw_kvb, out_first = up_tail(
        devices, lax.axis_size("tp"), d_latents, d_query_pre, w_qb.T, gw_kvb, d_attention, heads_out,
        q_latent, d_feed, activation, feed_part, tokens_in, attention, chunks // 2, 2,
    )
    grad_in, gw_qa, gw_kva, own_gains, out_second = down_tail(
        devices, lax.axis_size("tp"), sum_q, sum_lat, q_latent_pre, latent_raw, tokens_in,
        d_attention, gains, d_gain_mid, w_qa, w_kva.T, cosine, sine, feed_part, attention,
        chunks - chunks // 2, 3,
    )
    out = jnp.concatenate([out_first, out_second], axis=0)
    grads = (gw_qa, gw_kva, gw_qb, gw_kvb, gw_out, gw_gate, gw_up, gw_down)
    return (
        out,
        grad_in,
        *[grad.astype(jnp.float32) for grad in grads],
        own_gains[0],
        own_gains[2],
        own_gains[3],
        own_gains[1],
    )


def solution(mesh):
    return jax.shard_map(
        on_device,
        mesh=mesh,
        in_specs=(
            P("ctx", None),
            P(),
            P(),
            P(None, "tp"),
            P(None, "tp"),
            P(None, "tp"),
            P(None, "tp"),
            P(None, "tp"),
            P(None, "tp"),
            P(),
            P(),
            P(),
            P(),
            P("ctx", None),
            P(),
            P(),
        ),
        out_specs=(
            P("ctx", None),
            P("ctx", None),
            P("ctx", None),
            P("ctx", None),
            P("ctx", "tp"),
            P("ctx", "tp"),
            P("ctx", "tp"),
            P("ctx", "tp"),
            P("ctx", "tp"),
            P("ctx", "tp"),
            P("ctx"),
            P("ctx"),
            P("ctx"),
            P("ctx"),
        ),
        check_vma=False,
    )
```

```python
import functools
import math

import jax
import jax.numpy as jnp
import numpy as np
from jax import lax
from jax.experimental import pallas as pl
from jax.experimental.pallas import tpu as pltpu
from jax.sharding import PartitionSpec as P

KVR = 256
NOPE = 64
ROPE = 32
VDIM = 64
HEAD = NOPE + VDIM
WIDE = 2 * HEAD
MASKED = -1e30
SCORE_SCALE = (NOPE + ROPE) ** (-0.5)
EXP2_SCALE = SCORE_SCALE * math.log2(math.e)
FOLD_AT = 96
SUM_ROWS = 16
VMEM_LIMIT = 56 * 1024 * 1024

EPSILON = 1e-05
ROPE_BASE = 10000.0
RESIDUAL_SCALE = 1.4 / math.sqrt(62.0)


def dot_nn(left_op, right_op):
    return jnp.dot(left_op, right_op, preferred_element_type=jnp.float32)


def dot_nt(left_op, right_op):
    return lax.dot_general(
        left_op, right_op, (((1,), (1,)), ((), ())), preferred_element_type=jnp.float32
    )


def starts_of(lengths):
    starts = [jnp.int32(0)]
    for s in range(lengths.shape[0] - 1):
        starts.append(starts[-1] + lengths[s])
    return starts


def begin_of(place, starts):
    begin = jnp.zeros_like(place)
    for start in starts:
        begin = jnp.where(start <= place, start, begin)
    return begin


def pair_kind(key_block, query_block, starts, block_rows):
    key_first = key_block * block_rows
    query_first = query_block * block_rows
    early = begin_of(query_first, starts)
    late = begin_of(query_first + block_rows - 1, starts)
    needed = (key_block <= query_block) & (key_first + block_rows - 1 >= early)
    whole = (key_block < query_block) & (late <= key_first)
    return needed, whole


def mask_bias(key_block, query_block, starts, block_rows, keys_first):
    key_dim = 0 if keys_first else 1
    shape = (block_rows, block_rows)
    key_place = key_block * block_rows + lax.broadcasted_iota(jnp.int32, shape, key_dim)
    query_place = query_block * block_rows + lax.broadcasted_iota(jnp.int32, shape, 1 - key_dim)
    begin = jnp.zeros(shape, jnp.int32)
    for start in starts:
        begin = jnp.where(start <= query_place, start, begin)
    allowed = (key_place <= query_place) & (key_place >= begin)
    return jnp.where(allowed, 0.0, MASKED)


def shared_key_tile(rope_rows, block_rows):
    place = lax.broadcasted_iota(jnp.int32, (ROPE, HEAD), 0)
    lane = lax.broadcasted_iota(jnp.int32, (ROPE, HEAD), 1)
    eye = jnp.where(place == lane, 1.0, 0.0).astype(jnp.bfloat16)
    tile = dot_nn(rope_rows, eye)
    lanes = lax.broadcasted_iota(jnp.int32, (block_rows, HEAD), 1)
    ones = (lanes >= FOLD_AT) & (lanes < FOLD_AT + 3)
    return jnp.where(ones, 1.0, tile).astype(jnp.bfloat16)


def head_window(h):
    at = h * (NOPE + ROPE)
    return at // HEAD * HEAD, at % HEAD


def window_columns(heads):
    return head_window(heads - 1)[0] + WIDE


def head_groups(heads):
    return [(h, min(h + 2, heads)) for h in range(0, heads, 2)]


def forward_kernel(
    blocks, heads, block_map, lengths, qx, lat, wkvb, o_out, ob_out, u_out,
    wkvt, xs, xr, vt, top, acc, bias, s_ref, p_ref,
):
    block_rows = bias.shape[0]
    q_blocks = qx.shape[0]
    starts = starts_of(lengths)
    own = [block_map[j, lax.axis_index("ctx")] for j in range(q_blocks)]
    for first, last in head_groups(heads):
        wkvt[first * HEAD : last * HEAD, :] = (
            wkvb[:, first * HEAD : last * HEAD].astype(jnp.float32).T.astype(jnp.bfloat16)
        )
    top[...] = jnp.full(top.shape, MASKED, jnp.float32)
    vt[:, VDIM:, :] = jnp.ones((heads, SUM_ROWS, block_rows), jnp.bfloat16)
    acc[...] = jnp.zeros(acc.shape, jnp.float32)

    def pair(j, masked):
        def one(h):
            keys = jnp.concatenate([xs[h], xr[...]], axis=1)
            s_ref[h % 3] = dot_nt(keys, qx[j, h])

        def weigh(h):
            old = top[j, h]
            new = old
            for k in range(0, block_rows, 128):
                part = s_ref[h % 3, k : k + 128, :]
                if masked:
                    part = part + bias[k : k + 128, :]
                    s_ref[h % 3, k : k + 128, :] = part
                new = jnp.maximum(new, jnp.max(part, axis=0, keepdims=True))
            fade = jnp.exp2((old - new) * EXP2_SCALE)
            top[j, h] = new
            for k in range(0, block_rows, 128):
                terms = jnp.exp2((s_ref[h % 3, k : k + 128, :] - new) * EXP2_SCALE)
                p_ref[h % 3, k : k + 128, :] = terms.astype(jnp.bfloat16)
            return fade

        def add(h, fade):
            acc[j, h] = fade * acc[j, h] + dot_nn(vt[h], p_ref[h % 3])

        one(0)
        if heads > 1:
            one(1)
        fades = {}
        for h in range(heads):
            if h + 2 < heads:
                one(h + 2)
            fades[h] = weigh(h)
            if h > 1:
                add(h - 2, fades[h - 2])
        for h in range(max(heads - 2, 0), heads):
            add(h, fades[h])

    def step(r, carry):
        key_block = block_map[lax.rem(r, 2), lax.div(r, 2)]
        kinds = [pair_kind(key_block, own[j], starts, block_rows) for j in range(q_blocks)]
        wanted = functools.reduce(jnp.logical_or, [k[0] for k in kinds])

        @pl.when(wanted)
        def _():
            here = pl.ds(pl.multiple_of(r * block_rows, block_rows), block_rows)
            latent = lat[here, :KVR]
            xr[...] = shared_key_tile(lat[here, KVR : KVR + ROPE], block_rows)
            for first, last in head_groups(heads):
                keys = dot_nn(latent, wkvb[:, first * HEAD : last * HEAD]).astype(jnp.bfloat16)
                values = dot_nt(wkvt[first * HEAD : last * HEAD, :], latent).astype(jnp.bfloat16)
                for h in range(first, last):
                    at = (h - first) * HEAD
                    xs[h] = keys[:, at : at + HEAD]
                    vt[h, :VDIM, :] = values[at + NOPE : at + HEAD, :]

        for j in range(q_blocks):
            needed, whole = kinds[j]

            @pl.when(needed & whole)
            def _():
                pair(j, False)

            @pl.when(needed & jnp.logical_not(whole))
            def _():
                bias[...] = mask_bias(key_block, own[j], starts, block_rows, True)
                pair(j, True)

        return carry

    lax.fori_loop(0, blocks, step, 0)
    for j in range(q_blocks):
        here = pl.ds(j * block_rows, block_rows)
        for first, last in head_groups(heads):
            parts = []
            for h in range(first, last):
                total = acc[j, h, VDIM : VDIM + 1, :]
                parts.append(acc[j, h, :VDIM, :] * (1.0 / total))
                u_out[j, h : h + 1, :] = top[j, h] + jnp.log2(total) * (1.0 / EXP2_SCALE)
            if len(parts) == 1:
                parts.append(jnp.zeros_like(parts[0]))
            both = jnp.concatenate(parts, axis=0).T
            width = (last - first) * VDIM
            o_out[here, first * VDIM : first * VDIM + width] = both[:, :width]
            ob_out[here, first * VDIM : first * VDIM + width] = both[:, :width].astype(jnp.bfloat16)


def attention_forward(block_map, lengths, qx, lat, wkvb):
    q_blocks, heads, block_rows, _ = qx.shape
    blocks = lat.shape[0] // block_rows
    rows = q_blocks * block_rows
    vmem = pl.BlockSpec(memory_space=pltpu.VMEM)
    smem = pl.BlockSpec(memory_space=pltpu.SMEM)
    pairs = q_blocks * blocks * heads // 2
    return pl.pallas_call(
        functools.partial(forward_kernel, blocks, heads),
        out_shape=(
            jax.ShapeDtypeStruct((rows, heads * VDIM), jnp.float32),
            jax.ShapeDtypeStruct((rows, heads * VDIM), jnp.bfloat16),
            jax.ShapeDtypeStruct((q_blocks, 16 * -(-heads // 16), block_rows), jnp.float32),
        ),
        in_specs=[smem] * 2 + [vmem] * 3,
        out_specs=(vmem,) * 3,
        scratch_shapes=[
            pltpu.VMEM((heads * HEAD, KVR), jnp.bfloat16),
            pltpu.VMEM((heads, block_rows, HEAD), jnp.bfloat16),
            pltpu.VMEM((block_rows, HEAD), jnp.bfloat16),
            pltpu.VMEM((heads, VDIM + SUM_ROWS, block_rows), jnp.bfloat16),
            pltpu.VMEM((q_blocks, heads, 1, block_rows), jnp.float32),
            pltpu.VMEM((q_blocks, heads, VDIM + SUM_ROWS, block_rows), jnp.float32),
            pltpu.VMEM((block_rows, block_rows), jnp.float32),
            pltpu.VMEM((3, block_rows, block_rows), jnp.float32),
            pltpu.VMEM((3, block_rows, block_rows), jnp.bfloat16),
        ],
        compiler_params=pltpu.CompilerParams(vmem_limit_bytes=VMEM_LIMIT),
        cost_estimate=pl.CostEstimate(
            flops=pairs * 4 * block_rows * block_rows * WIDE,
            bytes_accessed=16 * 1024 * 1024,
            transcendentals=pairs * block_rows * block_rows,
        ),
        name="attention_forward",
    )(block_map, lengths, qx, lat, wkvb)


def three_terms(column):
    first = column.astype(jnp.bfloat16).astype(jnp.float32)
    rest = column - first
    second = rest.astype(jnp.bfloat16).astype(jnp.float32)
    return first, second, rest - second


def fold_in(tile, column, lane):
    for k, term in enumerate(three_terms(column)):
        tile = jnp.where(lane == FOLD_AT + k, term, tile)
    return tile


def backward_kernel(
    blocks, heads, block_map, lengths, qx, qt, u_in, o_in, dob, lat, wkvb, cos, sin,
    dq_out, dlat, gkvb, xs, xr, qo, dt, dq, dkv, dkpe, gsum, bias, flat, s_ref, p_ref, d_ref,
):
    block_rows = bias.shape[0]
    q_blocks = qx.shape[0]
    starts = starts_of(lengths)
    own = [block_map[j, lax.axis_index("ctx")] for j in range(q_blocks)]
    lane = lax.broadcasted_iota(jnp.int32, (block_rows, HEAD), 1)
    for j in range(q_blocks):
        here = pl.ds(j * block_rows, block_rows)
        logs = u_in[j].T
        for first, last in head_groups(heads):
            d_pair = dob[here, first * VDIM : first * VDIM + HEAD].astype(jnp.float32)
            weighted = d_pair * o_in[here, first * VDIM : first * VDIM + HEAD]
            turned = pltpu.roll(d_pair, VDIM, 1)
            for h in range(first, last):
                mine = lane < VDIM if h == first else lane >= VDIM
                delta = jnp.sum(jnp.where(mine, weighted, 0.0), axis=1, keepdims=True)
                d_head = jnp.where(lane >= VDIM, turned if h == first else d_pair, 0.0)
                q_second = qx[j, h, :, HEAD:].astype(jnp.float32)
                qo[j, h, :block_rows, :HEAD] = qx[j, h, :, :HEAD]
                qo[j, h, :block_rows, HEAD:] = fold_in(q_second, -logs[:, h : h + 1], lane).astype(
                    jnp.bfloat16
                )
                qo[j, h, block_rows:, :HEAD] = d_head.astype(jnp.bfloat16)
                qo[j, h, block_rows:, HEAD:] = fold_in(
                    jnp.zeros((block_rows, HEAD), jnp.float32), -delta, lane
                ).astype(jnp.bfloat16)
                dt[j, h] = d_head.T[VDIM:, :].astype(jnp.bfloat16)
    dq[...] = jnp.zeros(dq.shape, jnp.float32)
    gsum[...] = jnp.zeros(gsum.shape, jnp.float32)

    def pair(j, masked):
        def raw(h):
            keys = jnp.concatenate([xs[h], xr[...]], axis=1)
            s_ref[h % 2] = dot_nt(qo[j, h], keys)

        def weigh(h):
            for k in range(0, block_rows, 128):
                scores = s_ref[h % 2, k : k + 128, :] * EXP2_SCALE
                if masked:
                    scores = scores + bias[k : k + 128, :]
                probs = jnp.exp2(scores)
                p_ref[h % 2, k : k + 128, :] = probs.astype(jnp.bfloat16)
                d_ref[h % 2, k : k + 128, :] = (
                    probs * s_ref[h % 2, block_rows + k : block_rows + k + 128, :]
                ).astype(jnp.bfloat16)

        def add(h):
            keys = jnp.concatenate([xs[h], xr[...]], axis=1)
            d_scores = d_ref[h % 2]
            dq[j, h] += dot_nn(d_scores, keys)
            d_keys = dot_nn(qt[j, h], d_scores)
            dkv[h, :NOPE, :] += d_keys[:NOPE]
            dkpe[...] += d_keys[NOPE:]
            dkv[h, NOPE:, :] += dot_nn(dt[j, h], p_ref[h % 2])

        raw(0)
        for h in range(heads):
            if h + 1 < heads:
                raw(h + 1)
            weigh(h)
            if h:
                add(h - 1)
        add(heads - 1)

    def step(r, carry):
        key_block = block_map[lax.rem(r, 2), lax.div(r, 2)]
        kinds = [pair_kind(key_block, own[j], starts, block_rows) for j in range(q_blocks)]
        wanted = functools.reduce(jnp.logical_or, [k[0] for k in kinds])
        here = pl.ds(pl.multiple_of(r * block_rows, block_rows), block_rows)

        @pl.when(wanted)
        def _():
            latent = lat[here, :KVR]
            xr[...] = shared_key_tile(lat[here, KVR : KVR + ROPE], block_rows)
            for first, last in head_groups(heads):
                keys = dot_nn(latent, wkvb[:, first * HEAD : last * HEAD]).astype(jnp.bfloat16)
                for h in range(first, last):
                    xs[h] = keys[:, (h - first) * HEAD : (h - first + 1) * HEAD]
            dkv[...] = jnp.zeros(dkv.shape, jnp.float32)
            dkpe[...] = jnp.zeros(dkpe.shape, jnp.float32)

        for j in range(q_blocks):
            needed, whole = kinds[j]

            @pl.when(needed & whole)
            def _():
                pair(j, False)

            @pl.when(needed & jnp.logical_not(whole))
            def _():
                bias[...] = mask_bias(key_block, own[j], starts, block_rows, False)
                pair(j, True)

        @pl.when(wanted)
        def _():
            latent = lat[here, :KVR]
            d_latent = jnp.zeros((KVR, block_rows), jnp.float32)
            for h in range(heads):
                d_head = jnp.concatenate(
                    [dkv[h, :NOPE, :] * SCORE_SCALE, dkv[h, NOPE:, :]], axis=0
                ).astype(jnp.bfloat16)
                d_latent += dot_nn(wkvb[:, h * HEAD : (h + 1) * HEAD], d_head)
                gsum[h * HEAD : (h + 1) * HEAD, :] += dot_nn(d_head, latent)
            dlat[here, :KVR] = d_latent.T.astype(jnp.bfloat16)
            rope = jnp.concatenate(
                [dkpe[...] * SCORE_SCALE, jnp.zeros((HEAD - ROPE, block_rows), jnp.float32)], axis=0
            )
            dlat[here, KVR:] = rope.T[:, :ROPE].astype(jnp.bfloat16)

        @pl.when(jnp.logical_not(wanted))
        def _():
            dlat[here, :] = jnp.zeros((block_rows, KVR + ROPE), jnp.bfloat16)

        return carry

    lax.fori_loop(0, blocks, step, 0)
    for h in range(heads):
        gkvb[:, h * HEAD : (h + 1) * HEAD] = gsum[h * HEAD : (h + 1) * HEAD, :].T.astype(
            jnp.bfloat16
        )
    for j in range(q_blocks):
        here = pl.ds(j * block_rows, block_rows)
        cos_j, sin_j = cos[here, :], sin[here, :]
        flat[...] = jnp.zeros(flat.shape, jnp.float32)
        for h in range(heads):
            nope = jnp.where(lane < NOPE, dq[j, h, :, :HEAD], 0.0)
            rope = dq[j, h, :, HEAD:]
            shifted = rope * sin_j
            left = pltpu.roll(shifted, HEAD - ROPE // 2, 1)
            right = pltpu.roll(shifted, ROPE // 2, 1)
            swapped = jnp.where(lane < ROPE // 2, left, jnp.where(lane < ROPE, -right, 0.0))
            back = pltpu.roll(jnp.where(lane < ROPE, rope * cos_j + swapped, 0.0), NOPE, 1)
            whole = jnp.concatenate([(nope + back) * SCORE_SCALE, jnp.zeros_like(nope)], axis=1)
            at, shift = head_window(h)
            flat[:, at : at + WIDE] += pltpu.roll(whole, shift, 1)
        dq_out[here, :] = flat[:, : heads * (NOPE + ROPE)].astype(jnp.bfloat16)


def attention_backward(block_map, lengths, qx, qt, u_in, o_in, dob, lat, wkvb, cos, sin):
    q_blocks, heads, block_rows, _ = qx.shape
    blocks = lat.shape[0] // block_rows
    rows = q_blocks * block_rows
    odd = -(heads * VDIM) % HEAD
    if odd:
        o_in = jnp.pad(o_in, ((0, 0), (0, odd)))
        dob = jnp.pad(dob, ((0, 0), (0, odd)))
    vmem = pl.BlockSpec(memory_space=pltpu.VMEM)
    smem = pl.BlockSpec(memory_space=pltpu.SMEM)
    pairs = q_blocks * blocks * heads // 2
    return pl.pallas_call(
        functools.partial(backward_kernel, blocks, heads),
        out_shape=(
            jax.ShapeDtypeStruct((rows, heads * (NOPE + ROPE)), jnp.bfloat16),
            jax.ShapeDtypeStruct((lat.shape[0], KVR + ROPE), jnp.bfloat16),
            jax.ShapeDtypeStruct((KVR, heads * HEAD), jnp.bfloat16),
        ),
        in_specs=[smem] * 2 + [vmem] * 9,
        out_specs=(vmem,) * 3,
        scratch_shapes=[
            pltpu.VMEM((heads, block_rows, HEAD), jnp.bfloat16),
            pltpu.VMEM((block_rows, HEAD), jnp.bfloat16),
            pltpu.VMEM((q_blocks, heads, 2 * block_rows, WIDE), jnp.bfloat16),
            pltpu.VMEM((q_blocks, heads, VDIM, block_rows), jnp.bfloat16),
            pltpu.VMEM((q_blocks, heads, block_rows, WIDE), jnp.float32),
            pltpu.VMEM((heads, HEAD, block_rows), jnp.float32),
            pltpu.VMEM((ROPE, block_rows), jnp.float32),
            pltpu.VMEM((heads * HEAD, KVR), jnp.float32),
            pltpu.VMEM((block_rows, block_rows), jnp.float32),
            pltpu.VMEM((block_rows, window_columns(heads)), jnp.float32),
            pltpu.VMEM((2, 2 * block_rows, block_rows), jnp.float32),
            pltpu.VMEM((2, block_rows, block_rows), jnp.bfloat16),
            pltpu.VMEM((2, block_rows, block_rows), jnp.bfloat16),
        ],
        compiler_params=pltpu.CompilerParams(vmem_limit_bytes=VMEM_LIMIT),
        cost_estimate=pl.CostEstimate(
            flops=pairs * 8 * block_rows * block_rows * WIDE,
            bytes_accessed=24 * 1024 * 1024,
            transcendentals=pairs * block_rows * block_rows,
        ),
        name="attention_backward",
    )(block_map, lengths, qx, qt, u_in, o_in, dob, lat, wkvb, cos, sin)


MESH = pl.DeviceIdType.MESH


class LineSum:
    def __init__(self, n, own, landing, total, sems, lag):
        self.n, self.own, self.landing, self.total, self.lag = n, own, landing, total, lag
        self.up_send, self.up_land, self.down_send, self.back_send, self.down_land = sems
        self.me = lax.axis_index("tp")
        self.root = (n - 1) // 2
        self.chunks = own.shape[0]
        self.has_left, self.has_right = self.me > 0, self.me < n - 1
        self.root_lag = (n - 1 - self.root) * lag
        self.land_lag = 2 * self.root_lag
        self.ticks = self.chunks + self.land_lag

    def greet(self, barrier):
        me = self.me
        for there, other in ((self.has_left, me - 1), (self.has_right, me + 1)):

            @pl.when(there)
            def _(other=other):
                pl.semaphore_signal(barrier, inc=1, device_id={"tp": other}, device_id_type=MESH)

    def wait_greetings(self, barrier, others):
        both = self.has_left & self.has_right

        @pl.when(both)
        def _():
            pl.semaphore_wait(barrier, 2 + others)

        @pl.when(jnp.logical_not(both))
        def _():
            pl.semaphore_wait(barrier, 1 + others)

    def copy_to(self, source, target, send, land, c, other):
        return pltpu.make_async_remote_copy(
            src_ref=source.at[c],
            dst_ref=target.at[c],
            send_sem=send.at[c],
            recv_sem=land.at[c],
            device_id={"tp": other},
            device_id_type=MESH,
        )

    def rise_left(self, c):
        return self.copy_to(self.own, self.landing, self.up_send, self.up_land, c, self.me + 1)

    def rise_right(self, c):
        return self.copy_to(self.own, self.landing, self.up_send, self.up_land, c, self.me - 1)

    def rise_last(self, c):
        return self.copy_to(self.own, self.total, self.up_send, self.down_land, c, self.me - 1)

    def fall_right(self, c):
        return self.copy_to(self.total, self.total, self.down_send, self.down_land, c, self.me + 1)

    def fall_left(self, c):
        return self.copy_to(self.total, self.total, self.back_send, self.down_land, c, self.me - 1)

    def rise(self, c):
        me, root = self.me, self.root
        rises = [(me == root + 1, self.rise_last)]
        if root:
            rises.append((me < root, self.rise_left))
        if self.n - 1 > root + 1:
            rises.append((me > root + 1, self.rise_right))
        for who, copy in rises:

            @pl.when(who)
            def _(copy=copy):
                copy(c).start()

    def inside(self, c):
        return (c >= 0) & (c < self.chunks)

    def added(self, refs, c):
        sums = refs[0][c].astype(jnp.float32)
        for ref in refs[1:]:
            sums = sums + ref[c].astype(jnp.float32)
        return sums.astype(self.total.dtype)

    def leaf(self, c):
        is_leaf = self.me == self.n - 1
        if self.root:
            is_leaf = is_leaf | (self.me == 0)

        @pl.when(is_leaf & self.inside(c))
        def _():
            self.rise(c)

    def leaves(self):
        def body(c, carry):
            self.leaf(c)
            return carry

        lax.fori_loop(0, self.chunks, body, 0)

    def pump(self, first, last):
        def body(t, carry):
            self.duty(t)
            return carry

        lax.fori_loop(first, last, body, 0)

    def duty(self, t):
        me, root = self.me, self.root
        if self.n > 3:
            c = t - self.lag * jnp.where(me < root, me, self.n - 1 - me)

            @pl.when((me != root) & self.has_left & self.has_right & self.inside(c))
            def _():
                self.rise_right(c).wait_recv()
                self.own[c] = self.added([self.own, self.landing], c)
                self.rise(c)

        c_root = t - self.root_lag

        @pl.when((me == root) & self.inside(c_root))
        def _():
            if root:
                self.rise_left(c_root).wait_recv()
            self.fall_right(c_root).wait_recv()
            terms = [self.own, self.landing, self.total] if root else [self.own, self.total]
            self.total[c_root] = self.added(terms, c_root)
            self.fall_right(c_root).start()
            if root:
                self.fall_left(c_root).start()

        c_fall = t - self.root_lag - self.lag * jnp.where(me < root, root - me, me - root)

        @pl.when((me != root) & self.inside(c_fall))
        def _():
            self.fall_right(c_fall).wait_recv()

            @pl.when((me > root) & self.has_right)
            def _():
                self.fall_right(c_fall).start()

            @pl.when((me < root) & self.has_left)
            def _():
                self.fall_left(c_fall).start()

    def landed(self, t):
        return t - self.land_lag

    def drain(self):
        me = self.me

        def body(c, carry):
            @pl.when(me != self.root)
            def _():
                self.rise_right(c).wait_send()

            @pl.when((me >= self.root) & self.has_right)
            def _():
                self.fall_right(c).wait_send()

            @pl.when((me <= self.root) & self.has_left)
            def _():
                self.fall_left(c).wait_send()

            return carry

        lax.fori_loop(0, self.chunks, body, 0)


def line_sems(chunks):
    return [pltpu.SemaphoreType.DMA((chunks,))] * 5


def scatter_blocks(bits_left):
    chips = []
    for value in range(1 << len(bits_left)):
        chip = 0
        for at, bit in enumerate(bits_left):
            chip = chip + (((value >> at) & 1) << (bit - 1))
        chips.append(chip)
    return chips


class Scatter:
    def __init__(self, n, rows, columns, is_given):
        self.n, self.rows, self.columns, self.is_given = n, rows, columns, is_given
        self.count = n.bit_length() - 1
        self.parts = 2 if rows % 32 == 0 else 1

    def scratch(self):
        n, count = self.n, self.count
        half = jnp.bfloat16
        dma = pltpu.SemaphoreType.DMA
        shapes = [pltpu.VMEM((n // 2, self.rows, self.columns), half)]
        if not self.is_given:
            shapes.append(pltpu.VMEM((n // 2, self.rows, self.columns), half))
        for step in range(count - 1):
            shapes.append(pltpu.VMEM((n >> (step + 2), self.rows, self.columns), half))
        shapes += [dma((n // 2,))] * 2
        for step in range(count - 1):
            shapes += [dma((2, n >> (step + 2)))] * 2
        return shapes

    def bind(self, take, source, emit):
        self.held = take(1)[0]
        self.sent = None if self.is_given else take(1)[0]
        self.landed = take(self.count - 1)
        self.core_sems = take(2)
        self.step_sems = [take(2) for _ in range(self.count - 1)]
        self.source, self.emit = source, emit
        self.me = lax.axis_index("ctx")
        self.core = self.me & 1
        self.chips = self.n // 2
        self.orders = (tuple(range(1, self.count)), tuple(range(self.count - 1, 0, -1)))
        self.tiles = [(c, min(c + 512, self.columns)) for c in range(0, self.columns, 512)]
        return self

    def own(self, dest, first, last):
        at = pl.ds(pl.multiple_of(dest * self.rows, 16), self.rows)
        if self.is_given:
            return self.source[at, first:last].astype(jnp.float32)
        return dot_nn(self.source[0][at, :], self.source[1][:, first:last])

    def core_copy(self, chip):
        if self.is_given:
            at = pl.ds(pl.multiple_of((2 * chip + 1 - self.core) * self.rows, 16), self.rows)
            source = self.source.at[at, :]
        else:
            source = self.sent.at[chip]
        return pltpu.make_async_remote_copy(
            src_ref=source,
            dst_ref=self.held.at[chip],
            send_sem=self.core_sems[0].at[chip],
            recv_sem=self.core_sems[1].at[chip],
            device_id={"ctx": self.me ^ 1},
            device_id_type=MESH,
        )

    def step_copies(self, step):
        half = self.rows // self.parts
        me = self.me
        copies = []
        for part, order in enumerate(self.orders[: self.parts]):
            bit = order[step]
            at = pl.ds(part * half, half)
            for slot, free in enumerate(scatter_blocks(sorted(order[step + 1 :]))):
                keep = free + ((me >> bit) & 1) * (1 << (bit - 1))
                send = free + (1 - ((me >> bit) & 1)) * (1 << (bit - 1))
                for b in order[:step]:
                    own = ((me >> b) & 1) * (1 << (b - 1))
                    keep, send = keep + own, send + own
                copy = pltpu.make_async_remote_copy(
                    src_ref=self.held.at[send, at, :],
                    dst_ref=self.landed[step].at[slot, at, :],
                    send_sem=self.step_sems[step][0].at[part, slot],
                    recv_sem=self.step_sems[step][1].at[part, slot],
                    device_id={"ctx": me ^ (1 << bit)},
                    device_id_type=MESH,
                )
                copies.append((copy, keep, slot, at))
        return copies

    def start_core(self, also=None):
        def body(chip, carry):
            if also is not None:
                also(chip)
            if not self.is_given:
                for first, last in self.tiles:
                    self.sent[chip, :, first:last] = self.own(
                        2 * chip + 1 - self.core, first, last
                    ).astype(jnp.bfloat16)
            self.core_copy(chip).start()
            return carry

        lax.fori_loop(0, self.chips, body, 0)

    def finish_core(self, also=None):
        def body(chip, carry):
            if also is not None:
                also(chip)
            self.core_copy(chip).wait_recv()
            for first, last in self.tiles:
                total = self.own(2 * chip + self.core, first, last)
                total = total + self.held[chip, :, first:last].astype(jnp.float32)
                self.held[chip, :, first:last] = total.astype(jnp.bfloat16)
            return carry

        lax.fori_loop(0, self.chips, body, 0)

    def start_step(self, step):
        for copy, _, _, _ in self.step_copies(step):
            copy.start()

    def finish_step(self, step):
        for copy, keep, slot, at in self.step_copies(step):
            copy.wait_recv()
            for first, last in self.tiles:
                total = self.held[keep, at, first:last].astype(jnp.float32)
                total = total + self.landed[step][slot, at, first:last].astype(jnp.float32)
                if step == self.count - 2:
                    self.emit(at, first, last, total)
                else:
                    self.held[keep, at, first:last] = total.astype(jnp.bfloat16)
        if step + 1 < self.count - 1:
            self.start_step(step + 1)

    def drain(self):
        def body(chip, carry):
            self.core_copy(chip).wait_send()
            return carry

        lax.fori_loop(0, self.chips, body, 0)
        for step in range(self.count - 1):
            for copy, _, _, _ in self.step_copies(step):
                copy.wait_send()


def taker(refs):
    refs = list(refs)

    def take(k):
        taken = refs[:k]
        del refs[:k]
        return taken

    return take


def store_in(ref):
    def emit(at, first, last, total):
        ref[at, first:last] = total.astype(ref.dtype)

    return emit


def turn(source, target):
    def body(c, carry):
        at = pl.ds(pl.multiple_of(c * 128, 128), 128)
        target[at, :] = source[:, at].astype(jnp.float32).T.astype(jnp.bfloat16)
        return carry

    lax.fori_loop(0, source.shape[1] // 128, body, 0)


def greet_ctx(n, barrier):
    me = lax.axis_index("ctx")
    count = n.bit_length() - 1
    for bit in range(count):
        pl.semaphore_signal(barrier, inc=1, device_id={"ctx": me ^ (1 << bit)}, device_id_type=MESH)
    return count


def spread(waits, ticks):
    portion = -(-ticks // waits)
    return [(min(k * portion, ticks), min((k + 1) * portion, ticks)) for k in range(waits)]


def gate_up_kernel(
    n, tp, plans, normed, d_gate, d_up, terms, tokens, attn, cot, gain_row, w_out,
    gate_out, up_out, d_attn, d_heads, g_mid, *refs,
):
    take = taker(refs)
    own, landing, sums, normed_t, slots, in_sems, own_sem = take(7)
    line = LineSum(tp, own, landing, sums, take(5), LAG)
    gate = plans[0].bind(take, (normed_t, d_gate), store_in(gate_out))
    up = plans[1].bind(take, (normed_t, d_up), store_in(up_out))
    width = normed.shape[1]
    blocks = normed.shape[0] // BLOCK
    per_block = BLOCK // CHUNK
    load = pltpu.make_async_copy(terms, own, own_sem)
    load.start()
    barrier = pltpu.get_barrier_semaphore()
    others = greet_ctx(n, barrier)
    line.greet(barrier)

    def fetch(b):
        rows = pl.ds(b * BLOCK, BLOCK)
        return [
            pltpu.make_async_copy(
                source.at[rows, :], slots.at[b % 2, k], in_sems.at[b % 2, k]
            )
            for k, source in enumerate((tokens, attn, cot))
        ]

    for b in range(min(2, blocks)):
        for copy in fetch(b):
            copy.start()
    g_mid[...] = jnp.zeros(g_mid.shape, jnp.float32)

    def norm(b):
        for copy in fetch(b):
            copy.wait()
        for part in range(0, BLOCK, 2 * CHUNK):
            rows = pl.ds(b * BLOCK + part, 2 * CHUNK)
            here = pl.ds(part, 2 * CHUNK)
            c = b * per_block + part // CHUNK
            incoming = jnp.concatenate([sums[c], sums[c + 1]], axis=0).astype(jnp.float32)
            middle = slots[b % 2, 0, here, :].astype(jnp.float32)
            middle = middle + RESIDUAL_SCALE * slots[b % 2, 1, here, :].astype(jnp.float32)
            d_norm, gain_terms = norm_back(
                incoming, middle, norm_scale(middle), gain_row[:, width : 2 * width]
            )
            g_mid[...] += gain_terms
            total = slots[b % 2, 2, here, :].astype(jnp.float32) + d_norm
            d_attn[rows, :] = (RESIDUAL_SCALE * total).astype(jnp.bfloat16)
        rows = pl.ds(b * BLOCK, BLOCK)
        d_heads[rows, :] = dot_nn(d_attn[rows, :], w_out[...]).astype(jnp.bfloat16)
        if b + 2 < blocks:
            for copy in fetch(b + 2):
                copy.start()

    load.wait()
    line.wait_greetings(barrier, others)
    line.leaves()
    turn(normed, normed_t)
    chips = n // 2
    gate.start_core()
    gate.finish_core(line.duty)
    gate.start_step(0)
    up.start_core(lambda chip: line.duty(chips + chip))
    up.finish_core(lambda chip: line.duty(2 * chips + chip))
    up.start_step(0)
    steps = [(item, step) for step in range(gate.count - 1) for item in (gate, up)]
    done = 3 * chips
    next_block = 0
    for (item, step), (first, last) in zip(steps, spread(len(steps), line.ticks - done)):
        line.pump(done + first, done + last)
        while next_block < blocks and line.landed(done + last - 1) >= (next_block + 1) * per_block - 1:
            norm(next_block)
            next_block += 1
        item.finish_step(step)
    for item in (gate, up, line):
        item.drain()


def gate_up_grads(
    n, tp, normed, d_gate, d_up, terms, tokens, attn, cot, gain_row, w_out, collective_id
):
    rows, width = normed.shape
    hidden = d_gate.shape[1]
    head_width = w_out.shape[1]
    vmem = pl.BlockSpec(memory_space=pltpu.VMEM)
    anywhere = pl.BlockSpec(memory_space=pl.ANY)
    half = jnp.bfloat16
    plans = [Scatter(n, width // n, hidden, False) for _ in range(2)]
    chunked = (rows // CHUNK, CHUNK, width)
    return pl.pallas_call(
        functools.partial(gate_up_kernel, n, tp, plans),
        out_shape=(
            jax.ShapeDtypeStruct((width // n, hidden), half),
            jax.ShapeDtypeStruct((width // n, hidden), half),
            jax.ShapeDtypeStruct((rows, width), half),
            jax.ShapeDtypeStruct((rows, head_width), half),
            jax.ShapeDtypeStruct((1, width), jnp.float32),
        ),
        in_specs=[vmem] * 3 + [anywhere] * 4 + [vmem] * 2,
        out_specs=(vmem,) * 5,
        scratch_shapes=[
            pltpu.VMEM(chunked, half),
            pltpu.VMEM(chunked, half),
            pltpu.VMEM(chunked, half),
            pltpu.VMEM((width, rows), half),
            pltpu.VMEM((2, 3, BLOCK, width), half),
            pltpu.SemaphoreType.DMA((2, 3)),
            pltpu.SemaphoreType.DMA,
            *line_sems(rows // CHUNK),
            *plans[0].scratch(),
            *plans[1].scratch(),
        ],
        compiler_params=pltpu.CompilerParams(
            vmem_limit_bytes=MIDDLE_VMEM, collective_id=collective_id, has_side_effects=True
        ),
        cost_estimate=pl.CostEstimate(
            flops=2 * rows * width * (2 * hidden + head_width),
            bytes_accessed=28 * 1024 * 1024,
            transcendentals=0,
        ),
        name=f"gate_up_grads_{collective_id}",
    )(normed, d_gate, d_up, terms.reshape(chunked), tokens, attn, cot, gain_row, w_out)


class FeedSum:
    def __init__(self, tp, take, at, chunks, terms, tokens, attn, out):
        own, landing, sums, self.tokens, self.attn, sems = take(6)
        self.out = out
        some = pl.ds(at, chunks)
        pairs = ((terms, own), (tokens, self.tokens), (attn, self.attn))
        self.loads = [
            pltpu.make_async_copy(source.at[some], target, sems.at[k])
            for k, (source, target) in enumerate(pairs)
        ]
        self.line = LineSum(tp, own, landing, sums, take(5), FEED_LAG)
        self.ticks = self.line.ticks

    def load(self):
        for load in self.loads:
            load.start()

    def begin(self):
        for load in self.loads:
            load.wait()
        self.line.leaves()

    def duty(self, t):
        self.line.duty(t)
        c = self.line.landed(t)

        @pl.when(self.line.inside(c))
        def _():
            both = self.attn[c].astype(jnp.float32) + self.line.total[c].astype(jnp.float32)
            total = self.tokens[c].astype(jnp.float32) + RESIDUAL_SCALE * both
            self.out[c] = total.astype(jnp.bfloat16)

    def pump(self, first, last):
        def body(t, carry):
            self.duty(t)
            return carry

        lax.fori_loop(first, last, body, 0)


def feed_scratch(chunks, width):
    return [pltpu.VMEM((chunks, CHUNK, width), jnp.bfloat16)] * 5 + [
        pltpu.SemaphoreType.DMA((3,)),
        *line_sems(chunks),
    ]


TAIL_CHUNK = 64
FEED_LAG = 4


def up_tail_kernel(
    n, tp, plans, feed_chunks, d_lat, d_query, w_qb, g_kvb, d_attn, ob, q_latent, d_feed, act,
    f_part, tokens, attn, sum_q, sum_lat, down_out, out_out, qb_out, kvb_out, layer_out, *refs,
):
    take = taker(refs)
    own_q, land_q, own_lat, land_lat, d_attn_t, q_latent_t, d_feed_t = take(7)
    line_q = LineSum(tp, own_q, land_q, sum_q, take(5), LAG + 1)
    line_lat = LineSum(tp, own_lat, land_lat, sum_lat, take(5), LAG)
    feed = FeedSum(tp, take, 0, feed_chunks, f_part, tokens, attn, layer_out)
    feed.load()
    chunk = own_q.shape[1]

    def store_lat(at, first, last, total):
        for k in range(at.size // chunk):
            own_lat[at.start // chunk + k, :, first:last] = total[
                k * chunk : (k + 1) * chunk
            ].astype(jnp.bfloat16)

    lat, down, out, qb, kvb = plans
    lat.bind(take, d_lat, store_lat)
    down.bind(take, (d_feed_t, act), store_in(down_out))
    out.bind(take, (d_attn_t, ob), store_in(out_out))
    qb.bind(take, (q_latent_t, d_query), store_in(qb_out))
    kvb.bind(take, g_kvb, store_in(kvb_out))
    barrier = pltpu.get_barrier_semaphore()
    others = greet_ctx(n, barrier)
    line_q.greet(barrier)
    line_q.wait_greetings(barrier, others)
    lat.start_core()

    def query(c, carry):
        rows = pl.ds(pl.multiple_of(c * 2 * chunk, 2 * chunk), 2 * chunk)
        part = dot_nn(d_query[rows, :], w_qb[...]).astype(jnp.bfloat16)
        for k in range(2):
            own_q[2 * c + k] = part[k * chunk : (k + 1) * chunk]
            line_q.leaf(2 * c + k)
        return carry

    lax.fori_loop(0, own_q.shape[0] // 2, query, 0)
    lat.finish_core()
    lat.start_step(0)
    turn(d_feed, d_feed_t)
    down.start_core()
    lat.finish_step(0)
    down.finish_core()
    for step in range(1, lat.count - 1):
        lat.finish_step(step)
    line_lat.leaves()
    down.start_step(0)
    feed.begin()
    chips = n // 2

    def both(line, line_first, feed_first):
        def also(chip):
            if line is not None:
                line.duty(line_first + chip)
            feed.duty(feed_first + chip)

        return also

    turn(d_attn, d_attn_t)
    out.start_core(both(line_q, 0, 0))
    out.finish_core(both(line_q, chips, chips))
    out.start_step(0)
    kvb.start_core(both(None, 0, 2 * chips))
    turn(q_latent, q_latent_t)
    qb.start_core(both(line_q, 2 * chips, 3 * chips))
    kvb.finish_core(both(line_lat, 0, 4 * chips))
    kvb.start_step(0)
    qb.finish_core(both(line_lat, chips, 5 * chips))
    qb.start_step(0)
    steps = [(item, step) for step in range(lat.count - 1) for item in (down, out, kvb, qb)]
    q_share = spread(len(steps), line_q.ticks - 3 * chips)
    lat_share = spread(len(steps), line_lat.ticks - 2 * chips)
    feed_share = spread(len(steps), feed.ticks - 6 * chips)
    for (item, step), (a, b), (c, d), (e, f) in zip(steps, q_share, lat_share, feed_share):
        line_q.pump(3 * chips + a, 3 * chips + b)
        line_lat.pump(2 * chips + c, 2 * chips + d)
        feed.pump(6 * chips + e, 6 * chips + f)
        item.finish_step(step)
    for item in (*plans, line_q, line_lat, feed.line):
        item.drain()


def up_tail(
    n, tp, d_lat, d_query, w_qb, g_kvb, d_attn, ob, q_latent, d_feed, act, f_part, tokens, attn,
    feed_chunks, collective_id,
):
    rows, width = d_attn.shape
    rank = q_latent.shape[1]
    hidden = act.shape[1]
    lat_width = d_lat.shape[1]
    vmem = pl.BlockSpec(memory_space=pltpu.VMEM)
    half = jnp.bfloat16
    plans = [
        Scatter(n, rows, lat_width, True),
        Scatter(n, width // n, hidden, False),
        Scatter(n, width // n, ob.shape[1], False),
        Scatter(n, rank // n, d_query.shape[1], False),
        Scatter(n, KVR // n, g_kvb.shape[1], True),
    ]
    q_shape = (rows // TAIL_CHUNK, TAIL_CHUNK, rank)
    lat_shape = (rows // TAIL_CHUNK, TAIL_CHUNK, lat_width)
    anywhere = pl.BlockSpec(memory_space=pl.ANY)
    chunked = (-1, CHUNK, width)
    sum_q, sum_lat, *grads, layer_out = pl.pallas_call(
        functools.partial(up_tail_kernel, n, tp, plans, feed_chunks),
        out_shape=(
            jax.ShapeDtypeStruct(q_shape, half),
            jax.ShapeDtypeStruct(lat_shape, half),
            *[jax.ShapeDtypeStruct((plan.rows, plan.columns), half) for plan in plans[1:]],
            jax.ShapeDtypeStruct((feed_chunks, CHUNK, width), half),
        ),
        in_specs=[vmem] * 9 + [anywhere] * 3,
        out_specs=(vmem,) * 7,
        scratch_shapes=[
            pltpu.VMEM(q_shape, half),
            pltpu.VMEM(q_shape, half),
            pltpu.VMEM(lat_shape, half),
            pltpu.VMEM(lat_shape, half),
            pltpu.VMEM((width, rows), half),
            pltpu.VMEM((rank, rows), half),
            pltpu.VMEM((width, rows), half),
            *line_sems(rows // TAIL_CHUNK),
            *line_sems(rows // TAIL_CHUNK),
            *feed_scratch(feed_chunks, width),
            *[shape for plan in plans for shape in plan.scratch()],
        ],
        compiler_params=pltpu.CompilerParams(
            vmem_limit_bytes=MIDDLE_VMEM, collective_id=collective_id, has_side_effects=True
        ),
        cost_estimate=pl.CostEstimate(
            flops=2 * rows * width * (hidden + ob.shape[1]) + 4 * rows * rank * d_query.shape[1],
            bytes_accessed=32 * 1024 * 1024,
            transcendentals=0,
        ),
        name=f"up_tail_{collective_id}",
    )(
        d_lat,
        d_query,
        w_qb,
        g_kvb,
        d_attn,
        ob,
        q_latent,
        d_feed,
        act,
        *[array.reshape(chunked) for array in (f_part, tokens, attn)],
    )
    return (
        sum_q.reshape(rows, rank),
        sum_lat.reshape(rows, lat_width),
        *grads,
        layer_out.reshape(-1, width),
    )


def down_tail_kernel(
    n, tp, plans, feed_chunks, sum_q, sum_lat, q_pre, lat_raw, tokens, d_attn, gain_row, g_mid, w_qa,
    w_kva, cos, sin, f_part, tokens_chunked, attn, grad_in, qa_out, kva_out, gains_out, layer_out,
    d_q, d_kv, normed_t, scales, g_in, g_q, g_kv, packed, packing, grad_slots, out_sems, *refs,
):
    take = taker(refs)
    qa, kva, gains = plans
    qa.bind(take, (normed_t, d_q), store_in(qa_out))
    kva.bind(take, (normed_t, d_kv), store_in(kva_out))
    gains.bind(take, packed, store_in(gains_out))
    at = f_part.shape[0] - feed_chunks
    feed = FeedSum(tp, take, at, feed_chunks, f_part, tokens_chunked, attn, layer_out)
    feed.load()
    rows = tokens.shape[0]
    block = rows // 4
    gain_in, _, gain_q, gain_kv = split_gains(gain_row, tokens.shape[1], q_pre.shape[1])
    lane = lax.broadcasted_iota(jnp.int32, (block, HEAD), 1)
    barrier = pltpu.get_barrier_semaphore()
    others = greet_ctx(n, barrier)
    feed.line.greet(barrier)

    def rows_of(k):
        return pl.ds(pl.multiple_of(k * block, block), block)

    def deliver(k, slot):
        return pltpu.make_async_copy(
            grad_slots.at[slot], grad_in.at[rows_of(k), :], out_sems.at[slot]
        )

    feed.line.wait_greetings(barrier, others)
    feed.begin()
    for ref in (g_in, g_q, g_kv):
        ref[...] = jnp.zeros(ref.shape, jnp.float32)

    def norms(k, carry):
        feed.duty(k)
        at = rows_of(k)
        pre = q_pre[at, :]
        d_pre, terms = norm_back(
            sum_q[at, :].astype(jnp.float32), pre, norm_scale(pre), gain_q
        )
        g_q[...] += terms
        d_q[at, :] = d_pre.astype(jnp.bfloat16)
        raw = lat_raw[at, :]
        d_raw, terms = norm_back(
            sum_lat[at, :KVR].astype(jnp.float32), raw, norm_scale(raw), gain_kv
        )
        g_kv[...] += terms
        d_kv[at, :KVR] = d_raw.astype(jnp.bfloat16)
        rope = sum_lat[at, KVR:].astype(jnp.float32)
        rope = jnp.concatenate([rope, jnp.zeros((block, HEAD - ROPE), jnp.float32)], axis=1)
        rope = rope_tile_back(rope, cos[at, :], sin[at, :], lane)
        d_kv[at, KVR:] = rope[:, :ROPE].astype(jnp.bfloat16)
        values = tokens[at, :].astype(jnp.float32)
        scale = norm_scale(values)
        scales[at, :] = jnp.broadcast_to(scale, (block, HEAD))
        normed = values * scale * gain_in
        for c in range(0, normed.shape[1], 128):
            normed_t[c : c + 128, at] = normed[:, c : c + 128].T.astype(jnp.bfloat16)
        return carry

    lax.fori_loop(0, 4, norms, 0)
    chips = n // 2
    qa.start_core(lambda chip: feed.duty(4 + chip))
    qa.finish_core(lambda chip: feed.duty(4 + chips + chip))
    qa.start_step(0)
    kva.start_core(lambda chip: feed.duty(4 + 2 * chips + chip))
    kva.finish_core(lambda chip: feed.duty(4 + 3 * chips + chip))
    kva.start_step(0)
    done = 4 + 4 * chips
    shares = [(done + a, done + b) for a, b in spread(4 + 3, max(feed.ticks - done, 0))]
    for k in range(4):
        at = pl.ds(k * block, block)
        feed.pump(*shares[k])
        if k >= 2:
            deliver(k - 2, k % 2).wait()
        d_normed = dot_nt(d_q[at, :], w_qa[...]) + dot_nn(d_kv[at, :], w_kva[...])
        d_values, terms = norm_back(
            d_normed, tokens[at, :].astype(jnp.float32), scales[at, :1], gain_in
        )
        g_in[...] += terms
        d_middle = d_attn[at, :].astype(jnp.float32) * (1.0 / RESIDUAL_SCALE)
        grad_slots[k % 2] = d_middle + d_values
        deliver(k, k % 2).start()
    packing[...] = jnp.zeros(packing.shape, jnp.float32)
    lines = gains.rows
    at = 0
    for whole in (g_in, g_mid, g_q, g_kv):
        share = whole.shape[1] // n
        piece = 32 if share % 32 == 0 else 16
        for dest in range(n):
            for place in range(0, share, piece):
                row, column = divmod(at + place, HEAD)
                row += dest * lines
                first = dest * share + place
                packing[row : row + 1, column : column + piece] = whole[:, first : first + piece]
        at += share
    packed[...] = packing[...].astype(jnp.bfloat16)
    gains.start_core()
    feed.pump(*shares[4])
    gains.finish_core()
    gains.start_step(0)
    feed.pump(*shares[5])
    feed.pump(*shares[6])
    for step in range(qa.count - 1):
        for item in (qa, kva, gains):
            item.finish_step(step)
    deliver(2, 0).wait()
    deliver(3, 1).wait()
    for item in (*plans, feed.line):
        item.drain()


def down_tail(
    n, tp, sum_q, sum_lat, q_pre, lat_raw, tokens, d_attn, gain_row, g_mid, w_qa, w_kva, cos, sin,
    f_part, attn, feed_chunks, collective_id,
):
    rows, width = tokens.shape
    rank = q_pre.shape[1]
    vmem = pl.BlockSpec(memory_space=pltpu.VMEM)
    anywhere = pl.BlockSpec(memory_space=pl.ANY)
    half, full = jnp.bfloat16, jnp.float32
    dma = pltpu.SemaphoreType.DMA
    share = (2 * width + rank + KVR) // n
    lines = -(-share // (32 * HEAD)) * 32
    plans = [
        Scatter(n, width // n, rank, False),
        Scatter(n, width // n, KVR + ROPE, False),
        Scatter(n, lines, HEAD, True),
    ]
    slots = pltpu.VMEM((2, rows // 4, width), full)
    chunked = (-1, CHUNK, width)
    grad_in, qa, kva, gains, layer_out = pl.pallas_call(
        functools.partial(down_tail_kernel, n, tp, plans, feed_chunks),
        out_shape=(
            jax.ShapeDtypeStruct((rows, width), full),
            *[jax.ShapeDtypeStruct((plan.rows, plan.columns), half) for plan in plans],
            jax.ShapeDtypeStruct((feed_chunks, CHUNK, width), half),
        ),
        in_specs=[vmem] * 12 + [anywhere] * 3,
        out_specs=(anywhere, vmem, vmem, vmem, vmem),
        scratch_shapes=[
            pltpu.VMEM((rows, rank), half),
            pltpu.VMEM((rows, KVR + ROPE), half),
            pltpu.VMEM((width, rows), half),
            pltpu.VMEM((rows, HEAD), full),
            pltpu.VMEM((1, width), full),
            pltpu.VMEM((1, rank), full),
            pltpu.VMEM((1, KVR), full),
            pltpu.VMEM((n * lines, HEAD), half),
            pltpu.VMEM((n * lines, HEAD), full),
            slots,
            dma((2,)),
            *[shape for plan in plans for shape in plan.scratch()],
            *feed_scratch(feed_chunks, width),
        ],
        compiler_params=pltpu.CompilerParams(
            vmem_limit_bytes=MIDDLE_VMEM, collective_id=collective_id, has_side_effects=True
        ),
        cost_estimate=pl.CostEstimate(
            flops=4 * rows * width * (rank + KVR + ROPE),
            bytes_accessed=40 * 1024 * 1024,
            transcendentals=rows,
        ),
        name=f"down_tail_{collective_id}",
    )(
        sum_q,
        sum_lat,
        q_pre,
        lat_raw,
        tokens,
        d_attn,
        gain_row,
        g_mid,
        w_qa,
        w_kva,
        cos,
        sin,
        *[array.reshape(chunked) for array in (f_part, tokens, attn)],
    )
    gains = gains.astype(full).reshape(-1)
    ends = [0]
    for size in (width, width, rank, KVR):
        ends.append(ends[-1] + size // n)
    own_gains = [gains[first:last] for first, last in zip(ends, ends[1:])]
    return grad_in, qa, kva, own_gains, layer_out.reshape(-1, width)


CHUNK = 16
BLOCK = 8 * CHUNK
LAG = 2
MIDDLE_VMEM = 63 * 1024 * 1024


def middle_kernel(
    n, lag, ob, tokens_in, cot_in, gain, w_out, w_gate, w_up, w_down,
    tt_to, d_to, f_to, act_to, dg_to, du_to, h_to, df_to,
    tt, d_out, f_out, act_out, dg_out, du_out, h_out, df_out,
    tokens, cot, own, up, wo, wg, wu, wd, d_acc, f_acc, w_sems, out_sems, *sems,
):
    line = LineSum(n, own, up, tt, sems, lag)
    width = tokens.shape[1]
    hidden = wg.shape[0]
    chunks, chunk = own.shape[:2]
    per_block = BLOCK // chunk
    blocks = chunks // per_block
    block_lag = -(-(per_block + line.land_lag) // per_block)
    tiles = [(c, min(c + 512, width)) for c in range(0, width, 512)]
    quarter = hidden // 4 // 128 * 128
    cuts = [0, quarter, 2 * quarter, 3 * quarter, hidden]
    loads = [
        pltpu.make_async_copy(source, target, w_sems.at[k])
        for k, (source, target) in enumerate(
            (
                (w_out, wo),
                (tokens_in, tokens),
                (cot_in, cot),
                (w_gate, wg),
                (w_up, wu),
                (w_down, wd),
            )
        )
    ]
    kept = ((d_out, d_to), (f_out, f_to), (act_out, act_to), (dg_out, dg_to), (du_out, du_to))
    kept += ((h_out, h_to), (df_out, df_to))

    def keep(b):
        rows = pl.ds(pl.multiple_of(b * BLOCK, BLOCK), BLOCK)
        copies = [
            pltpu.make_async_copy(source.at[rows, :], target.at[rows, :], out_sems.at[k, b])
            for k, (source, target) in enumerate(kept)
        ]
        some = pl.ds(b * per_block, per_block)
        return copies + [
            pltpu.make_async_copy(tt.at[some], tt_to.at[some], out_sems.at[len(kept), b])
        ]

    for load in loads:
        load.start()
    barrier = pltpu.get_barrier_semaphore()
    line.greet(barrier)
    line.wait_greetings(barrier, 0)

    def project(b, carry):
        rows = pl.ds(pl.multiple_of(b * BLOCK, BLOCK), BLOCK)
        for first, last in tiles:
            part = dot_nt(ob[rows, :], wo[first:last, :]).astype(jnp.bfloat16)
            for k in range(per_block):
                own[per_block * b + k, :, first:last] = part[k * chunk : (k + 1) * chunk, :]
        for k in range(per_block):
            line.leaf(per_block * b + k)
        return carry

    def normalize(b, part):
        for k in range(part * per_block // 2, (part + 1) * per_block // 2, 2):
            rows = pl.ds(pl.multiple_of(b * BLOCK + k * chunk, 2 * chunk), 2 * chunk)
            sums = jnp.concatenate([tt[b * per_block + k], tt[b * per_block + k + 1]], axis=0)
            middle = tokens[rows, :].astype(jnp.float32) + RESIDUAL_SCALE * sums.astype(jnp.float32)
            h_out[rows, :] = (middle * norm_scale(middle) * gain[:, width : 2 * width]).astype(jnp.bfloat16)

    def feed(b, i):
        rows = pl.ds(pl.multiple_of(b * BLOCK, BLOCK), BLOCK)
        first, last = cuts[i], cuts[i + 1]
        if i == 0:
            normalize(b, 0)
            normalize(b, 1)
            df_out[rows, :] = (RESIDUAL_SCALE * cot[rows, :].astype(jnp.float32)).astype(
                jnp.bfloat16
            )
        gate = dot_nt(h_out[rows, :], wg[first:last, :])
        upper = dot_nt(h_out[rows, :], wu[first:last, :])
        d_act = dot_nt(df_out[rows, :], wd[first:last, :])
        sig = jax.nn.sigmoid(gate)
        silu = gate * sig
        act_out[rows, first:last] = (silu * upper).astype(jnp.bfloat16)
        dg_out[rows, first:last] = (d_act * upper * sig * (1.0 + gate * (1.0 - sig))).astype(
            jnp.bfloat16
        )
        du_out[rows, first:last] = (d_act * silu).astype(jnp.bfloat16)

    def feed_back(b, i):
        rows = pl.ds(pl.multiple_of(b * BLOCK, BLOCK), BLOCK)
        first, last = cuts[i], cuts[i + 1]
        act, dg, du = (ref[rows, first:last] for ref in (act_out, dg_out, du_out))
        for lo, hi in tiles:
            d_part = dot_nn(dg, wg[first:last, lo:hi]) + dot_nn(du, wu[first:last, lo:hi])
            f_part = dot_nn(act, wd[first:last, lo:hi])
            if i:
                d_part = d_part + d_acc[:, lo:hi]
                f_part = f_part + f_acc[:, lo:hi]
            if i < 3:
                d_acc[:, lo:hi] = d_part
                f_acc[:, lo:hi] = f_part
            else:
                d_out[rows, lo:hi] = d_part.astype(jnp.bfloat16)
                f_out[rows, lo:hi] = f_part.astype(jnp.bfloat16)

    loads[0].wait()
    lax.fori_loop(0, blocks, project, 0)

    def outer(o, carry):
        b = o - block_lag

        @pl.when(b == 0)
        def _():
            for load in loads[1:]:
                load.wait()

        share = per_block // 8
        for i in range(4):
            for step, work in enumerate((feed, feed_back)):

                @pl.when(o * per_block < line.ticks)
                def _(at=(2 * i + step) * share):
                    for k in range(share):
                        line.duty(o * per_block + at + k)

                @pl.when(b >= 0)
                def _(i=i, work=work):
                    work(b, i)

        @pl.when(b >= 0)
        def _():
            for copy in keep(b):
                copy.start()

        return carry

    lax.fori_loop(0, blocks + block_lag, outer, 0)
    line.drain()

    def finish(b, carry):
        for copy in keep(b):
            copy.wait()
        return carry

    lax.fori_loop(0, blocks, finish, 0)


def middle_layer(n, ob, tokens, cot, gains, w_out, w_gate, w_up, w_down, collective_id):
    rows, width = tokens.shape
    hidden = w_gate.shape[0]
    chunks = rows // CHUNK
    vmem = pl.BlockSpec(memory_space=pltpu.VMEM)
    anywhere = pl.BlockSpec(memory_space=pl.ANY)
    half = jnp.bfloat16
    dma = pltpu.SemaphoreType.DMA
    attn, *rest = pl.pallas_call(
        functools.partial(middle_kernel, n, LAG),
        out_shape=(
            jax.ShapeDtypeStruct((chunks, CHUNK, width), half),
            jax.ShapeDtypeStruct((rows, width), half),
            jax.ShapeDtypeStruct((rows, width), half),
            jax.ShapeDtypeStruct((rows, hidden), half),
            jax.ShapeDtypeStruct((rows, hidden), half),
            jax.ShapeDtypeStruct((rows, hidden), half),
            jax.ShapeDtypeStruct((rows, width), half),
            jax.ShapeDtypeStruct((rows, width), half),
        ),
        in_specs=[vmem, anywhere, anywhere, vmem] + [anywhere] * 4,
        out_specs=(anywhere,) * 8,
        scratch_shapes=[
            pltpu.VMEM((chunks, CHUNK, width), half),
            pltpu.VMEM((rows, width), half),
            pltpu.VMEM((rows, width), half),
            pltpu.VMEM((rows, hidden), half),
            pltpu.VMEM((rows, hidden), half),
            pltpu.VMEM((rows, hidden), half),
            pltpu.VMEM((rows, width), half),
            pltpu.VMEM((rows, width), half),
            pltpu.VMEM((rows, width), half),
            pltpu.VMEM((rows, width), half),
            pltpu.VMEM((chunks, CHUNK, width), half),
            pltpu.VMEM((chunks, CHUNK, width), half),
            pltpu.VMEM(w_out.shape, half),
            pltpu.VMEM(w_gate.shape, half),
            pltpu.VMEM(w_up.shape, half),
            pltpu.VMEM(w_down.shape, half),
            pltpu.VMEM((BLOCK, width), jnp.float32),
            pltpu.VMEM((BLOCK, width), jnp.float32),
            dma((6,)),
            dma((8, rows // BLOCK)),
            *line_sems(chunks),
        ],
        compiler_params=pltpu.CompilerParams(
            vmem_limit_bytes=MIDDLE_VMEM, collective_id=collective_id, has_side_effects=True
        ),
        cost_estimate=pl.CostEstimate(
            flops=2 * rows * width * (6 * hidden + ob.shape[1]),
            bytes_accessed=64 * 1024 * 1024,
            transcendentals=rows * hidden,
        ),
        name=f"middle_layer_{collective_id}",
    )(ob, tokens, cot, gains, w_out, w_gate, w_up, w_down)
    return attn.reshape(rows, width), *rest


def norm_scale(values):
    return lax.rsqrt(jnp.mean(values * values, axis=-1, keepdims=True) + EPSILON)


def norm_back(incoming, values, inv_rms, gain_vec):
    weighted = incoming * gain_vec
    mean = jnp.mean(weighted * values, axis=-1, keepdims=True)
    d_values = inv_rms * weighted - values * (inv_rms * inv_rms * inv_rms) * mean
    return d_values, jnp.sum(incoming * values * inv_rms, axis=0, keepdims=True)


def rope_tile(tile, cos, sin, lane):
    left = pltpu.roll(tile, HEAD - ROPE // 2, 1)
    right = pltpu.roll(tile, ROPE // 2, 1)
    swapped = jnp.where(lane < ROPE // 2, -left, right)
    return jnp.where(lane < ROPE, tile * cos + swapped * sin, 0.0)


def rope_tile_back(tile, cos, sin, lane):
    shifted = tile * sin
    left = pltpu.roll(shifted, HEAD - ROPE // 2, 1)
    right = pltpu.roll(shifted, ROPE // 2, 1)
    swapped = jnp.where(lane < ROPE // 2, left, -right)
    return jnp.where(lane < ROPE, tile * cos + swapped, 0.0)


def split_gains(gains, width, rank):
    ends = (0, width, 2 * width, 2 * width + rank, 2 * width + rank + KVR)
    return [gains[:, first:last] for first, last in zip(ends, ends[1:])]


def head_kernel(
    n, block_map, lengths, tokens, gains, rates, w_qa, w_kva, w_qb,
    out, q_latent, q_pre, lat_raw, cos, sin, qx, qt,
    own, normed, w_rope, flat, local_sem, step_sends, step_lands, core_sends, core_lands,
):
    gain_in, _, gain_q, gain_kv = split_gains(gains, tokens.shape[1], w_qa.shape[1])
    heads = qx.shape[1]
    count = n.bit_length() - 1
    me = lax.axis_index("ctx")
    rows = own.shape[0]
    half = rows // 2
    block = rows // 4
    barrier = pltpu.get_barrier_semaphore()
    for bit in range(count):
        pl.semaphore_signal(barrier, inc=1, device_id={"ctx": me ^ (1 << bit)}, device_id_type=MESH)
    orders = (tuple(range(1, count)), tuple(range(count - 1, 0, -1)))
    lane = lax.broadcasted_iota(jnp.int32, (block, HEAD), 1)
    w_rope[...] = jnp.zeros(w_rope.shape, jnp.bfloat16)
    w_rope[:ROPE, :] = w_kva[KVR : KVR + ROPE, :]

    starts = starts_of(lengths)
    places = lax.broadcasted_iota(jnp.int32, (half, HEAD), 0)
    lanes = lax.broadcasted_iota(jnp.int32, (half, HEAD), 1)
    for j in range(2):
        at = pl.ds(j * half, half)
        place = block_map[j, me] * half + places
        angles = (place - begin_of(place, starts)).astype(jnp.float32) * rates[...]
        cos[at, :] = jnp.where(lanes < ROPE, jnp.cos(angles), 0.0)
        sin[at, :] = jnp.where(lanes < ROPE, jnp.sin(angles), 0.0)

    def latents(k, carry):
        at = pl.ds(pl.multiple_of(k * block, block), block)
        values = tokens[at, :].astype(jnp.float32)
        normed[at, :] = (values * norm_scale(values) * gain_in).astype(jnp.bfloat16)
        raw = dot_nt(normed[at, :], w_kva[:KVR, :])
        lat_raw[at, :] = raw
        own[at, :KVR] = (raw * norm_scale(raw) * gain_kv).astype(jnp.bfloat16)
        rope = rope_tile(dot_nt(normed[at, :], w_rope[...]), cos[at, :], sin[at, :], lane)
        own[at, KVR:] = rope[:, :ROPE].astype(jnp.bfloat16)
        return carry

    lax.fori_loop(0, 4, latents, 0)
    pl.semaphore_wait(barrier, count)
    local = pltpu.make_async_copy(own, out.at[me], local_sem)
    local.start()

    def chip_copy(part, step, slot, block, first):
        at = pl.ds(part * half, half)
        return pltpu.make_async_remote_copy(
            src_ref=own.at[at, :] if first else out.at[block, at, :],
            dst_ref=out.at[block, at, :],
            send_sem=step_sends.at[part, step, slot],
            recv_sem=step_lands.at[part, step, slot],
            device_id={"ctx": me ^ (1 << orders[part][step])},
            device_id_type=MESH,
        )

    def core_copy(block, slot, first):
        return pltpu.make_async_remote_copy(
            src_ref=own if first else out.at[block],
            dst_ref=out.at[block],
            send_sem=core_sends.at[slot],
            recv_sem=core_lands.at[slot],
            device_id={"ctx": me ^ 1},
            device_id_type=MESH,
        )

    def query(k, carry):
        at = pl.ds(pl.multiple_of(k * block, block), block)
        pre = dot_nn(normed[at, :], w_qa[...])
        q_pre[at, :] = pre
        q_latent[at, :] = (pre * norm_scale(pre) * gain_q).astype(jnp.bfloat16)
        return carry

    def queries(j):
        here = pl.ds(j * half, half)
        cos_j, sin_j = cos[here, :], sin[here, :]
        width = heads * (NOPE + ROPE)
        for at in range(0, width, WIDE):
            end = min(at + WIDE, width)
            flat[:, at:end] = dot_nt(q_latent[here, :], w_qb[at:end, :])
        for h in range(heads):
            at, shift = head_window(h)
            own_part = pltpu.roll(flat[:, at : at + WIDE], (WIDE - shift) % WIDE, 1)[:, :HEAD]
            nope = jnp.where(lanes < NOPE, own_part, 0.0)
            rope = rope_tile(pltpu.roll(own_part, NOPE, 1), cos_j, sin_j, lanes)
            qx[j, h, :, :HEAD] = nope.astype(jnp.bfloat16)
            qx[j, h, :, HEAD:] = rope.astype(jnp.bfloat16)
            qt[j, h, :NOPE, :] = nope.T[:NOPE, :].astype(jnp.bfloat16)
            qt[j, h, NOPE:, :] = rope.T[:ROPE, :].astype(jnp.bfloat16)

    started = []
    for step in range(count - 1):
        for part, order in enumerate(orders):
            for slot in range(1 << step):
                flips = 0
                for at in range(step):
                    flips |= ((slot >> at) & 1) << order[at]
                copy = chip_copy(part, step, slot, me ^ flips, slot == 0)
                copy.start()
                started.append(copy)
        if step == 0:
            core_copy(me, 0, True).start()
        lax.fori_loop(min(2 * step, 4), min(2 * step + 2, 4) if step < count - 2 else 4, query, 0)
        if step == count - 2:
            queries(0)
        for part, order in enumerate(orders):
            for slot in range(1 << step):
                chip_copy(part, step, slot, me, slot == 0).wait_recv()
    for chip in range(1, n // 2):
        core_copy(me ^ (2 * chip), chip, False).start()
    queries(1)
    for chip in range(n // 2):
        core_copy(me, chip, chip == 0).wait_recv()
    for copy in started:
        copy.wait_send()
    for chip in range(n // 2):
        core_copy(me, chip, chip == 0).wait_send()
    local.wait()


def head_layer(n, block_map, lengths, tokens, gains, w_qa, w_kva, w_qb, collective_id):
    rows, width = tokens.shape
    rank = w_qa.shape[1]
    count = n.bit_length() - 1
    vmem = pl.BlockSpec(memory_space=pltpu.VMEM)
    slots = max(n // 4, 1)
    dma = pltpu.SemaphoreType.DMA
    smem = pl.BlockSpec(memory_space=pltpu.SMEM)
    heads = w_qb.shape[0] // (NOPE + ROPE)
    pairs = (2, heads)
    lane = np.arange(HEAD)
    rates = ROPE_BASE ** (-2.0 * (lane % (ROPE // 2)) / ROPE)
    gathered, *rest = pl.pallas_call(
        functools.partial(head_kernel, n),
        out_shape=(
            jax.ShapeDtypeStruct((n, rows, KVR + ROPE), jnp.bfloat16),
            jax.ShapeDtypeStruct((rows, rank), jnp.bfloat16),
            jax.ShapeDtypeStruct((rows, rank), jnp.float32),
            jax.ShapeDtypeStruct((rows, KVR), jnp.float32),
            jax.ShapeDtypeStruct((rows, HEAD), jnp.float32),
            jax.ShapeDtypeStruct((rows, HEAD), jnp.float32),
            jax.ShapeDtypeStruct((*pairs, rows // 2, WIDE), jnp.bfloat16),
            jax.ShapeDtypeStruct((*pairs, NOPE + ROPE, rows // 2), jnp.bfloat16),
        ),
        in_specs=[smem] * 2 + [vmem] * 6,
        out_specs=(vmem,) * 8,
        scratch_shapes=[
            pltpu.VMEM((rows, KVR + ROPE), jnp.bfloat16),
            pltpu.VMEM((rows, width), jnp.bfloat16),
            pltpu.VMEM((HEAD, width), jnp.bfloat16),
            pltpu.VMEM((rows // 2, window_columns(heads)), jnp.float32),
            dma,
            dma((2, count - 1, slots)),
            dma((2, count - 1, slots)),
            dma((n // 2,)),
            dma((n // 2,)),
        ],
        compiler_params=pltpu.CompilerParams(
            vmem_limit_bytes=VMEM_LIMIT, collective_id=collective_id, has_side_effects=True
        ),
        cost_estimate=pl.CostEstimate(
            flops=2 * rows * width * (rank + KVR + ROPE),
            bytes_accessed=24 * 1024 * 1024,
            transcendentals=rows,
        ),
        name=f"head_layer_{collective_id}",
    )(
        block_map,
        lengths,
        tokens,
        gains,
        jnp.asarray(rates.astype(np.float32).reshape(1, -1)),
        w_qa,
        w_kva,
        w_qb,
    )
    return gathered.reshape(n * rows, -1), *rest


def on_device(
    tokens_in,
    w_qa,
    w_kva,
    w_qb,
    w_kvb,
    w_out,
    w_gate,
    w_up,
    w_down,
    gain_in,
    gain_q,
    gain_kv,
    gain_mid,
    cotangent,
    block_map,
    doc_lengths,
):
    devices = lax.axis_size("ctx")
    block_map = block_map.T
    gains = jnp.concatenate([gain_in, gain_mid, gain_q, gain_kv]).reshape(1, -1)
    latents, q_latent, q_latent_pre, latent_raw, cosine, sine, queries, queries_t = head_layer(
        devices, block_map, doc_lengths, tokens_in, gains, w_qa, w_kva.T, w_qb.T, 0
    )
    attn_f, heads_out, log_totals = attention_forward(
        block_map, doc_lengths, queries, latents, w_kvb
    )
    attention, d_part, feed_part, activation, d_gate, d_up, normed_mid, d_feed = middle_layer(
        lax.axis_size("tp"), heads_out, tokens_in, cotangent, gains, w_out, w_gate.T, w_up.T,
        w_down.T, 5,
    )
    gw_gate, gw_up, d_attention, d_heads, d_gain_mid = gate_up_grads(
        devices, lax.axis_size("tp"), normed_mid, d_gate, d_up, d_part, tokens_in, attention,
        cotangent, gains, w_out, 1,
    )
    d_query_pre, d_latents, gw_kvb = attention_backward(
        block_map, doc_lengths, queries, queries_t, log_totals, attn_f, d_heads, latents, w_kvb,
        cosine, sine,
    )
    chunks = tokens_in.shape[0] // CHUNK
    first_chunks = 3 * chunks // 4
    sum_q, sum_lat, gw_down, gw_out, gw_qb, gw_kvb, out_first = up_tail(
        devices, lax.axis_size("tp"), d_latents, d_query_pre, w_qb.T, gw_kvb, d_attention, heads_out,
        q_latent, d_feed, activation, feed_part, tokens_in, attention, first_chunks, 2,
    )
    grad_in, gw_qa, gw_kva, own_gains, out_second = down_tail(
        devices, lax.axis_size("tp"), sum_q, sum_lat, q_latent_pre, latent_raw, tokens_in,
        d_attention, gains, d_gain_mid, w_qa, w_kva.T, cosine, sine, feed_part, attention,
        chunks - first_chunks, 3,
    )
    out = jnp.concatenate([out_first, out_second], axis=0)
    grads = (gw_qa, gw_kva, gw_qb, gw_kvb, gw_out, gw_gate, gw_up, gw_down)
    return (
        out,
        grad_in,
        *[grad.astype(jnp.float32) for grad in grads],
        own_gains[0],
        own_gains[2],
        own_gains[3],
        own_gains[1],
    )


def solution(mesh):
    return jax.shard_map(
        on_device,
        mesh=mesh,
        in_specs=(
            P("ctx", None),
            P(),
            P(),
            P(None, "tp"),
            P(None, "tp"),
            P(None, "tp"),
            P(None, "tp"),
            P(None, "tp"),
            P(None, "tp"),
            P(),
            P(),
            P(),
            P(),
            P("ctx", None),
            P(),
            P(),
        ),
        out_specs=(
            P("ctx", None),
            P("ctx", None),
            P("ctx", None),
            P("ctx", None),
            P("ctx", "tp"),
            P("ctx", "tp"),
            P("ctx", "tp"),
            P("ctx", "tp"),
            P("ctx", "tp"),
            P("ctx", "tp"),
            P("ctx"),
            P("ctx"),
            P("ctx"),
            P("ctx"),
        ),
        check_vma=False,
    )
```

```python
import functools
import math

import jax
import jax.numpy as jnp
import numpy as np
from jax import lax
from jax.experimental import pallas as pl
from jax.experimental.pallas import tpu as pltpu
from jax.sharding import PartitionSpec as P

KVR = 256
NOPE = 64
ROPE = 32
VDIM = 64
HEAD = NOPE + VDIM
WIDE = 2 * HEAD
MASKED = -1e30
SCORE_SCALE = (NOPE + ROPE) ** (-0.5)
EXP2_SCALE = SCORE_SCALE * math.log2(math.e)
FOLD_AT = 96
SUM_ROWS = 16
VMEM_LIMIT = 56 * 1024 * 1024

EPSILON = 1e-05
ROPE_BASE = 10000.0
RESIDUAL_SCALE = 1.4 / math.sqrt(62.0)


def dot_nn(left_op, right_op):
    return jnp.dot(left_op, right_op, preferred_element_type=jnp.float32)


def dot_nt(left_op, right_op):
    return lax.dot_general(
        left_op, right_op, (((1,), (1,)), ((), ())), preferred_element_type=jnp.float32
    )


def starts_of(lengths):
    starts = [jnp.int32(0)]
    for s in range(lengths.shape[0] - 1):
        starts.append(starts[-1] + lengths[s])
    return starts


def begin_of(place, starts):
    begin = jnp.zeros_like(place)
    for start in starts:
        begin = jnp.where(start <= place, start, begin)
    return begin


def pair_kind(key_block, query_block, starts, block_rows):
    key_first = key_block * block_rows
    query_first = query_block * block_rows
    early = begin_of(query_first, starts)
    late = begin_of(query_first + block_rows - 1, starts)
    needed = (key_block <= query_block) & (key_first + block_rows - 1 >= early)
    whole = (key_block < query_block) & (late <= key_first)
    return needed, whole


def mask_bias(key_block, query_block, starts, block_rows, keys_first):
    key_dim = 0 if keys_first else 1
    shape = (block_rows, block_rows)
    key_place = key_block * block_rows + lax.broadcasted_iota(jnp.int32, shape, key_dim)
    query_place = query_block * block_rows + lax.broadcasted_iota(jnp.int32, shape, 1 - key_dim)
    begin = jnp.zeros(shape, jnp.int32)
    for start in starts:
        begin = jnp.where(start <= query_place, start, begin)
    allowed = (key_place <= query_place) & (key_place >= begin)
    return jnp.where(allowed, 0.0, MASKED)


def shared_key_tile(rope_rows, block_rows):
    place = lax.broadcasted_iota(jnp.int32, (ROPE, HEAD), 0)
    lane = lax.broadcasted_iota(jnp.int32, (ROPE, HEAD), 1)
    eye = jnp.where(place == lane, 1.0, 0.0).astype(jnp.bfloat16)
    tile = dot_nn(rope_rows, eye)
    lanes = lax.broadcasted_iota(jnp.int32, (block_rows, HEAD), 1)
    ones = (lanes >= FOLD_AT) & (lanes < FOLD_AT + 3)
    return jnp.where(ones, 1.0, tile).astype(jnp.bfloat16)


def head_window(h):
    at = h * (NOPE + ROPE)
    return at // HEAD * HEAD, at % HEAD


def window_columns(heads):
    return head_window(heads - 1)[0] + WIDE


def head_groups(heads):
    return [(h, min(h + 2, heads)) for h in range(0, heads, 2)]


def forward_kernel(
    blocks, heads, block_map, lengths, qx, lat, wkvb, o_out, ob_out, u_out,
    wkvt, xs, xr, vt, top, acc, bias, s_ref, p_ref,
):
    block_rows = bias.shape[0]
    q_blocks = qx.shape[0]
    starts = starts_of(lengths)
    own = [block_map[j, lax.axis_index("ctx")] for j in range(q_blocks)]
    for first, last in head_groups(heads):
        wkvt[first * HEAD : last * HEAD, :] = (
            wkvb[:, first * HEAD : last * HEAD].astype(jnp.float32).T.astype(jnp.bfloat16)
        )
    top[...] = jnp.full(top.shape, MASKED, jnp.float32)
    vt[:, VDIM:, :] = jnp.ones((heads, SUM_ROWS, block_rows), jnp.bfloat16)
    acc[...] = jnp.zeros(acc.shape, jnp.float32)

    def pair(j, masked):
        def one(h):
            keys = jnp.concatenate([xs[h], xr[...]], axis=1)
            s_ref[h % 3] = dot_nt(keys, qx[j, h])

        def weigh(h):
            old = top[j, h]
            new = old
            for k in range(0, block_rows, 128):
                part = s_ref[h % 3, k : k + 128, :]
                if masked:
                    part = part + bias[k : k + 128, :]
                    s_ref[h % 3, k : k + 128, :] = part
                new = jnp.maximum(new, jnp.max(part, axis=0, keepdims=True))
            fade = jnp.exp2((old - new) * EXP2_SCALE)
            top[j, h] = new
            for k in range(0, block_rows, 128):
                terms = jnp.exp2((s_ref[h % 3, k : k + 128, :] - new) * EXP2_SCALE)
                p_ref[h % 3, k : k + 128, :] = terms.astype(jnp.bfloat16)
            return fade

        def add(h, fade):
            acc[j, h] = fade * acc[j, h] + dot_nn(vt[h], p_ref[h % 3])

        one(0)
        if heads > 1:
            one(1)
        fades = {}
        for h in range(heads):
            if h + 2 < heads:
                one(h + 2)
            fades[h] = weigh(h)
            if h > 1:
                add(h - 2, fades[h - 2])
        for h in range(max(heads - 2, 0), heads):
            add(h, fades[h])

    def step(r, carry):
        key_block = block_map[lax.rem(r, 2), lax.div(r, 2)]
        kinds = [pair_kind(key_block, own[j], starts, block_rows) for j in range(q_blocks)]
        wanted = functools.reduce(jnp.logical_or, [k[0] for k in kinds])

        @pl.when(wanted)
        def _():
            here = pl.ds(pl.multiple_of(r * block_rows, block_rows), block_rows)
            latent = lat[here, :KVR]
            xr[...] = shared_key_tile(lat[here, KVR : KVR + ROPE], block_rows)
            for first, last in head_groups(heads):
                keys = dot_nn(latent, wkvb[:, first * HEAD : last * HEAD]).astype(jnp.bfloat16)
                values = dot_nt(wkvt[first * HEAD : last * HEAD, :], latent).astype(jnp.bfloat16)
                for h in range(first, last):
                    at = (h - first) * HEAD
                    xs[h] = keys[:, at : at + HEAD]
                    vt[h, :VDIM, :] = values[at + NOPE : at + HEAD, :]

        for j in range(q_blocks):
            needed, whole = kinds[j]

            @pl.when(needed & whole)
            def _():
                pair(j, False)

            @pl.when(needed & jnp.logical_not(whole))
            def _():
                bias[...] = mask_bias(key_block, own[j], starts, block_rows, True)
                pair(j, True)

        return carry

    lax.fori_loop(0, blocks, step, 0)
    for j in range(q_blocks):
        here = pl.ds(j * block_rows, block_rows)
        for first, last in head_groups(heads):
            parts = []
            for h in range(first, last):
                total = acc[j, h, VDIM : VDIM + 1, :]
                parts.append(acc[j, h, :VDIM, :] * (1.0 / total))
                u_out[j, h : h + 1, :] = top[j, h] + jnp.log2(total) * (1.0 / EXP2_SCALE)
            if len(parts) == 1:
                parts.append(jnp.zeros_like(parts[0]))
            both = jnp.concatenate(parts, axis=0).T
            width = (last - first) * VDIM
            o_out[here, first * VDIM : first * VDIM + width] = both[:, :width]
            ob_out[here, first * VDIM : first * VDIM + width] = both[:, :width].astype(jnp.bfloat16)


def attention_forward(block_map, lengths, qx, lat, wkvb):
    q_blocks, heads, block_rows, _ = qx.shape
    blocks = lat.shape[0] // block_rows
    rows = q_blocks * block_rows
    vmem = pl.BlockSpec(memory_space=pltpu.VMEM)
    smem = pl.BlockSpec(memory_space=pltpu.SMEM)
    pairs = q_blocks * blocks * heads // 2
    return pl.pallas_call(
        functools.partial(forward_kernel, blocks, heads),
        out_shape=(
            jax.ShapeDtypeStruct((rows, heads * VDIM), jnp.float32),
            jax.ShapeDtypeStruct((rows, heads * VDIM), jnp.bfloat16),
            jax.ShapeDtypeStruct((q_blocks, 16 * -(-heads // 16), block_rows), jnp.float32),
        ),
        in_specs=[smem] * 2 + [vmem] * 3,
        out_specs=(vmem,) * 3,
        scratch_shapes=[
            pltpu.VMEM((heads * HEAD, KVR), jnp.bfloat16),
            pltpu.VMEM((heads, block_rows, HEAD), jnp.bfloat16),
            pltpu.VMEM((block_rows, HEAD), jnp.bfloat16),
            pltpu.VMEM((heads, VDIM + SUM_ROWS, block_rows), jnp.bfloat16),
            pltpu.VMEM((q_blocks, heads, 1, block_rows), jnp.float32),
            pltpu.VMEM((q_blocks, heads, VDIM + SUM_ROWS, block_rows), jnp.float32),
            pltpu.VMEM((block_rows, block_rows), jnp.float32),
            pltpu.VMEM((3, block_rows, block_rows), jnp.float32),
            pltpu.VMEM((3, block_rows, block_rows), jnp.bfloat16),
        ],
        compiler_params=pltpu.CompilerParams(vmem_limit_bytes=VMEM_LIMIT),
        cost_estimate=pl.CostEstimate(
            flops=pairs * 4 * block_rows * block_rows * WIDE,
            bytes_accessed=16 * 1024 * 1024,
            transcendentals=pairs * block_rows * block_rows,
        ),
        name="attention_forward",
    )(block_map, lengths, qx, lat, wkvb)


def three_terms(column):
    first = column.astype(jnp.bfloat16).astype(jnp.float32)
    rest = column - first
    second = rest.astype(jnp.bfloat16).astype(jnp.float32)
    return first, second, rest - second


def fold_in(tile, column, lane):
    for k, term in enumerate(three_terms(column)):
        tile = jnp.where(lane == FOLD_AT + k, term, tile)
    return tile


def backward_kernel(
    blocks, heads, block_map, lengths, qx, qt, u_in, o_in, dob, lat, wkvb, cos, sin,
    dq_out, dlat, gkvb, xs, xr, qo, dt, dq, dkv, dkpe, gsum, bias, flat, s_ref, p_ref, d_ref,
):
    block_rows = bias.shape[0]
    q_blocks = qx.shape[0]
    starts = starts_of(lengths)
    own = [block_map[j, lax.axis_index("ctx")] for j in range(q_blocks)]
    lane = lax.broadcasted_iota(jnp.int32, (block_rows, HEAD), 1)
    for j in range(q_blocks):
        here = pl.ds(j * block_rows, block_rows)
        logs = u_in[j].T
        for first, last in head_groups(heads):
            d_pair = dob[here, first * VDIM : first * VDIM + HEAD].astype(jnp.float32)
            weighted = d_pair * o_in[here, first * VDIM : first * VDIM + HEAD]
            turned = pltpu.roll(d_pair, VDIM, 1)
            for h in range(first, last):
                mine = lane < VDIM if h == first else lane >= VDIM
                delta = jnp.sum(jnp.where(mine, weighted, 0.0), axis=1, keepdims=True)
                d_head = jnp.where(lane >= VDIM, turned if h == first else d_pair, 0.0)
                q_second = qx[j, h, :, HEAD:].astype(jnp.float32)
                qo[j, h, :block_rows, :HEAD] = qx[j, h, :, :HEAD]
                qo[j, h, :block_rows, HEAD:] = fold_in(q_second, -logs[:, h : h + 1], lane).astype(
                    jnp.bfloat16
                )
                qo[j, h, block_rows:, :HEAD] = d_head.astype(jnp.bfloat16)
                qo[j, h, block_rows:, HEAD:] = fold_in(
                    jnp.zeros((block_rows, HEAD), jnp.float32), -delta, lane
                ).astype(jnp.bfloat16)
                dt[j, h] = d_head.T[VDIM:, :].astype(jnp.bfloat16)
    dq[...] = jnp.zeros(dq.shape, jnp.float32)
    gsum[...] = jnp.zeros(gsum.shape, jnp.float32)

    def pair(j, masked):
        def raw(h):
            keys = jnp.concatenate([xs[h], xr[...]], axis=1)
            s_ref[h % 2] = dot_nt(qo[j, h], keys)

        def weigh(h):
            for k in range(0, block_rows, 128):
                scores = s_ref[h % 2, k : k + 128, :] * EXP2_SCALE
                if masked:
                    scores = scores + bias[k : k + 128, :]
                probs = jnp.exp2(scores)
                p_ref[h % 2, k : k + 128, :] = probs.astype(jnp.bfloat16)
                d_ref[h % 2, k : k + 128, :] = (
                    probs * s_ref[h % 2, block_rows + k : block_rows + k + 128, :]
                ).astype(jnp.bfloat16)

        def add(h):
            keys = jnp.concatenate([xs[h], xr[...]], axis=1)
            d_scores = d_ref[h % 2]
            dq[j, h] += dot_nn(d_scores, keys)
            d_keys = dot_nn(qt[j, h], d_scores)
            dkv[h, :NOPE, :] += d_keys[:NOPE]
            dkpe[...] += d_keys[NOPE:]
            dkv[h, NOPE:, :] += dot_nn(dt[j, h], p_ref[h % 2])

        raw(0)
        for h in range(heads):
            if h + 1 < heads:
                raw(h + 1)
            weigh(h)
            if h:
                add(h - 1)
        add(heads - 1)

    def step(r, carry):
        key_block = block_map[lax.rem(r, 2), lax.div(r, 2)]
        kinds = [pair_kind(key_block, own[j], starts, block_rows) for j in range(q_blocks)]
        wanted = functools.reduce(jnp.logical_or, [k[0] for k in kinds])
        here = pl.ds(pl.multiple_of(r * block_rows, block_rows), block_rows)

        @pl.when(wanted)
        def _():
            latent = lat[here, :KVR]
            xr[...] = shared_key_tile(lat[here, KVR : KVR + ROPE], block_rows)
            for first, last in head_groups(heads):
                keys = dot_nn(latent, wkvb[:, first * HEAD : last * HEAD]).astype(jnp.bfloat16)
                for h in range(first, last):
                    xs[h] = keys[:, (h - first) * HEAD : (h - first + 1) * HEAD]
            dkv[...] = jnp.zeros(dkv.shape, jnp.float32)
            dkpe[...] = jnp.zeros(dkpe.shape, jnp.float32)

        for j in range(q_blocks):
            needed, whole = kinds[j]

            @pl.when(needed & whole)
            def _():
                pair(j, False)

            @pl.when(needed & jnp.logical_not(whole))
            def _():
                bias[...] = mask_bias(key_block, own[j], starts, block_rows, False)
                pair(j, True)

        @pl.when(wanted)
        def _():
            latent = lat[here, :KVR]
            d_latent = jnp.zeros((KVR, block_rows), jnp.float32)
            for h in range(heads):
                d_head = jnp.concatenate(
                    [dkv[h, :NOPE, :] * SCORE_SCALE, dkv[h, NOPE:, :]], axis=0
                ).astype(jnp.bfloat16)
                d_latent += dot_nn(wkvb[:, h * HEAD : (h + 1) * HEAD], d_head)
                gsum[h * HEAD : (h + 1) * HEAD, :] += dot_nn(d_head, latent)
            dlat[here, :KVR] = d_latent.T.astype(jnp.bfloat16)
            rope = jnp.concatenate(
                [dkpe[...] * SCORE_SCALE, jnp.zeros((HEAD - ROPE, block_rows), jnp.float32)], axis=0
            )
            dlat[here, KVR:] = rope.T[:, :ROPE].astype(jnp.bfloat16)

        @pl.when(jnp.logical_not(wanted))
        def _():
            dlat[here, :] = jnp.zeros((block_rows, KVR + ROPE), jnp.bfloat16)

        return carry

    lax.fori_loop(0, blocks, step, 0)
    for h in range(heads):
        gkvb[:, h * HEAD : (h + 1) * HEAD] = gsum[h * HEAD : (h + 1) * HEAD, :].T.astype(
            jnp.bfloat16
        )
    for j in range(q_blocks):
        here = pl.ds(j * block_rows, block_rows)
        cos_j, sin_j = cos[here, :], sin[here, :]
        flat[...] = jnp.zeros(flat.shape, jnp.float32)
        for h in range(heads):
            nope = jnp.where(lane < NOPE, dq[j, h, :, :HEAD], 0.0)
            rope = dq[j, h, :, HEAD:]
            shifted = rope * sin_j
            left = pltpu.roll(shifted, HEAD - ROPE // 2, 1)
            right = pltpu.roll(shifted, ROPE // 2, 1)
            swapped = jnp.where(lane < ROPE // 2, left, jnp.where(lane < ROPE, -right, 0.0))
            back = pltpu.roll(jnp.where(lane < ROPE, rope * cos_j + swapped, 0.0), NOPE, 1)
            whole = jnp.concatenate([(nope + back) * SCORE_SCALE, jnp.zeros_like(nope)], axis=1)
            at, shift = head_window(h)
            flat[:, at : at + WIDE] += pltpu.roll(whole, shift, 1)
        dq_out[here, :] = flat[:, : heads * (NOPE + ROPE)].astype(jnp.bfloat16)


def attention_backward(block_map, lengths, qx, qt, u_in, o_in, dob, lat, wkvb, cos, sin):
    q_blocks, heads, block_rows, _ = qx.shape
    blocks = lat.shape[0] // block_rows
    rows = q_blocks * block_rows
    odd = -(heads * VDIM) % HEAD
    if odd:
        o_in = jnp.pad(o_in, ((0, 0), (0, odd)))
        dob = jnp.pad(dob, ((0, 0), (0, odd)))
    vmem = pl.BlockSpec(memory_space=pltpu.VMEM)
    smem = pl.BlockSpec(memory_space=pltpu.SMEM)
    pairs = q_blocks * blocks * heads // 2
    return pl.pallas_call(
        functools.partial(backward_kernel, blocks, heads),
        out_shape=(
            jax.ShapeDtypeStruct((rows, heads * (NOPE + ROPE)), jnp.bfloat16),
            jax.ShapeDtypeStruct((lat.shape[0], KVR + ROPE), jnp.bfloat16),
            jax.ShapeDtypeStruct((KVR, heads * HEAD), jnp.bfloat16),
        ),
        in_specs=[smem] * 2 + [vmem] * 9,
        out_specs=(vmem,) * 3,
        scratch_shapes=[
            pltpu.VMEM((heads, block_rows, HEAD), jnp.bfloat16),
            pltpu.VMEM((block_rows, HEAD), jnp.bfloat16),
            pltpu.VMEM((q_blocks, heads, 2 * block_rows, WIDE), jnp.bfloat16),
            pltpu.VMEM((q_blocks, heads, VDIM, block_rows), jnp.bfloat16),
            pltpu.VMEM((q_blocks, heads, block_rows, WIDE), jnp.float32),
            pltpu.VMEM((heads, HEAD, block_rows), jnp.float32),
            pltpu.VMEM((ROPE, block_rows), jnp.float32),
            pltpu.VMEM((heads * HEAD, KVR), jnp.float32),
            pltpu.VMEM((block_rows, block_rows), jnp.float32),
            pltpu.VMEM((block_rows, window_columns(heads)), jnp.float32),
            pltpu.VMEM((2, 2 * block_rows, block_rows), jnp.float32),
            pltpu.VMEM((2, block_rows, block_rows), jnp.bfloat16),
            pltpu.VMEM((2, block_rows, block_rows), jnp.bfloat16),
        ],
        compiler_params=pltpu.CompilerParams(vmem_limit_bytes=VMEM_LIMIT),
        cost_estimate=pl.CostEstimate(
            flops=pairs * 8 * block_rows * block_rows * WIDE,
            bytes_accessed=24 * 1024 * 1024,
            transcendentals=pairs * block_rows * block_rows,
        ),
        name="attention_backward",
    )(block_map, lengths, qx, qt, u_in, o_in, dob, lat, wkvb, cos, sin)


MESH = pl.DeviceIdType.MESH


class LineSum:
    def __init__(self, n, own, landing, total, sems, lag):
        self.n, self.own, self.landing, self.total, self.lag = n, own, landing, total, lag
        self.up_send, self.up_land, self.down_send, self.back_send, self.down_land = sems
        self.me = lax.axis_index("tp")
        self.root = (n - 1) // 2
        self.chunks = own.shape[0]
        self.has_left, self.has_right = self.me > 0, self.me < n - 1
        self.root_lag = (n - 1 - self.root) * lag
        self.land_lag = 2 * self.root_lag
        self.ticks = self.chunks + self.land_lag

    def greet(self, barrier):
        me = self.me
        for there, other in ((self.has_left, me - 1), (self.has_right, me + 1)):

            @pl.when(there)
            def _(other=other):
                pl.semaphore_signal(barrier, inc=1, device_id={"tp": other}, device_id_type=MESH)

    def wait_greetings(self, barrier, others):
        both = self.has_left & self.has_right

        @pl.when(both)
        def _():
            pl.semaphore_wait(barrier, 2 + others)

        @pl.when(jnp.logical_not(both))
        def _():
            pl.semaphore_wait(barrier, 1 + others)

    def copy_to(self, source, target, send, land, c, other):
        return pltpu.make_async_remote_copy(
            src_ref=source.at[c],
            dst_ref=target.at[c],
            send_sem=send.at[c],
            recv_sem=land.at[c],
            device_id={"tp": other},
            device_id_type=MESH,
        )

    def rise_left(self, c):
        return self.copy_to(self.own, self.landing, self.up_send, self.up_land, c, self.me + 1)

    def rise_right(self, c):
        return self.copy_to(self.own, self.landing, self.up_send, self.up_land, c, self.me - 1)

    def rise_last(self, c):
        return self.copy_to(self.own, self.total, self.up_send, self.down_land, c, self.me - 1)

    def fall_right(self, c):
        return self.copy_to(self.total, self.total, self.down_send, self.down_land, c, self.me + 1)

    def fall_left(self, c):
        return self.copy_to(self.total, self.total, self.back_send, self.down_land, c, self.me - 1)

    def rise(self, c):
        me, root = self.me, self.root
        rises = [(me == root + 1, self.rise_last)]
        if root:
            rises.append((me < root, self.rise_left))
        if self.n - 1 > root + 1:
            rises.append((me > root + 1, self.rise_right))
        for who, copy in rises:

            @pl.when(who)
            def _(copy=copy):
                copy(c).start()

    def inside(self, c):
        return (c >= 0) & (c < self.chunks)

    def added(self, refs, c):
        sums = refs[0][c].astype(jnp.float32)
        for ref in refs[1:]:
            sums = sums + ref[c].astype(jnp.float32)
        return sums.astype(self.total.dtype)

    def leaf(self, c):
        is_leaf = self.me == self.n - 1
        if self.root:
            is_leaf = is_leaf | (self.me == 0)

        @pl.when(is_leaf & self.inside(c))
        def _():
            self.rise(c)

    def leaves(self):
        def body(c, carry):
            self.leaf(c)
            return carry

        lax.fori_loop(0, self.chunks, body, 0)

    def pump(self, first, last):
        def body(t, carry):
            self.duty(t)
            return carry

        lax.fori_loop(first, last, body, 0)

    def duty(self, t):
        me, root = self.me, self.root
        if self.n > 3:
            c = t - self.lag * jnp.where(me < root, me, self.n - 1 - me)

            @pl.when((me != root) & self.has_left & self.has_right & self.inside(c))
            def _():
                self.rise_right(c).wait_recv()
                self.own[c] = self.added([self.own, self.landing], c)
                self.rise(c)

        c_root = t - self.root_lag

        @pl.when((me == root) & self.inside(c_root))
        def _():
            if root:
                self.rise_left(c_root).wait_recv()
            self.fall_right(c_root).wait_recv()
            terms = [self.own, self.landing, self.total] if root else [self.own, self.total]
            self.total[c_root] = self.added(terms, c_root)
            self.fall_right(c_root).start()
            if root:
                self.fall_left(c_root).start()

        c_fall = t - self.root_lag - self.lag * jnp.where(me < root, root - me, me - root)

        @pl.when((me != root) & self.inside(c_fall))
        def _():
            self.fall_right(c_fall).wait_recv()

            @pl.when((me > root) & self.has_right)
            def _():
                self.fall_right(c_fall).start()

            @pl.when((me < root) & self.has_left)
            def _():
                self.fall_left(c_fall).start()

    def landed(self, t):
        return t - self.land_lag

    def drain(self):
        me = self.me

        def body(c, carry):
            @pl.when(me != self.root)
            def _():
                self.rise_right(c).wait_send()

            @pl.when((me >= self.root) & self.has_right)
            def _():
                self.fall_right(c).wait_send()

            @pl.when((me <= self.root) & self.has_left)
            def _():
                self.fall_left(c).wait_send()

            return carry

        lax.fori_loop(0, self.chunks, body, 0)


def line_sems(chunks):
    return [pltpu.SemaphoreType.DMA((chunks,))] * 5


def scatter_blocks(bits_left):
    chips = []
    for value in range(1 << len(bits_left)):
        chip = 0
        for at, bit in enumerate(bits_left):
            chip = chip + (((value >> at) & 1) << (bit - 1))
        chips.append(chip)
    return chips


class Scatter:
    def __init__(self, n, rows, columns, is_given):
        self.n, self.rows, self.columns, self.is_given = n, rows, columns, is_given
        self.count = n.bit_length() - 1
        self.parts = 2 if rows % 32 == 0 else 1

    def scratch(self):
        n, count = self.n, self.count
        half = jnp.bfloat16
        dma = pltpu.SemaphoreType.DMA
        shapes = [pltpu.VMEM((n // 2, self.rows, self.columns), half)]
        if not self.is_given:
            shapes.append(pltpu.VMEM((n // 2, self.rows, self.columns), half))
        for step in range(count - 1):
            shapes.append(pltpu.VMEM((n >> (step + 2), self.rows, self.columns), half))
        shapes += [dma((n // 2,))] * 2
        for step in range(count - 1):
            shapes += [dma((2, n >> (step + 2)))] * 2
        return shapes

    def bind(self, take, source, emit):
        self.held = take(1)[0]
        self.sent = None if self.is_given else take(1)[0]
        self.landed = take(self.count - 1)
        self.core_sems = take(2)
        self.step_sems = [take(2) for _ in range(self.count - 1)]
        self.source, self.emit = source, emit
        self.me = lax.axis_index("ctx")
        self.core = self.me & 1
        self.chips = self.n // 2
        self.orders = (tuple(range(1, self.count)), tuple(range(self.count - 1, 0, -1)))
        self.tiles = [(c, min(c + 512, self.columns)) for c in range(0, self.columns, 512)]
        return self

    def own(self, dest, first, last):
        at = pl.ds(pl.multiple_of(dest * self.rows, 16), self.rows)
        if self.is_given:
            return self.source[at, first:last].astype(jnp.float32)
        return dot_nn(self.source[0][at, :], self.source[1][:, first:last])

    def core_copy(self, chip):
        if self.is_given:
            at = pl.ds(pl.multiple_of((2 * chip + 1 - self.core) * self.rows, 16), self.rows)
            source = self.source.at[at, :]
        else:
            source = self.sent.at[chip]
        return pltpu.make_async_remote_copy(
            src_ref=source,
            dst_ref=self.held.at[chip],
            send_sem=self.core_sems[0].at[chip],
            recv_sem=self.core_sems[1].at[chip],
            device_id={"ctx": self.me ^ 1},
            device_id_type=MESH,
        )

    def step_copies(self, step):
        half = self.rows // self.parts
        me = self.me
        copies = []
        for part, order in enumerate(self.orders[: self.parts]):
            bit = order[step]
            at = pl.ds(part * half, half)
            for slot, free in enumerate(scatter_blocks(sorted(order[step + 1 :]))):
                keep = free + ((me >> bit) & 1) * (1 << (bit - 1))
                send = free + (1 - ((me >> bit) & 1)) * (1 << (bit - 1))
                for b in order[:step]:
                    own = ((me >> b) & 1) * (1 << (b - 1))
                    keep, send = keep + own, send + own
                copy = pltpu.make_async_remote_copy(
                    src_ref=self.held.at[send, at, :],
                    dst_ref=self.landed[step].at[slot, at, :],
                    send_sem=self.step_sems[step][0].at[part, slot],
                    recv_sem=self.step_sems[step][1].at[part, slot],
                    device_id={"ctx": me ^ (1 << bit)},
                    device_id_type=MESH,
                )
                copies.append((copy, keep, slot, at))
        return copies

    def start_core(self, also=None):
        def body(chip, carry):
            if also is not None:
                also(chip)
            if not self.is_given:
                for first, last in self.tiles:
                    self.sent[chip, :, first:last] = self.own(
                        2 * chip + 1 - self.core, first, last
                    ).astype(jnp.bfloat16)
            self.core_copy(chip).start()
            return carry

        lax.fori_loop(0, self.chips, body, 0)

    def finish_core(self, also=None):
        def body(chip, carry):
            if also is not None:
                also(chip)
            self.core_copy(chip).wait_recv()
            for first, last in self.tiles:
                total = self.own(2 * chip + self.core, first, last)
                total = total + self.held[chip, :, first:last].astype(jnp.float32)
                self.held[chip, :, first:last] = total.astype(jnp.bfloat16)
            return carry

        lax.fori_loop(0, self.chips, body, 0)

    def start_step(self, step):
        for copy, _, _, _ in self.step_copies(step):
            copy.start()

    def finish_step(self, step):
        for copy, keep, slot, at in self.step_copies(step):
            copy.wait_recv()
            for first, last in self.tiles:
                total = self.held[keep, at, first:last].astype(jnp.float32)
                total = total + self.landed[step][slot, at, first:last].astype(jnp.float32)
                if step == self.count - 2:
                    self.emit(at, first, last, total)
                else:
                    self.held[keep, at, first:last] = total.astype(jnp.bfloat16)
        if step + 1 < self.count - 1:
            self.start_step(step + 1)

    def drain(self):
        def body(chip, carry):
            self.core_copy(chip).wait_send()
            return carry

        lax.fori_loop(0, self.chips, body, 0)
        for step in range(self.count - 1):
            for copy, _, _, _ in self.step_copies(step):
                copy.wait_send()


def taker(refs):
    refs = list(refs)

    def take(k):
        taken = refs[:k]
        del refs[:k]
        return taken

    return take


def store_in(ref):
    def emit(at, first, last, total):
        ref[at, first:last] = total.astype(ref.dtype)

    return emit


def turn(source, target):
    def body(c, carry):
        at = pl.ds(pl.multiple_of(c * 128, 128), 128)
        target[at, :] = source[:, at].astype(jnp.float32).T.astype(jnp.bfloat16)
        return carry

    lax.fori_loop(0, source.shape[1] // 128, body, 0)


def greet_ctx(n, barrier):
    me = lax.axis_index("ctx")
    count = n.bit_length() - 1
    for bit in range(count):
        pl.semaphore_signal(barrier, inc=1, device_id={"ctx": me ^ (1 << bit)}, device_id_type=MESH)
    return count


def spread(waits, ticks):
    portion = -(-ticks // waits)
    return [(min(k * portion, ticks), min((k + 1) * portion, ticks)) for k in range(waits)]


def gate_up_kernel(
    n, tp, plans, normed, d_gate, d_up, terms, tokens, attn, cot, gain_row, w_out,
    gate_out, up_out, d_attn, d_heads, g_mid, *refs,
):
    take = taker(refs)
    own, landing, sums, normed_t, slots, in_sems, own_sem = take(7)
    line = LineSum(tp, own, landing, sums, take(5), LAG)
    gate = plans[0].bind(take, (normed_t, d_gate), store_in(gate_out))
    up = plans[1].bind(take, (normed_t, d_up), store_in(up_out))
    width = normed.shape[1]
    blocks = normed.shape[0] // BLOCK
    per_block = BLOCK // CHUNK
    load = pltpu.make_async_copy(terms, own, own_sem)
    load.start()
    barrier = pltpu.get_barrier_semaphore()
    others = greet_ctx(n, barrier)
    line.greet(barrier)

    def fetch(b):
        rows = pl.ds(b * BLOCK, BLOCK)
        return [
            pltpu.make_async_copy(
                source.at[rows, :], slots.at[b % 2, k], in_sems.at[b % 2, k]
            )
            for k, source in enumerate((tokens, attn, cot))
        ]

    for b in range(min(2, blocks)):
        for copy in fetch(b):
            copy.start()
    g_mid[...] = jnp.zeros(g_mid.shape, jnp.float32)

    def norm(b):
        for copy in fetch(b):
            copy.wait()
        for part in range(0, BLOCK, 2 * CHUNK):
            rows = pl.ds(b * BLOCK + part, 2 * CHUNK)
            here = pl.ds(part, 2 * CHUNK)
            c = b * per_block + part // CHUNK
            incoming = jnp.concatenate([sums[c], sums[c + 1]], axis=0).astype(jnp.float32)
            middle = slots[b % 2, 0, here, :].astype(jnp.float32)
            middle = middle + RESIDUAL_SCALE * slots[b % 2, 1, here, :].astype(jnp.float32)
            d_norm, gain_terms = norm_back(
                incoming, middle, norm_scale(middle), gain_row[:, width : 2 * width]
            )
            g_mid[...] += gain_terms
            total = slots[b % 2, 2, here, :].astype(jnp.float32) + d_norm
            d_attn[rows, :] = (RESIDUAL_SCALE * total).astype(jnp.bfloat16)
        rows = pl.ds(b * BLOCK, BLOCK)
        d_heads[rows, :] = dot_nn(d_attn[rows, :], w_out[...]).astype(jnp.bfloat16)
        if b + 2 < blocks:
            for copy in fetch(b + 2):
                copy.start()

    load.wait()
    line.wait_greetings(barrier, others)
    line.leaves()
    turn(normed, normed_t)
    chips = n // 2
    gate.start_core()
    gate.finish_core(line.duty)
    gate.start_step(0)
    up.start_core(lambda chip: line.duty(chips + chip))
    up.finish_core(lambda chip: line.duty(2 * chips + chip))
    up.start_step(0)
    steps = [(item, step) for step in range(gate.count - 1) for item in (gate, up)]
    done = 3 * chips
    next_block = 0
    for (item, step), (first, last) in zip(steps, spread(len(steps), line.ticks - done)):
        line.pump(done + first, done + last)
        while next_block < blocks and line.landed(done + last - 1) >= (next_block + 1) * per_block - 1:
            norm(next_block)
            next_block += 1
        item.finish_step(step)
    for item in (gate, up, line):
        item.drain()


def gate_up_grads(
    n, tp, normed, d_gate, d_up, terms, tokens, attn, cot, gain_row, w_out, collective_id
):
    rows, width = normed.shape
    hidden = d_gate.shape[1]
    head_width = w_out.shape[1]
    vmem = pl.BlockSpec(memory_space=pltpu.VMEM)
    anywhere = pl.BlockSpec(memory_space=pl.ANY)
    half = jnp.bfloat16
    plans = [Scatter(n, width // n, hidden, False) for _ in range(2)]
    chunked = (rows // CHUNK, CHUNK, width)
    return pl.pallas_call(
        functools.partial(gate_up_kernel, n, tp, plans),
        out_shape=(
            jax.ShapeDtypeStruct((width // n, hidden), half),
            jax.ShapeDtypeStruct((width // n, hidden), half),
            jax.ShapeDtypeStruct((rows, width), half),
            jax.ShapeDtypeStruct((rows, head_width), half),
            jax.ShapeDtypeStruct((1, width), jnp.float32),
        ),
        in_specs=[vmem] * 3 + [anywhere] * 4 + [vmem] * 2,
        out_specs=(vmem,) * 5,
        scratch_shapes=[
            pltpu.VMEM(chunked, half),
            pltpu.VMEM(chunked, half),
            pltpu.VMEM(chunked, half),
            pltpu.VMEM((width, rows), half),
            pltpu.VMEM((2, 3, BLOCK, width), half),
            pltpu.SemaphoreType.DMA((2, 3)),
            pltpu.SemaphoreType.DMA,
            *line_sems(rows // CHUNK),
            *plans[0].scratch(),
            *plans[1].scratch(),
        ],
        compiler_params=pltpu.CompilerParams(
            vmem_limit_bytes=MIDDLE_VMEM, collective_id=collective_id, has_side_effects=True
        ),
        cost_estimate=pl.CostEstimate(
            flops=2 * rows * width * (2 * hidden + head_width),
            bytes_accessed=28 * 1024 * 1024,
            transcendentals=0,
        ),
        name=f"gate_up_grads_{collective_id}",
    )(normed, d_gate, d_up, terms.reshape(chunked), tokens, attn, cot, gain_row, w_out)


TAIL_CHUNK = 64


def up_tail_kernel(
    n, tp, plans, d_lat, d_query, w_qb, g_kvb, d_attn, ob, q_latent, d_feed, act,
    sum_q, sum_lat, down_out, out_out, qb_out, kvb_out, *refs,
):
    take = taker(refs)
    own_q, land_q, own_lat, land_lat, d_attn_t, q_latent_t, d_feed_t = take(7)
    line_q = LineSum(tp, own_q, land_q, sum_q, take(5), LAG)
    line_lat = LineSum(tp, own_lat, land_lat, sum_lat, take(5), LAG)
    chunk = own_q.shape[1]

    def store_lat(at, first, last, total):
        for k in range(at.size // chunk):
            own_lat[at.start // chunk + k, :, first:last] = total[
                k * chunk : (k + 1) * chunk
            ].astype(jnp.bfloat16)

    lat, down, out, qb, kvb = plans
    lat.bind(take, d_lat, store_lat)
    down.bind(take, (d_feed_t, act), store_in(down_out))
    out.bind(take, (d_attn_t, ob), store_in(out_out))
    qb.bind(take, (q_latent_t, d_query), store_in(qb_out))
    kvb.bind(take, g_kvb, store_in(kvb_out))
    barrier = pltpu.get_barrier_semaphore()
    others = greet_ctx(n, barrier)
    line_q.greet(barrier)
    line_q.wait_greetings(barrier, others)
    lat.start_core()

    def query(c, carry):
        rows = pl.ds(pl.multiple_of(c * 2 * chunk, 2 * chunk), 2 * chunk)
        part = dot_nn(d_query[rows, :], w_qb[...]).astype(jnp.bfloat16)
        for k in range(2):
            own_q[2 * c + k] = part[k * chunk : (k + 1) * chunk]
            line_q.leaf(2 * c + k)
        return carry

    lax.fori_loop(0, own_q.shape[0] // 2, query, 0)
    lat.finish_core()
    lat.start_step(0)
    turn(d_feed, d_feed_t)
    down.start_core()
    lat.finish_step(0)
    down.finish_core()
    for step in range(1, lat.count - 1):
        lat.finish_step(step)
    line_lat.leaves()
    down.start_step(0)
    chips = n // 2
    turn(d_attn, d_attn_t)
    out.start_core(line_q.duty)
    out.finish_core(lambda chip: line_q.duty(chips + chip))
    out.start_step(0)
    kvb.start_core()
    turn(q_latent, q_latent_t)
    qb.start_core(lambda chip: line_q.duty(2 * chips + chip))
    kvb.finish_core()
    kvb.start_step(0)
    qb.finish_core(line_lat.duty)
    qb.start_step(0)
    steps = [(item, step) for step in range(lat.count - 1) for item in (down, out, kvb, qb)]
    q_share = spread(len(steps), line_q.ticks - 3 * chips)
    lat_share = spread(len(steps), line_lat.ticks - chips)
    for (item, step), (a, b), (c, d) in zip(steps, q_share, lat_share):
        line_q.pump(3 * chips + a, 3 * chips + b)
        line_lat.pump(chips + c, chips + d)
        item.finish_step(step)
    for item in (*plans, line_q, line_lat):
        item.drain()


def up_tail(n, tp, d_lat, d_query, w_qb, g_kvb, d_attn, ob, q_latent, d_feed, act, collective_id):
    rows, width = d_attn.shape
    rank = q_latent.shape[1]
    hidden = act.shape[1]
    lat_width = d_lat.shape[1]
    vmem = pl.BlockSpec(memory_space=pltpu.VMEM)
    half = jnp.bfloat16
    plans = [
        Scatter(n, rows, lat_width, True),
        Scatter(n, width // n, hidden, False),
        Scatter(n, width // n, ob.shape[1], False),
        Scatter(n, rank // n, d_query.shape[1], False),
        Scatter(n, KVR // n, g_kvb.shape[1], True),
    ]
    q_shape = (rows // TAIL_CHUNK, TAIL_CHUNK, rank)
    lat_shape = (rows // TAIL_CHUNK, TAIL_CHUNK, lat_width)
    sum_q, sum_lat, *grads = pl.pallas_call(
        functools.partial(up_tail_kernel, n, tp, plans),
        out_shape=(
            jax.ShapeDtypeStruct(q_shape, half),
            jax.ShapeDtypeStruct(lat_shape, half),
            *[jax.ShapeDtypeStruct((plan.rows, plan.columns), half) for plan in plans[1:]],
        ),
        in_specs=[vmem] * 9,
        out_specs=(vmem,) * 6,
        scratch_shapes=[
            pltpu.VMEM(q_shape, half),
            pltpu.VMEM(q_shape, half),
            pltpu.VMEM(lat_shape, half),
            pltpu.VMEM(lat_shape, half),
            pltpu.VMEM((width, rows), half),
            pltpu.VMEM((rank, rows), half),
            pltpu.VMEM((width, rows), half),
            *line_sems(rows // TAIL_CHUNK),
            *line_sems(rows // TAIL_CHUNK),
            *[shape for plan in plans for shape in plan.scratch()],
        ],
        compiler_params=pltpu.CompilerParams(
            vmem_limit_bytes=MIDDLE_VMEM, collective_id=collective_id, has_side_effects=True
        ),
        cost_estimate=pl.CostEstimate(
            flops=2 * rows * width * (hidden + ob.shape[1]) + 4 * rows * rank * d_query.shape[1],
            bytes_accessed=32 * 1024 * 1024,
            transcendentals=0,
        ),
        name=f"up_tail_{collective_id}",
    )(d_lat, d_query, w_qb, g_kvb, d_attn, ob, q_latent, d_feed, act)
    return sum_q.reshape(rows, rank), sum_lat.reshape(rows, lat_width), *grads


def down_tail_kernel(
    n, plans, sum_q, sum_lat, q_pre, lat_raw, tokens, d_attn, gain_row, g_mid, w_qa, w_kva, cos, sin, grad_in, qa_out, kva_out, gains_out,
    d_q, d_kv, normed_t, scales, g_in, g_q, g_kv, packed, packing, grad_slots, out_sems,
    *refs,
):
    take = taker(refs)
    qa, kva, gains = plans
    qa.bind(take, (normed_t, d_q), store_in(qa_out))
    kva.bind(take, (normed_t, d_kv), store_in(kva_out))
    gains.bind(take, packed, store_in(gains_out))
    rows = tokens.shape[0]
    block = rows // 4
    gain_in, _, gain_q, gain_kv = split_gains(gain_row, tokens.shape[1], q_pre.shape[1])
    lane = lax.broadcasted_iota(jnp.int32, (block, HEAD), 1)
    barrier = pltpu.get_barrier_semaphore()
    others = greet_ctx(n, barrier)

    def rows_of(k):
        return pl.ds(pl.multiple_of(k * block, block), block)

    def deliver(k, slot):
        return pltpu.make_async_copy(
            grad_slots.at[slot], grad_in.at[rows_of(k), :], out_sems.at[slot]
        )

    for ref in (g_in, g_q, g_kv):
        ref[...] = jnp.zeros(ref.shape, jnp.float32)

    def norms(k, carry):
        at = rows_of(k)
        pre = q_pre[at, :]
        d_pre, terms = norm_back(
            sum_q[at, :].astype(jnp.float32), pre, norm_scale(pre), gain_q
        )
        g_q[...] += terms
        d_q[at, :] = d_pre.astype(jnp.bfloat16)
        raw = lat_raw[at, :]
        d_raw, terms = norm_back(
            sum_lat[at, :KVR].astype(jnp.float32), raw, norm_scale(raw), gain_kv
        )
        g_kv[...] += terms
        d_kv[at, :KVR] = d_raw.astype(jnp.bfloat16)
        rope = sum_lat[at, KVR:].astype(jnp.float32)
        rope = jnp.concatenate([rope, jnp.zeros((block, HEAD - ROPE), jnp.float32)], axis=1)
        rope = rope_tile_back(rope, cos[at, :], sin[at, :], lane)
        d_kv[at, KVR:] = rope[:, :ROPE].astype(jnp.bfloat16)
        values = tokens[at, :].astype(jnp.float32)
        scale = norm_scale(values)
        scales[at, :] = jnp.broadcast_to(scale, (block, HEAD))
        normed = values * scale * gain_in
        for c in range(0, normed.shape[1], 128):
            normed_t[c : c + 128, at] = normed[:, c : c + 128].T.astype(jnp.bfloat16)
        return carry

    lax.fori_loop(0, 4, norms, 0)
    pl.semaphore_wait(barrier, others)
    qa.start_core()
    kva.start_core()
    qa.finish_core()
    qa.start_step(0)
    kva.finish_core()
    kva.start_step(0)
    for k in range(4):
        at = pl.ds(k * block, block)
        if k >= 2:
            deliver(k - 2, k % 2).wait()
        d_normed = dot_nt(d_q[at, :], w_qa[...]) + dot_nn(d_kv[at, :], w_kva[...])
        d_values, terms = norm_back(
            d_normed, tokens[at, :].astype(jnp.float32), scales[at, :1], gain_in
        )
        g_in[...] += terms
        d_middle = d_attn[at, :].astype(jnp.float32) * (1.0 / RESIDUAL_SCALE)
        grad_slots[k % 2] = d_middle + d_values
        deliver(k, k % 2).start()
    packing[...] = jnp.zeros(packing.shape, jnp.float32)
    lines = gains.rows
    at = 0
    for whole in (g_in, g_mid, g_q, g_kv):
        share = whole.shape[1] // n
        piece = 32 if share % 32 == 0 else 16
        for dest in range(n):
            for place in range(0, share, piece):
                row, column = divmod(at + place, HEAD)
                row += dest * lines
                first = dest * share + place
                packing[row : row + 1, column : column + piece] = whole[:, first : first + piece]
        at += share
    packed[...] = packing[...].astype(jnp.bfloat16)
    gains.start_core()
    gains.finish_core()
    gains.start_step(0)
    for step in range(qa.count - 1):
        for item in (qa, kva, gains):
            item.finish_step(step)
    deliver(2, 0).wait()
    deliver(3, 1).wait()
    for item in plans:
        item.drain()


def down_tail(
    n, sum_q, sum_lat, q_pre, lat_raw, tokens, d_attn, gain_row, g_mid, w_qa, w_kva, cos, sin,
    collective_id,
):
    rows, width = tokens.shape
    rank = q_pre.shape[1]
    vmem = pl.BlockSpec(memory_space=pltpu.VMEM)
    anywhere = pl.BlockSpec(memory_space=pl.ANY)
    half, full = jnp.bfloat16, jnp.float32
    dma = pltpu.SemaphoreType.DMA
    share = (2 * width + rank + KVR) // n
    lines = -(-share // (32 * HEAD)) * 32
    plans = [
        Scatter(n, width // n, rank, False),
        Scatter(n, width // n, KVR + ROPE, False),
        Scatter(n, lines, HEAD, True),
    ]
    slots = pltpu.VMEM((2, rows // 4, width), full)
    grad_in, qa, kva, gains = pl.pallas_call(
        functools.partial(down_tail_kernel, n, plans),
        out_shape=(
            jax.ShapeDtypeStruct((rows, width), full),
            *[jax.ShapeDtypeStruct((plan.rows, plan.columns), half) for plan in plans],
        ),
        in_specs=[vmem] * 12,
        out_specs=(anywhere, vmem, vmem, vmem),
        scratch_shapes=[
            pltpu.VMEM((rows, rank), half),
            pltpu.VMEM((rows, KVR + ROPE), half),
            pltpu.VMEM((width, rows), half),
            pltpu.VMEM((rows, HEAD), full),
            pltpu.VMEM((1, width), full),
            pltpu.VMEM((1, rank), full),
            pltpu.VMEM((1, KVR), full),
            pltpu.VMEM((n * lines, HEAD), half),
            pltpu.VMEM((n * lines, HEAD), full),
            slots,
            dma((2,)),
            *[shape for plan in plans for shape in plan.scratch()],
        ],
        compiler_params=pltpu.CompilerParams(
            vmem_limit_bytes=MIDDLE_VMEM, collective_id=collective_id, has_side_effects=True
        ),
        cost_estimate=pl.CostEstimate(
            flops=4 * rows * width * (rank + KVR + ROPE),
            bytes_accessed=40 * 1024 * 1024,
            transcendentals=rows,
        ),
        name=f"down_tail_{collective_id}",
    )(
        sum_q,
        sum_lat,
        q_pre,
        lat_raw,
        tokens,
        d_attn,
        gain_row,
        g_mid,
        w_qa,
        w_kva,
        cos,
        sin,
    )
    gains = gains.astype(full).reshape(-1)
    ends = [0]
    for size in (width, width, rank, KVR):
        ends.append(ends[-1] + size // n)
    return grad_in, qa, kva, [gains[first:last] for first, last in zip(ends, ends[1:])]


CHUNK = 16
BLOCK = 8 * CHUNK
LAG = 2
MIDDLE_VMEM = 63 * 1024 * 1024


def middle_kernel(
    n, lag, ob, tokens_in, cot_in, gain, w_out, w_gate, w_up, w_down,
    tt_to, d_to, f_to, act_to, dg_to, du_to, h_to, df_to,
    tt, d_out, f_out, act_out, dg_out, du_out, h_out, df_out,
    tokens, cot, own, up, wo, wg, wu, wd, d_acc, f_acc, w_sems, out_sems, *sems,
):
    line = LineSum(n, own, up, tt, sems, lag)
    width = tokens.shape[1]
    hidden = wg.shape[0]
    chunks, chunk = own.shape[:2]
    per_block = BLOCK // chunk
    blocks = chunks // per_block
    block_lag = -(-(per_block + line.land_lag) // per_block)
    tiles = [(c, min(c + 512, width)) for c in range(0, width, 512)]
    quarter = hidden // 4 // 128 * 128
    cuts = [0, quarter, 2 * quarter, 3 * quarter, hidden]
    loads = [
        pltpu.make_async_copy(source, target, w_sems.at[k])
        for k, (source, target) in enumerate(
            (
                (w_out, wo),
                (tokens_in, tokens),
                (cot_in, cot),
                (w_gate, wg),
                (w_up, wu),
                (w_down, wd),
            )
        )
    ]
    kept = ((d_out, d_to), (f_out, f_to), (act_out, act_to), (dg_out, dg_to), (du_out, du_to))
    kept += ((h_out, h_to), (df_out, df_to))

    def keep(b):
        rows = pl.ds(pl.multiple_of(b * BLOCK, BLOCK), BLOCK)
        copies = [
            pltpu.make_async_copy(source.at[rows, :], target.at[rows, :], out_sems.at[k, b])
            for k, (source, target) in enumerate(kept)
        ]
        some = pl.ds(b * per_block, per_block)
        return copies + [
            pltpu.make_async_copy(tt.at[some], tt_to.at[some], out_sems.at[len(kept), b])
        ]

    for load in loads:
        load.start()
    barrier = pltpu.get_barrier_semaphore()
    line.greet(barrier)
    line.wait_greetings(barrier, 0)

    def project(b, carry):
        rows = pl.ds(pl.multiple_of(b * BLOCK, BLOCK), BLOCK)
        for first, last in tiles:
            part = dot_nt(ob[rows, :], wo[first:last, :]).astype(jnp.bfloat16)
            for k in range(per_block):
                own[per_block * b + k, :, first:last] = part[k * chunk : (k + 1) * chunk, :]
        for k in range(per_block):
            line.leaf(per_block * b + k)
        return carry

    def normalize(b, part):
        for k in range(part * per_block // 2, (part + 1) * per_block // 2, 2):
            rows = pl.ds(pl.multiple_of(b * BLOCK + k * chunk, 2 * chunk), 2 * chunk)
            sums = jnp.concatenate([tt[b * per_block + k], tt[b * per_block + k + 1]], axis=0)
            middle = tokens[rows, :].astype(jnp.float32) + RESIDUAL_SCALE * sums.astype(jnp.float32)
            h_out[rows, :] = (middle * norm_scale(middle) * gain[:, width : 2 * width]).astype(jnp.bfloat16)

    def feed(b, i):
        rows = pl.ds(pl.multiple_of(b * BLOCK, BLOCK), BLOCK)
        first, last = cuts[i], cuts[i + 1]
        if i == 0:
            normalize(b, 0)
            normalize(b, 1)
            df_out[rows, :] = (RESIDUAL_SCALE * cot[rows, :].astype(jnp.float32)).astype(
                jnp.bfloat16
            )
        gate = dot_nt(h_out[rows, :], wg[first:last, :])
        upper = dot_nt(h_out[rows, :], wu[first:last, :])
        d_act = dot_nt(df_out[rows, :], wd[first:last, :])
        sig = jax.nn.sigmoid(gate)
        silu = gate * sig
        act_out[rows, first:last] = (silu * upper).astype(jnp.bfloat16)
        dg_out[rows, first:last] = (d_act * upper * sig * (1.0 + gate * (1.0 - sig))).astype(
            jnp.bfloat16
        )
        du_out[rows, first:last] = (d_act * silu).astype(jnp.bfloat16)

    def feed_back(b, i):
        rows = pl.ds(pl.multiple_of(b * BLOCK, BLOCK), BLOCK)
        first, last = cuts[i], cuts[i + 1]
        act, dg, du = (ref[rows, first:last] for ref in (act_out, dg_out, du_out))
        for lo, hi in tiles:
            d_part = dot_nn(dg, wg[first:last, lo:hi]) + dot_nn(du, wu[first:last, lo:hi])
            f_part = dot_nn(act, wd[first:last, lo:hi])
            if i:
                d_part = d_part + d_acc[:, lo:hi]
                f_part = f_part + f_acc[:, lo:hi]
            if i < 3:
                d_acc[:, lo:hi] = d_part
                f_acc[:, lo:hi] = f_part
            else:
                d_out[rows, lo:hi] = d_part.astype(jnp.bfloat16)
                f_out[rows, lo:hi] = f_part.astype(jnp.bfloat16)

    loads[0].wait()
    lax.fori_loop(0, blocks, project, 0)

    def outer(o, carry):
        b = o - block_lag

        @pl.when(b == 0)
        def _():
            for load in loads[1:]:
                load.wait()

        share = per_block // 8
        for i in range(4):
            for step, work in enumerate((feed, feed_back)):

                @pl.when(o * per_block < line.ticks)
                def _(at=(2 * i + step) * share):
                    for k in range(share):
                        line.duty(o * per_block + at + k)

                @pl.when(b >= 0)
                def _(i=i, work=work):
                    work(b, i)

        @pl.when(b >= 0)
        def _():
            for copy in keep(b):
                copy.start()

        return carry

    lax.fori_loop(0, blocks + block_lag, outer, 0)
    line.drain()

    def finish(b, carry):
        for copy in keep(b):
            copy.wait()
        return carry

    lax.fori_loop(0, blocks, finish, 0)


def middle_layer(n, ob, tokens, cot, gains, w_out, w_gate, w_up, w_down, collective_id):
    rows, width = tokens.shape
    hidden = w_gate.shape[0]
    chunks = rows // CHUNK
    vmem = pl.BlockSpec(memory_space=pltpu.VMEM)
    anywhere = pl.BlockSpec(memory_space=pl.ANY)
    half = jnp.bfloat16
    dma = pltpu.SemaphoreType.DMA
    attn, *rest = pl.pallas_call(
        functools.partial(middle_kernel, n, LAG),
        out_shape=(
            jax.ShapeDtypeStruct((chunks, CHUNK, width), half),
            jax.ShapeDtypeStruct((rows, width), half),
            jax.ShapeDtypeStruct((rows, width), half),
            jax.ShapeDtypeStruct((rows, hidden), half),
            jax.ShapeDtypeStruct((rows, hidden), half),
            jax.ShapeDtypeStruct((rows, hidden), half),
            jax.ShapeDtypeStruct((rows, width), half),
            jax.ShapeDtypeStruct((rows, width), half),
        ),
        in_specs=[vmem, anywhere, anywhere, vmem] + [anywhere] * 4,
        out_specs=(anywhere,) * 8,
        scratch_shapes=[
            pltpu.VMEM((chunks, CHUNK, width), half),
            pltpu.VMEM((rows, width), half),
            pltpu.VMEM((rows, width), half),
            pltpu.VMEM((rows, hidden), half),
            pltpu.VMEM((rows, hidden), half),
            pltpu.VMEM((rows, hidden), half),
            pltpu.VMEM((rows, width), half),
            pltpu.VMEM((rows, width), half),
            pltpu.VMEM((rows, width), half),
            pltpu.VMEM((rows, width), half),
            pltpu.VMEM((chunks, CHUNK, width), half),
            pltpu.VMEM((chunks, CHUNK, width), half),
            pltpu.VMEM(w_out.shape, half),
            pltpu.VMEM(w_gate.shape, half),
            pltpu.VMEM(w_up.shape, half),
            pltpu.VMEM(w_down.shape, half),
            pltpu.VMEM((BLOCK, width), jnp.float32),
            pltpu.VMEM((BLOCK, width), jnp.float32),
            dma((6,)),
            dma((8, rows // BLOCK)),
            *line_sems(chunks),
        ],
        compiler_params=pltpu.CompilerParams(
            vmem_limit_bytes=MIDDLE_VMEM, collective_id=collective_id, has_side_effects=True
        ),
        cost_estimate=pl.CostEstimate(
            flops=2 * rows * width * (6 * hidden + ob.shape[1]),
            bytes_accessed=64 * 1024 * 1024,
            transcendentals=rows * hidden,
        ),
        name=f"middle_layer_{collective_id}",
    )(ob, tokens, cot, gains, w_out, w_gate, w_up, w_down)
    return attn.reshape(rows, width), *rest


def norm_scale(values):
    return lax.rsqrt(jnp.mean(values * values, axis=-1, keepdims=True) + EPSILON)


def norm_back(incoming, values, inv_rms, gain_vec):
    weighted = incoming * gain_vec
    mean = jnp.mean(weighted * values, axis=-1, keepdims=True)
    d_values = inv_rms * weighted - values * (inv_rms * inv_rms * inv_rms) * mean
    return d_values, jnp.sum(incoming * values * inv_rms, axis=0, keepdims=True)


def rope_tile(tile, cos, sin, lane):
    left = pltpu.roll(tile, HEAD - ROPE // 2, 1)
    right = pltpu.roll(tile, ROPE // 2, 1)
    swapped = jnp.where(lane < ROPE // 2, -left, right)
    return jnp.where(lane < ROPE, tile * cos + swapped * sin, 0.0)


def rope_tile_back(tile, cos, sin, lane):
    shifted = tile * sin
    left = pltpu.roll(shifted, HEAD - ROPE // 2, 1)
    right = pltpu.roll(shifted, ROPE // 2, 1)
    swapped = jnp.where(lane < ROPE // 2, left, -right)
    return jnp.where(lane < ROPE, tile * cos + swapped, 0.0)


def split_gains(gains, width, rank):
    ends = (0, width, 2 * width, 2 * width + rank, 2 * width + rank + KVR)
    return [gains[:, first:last] for first, last in zip(ends, ends[1:])]


def head_kernel(
    n, block_map, lengths, tokens, gains, rates, w_qa, w_kva, w_qb,
    out, q_latent, q_pre, lat_raw, cos, sin, qx, qt,
    own, normed, w_rope, flat, local_sem, step_sends, step_lands, core_sends, core_lands,
):
    gain_in, _, gain_q, gain_kv = split_gains(gains, tokens.shape[1], w_qa.shape[1])
    heads = qx.shape[1]
    count = n.bit_length() - 1
    me = lax.axis_index("ctx")
    rows = own.shape[0]
    half = rows // 2
    block = rows // 4
    barrier = pltpu.get_barrier_semaphore()
    for bit in range(count):
        pl.semaphore_signal(barrier, inc=1, device_id={"ctx": me ^ (1 << bit)}, device_id_type=MESH)
    orders = (tuple(range(1, count)), tuple(range(count - 1, 0, -1)))
    lane = lax.broadcasted_iota(jnp.int32, (block, HEAD), 1)
    w_rope[...] = jnp.zeros(w_rope.shape, jnp.bfloat16)
    w_rope[:ROPE, :] = w_kva[KVR : KVR + ROPE, :]

    starts = starts_of(lengths)
    places = lax.broadcasted_iota(jnp.int32, (half, HEAD), 0)
    lanes = lax.broadcasted_iota(jnp.int32, (half, HEAD), 1)
    for j in range(2):
        at = pl.ds(j * half, half)
        place = block_map[j, me] * half + places
        angles = (place - begin_of(place, starts)).astype(jnp.float32) * rates[...]
        cos[at, :] = jnp.where(lanes < ROPE, jnp.cos(angles), 0.0)
        sin[at, :] = jnp.where(lanes < ROPE, jnp.sin(angles), 0.0)

    def latents(k, carry):
        at = pl.ds(pl.multiple_of(k * block, block), block)
        values = tokens[at, :].astype(jnp.float32)
        normed[at, :] = (values * norm_scale(values) * gain_in).astype(jnp.bfloat16)
        raw = dot_nt(normed[at, :], w_kva[:KVR, :])
        lat_raw[at, :] = raw
        own[at, :KVR] = (raw * norm_scale(raw) * gain_kv).astype(jnp.bfloat16)
        rope = rope_tile(dot_nt(normed[at, :], w_rope[...]), cos[at, :], sin[at, :], lane)
        own[at, KVR:] = rope[:, :ROPE].astype(jnp.bfloat16)
        return carry

    lax.fori_loop(0, 4, latents, 0)
    pl.semaphore_wait(barrier, count)
    local = pltpu.make_async_copy(own, out.at[me], local_sem)
    local.start()

    def chip_copy(part, step, slot, block, first):
        at = pl.ds(part * half, half)
        return pltpu.make_async_remote_copy(
            src_ref=own.at[at, :] if first else out.at[block, at, :],
            dst_ref=out.at[block, at, :],
            send_sem=step_sends.at[part, step, slot],
            recv_sem=step_lands.at[part, step, slot],
            device_id={"ctx": me ^ (1 << orders[part][step])},
            device_id_type=MESH,
        )

    def core_copy(block, slot, first):
        return pltpu.make_async_remote_copy(
            src_ref=own if first else out.at[block],
            dst_ref=out.at[block],
            send_sem=core_sends.at[slot],
            recv_sem=core_lands.at[slot],
            device_id={"ctx": me ^ 1},
            device_id_type=MESH,
        )

    def query(k, carry):
        at = pl.ds(pl.multiple_of(k * block, block), block)
        pre = dot_nn(normed[at, :], w_qa[...])
        q_pre[at, :] = pre
        q_latent[at, :] = (pre * norm_scale(pre) * gain_q).astype(jnp.bfloat16)
        return carry

    def queries(j):
        here = pl.ds(j * half, half)
        cos_j, sin_j = cos[here, :], sin[here, :]
        width = heads * (NOPE + ROPE)
        for at in range(0, width, WIDE):
            end = min(at + WIDE, width)
            flat[:, at:end] = dot_nt(q_latent[here, :], w_qb[at:end, :])
        for h in range(heads):
            at, shift = head_window(h)
            own_part = pltpu.roll(flat[:, at : at + WIDE], (WIDE - shift) % WIDE, 1)[:, :HEAD]
            nope = jnp.where(lanes < NOPE, own_part, 0.0)
            rope = rope_tile(pltpu.roll(own_part, NOPE, 1), cos_j, sin_j, lanes)
            qx[j, h, :, :HEAD] = nope.astype(jnp.bfloat16)
            qx[j, h, :, HEAD:] = rope.astype(jnp.bfloat16)
            qt[j, h, :NOPE, :] = nope.T[:NOPE, :].astype(jnp.bfloat16)
            qt[j, h, NOPE:, :] = rope.T[:ROPE, :].astype(jnp.bfloat16)

    started = []
    for step in range(count - 1):
        for part, order in enumerate(orders):
            for slot in range(1 << step):
                flips = 0
                for at in range(step):
                    flips |= ((slot >> at) & 1) << order[at]
                copy = chip_copy(part, step, slot, me ^ flips, slot == 0)
                copy.start()
                started.append(copy)
        if step == 0:
            core_copy(me, 0, True).start()
        lax.fori_loop(min(2 * step, 4), min(2 * step + 2, 4) if step < count - 2 else 4, query, 0)
        if step == count - 2:
            queries(0)
        for part, order in enumerate(orders):
            for slot in range(1 << step):
                chip_copy(part, step, slot, me, slot == 0).wait_recv()
    for chip in range(1, n // 2):
        core_copy(me ^ (2 * chip), chip, False).start()
    queries(1)
    for chip in range(n // 2):
        core_copy(me, chip, chip == 0).wait_recv()
    for copy in started:
        copy.wait_send()
    for chip in range(n // 2):
        core_copy(me, chip, chip == 0).wait_send()
    local.wait()


def head_layer(n, block_map, lengths, tokens, gains, w_qa, w_kva, w_qb, collective_id):
    rows, width = tokens.shape
    rank = w_qa.shape[1]
    count = n.bit_length() - 1
    vmem = pl.BlockSpec(memory_space=pltpu.VMEM)
    slots = max(n // 4, 1)
    dma = pltpu.SemaphoreType.DMA
    smem = pl.BlockSpec(memory_space=pltpu.SMEM)
    heads = w_qb.shape[0] // (NOPE + ROPE)
    pairs = (2, heads)
    lane = np.arange(HEAD)
    rates = ROPE_BASE ** (-2.0 * (lane % (ROPE // 2)) / ROPE)
    gathered, *rest = pl.pallas_call(
        functools.partial(head_kernel, n),
        out_shape=(
            jax.ShapeDtypeStruct((n, rows, KVR + ROPE), jnp.bfloat16),
            jax.ShapeDtypeStruct((rows, rank), jnp.bfloat16),
            jax.ShapeDtypeStruct((rows, rank), jnp.float32),
            jax.ShapeDtypeStruct((rows, KVR), jnp.float32),
            jax.ShapeDtypeStruct((rows, HEAD), jnp.float32),
            jax.ShapeDtypeStruct((rows, HEAD), jnp.float32),
            jax.ShapeDtypeStruct((*pairs, rows // 2, WIDE), jnp.bfloat16),
            jax.ShapeDtypeStruct((*pairs, NOPE + ROPE, rows // 2), jnp.bfloat16),
        ),
        in_specs=[smem] * 2 + [vmem] * 6,
        out_specs=(vmem,) * 8,
        scratch_shapes=[
            pltpu.VMEM((rows, KVR + ROPE), jnp.bfloat16),
            pltpu.VMEM((rows, width), jnp.bfloat16),
            pltpu.VMEM((HEAD, width), jnp.bfloat16),
            pltpu.VMEM((rows // 2, window_columns(heads)), jnp.float32),
            dma,
            dma((2, count - 1, slots)),
            dma((2, count - 1, slots)),
            dma((n // 2,)),
            dma((n // 2,)),
        ],
        compiler_params=pltpu.CompilerParams(
            vmem_limit_bytes=VMEM_LIMIT, collective_id=collective_id, has_side_effects=True
        ),
        cost_estimate=pl.CostEstimate(
            flops=2 * rows * width * (rank + KVR + ROPE),
            bytes_accessed=24 * 1024 * 1024,
            transcendentals=rows,
        ),
        name=f"head_layer_{collective_id}",
    )(
        block_map,
        lengths,
        tokens,
        gains,
        jnp.asarray(rates.astype(np.float32).reshape(1, -1)),
        w_qa,
        w_kva,
        w_qb,
    )
    return gathered.reshape(n * rows, -1), *rest


def on_device(
    tokens_in,
    w_qa,
    w_kva,
    w_qb,
    w_kvb,
    w_out,
    w_gate,
    w_up,
    w_down,
    gain_in,
    gain_q,
    gain_kv,
    gain_mid,
    cotangent,
    block_map,
    doc_lengths,
):
    devices = lax.axis_size("ctx")
    block_map = block_map.T
    gains = jnp.concatenate([gain_in, gain_mid, gain_q, gain_kv]).reshape(1, -1)
    latents, q_latent, q_latent_pre, latent_raw, cosine, sine, queries, queries_t = head_layer(
        devices, block_map, doc_lengths, tokens_in, gains, w_qa, w_kva.T, w_qb.T, 0
    )
    attn_f, heads_out, log_totals = attention_forward(
        block_map, doc_lengths, queries, latents, w_kvb
    )
    attention, d_part, feed_part, activation, d_gate, d_up, normed_mid, d_feed = middle_layer(
        lax.axis_size("tp"), heads_out, tokens_in, cotangent, gains, w_out, w_gate.T, w_up.T,
        w_down.T, 5,
    )
    gw_gate, gw_up, d_attention, d_heads, d_gain_mid = gate_up_grads(
        devices, lax.axis_size("tp"), normed_mid, d_gate, d_up, d_part, tokens_in, attention,
        cotangent, gains, w_out, 1,
    )
    d_heads, feed_part = lax.optimization_barrier((d_heads, feed_part))
    feed_own = lax.psum_scatter(feed_part, "tp", scatter_dimension=0, tiled=True)
    own_rows = feed_own.shape[0]
    own_at = lax.axis_index("tp") * own_rows
    tokens_own = lax.dynamic_slice_in_dim(tokens_in, own_at, own_rows, 0).astype(jnp.float32)
    attention_own = lax.dynamic_slice_in_dim(attention, own_at, own_rows, 0).astype(jnp.float32)
    middle_own = tokens_own + RESIDUAL_SCALE * attention_own
    out_own = (middle_own + RESIDUAL_SCALE * feed_own.astype(jnp.float32)).astype(jnp.bfloat16)
    d_query_pre, d_latents, gw_kvb = attention_backward(
        block_map, doc_lengths, queries, queries_t, log_totals, attn_f, d_heads, latents, w_kvb,
        cosine, sine,
    )
    sum_q, sum_lat, gw_down, gw_out, gw_qb, gw_kvb = up_tail(
        devices, lax.axis_size("tp"), d_latents, d_query_pre, w_qb.T, gw_kvb, d_attention, heads_out,
        q_latent, d_feed, activation, 2,
    )
    sum_q, out_own = lax.optimization_barrier((sum_q, out_own))
    out = lax.all_gather(out_own, "tp", axis=0, tiled=True)
    grad_in, gw_qa, gw_kva, own_gains = down_tail(
        devices, sum_q, sum_lat, q_latent_pre, latent_raw, tokens_in, d_attention, gains,
        d_gain_mid, w_qa, w_kva.T, cosine, sine, 3,
    )
    grads = (gw_qa, gw_kva, gw_qb, gw_kvb, gw_out, gw_gate, gw_up, gw_down)
    return (
        out,
        grad_in,
        *[grad.astype(jnp.float32) for grad in grads],
        own_gains[0],
        own_gains[2],
        own_gains[3],
        own_gains[1],
    )


def solution(mesh):
    return jax.shard_map(
        on_device,
        mesh=mesh,
        in_specs=(
            P("ctx", None),
            P(),
            P(),
            P(None, "tp"),
            P(None, "tp"),
            P(None, "tp"),
            P(None, "tp"),
            P(None, "tp"),
            P(None, "tp"),
            P(),
            P(),
            P(),
            P(),
            P("ctx", None),
            P(),
            P(),
        ),
        out_specs=(
            P("ctx", None),
            P("ctx", None),
            P("ctx", None),
            P("ctx", None),
            P("ctx", "tp"),
            P("ctx", "tp"),
            P("ctx", "tp"),
            P("ctx", "tp"),
            P("ctx", "tp"),
            P("ctx", "tp"),
            P("ctx"),
            P("ctx"),
            P("ctx"),
            P("ctx"),
        ),
        check_vma=False,
    )
```

```python
import functools
import math

import jax
import jax.numpy as jnp
import numpy as np
from jax import lax
from jax.experimental import pallas as pl
from jax.experimental.pallas import tpu as pltpu
from jax.sharding import PartitionSpec as P

KVR = 256
NOPE = 64
ROPE = 32
VDIM = 64
HEAD = NOPE + VDIM
WIDE = 2 * HEAD
MASKED = -1e30
SCORE_SCALE = (NOPE + ROPE) ** (-0.5)
EXP2_SCALE = SCORE_SCALE * math.log2(math.e)
FOLD_AT = 96
SUM_ROWS = 16
VMEM_LIMIT = 56 * 1024 * 1024

EPSILON = 1e-05
ROPE_BASE = 10000.0
RESIDUAL_SCALE = 1.4 / math.sqrt(62.0)


def dot_nn(left_op, right_op):
    return jnp.dot(left_op, right_op, preferred_element_type=jnp.float32)


def dot_nt(left_op, right_op):
    return lax.dot_general(
        left_op, right_op, (((1,), (1,)), ((), ())), preferred_element_type=jnp.float32
    )


def starts_of(lengths):
    starts = [jnp.int32(0)]
    for s in range(lengths.shape[0] - 1):
        starts.append(starts[-1] + lengths[s])
    return starts


def begin_of(place, starts):
    begin = jnp.zeros_like(place)
    for start in starts:
        begin = jnp.where(start <= place, start, begin)
    return begin


def pair_kind(key_block, query_block, starts, block_rows):
    key_first = key_block * block_rows
    query_first = query_block * block_rows
    early = begin_of(query_first, starts)
    late = begin_of(query_first + block_rows - 1, starts)
    needed = (key_block <= query_block) & (key_first + block_rows - 1 >= early)
    whole = (key_block < query_block) & (late <= key_first)
    return needed, whole


def mask_bias(key_block, query_block, starts, block_rows, keys_first):
    key_dim = 0 if keys_first else 1
    shape = (block_rows, block_rows)
    key_place = key_block * block_rows + lax.broadcasted_iota(jnp.int32, shape, key_dim)
    query_place = query_block * block_rows + lax.broadcasted_iota(jnp.int32, shape, 1 - key_dim)
    begin = jnp.zeros(shape, jnp.int32)
    for start in starts:
        begin = jnp.where(start <= query_place, start, begin)
    allowed = (key_place <= query_place) & (key_place >= begin)
    return jnp.where(allowed, 0.0, MASKED)


def shared_key_tile(rope_rows, block_rows):
    place = lax.broadcasted_iota(jnp.int32, (ROPE, HEAD), 0)
    lane = lax.broadcasted_iota(jnp.int32, (ROPE, HEAD), 1)
    eye = jnp.where(place == lane, 1.0, 0.0).astype(jnp.bfloat16)
    tile = dot_nn(rope_rows, eye)
    lanes = lax.broadcasted_iota(jnp.int32, (block_rows, HEAD), 1)
    ones = (lanes >= FOLD_AT) & (lanes < FOLD_AT + 3)
    return jnp.where(ones, 1.0, tile).astype(jnp.bfloat16)


def head_window(h):
    at = h * (NOPE + ROPE)
    return at // HEAD * HEAD, at % HEAD


def window_columns(heads):
    return head_window(heads - 1)[0] + WIDE


def head_groups(heads):
    return [(h, min(h + 2, heads)) for h in range(0, heads, 2)]


def forward_kernel(
    blocks, heads, block_map, lengths, qx, lat, wkvb, o_out, ob_out, u_out,
    wkvt, xs, xr, vt, top, acc, bias, s_ref, p_ref,
):
    block_rows = bias.shape[0]
    q_blocks = qx.shape[0]
    starts = starts_of(lengths)
    own = [block_map[j, lax.axis_index("ctx")] for j in range(q_blocks)]
    for first, last in head_groups(heads):
        wkvt[first * HEAD : last * HEAD, :] = (
            wkvb[:, first * HEAD : last * HEAD].astype(jnp.float32).T.astype(jnp.bfloat16)
        )
    top[...] = jnp.full(top.shape, MASKED, jnp.float32)
    vt[:, VDIM:, :] = jnp.ones((heads, SUM_ROWS, block_rows), jnp.bfloat16)
    acc[...] = jnp.zeros(acc.shape, jnp.float32)

    def pair(j, masked):
        def one(h):
            keys = jnp.concatenate([xs[h], xr[...]], axis=1)
            s_ref[h % 3] = dot_nt(keys, qx[j, h])

        def weigh(h):
            old = top[j, h]
            new = old
            for k in range(0, block_rows, 128):
                part = s_ref[h % 3, k : k + 128, :]
                if masked:
                    part = part + bias[k : k + 128, :]
                    s_ref[h % 3, k : k + 128, :] = part
                new = jnp.maximum(new, jnp.max(part, axis=0, keepdims=True))
            fade = jnp.exp2((old - new) * EXP2_SCALE)
            top[j, h] = new
            for k in range(0, block_rows, 128):
                terms = jnp.exp2((s_ref[h % 3, k : k + 128, :] - new) * EXP2_SCALE)
                p_ref[h % 3, k : k + 128, :] = terms.astype(jnp.bfloat16)
            return fade

        def add(h, fade):
            acc[j, h] = fade * acc[j, h] + dot_nn(vt[h], p_ref[h % 3])

        one(0)
        if heads > 1:
            one(1)
        fades = {}
        for h in range(heads):
            if h + 2 < heads:
                one(h + 2)
            fades[h] = weigh(h)
            if h > 1:
                add(h - 2, fades[h - 2])
        for h in range(max(heads - 2, 0), heads):
            add(h, fades[h])

    def step(r, carry):
        key_block = block_map[lax.rem(r, 2), lax.div(r, 2)]
        kinds = [pair_kind(key_block, own[j], starts, block_rows) for j in range(q_blocks)]
        wanted = functools.reduce(jnp.logical_or, [k[0] for k in kinds])

        @pl.when(wanted)
        def _():
            here = pl.ds(pl.multiple_of(r * block_rows, block_rows), block_rows)
            latent = lat[here, :KVR]
            xr[...] = shared_key_tile(lat[here, KVR : KVR + ROPE], block_rows)
            for first, last in head_groups(heads):
                keys = dot_nn(latent, wkvb[:, first * HEAD : last * HEAD]).astype(jnp.bfloat16)
                values = dot_nt(wkvt[first * HEAD : last * HEAD, :], latent).astype(jnp.bfloat16)
                for h in range(first, last):
                    at = (h - first) * HEAD
                    xs[h] = keys[:, at : at + HEAD]
                    vt[h, :VDIM, :] = values[at + NOPE : at + HEAD, :]

        for j in range(q_blocks):
            needed, whole = kinds[j]

            @pl.when(needed & whole)
            def _():
                pair(j, False)

            @pl.when(needed & jnp.logical_not(whole))
            def _():
                bias[...] = mask_bias(key_block, own[j], starts, block_rows, True)
                pair(j, True)

        return carry

    lax.fori_loop(0, blocks, step, 0)
    for j in range(q_blocks):
        here = pl.ds(j * block_rows, block_rows)
        for first, last in head_groups(heads):
            parts = []
            for h in range(first, last):
                total = acc[j, h, VDIM : VDIM + 1, :]
                parts.append(acc[j, h, :VDIM, :] * (1.0 / total))
                u_out[j, h : h + 1, :] = top[j, h] + jnp.log2(total) * (1.0 / EXP2_SCALE)
            if len(parts) == 1:
                parts.append(jnp.zeros_like(parts[0]))
            both = jnp.concatenate(parts, axis=0).T
            width = (last - first) * VDIM
            o_out[here, first * VDIM : first * VDIM + width] = both[:, :width]
            ob_out[here, first * VDIM : first * VDIM + width] = both[:, :width].astype(jnp.bfloat16)


def attention_forward(block_map, lengths, qx, lat, wkvb):
    q_blocks, heads, block_rows, _ = qx.shape
    blocks = lat.shape[0] // block_rows
    rows = q_blocks * block_rows
    vmem = pl.BlockSpec(memory_space=pltpu.VMEM)
    smem = pl.BlockSpec(memory_space=pltpu.SMEM)
    pairs = q_blocks * blocks * heads // 2
    return pl.pallas_call(
        functools.partial(forward_kernel, blocks, heads),
        out_shape=(
            jax.ShapeDtypeStruct((rows, heads * VDIM), jnp.float32),
            jax.ShapeDtypeStruct((rows, heads * VDIM), jnp.bfloat16),
            jax.ShapeDtypeStruct((q_blocks, 16 * -(-heads // 16), block_rows), jnp.float32),
        ),
        in_specs=[smem] * 2 + [vmem] * 3,
        out_specs=(vmem,) * 3,
        scratch_shapes=[
            pltpu.VMEM((heads * HEAD, KVR), jnp.bfloat16),
            pltpu.VMEM((heads, block_rows, HEAD), jnp.bfloat16),
            pltpu.VMEM((block_rows, HEAD), jnp.bfloat16),
            pltpu.VMEM((heads, VDIM + SUM_ROWS, block_rows), jnp.bfloat16),
            pltpu.VMEM((q_blocks, heads, 1, block_rows), jnp.float32),
            pltpu.VMEM((q_blocks, heads, VDIM + SUM_ROWS, block_rows), jnp.float32),
            pltpu.VMEM((block_rows, block_rows), jnp.float32),
            pltpu.VMEM((3, block_rows, block_rows), jnp.float32),
            pltpu.VMEM((3, block_rows, block_rows), jnp.bfloat16),
        ],
        compiler_params=pltpu.CompilerParams(vmem_limit_bytes=VMEM_LIMIT),
        cost_estimate=pl.CostEstimate(
            flops=pairs * 4 * block_rows * block_rows * WIDE,
            bytes_accessed=16 * 1024 * 1024,
            transcendentals=pairs * block_rows * block_rows,
        ),
        name="attention_forward",
    )(block_map, lengths, qx, lat, wkvb)


def three_terms(column):
    first = column.astype(jnp.bfloat16).astype(jnp.float32)
    rest = column - first
    second = rest.astype(jnp.bfloat16).astype(jnp.float32)
    return first, second, rest - second


def fold_in(tile, column, lane):
    for k, term in enumerate(three_terms(column)):
        tile = jnp.where(lane == FOLD_AT + k, term, tile)
    return tile


def backward_kernel(
    blocks, heads, block_map, lengths, qx, qt, u_in, o_in, dob, lat, wkvb, cos, sin,
    dq_out, dlat, gkvb, xs, xr, qo, dt, dq, dkv, dkpe, gsum, bias, flat, s_ref, p_ref, d_ref,
):
    block_rows = bias.shape[0]
    q_blocks = qx.shape[0]
    starts = starts_of(lengths)
    own = [block_map[j, lax.axis_index("ctx")] for j in range(q_blocks)]
    lane = lax.broadcasted_iota(jnp.int32, (block_rows, HEAD), 1)
    for j in range(q_blocks):
        here = pl.ds(j * block_rows, block_rows)
        logs = u_in[j].T
        for first, last in head_groups(heads):
            d_pair = dob[here, first * VDIM : first * VDIM + HEAD].astype(jnp.float32)
            weighted = d_pair * o_in[here, first * VDIM : first * VDIM + HEAD]
            turned = pltpu.roll(d_pair, VDIM, 1)
            for h in range(first, last):
                mine = lane < VDIM if h == first else lane >= VDIM
                delta = jnp.sum(jnp.where(mine, weighted, 0.0), axis=1, keepdims=True)
                d_head = jnp.where(lane >= VDIM, turned if h == first else d_pair, 0.0)
                q_second = qx[j, h, :, HEAD:].astype(jnp.float32)
                qo[j, h, :block_rows, :HEAD] = qx[j, h, :, :HEAD]
                qo[j, h, :block_rows, HEAD:] = fold_in(q_second, -logs[:, h : h + 1], lane).astype(
                    jnp.bfloat16
                )
                qo[j, h, block_rows:, :HEAD] = d_head.astype(jnp.bfloat16)
                qo[j, h, block_rows:, HEAD:] = fold_in(
                    jnp.zeros((block_rows, HEAD), jnp.float32), -delta, lane
                ).astype(jnp.bfloat16)
                dt[j, h] = d_head.T[VDIM:, :].astype(jnp.bfloat16)
    dq[...] = jnp.zeros(dq.shape, jnp.float32)
    gsum[...] = jnp.zeros(gsum.shape, jnp.float32)

    def pair(j, masked):
        def raw(h):
            keys = jnp.concatenate([xs[h], xr[...]], axis=1)
            s_ref[h % 2] = dot_nt(qo[j, h], keys)

        def weigh(h):
            for k in range(0, block_rows, 128):
                scores = s_ref[h % 2, k : k + 128, :] * EXP2_SCALE
                if masked:
                    scores = scores + bias[k : k + 128, :]
                probs = jnp.exp2(scores)
                p_ref[h % 2, k : k + 128, :] = probs.astype(jnp.bfloat16)
                d_ref[h % 2, k : k + 128, :] = (
                    probs * s_ref[h % 2, block_rows + k : block_rows + k + 128, :]
                ).astype(jnp.bfloat16)

        def add(h):
            keys = jnp.concatenate([xs[h], xr[...]], axis=1)
            d_scores = d_ref[h % 2]
            dq[j, h] += dot_nn(d_scores, keys)
            d_keys = dot_nn(qt[j, h], d_scores)
            dkv[h, :NOPE, :] += d_keys[:NOPE]
            dkpe[...] += d_keys[NOPE:]
            dkv[h, NOPE:, :] += dot_nn(dt[j, h], p_ref[h % 2])

        raw(0)
        for h in range(heads):
            if h + 1 < heads:
                raw(h + 1)
            weigh(h)
            if h:
                add(h - 1)
        add(heads - 1)

    def step(r, carry):
        key_block = block_map[lax.rem(r, 2), lax.div(r, 2)]
        kinds = [pair_kind(key_block, own[j], starts, block_rows) for j in range(q_blocks)]
        wanted = functools.reduce(jnp.logical_or, [k[0] for k in kinds])
        here = pl.ds(pl.multiple_of(r * block_rows, block_rows), block_rows)

        @pl.when(wanted)
        def _():
            latent = lat[here, :KVR]
            xr[...] = shared_key_tile(lat[here, KVR : KVR + ROPE], block_rows)
            for first, last in head_groups(heads):
                keys = dot_nn(latent, wkvb[:, first * HEAD : last * HEAD]).astype(jnp.bfloat16)
                for h in range(first, last):
                    xs[h] = keys[:, (h - first) * HEAD : (h - first + 1) * HEAD]
            dkv[...] = jnp.zeros(dkv.shape, jnp.float32)
            dkpe[...] = jnp.zeros(dkpe.shape, jnp.float32)

        for j in range(q_blocks):
            needed, whole = kinds[j]

            @pl.when(needed & whole)
            def _():
                pair(j, False)

            @pl.when(needed & jnp.logical_not(whole))
            def _():
                bias[...] = mask_bias(key_block, own[j], starts, block_rows, False)
                pair(j, True)

        @pl.when(wanted)
        def _():
            latent = lat[here, :KVR]
            d_latent = jnp.zeros((KVR, block_rows), jnp.float32)
            for h in range(heads):
                d_head = jnp.concatenate(
                    [dkv[h, :NOPE, :] * SCORE_SCALE, dkv[h, NOPE:, :]], axis=0
                ).astype(jnp.bfloat16)
                d_latent += dot_nn(wkvb[:, h * HEAD : (h + 1) * HEAD], d_head)
                gsum[h * HEAD : (h + 1) * HEAD, :] += dot_nn(d_head, latent)
            dlat[here, :KVR] = d_latent.T.astype(jnp.bfloat16)
            rope = jnp.concatenate(
                [dkpe[...] * SCORE_SCALE, jnp.zeros((HEAD - ROPE, block_rows), jnp.float32)], axis=0
            )
            dlat[here, KVR:] = rope.T[:, :ROPE].astype(jnp.bfloat16)

        @pl.when(jnp.logical_not(wanted))
        def _():
            dlat[here, :] = jnp.zeros((block_rows, KVR + ROPE), jnp.bfloat16)

        return carry

    lax.fori_loop(0, blocks, step, 0)
    for h in range(heads):
        gkvb[:, h * HEAD : (h + 1) * HEAD] = gsum[h * HEAD : (h + 1) * HEAD, :].T.astype(
            jnp.bfloat16
        )
    for j in range(q_blocks):
        here = pl.ds(j * block_rows, block_rows)
        cos_j, sin_j = cos[here, :], sin[here, :]
        flat[...] = jnp.zeros(flat.shape, jnp.float32)
        for h in range(heads):
            nope = jnp.where(lane < NOPE, dq[j, h, :, :HEAD], 0.0)
            rope = dq[j, h, :, HEAD:]
            shifted = rope * sin_j
            left = pltpu.roll(shifted, HEAD - ROPE // 2, 1)
            right = pltpu.roll(shifted, ROPE // 2, 1)
            swapped = jnp.where(lane < ROPE // 2, left, jnp.where(lane < ROPE, -right, 0.0))
            back = pltpu.roll(jnp.where(lane < ROPE, rope * cos_j + swapped, 0.0), NOPE, 1)
            whole = jnp.concatenate([(nope + back) * SCORE_SCALE, jnp.zeros_like(nope)], axis=1)
            at, shift = head_window(h)
            flat[:, at : at + WIDE] += pltpu.roll(whole, shift, 1)
        dq_out[here, :] = flat[:, : heads * (NOPE + ROPE)].astype(jnp.bfloat16)


def attention_backward(block_map, lengths, qx, qt, u_in, o_in, dob, lat, wkvb, cos, sin):
    q_blocks, heads, block_rows, _ = qx.shape
    blocks = lat.shape[0] // block_rows
    rows = q_blocks * block_rows
    odd = -(heads * VDIM) % HEAD
    if odd:
        o_in = jnp.pad(o_in, ((0, 0), (0, odd)))
        dob = jnp.pad(dob, ((0, 0), (0, odd)))
    vmem = pl.BlockSpec(memory_space=pltpu.VMEM)
    smem = pl.BlockSpec(memory_space=pltpu.SMEM)
    pairs = q_blocks * blocks * heads // 2
    return pl.pallas_call(
        functools.partial(backward_kernel, blocks, heads),
        out_shape=(
            jax.ShapeDtypeStruct((rows, heads * (NOPE + ROPE)), jnp.bfloat16),
            jax.ShapeDtypeStruct((lat.shape[0], KVR + ROPE), jnp.bfloat16),
            jax.ShapeDtypeStruct((KVR, heads * HEAD), jnp.bfloat16),
        ),
        in_specs=[smem] * 2 + [vmem] * 9,
        out_specs=(vmem,) * 3,
        scratch_shapes=[
            pltpu.VMEM((heads, block_rows, HEAD), jnp.bfloat16),
            pltpu.VMEM((block_rows, HEAD), jnp.bfloat16),
            pltpu.VMEM((q_blocks, heads, 2 * block_rows, WIDE), jnp.bfloat16),
            pltpu.VMEM((q_blocks, heads, VDIM, block_rows), jnp.bfloat16),
            pltpu.VMEM((q_blocks, heads, block_rows, WIDE), jnp.float32),
            pltpu.VMEM((heads, HEAD, block_rows), jnp.float32),
            pltpu.VMEM((ROPE, block_rows), jnp.float32),
            pltpu.VMEM((heads * HEAD, KVR), jnp.float32),
            pltpu.VMEM((block_rows, block_rows), jnp.float32),
            pltpu.VMEM((block_rows, window_columns(heads)), jnp.float32),
            pltpu.VMEM((2, 2 * block_rows, block_rows), jnp.float32),
            pltpu.VMEM((2, block_rows, block_rows), jnp.bfloat16),
            pltpu.VMEM((2, block_rows, block_rows), jnp.bfloat16),
        ],
        compiler_params=pltpu.CompilerParams(vmem_limit_bytes=VMEM_LIMIT),
        cost_estimate=pl.CostEstimate(
            flops=pairs * 8 * block_rows * block_rows * WIDE,
            bytes_accessed=24 * 1024 * 1024,
            transcendentals=pairs * block_rows * block_rows,
        ),
        name="attention_backward",
    )(block_map, lengths, qx, qt, u_in, o_in, dob, lat, wkvb, cos, sin)


MESH = pl.DeviceIdType.MESH


class LineSum:
    def __init__(self, n, own, landing, total, sems, lag):
        self.n, self.own, self.landing, self.total, self.lag = n, own, landing, total, lag
        self.up_send, self.up_land, self.down_send, self.back_send, self.down_land = sems
        self.me = lax.axis_index("tp")
        self.root = (n - 1) // 2
        self.chunks = own.shape[0]
        self.has_left, self.has_right = self.me > 0, self.me < n - 1
        self.root_lag = (n - 1 - self.root) * lag
        self.land_lag = 2 * self.root_lag
        self.ticks = self.chunks + self.land_lag

    def greet(self, barrier):
        me = self.me
        for there, other in ((self.has_left, me - 1), (self.has_right, me + 1)):

            @pl.when(there)
            def _(other=other):
                pl.semaphore_signal(barrier, inc=1, device_id={"tp": other}, device_id_type=MESH)

    def wait_greetings(self, barrier, others):
        both = self.has_left & self.has_right

        @pl.when(both)
        def _():
            pl.semaphore_wait(barrier, 2 + others)

        @pl.when(jnp.logical_not(both))
        def _():
            pl.semaphore_wait(barrier, 1 + others)

    def copy_to(self, source, target, send, land, c, other):
        return pltpu.make_async_remote_copy(
            src_ref=source.at[c],
            dst_ref=target.at[c],
            send_sem=send.at[c],
            recv_sem=land.at[c],
            device_id={"tp": other},
            device_id_type=MESH,
        )

    def rise_left(self, c):
        return self.copy_to(self.own, self.landing, self.up_send, self.up_land, c, self.me + 1)

    def rise_right(self, c):
        return self.copy_to(self.own, self.landing, self.up_send, self.up_land, c, self.me - 1)

    def rise_last(self, c):
        return self.copy_to(self.own, self.total, self.up_send, self.down_land, c, self.me - 1)

    def fall_right(self, c):
        return self.copy_to(self.total, self.total, self.down_send, self.down_land, c, self.me + 1)

    def fall_left(self, c):
        return self.copy_to(self.total, self.total, self.back_send, self.down_land, c, self.me - 1)

    def rise(self, c):
        me, root = self.me, self.root
        rises = [(me == root + 1, self.rise_last)]
        if root:
            rises.append((me < root, self.rise_left))
        if self.n - 1 > root + 1:
            rises.append((me > root + 1, self.rise_right))
        for who, copy in rises:

            @pl.when(who)
            def _(copy=copy):
                copy(c).start()

    def inside(self, c):
        return (c >= 0) & (c < self.chunks)

    def added(self, refs, c):
        sums = refs[0][c].astype(jnp.float32)
        for ref in refs[1:]:
            sums = sums + ref[c].astype(jnp.float32)
        return sums.astype(self.total.dtype)

    def leaf(self, c):
        is_leaf = self.me == self.n - 1
        if self.root:
            is_leaf = is_leaf | (self.me == 0)

        @pl.when(is_leaf & self.inside(c))
        def _():
            self.rise(c)

    def leaves(self):
        def body(c, carry):
            self.leaf(c)
            return carry

        lax.fori_loop(0, self.chunks, body, 0)

    def pump(self, first, last):
        def body(t, carry):
            self.duty(t)
            return carry

        lax.fori_loop(first, last, body, 0)

    def duty(self, t):
        me, root = self.me, self.root
        if self.n > 3:
            c = t - self.lag * jnp.where(me < root, me, self.n - 1 - me)

            @pl.when((me != root) & self.has_left & self.has_right & self.inside(c))
            def _():
                self.rise_right(c).wait_recv()
                self.own[c] = self.added([self.own, self.landing], c)
                self.rise(c)

        c_root = t - self.root_lag

        @pl.when((me == root) & self.inside(c_root))
        def _():
            if root:
                self.rise_left(c_root).wait_recv()
            self.fall_right(c_root).wait_recv()
            terms = [self.own, self.landing, self.total] if root else [self.own, self.total]
            self.total[c_root] = self.added(terms, c_root)
            self.fall_right(c_root).start()
            if root:
                self.fall_left(c_root).start()

        c_fall = t - self.root_lag - self.lag * jnp.where(me < root, root - me, me - root)

        @pl.when((me != root) & self.inside(c_fall))
        def _():
            self.fall_right(c_fall).wait_recv()

            @pl.when((me > root) & self.has_right)
            def _():
                self.fall_right(c_fall).start()

            @pl.when((me < root) & self.has_left)
            def _():
                self.fall_left(c_fall).start()

    def landed(self, t):
        return t - self.land_lag

    def drain(self):
        me = self.me

        def body(c, carry):
            @pl.when(me != self.root)
            def _():
                self.rise_right(c).wait_send()

            @pl.when((me >= self.root) & self.has_right)
            def _():
                self.fall_right(c).wait_send()

            @pl.when((me <= self.root) & self.has_left)
            def _():
                self.fall_left(c).wait_send()

            return carry

        lax.fori_loop(0, self.chunks, body, 0)


def line_sems(chunks):
    return [pltpu.SemaphoreType.DMA((chunks,))] * 5


def scatter_blocks(bits_left):
    chips = []
    for value in range(1 << len(bits_left)):
        chip = 0
        for at, bit in enumerate(bits_left):
            chip = chip + (((value >> at) & 1) << (bit - 1))
        chips.append(chip)
    return chips


class Scatter:
    def __init__(self, n, rows, columns, is_given):
        self.n, self.rows, self.columns, self.is_given = n, rows, columns, is_given
        self.count = n.bit_length() - 1
        self.parts = 2 if rows % 32 == 0 else 1

    def scratch(self):
        n, count = self.n, self.count
        half = jnp.bfloat16
        dma = pltpu.SemaphoreType.DMA
        shapes = [pltpu.VMEM((n // 2, self.rows, self.columns), half)]
        if not self.is_given:
            shapes.append(pltpu.VMEM((n // 2, self.rows, self.columns), half))
        for step in range(count - 1):
            shapes.append(pltpu.VMEM((n >> (step + 2), self.rows, self.columns), half))
        shapes += [dma((n // 2,))] * 2
        for step in range(count - 1):
            shapes += [dma((2, n >> (step + 2)))] * 2
        return shapes

    def bind(self, take, source, emit):
        self.held = take(1)[0]
        self.sent = None if self.is_given else take(1)[0]
        self.landed = take(self.count - 1)
        self.core_sems = take(2)
        self.step_sems = [take(2) for _ in range(self.count - 1)]
        self.source, self.emit = source, emit
        self.me = lax.axis_index("ctx")
        self.core = self.me & 1
        self.chips = self.n // 2
        self.orders = (tuple(range(1, self.count)), tuple(range(self.count - 1, 0, -1)))
        self.tiles = [(c, min(c + 512, self.columns)) for c in range(0, self.columns, 512)]
        return self

    def own(self, dest, first, last):
        at = pl.ds(pl.multiple_of(dest * self.rows, 16), self.rows)
        if self.is_given:
            return self.source[at, first:last].astype(jnp.float32)
        return dot_nn(self.source[0][at, :], self.source[1][:, first:last])

    def core_copy(self, chip):
        if self.is_given:
            at = pl.ds(pl.multiple_of((2 * chip + 1 - self.core) * self.rows, 16), self.rows)
            source = self.source.at[at, :]
        else:
            source = self.sent.at[chip]
        return pltpu.make_async_remote_copy(
            src_ref=source,
            dst_ref=self.held.at[chip],
            send_sem=self.core_sems[0].at[chip],
            recv_sem=self.core_sems[1].at[chip],
            device_id={"ctx": self.me ^ 1},
            device_id_type=MESH,
        )

    def step_copies(self, step):
        half = self.rows // self.parts
        me = self.me
        copies = []
        for part, order in enumerate(self.orders[: self.parts]):
            bit = order[step]
            at = pl.ds(part * half, half)
            for slot, free in enumerate(scatter_blocks(sorted(order[step + 1 :]))):
                keep = free + ((me >> bit) & 1) * (1 << (bit - 1))
                send = free + (1 - ((me >> bit) & 1)) * (1 << (bit - 1))
                for b in order[:step]:
                    own = ((me >> b) & 1) * (1 << (b - 1))
                    keep, send = keep + own, send + own
                copy = pltpu.make_async_remote_copy(
                    src_ref=self.held.at[send, at, :],
                    dst_ref=self.landed[step].at[slot, at, :],
                    send_sem=self.step_sems[step][0].at[part, slot],
                    recv_sem=self.step_sems[step][1].at[part, slot],
                    device_id={"ctx": me ^ (1 << bit)},
                    device_id_type=MESH,
                )
                copies.append((copy, keep, slot, at))
        return copies

    def start_core(self, also=None):
        def body(chip, carry):
            if also is not None:
                also(chip)
            if not self.is_given:
                for first, last in self.tiles:
                    self.sent[chip, :, first:last] = self.own(
                        2 * chip + 1 - self.core, first, last
                    ).astype(jnp.bfloat16)
            self.core_copy(chip).start()
            return carry

        lax.fori_loop(0, self.chips, body, 0)

    def finish_core(self, also=None):
        def body(chip, carry):
            if also is not None:
                also(chip)
            self.core_copy(chip).wait_recv()
            for first, last in self.tiles:
                total = self.own(2 * chip + self.core, first, last)
                total = total + self.held[chip, :, first:last].astype(jnp.float32)
                self.held[chip, :, first:last] = total.astype(jnp.bfloat16)
            return carry

        lax.fori_loop(0, self.chips, body, 0)

    def start_step(self, step):
        for copy, _, _, _ in self.step_copies(step):
            copy.start()

    def finish_step(self, step):
        for copy, keep, slot, at in self.step_copies(step):
            copy.wait_recv()
            for first, last in self.tiles:
                total = self.held[keep, at, first:last].astype(jnp.float32)
                total = total + self.landed[step][slot, at, first:last].astype(jnp.float32)
                if step == self.count - 2:
                    self.emit(at, first, last, total)
                else:
                    self.held[keep, at, first:last] = total.astype(jnp.bfloat16)
        if step + 1 < self.count - 1:
            self.start_step(step + 1)

    def drain(self):
        def body(chip, carry):
            self.core_copy(chip).wait_send()
            return carry

        lax.fori_loop(0, self.chips, body, 0)
        for step in range(self.count - 1):
            for copy, _, _, _ in self.step_copies(step):
                copy.wait_send()


def taker(refs):
    refs = list(refs)

    def take(k):
        taken = refs[:k]
        del refs[:k]
        return taken

    return take


def store_in(ref):
    def emit(at, first, last, total):
        ref[at, first:last] = total.astype(ref.dtype)

    return emit


def turn(source, target):
    def body(c, carry):
        at = pl.ds(pl.multiple_of(c * 128, 128), 128)
        target[at, :] = source[:, at].astype(jnp.float32).T.astype(jnp.bfloat16)
        return carry

    lax.fori_loop(0, source.shape[1] // 128, body, 0)


def greet_ctx(n, barrier):
    me = lax.axis_index("ctx")
    count = n.bit_length() - 1
    for bit in range(count):
        pl.semaphore_signal(barrier, inc=1, device_id={"ctx": me ^ (1 << bit)}, device_id_type=MESH)
    return count


def spread(waits, ticks):
    portion = -(-ticks // waits)
    return [(min(k * portion, ticks), min((k + 1) * portion, ticks)) for k in range(waits)]


def gate_up_kernel(
    n, tp, plans, normed, d_gate, d_up, terms, tokens, attn, cot, w_out_in, gain_row,
    gate_out, up_out, d_attn, d_heads, g_mid, *refs,
):
    take = taker(refs)
    own, landing, sums, normed_t, slots, in_sems, own_sem, w_out, w_sem = take(9)
    w_load = pltpu.make_async_copy(w_out_in, w_out, w_sem)
    line = LineSum(tp, own, landing, sums, take(5), LAG)
    gate = plans[0].bind(take, (normed_t, d_gate), store_in(gate_out))
    up = plans[1].bind(take, (normed_t, d_up), store_in(up_out))
    width = normed.shape[1]
    blocks = normed.shape[0] // BLOCK
    per_block = BLOCK // CHUNK
    load = pltpu.make_async_copy(terms, own, own_sem)
    load.start()
    barrier = pltpu.get_barrier_semaphore()
    others = greet_ctx(n, barrier)
    line.greet(barrier)

    def fetch(b):
        rows = pl.ds(b * BLOCK, BLOCK)
        return [
            pltpu.make_async_copy(
                source.at[rows, :], slots.at[b % 2, k], in_sems.at[b % 2, k]
            )
            for k, source in enumerate((tokens, attn, cot))
        ]

    for b in range(min(2, blocks)):
        for copy in fetch(b):
            copy.start()
    w_load.start()
    g_mid[...] = jnp.zeros(g_mid.shape, jnp.float32)

    def norm(b):
        if b == 0:
            w_load.wait()
        for copy in fetch(b):
            copy.wait()
        for part in range(0, BLOCK, 2 * CHUNK):
            rows = pl.ds(b * BLOCK + part, 2 * CHUNK)
            here = pl.ds(part, 2 * CHUNK)
            c = b * per_block + part // CHUNK
            incoming = jnp.concatenate([sums[c], sums[c + 1]], axis=0).astype(jnp.float32)
            middle = slots[b % 2, 0, here, :].astype(jnp.float32)
            middle = middle + RESIDUAL_SCALE * slots[b % 2, 1, here, :].astype(jnp.float32)
            d_norm, gain_terms = norm_back(
                incoming, middle, norm_scale(middle), gain_row[:, width : 2 * width]
            )
            g_mid[...] += gain_terms
            total = slots[b % 2, 2, here, :].astype(jnp.float32) + d_norm
            d_attn[rows, :] = (RESIDUAL_SCALE * total).astype(jnp.bfloat16)
        rows = pl.ds(b * BLOCK, BLOCK)
        d_heads[rows, :] = dot_nn(d_attn[rows, :], w_out[...]).astype(jnp.bfloat16)
        if b + 2 < blocks:
            for copy in fetch(b + 2):
                copy.start()

    load.wait()
    line.wait_greetings(barrier, others)
    line.leaves()
    turn(normed, normed_t)
    chips = n // 2
    gate.start_core()
    gate.finish_core(line.duty)
    gate.start_step(0)
    up.start_core(lambda chip: line.duty(chips + chip))
    up.finish_core(lambda chip: line.duty(2 * chips + chip))
    up.start_step(0)
    steps = [(item, step) for step in range(gate.count - 1) for item in (gate, up)]
    done = 3 * chips
    next_block = 0
    for (item, step), (first, last) in zip(steps, spread(len(steps), line.ticks - done)):
        line.pump(done + first, done + last)
        while next_block < blocks and line.landed(done + last - 1) >= (next_block + 1) * per_block - 1:
            norm(next_block)
            next_block += 1
        item.finish_step(step)
    for item in (gate, up, line):
        item.drain()


def gate_up_grads(
    n, tp, normed, d_gate, d_up, terms, tokens, attn, cot, gain_row, w_out, collective_id
):
    rows, width = normed.shape
    hidden = d_gate.shape[1]
    head_width = w_out.shape[1]
    vmem = pl.BlockSpec(memory_space=pltpu.VMEM)
    anywhere = pl.BlockSpec(memory_space=pl.ANY)
    half = jnp.bfloat16
    plans = [Scatter(n, width // n, hidden, False) for _ in range(2)]
    chunked = (rows // CHUNK, CHUNK, width)
    return pl.pallas_call(
        functools.partial(gate_up_kernel, n, tp, plans),
        out_shape=(
            jax.ShapeDtypeStruct((width // n, hidden), half),
            jax.ShapeDtypeStruct((width // n, hidden), half),
            jax.ShapeDtypeStruct((rows, width), half),
            jax.ShapeDtypeStruct((rows, head_width), half),
            jax.ShapeDtypeStruct((1, width), jnp.float32),
        ),
        in_specs=[vmem] * 3 + [anywhere] * 5 + [vmem],
        out_specs=(vmem,) * 5,
        scratch_shapes=[
            pltpu.VMEM(chunked, half),
            pltpu.VMEM(chunked, half),
            pltpu.VMEM(chunked, half),
            pltpu.VMEM((width, rows), half),
            pltpu.VMEM((2, 3, BLOCK, width), half),
            pltpu.SemaphoreType.DMA((2, 3)),
            pltpu.SemaphoreType.DMA,
            pltpu.VMEM(w_out.shape, half),
            pltpu.SemaphoreType.DMA,
            *line_sems(rows // CHUNK),
            *plans[0].scratch(),
            *plans[1].scratch(),
        ],
        compiler_params=pltpu.CompilerParams(
            vmem_limit_bytes=MIDDLE_VMEM, collective_id=collective_id, has_side_effects=True
        ),
        cost_estimate=pl.CostEstimate(
            flops=2 * rows * width * (2 * hidden + head_width),
            bytes_accessed=28 * 1024 * 1024,
            transcendentals=0,
        ),
        name=f"gate_up_grads_{collective_id}",
    )(normed, d_gate, d_up, terms.reshape(chunked), tokens, attn, cot, w_out, gain_row)


TAIL_CHUNK = 64


def up_tail_kernel(
    n, tp, plans, d_lat, d_query, w_qb, g_kvb_in, d_attn_in, ob_in, q_latent_in, d_feed_in, act_in,
    sum_q, sum_lat, down_out, out_out, qb_out, kvb_out, *refs,
):
    take = taker(refs)
    own_q, land_q, own_lat, land_lat, d_attn_t, q_latent_t, d_feed_t = take(7)
    g_kvb, d_attn, ob, q_latent, d_feed, act, in_sems = take(7)
    loads = {}
    pairs = ((d_feed_in, d_feed), (act_in, act), (d_attn_in, d_attn), (ob_in, ob))
    pairs += ((q_latent_in, q_latent), (g_kvb_in, g_kvb))
    for k, (source, target) in enumerate(pairs):
        loads[id(target)] = pltpu.make_async_copy(source, target, in_sems.at[k])
        loads[id(target)].start()
    line_q = LineSum(tp, own_q, land_q, sum_q, take(5), LAG)
    line_lat = LineSum(tp, own_lat, land_lat, sum_lat, take(5), LAG)
    chunk = own_q.shape[1]

    def store_lat(at, first, last, total):
        for k in range(at.size // chunk):
            own_lat[at.start // chunk + k, :, first:last] = total[
                k * chunk : (k + 1) * chunk
            ].astype(jnp.bfloat16)

    lat, down, out, qb, kvb = plans
    lat.bind(take, d_lat, store_lat)
    down.bind(take, (d_feed_t, act), store_in(down_out))
    out.bind(take, (d_attn_t, ob), store_in(out_out))
    qb.bind(take, (q_latent_t, d_query), store_in(qb_out))
    kvb.bind(take, g_kvb, store_in(kvb_out))
    barrier = pltpu.get_barrier_semaphore()
    others = greet_ctx(n, barrier)
    line_q.greet(barrier)
    line_q.wait_greetings(barrier, others)
    lat.start_core()

    def query(c, carry):
        rows = pl.ds(pl.multiple_of(c * 2 * chunk, 2 * chunk), 2 * chunk)
        part = dot_nn(d_query[rows, :], w_qb[...]).astype(jnp.bfloat16)
        for k in range(2):
            own_q[2 * c + k] = part[k * chunk : (k + 1) * chunk]
            line_q.leaf(2 * c + k)
        return carry

    lax.fori_loop(0, own_q.shape[0] // 2, query, 0)
    lat.finish_core()
    lat.start_step(0)
    loads[id(d_feed)].wait()
    turn(d_feed, d_feed_t)
    loads[id(act)].wait()
    down.start_core()
    lat.finish_step(0)
    down.finish_core()
    for step in range(1, lat.count - 1):
        lat.finish_step(step)
    line_lat.leaves()
    down.start_step(0)
    chips = n // 2
    loads[id(d_attn)].wait()
    turn(d_attn, d_attn_t)
    loads[id(ob)].wait()
    out.start_core(line_q.duty)
    out.finish_core(lambda chip: line_q.duty(chips + chip))
    out.start_step(0)
    loads[id(g_kvb)].wait()
    kvb.start_core()
    loads[id(q_latent)].wait()
    turn(q_latent, q_latent_t)
    qb.start_core(lambda chip: line_q.duty(2 * chips + chip))
    kvb.finish_core()
    kvb.start_step(0)
    qb.finish_core(line_lat.duty)
    qb.start_step(0)
    steps = [(item, step) for step in range(lat.count - 1) for item in (down, out, kvb, qb)]
    q_share = spread(len(steps), line_q.ticks - 3 * chips)
    lat_share = spread(len(steps), line_lat.ticks - chips)
    for (item, step), (a, b), (c, d) in zip(steps, q_share, lat_share):
        line_q.pump(3 * chips + a, 3 * chips + b)
        line_lat.pump(chips + c, chips + d)
        item.finish_step(step)
    for item in (*plans, line_q, line_lat):
        item.drain()


def up_tail(n, tp, d_lat, d_query, w_qb, g_kvb, d_attn, ob, q_latent, d_feed, act, collective_id):
    rows, width = d_attn.shape
    rank = q_latent.shape[1]
    hidden = act.shape[1]
    lat_width = d_lat.shape[1]
    vmem = pl.BlockSpec(memory_space=pltpu.VMEM)
    half = jnp.bfloat16
    plans = [
        Scatter(n, rows, lat_width, True),
        Scatter(n, width // n, hidden, False),
        Scatter(n, width // n, ob.shape[1], False),
        Scatter(n, rank // n, d_query.shape[1], False),
        Scatter(n, KVR // n, g_kvb.shape[1], True),
    ]
    q_shape = (rows // TAIL_CHUNK, TAIL_CHUNK, rank)
    lat_shape = (rows // TAIL_CHUNK, TAIL_CHUNK, lat_width)
    sum_q, sum_lat, *grads = pl.pallas_call(
        functools.partial(up_tail_kernel, n, tp, plans),
        out_shape=(
            jax.ShapeDtypeStruct(q_shape, half),
            jax.ShapeDtypeStruct(lat_shape, half),
            *[jax.ShapeDtypeStruct((plan.rows, plan.columns), half) for plan in plans[1:]],
        ),
        in_specs=[vmem] * 3 + [pl.BlockSpec(memory_space=pl.ANY)] * 6,
        out_specs=(vmem,) * 6,
        scratch_shapes=[
            pltpu.VMEM(q_shape, half),
            pltpu.VMEM(q_shape, half),
            pltpu.VMEM(lat_shape, half),
            pltpu.VMEM(lat_shape, half),
            pltpu.VMEM((width, rows), half),
            pltpu.VMEM((rank, rows), half),
            pltpu.VMEM((width, rows), half),
            *[pltpu.VMEM(late.shape, half) for late in (g_kvb, d_attn, ob, q_latent, d_feed, act)],
            pltpu.SemaphoreType.DMA((6,)),
            *line_sems(rows // TAIL_CHUNK),
            *line_sems(rows // TAIL_CHUNK),
            *[shape for plan in plans for shape in plan.scratch()],
        ],
        compiler_params=pltpu.CompilerParams(
            vmem_limit_bytes=MIDDLE_VMEM, collective_id=collective_id, has_side_effects=True
        ),
        cost_estimate=pl.CostEstimate(
            flops=2 * rows * width * (hidden + ob.shape[1]) + 4 * rows * rank * d_query.shape[1],
            bytes_accessed=32 * 1024 * 1024,
            transcendentals=0,
        ),
        name=f"up_tail_{collective_id}",
    )(d_lat, d_query, w_qb, g_kvb, d_attn, ob, q_latent, d_feed, act)
    return sum_q.reshape(rows, rank), sum_lat.reshape(rows, lat_width), *grads


def down_tail_kernel(
    n, plans, sum_q, sum_lat, q_pre, lat_raw, tokens, d_attn_in, gain_row, g_mid, w_qa_in, w_kva_in, cos, sin, grad_in, qa_out, kva_out, gains_out,
    d_q, d_kv, normed_t, scales, g_in, g_q, g_kv, packed, packing, grad_slots, out_sems, d_attn, w_qa, w_kva, in_sems,
    *refs,
):
    take = taker(refs)
    qa, kva, gains = plans
    pairs = ((w_qa_in, w_qa), (w_kva_in, w_kva), (d_attn_in, d_attn))
    loads = [
        pltpu.make_async_copy(source, target, in_sems.at[k])
        for k, (source, target) in enumerate(pairs)
    ]
    for load in loads:
        load.start()
    qa.bind(take, (normed_t, d_q), store_in(qa_out))
    kva.bind(take, (normed_t, d_kv), store_in(kva_out))
    gains.bind(take, packed, store_in(gains_out))
    rows = tokens.shape[0]
    block = rows // 4
    gain_in, _, gain_q, gain_kv = split_gains(gain_row, tokens.shape[1], q_pre.shape[1])
    lane = lax.broadcasted_iota(jnp.int32, (block, HEAD), 1)
    barrier = pltpu.get_barrier_semaphore()
    others = greet_ctx(n, barrier)

    def rows_of(k):
        return pl.ds(pl.multiple_of(k * block, block), block)

    def deliver(k, slot):
        return pltpu.make_async_copy(
            grad_slots.at[slot], grad_in.at[rows_of(k), :], out_sems.at[slot]
        )

    for ref in (g_in, g_q, g_kv):
        ref[...] = jnp.zeros(ref.shape, jnp.float32)

    def norms(k, carry):
        at = rows_of(k)
        pre = q_pre[at, :]
        d_pre, terms = norm_back(
            sum_q[at, :].astype(jnp.float32), pre, norm_scale(pre), gain_q
        )
        g_q[...] += terms
        d_q[at, :] = d_pre.astype(jnp.bfloat16)
        raw = lat_raw[at, :]
        d_raw, terms = norm_back(
            sum_lat[at, :KVR].astype(jnp.float32), raw, norm_scale(raw), gain_kv
        )
        g_kv[...] += terms
        d_kv[at, :KVR] = d_raw.astype(jnp.bfloat16)
        rope = sum_lat[at, KVR:].astype(jnp.float32)
        rope = jnp.concatenate([rope, jnp.zeros((block, HEAD - ROPE), jnp.float32)], axis=1)
        rope = rope_tile_back(rope, cos[at, :], sin[at, :], lane)
        d_kv[at, KVR:] = rope[:, :ROPE].astype(jnp.bfloat16)
        values = tokens[at, :].astype(jnp.float32)
        scale = norm_scale(values)
        scales[at, :] = jnp.broadcast_to(scale, (block, HEAD))
        normed = values * scale * gain_in
        for c in range(0, normed.shape[1], 128):
            normed_t[c : c + 128, at] = normed[:, c : c + 128].T.astype(jnp.bfloat16)
        return carry

    lax.fori_loop(0, 4, norms, 0)
    pl.semaphore_wait(barrier, others)
    qa.start_core()
    kva.start_core()
    qa.finish_core()
    qa.start_step(0)
    kva.finish_core()
    kva.start_step(0)
    for load in loads:
        load.wait()
    for k in range(4):
        at = pl.ds(k * block, block)
        if k >= 2:
            deliver(k - 2, k % 2).wait()
        d_normed = dot_nt(d_q[at, :], w_qa[...]) + dot_nn(d_kv[at, :], w_kva[...])
        d_values, terms = norm_back(
            d_normed, tokens[at, :].astype(jnp.float32), scales[at, :1], gain_in
        )
        g_in[...] += terms
        d_middle = d_attn[at, :].astype(jnp.float32) * (1.0 / RESIDUAL_SCALE)
        grad_slots[k % 2] = d_middle + d_values
        deliver(k, k % 2).start()
    packing[...] = jnp.zeros(packing.shape, jnp.float32)
    lines = gains.rows
    at = 0
    for whole in (g_in, g_mid, g_q, g_kv):
        share = whole.shape[1] // n
        piece = 32 if share % 32 == 0 else 16
        for dest in range(n):
            for place in range(0, share, piece):
                row, column = divmod(at + place, HEAD)
                row += dest * lines
                first = dest * share + place
                packing[row : row + 1, column : column + piece] = whole[:, first : first + piece]
        at += share
    packed[...] = packing[...].astype(jnp.bfloat16)
    gains.start_core()
    gains.finish_core()
    gains.start_step(0)
    for step in range(qa.count - 1):
        for item in (qa, kva, gains):
            item.finish_step(step)
    deliver(2, 0).wait()
    deliver(3, 1).wait()
    for item in plans:
        item.drain()


def down_tail(
    n, sum_q, sum_lat, q_pre, lat_raw, tokens, d_attn, gain_row, g_mid, w_qa, w_kva, cos, sin,
    collective_id,
):
    rows, width = tokens.shape
    rank = q_pre.shape[1]
    vmem = pl.BlockSpec(memory_space=pltpu.VMEM)
    anywhere = pl.BlockSpec(memory_space=pl.ANY)
    half, full = jnp.bfloat16, jnp.float32
    dma = pltpu.SemaphoreType.DMA
    share = (2 * width + rank + KVR) // n
    lines = -(-share // (32 * HEAD)) * 32
    plans = [
        Scatter(n, width // n, rank, False),
        Scatter(n, width // n, KVR + ROPE, False),
        Scatter(n, lines, HEAD, True),
    ]
    slots = pltpu.VMEM((2, rows // 4, width), full)
    grad_in, qa, kva, gains = pl.pallas_call(
        functools.partial(down_tail_kernel, n, plans),
        out_shape=(
            jax.ShapeDtypeStruct((rows, width), full),
            *[jax.ShapeDtypeStruct((plan.rows, plan.columns), half) for plan in plans],
        ),
        in_specs=[vmem] * 5
        + [anywhere]
        + [vmem] * 2
        + [anywhere] * 2
        + [vmem] * 2,
        out_specs=(anywhere, vmem, vmem, vmem),
        scratch_shapes=[
            pltpu.VMEM((rows, rank), half),
            pltpu.VMEM((rows, KVR + ROPE), half),
            pltpu.VMEM((width, rows), half),
            pltpu.VMEM((rows, HEAD), full),
            pltpu.VMEM((1, width), full),
            pltpu.VMEM((1, rank), full),
            pltpu.VMEM((1, KVR), full),
            pltpu.VMEM((n * lines, HEAD), half),
            pltpu.VMEM((n * lines, HEAD), full),
            slots,
            dma((2,)),
            pltpu.VMEM((rows, width), half),
            pltpu.VMEM(w_qa.shape, half),
            pltpu.VMEM(w_kva.shape, half),
            dma((3,)),
            *[shape for plan in plans for shape in plan.scratch()],
        ],
        compiler_params=pltpu.CompilerParams(
            vmem_limit_bytes=MIDDLE_VMEM, collective_id=collective_id, has_side_effects=True
        ),
        cost_estimate=pl.CostEstimate(
            flops=4 * rows * width * (rank + KVR + ROPE),
            bytes_accessed=40 * 1024 * 1024,
            transcendentals=rows,
        ),
        name=f"down_tail_{collective_id}",
    )(
        sum_q,
        sum_lat,
        q_pre,
        lat_raw,
        tokens,
        d_attn,
        gain_row,
        g_mid,
        w_qa,
        w_kva,
        cos,
        sin,
    )
    gains = gains.astype(full).reshape(-1)
    ends = [0]
    for size in (width, width, rank, KVR):
        ends.append(ends[-1] + size // n)
    return grad_in, qa, kva, [gains[first:last] for first, last in zip(ends, ends[1:])]


CHUNK = 16
BLOCK = 8 * CHUNK
LAG = 2
MIDDLE_VMEM = 63 * 1024 * 1024


def middle_kernel(
    n, lag, ob, tokens_in, cot_in, gain, w_out, w_gate, w_up, w_down,
    tt_to, d_to, f_to, act_to, dg_to, du_to, h_to, df_to,
    tt, d_out, f_out, act_out, dg_out, du_out, h_out, df_out,
    tokens, cot, own, up, wo, wg, wu, wd, d_acc, f_acc, w_sems, out_sems, *sems,
):
    line = LineSum(n, own, up, tt, sems, lag)
    width = tokens.shape[1]
    hidden = wg.shape[0]
    chunks, chunk = own.shape[:2]
    per_block = BLOCK // chunk
    blocks = chunks // per_block
    block_lag = -(-(per_block + line.land_lag) // per_block)
    tiles = [(c, min(c + 512, width)) for c in range(0, width, 512)]
    quarter = hidden // 4 // 128 * 128
    cuts = [0, quarter, 2 * quarter, 3 * quarter, hidden]
    loads = [
        pltpu.make_async_copy(source, target, w_sems.at[k])
        for k, (source, target) in enumerate(
            (
                (w_out, wo),
                (tokens_in, tokens),
                (cot_in, cot),
                (w_gate, wg),
                (w_up, wu),
                (w_down, wd),
            )
        )
    ]
    kept = ((d_out, d_to), (f_out, f_to), (act_out, act_to), (dg_out, dg_to), (du_out, du_to))
    kept += ((h_out, h_to), (df_out, df_to))

    def keep(b):
        rows = pl.ds(pl.multiple_of(b * BLOCK, BLOCK), BLOCK)
        copies = [
            pltpu.make_async_copy(source.at[rows, :], target.at[rows, :], out_sems.at[k, b])
            for k, (source, target) in enumerate(kept)
        ]
        some = pl.ds(b * per_block, per_block)
        return copies + [
            pltpu.make_async_copy(tt.at[some], tt_to.at[some], out_sems.at[len(kept), b])
        ]

    for load in loads:
        load.start()
    barrier = pltpu.get_barrier_semaphore()
    line.greet(barrier)
    line.wait_greetings(barrier, 0)

    def project(b, carry):
        rows = pl.ds(pl.multiple_of(b * BLOCK, BLOCK), BLOCK)
        for first, last in tiles:
            part = dot_nt(ob[rows, :], wo[first:last, :]).astype(jnp.bfloat16)
            for k in range(per_block):
                own[per_block * b + k, :, first:last] = part[k * chunk : (k + 1) * chunk, :]
        for k in range(per_block):
            line.leaf(per_block * b + k)
        return carry

    def normalize(b, part):
        for k in range(part * per_block // 2, (part + 1) * per_block // 2, 2):
            rows = pl.ds(pl.multiple_of(b * BLOCK + k * chunk, 2 * chunk), 2 * chunk)
            sums = jnp.concatenate([tt[b * per_block + k], tt[b * per_block + k + 1]], axis=0)
            middle = tokens[rows, :].astype(jnp.float32) + RESIDUAL_SCALE * sums.astype(jnp.float32)
            h_out[rows, :] = (middle * norm_scale(middle) * gain[:, width : 2 * width]).astype(jnp.bfloat16)

    def feed(b, i):
        rows = pl.ds(pl.multiple_of(b * BLOCK, BLOCK), BLOCK)
        first, last = cuts[i], cuts[i + 1]
        if i == 0:
            normalize(b, 0)
            normalize(b, 1)
            df_out[rows, :] = (RESIDUAL_SCALE * cot[rows, :].astype(jnp.float32)).astype(
                jnp.bfloat16
            )
        gate = dot_nt(h_out[rows, :], wg[first:last, :])
        upper = dot_nt(h_out[rows, :], wu[first:last, :])
        d_act = dot_nt(df_out[rows, :], wd[first:last, :])
        sig = jax.nn.sigmoid(gate)
        silu = gate * sig
        act_out[rows, first:last] = (silu * upper).astype(jnp.bfloat16)
        dg_out[rows, first:last] = (d_act * upper * sig * (1.0 + gate * (1.0 - sig))).astype(
            jnp.bfloat16
        )
        du_out[rows, first:last] = (d_act * silu).astype(jnp.bfloat16)

    def feed_back(b, i):
        rows = pl.ds(pl.multiple_of(b * BLOCK, BLOCK), BLOCK)
        first, last = cuts[i], cuts[i + 1]
        act, dg, du = (ref[rows, first:last] for ref in (act_out, dg_out, du_out))
        for lo, hi in tiles:
            d_part = dot_nn(dg, wg[first:last, lo:hi]) + dot_nn(du, wu[first:last, lo:hi])
            f_part = dot_nn(act, wd[first:last, lo:hi])
            if i:
                d_part = d_part + d_acc[:, lo:hi]
                f_part = f_part + f_acc[:, lo:hi]
            if i < 3:
                d_acc[:, lo:hi] = d_part
                f_acc[:, lo:hi] = f_part
            else:
                d_out[rows, lo:hi] = d_part.astype(jnp.bfloat16)
                f_out[rows, lo:hi] = f_part.astype(jnp.bfloat16)

    loads[0].wait()
    lax.fori_loop(0, blocks, project, 0)

    def outer(o, carry):
        b = o - block_lag

        @pl.when(b == 0)
        def _():
            for load in loads[1:]:
                load.wait()

        share = per_block // 8
        for i in range(4):
            for step, work in enumerate((feed, feed_back)):

                @pl.when(o * per_block < line.ticks)
                def _(at=(2 * i + step) * share):
                    for k in range(share):
                        line.duty(o * per_block + at + k)

                @pl.when(b >= 0)
                def _(i=i, work=work):
                    work(b, i)

        @pl.when(b >= 0)
        def _():
            for copy in keep(b):
                copy.start()

        return carry

    lax.fori_loop(0, blocks + block_lag, outer, 0)
    line.drain()

    def finish(b, carry):
        for copy in keep(b):
            copy.wait()
        return carry

    lax.fori_loop(0, blocks, finish, 0)


def middle_layer(n, ob, tokens, cot, gains, w_out, w_gate, w_up, w_down, collective_id):
    rows, width = tokens.shape
    hidden = w_gate.shape[0]
    chunks = rows // CHUNK
    vmem = pl.BlockSpec(memory_space=pltpu.VMEM)
    anywhere = pl.BlockSpec(memory_space=pl.ANY)
    half = jnp.bfloat16
    dma = pltpu.SemaphoreType.DMA
    attn, *rest = pl.pallas_call(
        functools.partial(middle_kernel, n, LAG),
        out_shape=(
            jax.ShapeDtypeStruct((chunks, CHUNK, width), half),
            jax.ShapeDtypeStruct((rows, width), half),
            jax.ShapeDtypeStruct((rows, width), half),
            jax.ShapeDtypeStruct((rows, hidden), half),
            jax.ShapeDtypeStruct((rows, hidden), half),
            jax.ShapeDtypeStruct((rows, hidden), half),
            jax.ShapeDtypeStruct((rows, width), half),
            jax.ShapeDtypeStruct((rows, width), half),
        ),
        in_specs=[vmem, anywhere, anywhere, vmem] + [anywhere] * 4,
        out_specs=(anywhere,) * 8,
        scratch_shapes=[
            pltpu.VMEM((chunks, CHUNK, width), half),
            pltpu.VMEM((rows, width), half),
            pltpu.VMEM((rows, width), half),
            pltpu.VMEM((rows, hidden), half),
            pltpu.VMEM((rows, hidden), half),
            pltpu.VMEM((rows, hidden), half),
            pltpu.VMEM((rows, width), half),
            pltpu.VMEM((rows, width), half),
            pltpu.VMEM((rows, width), half),
            pltpu.VMEM((rows, width), half),
            pltpu.VMEM((chunks, CHUNK, width), half),
            pltpu.VMEM((chunks, CHUNK, width), half),
            pltpu.VMEM(w_out.shape, half),
            pltpu.VMEM(w_gate.shape, half),
            pltpu.VMEM(w_up.shape, half),
            pltpu.VMEM(w_down.shape, half),
            pltpu.VMEM((BLOCK, width), jnp.float32),
            pltpu.VMEM((BLOCK, width), jnp.float32),
            dma((6,)),
            dma((8, rows // BLOCK)),
            *line_sems(chunks),
        ],
        compiler_params=pltpu.CompilerParams(
            vmem_limit_bytes=MIDDLE_VMEM, collective_id=collective_id, has_side_effects=True
        ),
        cost_estimate=pl.CostEstimate(
            flops=2 * rows * width * (6 * hidden + ob.shape[1]),
            bytes_accessed=64 * 1024 * 1024,
            transcendentals=rows * hidden,
        ),
        name=f"middle_layer_{collective_id}",
    )(ob, tokens, cot, gains, w_out, w_gate, w_up, w_down)
    return attn.reshape(rows, width), *rest


def norm_scale(values):
    return lax.rsqrt(jnp.mean(values * values, axis=-1, keepdims=True) + EPSILON)


def norm_back(incoming, values, inv_rms, gain_vec):
    weighted = incoming * gain_vec
    mean = jnp.mean(weighted * values, axis=-1, keepdims=True)
    d_values = inv_rms * weighted - values * (inv_rms * inv_rms * inv_rms) * mean
    return d_values, jnp.sum(incoming * values * inv_rms, axis=0, keepdims=True)


def rope_tile(tile, cos, sin, lane):
    left = pltpu.roll(tile, HEAD - ROPE // 2, 1)
    right = pltpu.roll(tile, ROPE // 2, 1)
    swapped = jnp.where(lane < ROPE // 2, -left, right)
    return jnp.where(lane < ROPE, tile * cos + swapped * sin, 0.0)


def rope_tile_back(tile, cos, sin, lane):
    shifted = tile * sin
    left = pltpu.roll(shifted, HEAD - ROPE // 2, 1)
    right = pltpu.roll(shifted, ROPE // 2, 1)
    swapped = jnp.where(lane < ROPE // 2, left, -right)
    return jnp.where(lane < ROPE, tile * cos + swapped, 0.0)


def split_gains(gains, width, rank):
    ends = (0, width, 2 * width, 2 * width + rank, 2 * width + rank + KVR)
    return [gains[:, first:last] for first, last in zip(ends, ends[1:])]


def head_kernel(
    n, block_map, lengths, tokens, gains, rates, w_qa_in, w_kva, w_qb_in,
    out, q_latent_to, q_pre_to, lat_raw_to, cos_to, sin_to, qx_to, qt_to,
    q_latent, q_pre, lat_raw, cos, sin, qx, qt, w_qa, w_qb, in_sems, out_sems,
    own, normed, w_rope, flat, local_sem, step_sends, step_lands, core_sends, core_lands,
):
    gain_in, _, gain_q, gain_kv = split_gains(gains, tokens.shape[1], w_qa.shape[1])
    heads = qx.shape[1]
    loads = [
        pltpu.make_async_copy(w_qa_in, w_qa, in_sems.at[0]),
        pltpu.make_async_copy(w_qb_in, w_qb, in_sems.at[1]),
    ]
    for load in loads:
        load.start()
    kept = []

    def keep(*pairs):
        for source, target in pairs:
            copy = pltpu.make_async_copy(source, target, out_sems.at[len(kept)])
            copy.start()
            kept.append(copy)

    count = n.bit_length() - 1
    me = lax.axis_index("ctx")
    rows = own.shape[0]
    half = rows // 2
    block = rows // 4
    barrier = pltpu.get_barrier_semaphore()
    for bit in range(count):
        pl.semaphore_signal(barrier, inc=1, device_id={"ctx": me ^ (1 << bit)}, device_id_type=MESH)
    orders = (tuple(range(1, count)), tuple(range(count - 1, 0, -1)))
    lane = lax.broadcasted_iota(jnp.int32, (block, HEAD), 1)
    w_rope[...] = jnp.zeros(w_rope.shape, jnp.bfloat16)
    w_rope[:ROPE, :] = w_kva[KVR : KVR + ROPE, :]

    starts = starts_of(lengths)
    places = lax.broadcasted_iota(jnp.int32, (half, HEAD), 0)
    lanes = lax.broadcasted_iota(jnp.int32, (half, HEAD), 1)
    for j in range(2):
        at = pl.ds(j * half, half)
        place = block_map[j, me] * half + places
        angles = (place - begin_of(place, starts)).astype(jnp.float32) * rates[...]
        cos[at, :] = jnp.where(lanes < ROPE, jnp.cos(angles), 0.0)
        sin[at, :] = jnp.where(lanes < ROPE, jnp.sin(angles), 0.0)

    def latents(k, carry):
        at = pl.ds(pl.multiple_of(k * block, block), block)
        values = tokens[at, :].astype(jnp.float32)
        normed[at, :] = (values * norm_scale(values) * gain_in).astype(jnp.bfloat16)
        raw = dot_nt(normed[at, :], w_kva[:KVR, :])
        lat_raw[at, :] = raw
        own[at, :KVR] = (raw * norm_scale(raw) * gain_kv).astype(jnp.bfloat16)
        rope = rope_tile(dot_nt(normed[at, :], w_rope[...]), cos[at, :], sin[at, :], lane)
        own[at, KVR:] = rope[:, :ROPE].astype(jnp.bfloat16)
        return carry

    keep((cos, cos_to), (sin, sin_to))
    lax.fori_loop(0, 4, latents, 0)
    pl.semaphore_wait(barrier, count)
    local = pltpu.make_async_copy(own, out.at[me], local_sem)
    local.start()

    def chip_copy(part, step, slot, block, first):
        at = pl.ds(part * half, half)
        return pltpu.make_async_remote_copy(
            src_ref=own.at[at, :] if first else out.at[block, at, :],
            dst_ref=out.at[block, at, :],
            send_sem=step_sends.at[part, step, slot],
            recv_sem=step_lands.at[part, step, slot],
            device_id={"ctx": me ^ (1 << orders[part][step])},
            device_id_type=MESH,
        )

    def core_copy(block, slot, first):
        return pltpu.make_async_remote_copy(
            src_ref=own if first else out.at[block],
            dst_ref=out.at[block],
            send_sem=core_sends.at[slot],
            recv_sem=core_lands.at[slot],
            device_id={"ctx": me ^ 1},
            device_id_type=MESH,
        )

    def query(k, carry):
        at = pl.ds(pl.multiple_of(k * block, block), block)
        pre = dot_nn(normed[at, :], w_qa[...])
        q_pre[at, :] = pre
        q_latent[at, :] = (pre * norm_scale(pre) * gain_q).astype(jnp.bfloat16)
        return carry

    def queries(j):
        here = pl.ds(j * half, half)
        cos_j, sin_j = cos[here, :], sin[here, :]
        width = heads * (NOPE + ROPE)
        for at in range(0, width, WIDE):
            end = min(at + WIDE, width)
            flat[:, at:end] = dot_nt(q_latent[here, :], w_qb[at:end, :])
        for h in range(heads):
            at, shift = head_window(h)
            own_part = pltpu.roll(flat[:, at : at + WIDE], (WIDE - shift) % WIDE, 1)[:, :HEAD]
            nope = jnp.where(lanes < NOPE, own_part, 0.0)
            rope = rope_tile(pltpu.roll(own_part, NOPE, 1), cos_j, sin_j, lanes)
            qx[j, h, :, :HEAD] = nope.astype(jnp.bfloat16)
            qx[j, h, :, HEAD:] = rope.astype(jnp.bfloat16)
            qt[j, h, :NOPE, :] = nope.T[:NOPE, :].astype(jnp.bfloat16)
            qt[j, h, NOPE:, :] = rope.T[:ROPE, :].astype(jnp.bfloat16)
        keep((qx.at[j], qx_to.at[j]), (qt.at[j], qt_to.at[j]))

    started = []
    for step in range(count - 1):
        for part, order in enumerate(orders):
            for slot in range(1 << step):
                flips = 0
                for at in range(step):
                    flips |= ((slot >> at) & 1) << order[at]
                copy = chip_copy(part, step, slot, me ^ flips, slot == 0)
                copy.start()
                started.append(copy)
        if step == 0:
            core_copy(me, 0, True).start()
            keep((lat_raw, lat_raw_to))
            for load in loads:
                load.wait()
        lax.fori_loop(min(2 * step, 4), min(2 * step + 2, 4) if step < count - 2 else 4, query, 0)
        if step == count - 2:
            keep((q_pre, q_pre_to), (q_latent, q_latent_to))
            queries(0)
        for part, order in enumerate(orders):
            for slot in range(1 << step):
                chip_copy(part, step, slot, me, slot == 0).wait_recv()
    for chip in range(1, n // 2):
        core_copy(me ^ (2 * chip), chip, False).start()
    queries(1)
    for chip in range(n // 2):
        core_copy(me, chip, chip == 0).wait_recv()
    for copy in started:
        copy.wait_send()
    for chip in range(n // 2):
        core_copy(me, chip, chip == 0).wait_send()
    local.wait()
    for copy in kept:
        copy.wait()


def head_layer(n, block_map, lengths, tokens, gains, w_qa, w_kva, w_qb, collective_id):
    rows, width = tokens.shape
    rank = w_qa.shape[1]
    count = n.bit_length() - 1
    vmem = pl.BlockSpec(memory_space=pltpu.VMEM)
    slots = max(n // 4, 1)
    dma = pltpu.SemaphoreType.DMA
    smem = pl.BlockSpec(memory_space=pltpu.SMEM)
    anywhere = pl.BlockSpec(memory_space=pl.ANY)
    heads = w_qb.shape[0] // (NOPE + ROPE)
    pairs = (2, heads)
    lane = np.arange(HEAD)
    rates = ROPE_BASE ** (-2.0 * (lane % (ROPE // 2)) / ROPE)
    gathered, *rest = pl.pallas_call(
        functools.partial(head_kernel, n),
        out_shape=(
            jax.ShapeDtypeStruct((n, rows, KVR + ROPE), jnp.bfloat16),
            jax.ShapeDtypeStruct((rows, rank), jnp.bfloat16),
            jax.ShapeDtypeStruct((rows, rank), jnp.float32),
            jax.ShapeDtypeStruct((rows, KVR), jnp.float32),
            jax.ShapeDtypeStruct((rows, HEAD), jnp.float32),
            jax.ShapeDtypeStruct((rows, HEAD), jnp.float32),
            jax.ShapeDtypeStruct((*pairs, rows // 2, WIDE), jnp.bfloat16),
            jax.ShapeDtypeStruct((*pairs, NOPE + ROPE, rows // 2), jnp.bfloat16),
        ),
        in_specs=[smem] * 2 + [vmem] * 3 + [anywhere, vmem, anywhere],
        out_specs=(vmem,) + (anywhere,) * 7,
        scratch_shapes=[
            pltpu.VMEM((rows, rank), jnp.bfloat16),
            pltpu.VMEM((rows, rank), jnp.float32),
            pltpu.VMEM((rows, KVR), jnp.float32),
            pltpu.VMEM((rows, HEAD), jnp.float32),
            pltpu.VMEM((rows, HEAD), jnp.float32),
            pltpu.VMEM((*pairs, rows // 2, WIDE), jnp.bfloat16),
            pltpu.VMEM((*pairs, NOPE + ROPE, rows // 2), jnp.bfloat16),
            pltpu.VMEM(w_qa.shape, jnp.bfloat16),
            pltpu.VMEM(w_qb.shape, jnp.bfloat16),
            dma((2,)),
            dma((9,)),
            pltpu.VMEM((rows, KVR + ROPE), jnp.bfloat16),
            pltpu.VMEM((rows, width), jnp.bfloat16),
            pltpu.VMEM((HEAD, width), jnp.bfloat16),
            pltpu.VMEM((rows // 2, window_columns(heads)), jnp.float32),
            dma,
            dma((2, count - 1, slots)),
            dma((2, count - 1, slots)),
            dma((n // 2,)),
            dma((n // 2,)),
        ],
        compiler_params=pltpu.CompilerParams(
            vmem_limit_bytes=VMEM_LIMIT, collective_id=collective_id, has_side_effects=True
        ),
        cost_estimate=pl.CostEstimate(
            flops=2 * rows * width * (rank + KVR + ROPE),
            bytes_accessed=24 * 1024 * 1024,
            transcendentals=rows,
        ),
        name=f"head_layer_{collective_id}",
    )(
        block_map,
        lengths,
        tokens,
        gains,
        jnp.asarray(rates.astype(np.float32).reshape(1, -1)),
        w_qa,
        w_kva,
        w_qb,
    )
    return gathered.reshape(n * rows, -1), *rest


def on_device(
    tokens_in,
    w_qa,
    w_kva,
    w_qb,
    w_kvb,
    w_out,
    w_gate,
    w_up,
    w_down,
    gain_in,
    gain_q,
    gain_kv,
    gain_mid,
    cotangent,
    block_map,
    doc_lengths,
):
    devices = lax.axis_size("ctx")
    block_map = block_map.T
    gains = jnp.concatenate([gain_in, gain_mid, gain_q, gain_kv]).reshape(1, -1)
    latents, q_latent, q_latent_pre, latent_raw, cosine, sine, queries, queries_t = head_layer(
        devices, block_map, doc_lengths, tokens_in, gains, w_qa, w_kva.T, w_qb.T, 0
    )
    attn_f, heads_out, log_totals = attention_forward(
        block_map, doc_lengths, queries, latents, w_kvb
    )
    attention, d_part, feed_part, activation, d_gate, d_up, normed_mid, d_feed = middle_layer(
        lax.axis_size("tp"), heads_out, tokens_in, cotangent, gains, w_out, w_gate.T, w_up.T,
        w_down.T, 5,
    )
    gw_gate, gw_up, d_attention, d_heads, d_gain_mid = gate_up_grads(
        devices, lax.axis_size("tp"), normed_mid, d_gate, d_up, d_part, tokens_in, attention,
        cotangent, gains, w_out, 1,
    )
    d_heads, feed_part = lax.optimization_barrier((d_heads, feed_part))
    feed_own = lax.psum_scatter(feed_part, "tp", scatter_dimension=0, tiled=True)
    own_rows = feed_own.shape[0]
    own_at = lax.axis_index("tp") * own_rows
    tokens_own = lax.dynamic_slice_in_dim(tokens_in, own_at, own_rows, 0).astype(jnp.float32)
    attention_own = lax.dynamic_slice_in_dim(attention, own_at, own_rows, 0).astype(jnp.float32)
    middle_own = tokens_own + RESIDUAL_SCALE * attention_own
    out_own = (middle_own + RESIDUAL_SCALE * feed_own.astype(jnp.float32)).astype(jnp.bfloat16)
    d_query_pre, d_latents, gw_kvb = attention_backward(
        block_map, doc_lengths, queries, queries_t, log_totals, attn_f, d_heads, latents, w_kvb,
        cosine, sine,
    )
    sum_q, sum_lat, gw_down, gw_out, gw_qb, gw_kvb = up_tail(
        devices, lax.axis_size("tp"), d_latents, d_query_pre, w_qb.T, gw_kvb, d_attention, heads_out,
        q_latent, d_feed, activation, 2,
    )
    sum_q, out_own = lax.optimization_barrier((sum_q, out_own))
    out = lax.all_gather(out_own, "tp", axis=0, tiled=True)
    grad_in, gw_qa, gw_kva, own_gains = down_tail(
        devices, sum_q, sum_lat, q_latent_pre, latent_raw, tokens_in, d_attention, gains,
        d_gain_mid, w_qa, w_kva.T, cosine, sine, 3,
    )
    grads = (gw_qa, gw_kva, gw_qb, gw_kvb, gw_out, gw_gate, gw_up, gw_down)
    return (
        out,
        grad_in,
        *[grad.astype(jnp.float32) for grad in grads],
        own_gains[0],
        own_gains[2],
        own_gains[3],
        own_gains[1],
    )


def solution(mesh):
    return jax.shard_map(
        on_device,
        mesh=mesh,
        in_specs=(
            P("ctx", None),
            P(),
            P(),
            P(None, "tp"),
            P(None, "tp"),
            P(None, "tp"),
            P(None, "tp"),
            P(None, "tp"),
            P(None, "tp"),
            P(),
            P(),
            P(),
            P(),
            P("ctx", None),
            P(),
            P(),
        ),
        out_specs=(
            P("ctx", None),
            P("ctx", None),
            P("ctx", None),
            P("ctx", None),
            P("ctx", "tp"),
            P("ctx", "tp"),
            P("ctx", "tp"),
            P("ctx", "tp"),
            P("ctx", "tp"),
            P("ctx", "tp"),
            P("ctx"),
            P("ctx"),
            P("ctx"),
            P("ctx"),
        ),
        check_vma=False,
    )
```

```python
import functools
import math

import jax
import jax.numpy as jnp
import numpy as np
from jax import lax
from jax.experimental import pallas as pl
from jax.experimental.pallas import tpu as pltpu
from jax.sharding import PartitionSpec as P

KVR = 256
NOPE = 64
ROPE = 32
VDIM = 64
HEAD = NOPE + VDIM
WIDE = 2 * HEAD
MASKED = -1e30
SCORE_SCALE = (NOPE + ROPE) ** (-0.5)
EXP2_SCALE = SCORE_SCALE * math.log2(math.e)
FOLD_AT = 96
SUM_ROWS = 16
VMEM_LIMIT = 56 * 1024 * 1024

EPSILON = 1e-05
ROPE_BASE = 10000.0
RESIDUAL_SCALE = 1.4 / math.sqrt(62.0)


def dot_nn(left_op, right_op):
    return jnp.dot(left_op, right_op, preferred_element_type=jnp.float32)


def dot_nt(left_op, right_op):
    return lax.dot_general(
        left_op, right_op, (((1,), (1,)), ((), ())), preferred_element_type=jnp.float32
    )


def starts_of(lengths):
    starts = [jnp.int32(0)]
    for s in range(lengths.shape[0] - 1):
        starts.append(starts[-1] + lengths[s])
    return starts


def begin_of(place, starts):
    begin = jnp.zeros_like(place)
    for start in starts:
        begin = jnp.where(start <= place, start, begin)
    return begin


def pair_kind(key_block, query_block, starts, block_rows):
    key_first = key_block * block_rows
    query_first = query_block * block_rows
    early = begin_of(query_first, starts)
    late = begin_of(query_first + block_rows - 1, starts)
    needed = (key_block <= query_block) & (key_first + block_rows - 1 >= early)
    whole = (key_block < query_block) & (late <= key_first)
    return needed, whole


def mask_bias(key_block, query_block, starts, block_rows, keys_first):
    key_dim = 0 if keys_first else 1
    shape = (block_rows, block_rows)
    key_place = key_block * block_rows + lax.broadcasted_iota(jnp.int32, shape, key_dim)
    query_place = query_block * block_rows + lax.broadcasted_iota(jnp.int32, shape, 1 - key_dim)
    begin = jnp.zeros(shape, jnp.int32)
    for start in starts:
        begin = jnp.where(start <= query_place, start, begin)
    allowed = (key_place <= query_place) & (key_place >= begin)
    return jnp.where(allowed, 0.0, MASKED)


def shared_key_tile(rope_rows, block_rows):
    place = lax.broadcasted_iota(jnp.int32, (ROPE, HEAD), 0)
    lane = lax.broadcasted_iota(jnp.int32, (ROPE, HEAD), 1)
    eye = jnp.where(place == lane, 1.0, 0.0).astype(jnp.bfloat16)
    tile = dot_nn(rope_rows, eye)
    lanes = lax.broadcasted_iota(jnp.int32, (block_rows, HEAD), 1)
    ones = (lanes >= FOLD_AT) & (lanes < FOLD_AT + 3)
    return jnp.where(ones, 1.0, tile).astype(jnp.bfloat16)


def head_window(h):
    at = h * (NOPE + ROPE)
    return at // HEAD * HEAD, at % HEAD


def window_columns(heads):
    return head_window(heads - 1)[0] + WIDE


def head_groups(heads):
    return [(h, min(h + 2, heads)) for h in range(0, heads, 2)]


def forward_kernel(
    blocks, heads, block_map, lengths, qx, lat, wkvb, o_out, ob_out, u_out,
    wkvt, xs, xr, vt, top, acc, bias, s_ref, p_ref,
):
    block_rows = bias.shape[0]
    q_blocks = qx.shape[0]
    starts = starts_of(lengths)
    own = [block_map[j, lax.axis_index("ctx")] for j in range(q_blocks)]
    for first, last in head_groups(heads):
        wkvt[first * HEAD : last * HEAD, :] = (
            wkvb[:, first * HEAD : last * HEAD].astype(jnp.float32).T.astype(jnp.bfloat16)
        )
    top[...] = jnp.full(top.shape, MASKED, jnp.float32)
    vt[:, VDIM:, :] = jnp.ones((heads, SUM_ROWS, block_rows), jnp.bfloat16)
    acc[...] = jnp.zeros(acc.shape, jnp.float32)

    def pair(j, masked):
        def one(h):
            keys = jnp.concatenate([xs[h], xr[...]], axis=1)
            s_ref[h % 3] = dot_nt(keys, qx[j, h])

        def weigh(h):
            old = top[j, h]
            new = old
            for k in range(0, block_rows, 128):
                part = s_ref[h % 3, k : k + 128, :]
                if masked:
                    part = part + bias[k : k + 128, :]
                    s_ref[h % 3, k : k + 128, :] = part
                new = jnp.maximum(new, jnp.max(part, axis=0, keepdims=True))
            fade = jnp.exp2((old - new) * EXP2_SCALE)
            top[j, h] = new
            for k in range(0, block_rows, 128):
                terms = jnp.exp2((s_ref[h % 3, k : k + 128, :] - new) * EXP2_SCALE)
                p_ref[h % 3, k : k + 128, :] = terms.astype(jnp.bfloat16)
            return fade

        def add(h, fade):
            acc[j, h] = fade * acc[j, h] + dot_nn(vt[h], p_ref[h % 3])

        one(0)
        if heads > 1:
            one(1)
        fades = {}
        for h in range(heads):
            if h + 2 < heads:
                one(h + 2)
            fades[h] = weigh(h)
            if h > 1:
                add(h - 2, fades[h - 2])
        for h in range(max(heads - 2, 0), heads):
            add(h, fades[h])

    def step(r, carry):
        key_block = block_map[lax.rem(r, 2), lax.div(r, 2)]
        kinds = [pair_kind(key_block, own[j], starts, block_rows) for j in range(q_blocks)]
        wanted = functools.reduce(jnp.logical_or, [k[0] for k in kinds])

        @pl.when(wanted)
        def _():
            here = pl.ds(pl.multiple_of(r * block_rows, block_rows), block_rows)
            latent = lat[here, :KVR]
            xr[...] = shared_key_tile(lat[here, KVR : KVR + ROPE], block_rows)
            for first, last in head_groups(heads):
                keys = dot_nn(latent, wkvb[:, first * HEAD : last * HEAD]).astype(jnp.bfloat16)
                values = dot_nt(wkvt[first * HEAD : last * HEAD, :], latent).astype(jnp.bfloat16)
                for h in range(first, last):
                    at = (h - first) * HEAD
                    xs[h] = keys[:, at : at + HEAD]
                    vt[h, :VDIM, :] = values[at + NOPE : at + HEAD, :]

        for j in range(q_blocks):
            needed, whole = kinds[j]

            @pl.when(needed & whole)
            def _():
                pair(j, False)

            @pl.when(needed & jnp.logical_not(whole))
            def _():
                bias[...] = mask_bias(key_block, own[j], starts, block_rows, True)
                pair(j, True)

        return carry

    lax.fori_loop(0, blocks, step, 0)
    for j in range(q_blocks):
        here = pl.ds(j * block_rows, block_rows)
        for first, last in head_groups(heads):
            parts = []
            for h in range(first, last):
                total = acc[j, h, VDIM : VDIM + 1, :]
                parts.append(acc[j, h, :VDIM, :] * (1.0 / total))
                u_out[j, h : h + 1, :] = top[j, h] + jnp.log2(total) * (1.0 / EXP2_SCALE)
            if len(parts) == 1:
                parts.append(jnp.zeros_like(parts[0]))
            both = jnp.concatenate(parts, axis=0).T
            width = (last - first) * VDIM
            o_out[here, first * VDIM : first * VDIM + width] = both[:, :width]
            ob_out[here, first * VDIM : first * VDIM + width] = both[:, :width].astype(jnp.bfloat16)


def attention_forward(block_map, lengths, qx, lat, wkvb):
    q_blocks, heads, block_rows, _ = qx.shape
    blocks = lat.shape[0] // block_rows
    rows = q_blocks * block_rows
    vmem = pl.BlockSpec(memory_space=pltpu.VMEM)
    smem = pl.BlockSpec(memory_space=pltpu.SMEM)
    pairs = q_blocks * blocks * heads // 2
    return pl.pallas_call(
        functools.partial(forward_kernel, blocks, heads),
        out_shape=(
            jax.ShapeDtypeStruct((rows, heads * VDIM), jnp.float32),
            jax.ShapeDtypeStruct((rows, heads * VDIM), jnp.bfloat16),
            jax.ShapeDtypeStruct((q_blocks, 16 * -(-heads // 16), block_rows), jnp.float32),
        ),
        in_specs=[smem] * 2 + [vmem] * 3,
        out_specs=(vmem,) * 3,
        scratch_shapes=[
            pltpu.VMEM((heads * HEAD, KVR), jnp.bfloat16),
            pltpu.VMEM((heads, block_rows, HEAD), jnp.bfloat16),
            pltpu.VMEM((block_rows, HEAD), jnp.bfloat16),
            pltpu.VMEM((heads, VDIM + SUM_ROWS, block_rows), jnp.bfloat16),
            pltpu.VMEM((q_blocks, heads, 1, block_rows), jnp.float32),
            pltpu.VMEM((q_blocks, heads, VDIM + SUM_ROWS, block_rows), jnp.float32),
            pltpu.VMEM((block_rows, block_rows), jnp.float32),
            pltpu.VMEM((3, block_rows, block_rows), jnp.float32),
            pltpu.VMEM((3, block_rows, block_rows), jnp.bfloat16),
        ],
        compiler_params=pltpu.CompilerParams(vmem_limit_bytes=VMEM_LIMIT),
        cost_estimate=pl.CostEstimate(
            flops=pairs * 4 * block_rows * block_rows * WIDE,
            bytes_accessed=16 * 1024 * 1024,
            transcendentals=pairs * block_rows * block_rows,
        ),
        name="attention_forward",
    )(block_map, lengths, qx, lat, wkvb)


def three_terms(column):
    first = column.astype(jnp.bfloat16).astype(jnp.float32)
    rest = column - first
    second = rest.astype(jnp.bfloat16).astype(jnp.float32)
    return first, second, rest - second


def fold_in(tile, column, lane):
    for k, term in enumerate(three_terms(column)):
        tile = jnp.where(lane == FOLD_AT + k, term, tile)
    return tile


def backward_kernel(
    blocks, heads, block_map, lengths, qx, qt, u_in, o_in, dob, lat, wkvb, cos, sin,
    dq_out, dlat, gkvb, xs, xr, qo, dt, dq, dkv, dkpe, gsum, bias, flat, s_ref, p_ref, d_ref,
):
    block_rows = bias.shape[0]
    q_blocks = qx.shape[0]
    starts = starts_of(lengths)
    own = [block_map[j, lax.axis_index("ctx")] for j in range(q_blocks)]
    lane = lax.broadcasted_iota(jnp.int32, (block_rows, HEAD), 1)
    for j in range(q_blocks):
        here = pl.ds(j * block_rows, block_rows)
        logs = u_in[j].T
        for first, last in head_groups(heads):
            d_pair = dob[here, first * VDIM : first * VDIM + HEAD].astype(jnp.float32)
            weighted = d_pair * o_in[here, first * VDIM : first * VDIM + HEAD]
            turned = pltpu.roll(d_pair, VDIM, 1)
            for h in range(first, last):
                mine = lane < VDIM if h == first else lane >= VDIM
                delta = jnp.sum(jnp.where(mine, weighted, 0.0), axis=1, keepdims=True)
                d_head = jnp.where(lane >= VDIM, turned if h == first else d_pair, 0.0)
                q_second = qx[j, h, :, HEAD:].astype(jnp.float32)
                qo[j, h, :block_rows, :HEAD] = qx[j, h, :, :HEAD]
                qo[j, h, :block_rows, HEAD:] = fold_in(q_second, -logs[:, h : h + 1], lane).astype(
                    jnp.bfloat16
                )
                qo[j, h, block_rows:, :HEAD] = d_head.astype(jnp.bfloat16)
                qo[j, h, block_rows:, HEAD:] = fold_in(
                    jnp.zeros((block_rows, HEAD), jnp.float32), -delta, lane
                ).astype(jnp.bfloat16)
                dt[j, h] = d_head.T[VDIM:, :].astype(jnp.bfloat16)
    dq[...] = jnp.zeros(dq.shape, jnp.float32)
    gsum[...] = jnp.zeros(gsum.shape, jnp.float32)

    def pair(j, masked):
        def raw(h):
            keys = jnp.concatenate([xs[h], xr[...]], axis=1)
            s_ref[h % 2] = dot_nt(qo[j, h], keys)

        def weigh(h):
            for k in range(0, block_rows, 128):
                scores = s_ref[h % 2, k : k + 128, :] * EXP2_SCALE
                if masked:
                    scores = scores + bias[k : k + 128, :]
                probs = jnp.exp2(scores)
                p_ref[h % 2, k : k + 128, :] = probs.astype(jnp.bfloat16)
                d_ref[h % 2, k : k + 128, :] = (
                    probs * s_ref[h % 2, block_rows + k : block_rows + k + 128, :]
                ).astype(jnp.bfloat16)

        def add(h):
            keys = jnp.concatenate([xs[h], xr[...]], axis=1)
            d_scores = d_ref[h % 2]
            dq[j, h] += dot_nn(d_scores, keys)
            d_keys = dot_nn(qt[j, h], d_scores)
            dkv[h, :NOPE, :] += d_keys[:NOPE]
            dkpe[...] += d_keys[NOPE:]
            dkv[h, NOPE:, :] += dot_nn(dt[j, h], p_ref[h % 2])

        raw(0)
        for h in range(heads):
            if h + 1 < heads:
                raw(h + 1)
            weigh(h)
            if h:
                add(h - 1)
        add(heads - 1)

    def step(r, carry):
        key_block = block_map[lax.rem(r, 2), lax.div(r, 2)]
        kinds = [pair_kind(key_block, own[j], starts, block_rows) for j in range(q_blocks)]
        wanted = functools.reduce(jnp.logical_or, [k[0] for k in kinds])
        here = pl.ds(pl.multiple_of(r * block_rows, block_rows), block_rows)

        @pl.when(wanted)
        def _():
            latent = lat[here, :KVR]
            xr[...] = shared_key_tile(lat[here, KVR : KVR + ROPE], block_rows)
            for first, last in head_groups(heads):
                keys = dot_nn(latent, wkvb[:, first * HEAD : last * HEAD]).astype(jnp.bfloat16)
                for h in range(first, last):
                    xs[h] = keys[:, (h - first) * HEAD : (h - first + 1) * HEAD]
            dkv[...] = jnp.zeros(dkv.shape, jnp.float32)
            dkpe[...] = jnp.zeros(dkpe.shape, jnp.float32)

        for j in range(q_blocks):
            needed, whole = kinds[j]

            @pl.when(needed & whole)
            def _():
                pair(j, False)

            @pl.when(needed & jnp.logical_not(whole))
            def _():
                bias[...] = mask_bias(key_block, own[j], starts, block_rows, False)
                pair(j, True)

        @pl.when(wanted)
        def _():
            latent = lat[here, :KVR]
            d_latent = jnp.zeros((KVR, block_rows), jnp.float32)
            for h in range(heads):
                d_head = jnp.concatenate(
                    [dkv[h, :NOPE, :] * SCORE_SCALE, dkv[h, NOPE:, :]], axis=0
                ).astype(jnp.bfloat16)
                d_latent += dot_nn(wkvb[:, h * HEAD : (h + 1) * HEAD], d_head)
                gsum[h * HEAD : (h + 1) * HEAD, :] += dot_nn(d_head, latent)
            dlat[here, :KVR] = d_latent.T.astype(jnp.bfloat16)
            rope = jnp.concatenate(
                [dkpe[...] * SCORE_SCALE, jnp.zeros((HEAD - ROPE, block_rows), jnp.float32)], axis=0
            )
            dlat[here, KVR:] = rope.T[:, :ROPE].astype(jnp.bfloat16)

        @pl.when(jnp.logical_not(wanted))
        def _():
            dlat[here, :] = jnp.zeros((block_rows, KVR + ROPE), jnp.bfloat16)

        return carry

    lax.fori_loop(0, blocks, step, 0)
    for h in range(heads):
        gkvb[:, h * HEAD : (h + 1) * HEAD] = gsum[h * HEAD : (h + 1) * HEAD, :].T.astype(
            jnp.bfloat16
        )
    for j in range(q_blocks):
        here = pl.ds(j * block_rows, block_rows)
        cos_j, sin_j = cos[here, :], sin[here, :]
        flat[...] = jnp.zeros(flat.shape, jnp.float32)
        for h in range(heads):
            nope = jnp.where(lane < NOPE, dq[j, h, :, :HEAD], 0.0)
            rope = dq[j, h, :, HEAD:]
            shifted = rope * sin_j
            left = pltpu.roll(shifted, HEAD - ROPE // 2, 1)
            right = pltpu.roll(shifted, ROPE // 2, 1)
            swapped = jnp.where(lane < ROPE // 2, left, jnp.where(lane < ROPE, -right, 0.0))
            back = pltpu.roll(jnp.where(lane < ROPE, rope * cos_j + swapped, 0.0), NOPE, 1)
            whole = jnp.concatenate([(nope + back) * SCORE_SCALE, jnp.zeros_like(nope)], axis=1)
            at, shift = head_window(h)
            flat[:, at : at + WIDE] += pltpu.roll(whole, shift, 1)
        dq_out[here, :] = flat[:, : heads * (NOPE + ROPE)].astype(jnp.bfloat16)


def attention_backward(block_map, lengths, qx, qt, u_in, o_in, dob, lat, wkvb, cos, sin):
    q_blocks, heads, block_rows, _ = qx.shape
    blocks = lat.shape[0] // block_rows
    rows = q_blocks * block_rows
    odd = -(heads * VDIM) % HEAD
    if odd:
        o_in = jnp.pad(o_in, ((0, 0), (0, odd)))
        dob = jnp.pad(dob, ((0, 0), (0, odd)))
    vmem = pl.BlockSpec(memory_space=pltpu.VMEM)
    smem = pl.BlockSpec(memory_space=pltpu.SMEM)
    pairs = q_blocks * blocks * heads // 2
    return pl.pallas_call(
        functools.partial(backward_kernel, blocks, heads),
        out_shape=(
            jax.ShapeDtypeStruct((rows, heads * (NOPE + ROPE)), jnp.bfloat16),
            jax.ShapeDtypeStruct((lat.shape[0], KVR + ROPE), jnp.bfloat16),
            jax.ShapeDtypeStruct((KVR, heads * HEAD), jnp.bfloat16),
        ),
        in_specs=[smem] * 2 + [vmem] * 9,
        out_specs=(vmem,) * 3,
        scratch_shapes=[
            pltpu.VMEM((heads, block_rows, HEAD), jnp.bfloat16),
            pltpu.VMEM((block_rows, HEAD), jnp.bfloat16),
            pltpu.VMEM((q_blocks, heads, 2 * block_rows, WIDE), jnp.bfloat16),
            pltpu.VMEM((q_blocks, heads, VDIM, block_rows), jnp.bfloat16),
            pltpu.VMEM((q_blocks, heads, block_rows, WIDE), jnp.float32),
            pltpu.VMEM((heads, HEAD, block_rows), jnp.float32),
            pltpu.VMEM((ROPE, block_rows), jnp.float32),
            pltpu.VMEM((heads * HEAD, KVR), jnp.float32),
            pltpu.VMEM((block_rows, block_rows), jnp.float32),
            pltpu.VMEM((block_rows, window_columns(heads)), jnp.float32),
            pltpu.VMEM((2, 2 * block_rows, block_rows), jnp.float32),
            pltpu.VMEM((2, block_rows, block_rows), jnp.bfloat16),
            pltpu.VMEM((2, block_rows, block_rows), jnp.bfloat16),
        ],
        compiler_params=pltpu.CompilerParams(vmem_limit_bytes=VMEM_LIMIT),
        cost_estimate=pl.CostEstimate(
            flops=pairs * 8 * block_rows * block_rows * WIDE,
            bytes_accessed=24 * 1024 * 1024,
            transcendentals=pairs * block_rows * block_rows,
        ),
        name="attention_backward",
    )(block_map, lengths, qx, qt, u_in, o_in, dob, lat, wkvb, cos, sin)


MESH = pl.DeviceIdType.MESH


class LineSum:
    def __init__(self, n, own, landing, total, sems, lag):
        self.n, self.own, self.landing, self.total, self.lag = n, own, landing, total, lag
        self.up_send, self.up_land, self.down_send, self.back_send, self.down_land = sems
        self.me = lax.axis_index("tp")
        self.root = (n - 1) // 2
        self.chunks = own.shape[0]
        self.has_left, self.has_right = self.me > 0, self.me < n - 1
        self.root_lag = (n - 1 - self.root) * lag
        self.land_lag = 2 * self.root_lag
        self.ticks = self.chunks + self.land_lag

    def greet(self, barrier):
        me = self.me
        for there, other in ((self.has_left, me - 1), (self.has_right, me + 1)):

            @pl.when(there)
            def _(other=other):
                pl.semaphore_signal(barrier, inc=1, device_id={"tp": other}, device_id_type=MESH)

    def wait_greetings(self, barrier, others):
        both = self.has_left & self.has_right

        @pl.when(both)
        def _():
            pl.semaphore_wait(barrier, 2 + others)

        @pl.when(jnp.logical_not(both))
        def _():
            pl.semaphore_wait(barrier, 1 + others)

    def copy_to(self, source, target, send, land, c, other):
        return pltpu.make_async_remote_copy(
            src_ref=source.at[c],
            dst_ref=target.at[c],
            send_sem=send.at[c],
            recv_sem=land.at[c],
            device_id={"tp": other},
            device_id_type=MESH,
        )

    def rise_left(self, c):
        return self.copy_to(self.own, self.landing, self.up_send, self.up_land, c, self.me + 1)

    def rise_right(self, c):
        return self.copy_to(self.own, self.landing, self.up_send, self.up_land, c, self.me - 1)

    def rise_last(self, c):
        return self.copy_to(self.own, self.total, self.up_send, self.down_land, c, self.me - 1)

    def fall_right(self, c):
        return self.copy_to(self.total, self.total, self.down_send, self.down_land, c, self.me + 1)

    def fall_left(self, c):
        return self.copy_to(self.total, self.total, self.back_send, self.down_land, c, self.me - 1)

    def rise(self, c):
        me, root = self.me, self.root
        rises = [(me == root + 1, self.rise_last)]
        if root:
            rises.append((me < root, self.rise_left))
        if self.n - 1 > root + 1:
            rises.append((me > root + 1, self.rise_right))
        for who, copy in rises:

            @pl.when(who)
            def _(copy=copy):
                copy(c).start()

    def inside(self, c):
        return (c >= 0) & (c < self.chunks)

    def added(self, refs, c):
        sums = refs[0][c].astype(jnp.float32)
        for ref in refs[1:]:
            sums = sums + ref[c].astype(jnp.float32)
        return sums.astype(self.total.dtype)

    def leaf(self, c):
        is_leaf = self.me == self.n - 1
        if self.root:
            is_leaf = is_leaf | (self.me == 0)

        @pl.when(is_leaf & self.inside(c))
        def _():
            self.rise(c)

    def leaves(self):
        def body(c, carry):
            self.leaf(c)
            return carry

        lax.fori_loop(0, self.chunks, body, 0)

    def pump(self, first, last):
        def body(t, carry):
            self.duty(t)
            return carry

        lax.fori_loop(first, last, body, 0)

    def duty(self, t):
        me, root = self.me, self.root
        if self.n > 3:
            c = t - self.lag * jnp.where(me < root, me, self.n - 1 - me)

            @pl.when((me != root) & self.has_left & self.has_right & self.inside(c))
            def _():
                self.rise_right(c).wait_recv()
                self.own[c] = self.added([self.own, self.landing], c)
                self.rise(c)

        c_root = t - self.root_lag

        @pl.when((me == root) & self.inside(c_root))
        def _():
            if root:
                self.rise_left(c_root).wait_recv()
            self.fall_right(c_root).wait_recv()
            terms = [self.own, self.landing, self.total] if root else [self.own, self.total]
            self.total[c_root] = self.added(terms, c_root)
            self.fall_right(c_root).start()
            if root:
                self.fall_left(c_root).start()

        c_fall = t - self.root_lag - self.lag * jnp.where(me < root, root - me, me - root)

        @pl.when((me != root) & self.inside(c_fall))
        def _():
            self.fall_right(c_fall).wait_recv()

            @pl.when((me > root) & self.has_right)
            def _():
                self.fall_right(c_fall).start()

            @pl.when((me < root) & self.has_left)
            def _():
                self.fall_left(c_fall).start()

    def landed(self, t):
        return t - self.land_lag

    def drain(self):
        me = self.me

        def body(c, carry):
            @pl.when(me != self.root)
            def _():
                self.rise_right(c).wait_send()

            @pl.when((me >= self.root) & self.has_right)
            def _():
                self.fall_right(c).wait_send()

            @pl.when((me <= self.root) & self.has_left)
            def _():
                self.fall_left(c).wait_send()

            return carry

        lax.fori_loop(0, self.chunks, body, 0)


def line_sems(chunks):
    return [pltpu.SemaphoreType.DMA((chunks,))] * 5


def scatter_blocks(bits_left):
    chips = []
    for value in range(1 << len(bits_left)):
        chip = 0
        for at, bit in enumerate(bits_left):
            chip = chip + (((value >> at) & 1) << (bit - 1))
        chips.append(chip)
    return chips


class Scatter:
    def __init__(self, n, rows, columns, is_given):
        self.n, self.rows, self.columns, self.is_given = n, rows, columns, is_given
        self.count = n.bit_length() - 1
        self.parts = 2 if rows % 32 == 0 else 1

    def scratch(self):
        n, count = self.n, self.count
        half = jnp.bfloat16
        dma = pltpu.SemaphoreType.DMA
        shapes = [pltpu.VMEM((n // 2, self.rows, self.columns), half)]
        if not self.is_given:
            shapes.append(pltpu.VMEM((n // 2, self.rows, self.columns), half))
        for step in range(count - 1):
            shapes.append(pltpu.VMEM((n >> (step + 2), self.rows, self.columns), half))
        shapes += [dma((n // 2,))] * 2
        for step in range(count - 1):
            shapes += [dma((2, n >> (step + 2)))] * 2
        return shapes

    def bind(self, take, source, emit):
        self.held = take(1)[0]
        self.sent = None if self.is_given else take(1)[0]
        self.landed = take(self.count - 1)
        self.core_sems = take(2)
        self.step_sems = [take(2) for _ in range(self.count - 1)]
        self.source, self.emit = source, emit
        self.me = lax.axis_index("ctx")
        self.core = self.me & 1
        self.chips = self.n // 2
        self.orders = (tuple(range(1, self.count)), tuple(range(self.count - 1, 0, -1)))
        self.tiles = [(c, min(c + 512, self.columns)) for c in range(0, self.columns, 512)]
        return self

    def own(self, dest, first, last):
        at = pl.ds(pl.multiple_of(dest * self.rows, 16), self.rows)
        if self.is_given:
            return self.source[at, first:last].astype(jnp.float32)
        return dot_nn(self.source[0][at, :], self.source[1][:, first:last])

    def core_copy(self, chip):
        if self.is_given:
            at = pl.ds(pl.multiple_of((2 * chip + 1 - self.core) * self.rows, 16), self.rows)
            source = self.source.at[at, :]
        else:
            source = self.sent.at[chip]
        return pltpu.make_async_remote_copy(
            src_ref=source,
            dst_ref=self.held.at[chip],
            send_sem=self.core_sems[0].at[chip],
            recv_sem=self.core_sems[1].at[chip],
            device_id={"ctx": self.me ^ 1},
            device_id_type=MESH,
        )

    def step_copies(self, step):
        half = self.rows // self.parts
        me = self.me
        copies = []
        for part, order in enumerate(self.orders[: self.parts]):
            bit = order[step]
            at = pl.ds(part * half, half)
            for slot, free in enumerate(scatter_blocks(sorted(order[step + 1 :]))):
                keep = free + ((me >> bit) & 1) * (1 << (bit - 1))
                send = free + (1 - ((me >> bit) & 1)) * (1 << (bit - 1))
                for b in order[:step]:
                    own = ((me >> b) & 1) * (1 << (b - 1))
                    keep, send = keep + own, send + own
                copy = pltpu.make_async_remote_copy(
                    src_ref=self.held.at[send, at, :],
                    dst_ref=self.landed[step].at[slot, at, :],
                    send_sem=self.step_sems[step][0].at[part, slot],
                    recv_sem=self.step_sems[step][1].at[part, slot],
                    device_id={"ctx": me ^ (1 << bit)},
                    device_id_type=MESH,
                )
                copies.append((copy, keep, slot, at))
        return copies

    def start_core(self, also=None):
        def body(chip, carry):
            if also is not None:
                also(chip)
            if not self.is_given:
                for first, last in self.tiles:
                    self.sent[chip, :, first:last] = self.own(
                        2 * chip + 1 - self.core, first, last
                    ).astype(jnp.bfloat16)
            self.core_copy(chip).start()
            return carry

        lax.fori_loop(0, self.chips, body, 0)

    def finish_core(self, also=None):
        def body(chip, carry):
            if also is not None:
                also(chip)
            self.core_copy(chip).wait_recv()
            for first, last in self.tiles:
                total = self.own(2 * chip + self.core, first, last)
                total = total + self.held[chip, :, first:last].astype(jnp.float32)
                self.held[chip, :, first:last] = total.astype(jnp.bfloat16)
            return carry

        lax.fori_loop(0, self.chips, body, 0)

    def start_step(self, step):
        for copy, _, _, _ in self.step_copies(step):
            copy.start()

    def finish_step(self, step):
        for copy, keep, slot, at in self.step_copies(step):
            copy.wait_recv()
            for first, last in self.tiles:
                total = self.held[keep, at, first:last].astype(jnp.float32)
                total = total + self.landed[step][slot, at, first:last].astype(jnp.float32)
                if step == self.count - 2:
                    self.emit(at, first, last, total)
                else:
                    self.held[keep, at, first:last] = total.astype(jnp.bfloat16)
        if step + 1 < self.count - 1:
            self.start_step(step + 1)

    def drain(self):
        def body(chip, carry):
            self.core_copy(chip).wait_send()
            return carry

        lax.fori_loop(0, self.chips, body, 0)
        for step in range(self.count - 1):
            for copy, _, _, _ in self.step_copies(step):
                copy.wait_send()


def taker(refs):
    refs = list(refs)

    def take(k):
        taken = refs[:k]
        del refs[:k]
        return taken

    return take


def store_in(ref):
    def emit(at, first, last, total):
        ref[at, first:last] = total.astype(ref.dtype)

    return emit


def turn(source, target):
    def body(c, carry):
        at = pl.ds(pl.multiple_of(c * 128, 128), 128)
        target[at, :] = source[:, at].astype(jnp.float32).T.astype(jnp.bfloat16)
        return carry

    lax.fori_loop(0, source.shape[1] // 128, body, 0)


def greet_ctx(n, barrier):
    me = lax.axis_index("ctx")
    count = n.bit_length() - 1
    for bit in range(count):
        pl.semaphore_signal(barrier, inc=1, device_id={"ctx": me ^ (1 << bit)}, device_id_type=MESH)
    return count


def spread(waits, ticks):
    portion = -(-ticks // waits)
    return [(min(k * portion, ticks), min((k + 1) * portion, ticks)) for k in range(waits)]


def gate_up_kernel(
    n, tp, plans, normed, d_gate, d_up, terms, tokens, attn, cot, w_out_in, gain_row,
    gate_out, up_out, d_attn, d_heads, g_mid, *refs,
):
    take = taker(refs)
    own, landing, sums, normed_t, slots, in_sems, own_sem, w_out, w_sem = take(9)
    w_load = pltpu.make_async_copy(w_out_in, w_out, w_sem)
    line = LineSum(tp, own, landing, sums, take(5), LAG)
    gate = plans[0].bind(take, (normed_t, d_gate), store_in(gate_out))
    up = plans[1].bind(take, (normed_t, d_up), store_in(up_out))
    width = normed.shape[1]
    blocks = normed.shape[0] // BLOCK
    per_block = BLOCK // CHUNK
    load = pltpu.make_async_copy(terms, own, own_sem)
    load.start()
    barrier = pltpu.get_barrier_semaphore()
    others = greet_ctx(n, barrier)
    line.greet(barrier)

    def fetch(b):
        rows = pl.ds(b * BLOCK, BLOCK)
        return [
            pltpu.make_async_copy(
                source.at[rows, :], slots.at[b % 2, k], in_sems.at[b % 2, k]
            )
            for k, source in enumerate((tokens, attn, cot))
        ]

    for b in range(min(2, blocks)):
        for copy in fetch(b):
            copy.start()
    w_load.start()
    g_mid[...] = jnp.zeros(g_mid.shape, jnp.float32)

    def norm(b):
        if b == 0:
            w_load.wait()
        for copy in fetch(b):
            copy.wait()
        for part in range(0, BLOCK, 2 * CHUNK):
            rows = pl.ds(b * BLOCK + part, 2 * CHUNK)
            here = pl.ds(part, 2 * CHUNK)
            c = b * per_block + part // CHUNK
            incoming = jnp.concatenate([sums[c], sums[c + 1]], axis=0).astype(jnp.float32)
            middle = slots[b % 2, 0, here, :].astype(jnp.float32)
            middle = middle + RESIDUAL_SCALE * slots[b % 2, 1, here, :].astype(jnp.float32)
            d_norm, gain_terms = norm_back(
                incoming, middle, norm_scale(middle), gain_row[:, width : 2 * width]
            )
            g_mid[...] += gain_terms
            total = slots[b % 2, 2, here, :].astype(jnp.float32) + d_norm
            d_attn[rows, :] = (RESIDUAL_SCALE * total).astype(jnp.bfloat16)
        rows = pl.ds(b * BLOCK, BLOCK)
        d_heads[rows, :] = dot_nn(d_attn[rows, :], w_out[...]).astype(jnp.bfloat16)
        if b + 2 < blocks:
            for copy in fetch(b + 2):
                copy.start()

    load.wait()
    line.wait_greetings(barrier, others)
    line.leaves()
    turn(normed, normed_t)
    chips = n // 2
    gate.start_core()
    gate.finish_core(line.duty)
    gate.start_step(0)
    up.start_core(lambda chip: line.duty(chips + chip))
    up.finish_core(lambda chip: line.duty(2 * chips + chip))
    up.start_step(0)
    steps = [(item, step) for step in range(gate.count - 1) for item in (gate, up)]
    done = 3 * chips
    next_block = 0
    for (item, step), (first, last) in zip(steps, spread(len(steps), line.ticks - done)):
        line.pump(done + first, done + last)
        while next_block < blocks and line.landed(done + last - 1) >= (next_block + 1) * per_block - 1:
            norm(next_block)
            next_block += 1
        item.finish_step(step)
    for item in (gate, up, line):
        item.drain()


def gate_up_grads(
    n, tp, normed, d_gate, d_up, terms, tokens, attn, cot, gain_row, w_out, collective_id
):
    rows, width = normed.shape
    hidden = d_gate.shape[1]
    head_width = w_out.shape[1]
    vmem = pl.BlockSpec(memory_space=pltpu.VMEM)
    anywhere = pl.BlockSpec(memory_space=pl.ANY)
    half = jnp.bfloat16
    plans = [Scatter(n, width // n, hidden, False) for _ in range(2)]
    chunked = (rows // CHUNK, CHUNK, width)
    return pl.pallas_call(
        functools.partial(gate_up_kernel, n, tp, plans),
        out_shape=(
            jax.ShapeDtypeStruct((width // n, hidden), half),
            jax.ShapeDtypeStruct((width // n, hidden), half),
            jax.ShapeDtypeStruct((rows, width), half),
            jax.ShapeDtypeStruct((rows, head_width), half),
            jax.ShapeDtypeStruct((1, width), jnp.float32),
        ),
        in_specs=[vmem] * 3 + [anywhere] * 5 + [vmem],
        out_specs=(vmem,) * 5,
        scratch_shapes=[
            pltpu.VMEM(chunked, half),
            pltpu.VMEM(chunked, half),
            pltpu.VMEM(chunked, half),
            pltpu.VMEM((width, rows), half),
            pltpu.VMEM((2, 3, BLOCK, width), half),
            pltpu.SemaphoreType.DMA((2, 3)),
            pltpu.SemaphoreType.DMA,
            pltpu.VMEM(w_out.shape, half),
            pltpu.SemaphoreType.DMA,
            *line_sems(rows // CHUNK),
            *plans[0].scratch(),
            *plans[1].scratch(),
        ],
        compiler_params=pltpu.CompilerParams(
            vmem_limit_bytes=MIDDLE_VMEM, collective_id=collective_id, has_side_effects=True
        ),
        cost_estimate=pl.CostEstimate(
            flops=2 * rows * width * (2 * hidden + head_width),
            bytes_accessed=28 * 1024 * 1024,
            transcendentals=0,
        ),
        name=f"gate_up_grads_{collective_id}",
    )(normed, d_gate, d_up, terms.reshape(chunked), tokens, attn, cot, w_out, gain_row)


TAIL_CHUNK = 64


def up_tail_kernel(
    n, tp, plans, d_lat, d_query, w_qb, g_kvb_in, d_attn_in, ob_in, q_latent_in, d_feed_in, act_in,
    sum_q, sum_lat, down_out, out_out, qb_out, kvb_out, *refs,
):
    take = taker(refs)
    own_q, land_q, own_lat, land_lat, d_attn_t, q_latent_t, d_feed_t = take(7)
    g_kvb, d_attn, ob, q_latent, d_feed, act, in_sems = take(7)
    loads = {}
    pairs = ((d_feed_in, d_feed), (act_in, act), (d_attn_in, d_attn), (ob_in, ob))
    pairs += ((q_latent_in, q_latent), (g_kvb_in, g_kvb))
    for k, (source, target) in enumerate(pairs):
        loads[id(target)] = pltpu.make_async_copy(source, target, in_sems.at[k])
        loads[id(target)].start()
    line_q = LineSum(tp, own_q, land_q, sum_q, take(5), LAG)
    line_lat = LineSum(tp, own_lat, land_lat, sum_lat, take(5), LAG)
    chunk = own_q.shape[1]

    def store_lat(at, first, last, total):
        for k in range(at.size // chunk):
            own_lat[at.start // chunk + k, :, first:last] = total[
                k * chunk : (k + 1) * chunk
            ].astype(jnp.bfloat16)

    lat, down, out, qb, kvb = plans
    lat.bind(take, d_lat, store_lat)
    down.bind(take, (d_feed_t, act), store_in(down_out))
    out.bind(take, (d_attn_t, ob), store_in(out_out))
    qb.bind(take, (q_latent_t, d_query), store_in(qb_out))
    kvb.bind(take, g_kvb, store_in(kvb_out))
    barrier = pltpu.get_barrier_semaphore()
    others = greet_ctx(n, barrier)
    line_q.greet(barrier)
    line_q.wait_greetings(barrier, others)
    lat.start_core()

    def query(c, carry):
        rows = pl.ds(pl.multiple_of(c * 2 * chunk, 2 * chunk), 2 * chunk)
        part = dot_nn(d_query[rows, :], w_qb[...]).astype(jnp.bfloat16)
        for k in range(2):
            own_q[2 * c + k] = part[k * chunk : (k + 1) * chunk]
            line_q.leaf(2 * c + k)
        return carry

    lax.fori_loop(0, own_q.shape[0] // 2, query, 0)
    lat.finish_core()
    lat.start_step(0)
    loads[id(d_feed)].wait()
    turn(d_feed, d_feed_t)
    loads[id(act)].wait()
    down.start_core()
    lat.finish_step(0)
    down.finish_core()
    for step in range(1, lat.count - 1):
        lat.finish_step(step)
    line_lat.leaves()
    down.start_step(0)
    chips = n // 2
    loads[id(d_attn)].wait()
    turn(d_attn, d_attn_t)
    loads[id(ob)].wait()
    out.start_core(line_q.duty)
    out.finish_core(lambda chip: line_q.duty(chips + chip))
    out.start_step(0)
    loads[id(g_kvb)].wait()
    kvb.start_core()
    loads[id(q_latent)].wait()
    turn(q_latent, q_latent_t)
    qb.start_core(lambda chip: line_q.duty(2 * chips + chip))
    kvb.finish_core()
    kvb.start_step(0)
    qb.finish_core(line_lat.duty)
    qb.start_step(0)
    steps = [(item, step) for step in range(lat.count - 1) for item in (down, out, kvb, qb)]
    q_share = spread(len(steps), line_q.ticks - 3 * chips)
    lat_share = spread(len(steps), line_lat.ticks - chips)
    for (item, step), (a, b), (c, d) in zip(steps, q_share, lat_share):
        line_q.pump(3 * chips + a, 3 * chips + b)
        line_lat.pump(chips + c, chips + d)
        item.finish_step(step)
    for item in (*plans, line_q, line_lat):
        item.drain()


def up_tail(n, tp, d_lat, d_query, w_qb, g_kvb, d_attn, ob, q_latent, d_feed, act, collective_id):
    rows, width = d_attn.shape
    rank = q_latent.shape[1]
    hidden = act.shape[1]
    lat_width = d_lat.shape[1]
    vmem = pl.BlockSpec(memory_space=pltpu.VMEM)
    half = jnp.bfloat16
    plans = [
        Scatter(n, rows, lat_width, True),
        Scatter(n, width // n, hidden, False),
        Scatter(n, width // n, ob.shape[1], False),
        Scatter(n, rank // n, d_query.shape[1], False),
        Scatter(n, KVR // n, g_kvb.shape[1], True),
    ]
    q_shape = (rows // TAIL_CHUNK, TAIL_CHUNK, rank)
    lat_shape = (rows // TAIL_CHUNK, TAIL_CHUNK, lat_width)
    sum_q, sum_lat, *grads = pl.pallas_call(
        functools.partial(up_tail_kernel, n, tp, plans),
        out_shape=(
            jax.ShapeDtypeStruct(q_shape, half),
            jax.ShapeDtypeStruct(lat_shape, half),
            *[jax.ShapeDtypeStruct((plan.rows, plan.columns), half) for plan in plans[1:]],
        ),
        in_specs=[vmem] * 3 + [pl.BlockSpec(memory_space=pl.ANY)] * 6,
        out_specs=(vmem,) * 6,
        scratch_shapes=[
            pltpu.VMEM(q_shape, half),
            pltpu.VMEM(q_shape, half),
            pltpu.VMEM(lat_shape, half),
            pltpu.VMEM(lat_shape, half),
            pltpu.VMEM((width, rows), half),
            pltpu.VMEM((rank, rows), half),
            pltpu.VMEM((width, rows), half),
            *[pltpu.VMEM(late.shape, half) for late in (g_kvb, d_attn, ob, q_latent, d_feed, act)],
            pltpu.SemaphoreType.DMA((6,)),
            *line_sems(rows // TAIL_CHUNK),
            *line_sems(rows // TAIL_CHUNK),
            *[shape for plan in plans for shape in plan.scratch()],
        ],
        compiler_params=pltpu.CompilerParams(
            vmem_limit_bytes=MIDDLE_VMEM, collective_id=collective_id, has_side_effects=True
        ),
        cost_estimate=pl.CostEstimate(
            flops=2 * rows * width * (hidden + ob.shape[1]) + 4 * rows * rank * d_query.shape[1],
            bytes_accessed=32 * 1024 * 1024,
            transcendentals=0,
        ),
        name=f"up_tail_{collective_id}",
    )(d_lat, d_query, w_qb, g_kvb, d_attn, ob, q_latent, d_feed, act)
    return sum_q.reshape(rows, rank), sum_lat.reshape(rows, lat_width), *grads


def down_tail_kernel(
    n, plans, sum_q, sum_lat, q_pre, lat_raw, tokens, d_attn_in, gain_row, g_mid, w_qa_in, w_kva_in, cos, sin, grad_in, qa_out, kva_out, gains_out,
    d_q, d_kv, normed_t, scales, g_in, g_q, g_kv, packed, packing, grad_slots, out_sems, d_attn, w_qa, w_kva, in_sems,
    *refs,
):
    take = taker(refs)
    qa, kva, gains = plans
    pairs = ((w_qa_in, w_qa), (w_kva_in, w_kva), (d_attn_in, d_attn))
    loads = [
        pltpu.make_async_copy(source, target, in_sems.at[k])
        for k, (source, target) in enumerate(pairs)
    ]
    for load in loads:
        load.start()
    qa.bind(take, (normed_t, d_q), store_in(qa_out))
    kva.bind(take, (normed_t, d_kv), store_in(kva_out))
    gains.bind(take, packed, store_in(gains_out))
    rows = tokens.shape[0]
    block = rows // 4
    gain_in, _, gain_q, gain_kv = split_gains(gain_row, tokens.shape[1], q_pre.shape[1])
    lane = lax.broadcasted_iota(jnp.int32, (block, HEAD), 1)
    barrier = pltpu.get_barrier_semaphore()
    others = greet_ctx(n, barrier)

    def rows_of(k):
        return pl.ds(pl.multiple_of(k * block, block), block)

    def deliver(k, slot):
        return pltpu.make_async_copy(
            grad_slots.at[slot], grad_in.at[rows_of(k), :], out_sems.at[slot]
        )

    for ref in (g_in, g_q, g_kv):
        ref[...] = jnp.zeros(ref.shape, jnp.float32)

    def norms(k, carry):
        at = rows_of(k)
        pre = q_pre[at, :]
        d_pre, terms = norm_back(
            sum_q[at, :].astype(jnp.float32), pre, norm_scale(pre), gain_q
        )
        g_q[...] += terms
        d_q[at, :] = d_pre.astype(jnp.bfloat16)
        raw = lat_raw[at, :]
        d_raw, terms = norm_back(
            sum_lat[at, :KVR].astype(jnp.float32), raw, norm_scale(raw), gain_kv
        )
        g_kv[...] += terms
        d_kv[at, :KVR] = d_raw.astype(jnp.bfloat16)
        rope = sum_lat[at, KVR:].astype(jnp.float32)
        rope = jnp.concatenate([rope, jnp.zeros((block, HEAD - ROPE), jnp.float32)], axis=1)
        rope = rope_tile_back(rope, cos[at, :], sin[at, :], lane)
        d_kv[at, KVR:] = rope[:, :ROPE].astype(jnp.bfloat16)
        values = tokens[at, :].astype(jnp.float32)
        scale = norm_scale(values)
        scales[at, :] = jnp.broadcast_to(scale, (block, HEAD))
        normed = values * scale * gain_in
        for c in range(0, normed.shape[1], 128):
            normed_t[c : c + 128, at] = normed[:, c : c + 128].T.astype(jnp.bfloat16)
        return carry

    lax.fori_loop(0, 4, norms, 0)
    pl.semaphore_wait(barrier, others)
    qa.start_core()
    kva.start_core()
    qa.finish_core()
    qa.start_step(0)
    kva.finish_core()
    kva.start_step(0)
    for load in loads:
        load.wait()
    for k in range(4):
        at = pl.ds(k * block, block)
        if k >= 2:
            deliver(k - 2, k % 2).wait()
        d_normed = dot_nt(d_q[at, :], w_qa[...]) + dot_nn(d_kv[at, :], w_kva[...])
        d_values, terms = norm_back(
            d_normed, tokens[at, :].astype(jnp.float32), scales[at, :1], gain_in
        )
        g_in[...] += terms
        d_middle = d_attn[at, :].astype(jnp.float32) * (1.0 / RESIDUAL_SCALE)
        grad_slots[k % 2] = d_middle + d_values
        deliver(k, k % 2).start()
    packing[...] = jnp.zeros(packing.shape, jnp.float32)
    lines = gains.rows
    at = 0
    for whole in (g_in, g_mid, g_q, g_kv):
        share = whole.shape[1] // n
        piece = 32 if share % 32 == 0 else 16
        for dest in range(n):
            for place in range(0, share, piece):
                row, column = divmod(at + place, HEAD)
                row += dest * lines
                first = dest * share + place
                packing[row : row + 1, column : column + piece] = whole[:, first : first + piece]
        at += share
    packed[...] = packing[...].astype(jnp.bfloat16)
    gains.start_core()
    gains.finish_core()
    gains.start_step(0)
    for step in range(qa.count - 1):
        for item in (qa, kva, gains):
            item.finish_step(step)
    deliver(2, 0).wait()
    deliver(3, 1).wait()
    for item in plans:
        item.drain()


def down_tail(
    n, sum_q, sum_lat, q_pre, lat_raw, tokens, d_attn, gain_row, g_mid, w_qa, w_kva, cos, sin,
    collective_id,
):
    rows, width = tokens.shape
    rank = q_pre.shape[1]
    vmem = pl.BlockSpec(memory_space=pltpu.VMEM)
    anywhere = pl.BlockSpec(memory_space=pl.ANY)
    half, full = jnp.bfloat16, jnp.float32
    dma = pltpu.SemaphoreType.DMA
    share = (2 * width + rank + KVR) // n
    lines = -(-share // (32 * HEAD)) * 32
    plans = [
        Scatter(n, width // n, rank, False),
        Scatter(n, width // n, KVR + ROPE, False),
        Scatter(n, lines, HEAD, True),
    ]
    slots = pltpu.VMEM((2, rows // 4, width), full)
    grad_in, qa, kva, gains = pl.pallas_call(
        functools.partial(down_tail_kernel, n, plans),
        out_shape=(
            jax.ShapeDtypeStruct((rows, width), full),
            *[jax.ShapeDtypeStruct((plan.rows, plan.columns), half) for plan in plans],
        ),
        in_specs=[vmem] * 5
        + [anywhere]
        + [vmem] * 2
        + [anywhere] * 2
        + [vmem] * 2,
        out_specs=(anywhere, vmem, vmem, vmem),
        scratch_shapes=[
            pltpu.VMEM((rows, rank), half),
            pltpu.VMEM((rows, KVR + ROPE), half),
            pltpu.VMEM((width, rows), half),
            pltpu.VMEM((rows, HEAD), full),
            pltpu.VMEM((1, width), full),
            pltpu.VMEM((1, rank), full),
            pltpu.VMEM((1, KVR), full),
            pltpu.VMEM((n * lines, HEAD), half),
            pltpu.VMEM((n * lines, HEAD), full),
            slots,
            dma((2,)),
            pltpu.VMEM((rows, width), half),
            pltpu.VMEM(w_qa.shape, half),
            pltpu.VMEM(w_kva.shape, half),
            dma((3,)),
            *[shape for plan in plans for shape in plan.scratch()],
        ],
        compiler_params=pltpu.CompilerParams(
            vmem_limit_bytes=MIDDLE_VMEM, collective_id=collective_id, has_side_effects=True
        ),
        cost_estimate=pl.CostEstimate(
            flops=4 * rows * width * (rank + KVR + ROPE),
            bytes_accessed=40 * 1024 * 1024,
            transcendentals=rows,
        ),
        name=f"down_tail_{collective_id}",
    )(
        sum_q,
        sum_lat,
        q_pre,
        lat_raw,
        tokens,
        d_attn,
        gain_row,
        g_mid,
        w_qa,
        w_kva,
        cos,
        sin,
    )
    gains = gains.astype(full).reshape(-1)
    ends = [0]
    for size in (width, width, rank, KVR):
        ends.append(ends[-1] + size // n)
    return grad_in, qa, kva, [gains[first:last] for first, last in zip(ends, ends[1:])]


CHUNK = 16
BLOCK = 8 * CHUNK
LAG = 2
MIDDLE_VMEM = 63 * 1024 * 1024


def middle_kernel(
    n, lag, ob, tokens_in, cot_in, gain, w_out, w_gate, w_up, w_down,
    tt_to, d_to, f_to, act_to, dg_to, du_to, h_to, df_to,
    tt, d_out, f_out, act_out, dg_out, du_out, h_out, df_out,
    tokens, cot, own, up, wo, wg, wu, wd, d_acc, f_acc, w_sems, out_sems, *sems,
):
    line = LineSum(n, own, up, tt, sems, lag)
    width = tokens.shape[1]
    hidden = wg.shape[0]
    chunks, chunk = own.shape[:2]
    per_block = BLOCK // chunk
    blocks = chunks // per_block
    block_lag = -(-(per_block + line.land_lag) // per_block)
    tiles = [(c, min(c + 512, width)) for c in range(0, width, 512)]
    quarter = hidden // 4 // 128 * 128
    cuts = [0, quarter, 2 * quarter, 3 * quarter, hidden]
    loads = [
        pltpu.make_async_copy(source, target, w_sems.at[k])
        for k, (source, target) in enumerate(
            (
                (w_out, wo),
                (cot_in, cot),
                (w_down, wd),
                (tokens_in, tokens),
                (w_gate, wg),
                (w_up, wu),
            )
        )
    ]
    kept = ((d_out, d_to), (f_out, f_to), (act_out, act_to), (dg_out, dg_to), (du_out, du_to))
    kept += ((h_out, h_to), (df_out, df_to))

    def keep(b):
        rows = pl.ds(pl.multiple_of(b * BLOCK, BLOCK), BLOCK)
        copies = [
            pltpu.make_async_copy(source.at[rows, :], target.at[rows, :], out_sems.at[k, b])
            for k, (source, target) in enumerate(kept)
        ]
        some = pl.ds(b * per_block, per_block)
        return copies + [
            pltpu.make_async_copy(tt.at[some], tt_to.at[some], out_sems.at[len(kept), b])
        ]

    for load in loads:
        load.start()
    barrier = pltpu.get_barrier_semaphore()
    line.greet(barrier)
    line.wait_greetings(barrier, 0)

    def project(b, carry):
        rows = pl.ds(pl.multiple_of(b * BLOCK, BLOCK), BLOCK)
        for first, last in tiles:
            part = dot_nt(ob[rows, :], wo[first:last, :]).astype(jnp.bfloat16)
            for k in range(per_block):
                own[per_block * b + k, :, first:last] = part[k * chunk : (k + 1) * chunk, :]
        for k in range(per_block):
            line.leaf(per_block * b + k)
        return carry

    def normalize(b, part):
        for k in range(part * per_block // 2, (part + 1) * per_block // 2, 2):
            rows = pl.ds(pl.multiple_of(b * BLOCK + k * chunk, 2 * chunk), 2 * chunk)
            sums = jnp.concatenate([tt[b * per_block + k], tt[b * per_block + k + 1]], axis=0)
            middle = tokens[rows, :].astype(jnp.float32) + RESIDUAL_SCALE * sums.astype(jnp.float32)
            h_out[rows, :] = (middle * norm_scale(middle) * gain[:, width : 2 * width]).astype(jnp.bfloat16)

    def feed_first(b, i):
        rows = pl.ds(pl.multiple_of(b * BLOCK, BLOCK), BLOCK)
        first, last = cuts[i], cuts[i + 1]
        if i == 0:
            df_out[rows, :] = (RESIDUAL_SCALE * cot[rows, :].astype(jnp.float32)).astype(
                jnp.bfloat16
            )
        du_out[rows, first:last] = dot_nt(df_out[rows, :], wd[first:last, :]).astype(jnp.bfloat16)

    def feed(b, i):
        rows = pl.ds(pl.multiple_of(b * BLOCK, BLOCK), BLOCK)
        first, last = cuts[i], cuts[i + 1]
        if i == 0:
            normalize(b, 0)
            normalize(b, 1)
        gate = dot_nt(h_out[rows, :], wg[first:last, :])
        upper = dot_nt(h_out[rows, :], wu[first:last, :])
        d_act = du_out[rows, first:last].astype(jnp.float32)
        sig = jax.nn.sigmoid(gate)
        silu = gate * sig
        act_out[rows, first:last] = (silu * upper).astype(jnp.bfloat16)
        dg_out[rows, first:last] = (d_act * upper * sig * (1.0 + gate * (1.0 - sig))).astype(
            jnp.bfloat16
        )
        du_out[rows, first:last] = (d_act * silu).astype(jnp.bfloat16)

    def feed_back(b, i):
        rows = pl.ds(pl.multiple_of(b * BLOCK, BLOCK), BLOCK)
        first, last = cuts[i], cuts[i + 1]
        act, dg, du = (ref[rows, first:last] for ref in (act_out, dg_out, du_out))
        for lo, hi in tiles:
            d_part = dot_nn(dg, wg[first:last, lo:hi]) + dot_nn(du, wu[first:last, lo:hi])
            f_part = dot_nn(act, wd[first:last, lo:hi])
            if i:
                d_part = d_part + d_acc[:, lo:hi]
                f_part = f_part + f_acc[:, lo:hi]
            if i < 3:
                d_acc[:, lo:hi] = d_part
                f_acc[:, lo:hi] = f_part
            else:
                d_out[rows, lo:hi] = d_part.astype(jnp.bfloat16)
                f_out[rows, lo:hi] = f_part.astype(jnp.bfloat16)

    loads[0].wait()
    lax.fori_loop(0, blocks, project, 0)
    for load in loads[1:3]:
        load.wait()

    def outer(o, carry):
        b = o - block_lag

        @pl.when(b == 0)
        def _():
            for load in loads[3:]:
                load.wait()

        share = per_block // 8
        for i in range(4):
            for step, work in enumerate((feed, feed_back)):

                @pl.when(o * per_block < line.ticks)
                def _(at=(2 * i + step) * share):
                    for k in range(share):
                        line.duty(o * per_block + at + k)

                @pl.when(2 * o < blocks)
                def _(slot=2 * i + step):
                    feed_first(2 * o + slot // 4, slot % 4)

                @pl.when(b >= 0)
                def _(i=i, work=work):
                    work(b, i)

        @pl.when(b >= 0)
        def _():
            for copy in keep(b):
                copy.start()

        return carry

    lax.fori_loop(0, blocks + block_lag, outer, 0)
    line.drain()

    def finish(b, carry):
        for copy in keep(b):
            copy.wait()
        return carry

    lax.fori_loop(0, blocks, finish, 0)


def middle_layer(n, ob, tokens, cot, gains, w_out, w_gate, w_up, w_down, collective_id):
    rows, width = tokens.shape
    hidden = w_gate.shape[0]
    chunks = rows // CHUNK
    vmem = pl.BlockSpec(memory_space=pltpu.VMEM)
    anywhere = pl.BlockSpec(memory_space=pl.ANY)
    half = jnp.bfloat16
    dma = pltpu.SemaphoreType.DMA
    attn, *rest = pl.pallas_call(
        functools.partial(middle_kernel, n, LAG),
        out_shape=(
            jax.ShapeDtypeStruct((chunks, CHUNK, width), half),
            jax.ShapeDtypeStruct((rows, width), half),
            jax.ShapeDtypeStruct((rows, width), half),
            jax.ShapeDtypeStruct((rows, hidden), half),
            jax.ShapeDtypeStruct((rows, hidden), half),
            jax.ShapeDtypeStruct((rows, hidden), half),
            jax.ShapeDtypeStruct((rows, width), half),
            jax.ShapeDtypeStruct((rows, width), half),
        ),
        in_specs=[vmem, anywhere, anywhere, vmem] + [anywhere] * 4,
        out_specs=(anywhere,) * 8,
        scratch_shapes=[
            pltpu.VMEM((chunks, CHUNK, width), half),
            pltpu.VMEM((rows, width), half),
            pltpu.VMEM((rows, width), half),
            pltpu.VMEM((rows, hidden), half),
            pltpu.VMEM((rows, hidden), half),
            pltpu.VMEM((rows, hidden), half),
            pltpu.VMEM((rows, width), half),
            pltpu.VMEM((rows, width), half),
            pltpu.VMEM((rows, width), half),
            pltpu.VMEM((rows, width), half),
            pltpu.VMEM((chunks, CHUNK, width), half),
            pltpu.VMEM((chunks, CHUNK, width), half),
            pltpu.VMEM(w_out.shape, half),
            pltpu.VMEM(w_gate.shape, half),
            pltpu.VMEM(w_up.shape, half),
            pltpu.VMEM(w_down.shape, half),
            pltpu.VMEM((BLOCK, width), jnp.float32),
            pltpu.VMEM((BLOCK, width), jnp.float32),
            dma((6,)),
            dma((8, rows // BLOCK)),
            *line_sems(chunks),
        ],
        compiler_params=pltpu.CompilerParams(
            vmem_limit_bytes=MIDDLE_VMEM, collective_id=collective_id, has_side_effects=True
        ),
        cost_estimate=pl.CostEstimate(
            flops=2 * rows * width * (6 * hidden + ob.shape[1]),
            bytes_accessed=64 * 1024 * 1024,
            transcendentals=rows * hidden,
        ),
        name=f"middle_layer_{collective_id}",
    )(ob, tokens, cot, gains, w_out, w_gate, w_up, w_down)
    return attn.reshape(rows, width), *rest


def norm_scale(values):
    return lax.rsqrt(jnp.mean(values * values, axis=-1, keepdims=True) + EPSILON)


def norm_back(incoming, values, inv_rms, gain_vec):
    weighted = incoming * gain_vec
    mean = jnp.mean(weighted * values, axis=-1, keepdims=True)
    d_values = inv_rms * weighted - values * (inv_rms * inv_rms * inv_rms) * mean
    return d_values, jnp.sum(incoming * values * inv_rms, axis=0, keepdims=True)


def rope_tile(tile, cos, sin, lane):
    left = pltpu.roll(tile, HEAD - ROPE // 2, 1)
    right = pltpu.roll(tile, ROPE // 2, 1)
    swapped = jnp.where(lane < ROPE // 2, -left, right)
    return jnp.where(lane < ROPE, tile * cos + swapped * sin, 0.0)


def rope_tile_back(tile, cos, sin, lane):
    shifted = tile * sin
    left = pltpu.roll(shifted, HEAD - ROPE // 2, 1)
    right = pltpu.roll(shifted, ROPE // 2, 1)
    swapped = jnp.where(lane < ROPE // 2, left, -right)
    return jnp.where(lane < ROPE, tile * cos + swapped, 0.0)


def split_gains(gains, width, rank):
    ends = (0, width, 2 * width, 2 * width + rank, 2 * width + rank + KVR)
    return [gains[:, first:last] for first, last in zip(ends, ends[1:])]


def head_kernel(
    n, block_map, lengths, tokens, gains, rates, w_qa_in, w_kva, w_qb_in,
    out, q_latent_to, q_pre_to, lat_raw_to, cos_to, sin_to, qx_to, qt_to,
    q_latent, q_pre, lat_raw, cos, sin, qx, qt, w_qa, w_qb, in_sems, out_sems,
    own, normed, w_rope, flat, local_sem, step_sends, step_lands, core_sends, core_lands,
):
    gain_in, _, gain_q, gain_kv = split_gains(gains, tokens.shape[1], w_qa.shape[1])
    heads = qx.shape[1]
    loads = [
        pltpu.make_async_copy(w_qa_in, w_qa, in_sems.at[0]),
        pltpu.make_async_copy(w_qb_in, w_qb, in_sems.at[1]),
    ]
    for load in loads:
        load.start()
    kept = []

    def keep(*pairs):
        for source, target in pairs:
            copy = pltpu.make_async_copy(source, target, out_sems.at[len(kept)])
            copy.start()
            kept.append(copy)

    count = n.bit_length() - 1
    me = lax.axis_index("ctx")
    rows = own.shape[0]
    half = rows // 2
    block = rows // 4
    barrier = pltpu.get_barrier_semaphore()
    for bit in range(count):
        pl.semaphore_signal(barrier, inc=1, device_id={"ctx": me ^ (1 << bit)}, device_id_type=MESH)
    orders = (tuple(range(1, count)), tuple(range(count - 1, 0, -1)))
    lane = lax.broadcasted_iota(jnp.int32, (block, HEAD), 1)
    w_rope[...] = jnp.zeros(w_rope.shape, jnp.bfloat16)
    w_rope[:ROPE, :] = w_kva[KVR : KVR + ROPE, :]

    starts = starts_of(lengths)
    places = lax.broadcasted_iota(jnp.int32, (half, HEAD), 0)
    lanes = lax.broadcasted_iota(jnp.int32, (half, HEAD), 1)
    for j in range(2):
        at = pl.ds(j * half, half)
        place = block_map[j, me] * half + places
        angles = (place - begin_of(place, starts)).astype(jnp.float32) * rates[...]
        cos[at, :] = jnp.where(lanes < ROPE, jnp.cos(angles), 0.0)
        sin[at, :] = jnp.where(lanes < ROPE, jnp.sin(angles), 0.0)

    def latents(k, carry):
        at = pl.ds(pl.multiple_of(k * block, block), block)
        values = tokens[at, :].astype(jnp.float32)
        normed[at, :] = (values * norm_scale(values) * gain_in).astype(jnp.bfloat16)
        raw = dot_nt(normed[at, :], w_kva[:KVR, :])
        lat_raw[at, :] = raw
        own[at, :KVR] = (raw * norm_scale(raw) * gain_kv).astype(jnp.bfloat16)
        rope = rope_tile(dot_nt(normed[at, :], w_rope[...]), cos[at, :], sin[at, :], lane)
        own[at, KVR:] = rope[:, :ROPE].astype(jnp.bfloat16)
        return carry

    keep((cos, cos_to), (sin, sin_to))
    lax.fori_loop(0, 4, latents, 0)
    pl.semaphore_wait(barrier, count)
    local = pltpu.make_async_copy(own, out.at[me], local_sem)
    local.start()

    def chip_copy(part, step, slot, block, first):
        at = pl.ds(part * half, half)
        return pltpu.make_async_remote_copy(
            src_ref=own.at[at, :] if first else out.at[block, at, :],
            dst_ref=out.at[block, at, :],
            send_sem=step_sends.at[part, step, slot],
            recv_sem=step_lands.at[part, step, slot],
            device_id={"ctx": me ^ (1 << orders[part][step])},
            device_id_type=MESH,
        )

    def core_copy(block, slot, first):
        return pltpu.make_async_remote_copy(
            src_ref=own if first else out.at[block],
            dst_ref=out.at[block],
            send_sem=core_sends.at[slot],
            recv_sem=core_lands.at[slot],
            device_id={"ctx": me ^ 1},
            device_id_type=MESH,
        )

    def query(k, carry):
        at = pl.ds(pl.multiple_of(k * block, block), block)
        pre = dot_nn(normed[at, :], w_qa[...])
        q_pre[at, :] = pre
        q_latent[at, :] = (pre * norm_scale(pre) * gain_q).astype(jnp.bfloat16)
        return carry

    def queries(j):
        here = pl.ds(j * half, half)
        cos_j, sin_j = cos[here, :], sin[here, :]
        width = heads * (NOPE + ROPE)
        for at in range(0, width, WIDE):
            end = min(at + WIDE, width)
            flat[:, at:end] = dot_nt(q_latent[here, :], w_qb[at:end, :])
        for h in range(heads):
            at, shift = head_window(h)
            own_part = pltpu.roll(flat[:, at : at + WIDE], (WIDE - shift) % WIDE, 1)[:, :HEAD]
            nope = jnp.where(lanes < NOPE, own_part, 0.0)
            rope = rope_tile(pltpu.roll(own_part, NOPE, 1), cos_j, sin_j, lanes)
            qx[j, h, :, :HEAD] = nope.astype(jnp.bfloat16)
            qx[j, h, :, HEAD:] = rope.astype(jnp.bfloat16)
            qt[j, h, :NOPE, :] = nope.T[:NOPE, :].astype(jnp.bfloat16)
            qt[j, h, NOPE:, :] = rope.T[:ROPE, :].astype(jnp.bfloat16)
        keep((qx.at[j], qx_to.at[j]), (qt.at[j], qt_to.at[j]))

    started = []
    for step in range(count - 1):
        for part, order in enumerate(orders):
            for slot in range(1 << step):
                flips = 0
                for at in range(step):
                    flips |= ((slot >> at) & 1) << order[at]
                copy = chip_copy(part, step, slot, me ^ flips, slot == 0)
                copy.start()
                started.append(copy)
        if step == 0:
            core_copy(me, 0, True).start()
            keep((lat_raw, lat_raw_to))
            for load in loads:
                load.wait()
        lax.fori_loop(min(2 * step, 4), min(2 * step + 2, 4) if step < count - 2 else 4, query, 0)
        if step == count - 2:
            keep((q_pre, q_pre_to), (q_latent, q_latent_to))
            queries(0)
        for part, order in enumerate(orders):
            for slot in range(1 << step):
                chip_copy(part, step, slot, me, slot == 0).wait_recv()
    for chip in range(1, n // 2):
        core_copy(me ^ (2 * chip), chip, False).start()
    queries(1)
    for chip in range(n // 2):
        core_copy(me, chip, chip == 0).wait_recv()
    for copy in started:
        copy.wait_send()
    for chip in range(n // 2):
        core_copy(me, chip, chip == 0).wait_send()
    local.wait()
    for copy in kept:
        copy.wait()


def head_layer(n, block_map, lengths, tokens, gains, w_qa, w_kva, w_qb, collective_id):
    rows, width = tokens.shape
    rank = w_qa.shape[1]
    count = n.bit_length() - 1
    vmem = pl.BlockSpec(memory_space=pltpu.VMEM)
    slots = max(n // 4, 1)
    dma = pltpu.SemaphoreType.DMA
    smem = pl.BlockSpec(memory_space=pltpu.SMEM)
    anywhere = pl.BlockSpec(memory_space=pl.ANY)
    heads = w_qb.shape[0] // (NOPE + ROPE)
    pairs = (2, heads)
    lane = np.arange(HEAD)
    rates = ROPE_BASE ** (-2.0 * (lane % (ROPE // 2)) / ROPE)
    gathered, *rest = pl.pallas_call(
        functools.partial(head_kernel, n),
        out_shape=(
            jax.ShapeDtypeStruct((n, rows, KVR + ROPE), jnp.bfloat16),
            jax.ShapeDtypeStruct((rows, rank), jnp.bfloat16),
            jax.ShapeDtypeStruct((rows, rank), jnp.float32),
            jax.ShapeDtypeStruct((rows, KVR), jnp.float32),
            jax.ShapeDtypeStruct((rows, HEAD), jnp.float32),
            jax.ShapeDtypeStruct((rows, HEAD), jnp.float32),
            jax.ShapeDtypeStruct((*pairs, rows // 2, WIDE), jnp.bfloat16),
            jax.ShapeDtypeStruct((*pairs, NOPE + ROPE, rows // 2), jnp.bfloat16),
        ),
        in_specs=[smem] * 2 + [vmem] * 3 + [anywhere, vmem, anywhere],
        out_specs=(vmem,) + (anywhere,) * 7,
        scratch_shapes=[
            pltpu.VMEM((rows, rank), jnp.bfloat16),
            pltpu.VMEM((rows, rank), jnp.float32),
            pltpu.VMEM((rows, KVR), jnp.float32),
            pltpu.VMEM((rows, HEAD), jnp.float32),
            pltpu.VMEM((rows, HEAD), jnp.float32),
            pltpu.VMEM((*pairs, rows // 2, WIDE), jnp.bfloat16),
            pltpu.VMEM((*pairs, NOPE + ROPE, rows // 2), jnp.bfloat16),
            pltpu.VMEM(w_qa.shape, jnp.bfloat16),
            pltpu.VMEM(w_qb.shape, jnp.bfloat16),
            dma((2,)),
            dma((9,)),
            pltpu.VMEM((rows, KVR + ROPE), jnp.bfloat16),
            pltpu.VMEM((rows, width), jnp.bfloat16),
            pltpu.VMEM((HEAD, width), jnp.bfloat16),
            pltpu.VMEM((rows // 2, window_columns(heads)), jnp.float32),
            dma,
            dma((2, count - 1, slots)),
            dma((2, count - 1, slots)),
            dma((n // 2,)),
            dma((n // 2,)),
        ],
        compiler_params=pltpu.CompilerParams(
            vmem_limit_bytes=VMEM_LIMIT, collective_id=collective_id, has_side_effects=True
        ),
        cost_estimate=pl.CostEstimate(
            flops=2 * rows * width * (rank + KVR + ROPE),
            bytes_accessed=24 * 1024 * 1024,
            transcendentals=rows,
        ),
        name=f"head_layer_{collective_id}",
    )(
        block_map,
        lengths,
        tokens,
        gains,
        jnp.asarray(rates.astype(np.float32).reshape(1, -1)),
        w_qa,
        w_kva,
        w_qb,
    )
    return gathered.reshape(n * rows, -1), *rest


def on_device(
    tokens_in,
    w_qa,
    w_kva,
    w_qb,
    w_kvb,
    w_out,
    w_gate,
    w_up,
    w_down,
    gain_in,
    gain_q,
    gain_kv,
    gain_mid,
    cotangent,
    block_map,
    doc_lengths,
):
    devices = lax.axis_size("ctx")
    block_map = block_map.T
    gains = jnp.concatenate([gain_in, gain_mid, gain_q, gain_kv]).reshape(1, -1)
    latents, q_latent, q_latent_pre, latent_raw, cosine, sine, queries, queries_t = head_layer(
        devices, block_map, doc_lengths, tokens_in, gains, w_qa, w_kva.T, w_qb.T, 0
    )
    attn_f, heads_out, log_totals = attention_forward(
        block_map, doc_lengths, queries, latents, w_kvb
    )
    attention, d_part, feed_part, activation, d_gate, d_up, normed_mid, d_feed = middle_layer(
        lax.axis_size("tp"), heads_out, tokens_in, cotangent, gains, w_out, w_gate.T, w_up.T,
        w_down.T, 5,
    )
    gw_gate, gw_up, d_attention, d_heads, d_gain_mid = gate_up_grads(
        devices, lax.axis_size("tp"), normed_mid, d_gate, d_up, d_part, tokens_in, attention,
        cotangent, gains, w_out, 1,
    )
    d_heads, feed_part = lax.optimization_barrier((d_heads, feed_part))
    feed_own = lax.psum_scatter(feed_part, "tp", scatter_dimension=0, tiled=True)
    own_rows = feed_own.shape[0]
    own_at = lax.axis_index("tp") * own_rows
    tokens_own = lax.dynamic_slice_in_dim(tokens_in, own_at, own_rows, 0).astype(jnp.float32)
    attention_own = lax.dynamic_slice_in_dim(attention, own_at, own_rows, 0).astype(jnp.float32)
    middle_own = tokens_own + RESIDUAL_SCALE * attention_own
    out_own = (middle_own + RESIDUAL_SCALE * feed_own.astype(jnp.float32)).astype(jnp.bfloat16)
    d_query_pre, d_latents, gw_kvb = attention_backward(
        block_map, doc_lengths, queries, queries_t, log_totals, attn_f, d_heads, latents, w_kvb,
        cosine, sine,
    )
    sum_q, sum_lat, gw_down, gw_out, gw_qb, gw_kvb = up_tail(
        devices, lax.axis_size("tp"), d_latents, d_query_pre, w_qb.T, gw_kvb, d_attention, heads_out,
        q_latent, d_feed, activation, 2,
    )
    sum_q, out_own = lax.optimization_barrier((sum_q, out_own))
    out = lax.all_gather(out_own, "tp", axis=0, tiled=True)
    grad_in, gw_qa, gw_kva, own_gains = down_tail(
        devices, sum_q, sum_lat, q_latent_pre, latent_raw, tokens_in, d_attention, gains,
        d_gain_mid, w_qa, w_kva.T, cosine, sine, 3,
    )
    grads = (gw_qa, gw_kva, gw_qb, gw_kvb, gw_out, gw_gate, gw_up, gw_down)
    return (
        out,
        grad_in,
        *[grad.astype(jnp.float32) for grad in grads],
        own_gains[0],
        own_gains[2],
        own_gains[3],
        own_gains[1],
    )


def solution(mesh):
    return jax.shard_map(
        on_device,
        mesh=mesh,
        in_specs=(
            P("ctx", None),
            P(),
            P(),
            P(None, "tp"),
            P(None, "tp"),
            P(None, "tp"),
            P(None, "tp"),
            P(None, "tp"),
            P(None, "tp"),
            P(),
            P(),
            P(),
            P(),
            P("ctx", None),
            P(),
            P(),
        ),
        out_specs=(
            P("ctx", None),
            P("ctx", None),
            P("ctx", None),
            P("ctx", None),
            P("ctx", "tp"),
            P("ctx", "tp"),
            P("ctx", "tp"),
            P("ctx", "tp"),
            P("ctx", "tp"),
            P("ctx", "tp"),
            P("ctx"),
            P("ctx"),
            P("ctx"),
            P("ctx"),
        ),
        check_vma=False,
    )
```
